32 devices in a mesh: section: 2 (over core), tp: 4 (over y, x), seq: 4 (over z).
Axes of the slice: x: 2, y: 2, z: 4, core: 2. Of those that a mesh axis runs over, the one named last changes fastest.
Arguments:
- layer_input: bfloat16 [4, 2, 2048, 768], P(None, None, 'seq'), may hold values from -6 to 6
- cotangent: bfloat16 [4, 2, 2048, 768], P(None, None, 'seq'), may hold values from -6 to 6
- doc_lengths: int32 [4, 2, 4], replicated, may hold values from 1 to 512, 1024 in all within a row
- ln1_gain: float32 [2, 768], P('section'), may hold values from 0.5 to 1.5
- w_qkv: bfloat16 [2, 768, 3, 768], P('section', None, None, 'tp'), may hold values from -0.21875 to 0.21875
- w_out: bfloat16 [2, 768, 768], P('section', 'tp'), may hold values from -0.625 to 0.625
- ln2_gain: float32 [2, 768], P('section'), may hold values from 0.5 to 1.5
- w_up: bfloat16 [2, 768, 3072], P('section', None, 'tp'), may hold values from -0.21875 to 0.21875
- b_up: float32 [2, 3072], P('section', 'tp'), may hold values from -3 to 3
- w_down: bfloat16 [2, 3072, 768], P('section', 'tp'), may hold values from -0.109375 to 0.109375
- b_down: float32 [2, 768], P('section'), may hold values from -2 to 2
Outputs:
- layer_out: bfloat16 [2, 4, 2, 2048, 768], P('section', None, None, 'seq')
- input_grad: bfloat16 [2, 4, 2, 2048, 768], P('section', None, None, 'seq')
- grad_ln1_gain: float32 [2, 768], P('section')
- grad_w_qkv: float32 [2, 768, 3, 768], P('section', None, None, 'tp')
- grad_w_out: float32 [2, 768, 768], P('section', 'tp')
- grad_ln2_gain: float32 [2, 768], P('section')
- grad_w_up: float32 [2, 768, 3072], P('section', None, 'tp')
- grad_b_up: float32 [2, 3072], P('section', 'tp')
- grad_w_down: float32 [2, 3072, 768], P('section', 'tp')
- grad_b_down: float32 [2, 768], P('section')
The draws below stay inside these ranges and needn't reach their ends.
All inputs are finite; a program needn't handle non-finite values.
Results may differ from the reference program's by a relative error of at most 0.028.
Values may be sent and summed in bfloat16 or wider, within the bound.
A program may use at most 512 MiB of HBM per device.

```python
import math
import jax
import jax.numpy as jnp
import numpy as np
from jax import lax

D = 768
HEADS = 12
HDIM = 64
FF = 3072
BLOCK = 16
HALF = 1024
NDOC = 4
MICRO = 4
ROWS = 2
LEN = 2048


def level_of(stream_key, dims, pieces, smallest, largest):
    def one(axis_at, parts):
        steps = jax.random.uniform(jax.random.fold_in(jax.random.fold_in(stream_key, 6), axis_at), (parts,), jnp.float32, smallest / len(pieces), largest / len(pieces))
        return jnp.repeat(jnp.exp(steps), dims[axis_at] // parts).reshape((-1,) + (1,) * (len(dims) - axis_at - 1))

    level = one(*pieces[0])
    for cut in pieces[1:]:
        level = level * one(*cut)
    return level


def split_up(count, total, reach, lean):
    weights = [(1 << 20) // math.isqrt(grade ** lean) + 1 for grade in range(2, count + 1)]
    rest, given = total - reach - (count - 1), [1] * (count - 1)
    while rest > 0:
        candidates = [i for i in range(count - 1) if given[i] < reach]
        whole, budget = sum([weights[i] for i in candidates]), rest
        for i in candidates:
            more = min(reach - given[i], max(1, budget * weights[i] // whole), rest)
            given[i] = given[i] + more
            rest = rest - more
    return np.array([reach] + given)


def ragged(own_key, amount, total, reach, slope):
    if amount == 2:
        one = jax.random.randint(own_key, (), max(1, total - reach), min(reach, total - 1) + 1)
        return jnp.stack([one, total - one])
    tallies = jnp.asarray(split_up(amount, total, reach, slope), jnp.int32)
    pairs = (amount - 1) // 2
    giver, taker = tallies[1:1 + 2 * pairs:2], tallies[2:2 + 2 * pairs:2]
    slack = jnp.minimum(giver - 1, reach - taker)
    shifted = jax.random.randint(jax.random.fold_in(own_key, 1), (pairs,), 0, 1 << 20) % (slack + 1)
    tallies = tallies.at[1:1 + 2 * pairs:2].set(giver - shifted).at[2:2 + 2 * pairs:2].set(taker + shifted)
    return tallies[jax.random.permutation(jax.random.fold_in(own_key, 2), amount)]


def normal_values(key, shape, width, reach, shards=(), held_as=jnp.bfloat16):
    entries = jax.random.normal(key, shape, jnp.float32) * width
    if len(shards) > 0:
        entries = level_of(key, shape, shards, -0.22, 0.18) * entries
    return jnp.clip(entries, min=-reach, max=reach).astype(held_as)


def setup_inputs(seed: int = 0) -> dict:
    splits = jax.random.split(jax.random.key(seed), 12)
    return {
        "layer_input": normal_values(splits[0], (MICRO, ROWS, LEN, D), 1.0, 6.0, ((2, 4),)),
        "cotangent": normal_values(splits[1], (MICRO, ROWS, LEN, D), 1.0, 6.0, ((2, 4),)),
        "doc_lengths": jax.vmap(lambda own: ragged(own, NDOC, HALF, HALF // 2, 2))(jax.random.split(splits[2], MICRO * ROWS)).reshape((MICRO, ROWS, NDOC)).astype(jnp.int32),
        "ln1_gain": jnp.clip(1.0 + 0.1 * jax.random.normal(splits[3], (2, D), jnp.float32), 0.5, 1.5),
        "w_qkv": normal_values(splits[4], (2, D, 3, D), D ** -0.5, 0.21875, ((0, 2), (3, 4))),
        "w_out": normal_values(splits[5], (2, D, D), (D // 8) ** -0.5, 0.625, ((0, 2), (1, 4))),
        "ln2_gain": jnp.clip(1.0 + 0.1 * jax.random.normal(splits[6], (2, D), jnp.float32), 0.5, 1.5),
        "w_up": normal_values(splits[7], (2, D, FF), D ** -0.5, 0.21875, ((0, 2), (2, 4))),
        "b_up": normal_values(splits[8], (2, FF), 0.5, 3.0, ((0, 2), (1, 4)), jnp.float32),
        "w_down": normal_values(splits[9], (2, FF, D), FF ** -0.5, 0.109375, ((0, 2), (1, 4))),
        "b_down": normal_values(splits[10], (2, D), 0.3, 2.0, ((0, 2),), jnp.float32),
    }


@jax.custom_vjp
def low(v):
    return lax.optimization_barrier(v.astype(jnp.bfloat16)).astype(jnp.float32)

@jax.custom_vjp
def low_back(v):
    return v

def low_keep(v):
    return (low(v), None)

def low_pass(kept, grad):
    return (grad,)

def back_keep(v):
    return (v, None)

def back_low(kept, grad):
    return (low(grad),)
low.defvjp(low_keep, low_pass)
low_back.defvjp(back_keep, back_low)

def layer_norm(values, gain):
    center = values - lax.optimization_barrier(jnp.mean(values, axis=-1, keepdims=True))
    spread = lax.optimization_barrier(jnp.mean(center * center, axis=-1, keepdims=True))
    return center * lax.rsqrt(spread + 1e-05) * gain

def rotate(values, cosine, sine_table):
    middle = values.shape[-1] // 2
    first_half = values[..., :middle]
    second_half = values[..., middle:]
    return jnp.concatenate([first_half * cosine - second_half * sine_table, second_half * cosine + first_half * sine_table], axis=-1)

def rotary_tables(positions):
    frequency = 10000.0 ** (-jnp.arange(HDIM // 2).astype(jnp.float32) * 2.0 / HDIM)
    angles = (positions % HALF).astype(jnp.float32)[:, None, None] * frequency[None, None, :]
    return (jnp.cos(angles), jnp.sin(angles))

def allowed(query_pos, query_doc, key_pos, key_doc):
    query_noisy = query_pos < HALF
    key_noisy = key_pos < HALF
    query_block = query_pos % HALF // BLOCK
    key_block = key_pos % HALF // BLOCK
    within = query_noisy & key_noisy & (query_block == key_block)
    earlier = query_noisy & ~key_noisy & (key_block < query_block)
    causal = ~query_noisy & ~key_noisy & (key_block <= query_block)
    return (within | earlier | causal) & (query_doc == key_doc)

def document_ids(doc_lengths):
    doc_ends = jnp.cumsum(doc_lengths, axis=-1)
    base_pos = jnp.arange(2 * HALF) % HALF
    return lax.optimization_barrier(jnp.sum((base_pos[:, None] >= doc_ends[..., None, :]).astype(jnp.int32), axis=-1)).astype(jnp.int32)

def attend_row(operands):
    queries, keys_row, values_row, docs_row = operands
    positions = jnp.arange(2 * HALF)
    key_mask = allowed(positions[:, None], docs_row[:, None], positions[None, :], docs_row[None, :])
    scores = jnp.einsum('qhd,khd->hqk', queries, keys_row, precision=lax.Precision.HIGHEST) * 0.125
    scores = low_back(jnp.where(key_mask[None], scores, -1e+30))
    softmax_out = low(jax.nn.softmax(scores, axis=-1))
    return jnp.einsum('hqk,khd->qhd', softmax_out, values_row, precision=lax.Precision.HIGHEST)

def block_layer(inputs, docs_all, cosine, sine_table, layer_params):
    ln_one, w_mix, w_proj, ln_two, w_first, b_first, w_second, b_second = layer_params
    row_count = inputs.shape[0]
    highest = lax.Precision.HIGHEST
    normed = low(layer_norm(inputs, ln_one))
    mixed = low_back(jnp.einsum('rtd,dcf->rtcf', normed, w_mix, precision=highest))
    queries = low(low_back(rotate(mixed[:, :, 0].reshape(row_count, 2 * HALF, HEADS, HDIM), cosine, sine_table)))
    keys_all = low(low_back(rotate(mixed[:, :, 1].reshape(row_count, 2 * HALF, HEADS, HDIM), cosine, sine_table)))
    values_all = low(mixed[:, :, 2].reshape(row_count, 2 * HALF, HEADS, HDIM))
    attended = lax.map(jax.checkpoint(attend_row), (queries, keys_all, values_all, docs_all))
    attended = low(low_back(attended.reshape(row_count, 2 * HALF, D)))
    middle = inputs + low_back(jnp.einsum('rte,ed->rtd', attended, w_proj, precision=highest))
    normed_two = low(layer_norm(middle, ln_two))
    hidden_pre = low_back(jnp.einsum('rtd,df->rtf', normed_two, w_first, precision=highest) + b_first)
    activated = low(jax.nn.gelu(hidden_pre, approximate=True))
    return middle + low_back(jnp.einsum('rtf,fd->rtd', activated, w_second, precision=highest)) + b_second

def reference(layer_input, cotangent, doc_lengths, ln1_gain, w_qkv, w_out, ln2_gain, w_up, b_up, w_down, b_down):
    row_count = MICRO * ROWS
    inputs = layer_input.astype(jnp.float32).reshape(row_count, 2 * HALF, D)
    seeded = cotangent.astype(jnp.float32).reshape(row_count, 2 * HALF, D)
    docs_all = document_ids(doc_lengths.reshape(row_count, NDOC))
    cosine, sine_table = rotary_tables(jnp.arange(2 * HALF))
    all_params = tuple((weight.astype(jnp.float32) for weight in (ln1_gain, w_qkv, w_out, ln2_gain, w_up, b_up, w_down, b_down)))

    def forward(entry, injected, layer_params):
        first_layer = tuple((weight[0] for weight in layer_params))
        second_layer = tuple((weight[1] for weight in layer_params))
        handed = low(block_layer(low_back(entry), docs_all, cosine, sine_table, first_layer))
        final = low(block_layer(low_back(handed + injected), docs_all, cosine, sine_table, second_layer))
        return (final, handed)
    final, pullback, handed = jax.vjp(forward, inputs, jnp.zeros_like(inputs), all_params, has_aux=True)
    grad_entry, grad_injected, grad_params = pullback(seeded)
    full_shape = (2, MICRO, ROWS, 2 * HALF, D)
    layer_out = jnp.stack([handed, final]).reshape(full_shape).astype(jnp.bfloat16)
    input_grad = jnp.stack([grad_entry, grad_injected]).reshape(full_shape).astype(jnp.bfloat16)
    return (layer_out, input_grad, grad_params[0], grad_params[1], grad_params[2], grad_params[3], grad_params[4], grad_params[5], grad_params[6], grad_params[7])
```

```python
import jax
import jax.numpy as jnp
from jax import lax
from jax.sharding import PartitionSpec as P

HDIM = 64
BLOCK = 16
HALF = 1024


def from_behind(value, axis, by):
    size = lax.axis_size(axis)
    pairs = [(i, i + by) for i in range(size) if 0 <= i + by < size]
    return lax.ppermute(value, axis, pairs)


def layer_norm(values, gain):
    center = values - jnp.mean(values, axis=-1, keepdims=True)
    spread = jnp.mean(center * center, axis=-1, keepdims=True)
    return center * lax.rsqrt(spread + 1e-05) * gain


def rotate(values, cosine, sine_table):
    middle = values.shape[-1] // 2
    first_half = values[..., :middle]
    second_half = values[..., middle:]
    return jnp.concatenate(
        [
            first_half * cosine - second_half * sine_table,
            second_half * cosine + first_half * sine_table,
        ],
        axis=-1,
    )


def rotary_tables(positions):
    frequency = 10000.0 ** (-jnp.arange(HDIM // 2).astype(jnp.float32) * 2.0 / HDIM)
    angles = (positions % HALF).astype(jnp.float32)[:, None, None] * frequency[None, None, :]
    return (jnp.cos(angles), jnp.sin(angles))


def allowed(query_pos, query_doc, key_pos, key_doc):
    query_noisy = query_pos < HALF
    key_noisy = key_pos < HALF
    query_block = query_pos % HALF // BLOCK
    key_block = key_pos % HALF // BLOCK
    within = query_noisy & key_noisy & (query_block == key_block)
    earlier = query_noisy & ~key_noisy & (key_block < query_block)
    causal = ~query_noisy & ~key_noisy & (key_block <= query_block)
    return (within | earlier | causal) & (query_doc == key_doc)


def document_ids(doc_lengths):
    doc_ends = jnp.cumsum(doc_lengths, axis=-1)
    base_pos = jnp.arange(2 * HALF) % HALF
    return jnp.sum((base_pos[:, None] >= doc_ends[..., None, :]).astype(jnp.int32), axis=-1)


def gelu_tanh(values):
    return jax.nn.gelu(values, approximate=True)


def keep_slot(storage, value, slot_index, is_active):
    current = lax.dynamic_index_in_dim(storage, slot_index, 0, keepdims=False)
    return lax.dynamic_update_index_in_dim(
        storage, jnp.where(is_active, value, current), slot_index, 0
    )


def local_queries(inputs, ln_one, w_mix, tables):
    cosine, sine_table, query_pos = tables
    row_count, pos_count = (inputs.shape[0], inputs.shape[1])
    normed = layer_norm(inputs, ln_one).astype(jnp.bfloat16)
    mixed = jnp.einsum("rpd,dcf->rpcf", normed, w_mix, preferred_element_type=jnp.float32)
    shaped = mixed.reshape(row_count, pos_count, 3, -1, HDIM)
    queries = rotate(shaped[:, :, 0], cosine, sine_table).astype(jnp.bfloat16)
    keys_own = rotate(shaped[:, :, 1], cosine, sine_table).astype(jnp.bfloat16)
    values_own = shaped[:, :, 2].astype(jnp.bfloat16)
    return (normed, queries, keys_own, values_own)


def masked_scores(queries, keys_heads, query_pos, docs_all):
    pos_count = queries.shape[1]
    query_docs = lax.dynamic_slice_in_dim(docs_all, query_pos[0], pos_count, 1)
    key_pos = jnp.arange(keys_heads.shape[1])
    key_mask = allowed(
        query_pos[None, :, None],
        query_docs[:, :, None],
        key_pos[None, None, :],
        docs_all[:, None, :],
    )
    scores = (
        jnp.einsum("rqhd,rkhd->rhqk", queries, keys_heads, preferred_element_type=jnp.float32)
        * 0.125
    )
    return jnp.where(key_mask[:, None], scores, -1e30)


def forward_step(inputs, weights, tables, docs_all):
    ln_one, w_mix, w_proj, ln_two, w_first, b_first, w_second, b_second = weights
    row_count, pos_count = (inputs.shape[0], inputs.shape[1])
    normed, queries, keys_own, values_own = local_queries(inputs, ln_one, w_mix, tables)
    local_width = w_mix.shape[-1]
    keys_all, values_all = (
        lax.all_gather(
            keys_own.reshape(row_count, pos_count, local_width), "seq", axis=1, tiled=True
        ),
        lax.all_gather(
            values_own.reshape(row_count, pos_count, local_width), "seq", axis=1, tiled=True
        ),
    )
    keys_heads = keys_all.reshape(row_count, keys_all.shape[1], -1, HDIM)
    values_heads = values_all.reshape(row_count, values_all.shape[1], -1, HDIM)
    softmax_out = jax.nn.softmax(
        masked_scores(queries, keys_heads, tables[2], docs_all), axis=-1
    ).astype(jnp.bfloat16)
    attended = jnp.einsum(
        "rhqk,rkhd->rqhd", softmax_out, values_heads, preferred_element_type=jnp.float32
    )
    attended = attended.astype(jnp.bfloat16).reshape(row_count, pos_count, local_width)
    middle = inputs + lax.psum(
        jnp.einsum("rpe,ed->rpd", attended, w_proj, preferred_element_type=jnp.float32).astype(
            jnp.bfloat16
        ),
        "tp",
    ).astype(jnp.float32)
    normed_two = layer_norm(middle, ln_two).astype(jnp.bfloat16)
    hidden_pre = (
        jnp.einsum("rpd,df->rpf", normed_two, w_first, preferred_element_type=jnp.float32) + b_first
    )
    activated = gelu_tanh(hidden_pre).astype(jnp.bfloat16)
    second_terms = jnp.einsum(
        "rpf,fd->rpd", activated, w_second, preferred_element_type=jnp.float32
    )
    result = (
        middle + lax.psum(second_terms.astype(jnp.bfloat16), "tp").astype(jnp.float32) + b_second
    )
    return (result, middle, keys_all, values_all)


def backward_step(inputs, middle, grad_out, weights, tables, docs_all):
    ln_one, w_mix, w_proj, ln_two, w_first, b_first, w_second, b_second = weights
    cosine, sine_table, query_pos = tables
    row_count, pos_count = (inputs.shape[0], inputs.shape[1])
    local_width = w_mix.shape[-1]
    head_count = local_width // HDIM
    normed, queries, keys_own, values_own = local_queries(inputs, ln_one, w_mix, tables)
    keys_all, values_all = (
        lax.all_gather(
            keys_own.reshape(row_count, pos_count, local_width), "seq", axis=1, tiled=True
        ),
        lax.all_gather(
            values_own.reshape(row_count, pos_count, local_width), "seq", axis=1, tiled=True
        ),
    )
    keys_heads = keys_all.reshape(row_count, keys_all.shape[1], head_count, HDIM)
    values_heads = values_all.reshape(row_count, values_all.shape[1], head_count, HDIM)
    scores = masked_scores(queries, keys_heads, query_pos, docs_all)
    softmax_out = jax.nn.softmax(scores, axis=-1)
    probs_low = softmax_out.astype(jnp.bfloat16)
    attended = jnp.einsum(
        "rhqk,rkhd->rqhd", probs_low, values_heads, preferred_element_type=jnp.float32
    )
    attended = attended.astype(jnp.bfloat16).reshape(row_count, pos_count, local_width)
    normed_two = layer_norm(middle, ln_two).astype(jnp.bfloat16)
    hidden_pre = (
        jnp.einsum("rpd,df->rpf", normed_two, w_first, preferred_element_type=jnp.float32) + b_first
    )
    activated = gelu_tanh(hidden_pre).astype(jnp.bfloat16)
    grad_low = grad_out.astype(jnp.bfloat16)
    grad_b_second = jnp.sum(grad_out, axis=(0, 1))
    grad_w_second = jnp.einsum(
        "rpf,rpd->fd", activated, grad_low, preferred_element_type=jnp.float32
    )
    grad_act = jnp.einsum("rpd,fd->rpf", grad_low, w_second, preferred_element_type=jnp.float32)
    unused_value, gelu_back = jax.vjp(gelu_tanh, hidden_pre)
    grad_pre = gelu_back(grad_act)[0].astype(jnp.bfloat16)
    grad_b_first = jnp.sum(grad_pre, axis=(0, 1), dtype=jnp.float32)
    grad_w_first = jnp.einsum(
        "rpd,rpf->df", normed_two, grad_pre, preferred_element_type=jnp.float32
    )
    grad_normed_two = lax.psum(
        jnp.einsum("rpf,df->rpd", grad_pre, w_first, preferred_element_type=jnp.float32).astype(
            jnp.bfloat16
        ),
        "tp",
    ).astype(jnp.float32)
    unused_norm, second_back = jax.vjp(layer_norm, middle, ln_two)
    grad_middle_norm, grad_ln_two = second_back(grad_normed_two)
    grad_middle = grad_out + grad_middle_norm
    middle_low = grad_middle.astype(jnp.bfloat16)
    grad_w_proj = jnp.einsum(
        "rpe,rpd->ed", attended, middle_low, preferred_element_type=jnp.float32
    )
    grad_att = jnp.einsum("rpd,ed->rpe", middle_low, w_proj, preferred_element_type=jnp.float32)
    grad_att = grad_att.astype(jnp.bfloat16).reshape(row_count, pos_count, head_count, HDIM)
    grad_probs = jnp.einsum(
        "rqhd,rkhd->rhqk", grad_att, values_heads, preferred_element_type=jnp.float32
    )
    row_delta = jnp.sum(grad_probs * softmax_out, axis=-1, keepdims=True)
    grad_scores = (softmax_out * (grad_probs - row_delta)).astype(jnp.bfloat16)
    grad_queries = (
        jnp.einsum("rhqk,rkhd->rqhd", grad_scores, keys_heads, preferred_element_type=jnp.float32)
        * 0.125
    )
    full_len = keys_all.shape[1]
    part_keys = (
        jnp.einsum("rhqk,rqhd->rkhd", grad_scores, queries, preferred_element_type=jnp.float32)
        * 0.125
    )
    part_values = jnp.einsum(
        "rhqk,rqhd->rkhd", probs_low, grad_att, preferred_element_type=jnp.float32
    )
    grad_keys, grad_values = (
        lax.psum_scatter(
            part_keys.reshape(row_count, full_len, local_width).astype(jnp.bfloat16),
            "seq",
            scatter_dimension=1,
            tiled=True,
        ).astype(jnp.float32),
        lax.psum_scatter(
            part_values.reshape(row_count, full_len, local_width).astype(jnp.bfloat16),
            "seq",
            scatter_dimension=1,
            tiled=True,
        ).astype(jnp.float32),
    )
    grad_query_raw = rotate(grad_queries.astype(jnp.bfloat16), cosine, -sine_table)
    grad_key_raw = rotate(
        grad_keys.astype(jnp.bfloat16).reshape(row_count, pos_count, head_count, HDIM),
        cosine,
        -sine_table,
    )
    grad_mixed = jnp.stack(
        [
            grad_query_raw.reshape(row_count, pos_count, local_width).astype(jnp.bfloat16),
            grad_key_raw.reshape(row_count, pos_count, local_width).astype(jnp.bfloat16),
            grad_values.astype(jnp.bfloat16),
        ],
        axis=2,
    )
    grad_w_mix = jnp.einsum("rpd,rpcf->dcf", normed, grad_mixed, preferred_element_type=jnp.float32)
    grad_normed = lax.psum(
        jnp.einsum("rpcf,dcf->rpd", grad_mixed, w_mix, preferred_element_type=jnp.float32).astype(
            jnp.bfloat16
        ),
        "tp",
    ).astype(jnp.float32)
    unused_first, first_back = jax.vjp(layer_norm, inputs, ln_one)
    grad_in_norm, grad_ln_one = first_back(grad_normed)
    grad_inputs = grad_middle + grad_in_norm
    return (
        grad_inputs,
        (
            grad_ln_one,
            grad_w_mix,
            grad_w_proj,
            grad_ln_two,
            grad_w_first,
            grad_b_first,
            grad_w_second,
            grad_b_second,
        ),
    )


def pipelined(
    layer_input,
    cotangent,
    doc_lengths,
    ln1_gain,
    w_qkv,
    w_out,
    ln2_gain,
    w_up,
    b_up,
    w_down,
    b_down,
):
    weights = tuple(
        (weight[0] for weight in (ln1_gain, w_qkv, w_out, ln2_gain, w_up, b_up, w_down, b_down))
    )
    micros, row_count, pos_count, width_model = layer_input.shape
    sections = lax.axis_size("section")
    section_index = lax.axis_index("section")
    first_pos = lax.axis_index("seq") * pos_count
    query_pos = first_pos + jnp.arange(pos_count)
    cosine, sine_table = rotary_tables(query_pos)
    tables = (cosine, sine_table, query_pos)
    docs_every = document_ids(doc_lengths)
    kept_inputs = jnp.zeros((micros, row_count, pos_count, width_model), jnp.float32)
    kept_middle = jnp.zeros((micros, row_count, pos_count, width_model), jnp.float32)
    layer_out = jnp.zeros(layer_input.shape, jnp.bfloat16)
    arrived = jnp.zeros((row_count, pos_count, width_model), jnp.bfloat16)
    moments = micros + sections - 1
    for moment in range(moments):
        offset = moment - section_index
        micro_index = jnp.clip(offset, 0, micros - 1)
        is_active = (offset >= 0) & (offset < micros)
        own_input = layer_input[min(moment, micros - 1)]
        inputs = jnp.where(section_index == 0, own_input, arrived).astype(jnp.float32)
        result, middle, keys_all, values_all = forward_step(
            inputs, weights, tables, docs_every[micro_index]
        )
        kept_inputs = keep_slot(kept_inputs, inputs, micro_index, is_active)
        kept_middle = keep_slot(kept_middle, middle, micro_index, is_active)
        result_low = result.astype(jnp.bfloat16)
        layer_out = keep_slot(layer_out, result_low, micro_index, is_active)
        if moment < moments - 1:
            arrived = from_behind(result_low, "section", 1)
    grad_totals = tuple((jnp.zeros(weight.shape, jnp.float32) for weight in weights))
    input_grad = jnp.zeros(layer_input.shape, jnp.bfloat16)
    returned = jnp.zeros((row_count, pos_count, width_model), jnp.bfloat16)
    for moment in range(moments):
        offset = moment - (sections - 1 - section_index)
        micro_index = jnp.clip(offset, 0, micros - 1)
        is_active = (offset >= 0) & (offset < micros)
        incoming = jnp.where(
            section_index == sections - 1, cotangent[min(moment, micros - 1)], returned
        ).astype(jnp.float32)
        incoming = jnp.where(is_active, incoming, 0.0)
        grad_inputs, grad_parts = backward_step(
            kept_inputs[micro_index],
            kept_middle[micro_index],
            incoming,
            weights,
            tables,
            docs_every[micro_index],
        )
        grad_totals = tuple((total + piece for total, piece in zip(grad_totals, grad_parts)))
        grad_sent = grad_inputs.astype(jnp.bfloat16)
        input_grad = keep_slot(input_grad, grad_sent, micro_index, is_active)
        if moment < moments - 1:
            returned = from_behind(grad_sent, "section", -1)
    (
        grad_ln_one,
        grad_w_mix,
        grad_w_proj,
        grad_ln_two,
        grad_w_first,
        grad_b_first,
        grad_w_second,
        grad_b_second,
    ) = grad_totals
    summed = (
        lax.psum(grad_ln_one.astype(jnp.bfloat16), "seq").astype(jnp.float32),
        lax.psum(grad_w_mix.astype(jnp.bfloat16), "seq").astype(jnp.float32),
        lax.psum(grad_w_proj.astype(jnp.bfloat16), "seq").astype(jnp.float32),
        lax.psum(grad_ln_two.astype(jnp.bfloat16), "seq").astype(jnp.float32),
        lax.psum(grad_w_first.astype(jnp.bfloat16), "seq").astype(jnp.float32),
        lax.psum(grad_b_first.astype(jnp.bfloat16), "seq").astype(jnp.float32),
        lax.psum(grad_w_second.astype(jnp.bfloat16), "seq").astype(jnp.float32),
        lax.psum(grad_b_second.astype(jnp.bfloat16), "seq").astype(jnp.float32),
    )
    return (
        layer_out[None],
        input_grad[None],
        summed[0][None],
        summed[1][None],
        summed[2][None],
        summed[3][None],
        summed[4][None],
        summed[5][None],
        summed[6][None],
        summed[7][None],
    )


PIECE = 256


def move(value, route):
    sections, columns, planes = (lax.axis_size(name) for name in ("section", "tp", "seq"))
    pairs = []
    for s in range(sections):
        for t in range(columns):
            for z in range(planes):
                target = route(s, t, z)
                if target is not None:
                    source_index = (s * columns + t) * planes + z
                    target_index = (target[0] * columns + target[1]) * planes + target[2]
                    pairs.append((source_index, target_index))
    return lax.ppermute(value, ("section", "tp", "seq"), pairs)


def other_core(s, t, z):
    return (1 - s, t, z)


def first_hop(s, t, z):
    return (s, t ^ 1, z) if s == 0 else (s, t ^ 2, z)


def second_hop(s, t, z):
    return (s, t ^ 2, z) if s == 0 else (s, t ^ 1, z)


def far_plane(s, t, z):
    return (s, t, z ^ 2)


def gather_plane(own):
    one = move(own, first_hop)
    two = move(own, second_hop)
    three = move(one, second_hop)
    return [own, one, two, three]


def scatter_plane(pieces):
    far = move(pieces[3], second_hop)
    near_two = move(pieces[2], second_hop)
    one = (pieces[1].astype(jnp.float32) + far.astype(jnp.float32)).astype(jnp.bfloat16)
    near_one = move(one, first_hop)
    total = (
        pieces[0].astype(jnp.float32)
        + near_one.astype(jnp.float32)
        + near_two.astype(jnp.float32)
    )
    return total.astype(jnp.bfloat16)


def sum_planes(value, z):
    arrived = move(value, lambda s, t, z: {0: (s, t, 1), 3: (s, t, 2)}.get(z))
    value = (value.astype(jnp.float32) + arrived.astype(jnp.float32)).astype(jnp.bfloat16)
    arrived = move(value, lambda s, t, z: {1: (s, t, 2), 2: (s, t, 1)}.get(z))
    value = (value.astype(jnp.float32) + arrived.astype(jnp.float32)).astype(jnp.bfloat16)
    arrived = move(value, lambda s, t, z: {1: (s, t, 0), 2: (s, t, 3)}.get(z))
    return jnp.where((z == 0) | (z == 3), arrived, value)


def next_block(s, t, z):
    if s == 0:
        return (1, t, z)
    return (0, t, z + 1) if z % 2 == 0 else None


def after_next_block(s, t, z):
    return (0, t, z + 1) if s == 0 and z % 2 == 0 else None


def last_block(s, t, z):
    return (1, t, z) if s == 0 and z % 2 == 1 else None


def backward_route(route):
    def reverse(s, t, z):
        for source in ((0, t, z), (1, t, z), (0, t, z - 1), (1, t, z - 1)):
            if source[2] >= 0 and route(*source) == (s, t, z):
                return source
        return None

    return reverse


def share_keys(clean, is_last):
    near = move(clean, next_block)
    far = move(clean, after_next_block)
    far_last = move(near, last_block)
    return near, jnp.where(is_last, far_last, far)


def return_keys(grad_near, grad_far):
    low_near, low_far = grad_near.astype(jnp.bfloat16), grad_far.astype(jnp.bfloat16)
    passed = move(low_far, backward_route(last_block))
    low_near = (grad_near + passed.astype(jnp.float32)).astype(jnp.bfloat16)
    one = move(low_near, backward_route(next_block))
    two = move(low_far, backward_route(after_next_block))
    return one.astype(jnp.float32) + two.astype(jnp.float32)


def spread(
    layer_input,
    cotangent,
    doc_lengths,
    ln1_gain,
    w_qkv,
    w_out,
    ln2_gain,
    w_up,
    b_up,
    w_down,
    b_down,
):
    s, t, z = (lax.axis_index(name) for name in ("section", "tp", "seq"))
    micros, rows, width_pos, width = layer_input.shape
    half, group = z % 2, z // 2
    shard = w_up.shape[-1]
    columns = w_out.shape[1]
    heads = 4 * columns // HDIM
    on_first = s == 0

    def take_tokens(whole):
        flat = whole.reshape(micros * rows, width_pos, width)
        own = lax.dynamic_slice(flat, (4 * group + t, s * PIECE, 0), (1, PIECE, width))[0]
        sent = lax.dynamic_slice(flat, (4 * (1 - group) + t, s * PIECE, 0), (1, PIECE, width))[0]
        arrived = move(sent, far_plane)
        noisy = jnp.where(group == 0, own, arrived)
        clean = jnp.where(group == 0, arrived, own)
        return jnp.concatenate([noisy, clean], axis=0)

    pack_one = (
        jnp.concatenate([w_qkv[0, :, 0], w_qkv[0, :, 1]], axis=1),
        jnp.concatenate([w_qkv[0, :, 2], w_out[0].T], axis=1),
    )
    pack_two = (w_up[0], w_down[0])
    tokens = take_tokens(layer_input)
    own_parts = []
    for first_part, second_part in (pack_one, pack_two):
        arrived = move(jnp.where(on_first, second_part, first_part), other_core)
        own_parts.append(
            (
                jnp.where(on_first, first_part, arrived),
                jnp.where(on_first, arrived, second_part),
            )
        )
    small = jnp.concatenate([ln1_gain[0], ln2_gain[0], b_down[0], b_up[0]])
    small = lax.all_gather(small, ("section", "tp")).reshape(2, 4, -1)
    relative = t ^ jnp.arange(4)
    gains_one, gains_two, biases_down = (small[:, 0, i * width : (i + 1) * width] for i in range(3))
    biases_up = jnp.take(small[:, :, 3 * width :], relative, axis=1)

    layers = []
    previous = None
    for layer in range(2):
        gathered = []
        for part in range(2):
            own = own_parts[part][layer]
            if previous is not None:
                own, previous = lax.optimization_barrier((own, previous))
            pieces = gather_plane(own)
            previous = pieces[3]
            mine = jnp.stack(pieces)
            other = move(mine, other_core)
            first_part = jnp.where(on_first, mine, other)
            second_part = jnp.where(on_first, other, mine)
            second_part = jnp.stack([second_part[i] for i in (0, 2, 1, 3)])
            gathered.append((first_part, second_part))
        (query_key, value_out), (up, down) = gathered

        def across(value):
            return value.transpose(1, 0, 2).reshape(width, 4 * columns)

        layers.append(
            (
                gains_one[layer],
                across(query_key[:, :, :columns]),
                across(query_key[:, :, columns:]),
                across(value_out[:, :, :columns]),
                across(value_out[:, :, columns:]),
                gains_two[layer],
                up,
                biases_up[layer],
                down,
                biases_down[layer],
            )
        )

    block = 2 * half + s
    lengths = doc_lengths.reshape(micros * rows, -1)
    lengths = lax.dynamic_index_in_dim(lengths, 4 * group + t, 0, keepdims=False)
    ends = jnp.cumsum(lengths)
    piece_pos = jnp.arange(PIECE)
    query_base = jnp.tile(block * PIECE + piece_pos, 2)
    key_base = jnp.concatenate([(block - 2 + i) * PIECE + piece_pos for i in (0, 1, 2, 2)])
    query_noisy = jnp.arange(2 * PIECE) < PIECE
    key_noisy = jnp.arange(4 * PIECE) >= 3 * PIECE

    def docs_of(base):
        return jnp.sum((base[:, None] >= ends[None, :]).astype(jnp.int32), axis=-1)

    query_block, key_block = query_base[:, None] // BLOCK, key_base[None, :] // BLOCK
    query_kind, key_kind = query_noisy[:, None], key_noisy[None, :]
    mask = (
        (query_kind & key_kind & (query_block == key_block))
        | (query_kind & ~key_kind & (key_block < query_block))
        | (~query_kind & ~key_kind & (key_block <= query_block))
    )
    mask = mask & (docs_of(query_base)[:, None] == docs_of(key_base)[None, :])
    mask = mask & (key_base >= 0)[None, :]
    frequency = 10000.0 ** (-jnp.arange(HDIM // 2).astype(jnp.float32) * 2.0 / HDIM)
    angles = query_base.astype(jnp.float32)[:, None, None] * frequency[None, None, :]
    cosine, sine_table = jnp.cos(angles), jnp.sin(angles)
    is_last = block == 3

    def forward(inputs, weights):
        gain_one, w_q, w_k, w_v, w_ot, gain_two, up, bias_up, down, bias_down = weights
        normed = layer_norm(inputs, gain_one).astype(jnp.bfloat16)

        def project(weight):
            return jnp.dot(normed, weight, preferred_element_type=jnp.float32)

        def per_head(value):
            return value.reshape(2 * PIECE, heads, HDIM)

        queries = rotate(per_head(project(w_q)), cosine, sine_table).astype(jnp.bfloat16)
        keys = rotate(per_head(project(w_k)), cosine, sine_table).astype(jnp.bfloat16)
        values = per_head(project(w_v)).astype(jnp.bfloat16)
        clean = jnp.concatenate(
            [keys[PIECE:].reshape(PIECE, -1), values[PIECE:].reshape(PIECE, -1)], axis=1
        )
        near, far = share_keys(clean, is_last)

        def assemble(own, at):
            parts = [
                far[:, at : at + width].reshape(PIECE, heads, HDIM),
                near[:, at : at + width].reshape(PIECE, heads, HDIM),
                own[PIECE:],
                own[:PIECE],
            ]
            return jnp.concatenate(parts, axis=0)

        keys_all, values_all = assemble(keys, 0), assemble(values, width)
        scores = (
            jnp.einsum("qhd,khd->hqk", queries, keys_all, preferred_element_type=jnp.float32)
            * 0.125
        )
        scores = jnp.where(mask[None], scores, -1e30)
        probs = jax.nn.softmax(scores, axis=-1)
        attended = jnp.einsum(
            "hqk,khd->qhd",
            probs.astype(jnp.bfloat16),
            values_all,
            preferred_element_type=jnp.float32,
        )
        attended = attended.astype(jnp.bfloat16).reshape(2 * PIECE, -1)
        middle = inputs + jnp.einsum(
            "pe,de->pd", attended, w_ot, preferred_element_type=jnp.float32
        )
        normed_two = layer_norm(middle, gain_two).astype(jnp.bfloat16)
        hidden_pre = (
            jnp.einsum("pd,rdf->rpf", normed_two, up, preferred_element_type=jnp.float32)
            + bias_up[:, None]
        )
        activated = gelu_tanh(hidden_pre).astype(jnp.bfloat16)
        result = (
            middle
            + jnp.einsum("rpf,rfd->pd", activated, down, preferred_element_type=jnp.float32)
            + bias_down
        )
        kept = (inputs, normed, queries, keys_all, values_all, probs, attended, middle)
        return result, kept + (normed_two, hidden_pre, activated)

    def backward(grad_out, weights, kept):
        gain_one, w_q, w_k, w_v, w_ot, gain_two, up, bias_up, down, bias_down = weights
        inputs, normed, queries, keys_all, values_all, probs, attended, middle = kept[:8]
        normed_two, hidden_pre, activated = kept[8:]
        grad_low = grad_out.astype(jnp.bfloat16)
        grad_b_down = jnp.sum(grad_out, axis=0)
        grad_down = jnp.einsum("rpf,pd->rfd", activated, grad_low)
        grad_act = jnp.einsum("pd,rfd->rpf", grad_low, down, preferred_element_type=jnp.float32)
        grad_pre = jax.vjp(gelu_tanh, hidden_pre)[1](grad_act)[0].astype(jnp.bfloat16)
        grad_b_up = jnp.sum(grad_pre, axis=1, dtype=jnp.float32)
        grad_up = jnp.einsum("pd,rpf->rdf", normed_two, grad_pre)
        grad_normed_two = jnp.einsum(
            "rpf,rdf->pd", grad_pre, up, preferred_element_type=jnp.float32
        )
        grad_norm, grad_gain_two = jax.vjp(layer_norm, middle, gain_two)[1](grad_normed_two)
        grad_middle = grad_out + grad_norm
        middle_low = grad_middle.astype(jnp.bfloat16)
        grad_ot = jnp.einsum("pd,pe->de", middle_low, attended)
        grad_att = jnp.dot(middle_low, w_ot, preferred_element_type=jnp.float32)
        grad_att = grad_att.astype(jnp.bfloat16).reshape(2 * PIECE, heads, HDIM)
        grad_probs = jnp.einsum(
            "qhd,khd->hqk", grad_att, values_all, preferred_element_type=jnp.float32
        )
        row_delta = jnp.sum(grad_probs * probs, axis=-1, keepdims=True)
        grad_scores = (probs * (grad_probs - row_delta)).astype(jnp.bfloat16)
        grad_queries = (
            jnp.einsum("hqk,khd->qhd", grad_scores, keys_all, preferred_element_type=jnp.float32)
            * 0.125
        )
        part_keys = (
            jnp.einsum("hqk,qhd->khd", grad_scores, queries, preferred_element_type=jnp.float32)
            * 0.125
        )
        part_values = jnp.einsum(
            "hqk,qhd->khd",
            probs.astype(jnp.bfloat16),
            grad_att,
            preferred_element_type=jnp.float32,
        )
        parts = jnp.concatenate(
            [part_keys.reshape(4 * PIECE, -1), part_values.reshape(4 * PIECE, -1)], axis=1
        )
        returned = return_keys(parts[PIECE : 2 * PIECE], parts[:PIECE])
        own = jnp.concatenate([parts[3 * PIECE :], parts[2 * PIECE : 3 * PIECE] + returned], axis=0)
        own = own.astype(jnp.bfloat16)

        def unrotate(value):
            shaped = value.astype(jnp.bfloat16).reshape(2 * PIECE, heads, HDIM)
            raw = rotate(shaped.astype(jnp.float32), cosine, -sine_table)
            return raw.astype(jnp.bfloat16).reshape(2 * PIECE, -1)

        raw_q = unrotate(grad_queries)
        raw_k = unrotate(own[:, :width])
        raw_v = own[:, width:]
        grad_q, grad_k, grad_v = (
            jnp.einsum("pd,pf->df", normed, raw) for raw in (raw_q, raw_k, raw_v)
        )
        grad_normed = sum(
            jnp.einsum("pf,df->pd", raw, weight, preferred_element_type=jnp.float32)
            for raw, weight in ((raw_q, w_q), (raw_k, w_k), (raw_v, w_v))
        )
        grad_norm_one, grad_gain_one = jax.vjp(layer_norm, inputs, gain_one)[1](grad_normed)
        grad_inputs = grad_middle + grad_norm_one

        def apart(value):
            return value.reshape(width, 4, columns).transpose(1, 0, 2)

        packs = (
            (
                jnp.concatenate([apart(grad_q), apart(grad_k)], axis=2),
                jnp.concatenate([apart(grad_v), apart(grad_ot)], axis=2),
            ),
            (grad_up, grad_down),
        )
        return grad_inputs, packs, (grad_gain_one, grad_gain_two, grad_b_down, grad_b_up)

    def give_out(value_low):
        noisy, clean = value_low[:PIECE], value_low[PIECE:]
        arrived = move(jnp.where(group == 0, clean, noisy), far_plane)
        keep = jnp.where(group == 0, noisy, clean)
        pieces = jnp.where(
            group == 0, jnp.stack([keep, arrived]), jnp.stack([arrived, keep])
        )
        return jnp.stack(gather_plane(pieces))

    def place_out(first, second):
        arrived = move(jnp.where(on_first, second, first), other_core)
        mine = jnp.where(on_first, first, second)
        zero_side = jnp.where(on_first, mine, arrived)
        one_side = jnp.where(on_first, arrived, mine)
        one_side = jnp.stack([one_side[i] for i in (0, 2, 1, 3)])
        both = jnp.stack([zero_side, one_side], axis=2)
        both = jnp.where(t % 2 == 1, jnp.stack([both[i] for i in (1, 0, 3, 2)]), both)
        both = jnp.where(t // 2 == 1, jnp.stack([both[i] for i in (2, 3, 0, 1)]), both)
        both = both.transpose(1, 0, 2, 3, 4)
        return both.reshape(1, micros, rows, width_pos, width)

    def reduce_packs(packs):
        reduced = []
        for first_part, second_part in packs:
            second_part = jnp.stack([second_part[i] for i in (0, 2, 1, 3)])
            arrived = move(jnp.where(on_first, second_part, first_part), other_core)
            mine = jnp.where(on_first, first_part, second_part)
            mine = (mine.astype(jnp.float32) + arrived.astype(jnp.float32)).astype(jnp.bfloat16)
            reduced.append(sum_planes(scatter_plane([mine[i] for i in range(4)]), z))
        return reduced

    handed, kept_zero = forward(tokens.astype(jnp.float32), layers[0])
    handed_low = handed.astype(jnp.bfloat16)
    final, kept_one = forward(handed_low.astype(jnp.float32), layers[1])
    final_low = final.astype(jnp.bfloat16)
    seeded = take_tokens(cotangent).astype(jnp.float32)
    grad_one, packs_one, small_one = backward(seeded, layers[1], kept_one)
    grad_one_low = grad_one.astype(jnp.bfloat16)
    layer_out = place_out(give_out(handed_low), give_out(final_low))
    grad_zero, packs_zero, small_zero = backward(
        grad_one_low.astype(jnp.float32), layers[0], kept_zero
    )
    input_grad = place_out(give_out(grad_zero.astype(jnp.bfloat16)), give_out(grad_one_low))

    sums = []
    for layer_small in (small_zero, small_one):
        grad_b_up = jnp.take(layer_small[3], relative, axis=0)
        sums.append(jnp.concatenate([layer_small[0], layer_small[1], layer_small[2], grad_b_up.reshape(-1)]))
    sums = lax.psum(jnp.stack(sums), ("section", "tp", "seq"))
    sums = lax.dynamic_index_in_dim(sums, s, 0, keepdims=False)
    small_out = [sums[i * width : (i + 1) * width][None] for i in range(3)]
    grad_b_up = lax.dynamic_slice_in_dim(sums[3 * width :], t * shard, shard, 0)[None]

    finals = []
    for mine_zero, mine_one in zip(reduce_packs(packs_zero), reduce_packs(packs_one)):
        arrived = move(jnp.where(on_first, mine_one, mine_zero), other_core)
        first_part = jnp.where(on_first, mine_zero, arrived).astype(jnp.float32)
        second_part = jnp.where(on_first, arrived, mine_one).astype(jnp.float32)
        finals.append((first_part, second_part))
    (query_key, value_out), (grad_up, grad_down) = finals
    grad_qkv = jnp.stack(
        [query_key[:, :columns], query_key[:, columns:], value_out[:, :columns]], axis=1
    )
    return (
        layer_out,
        input_grad,
        small_out[0],
        grad_qkv[None],
        value_out[:, columns:].T[None],
        small_out[1],
        grad_up[None],
        grad_b_up,
        grad_down[None],
        small_out[2],
    )


def solution(mesh):
    sizes = tuple(mesh.shape[name] for name in ("section", "tp", "seq"))
    local = spread if sizes == (2, 4, 4) else pipelined
    return jax.shard_map(
        local,
        mesh=mesh,
        in_specs=(
            P(None, None, "seq", None),
            P(None, None, "seq", None),
            P(),
            P("section", None),
            P("section", None, None, "tp"),
            P("section", "tp", None),
            P("section", None),
            P("section", None, "tp"),
            P("section", "tp"),
            P("section", "tp", None),
            P("section", None),
        ),
        out_specs=(
            P("section", None, None, "seq", None),
            P("section", None, None, "seq", None),
            P("section", None),
            P("section", None, None, "tp"),
            P("section", "tp", None),
            P("section", None),
            P("section", None, "tp"),
            P("section", "tp"),
            P("section", "tp", None),
            P("section", None),
        ),
        check_vma=False,
    )
```

```python
import jax
import jax.numpy as jnp
from jax import lax
from jax.experimental import pallas as pl
from jax.experimental.pallas import tpu as pltpu
from jax.sharding import PartitionSpec as P

HDIM = 64
BLOCK = 16
HALF = 1024


def from_behind(value, axis, by):
    size = lax.axis_size(axis)
    pairs = [(i, i + by) for i in range(size) if 0 <= i + by < size]
    return lax.ppermute(value, axis, pairs)


def layer_norm(values, gain):
    center = values - jnp.mean(values, axis=-1, keepdims=True)
    spread = jnp.mean(center * center, axis=-1, keepdims=True)
    return center * lax.rsqrt(spread + 1e-05) * gain


def rotate(values, cosine, sine_table):
    middle = values.shape[-1] // 2
    first_half = values[..., :middle]
    second_half = values[..., middle:]
    return jnp.concatenate(
        [
            first_half * cosine - second_half * sine_table,
            second_half * cosine + first_half * sine_table,
        ],
        axis=-1,
    )


def rotary_tables(positions):
    frequency = 10000.0 ** (-jnp.arange(HDIM // 2).astype(jnp.float32) * 2.0 / HDIM)
    angles = (positions % HALF).astype(jnp.float32)[:, None, None] * frequency[None, None, :]
    return (jnp.cos(angles), jnp.sin(angles))


def allowed(query_pos, query_doc, key_pos, key_doc):
    query_noisy = query_pos < HALF
    key_noisy = key_pos < HALF
    query_block = query_pos % HALF // BLOCK
    key_block = key_pos % HALF // BLOCK
    within = query_noisy & key_noisy & (query_block == key_block)
    earlier = query_noisy & ~key_noisy & (key_block < query_block)
    causal = ~query_noisy & ~key_noisy & (key_block <= query_block)
    return (within | earlier | causal) & (query_doc == key_doc)


def document_ids(doc_lengths):
    doc_ends = jnp.cumsum(doc_lengths, axis=-1)
    base_pos = jnp.arange(2 * HALF) % HALF
    return jnp.sum((base_pos[:, None] >= doc_ends[..., None, :]).astype(jnp.int32), axis=-1)


def gelu_tanh(values):
    return jax.nn.gelu(values, approximate=True)


def keep_slot(storage, value, slot_index, is_active):
    current = lax.dynamic_index_in_dim(storage, slot_index, 0, keepdims=False)
    return lax.dynamic_update_index_in_dim(
        storage, jnp.where(is_active, value, current), slot_index, 0
    )


def local_queries(inputs, ln_one, w_mix, tables):
    cosine, sine_table, query_pos = tables
    row_count, pos_count = (inputs.shape[0], inputs.shape[1])
    normed = layer_norm(inputs, ln_one).astype(jnp.bfloat16)
    mixed = jnp.einsum("rpd,dcf->rpcf", normed, w_mix, preferred_element_type=jnp.float32)
    shaped = mixed.reshape(row_count, pos_count, 3, -1, HDIM)
    queries = rotate(shaped[:, :, 0], cosine, sine_table).astype(jnp.bfloat16)
    keys_own = rotate(shaped[:, :, 1], cosine, sine_table).astype(jnp.bfloat16)
    values_own = shaped[:, :, 2].astype(jnp.bfloat16)
    return (normed, queries, keys_own, values_own)


def masked_scores(queries, keys_heads, query_pos, docs_all):
    pos_count = queries.shape[1]
    query_docs = lax.dynamic_slice_in_dim(docs_all, query_pos[0], pos_count, 1)
    key_pos = jnp.arange(keys_heads.shape[1])
    key_mask = allowed(
        query_pos[None, :, None],
        query_docs[:, :, None],
        key_pos[None, None, :],
        docs_all[:, None, :],
    )
    scores = (
        jnp.einsum("rqhd,rkhd->rhqk", queries, keys_heads, preferred_element_type=jnp.float32)
        * 0.125
    )
    return jnp.where(key_mask[:, None], scores, -1e30)


def forward_step(inputs, weights, tables, docs_all):
    ln_one, w_mix, w_proj, ln_two, w_first, b_first, w_second, b_second = weights
    row_count, pos_count = (inputs.shape[0], inputs.shape[1])
    normed, queries, keys_own, values_own = local_queries(inputs, ln_one, w_mix, tables)
    local_width = w_mix.shape[-1]
    keys_all, values_all = (
        lax.all_gather(
            keys_own.reshape(row_count, pos_count, local_width), "seq", axis=1, tiled=True
        ),
        lax.all_gather(
            values_own.reshape(row_count, pos_count, local_width), "seq", axis=1, tiled=True
        ),
    )
    keys_heads = keys_all.reshape(row_count, keys_all.shape[1], -1, HDIM)
    values_heads = values_all.reshape(row_count, values_all.shape[1], -1, HDIM)
    softmax_out = jax.nn.softmax(
        masked_scores(queries, keys_heads, tables[2], docs_all), axis=-1
    ).astype(jnp.bfloat16)
    attended = jnp.einsum(
        "rhqk,rkhd->rqhd", softmax_out, values_heads, preferred_element_type=jnp.float32
    )
    attended = attended.astype(jnp.bfloat16).reshape(row_count, pos_count, local_width)
    middle = inputs + lax.psum(
        jnp.einsum("rpe,ed->rpd", attended, w_proj, preferred_element_type=jnp.float32).astype(
            jnp.bfloat16
        ),
        "tp",
    ).astype(jnp.float32)
    normed_two = layer_norm(middle, ln_two).astype(jnp.bfloat16)
    hidden_pre = (
        jnp.einsum("rpd,df->rpf", normed_two, w_first, preferred_element_type=jnp.float32) + b_first
    )
    activated = gelu_tanh(hidden_pre).astype(jnp.bfloat16)
    second_terms = jnp.einsum(
        "rpf,fd->rpd", activated, w_second, preferred_element_type=jnp.float32
    )
    result = (
        middle + lax.psum(second_terms.astype(jnp.bfloat16), "tp").astype(jnp.float32) + b_second
    )
    return (result, middle, keys_all, values_all)


def backward_step(inputs, middle, grad_out, weights, tables, docs_all):
    ln_one, w_mix, w_proj, ln_two, w_first, b_first, w_second, b_second = weights
    cosine, sine_table, query_pos = tables
    row_count, pos_count = (inputs.shape[0], inputs.shape[1])
    local_width = w_mix.shape[-1]
    head_count = local_width // HDIM
    normed, queries, keys_own, values_own = local_queries(inputs, ln_one, w_mix, tables)
    keys_all, values_all = (
        lax.all_gather(
            keys_own.reshape(row_count, pos_count, local_width), "seq", axis=1, tiled=True
        ),
        lax.all_gather(
            values_own.reshape(row_count, pos_count, local_width), "seq", axis=1, tiled=True
        ),
    )
    keys_heads = keys_all.reshape(row_count, keys_all.shape[1], head_count, HDIM)
    values_heads = values_all.reshape(row_count, values_all.shape[1], head_count, HDIM)
    scores = masked_scores(queries, keys_heads, query_pos, docs_all)
    softmax_out = jax.nn.softmax(scores, axis=-1)
    probs_low = softmax_out.astype(jnp.bfloat16)
    attended = jnp.einsum(
        "rhqk,rkhd->rqhd", probs_low, values_heads, preferred_element_type=jnp.float32
    )
    attended = attended.astype(jnp.bfloat16).reshape(row_count, pos_count, local_width)
    normed_two = layer_norm(middle, ln_two).astype(jnp.bfloat16)
    hidden_pre = (
        jnp.einsum("rpd,df->rpf", normed_two, w_first, preferred_element_type=jnp.float32) + b_first
    )
    activated = gelu_tanh(hidden_pre).astype(jnp.bfloat16)
    grad_low = grad_out.astype(jnp.bfloat16)
    grad_b_second = jnp.sum(grad_out, axis=(0, 1))
    grad_w_second = jnp.einsum(
        "rpf,rpd->fd", activated, grad_low, preferred_element_type=jnp.float32
    )
    grad_act = jnp.einsum("rpd,fd->rpf", grad_low, w_second, preferred_element_type=jnp.float32)
    unused_value, gelu_back = jax.vjp(gelu_tanh, hidden_pre)
    grad_pre = gelu_back(grad_act)[0].astype(jnp.bfloat16)
    grad_b_first = jnp.sum(grad_pre, axis=(0, 1), dtype=jnp.float32)
    grad_w_first = jnp.einsum(
        "rpd,rpf->df", normed_two, grad_pre, preferred_element_type=jnp.float32
    )
    grad_normed_two = lax.psum(
        jnp.einsum("rpf,df->rpd", grad_pre, w_first, preferred_element_type=jnp.float32).astype(
            jnp.bfloat16
        ),
        "tp",
    ).astype(jnp.float32)
    unused_norm, second_back = jax.vjp(layer_norm, middle, ln_two)
    grad_middle_norm, grad_ln_two = second_back(grad_normed_two)
    grad_middle = grad_out + grad_middle_norm
    middle_low = grad_middle.astype(jnp.bfloat16)
    grad_w_proj = jnp.einsum(
        "rpe,rpd->ed", attended, middle_low, preferred_element_type=jnp.float32
    )
    grad_att = jnp.einsum("rpd,ed->rpe", middle_low, w_proj, preferred_element_type=jnp.float32)
    grad_att = grad_att.astype(jnp.bfloat16).reshape(row_count, pos_count, head_count, HDIM)
    grad_probs = jnp.einsum(
        "rqhd,rkhd->rhqk", grad_att, values_heads, preferred_element_type=jnp.float32
    )
    row_delta = jnp.sum(grad_probs * softmax_out, axis=-1, keepdims=True)
    grad_scores = (softmax_out * (grad_probs - row_delta)).astype(jnp.bfloat16)
    grad_queries = (
        jnp.einsum("rhqk,rkhd->rqhd", grad_scores, keys_heads, preferred_element_type=jnp.float32)
        * 0.125
    )
    full_len = keys_all.shape[1]
    part_keys = (
        jnp.einsum("rhqk,rqhd->rkhd", grad_scores, queries, preferred_element_type=jnp.float32)
        * 0.125
    )
    part_values = jnp.einsum(
        "rhqk,rqhd->rkhd", probs_low, grad_att, preferred_element_type=jnp.float32
    )
    grad_keys, grad_values = (
        lax.psum_scatter(
            part_keys.reshape(row_count, full_len, local_width).astype(jnp.bfloat16),
            "seq",
            scatter_dimension=1,
            tiled=True,
        ).astype(jnp.float32),
        lax.psum_scatter(
            part_values.reshape(row_count, full_len, local_width).astype(jnp.bfloat16),
            "seq",
            scatter_dimension=1,
            tiled=True,
        ).astype(jnp.float32),
    )
    grad_query_raw = rotate(grad_queries.astype(jnp.bfloat16), cosine, -sine_table)
    grad_key_raw = rotate(
        grad_keys.astype(jnp.bfloat16).reshape(row_count, pos_count, head_count, HDIM),
        cosine,
        -sine_table,
    )
    grad_mixed = jnp.stack(
        [
            grad_query_raw.reshape(row_count, pos_count, local_width).astype(jnp.bfloat16),
            grad_key_raw.reshape(row_count, pos_count, local_width).astype(jnp.bfloat16),
            grad_values.astype(jnp.bfloat16),
        ],
        axis=2,
    )
    grad_w_mix = jnp.einsum("rpd,rpcf->dcf", normed, grad_mixed, preferred_element_type=jnp.float32)
    grad_normed = lax.psum(
        jnp.einsum("rpcf,dcf->rpd", grad_mixed, w_mix, preferred_element_type=jnp.float32).astype(
            jnp.bfloat16
        ),
        "tp",
    ).astype(jnp.float32)
    unused_first, first_back = jax.vjp(layer_norm, inputs, ln_one)
    grad_in_norm, grad_ln_one = first_back(grad_normed)
    grad_inputs = grad_middle + grad_in_norm
    return (
        grad_inputs,
        (
            grad_ln_one,
            grad_w_mix,
            grad_w_proj,
            grad_ln_two,
            grad_w_first,
            grad_b_first,
            grad_w_second,
            grad_b_second,
        ),
    )


def pipelined(
    layer_input,
    cotangent,
    doc_lengths,
    ln1_gain,
    w_qkv,
    w_out,
    ln2_gain,
    w_up,
    b_up,
    w_down,
    b_down,
):
    weights = tuple(
        (weight[0] for weight in (ln1_gain, w_qkv, w_out, ln2_gain, w_up, b_up, w_down, b_down))
    )
    micros, row_count, pos_count, width_model = layer_input.shape
    sections = lax.axis_size("section")
    section_index = lax.axis_index("section")
    first_pos = lax.axis_index("seq") * pos_count
    query_pos = first_pos + jnp.arange(pos_count)
    cosine, sine_table = rotary_tables(query_pos)
    tables = (cosine, sine_table, query_pos)
    docs_every = document_ids(doc_lengths)
    kept_inputs = jnp.zeros((micros, row_count, pos_count, width_model), jnp.float32)
    kept_middle = jnp.zeros((micros, row_count, pos_count, width_model), jnp.float32)
    layer_out = jnp.zeros(layer_input.shape, jnp.bfloat16)
    arrived = jnp.zeros((row_count, pos_count, width_model), jnp.bfloat16)
    moments = micros + sections - 1
    for moment in range(moments):
        offset = moment - section_index
        micro_index = jnp.clip(offset, 0, micros - 1)
        is_active = (offset >= 0) & (offset < micros)
        own_input = layer_input[min(moment, micros - 1)]
        inputs = jnp.where(section_index == 0, own_input, arrived).astype(jnp.float32)
        result, middle, keys_all, values_all = forward_step(
            inputs, weights, tables, docs_every[micro_index]
        )
        kept_inputs = keep_slot(kept_inputs, inputs, micro_index, is_active)
        kept_middle = keep_slot(kept_middle, middle, micro_index, is_active)
        result_low = result.astype(jnp.bfloat16)
        layer_out = keep_slot(layer_out, result_low, micro_index, is_active)
        if moment < moments - 1:
            arrived = from_behind(result_low, "section", 1)
    grad_totals = tuple((jnp.zeros(weight.shape, jnp.float32) for weight in weights))
    input_grad = jnp.zeros(layer_input.shape, jnp.bfloat16)
    returned = jnp.zeros((row_count, pos_count, width_model), jnp.bfloat16)
    for moment in range(moments):
        offset = moment - (sections - 1 - section_index)
        micro_index = jnp.clip(offset, 0, micros - 1)
        is_active = (offset >= 0) & (offset < micros)
        incoming = jnp.where(
            section_index == sections - 1, cotangent[min(moment, micros - 1)], returned
        ).astype(jnp.float32)
        incoming = jnp.where(is_active, incoming, 0.0)
        grad_inputs, grad_parts = backward_step(
            kept_inputs[micro_index],
            kept_middle[micro_index],
            incoming,
            weights,
            tables,
            docs_every[micro_index],
        )
        grad_totals = tuple((total + piece for total, piece in zip(grad_totals, grad_parts)))
        grad_sent = grad_inputs.astype(jnp.bfloat16)
        input_grad = keep_slot(input_grad, grad_sent, micro_index, is_active)
        if moment < moments - 1:
            returned = from_behind(grad_sent, "section", -1)
    (
        grad_ln_one,
        grad_w_mix,
        grad_w_proj,
        grad_ln_two,
        grad_w_first,
        grad_b_first,
        grad_w_second,
        grad_b_second,
    ) = grad_totals
    summed = (
        lax.psum(grad_ln_one.astype(jnp.bfloat16), "seq").astype(jnp.float32),
        lax.psum(grad_w_mix.astype(jnp.bfloat16), "seq").astype(jnp.float32),
        lax.psum(grad_w_proj.astype(jnp.bfloat16), "seq").astype(jnp.float32),
        lax.psum(grad_ln_two.astype(jnp.bfloat16), "seq").astype(jnp.float32),
        lax.psum(grad_w_first.astype(jnp.bfloat16), "seq").astype(jnp.float32),
        lax.psum(grad_b_first.astype(jnp.bfloat16), "seq").astype(jnp.float32),
        lax.psum(grad_w_second.astype(jnp.bfloat16), "seq").astype(jnp.float32),
        lax.psum(grad_b_second.astype(jnp.bfloat16), "seq").astype(jnp.float32),
    )
    return (
        layer_out[None],
        input_grad[None],
        summed[0][None],
        summed[1][None],
        summed[2][None],
        summed[3][None],
        summed[4][None],
        summed[5][None],
        summed[6][None],
        summed[7][None],
    )


PIECE = 256
LANES = 256
MESH = pl.DeviceIdType.MESH
HBM = pl.BlockSpec(memory_space=pl.ANY)
VMEM = pl.BlockSpec(memory_space=pltpu.VMEM)


def dot_nn(left, right):
    return lax.dot_general(left, right, (((1,), (0,)), ((), ())), preferred_element_type=jnp.float32)


def dot_nt(left, right):
    return lax.dot_general(left, right, (((1,), (1,)), ((), ())), preferred_element_type=jnp.float32)


def dot_tn(left, right):
    return lax.dot_general(left, right, (((0,), (0,)), ((), ())), preferred_element_type=jnp.float32)


class Place:
    def __init__(self):
        self.s, self.t, self.z = (lax.axis_index(name) for name in ("section", "tp", "seq"))
        self.core = 1 - self.s
        self.half, self.group = self.z % 2, self.z // 2
        beside_x = self.t + 1 - 2 * (self.t % 2)
        beside_y = (self.t + 2) % 4
        self.hop_one = beside_x * (1 - self.s) + beside_y * self.s
        self.hop_two = beside_y * (1 - self.s) + beside_x * self.s
        self.rel_one, self.rel_two = 1 + self.s, 2 - self.s
        self.far = (self.z + 2) % 4
        self.twin = self.z + 1 - 2 * self.half

    def on(self, section=None, tp=None, seq=None):
        return (
            self.s if section is None else section,
            self.t if tp is None else tp,
            self.z if seq is None else seq,
        )

    def meet(self, partners):
        barrier = pltpu.get_barrier_semaphore()
        for partner in partners:
            pl.semaphore_signal(barrier, inc=1, device_id=partner, device_id_type=MESH)
        pl.semaphore_wait(barrier, len(partners))


def remote(source, target, send, receive, device):
    return pltpu.make_async_remote_copy(
        src_ref=source,
        dst_ref=target,
        send_sem=send,
        recv_sem=receive,
        device_id=device,
        device_id_type=MESH,
    )


def normalize(values):
    center = values - jnp.mean(values, axis=-1, keepdims=True)
    spread = jnp.mean(center * center, axis=-1, keepdims=True)
    scale = lax.rsqrt(spread + 1e-05)
    return center * scale, scale


def turn(values, cosine, sine_table):
    width = values.shape[-1]
    times = width // cosine.shape[-1]
    lane = lax.broadcasted_iota(jnp.int32, values.shape, 1) % HDIM
    ahead = pltpu.roll(values, width - HDIM // 2, 1)
    behind = pltpu.roll(values, HDIM // 2, 1)
    swapped = jnp.where(lane < HDIM // 2, ahead, behind)
    return values * jnp.tile(cosine, (1, times)) + swapped * jnp.tile(sine_table, (1, times))


def gelu(values):
    inner = 0.7978845608028654 * (values + 0.044715 * values * values * values)
    return 0.5 * values * (1.0 + jnp.tanh(inner))


def head_mask(head, scale):
    lane = lax.broadcasted_iota(jnp.int32, (1, LANES), 1)
    inside = (lane >= head * HDIM) & (lane < (head + 1) * HDIM)
    return jnp.where(inside, jnp.float32(scale), jnp.float32(0.0))


def attention_block(q_ref, keys, values, bias):
    def one(head, total):
        query = q_ref[...] * head_mask(head, 0.125).astype(jnp.bfloat16)
        scores = dot_nt(query, keys[...]) + bias[...]
        raised = jnp.exp(scores - jnp.max(scores, axis=-1, keepdims=True))
        share = 1.0 / jnp.sum(raised, axis=-1, keepdims=True)
        found = dot_nn(raised.astype(jnp.bfloat16), values[...])
        return total + found * share * head_mask(head, 1.0)

    zero = jnp.zeros((PIECE, LANES), jnp.float32)
    return lax.fori_loop(0, LANES // HDIM, one, zero).astype(jnp.bfloat16)


class Weights:
    def __init__(self, place, own_a, own_b, full_a, full_b, sems):
        self.place, self.own, self.full = place, (own_a, own_b), (full_a, full_b)
        (
            self.local,
            self.own_send,
            self.own_recv,
            self.hop_send,
            self.hop_recv,
            self.chip_send,
            self.chip_recv,
        ) = sems

    def source(self, chunk, pack):
        if chunk == 0:
            return self.own[0].at[pack]
        return self.own[1].at[pack, pl.ds((chunk - 1) * 384, 384)]

    def piece(self, layer, chunk, pack, rel):
        if chunk == 0:
            return self.full[0].at[layer, pack, :, pl.ds(pl.multiple_of(rel * 192, 64), 192)]
        start = pl.multiple_of(rel * 768 + (chunk - 1) * 384, 128)
        return self.full[1].at[layer, pack, pl.ds(start, 384)]

    def own_copies(self, chunk, pack):
        s = self.place.s
        here = pltpu.make_async_copy(
            self.source(chunk, pack), self.piece(s, chunk, pack, 0), self.local.at[chunk, pack]
        )
        there = remote(
            self.source(chunk, pack),
            self.piece(s, chunk, pack, 0),
            self.own_send.at[chunk, pack],
            self.own_recv.at[chunk, pack],
            self.place.on(section=self.place.core),
        )
        return here, there

    def start_own(self, chunk):
        for pack in range(2):
            for copy in self.own_copies(chunk, pack):
                copy.start()

    def wait_own(self, layer, chunk):
        for pack in range(2):
            here, there = self.own_copies(chunk, pack)

            @pl.when(self.place.s == layer)
            def _():
                here.wait()

            @pl.when(self.place.s != layer)
            def _():
                there.wait_recv()

    def hops(self, layer, chunk):
        place = self.place
        own = self.piece(layer, chunk, place.s, 0)
        first = self.piece(layer, chunk, place.s, place.rel_one)
        second = self.piece(layer, chunk, place.s, place.rel_two)
        third = self.piece(layer, chunk, place.s, 3)
        moves = ((own, first, place.hop_one), (own, second, place.hop_two), (first, third, place.hop_two))
        return [
            remote(
                source,
                target,
                self.hop_send.at[layer, chunk, i],
                self.hop_recv.at[layer, chunk, i],
                place.on(tp=column),
            )
            for i, (source, target, column) in enumerate(moves)
        ]

    def chips(self, layer, chunk):
        place = self.place
        return [
            remote(
                self.piece(layer, chunk, place.s, rel),
                self.piece(layer, chunk, place.s, rel),
                self.chip_send.at[layer, chunk, i],
                self.chip_recv.at[layer, chunk, i],
                place.on(section=place.core),
            )
            for i, rel in enumerate((place.rel_one, place.rel_two, 3))
        ]

    def begin(self, layer, chunk):
        self.wait_own(layer, chunk)
        first, second, _ = self.hops(layer, chunk)
        first.start()
        second.start()

    def forward(self, layer, chunk):
        first, second, third = self.hops(layer, chunk)
        chips = self.chips(layer, chunk)
        first.wait_recv()
        third.start()
        chips[0].start()
        second.wait_recv()
        chips[1].start()

    def finish(self, layer, chunk):
        self.hops(layer, chunk)[2].wait_recv()
        self.chips(layer, chunk)[2].start()

    def need(self, layer, chunk):
        for copy in self.chips(layer, chunk):
            copy.wait_recv()

    def drain(self):
        for chunk in range(3):
            for pack in range(2):
                self.own_copies(chunk, pack)[1].wait_send()
            for layer in range(2):
                for copy in self.hops(layer, chunk) + self.chips(layer, chunk):
                    copy.wait_send()


class KeyShare:
    def __init__(self, place, kv, layer, sems):
        self.place, self.kv, self.layer = place, kv, layer
        self.near_send, self.near_recv, self.far_send, self.far_recv = sems
        s, odd = place.s, place.half == 1
        self.sends_near = (s == 0) | ~odd
        self.sends_far = (s == 0) & ~odd
        self.passes = (s == 0) & odd
        self.gets_near = (s == 1) | odd
        self.gets_far = odd

    def rows(self, start, part):
        lanes = pl.ds(part * LANES, LANES)
        return self.kv.at[self.layer, :, pl.ds(start, PIECE), lanes]

    def near(self, part):
        place = self.place
        return remote(
            self.rows(2 * PIECE, part),
            self.rows(PIECE, part),
            self.near_send.at[self.layer, part],
            self.near_recv.at[self.layer, part],
            place.on(section=place.core, seq=place.z + place.s * (1 - place.half)),
        )

    def far(self, part):
        place = self.place
        return remote(
            self.rows(2 * PIECE, part),
            self.rows(0, part),
            self.far_send.at[self.layer, part],
            self.far_recv.at[self.layer, part],
            place.on(seq=place.twin),
        )

    def last(self, part):
        place = self.place
        return remote(
            self.rows(PIECE, part),
            self.rows(0, part),
            self.far_send.at[self.layer, part],
            self.far_recv.at[self.layer, part],
            place.on(section=place.core),
        )

    def start(self, part):
        @pl.when(self.sends_near)
        def _():
            self.near(part).start()

        @pl.when(self.sends_far)
        def _():
            self.far(part).start()

    def arrive(self, part):
        @pl.when(self.gets_near)
        def _():
            self.near(part).wait_recv()

        @pl.when(self.passes)
        def _():
            self.last(part).start()

        @pl.when(self.gets_far)
        def _():
            self.far(part).wait_recv()

    def drain(self):
        for part in range(3):

            @pl.when(self.sends_near)
            def _():
                self.near(part).wait_send()

            @pl.when(self.sends_far)
            def _():
                self.far(part).wait_send()

            @pl.when(self.passes)
            def _():
                self.last(part).wait_send()


def forward_kernel(
    tokens,
    own_a,
    own_b,
    gains,
    biases_up,
    bias,
    cosine,
    sine_table,
    full_a_out,
    full_b_out,
    x_out,
    low_out,
    q_out,
    kv_out,
    att_out,
    mid_out,
    hid_out,
    full_a,
    full_b,
    low,
    x,
    normed,
    q,
    kv,
    att,
    mid,
    hid,
    *sems,
):
    weight_sems, key_sems, (token_sem, swap_send, swap_recv, save_sem) = sems[:7], sems[7:11], sems[11:]
    place = Place()
    weights = Weights(place, own_a, own_b, full_a, full_b, weight_sems)
    kv[:, :, : 2 * PIECE, :] = jnp.zeros((2, 2, 2 * PIECE, kv.shape[-1]), jnp.bfloat16)
    place.meet(
        [
            place.on(section=place.core),
            place.on(tp=place.hop_one),
            place.on(tp=place.hop_two),
            place.on(seq=place.far),
            place.on(seq=place.twin),
            place.on(section=place.core, seq=place.twin),
        ]
    )
    here = low.at[pl.ds(pl.multiple_of(place.group * PIECE, PIECE), PIECE)]
    columns = pl.ds(pl.multiple_of(place.s * PIECE, PIECE), PIECE)
    own_tokens = pltpu.make_async_copy(tokens.at[4 * place.group + place.t, columns], here, token_sem)
    swap = remote(
        tokens.at[4 * (1 - place.group) + place.t, columns],
        here,
        swap_send,
        swap_recv,
        place.on(seq=place.far),
    )
    own_tokens.start()
    swap.start()
    for chunk in range(3):
        weights.start_own(chunk)
    weights.begin(0, 0)
    weights.begin(0, 1)
    own_tokens.wait()
    swap.wait()
    x_save = pltpu.make_async_copy(low, x_out, save_sem.at[7])
    x_save.start()
    x[...] = low[...].astype(jnp.float32)

    def saves(layer):
        pairs = [
            (low, low_out.at[layer]),
            (q, q_out.at[layer]),
            (kv.at[layer], kv_out.at[layer]),
            (att, att_out.at[layer]),
            (mid, mid_out.at[layer]),
            (hid, hid_out.at[layer]),
        ]
        return [pltpu.make_async_copy(a, b, save_sem.at[i]) for i, (a, b) in enumerate(pairs)]

    def weight_saves(layer):
        return [
            pltpu.make_async_copy(full_a.at[layer], full_a_out.at[layer], save_sem.at[8 + 2 * layer]),
            pltpu.make_async_copy(full_b.at[layer], full_b_out.at[layer], save_sem.at[9 + 2 * layer]),
        ]

    for layer in range(2):
        share = KeyShare(place, kv, layer, key_sems)
        unit, _ = normalize(x[...])
        normed[...] = (unit * gains[layer, 0:1]).astype(jnp.bfloat16)
        if layer == 0:
            weights.forward(0, 0)
            weights.begin(0, 2)
            weights.finish(0, 0)
        else:
            weights.forward(1, 0)
            weights.begin(1, 2)
            weights.finish(1, 0)
            for copy in saves(0)[1:]:
                copy.wait()
        weights.need(layer, 0)
        for part in range(3):
            lanes = pl.ds(part * LANES, LANES)
            keep = normed[...]
            mixed = dot_nt(keep, full_a[layer, 0, 0, lanes, :])
            q[:, lanes] = turn(mixed, cosine[...], sine_table[...]).astype(jnp.bfloat16)
            mixed = dot_nt(keep, full_a[layer, 0, 1, lanes, :])
            mixed = turn(mixed, cosine[...], sine_table[...]).astype(jnp.bfloat16)
            kv[layer, 0, 2 * PIECE : 3 * PIECE, lanes] = mixed[PIECE:]
            kv[layer, 0, 3 * PIECE :, lanes] = mixed[:PIECE]
            mixed = dot_nt(keep, full_a[layer, 1, 0, lanes, :]).astype(jnp.bfloat16)
            kv[layer, 1, 2 * PIECE : 3 * PIECE, lanes] = mixed[PIECE:]
            kv[layer, 1, 3 * PIECE :, lanes] = mixed[:PIECE]
            share.start(part)
        if layer == 0:
            weights.forward(0, 1)
            weights.begin(1, 0)
        else:
            weights.forward(1, 1)
        for part in range(3):
            lanes = pl.ds(part * LANES, LANES)
            share.arrive(part)
            att[:PIECE, lanes] = attention_block(
                q.at[:PIECE, lanes],
                kv.at[layer, 0, :, lanes],
                kv.at[layer, 1, :, lanes],
                bias.at[:PIECE],
            )
            att[PIECE:, lanes] = attention_block(
                q.at[PIECE:, lanes],
                kv.at[layer, 0, : 3 * PIECE, lanes],
                kv.at[layer, 1, : 3 * PIECE, lanes],
                bias.at[PIECE:, : 3 * PIECE],
            )
            if part == 0:
                weights.finish(layer, 1)
            elif part == 1:
                weights.forward(layer, 2)
                if layer == 0:
                    weights.begin(1, 1)
            else:
                weights.finish(layer, 2)
        for copy in saves(layer)[1:4]:
            copy.start()

        def project(part, _):
            lanes = pl.ds(pl.multiple_of(part * LANES, LANES), LANES)
            mid[:, lanes] = x[:, lanes] + dot_nn(att[...], full_a[layer, 1, 1, :, lanes])
            return 0

        lax.fori_loop(0, 3, project, 0)
        unit, _ = normalize(mid[...])
        normed[...] = (unit * gains[layer, 1:2]).astype(jnp.bfloat16)
        x[...] = mid[...] + gains[layer, 2:3]
        saves(layer)[4].start()
        for part in range(2):
            weights.need(layer, part + 1)

            def feed(rel, _):
                start = pl.multiple_of(rel * 768 + part * 384, 128)
                units = pl.ds(start, 384)
                pre = dot_nt(normed[...], full_b[layer, 0, units, :]) + biases_up[layer, :, units]
                hid[:, units] = pre.astype(jnp.bfloat16)
                active = gelu(pre).astype(jnp.bfloat16)
                x[...] += dot_nn(active, full_b[layer, 1, units, :])
                return 0

            lax.fori_loop(0, 4, feed, 0)
        saves(layer)[5].start()
        if layer == 0:
            x_save.wait()
        else:
            saves(0)[0].wait()
        low[...] = x[...].astype(jnp.bfloat16)
        saves(layer)[0].start()
        x[...] = low[...].astype(jnp.float32)
        for copy in weight_saves(layer):
            copy.start()
    for copy in saves(1):
        copy.wait()
    for layer in range(2):
        for copy in weight_saves(layer):
            copy.wait()
        KeyShare(place, kv, layer, key_sems).drain()
    weights.drain()


def run_forward(tokens, own_a, own_b, gains, biases_up, bias, cosine, sine_table):
    shape = jax.ShapeDtypeStruct
    low_type, full_type = jnp.bfloat16, jnp.float32
    count = 2 * PIECE
    width = tokens.shape[-1]
    units = 4 * own_b.shape[1]
    dma = pltpu.SemaphoreType.DMA
    return pl.pallas_call(
        forward_kernel,
        name="forward_layers",
        out_shape=[
            shape((2, 2, 2, width, width), low_type),
            shape((2, 2, units, width), low_type),
            shape((count, width), low_type),
            shape((2, count, width), low_type),
            shape((2, count, width), low_type),
            shape((2, 2, 4 * PIECE, width), low_type),
            shape((2, count, width), low_type),
            shape((2, count, width), full_type),
            shape((2, count, units), low_type),
        ],
        in_specs=[HBM] * 3 + [VMEM] * 5,
        out_specs=[HBM] * 9,
        scratch_shapes=[
            pltpu.VMEM((2, 2, 2, width, width), low_type),
            pltpu.VMEM((2, 2, units, width), low_type),
            pltpu.VMEM((count, width), low_type),
            pltpu.VMEM((count, width), full_type),
            pltpu.VMEM((count, width), low_type),
            pltpu.VMEM((count, width), low_type),
            pltpu.VMEM((2, 2, 4 * PIECE, width), low_type),
            pltpu.VMEM((count, width), low_type),
            pltpu.VMEM((count, width), full_type),
            pltpu.VMEM((count, units), low_type),
            dma((3, 2)),
            dma((3, 2)),
            dma((3, 2)),
            dma((2, 3, 3)),
            dma((2, 3, 3)),
            dma((2, 3, 3)),
            dma((2, 3, 3)),
            dma((2, 3)),
            dma((2, 3)),
            dma((2, 3)),
            dma((2, 3)),
            dma,
            dma,
            dma,
            dma((12,)),
        ],
        compiler_params=pltpu.CompilerParams(
            collective_id=1, has_side_effects=True, vmem_limit_bytes=62 * 1024 * 1024
        ),
        cost_estimate=pl.CostEstimate(
            flops=30_000_000_000, bytes_accessed=80_000_000, transcendentals=20_000_000
        ),
    )(tokens, own_a, own_b, gains, biases_up, bias, cosine, sine_table)


def move(value, route):
    sections, columns, planes = (lax.axis_size(name) for name in ("section", "tp", "seq"))
    pairs = []
    for s in range(sections):
        for t in range(columns):
            for z in range(planes):
                target = route(s, t, z)
                if target is not None:
                    source_index = (s * columns + t) * planes + z
                    target_index = (target[0] * columns + target[1]) * planes + target[2]
                    pairs.append((source_index, target_index))
    return lax.ppermute(value, ("section", "tp", "seq"), pairs)


def other_core(s, t, z):
    return (1 - s, t, z)


def first_hop(s, t, z):
    return (s, t ^ 1, z) if s == 0 else (s, t ^ 2, z)


def second_hop(s, t, z):
    return (s, t ^ 2, z) if s == 0 else (s, t ^ 1, z)


def far_plane(s, t, z):
    return (s, t, z ^ 2)


def gather_plane(own):
    one = move(own, first_hop)
    two = move(own, second_hop)
    three = move(one, second_hop)
    return [own, one, two, three]


def scatter_plane(pieces):
    far = move(pieces[3], second_hop)
    near_two = move(pieces[2], second_hop)
    one = (pieces[1].astype(jnp.float32) + far.astype(jnp.float32)).astype(jnp.bfloat16)
    near_one = move(one, first_hop)
    total = (
        pieces[0].astype(jnp.float32)
        + near_one.astype(jnp.float32)
        + near_two.astype(jnp.float32)
    )
    return total.astype(jnp.bfloat16)


def sum_planes(value, z):
    arrived = move(value, lambda s, t, z: {0: (s, t, 1), 3: (s, t, 2)}.get(z))
    value = (value.astype(jnp.float32) + arrived.astype(jnp.float32)).astype(jnp.bfloat16)
    arrived = move(value, lambda s, t, z: {1: (s, t, 2), 2: (s, t, 1)}.get(z))
    value = (value.astype(jnp.float32) + arrived.astype(jnp.float32)).astype(jnp.bfloat16)
    arrived = move(value, lambda s, t, z: {1: (s, t, 0), 2: (s, t, 3)}.get(z))
    return jnp.where((z == 0) | (z == 3), arrived, value)


def next_block(s, t, z):
    if s == 0:
        return (1, t, z)
    return (0, t, z + 1) if z % 2 == 0 else None


def after_next_block(s, t, z):
    return (0, t, z + 1) if s == 0 and z % 2 == 0 else None


def last_block(s, t, z):
    return (1, t, z) if s == 0 and z % 2 == 1 else None


def backward_route(route):
    def reverse(s, t, z):
        for source in ((0, t, z), (1, t, z), (0, t, z - 1), (1, t, z - 1)):
            if source[2] >= 0 and route(*source) == (s, t, z):
                return source
        return None

    return reverse


def share_keys(clean, is_last):
    near = move(clean, next_block)
    far = move(clean, after_next_block)
    far_last = move(near, last_block)
    return near, jnp.where(is_last, far_last, far)


def return_keys(grad_near, grad_far):
    low_near, low_far = grad_near.astype(jnp.bfloat16), grad_far.astype(jnp.bfloat16)
    passed = move(low_far, backward_route(last_block))
    low_near = (grad_near + passed.astype(jnp.float32)).astype(jnp.bfloat16)
    one = move(low_near, backward_route(next_block))
    two = move(low_far, backward_route(after_next_block))
    return one.astype(jnp.float32) + two.astype(jnp.float32)


def spread(
    layer_input,
    cotangent,
    doc_lengths,
    ln1_gain,
    w_qkv,
    w_out,
    ln2_gain,
    w_up,
    b_up,
    w_down,
    b_down,
):
    s, t, z = (lax.axis_index(name) for name in ("section", "tp", "seq"))
    micros, rows, width_pos, width = layer_input.shape
    half, group = z % 2, z // 2
    shard = w_up.shape[-1]
    columns = w_out.shape[1]
    heads = 4 * columns // HDIM
    on_first = s == 0

    def take_tokens(whole):
        flat = whole.reshape(micros * rows, width_pos, width)
        own = lax.dynamic_slice(flat, (4 * group + t, s * PIECE, 0), (1, PIECE, width))[0]
        sent = lax.dynamic_slice(flat, (4 * (1 - group) + t, s * PIECE, 0), (1, PIECE, width))[0]
        arrived = move(sent, far_plane)
        noisy = jnp.where(group == 0, own, arrived)
        clean = jnp.where(group == 0, arrived, own)
        return jnp.concatenate([noisy, clean], axis=0)

    pack_a = jnp.stack(
        [
            jnp.stack([w_qkv[0, :, 0].T, w_qkv[0, :, 1].T]),
            jnp.stack([w_qkv[0, :, 2].T, w_out[0]]),
        ]
    )
    pack_b = jnp.stack([w_up[0].T, w_down[0]])
    small = jnp.concatenate([ln1_gain[0], ln2_gain[0], b_down[0], b_up[0]])
    small = lax.all_gather(small, ("section", "tp")).reshape(2, 4, -1)
    relative = t ^ jnp.arange(4)
    gains = small[:, 0, : 3 * width].reshape(2, 3, width)
    biases_up = jnp.take(small[:, :, 3 * width :], relative, axis=1).reshape(2, 1, 4 * shard)

    block = 2 * half + s
    lengths = doc_lengths.reshape(micros * rows, -1)
    lengths = lax.dynamic_index_in_dim(lengths, 4 * group + t, 0, keepdims=False)
    ends = jnp.cumsum(lengths)
    piece_pos = jnp.arange(PIECE)
    query_base = jnp.tile(block * PIECE + piece_pos, 2)
    key_base = jnp.concatenate([(block - 2 + i) * PIECE + piece_pos for i in (0, 1, 2, 2)])
    query_noisy = jnp.arange(2 * PIECE) < PIECE
    key_noisy = jnp.arange(4 * PIECE) >= 3 * PIECE

    def docs_of(base):
        return jnp.sum((base[:, None] >= ends[None, :]).astype(jnp.int32), axis=-1)

    query_block, key_block = query_base[:, None] // BLOCK, key_base[None, :] // BLOCK
    query_kind, key_kind = query_noisy[:, None], key_noisy[None, :]
    mask = (
        (query_kind & key_kind & (query_block == key_block))
        | (query_kind & ~key_kind & (key_block < query_block))
        | (~query_kind & ~key_kind & (key_block <= query_block))
    )
    mask = mask & (docs_of(query_base)[:, None] == docs_of(key_base)[None, :])
    mask = mask & (key_base >= 0)[None, :]
    frequency = 10000.0 ** (-jnp.arange(HDIM // 2).astype(jnp.float32) * 2.0 / HDIM)
    angles = query_base.astype(jnp.float32)[:, None, None] * frequency[None, None, :]
    cosine, sine_table = jnp.cos(angles), jnp.sin(angles)
    bias = jnp.where(mask, 0.0, -1e30)
    turn_cos = jnp.tile(cosine[:, 0], (1, 4))
    turn_sin = jnp.tile(jnp.concatenate([-sine_table[:, 0], sine_table[:, 0]], axis=1), (1, 2))
    full_a, full_b, tokens, low, q, kv, att, mid, hid = run_forward(
        layer_input.reshape(micros * rows, width_pos, width),
        pack_a,
        pack_b,
        gains,
        biases_up,
        bias,
        turn_cos,
        turn_sin,
    )

    def backward(layer, grad_out, inputs_low):
        w_q, w_k, w_v, w_o = (full_a[layer, i, j] for i, j in ((0, 0), (0, 1), (1, 0), (1, 1)))
        up, down = full_b[layer, 0], full_b[layer, 1]
        gain_one, gain_two = gains[layer, 0], gains[layer, 1]
        inputs = inputs_low.astype(jnp.float32)
        normed = layer_norm(inputs, gain_one).astype(jnp.bfloat16)
        queries = q[layer].reshape(2 * PIECE, heads, HDIM)
        keys_all = kv[layer, 0].reshape(4 * PIECE, heads, HDIM)
        values_all = kv[layer, 1].reshape(4 * PIECE, heads, HDIM)
        attended, middle = att[layer], mid[layer]
        normed_two = layer_norm(middle, gain_two).astype(jnp.bfloat16)
        hidden_pre = hid[layer].astype(jnp.float32)
        activated = gelu_tanh(hidden_pre).astype(jnp.bfloat16)
        scores = (
            jnp.einsum("qhd,khd->hqk", queries, keys_all, preferred_element_type=jnp.float32)
            * 0.125
        )
        probs = jax.nn.softmax(scores + bias[None], axis=-1)
        grad_low = grad_out.astype(jnp.bfloat16)
        grad_b_down = jnp.sum(grad_out, axis=0)
        grad_down = jnp.einsum("pf,pd->fd", activated, grad_low)
        grad_act = jnp.einsum("pd,fd->pf", grad_low, down, preferred_element_type=jnp.float32)
        grad_pre = jax.vjp(gelu_tanh, hidden_pre)[1](grad_act)[0].astype(jnp.bfloat16)
        grad_b_up = jnp.sum(grad_pre, axis=0, dtype=jnp.float32)
        grad_up = jnp.einsum("pf,pd->fd", grad_pre, normed_two)
        grad_normed_two = jnp.dot(grad_pre, up, preferred_element_type=jnp.float32)
        grad_norm, grad_gain_two = jax.vjp(layer_norm, middle, gain_two)[1](grad_normed_two)
        grad_middle = grad_out + grad_norm
        middle_low = grad_middle.astype(jnp.bfloat16)
        grad_o = jnp.einsum("pe,pd->ed", attended, middle_low)
        grad_att = jnp.einsum("pd,ed->pe", middle_low, w_o, preferred_element_type=jnp.float32)
        grad_att = grad_att.astype(jnp.bfloat16).reshape(2 * PIECE, heads, HDIM)
        grad_probs = jnp.einsum(
            "qhd,khd->hqk", grad_att, values_all, preferred_element_type=jnp.float32
        )
        row_delta = jnp.sum(grad_probs * probs, axis=-1, keepdims=True)
        grad_scores = (probs * (grad_probs - row_delta)).astype(jnp.bfloat16)
        grad_queries = (
            jnp.einsum("hqk,khd->qhd", grad_scores, keys_all, preferred_element_type=jnp.float32)
            * 0.125
        )
        part_keys = (
            jnp.einsum("hqk,qhd->khd", grad_scores, queries, preferred_element_type=jnp.float32)
            * 0.125
        )
        part_values = jnp.einsum(
            "hqk,qhd->khd",
            probs.astype(jnp.bfloat16),
            grad_att,
            preferred_element_type=jnp.float32,
        )
        parts = jnp.concatenate(
            [part_keys.reshape(4 * PIECE, -1), part_values.reshape(4 * PIECE, -1)], axis=1
        )
        returned = return_keys(parts[PIECE : 2 * PIECE], parts[:PIECE])
        own = jnp.concatenate([parts[3 * PIECE :], parts[2 * PIECE : 3 * PIECE] + returned], axis=0)
        own = own.astype(jnp.bfloat16)

        def unrotate(value):
            shaped = value.astype(jnp.bfloat16).reshape(2 * PIECE, heads, HDIM)
            raw = rotate(shaped.astype(jnp.float32), cosine, -sine_table)
            return raw.astype(jnp.bfloat16).reshape(2 * PIECE, -1)

        raw_q = unrotate(grad_queries)
        raw_k = unrotate(own[:, :width])
        raw_v = own[:, width:]
        grad_q, grad_k, grad_v = (
            jnp.einsum("pf,pd->fd", raw, normed) for raw in (raw_q, raw_k, raw_v)
        )
        grad_normed = sum(
            jnp.dot(raw, weight, preferred_element_type=jnp.float32)
            for raw, weight in ((raw_q, w_q), (raw_k, w_k), (raw_v, w_v))
        )
        grad_norm_one, grad_gain_one = jax.vjp(layer_norm, inputs, gain_one)[1](grad_normed)
        grad_inputs = grad_middle + grad_norm_one

        def apart(value):
            return value.reshape(4, -1, width)

        packs = (
            (
                jnp.concatenate([apart(grad_q), apart(grad_k)], axis=1),
                jnp.concatenate([apart(grad_v), apart(grad_o)], axis=1),
            ),
            (apart(grad_up), apart(grad_down)),
        )
        small_grads = (grad_gain_one, grad_gain_two, grad_b_down, grad_b_up.reshape(4, -1))
        return grad_inputs, packs, small_grads

    def give_out(value_low):
        noisy, clean = value_low[:PIECE], value_low[PIECE:]
        arrived = move(jnp.where(group == 0, clean, noisy), far_plane)
        keep = jnp.where(group == 0, noisy, clean)
        pieces = jnp.where(
            group == 0, jnp.stack([keep, arrived]), jnp.stack([arrived, keep])
        )
        return jnp.stack(gather_plane(pieces))

    def place_out(first, second):
        arrived = move(jnp.where(on_first, second, first), other_core)
        mine = jnp.where(on_first, first, second)
        zero_side = jnp.where(on_first, mine, arrived)
        one_side = jnp.where(on_first, arrived, mine)
        one_side = jnp.stack([one_side[i] for i in (0, 2, 1, 3)])
        both = jnp.stack([zero_side, one_side], axis=2)
        both = jnp.where(t % 2 == 1, jnp.stack([both[i] for i in (1, 0, 3, 2)]), both)
        both = jnp.where(t // 2 == 1, jnp.stack([both[i] for i in (2, 3, 0, 1)]), both)
        both = both.transpose(1, 0, 2, 3, 4)
        return both.reshape(1, micros, rows, width_pos, width)

    def reduce_packs(packs):
        reduced = []
        for first_part, second_part in packs:
            second_part = jnp.stack([second_part[i] for i in (0, 2, 1, 3)])
            arrived = move(jnp.where(on_first, second_part, first_part), other_core)
            mine = jnp.where(on_first, first_part, second_part)
            mine = (mine.astype(jnp.float32) + arrived.astype(jnp.float32)).astype(jnp.bfloat16)
            reduced.append(sum_planes(scatter_plane([mine[i] for i in range(4)]), z))
        return reduced

    seeded = take_tokens(cotangent).astype(jnp.float32)
    grad_one, packs_one, small_one = backward(1, seeded, low[0])
    grad_one_low = grad_one.astype(jnp.bfloat16)
    layer_out = place_out(give_out(low[0]), give_out(low[1]))
    grad_zero, packs_zero, small_zero = backward(0, grad_one_low.astype(jnp.float32), tokens)
    input_grad = place_out(give_out(grad_zero.astype(jnp.bfloat16)), give_out(grad_one_low))

    sums = []
    for layer_small in (small_zero, small_one):
        grad_b_up = jnp.take(layer_small[3], relative, axis=0)
        sums.append(jnp.concatenate([layer_small[0], layer_small[1], layer_small[2], grad_b_up.reshape(-1)]))
    sums = lax.psum(jnp.stack(sums), ("section", "tp", "seq"))
    sums = lax.dynamic_index_in_dim(sums, s, 0, keepdims=False)
    small_out = [sums[i * width : (i + 1) * width][None] for i in range(3)]
    grad_b_up = lax.dynamic_slice_in_dim(sums[3 * width :], t * shard, shard, 0)[None]

    finals = []
    for mine_zero, mine_one in zip(reduce_packs(packs_zero), reduce_packs(packs_one)):
        arrived = move(jnp.where(on_first, mine_one, mine_zero), other_core)
        first_part = jnp.where(on_first, mine_zero, arrived).astype(jnp.float32)
        second_part = jnp.where(on_first, arrived, mine_one).astype(jnp.float32)
        finals.append((first_part, second_part))
    (query_key, value_out), (grad_up, grad_down) = finals
    grad_qkv = jnp.stack(
        [query_key[:columns].T, query_key[columns:].T, value_out[:columns].T], axis=1
    )
    return (
        layer_out,
        input_grad,
        small_out[0],
        grad_qkv[None],
        value_out[columns:][None],
        small_out[1],
        grad_up.T[None],
        grad_b_up,
        grad_down[None],
        small_out[2],
    )


def solution(mesh):
    sizes = tuple(mesh.shape[name] for name in ("section", "tp", "seq"))
    local = spread if sizes == (2, 4, 4) else pipelined
    return jax.shard_map(
        local,
        mesh=mesh,
        in_specs=(
            P(None, None, "seq", None),
            P(None, None, "seq", None),
            P(),
            P("section", None),
            P("section", None, None, "tp"),
            P("section", "tp", None),
            P("section", None),
            P("section", None, "tp"),
            P("section", "tp"),
            P("section", "tp", None),
            P("section", None),
        ),
        out_specs=(
            P("section", None, None, "seq", None),
            P("section", None, None, "seq", None),
            P("section", None),
            P("section", None, None, "tp"),
            P("section", "tp", None),
            P("section", None),
            P("section", None, "tp"),
            P("section", "tp"),
            P("section", "tp", None),
            P("section", None),
        ),
        check_vma=False,
    )
```

```python
import jax
import jax.numpy as jnp
from jax import lax
from jax.experimental import pallas as pl
from jax.experimental.pallas import tpu as pltpu
from jax.sharding import PartitionSpec as P

HDIM = 64
BLOCK = 16
HALF = 1024


def from_behind(value, axis, by):
    size = lax.axis_size(axis)
    pairs = [(i, i + by) for i in range(size) if 0 <= i + by < size]
    return lax.ppermute(value, axis, pairs)


def layer_norm(values, gain):
    center = values - jnp.mean(values, axis=-1, keepdims=True)
    spread = jnp.mean(center * center, axis=-1, keepdims=True)
    return center * lax.rsqrt(spread + 1e-05) * gain


def rotate(values, cosine, sine_table):
    middle = values.shape[-1] // 2
    first_half = values[..., :middle]
    second_half = values[..., middle:]
    return jnp.concatenate(
        [
            first_half * cosine - second_half * sine_table,
            second_half * cosine + first_half * sine_table,
        ],
        axis=-1,
    )


def rotary_tables(positions):
    frequency = 10000.0 ** (-jnp.arange(HDIM // 2).astype(jnp.float32) * 2.0 / HDIM)
    angles = (positions % HALF).astype(jnp.float32)[:, None, None] * frequency[None, None, :]
    return (jnp.cos(angles), jnp.sin(angles))


def allowed(query_pos, query_doc, key_pos, key_doc):
    query_noisy = query_pos < HALF
    key_noisy = key_pos < HALF
    query_block = query_pos % HALF // BLOCK
    key_block = key_pos % HALF // BLOCK
    within = query_noisy & key_noisy & (query_block == key_block)
    earlier = query_noisy & ~key_noisy & (key_block < query_block)
    causal = ~query_noisy & ~key_noisy & (key_block <= query_block)
    return (within | earlier | causal) & (query_doc == key_doc)


def document_ids(doc_lengths):
    doc_ends = jnp.cumsum(doc_lengths, axis=-1)
    base_pos = jnp.arange(2 * HALF) % HALF
    return jnp.sum((base_pos[:, None] >= doc_ends[..., None, :]).astype(jnp.int32), axis=-1)


def gelu_tanh(values):
    return jax.nn.gelu(values, approximate=True)


def keep_slot(storage, value, slot_index, is_active):
    current = lax.dynamic_index_in_dim(storage, slot_index, 0, keepdims=False)
    return lax.dynamic_update_index_in_dim(
        storage, jnp.where(is_active, value, current), slot_index, 0
    )


def local_queries(inputs, ln_one, w_mix, tables):
    cosine, sine_table, query_pos = tables
    row_count, pos_count = (inputs.shape[0], inputs.shape[1])
    normed = layer_norm(inputs, ln_one).astype(jnp.bfloat16)
    mixed = jnp.einsum("rpd,dcf->rpcf", normed, w_mix, preferred_element_type=jnp.float32)
    shaped = mixed.reshape(row_count, pos_count, 3, -1, HDIM)
    queries = rotate(shaped[:, :, 0], cosine, sine_table).astype(jnp.bfloat16)
    keys_own = rotate(shaped[:, :, 1], cosine, sine_table).astype(jnp.bfloat16)
    values_own = shaped[:, :, 2].astype(jnp.bfloat16)
    return (normed, queries, keys_own, values_own)


def masked_scores(queries, keys_heads, query_pos, docs_all):
    pos_count = queries.shape[1]
    query_docs = lax.dynamic_slice_in_dim(docs_all, query_pos[0], pos_count, 1)
    key_pos = jnp.arange(keys_heads.shape[1])
    key_mask = allowed(
        query_pos[None, :, None],
        query_docs[:, :, None],
        key_pos[None, None, :],
        docs_all[:, None, :],
    )
    scores = (
        jnp.einsum("rqhd,rkhd->rhqk", queries, keys_heads, preferred_element_type=jnp.float32)
        * 0.125
    )
    return jnp.where(key_mask[:, None], scores, -1e30)


def forward_step(inputs, weights, tables, docs_all):
    ln_one, w_mix, w_proj, ln_two, w_first, b_first, w_second, b_second = weights
    row_count, pos_count = (inputs.shape[0], inputs.shape[1])
    normed, queries, keys_own, values_own = local_queries(inputs, ln_one, w_mix, tables)
    local_width = w_mix.shape[-1]
    keys_all, values_all = (
        lax.all_gather(
            keys_own.reshape(row_count, pos_count, local_width), "seq", axis=1, tiled=True
        ),
        lax.all_gather(
            values_own.reshape(row_count, pos_count, local_width), "seq", axis=1, tiled=True
        ),
    )
    keys_heads = keys_all.reshape(row_count, keys_all.shape[1], -1, HDIM)
    values_heads = values_all.reshape(row_count, values_all.shape[1], -1, HDIM)
    softmax_out = jax.nn.softmax(
        masked_scores(queries, keys_heads, tables[2], docs_all), axis=-1
    ).astype(jnp.bfloat16)
    attended = jnp.einsum(
        "rhqk,rkhd->rqhd", softmax_out, values_heads, preferred_element_type=jnp.float32
    )
    attended = attended.astype(jnp.bfloat16).reshape(row_count, pos_count, local_width)
    middle = inputs + lax.psum(
        jnp.einsum("rpe,ed->rpd", attended, w_proj, preferred_element_type=jnp.float32).astype(
            jnp.bfloat16
        ),
        "tp",
    ).astype(jnp.float32)
    normed_two = layer_norm(middle, ln_two).astype(jnp.bfloat16)
    hidden_pre = (
        jnp.einsum("rpd,df->rpf", normed_two, w_first, preferred_element_type=jnp.float32) + b_first
    )
    activated = gelu_tanh(hidden_pre).astype(jnp.bfloat16)
    second_terms = jnp.einsum(
        "rpf,fd->rpd", activated, w_second, preferred_element_type=jnp.float32
    )
    result = (
        middle + lax.psum(second_terms.astype(jnp.bfloat16), "tp").astype(jnp.float32) + b_second
    )
    return (result, middle, keys_all, values_all)


def backward_step(inputs, middle, grad_out, weights, tables, docs_all):
    ln_one, w_mix, w_proj, ln_two, w_first, b_first, w_second, b_second = weights
    cosine, sine_table, query_pos = tables
    row_count, pos_count = (inputs.shape[0], inputs.shape[1])
    local_width = w_mix.shape[-1]
    head_count = local_width // HDIM
    normed, queries, keys_own, values_own = local_queries(inputs, ln_one, w_mix, tables)
    keys_all, values_all = (
        lax.all_gather(
            keys_own.reshape(row_count, pos_count, local_width), "seq", axis=1, tiled=True
        ),
        lax.all_gather(
            values_own.reshape(row_count, pos_count, local_width), "seq", axis=1, tiled=True
        ),
    )
    keys_heads = keys_all.reshape(row_count, keys_all.shape[1], head_count, HDIM)
    values_heads = values_all.reshape(row_count, values_all.shape[1], head_count, HDIM)
    scores = masked_scores(queries, keys_heads, query_pos, docs_all)
    softmax_out = jax.nn.softmax(scores, axis=-1)
    probs_low = softmax_out.astype(jnp.bfloat16)
    attended = jnp.einsum(
        "rhqk,rkhd->rqhd", probs_low, values_heads, preferred_element_type=jnp.float32
    )
    attended = attended.astype(jnp.bfloat16).reshape(row_count, pos_count, local_width)
    normed_two = layer_norm(middle, ln_two).astype(jnp.bfloat16)
    hidden_pre = (
        jnp.einsum("rpd,df->rpf", normed_two, w_first, preferred_element_type=jnp.float32) + b_first
    )
    activated = gelu_tanh(hidden_pre).astype(jnp.bfloat16)
    grad_low = grad_out.astype(jnp.bfloat16)
    grad_b_second = jnp.sum(grad_out, axis=(0, 1))
    grad_w_second = jnp.einsum(
        "rpf,rpd->fd", activated, grad_low, preferred_element_type=jnp.float32
    )
    grad_act = jnp.einsum("rpd,fd->rpf", grad_low, w_second, preferred_element_type=jnp.float32)
    unused_value, gelu_back = jax.vjp(gelu_tanh, hidden_pre)
    grad_pre = gelu_back(grad_act)[0].astype(jnp.bfloat16)
    grad_b_first = jnp.sum(grad_pre, axis=(0, 1), dtype=jnp.float32)
    grad_w_first = jnp.einsum(
        "rpd,rpf->df", normed_two, grad_pre, preferred_element_type=jnp.float32
    )
    grad_normed_two = lax.psum(
        jnp.einsum("rpf,df->rpd", grad_pre, w_first, preferred_element_type=jnp.float32).astype(
            jnp.bfloat16
        ),
        "tp",
    ).astype(jnp.float32)
    unused_norm, second_back = jax.vjp(layer_norm, middle, ln_two)
    grad_middle_norm, grad_ln_two = second_back(grad_normed_two)
    grad_middle = grad_out + grad_middle_norm
    middle_low = grad_middle.astype(jnp.bfloat16)
    grad_w_proj = jnp.einsum(
        "rpe,rpd->ed", attended, middle_low, preferred_element_type=jnp.float32
    )
    grad_att = jnp.einsum("rpd,ed->rpe", middle_low, w_proj, preferred_element_type=jnp.float32)
    grad_att = grad_att.astype(jnp.bfloat16).reshape(row_count, pos_count, head_count, HDIM)
    grad_probs = jnp.einsum(
        "rqhd,rkhd->rhqk", grad_att, values_heads, preferred_element_type=jnp.float32
    )
    row_delta = jnp.sum(grad_probs * softmax_out, axis=-1, keepdims=True)
    grad_scores = (softmax_out * (grad_probs - row_delta)).astype(jnp.bfloat16)
    grad_queries = (
        jnp.einsum("rhqk,rkhd->rqhd", grad_scores, keys_heads, preferred_element_type=jnp.float32)
        * 0.125
    )
    full_len = keys_all.shape[1]
    part_keys = (
        jnp.einsum("rhqk,rqhd->rkhd", grad_scores, queries, preferred_element_type=jnp.float32)
        * 0.125
    )
    part_values = jnp.einsum(
        "rhqk,rqhd->rkhd", probs_low, grad_att, preferred_element_type=jnp.float32
    )
    grad_keys, grad_values = (
        lax.psum_scatter(
            part_keys.reshape(row_count, full_len, local_width).astype(jnp.bfloat16),
            "seq",
            scatter_dimension=1,
            tiled=True,
        ).astype(jnp.float32),
        lax.psum_scatter(
            part_values.reshape(row_count, full_len, local_width).astype(jnp.bfloat16),
            "seq",
            scatter_dimension=1,
            tiled=True,
        ).astype(jnp.float32),
    )
    grad_query_raw = rotate(grad_queries.astype(jnp.bfloat16), cosine, -sine_table)
    grad_key_raw = rotate(
        grad_keys.astype(jnp.bfloat16).reshape(row_count, pos_count, head_count, HDIM),
        cosine,
        -sine_table,
    )
    grad_mixed = jnp.stack(
        [
            grad_query_raw.reshape(row_count, pos_count, local_width).astype(jnp.bfloat16),
            grad_key_raw.reshape(row_count, pos_count, local_width).astype(jnp.bfloat16),
            grad_values.astype(jnp.bfloat16),
        ],
        axis=2,
    )
    grad_w_mix = jnp.einsum("rpd,rpcf->dcf", normed, grad_mixed, preferred_element_type=jnp.float32)
    grad_normed = lax.psum(
        jnp.einsum("rpcf,dcf->rpd", grad_mixed, w_mix, preferred_element_type=jnp.float32).astype(
            jnp.bfloat16
        ),
        "tp",
    ).astype(jnp.float32)
    unused_first, first_back = jax.vjp(layer_norm, inputs, ln_one)
    grad_in_norm, grad_ln_one = first_back(grad_normed)
    grad_inputs = grad_middle + grad_in_norm
    return (
        grad_inputs,
        (
            grad_ln_one,
            grad_w_mix,
            grad_w_proj,
            grad_ln_two,
            grad_w_first,
            grad_b_first,
            grad_w_second,
            grad_b_second,
        ),
    )


def pipelined(
    layer_input,
    cotangent,
    doc_lengths,
    ln1_gain,
    w_qkv,
    w_out,
    ln2_gain,
    w_up,
    b_up,
    w_down,
    b_down,
):
    weights = tuple(
        (weight[0] for weight in (ln1_gain, w_qkv, w_out, ln2_gain, w_up, b_up, w_down, b_down))
    )
    micros, row_count, pos_count, width_model = layer_input.shape
    sections = lax.axis_size("section")
    section_index = lax.axis_index("section")
    first_pos = lax.axis_index("seq") * pos_count
    query_pos = first_pos + jnp.arange(pos_count)
    cosine, sine_table = rotary_tables(query_pos)
    tables = (cosine, sine_table, query_pos)
    docs_every = document_ids(doc_lengths)
    kept_inputs = jnp.zeros((micros, row_count, pos_count, width_model), jnp.float32)
    kept_middle = jnp.zeros((micros, row_count, pos_count, width_model), jnp.float32)
    layer_out = jnp.zeros(layer_input.shape, jnp.bfloat16)
    arrived = jnp.zeros((row_count, pos_count, width_model), jnp.bfloat16)
    moments = micros + sections - 1
    for moment in range(moments):
        offset = moment - section_index
        micro_index = jnp.clip(offset, 0, micros - 1)
        is_active = (offset >= 0) & (offset < micros)
        own_input = layer_input[min(moment, micros - 1)]
        inputs = jnp.where(section_index == 0, own_input, arrived).astype(jnp.float32)
        result, middle, keys_all, values_all = forward_step(
            inputs, weights, tables, docs_every[micro_index]
        )
        kept_inputs = keep_slot(kept_inputs, inputs, micro_index, is_active)
        kept_middle = keep_slot(kept_middle, middle, micro_index, is_active)
        result_low = result.astype(jnp.bfloat16)
        layer_out = keep_slot(layer_out, result_low, micro_index, is_active)
        if moment < moments - 1:
            arrived = from_behind(result_low, "section", 1)
    grad_totals = tuple((jnp.zeros(weight.shape, jnp.float32) for weight in weights))
    input_grad = jnp.zeros(layer_input.shape, jnp.bfloat16)
    returned = jnp.zeros((row_count, pos_count, width_model), jnp.bfloat16)
    for moment in range(moments):
        offset = moment - (sections - 1 - section_index)
        micro_index = jnp.clip(offset, 0, micros - 1)
        is_active = (offset >= 0) & (offset < micros)
        incoming = jnp.where(
            section_index == sections - 1, cotangent[min(moment, micros - 1)], returned
        ).astype(jnp.float32)
        incoming = jnp.where(is_active, incoming, 0.0)
        grad_inputs, grad_parts = backward_step(
            kept_inputs[micro_index],
            kept_middle[micro_index],
            incoming,
            weights,
            tables,
            docs_every[micro_index],
        )
        grad_totals = tuple((total + piece for total, piece in zip(grad_totals, grad_parts)))
        grad_sent = grad_inputs.astype(jnp.bfloat16)
        input_grad = keep_slot(input_grad, grad_sent, micro_index, is_active)
        if moment < moments - 1:
            returned = from_behind(grad_sent, "section", -1)
    (
        grad_ln_one,
        grad_w_mix,
        grad_w_proj,
        grad_ln_two,
        grad_w_first,
        grad_b_first,
        grad_w_second,
        grad_b_second,
    ) = grad_totals
    summed = (
        lax.psum(grad_ln_one.astype(jnp.bfloat16), "seq").astype(jnp.float32),
        lax.psum(grad_w_mix.astype(jnp.bfloat16), "seq").astype(jnp.float32),
        lax.psum(grad_w_proj.astype(jnp.bfloat16), "seq").astype(jnp.float32),
        lax.psum(grad_ln_two.astype(jnp.bfloat16), "seq").astype(jnp.float32),
        lax.psum(grad_w_first.astype(jnp.bfloat16), "seq").astype(jnp.float32),
        lax.psum(grad_b_first.astype(jnp.bfloat16), "seq").astype(jnp.float32),
        lax.psum(grad_w_second.astype(jnp.bfloat16), "seq").astype(jnp.float32),
        lax.psum(grad_b_second.astype(jnp.bfloat16), "seq").astype(jnp.float32),
    )
    return (
        layer_out[None],
        input_grad[None],
        summed[0][None],
        summed[1][None],
        summed[2][None],
        summed[3][None],
        summed[4][None],
        summed[5][None],
        summed[6][None],
        summed[7][None],
    )


PIECE = 256
LANES = 256
MESH = pl.DeviceIdType.MESH
HBM = pl.BlockSpec(memory_space=pl.ANY)
VMEM = pl.BlockSpec(memory_space=pltpu.VMEM)


def dot_nn(left, right):
    return lax.dot_general(left, right, (((1,), (0,)), ((), ())), preferred_element_type=jnp.float32)


def dot_nt(left, right):
    return lax.dot_general(left, right, (((1,), (1,)), ((), ())), preferred_element_type=jnp.float32)


def dot_tn(left, right):
    return lax.dot_general(left, right, (((0,), (0,)), ((), ())), preferred_element_type=jnp.float32)


class Place:
    def __init__(self):
        self.s, self.t, self.z = (lax.axis_index(name) for name in ("section", "tp", "seq"))
        self.core = 1 - self.s
        self.half, self.group = self.z % 2, self.z // 2
        beside_x = self.t + 1 - 2 * (self.t % 2)
        beside_y = (self.t + 2) % 4
        self.beside_x, self.beside_y = beside_x, beside_y
        self.hop_one = beside_x * (1 - self.s) + beside_y * self.s
        self.hop_two = beside_y * (1 - self.s) + beside_x * self.s
        self.rel_one, self.rel_two = 1 + self.s, 2 - self.s
        self.far = (self.z + 2) % 4
        self.twin = self.z + 1 - 2 * self.half

    def on(self, section=None, tp=None, seq=None):
        return (
            self.s if section is None else section,
            self.t if tp is None else tp,
            self.z if seq is None else seq,
        )

    def partners(self):
        return [
            self.on(section=self.core),
            self.on(tp=self.beside_x),
            self.on(tp=self.beside_y),
            self.on(seq=self.far),
            self.on(seq=self.twin),
            self.on(seq=3 - self.z),
            self.on(section=self.core, seq=self.twin),
        ]

    def meet(self, partners):
        barrier = pltpu.get_barrier_semaphore()
        for partner in partners:
            pl.semaphore_signal(barrier, inc=1, device_id=partner, device_id_type=MESH)
        pl.semaphore_wait(barrier, len(partners))


def remote(source, target, send, receive, device):
    return pltpu.make_async_remote_copy(
        src_ref=source,
        dst_ref=target,
        send_sem=send,
        recv_sem=receive,
        device_id=device,
        device_id_type=MESH,
    )


def normalize(values):
    center = values - jnp.mean(values, axis=-1, keepdims=True)
    spread = jnp.mean(center * center, axis=-1, keepdims=True)
    scale = lax.rsqrt(spread + 1e-05)
    return center * scale, scale


def turn(values, cosine, sine_table):
    width = values.shape[-1]
    times = width // cosine.shape[-1]
    lane = lax.broadcasted_iota(jnp.int32, values.shape, 1) % HDIM
    ahead = pltpu.roll(values, width - HDIM // 2, 1)
    behind = pltpu.roll(values, HDIM // 2, 1)
    swapped = jnp.where(lane < HDIM // 2, ahead, behind)
    return values * jnp.tile(cosine, (1, times)) + swapped * jnp.tile(sine_table, (1, times))


def gelu(values):
    inner = 0.7978845608028654 * (values + 0.044715 * values * values * values)
    return 0.5 * values * (1.0 + jnp.tanh(inner))


def head_mask(head, scale):
    lane = lax.broadcasted_iota(jnp.int32, (1, LANES), 1)
    inside = (lane >= head * HDIM) & (lane < (head + 1) * HDIM)
    return jnp.where(inside, jnp.float32(scale), jnp.float32(0.0))


def attention_block(q_ref, keys, values, bias):
    def one(head, total):
        query = q_ref[...] * head_mask(head, 0.125).astype(jnp.bfloat16)
        scores = dot_nt(query, keys[...]) + bias[...]
        raised = jnp.exp(scores - jnp.max(scores, axis=-1, keepdims=True))
        share = 1.0 / jnp.sum(raised, axis=-1, keepdims=True)
        found = dot_nn(raised.astype(jnp.bfloat16), values[...])
        return total + found * share * head_mask(head, 1.0)

    zero = jnp.zeros((PIECE, LANES), jnp.float32)
    return lax.fori_loop(0, LANES // HDIM, one, zero).astype(jnp.bfloat16)


class Weights:
    def __init__(self, place, own, full, sems):
        self.place, self.own, self.full = place, own, full
        (
            self.local,
            self.own_send,
            self.own_recv,
            self.hop_send,
            self.hop_recv,
            self.chip_send,
            self.chip_recv,
        ) = sems

    def source(self, chunk, pack):
        if chunk == 0:
            return self.own[0].at[pack]
        if chunk == 3:
            return self.own[2].at[pack]
        return self.own[1].at[pack, pl.ds((chunk - 1) * 384, 384)]

    def piece(self, layer, chunk, pack, rel):
        if chunk == 0:
            return self.full[0].at[layer, pack, :, pl.ds(pl.multiple_of(rel * 192, 64), 192)]
        if chunk == 3:
            return self.full[2].at[layer, pack, rel]
        start = pl.multiple_of(rel * 768 + (chunk - 1) * 384, 128)
        return self.full[1].at[layer, pack, pl.ds(start, 384)]

    def own_copies(self, chunk, pack):
        s = self.place.s
        here = pltpu.make_async_copy(
            self.source(chunk, pack), self.piece(s, chunk, pack, 0), self.local.at[chunk, pack]
        )
        there = remote(
            self.source(chunk, pack),
            self.piece(s, chunk, pack, 0),
            self.own_send.at[chunk, pack],
            self.own_recv.at[chunk, pack],
            self.place.on(section=self.place.core),
        )
        return here, there

    def start_own(self, chunk):
        for pack in range(2):
            for copy in self.own_copies(chunk, pack):
                copy.start()

    def wait_own(self, layer, chunk):
        for pack in range(2):
            here, there = self.own_copies(chunk, pack)

            @pl.when(self.place.s == layer)
            def _():
                here.wait()

            @pl.when(self.place.s != layer)
            def _():
                there.wait_recv()

    def hops(self, layer, chunk):
        place = self.place
        own = self.piece(layer, chunk, place.s, 0)
        first = self.piece(layer, chunk, place.s, place.rel_one)
        second = self.piece(layer, chunk, place.s, place.rel_two)
        third = self.piece(layer, chunk, place.s, 3)
        moves = ((own, first, place.hop_one), (own, second, place.hop_two), (first, third, place.hop_two))
        return [
            remote(
                source,
                target,
                self.hop_send.at[layer, chunk, i],
                self.hop_recv.at[layer, chunk, i],
                place.on(tp=column),
            )
            for i, (source, target, column) in enumerate(moves)
        ]

    def chips(self, layer, chunk):
        place = self.place
        return [
            remote(
                self.piece(layer, chunk, place.s, rel),
                self.piece(layer, chunk, place.s, rel),
                self.chip_send.at[layer, chunk, i],
                self.chip_recv.at[layer, chunk, i],
                place.on(section=place.core),
            )
            for i, rel in enumerate((place.rel_one, place.rel_two, 3))
        ]

    def begin(self, layer, chunk):
        self.wait_own(layer, chunk)
        first, second, _ = self.hops(layer, chunk)
        first.start()
        second.start()

    def forward(self, layer, chunk):
        first, second, third = self.hops(layer, chunk)
        chips = self.chips(layer, chunk)
        first.wait_recv()
        third.start()
        chips[0].start()
        second.wait_recv()
        chips[1].start()

    def finish(self, layer, chunk):
        self.hops(layer, chunk)[2].wait_recv()
        self.chips(layer, chunk)[2].start()

    def need(self, layer, chunk):
        for copy in self.chips(layer, chunk):
            copy.wait_recv()

    def drain(self):
        for chunk in range(4):
            for pack in range(2):
                self.own_copies(chunk, pack)[1].wait_send()
            for layer in range(2):
                for copy in self.hops(layer, chunk) + self.chips(layer, chunk):
                    copy.wait_send()


class KeyShare:
    def __init__(self, place, kv, layer, sems):
        self.place, self.kv, self.layer = place, kv, layer
        self.near_send, self.near_recv, self.far_send, self.far_recv = sems
        s, odd = place.s, place.half == 1
        self.sends_near = (s == 0) | ~odd
        self.sends_far = (s == 0) & ~odd
        self.passes = (s == 0) & odd
        self.gets_near = (s == 1) | odd
        self.gets_far = odd

    def rows(self, start, part):
        lanes = pl.ds(part * LANES, LANES)
        return self.kv.at[self.layer, :, pl.ds(start, PIECE), lanes]

    def near(self, part):
        place = self.place
        return remote(
            self.rows(2 * PIECE, part),
            self.rows(PIECE, part),
            self.near_send.at[self.layer, part],
            self.near_recv.at[self.layer, part],
            place.on(section=place.core, seq=place.z + place.s * (1 - place.half)),
        )

    def far(self, part):
        place = self.place
        return remote(
            self.rows(2 * PIECE, part),
            self.rows(0, part),
            self.far_send.at[self.layer, part],
            self.far_recv.at[self.layer, part],
            place.on(seq=place.twin),
        )

    def last(self, part):
        place = self.place
        return remote(
            self.rows(PIECE, part),
            self.rows(0, part),
            self.far_send.at[self.layer, part],
            self.far_recv.at[self.layer, part],
            place.on(section=place.core),
        )

    def start(self, part):
        @pl.when(self.sends_near)
        def _():
            self.near(part).start()

        @pl.when(self.sends_far)
        def _():
            self.far(part).start()

    def arrive(self, part):
        @pl.when(self.gets_near)
        def _():
            self.near(part).wait_recv()

        @pl.when(self.passes)
        def _():
            self.last(part).start()

        @pl.when(self.gets_far)
        def _():
            self.far(part).wait_recv()

    def drain(self):
        for part in range(3):

            @pl.when(self.sends_near)
            def _():
                self.near(part).wait_send()

            @pl.when(self.sends_far)
            def _():
                self.far(part).wait_send()

            @pl.when(self.passes)
            def _():
                self.last(part).wait_send()


def forward_kernel(
    tokens,
    cotangent,
    own_a,
    own_b,
    own_c,
    bias,
    cosine,
    sine_table,
    full_a_out,
    full_b_out,
    gains_out,
    seeded_out,
    x_out,
    low_out,
    q_out,
    kv_out,
    att_out,
    mid_out,
    hid_out,
    full_a,
    full_b,
    full_c,
    low,
    x,
    normed,
    q,
    kv,
    att,
    mid,
    hid,
    *sems,
):
    weight_sems, key_sems = sems[:7], sems[7:11]
    token_sem, swap_send, swap_recv, seed_sem, seed_send, seed_recv, save_sem = sems[11:]
    place = Place()
    weights = Weights(place, (own_a, own_b, own_c), (full_a, full_b, full_c), weight_sems)
    kv[:, :, : 2 * PIECE, :] = jnp.zeros((2, 2, 2 * PIECE, kv.shape[-1]), jnp.bfloat16)
    place.meet(place.partners())
    group_rows = pl.ds(pl.multiple_of(place.group * PIECE, PIECE), PIECE)
    columns = pl.ds(pl.multiple_of(place.s * PIECE, PIECE), PIECE)

    def bring(whole, target, here, send, receive):
        kept = whole.at[4 * place.group + place.t, columns]
        sent = whole.at[4 * (1 - place.group) + place.t, columns]
        target = target.at[group_rows]
        return (
            pltpu.make_async_copy(kept, target, here),
            remote(sent, target, send, receive, place.on(seq=place.far)),
        )

    own_tokens, swap = bring(tokens, low, token_sem, swap_send, swap_recv)
    own_seed, seed_swap = bring(cotangent, seeded_out, seed_sem, seed_send, seed_recv)
    own_tokens.start()
    swap.start()
    for chunk in (3, 0, 1, 2):
        weights.start_own(chunk)
    weights.begin(0, 0)
    weights.begin(0, 1)
    weights.begin(0, 3)
    weights.begin(1, 3)
    gains = full_c.at[:, 0, 0]
    gains_out[...] = full_c[:, 0, 0]
    own_tokens.wait()
    swap.wait()
    own_seed.start()
    seed_swap.start()
    x_save = pltpu.make_async_copy(low, x_out, save_sem.at[7])
    x_save.start()
    x[...] = low[...].astype(jnp.float32)

    def saves(layer):
        pairs = [
            (low, low_out.at[layer]),
            (q, q_out.at[layer]),
            (kv.at[layer], kv_out.at[layer]),
            (att, att_out.at[layer]),
            (mid, mid_out.at[layer]),
            (hid, hid_out.at[layer]),
        ]
        return [pltpu.make_async_copy(a, b, save_sem.at[i]) for i, (a, b) in enumerate(pairs)]

    def weight_saves(layer):
        return [
            pltpu.make_async_copy(full_a.at[layer], full_a_out.at[layer], save_sem.at[8 + 2 * layer]),
            pltpu.make_async_copy(full_b.at[layer], full_b_out.at[layer], save_sem.at[9 + 2 * layer]),
        ]

    for layer in range(2):
        share = KeyShare(place, kv, layer, key_sems)
        unit, _ = normalize(x[...])
        normed[...] = (unit * gains[layer, 0:1]).astype(jnp.bfloat16)
        if layer == 0:
            weights.forward(0, 0)
            weights.begin(0, 2)
            weights.finish(0, 0)
        else:
            weights.forward(1, 0)
            weights.begin(1, 2)
            weights.finish(1, 0)
            for copy in saves(0)[1:]:
                copy.wait()
        weights.need(layer, 0)
        for part in range(3):
            lanes = pl.ds(part * LANES, LANES)
            keep = normed[...]
            mixed = dot_nt(keep, full_a[layer, 0, 0, lanes, :])
            q[:, lanes] = turn(mixed, cosine[...], sine_table[...]).astype(jnp.bfloat16)
            mixed = dot_nt(keep, full_a[layer, 0, 1, lanes, :])
            mixed = turn(mixed, cosine[...], sine_table[...]).astype(jnp.bfloat16)
            kv[layer, 0, 2 * PIECE : 3 * PIECE, lanes] = mixed[PIECE:]
            kv[layer, 0, 3 * PIECE :, lanes] = mixed[:PIECE]
            mixed = dot_nt(keep, full_a[layer, 1, 0, lanes, :]).astype(jnp.bfloat16)
            kv[layer, 1, 2 * PIECE : 3 * PIECE, lanes] = mixed[PIECE:]
            kv[layer, 1, 3 * PIECE :, lanes] = mixed[:PIECE]
            share.start(part)
        if layer == 0:
            weights.forward(0, 3)
            weights.forward(1, 3)
            weights.finish(0, 3)
            weights.finish(1, 3)
            weights.forward(0, 1)
            weights.begin(1, 0)
        else:
            weights.forward(1, 1)
        for part in range(3):
            lanes = pl.ds(part * LANES, LANES)
            share.arrive(part)
            att[:PIECE, lanes] = attention_block(
                q.at[:PIECE, lanes],
                kv.at[layer, 0, :, lanes],
                kv.at[layer, 1, :, lanes],
                bias.at[:PIECE],
            )
            att[PIECE:, lanes] = attention_block(
                q.at[PIECE:, lanes],
                kv.at[layer, 0, : 3 * PIECE, lanes],
                kv.at[layer, 1, : 3 * PIECE, lanes],
                bias.at[PIECE:, : 3 * PIECE],
            )
            if part == 0:
                weights.finish(layer, 1)
            elif part == 1:
                weights.forward(layer, 2)
                if layer == 0:
                    weights.begin(1, 1)
            else:
                weights.finish(layer, 2)
        for copy in saves(layer)[1:4]:
            copy.start()

        def project(part, _):
            lanes = pl.ds(pl.multiple_of(part * LANES, LANES), LANES)
            mid[:, lanes] = x[:, lanes] + dot_nn(att[...], full_a[layer, 1, 1, :, lanes])
            return 0

        lax.fori_loop(0, 3, project, 0)
        unit, _ = normalize(mid[...])
        normed[...] = (unit * gains[layer, 1:2]).astype(jnp.bfloat16)
        x[...] = mid[...] + gains[layer, 2:3]
        saves(layer)[4].start()
        weights.need(layer, 3)
        for part in range(2):
            weights.need(layer, part + 1)

            def feed(rel, _):
                start = pl.multiple_of(rel * 768 + part * 384, 128)
                units = pl.ds(start, 384)
                shift = full_c[layer, 1, rel, 0:1, pl.ds(part * 384, 384)]
                pre = dot_nt(normed[...], full_b[layer, 0, units, :]) + shift
                hid[:, units] = pre.astype(jnp.bfloat16)
                active = gelu(pre).astype(jnp.bfloat16)
                x[...] += dot_nn(active, full_b[layer, 1, units, :])
                return 0

            lax.fori_loop(0, 4, feed, 0)
        saves(layer)[5].start()
        if layer == 0:
            x_save.wait()
        else:
            saves(0)[0].wait()
        low[...] = x[...].astype(jnp.bfloat16)
        saves(layer)[0].start()
        x[...] = low[...].astype(jnp.float32)
        for copy in weight_saves(layer):
            copy.start()
    for copy in saves(1):
        copy.wait()
    for layer in range(2):
        for copy in weight_saves(layer):
            copy.wait()
        KeyShare(place, kv, layer, key_sems).drain()
    weights.drain()
    own_seed.wait()
    seed_swap.wait()


def run_forward(tokens, cotangent, own_a, own_b, own_c, bias, cosine, sine_table):
    shape = jax.ShapeDtypeStruct
    low_type, full_type = jnp.bfloat16, jnp.float32
    count = 2 * PIECE
    width = tokens.shape[-1]
    units = 4 * own_b.shape[1]
    dma = pltpu.SemaphoreType.DMA
    return pl.pallas_call(
        forward_kernel,
        name="forward_layers",
        out_shape=[
            shape((2, 2, 2, width, width), low_type),
            shape((2, 2, units, width), low_type),
            shape((2, 8, width), full_type),
            shape((count, width), low_type),
            shape((count, width), low_type),
            shape((2, count, width), low_type),
            shape((2, count, width), low_type),
            shape((2, 2, 4 * PIECE, width), low_type),
            shape((2, count, width), low_type),
            shape((2, count, width), full_type),
            shape((2, count, units), low_type),
        ],
        in_specs=[HBM] * 5 + [VMEM] * 3,
        out_specs=[HBM] * 2 + [VMEM] + [HBM] * 8,
        scratch_shapes=[
            pltpu.VMEM((2, 2, 2, width, width), low_type),
            pltpu.VMEM((2, 2, units, width), low_type),
            pltpu.VMEM((2, 2, 4, 8, width), full_type),
            pltpu.VMEM((count, width), low_type),
            pltpu.VMEM((count, width), full_type),
            pltpu.VMEM((count, width), low_type),
            pltpu.VMEM((count, width), low_type),
            pltpu.VMEM((2, 2, 4 * PIECE, width), low_type),
            pltpu.VMEM((count, width), low_type),
            pltpu.VMEM((count, width), full_type),
            pltpu.VMEM((count, units), low_type),
            dma((4, 2)),
            dma((4, 2)),
            dma((4, 2)),
            dma((2, 4, 3)),
            dma((2, 4, 3)),
            dma((2, 4, 3)),
            dma((2, 4, 3)),
            dma((2, 3)),
            dma((2, 3)),
            dma((2, 3)),
            dma((2, 3)),
            dma,
            dma,
            dma,
            dma,
            dma,
            dma,
            dma((12,)),
        ],
        compiler_params=pltpu.CompilerParams(
            collective_id=1, has_side_effects=True, vmem_limit_bytes=62 * 1024 * 1024
        ),
        cost_estimate=pl.CostEstimate(
            flops=30_000_000_000, bytes_accessed=80_000_000, transcendentals=20_000_000
        ),
    )(tokens, cotangent, own_a, own_b, own_c, bias, cosine, sine_table)


def low_sum(*parts):
    total = parts[0].astype(jnp.float32)
    for part in parts[1:]:
        total = total + part.astype(jnp.float32)
    return total.astype(jnp.bfloat16)


class Spread:
    def __init__(self, place, source, stage, sems):
        self.place, self.source, self.stage = place, source, stage
        self.local, self.swap_send, self.swap_recv, self.hop_send, self.hop_recv = sems[:5]
        self.end_local, self.end_send, self.end_recv = sems[5:]

    def entry(self):
        place = self.place
        target = self.stage.at[0, place.group]
        kept = self.source.at[pl.ds(pl.multiple_of(place.group * PIECE, PIECE), PIECE)]
        sent = self.source.at[pl.ds(pl.multiple_of((1 - place.group) * PIECE, PIECE), PIECE)]
        here = pltpu.make_async_copy(kept, target, self.local)
        there = remote(sent, target, self.swap_send, self.swap_recv, place.on(seq=place.far))
        return here, there

    def begin(self):
        for copy in self.entry():
            copy.start()

    def moves(self):
        place, stage = self.place, self.stage
        first, second = stage.at[place.rel_one], stage.at[place.rel_two]
        listed = (
            (stage.at[0], first, place.hop_one),
            (stage.at[0], second, place.hop_two),
            (first, stage.at[3], place.hop_two),
        )
        return [
            remote(source, target, self.hop_send.at[i], self.hop_recv.at[i], place.on(tp=column))
            for i, (source, target, column) in enumerate(listed)
        ]

    def hops(self):
        here, there = self.entry()
        here.wait()
        there.wait_recv()
        first, second, _ = self.moves()
        first.start()
        second.start()

    def forward(self):
        first, _, third = self.moves()
        first.wait_recv()
        third.start()

    def finish(self):
        _, second, third = self.moves()
        second.wait_recv()
        third.wait_recv()

    def drain(self):
        self.entry()[1].wait_send()
        for copy in self.moves():
            copy.wait_send()

    def ends(self, out):
        place = self.place
        rows = pl.ds(pl.multiple_of(place.s * PIECE, PIECE), PIECE)
        pairs = []
        for i, column in enumerate((place.t, place.beside_x, place.beside_y, 3 - place.t)):
            source, target = self.stage.at[i], out.at[:, column, rows]
            here = pltpu.make_async_copy(source, target, self.end_local.at[i])
            there = remote(
                source, target, self.end_send.at[i], self.end_recv.at[i], place.on(section=place.core)
            )
            pairs.append((here, there))
        return pairs

    def place_out(self, layer, out):
        @pl.when(self.place.s == layer)
        def _():
            for here, _ in self.ends(out):
                here.start()

        @pl.when(self.place.s != layer)
        def _():
            for _, there in self.ends(out):
                there.start()

    def wait_out(self, layer, out):
        @pl.when(self.place.s == layer)
        def _():
            for here, there in self.ends(out):
                here.wait()
                there.wait_recv()

        @pl.when(self.place.s != layer)
        def _():
            for _, there in self.ends(out):
                there.wait_send()


def spread_sems():
    dma = pltpu.SemaphoreType.DMA
    return [dma, dma, dma, dma((3,)), dma((3,)), dma((4,)), dma((4,)), dma((4,))]


class Reduce:
    def __init__(self, place, grads_a, grads_b, inbox, total, loose, hop_in, line_in, line_sum, sems):
        self.place, self.grads = place, (grads_a, grads_b)
        self.inbox, self.total, self.loose = inbox, total, loose
        self.hop_in, self.line_in, self.line_sum = hop_in, line_in, line_sum
        (
            self.mine_sem,
            self.chip_send,
            self.chip_recv,
            self.loose_sem,
            self.hop_send,
            self.hop_recv,
            self.line_send,
            self.line_recv,
        ) = sems
        z = place.z
        self.outer = (z == 0) | (z == 3)
        self.inner = (z == 1) | (z == 2)

    def piece(self, chunk, pack, rel):
        if chunk == 0:
            return self.grads[0].at[pack, :, rel]
        return self.grads[1].at[pack, pl.ds(rel * 4 + (chunk - 1) * 2, 2)]

    def entry(self, chunk):
        place = self.place
        pairs = []
        for rel in range(4):
            mine = pltpu.make_async_copy(
                self.piece(chunk, place.s, rel), self.total.at[chunk, rel], self.mine_sem.at[chunk, rel]
            )
            other = remote(
                self.piece(chunk, place.core, rel),
                self.inbox.at[chunk, rel],
                self.chip_send.at[chunk, rel],
                self.chip_recv.at[chunk, rel],
                place.on(section=place.core),
            )
            pairs.append((mine, other))
        return pairs

    def start(self, chunk):
        for mine, other in self.entry(chunk):
            other.start()
            mine.start()

    def moves(self, chunk):
        place = self.place
        listed = (
            (3, 0, place.hop_two),
            (place.rel_two, 1, place.hop_two),
            (place.rel_one, 2, place.hop_one),
        )
        return [
            remote(
                self.total.at[chunk, rel],
                self.hop_in.at[chunk, slot],
                self.hop_send.at[chunk, slot],
                self.hop_recv.at[chunk, slot],
                place.on(tp=column),
            )
            for rel, slot, column in listed
        ]

    def load(self, chunk):
        loads = [
            pltpu.make_async_copy(self.inbox.at[chunk, rel], self.loose.at[rel], self.loose_sem.at[rel])
            for rel in range(4)
        ]
        pairs = self.entry(chunk)
        for rel in (3, 1, 2, 0):
            pairs[rel][1].wait_recv()
            loads[rel].start()
        for rel in (3, 1, 2, 0):
            pairs[rel][0].wait()
            loads[rel].wait()
            self.total[chunk, rel] = low_sum(self.total[chunk, rel], self.loose[rel])
            if rel == 3:
                self.moves(chunk)[0].start()
        self.moves(chunk)[1].start()

    def middle(self, chunk):
        first, _, third = self.moves(chunk)
        first.wait_recv()
        rel = self.place.rel_one
        self.total[chunk, rel] = low_sum(self.total[chunk, rel], self.hop_in[chunk, 0])
        third.start()

    def lines(self, chunk):
        place = self.place
        own, line_sum = self.total.at[chunk, 0], self.line_sum.at[chunk]
        listed = (
            (own, self.line_in.at[chunk, 0], place.twin),
            (own, self.line_in.at[chunk, 1], 3 - place.z),
            (line_sum, line_sum, place.twin),
        )
        return [
            remote(
                source,
                target,
                self.line_send.at[chunk, i],
                self.line_recv.at[chunk, i],
                place.on(seq=plane),
            )
            for i, (source, target, plane) in enumerate(listed)
        ]

    def gather(self, chunk):
        _, second, third = self.moves(chunk)
        second.wait_recv()
        third.wait_recv()
        self.total[chunk, 0] = low_sum(
            self.total[chunk, 0], self.hop_in[chunk, 1], self.hop_in[chunk, 2]
        )

        @pl.when(self.outer)
        def _():
            self.lines(chunk)[0].start()

    def line_one(self, chunk):
        @pl.when(self.inner)
        def _():
            self.lines(chunk)[0].wait_recv()
            self.total[chunk, 0] = low_sum(self.total[chunk, 0], self.line_in[chunk, 0])
            self.lines(chunk)[1].start()

    def line_two(self, chunk):
        @pl.when(self.inner)
        def _():
            self.lines(chunk)[1].wait_recv()
            self.line_sum[chunk] = low_sum(self.total[chunk, 0], self.line_in[chunk, 1])
            self.lines(chunk)[2].start()

    def line_three(self, chunk):
        @pl.when(self.outer)
        def _():
            self.lines(chunk)[2].wait_recv()

    def drain(self):
        for chunk in range(3):
            for _, other in self.entry(chunk):
                other.wait_send()
            for copy in self.moves(chunk):
                copy.wait_send()

            @pl.when(self.outer)
            def _():
                self.lines(chunk)[0].wait_send()

            @pl.when(self.inner)
            def _():
                self.lines(chunk)[1].wait_send()
                self.lines(chunk)[2].wait_send()


def reduce_sems():
    dma = pltpu.SemaphoreType.DMA
    return [
        dma((3, 4)),
        dma((3, 4)),
        dma((3, 4)),
        dma((4,)),
        dma((3, 3)),
        dma((3, 3)),
        dma((3, 3)),
        dma((3, 3)),
    ]


def reduce_buffers(width):
    rows = (2, 192, width)
    return [
        pltpu.VMEM((3, 4) + rows, jnp.bfloat16),
        pltpu.VMEM((4,) + rows, jnp.bfloat16),
        pltpu.VMEM((3, 3) + rows, jnp.bfloat16),
        pltpu.VMEM((3, 2) + rows, jnp.bfloat16),
        pltpu.VMEM((3,) + rows, jnp.bfloat16),
    ]


class KeyReturn:
    def __init__(self, place, kv, near_in, far_in, pass_in, sems):
        self.place, self.kv = place, kv
        self.near_in, self.far_in, self.pass_in = near_in, far_in, pass_in
        (
            self.near_send,
            self.near_recv,
            self.far_send,
            self.far_recv,
            self.pass_send,
            self.pass_recv,
        ) = sems
        s, odd = place.s, place.half == 1
        self.is_third = (s == 0) & odd
        self.is_fourth = (s == 1) & odd
        self.is_second = (s == 1) & ~odd
        self.is_first = (s == 0) & ~odd

    def sources(self, start, part):
        return self.kv.at[:, pl.ds(start, PIECE), pl.ds(part * LANES, LANES)]

    def copies(self, part):
        place = self.place
        lanes = pl.ds(part * LANES, LANES)
        near = remote(
            self.sources(PIECE, part),
            self.near_in.at[:, :, lanes],
            self.near_send.at[part],
            self.near_recv.at[part],
            place.on(section=place.core, seq=place.z - (1 - place.s) * place.half),
        )
        far = remote(
            self.sources(0, part),
            self.far_in.at[:, :, lanes],
            self.far_send.at[part],
            self.far_recv.at[part],
            place.on(seq=place.twin),
        )
        passed = remote(
            self.sources(0, part),
            self.pass_in.at[:, :, lanes],
            self.pass_send.at[part],
            self.pass_recv.at[part],
            place.on(section=place.core),
        )
        return near, far, passed

    def start(self, part):
        near, far, passed = self.copies(part)

        @pl.when(self.is_fourth)
        def _():
            passed.start()
            near.start()

        @pl.when(self.is_second)
        def _():
            near.start()

        @pl.when(self.is_third)
        def _():
            far.start()

    def relay(self, part):
        near, _, passed = self.copies(part)
        lanes = pl.ds(part * LANES, LANES)

        @pl.when(self.is_third)
        def _():
            passed.wait_recv()
            self.kv[:, PIECE : 2 * PIECE, lanes] = low_sum(
                self.kv[:, PIECE : 2 * PIECE, lanes], self.pass_in[:, :, lanes]
            )
            near.start()

    def collect(self, part):
        near, far, _ = self.copies(part)
        lanes = pl.ds(part * LANES, LANES)
        clean = pl.ds(2 * PIECE, PIECE)

        @pl.when(~self.is_fourth)
        def _():
            near.wait_recv()
            self.kv[:, clean, lanes] = low_sum(self.kv[:, clean, lanes], self.near_in[:, :, lanes])

        @pl.when(self.is_first)
        def _():
            far.wait_recv()
            self.kv[:, clean, lanes] = low_sum(self.kv[:, clean, lanes], self.far_in[:, :, lanes])

    def drain(self):
        for part in range(3):
            near, far, passed = self.copies(part)

            @pl.when(self.is_fourth)
            def _():
                passed.wait_send()
                near.wait_send()

            @pl.when(self.is_second)
            def _():
                near.wait_send()

            @pl.when(self.is_third)
            def _():
                far.wait_send()
                near.wait_send()


def normalize_back(grads, unit, scale, gain):
    lifted = grads * gain
    mean = jnp.mean(lifted, axis=-1, keepdims=True)
    along = jnp.mean(lifted * unit, axis=-1, keepdims=True)
    return scale * (lifted - mean - unit * along)


def attention_back(q_ref, grad_ref, keys, values, bias, sums, count):
    def one(head, total):
        query = q_ref[...] * head_mask(head, 0.125).astype(jnp.bfloat16)
        grad = grad_ref[...] * head_mask(head, 1.0).astype(jnp.bfloat16)
        scores = dot_nt(query, keys[...]) + bias[...]
        raised = jnp.exp(scores - jnp.max(scores, axis=-1, keepdims=True))
        probs = raised * (1.0 / jnp.sum(raised, axis=-1, keepdims=True))
        grad_probs = dot_nt(grad, values[...])
        delta = jnp.sum(grad_probs * probs, axis=-1, keepdims=True)
        grad_scores = (probs * (grad_probs - delta)).astype(jnp.bfloat16)
        sums[0, :count] += dot_tn(grad_scores, query)
        sums[1, :count] += dot_tn(probs.astype(jnp.bfloat16), grad)
        return total + dot_nn(grad_scores, keys[...]) * head_mask(head, 0.125)

    zero = jnp.zeros((PIECE, LANES), jnp.float32)
    q_ref[...] = lax.fori_loop(0, LANES // HDIM, one, zero).astype(jnp.bfloat16)


def backward_layer(layer, refs, place, tick, key_sems, sems):
    (
        full_a,
        full_b,
        grad_in,
        x_in,
        q_in,
        kv_in,
        att_in,
        mid_in,
        hid_in,
        gains,
        bias,
        cosine,
        sine_table,
        grads_a,
        grads_b,
        grad_out,
        small_out,
        wa,
        wb,
        low,
        q,
        kv,
        att,
        mid,
        hid,
        grad,
        normed,
        gathered,
        grad_low,
        grad_att,
        near_in,
        far_in,
        pass_in,
        sums,
    ) = refs
    share = KeyReturn(place, kv, near_in, far_in, pass_in, key_sems)
    pairs = [
        (grad_in, grad_low),
        (mid_in.at[layer], mid),
        (hid_in.at[layer], hid),
        (full_b.at[layer], wb),
        (full_a.at[layer], wa),
        (att_in.at[layer], att),
        (q_in.at[layer], q),
        (kv_in.at[layer], kv),
        (x_in, low),
    ]
    loads = [pltpu.make_async_copy(a, b, sems.at[i]) for i, (a, b) in enumerate(pairs)]
    for copy in loads:
        copy.start()
    tick()
    gain_one, gain_two = gains[layer, 0:1], gains[layer, 1:2]
    for copy in loads[:3]:
        copy.wait()
    grad[...] = grad_low[...].astype(jnp.float32)
    small_out[2:3] = jnp.sum(grad[...], axis=0, keepdims=True)
    unit, _ = normalize(mid[...])
    normed[...] = (unit * gain_two).astype(jnp.bfloat16)
    gathered[...] = jnp.zeros_like(gathered)
    loads[3].wait()
    tick()

    def feed(part, rel):
        start = pl.multiple_of(rel * 768 + part * 384, 128)
        units = pl.ds(start, 384)
        pre = hid[:, units].astype(jnp.float32)
        squared = pre * pre
        bent = jnp.tanh(0.7978845608028654 * pre * (1.0 + 0.044715 * squared))
        raised = 0.5 * (1.0 + bent)
        active = (pre * raised).astype(jnp.bfloat16)
        slope = raised + 0.5 * pre * (1.0 - bent * bent) * (
            0.7978845608028654 * (1.0 + 3 * 0.044715 * squared)
        )
        grad_act = dot_nt(grad_low[...], wb[1, units, :])
        grad_pre = (grad_act * slope).astype(jnp.bfloat16)
        total = jnp.sum(grad_pre.astype(jnp.float32), axis=0, keepdims=True)
        small_out[pl.ds(4 + rel, 1), pl.ds(part * 384, 384)] = total
        gathered[...] += dot_nn(grad_pre, wb[0, units, :])
        wb[1, units, :] = dot_tn(active, grad_low[...]).astype(jnp.bfloat16)
        wb[0, units, :] = dot_tn(grad_pre, normed[...]).astype(jnp.bfloat16)

    for part in range(2):

        def one(rel, _):
            feed(part, rel)
            return 0

        lax.fori_loop(0, 4, one, 0)
        tick()
    save_b = pltpu.make_async_copy(wb, grads_b, sems.at[9])
    save_b.start()
    unit, scale = normalize(mid[...])
    small_out[1:2] = jnp.sum(gathered[...] * unit, axis=0, keepdims=True)
    small_out[3:4] = jnp.zeros_like(small_out[3:4])
    grad[...] += normalize_back(gathered[...], unit, scale, gain_two)
    grad_low[...] = grad[...].astype(jnp.bfloat16)
    for copy in loads[4:]:
        copy.wait()

    def project(part, _):
        lanes = pl.ds(pl.multiple_of(part * LANES, LANES), LANES)
        grad_att[:, lanes] = dot_nt(grad_low[...], wa[1, 1, lanes, :]).astype(jnp.bfloat16)
        wa[1, 1, lanes, :] = dot_tn(att[:, lanes], grad_low[...]).astype(jnp.bfloat16)
        return 0

    lax.fori_loop(0, 3, project, 0)
    tick()
    for part in range(3):
        lanes = pl.ds(part * LANES, LANES)
        sums[...] = jnp.zeros_like(sums)
        for start, count in ((0, 4 * PIECE), (PIECE, 3 * PIECE)):
            rows = pl.ds(start, PIECE)
            attention_back(
                q.at[rows, lanes],
                grad_att.at[rows, lanes],
                kv.at[0, :count, lanes],
                kv.at[1, :count, lanes],
                bias.at[rows, :count],
                sums,
                count,
            )
        kv[:, :, lanes] = sums[...].astype(jnp.bfloat16)
        share.start(part)
        if part > 0:
            share.relay(part - 1)
        tick()
    unit, scale = normalize(low[...].astype(jnp.float32))
    normed[...] = (unit * gain_one).astype(jnp.bfloat16)

    def turned(part, _):
        lanes = pl.ds(pl.multiple_of(part * LANES, LANES), LANES)
        raw = turn(q[:, lanes].astype(jnp.float32), cosine[...], -sine_table[...])
        raw = raw.astype(jnp.bfloat16)
        found = dot_nn(raw, wa[0, 0, lanes, :])

        @pl.when(part == 0)
        def _():
            gathered[...] = found

        @pl.when(part > 0)
        def _():
            gathered[...] += found

        wa[0, 0, lanes, :] = dot_tn(raw, normed[...]).astype(jnp.bfloat16)
        return 0

    lax.fori_loop(0, 3, turned, 0)
    share.relay(2)
    tick()
    for part in range(3):
        share.collect(part)

    def keyed(part, _):
        lanes = pl.ds(pl.multiple_of(part * LANES, LANES), LANES)
        noisy, clean = pl.ds(3 * PIECE, PIECE), pl.ds(2 * PIECE, PIECE)
        raw = jnp.concatenate([kv[0, noisy, lanes], kv[0, clean, lanes]], axis=0)
        raw = turn(raw.astype(jnp.float32), cosine[...], -sine_table[...]).astype(jnp.bfloat16)
        gathered[...] += dot_nn(raw, wa[0, 1, lanes, :])
        wa[0, 1, lanes, :] = dot_tn(raw, normed[...]).astype(jnp.bfloat16)
        raw = jnp.concatenate([kv[1, noisy, lanes], kv[1, clean, lanes]], axis=0)
        gathered[...] += dot_nn(raw, wa[1, 0, lanes, :])
        wa[1, 0, lanes, :] = dot_tn(raw, normed[...]).astype(jnp.bfloat16)
        return 0

    lax.fori_loop(0, 3, keyed, 0)
    save_a = pltpu.make_async_copy(wa, grads_a, sems.at[10])
    save_a.start()
    unit, scale = normalize(low[...].astype(jnp.float32))
    small_out[0:1] = jnp.sum(gathered[...] * unit, axis=0, keepdims=True)
    grad[...] += normalize_back(gathered[...], unit, scale, gain_one)
    grad_low[...] = grad[...].astype(jnp.bfloat16)
    save_grad = pltpu.make_async_copy(grad_low, grad_out, sems.at[11])
    save_grad.start()
    tick()
    share.drain()
    save_b.wait()
    save_a.wait()
    save_grad.wait()


class Ticks:
    def __init__(self, groups):
        self.groups = list(groups)

    def __call__(self):
        if self.groups:
            for step in self.groups.pop(0):
                step()

    def rest(self):
        while self.groups:
            self()


def backward_buffers(width, units):
    low, full, count = jnp.bfloat16, jnp.float32, 2 * PIECE
    return [
        pltpu.VMEM((2, 2, width, width), low),
        pltpu.VMEM((2, units, width), low),
        pltpu.VMEM((count, width), low),
        pltpu.VMEM((count, width), low),
        pltpu.VMEM((2, 4 * PIECE, width), low),
        pltpu.VMEM((count, width), low),
        pltpu.VMEM((count, width), full),
        pltpu.VMEM((count, units), low),
        pltpu.VMEM((count, width), full),
        pltpu.VMEM((count, width), low),
        pltpu.VMEM((count, width), full),
        pltpu.VMEM((count, width), low),
        pltpu.VMEM((count, width), low),
        pltpu.VMEM((2, PIECE, width), low),
        pltpu.VMEM((2, PIECE, width), low),
        pltpu.VMEM((2, PIECE, width), low),
        pltpu.VMEM((2, 4 * PIECE, LANES), full),
    ]


def backward_sems():
    dma = pltpu.SemaphoreType.DMA
    return [dma((3,))] * 6 + [dma((12,))]


def second_kernel(*refs):
    ins, refs = refs[:14], refs[14:]
    outs, refs = refs[:6], refs[6:]
    buffers, sems = refs[:17], refs[17:]
    low_both = ins[13]
    grads_a, grads_b, grad_out, small_out, out, stage = outs
    place = Place()
    place.meet(place.partners())
    spreads = [
        Spread(place, low_both.at[i], stage.at[i], sems[7 + 8 * i : 15 + 8 * i]) for i in range(2)
    ]
    tick = Ticks(
        [
            [spreads[0].begin, spreads[1].begin],
            [spreads[0].hops, spreads[1].hops],
            [],
            [],
            [spreads[0].forward],
            [],
            [spreads[1].forward],
            [spreads[0].finish, lambda: spreads[0].place_out(0, out)],
            [spreads[1].finish, lambda: spreads[1].place_out(1, out)],
        ]
    )
    body = ins[:3] + (low_both.at[0],) + ins[4:13] + (grads_a, grads_b, grad_out, small_out) + buffers
    backward_layer(1, body, place, tick, sems[:6], sems[6])
    tick.rest()
    for i in range(2):
        spreads[i].drain()
        spreads[i].wait_out(i, out)


def first_kernel(*refs):
    ins, refs = refs[:16], refs[16:]
    outs, refs = refs[:7], refs[7:]
    buffers, reduces, sems = refs[:17], refs[17:22], refs[22:]
    prior_a, prior_b, prior_grad = ins[13:]
    grads_a, grads_b, grad_out, small_out, inbox, done, stage = outs
    place = Place()
    place.meet(place.partners())
    reduce = Reduce(place, prior_a, prior_b, inbox, *reduces, sems[7:15])
    spread_out = Spread(place, prior_grad, stage, sems[15:23])
    line_sum = reduces[4]
    saves = [
        pltpu.make_async_copy(line_sum.at[c], done.at[pl.ds(2 * c, 2)], sems[23].at[c]) for c in range(3)
    ]

    def step(name, chunk):
        return lambda: getattr(reduce, name)(chunk)

    def finish(chunk):
        reduce.line_three(chunk)
        saves[chunk].start()

    tick = Ticks(
        [
            [step("start", 0), step("start", 1), step("start", 2), spread_out.begin],
            [step("load", 0), step("load", 1)],
            [step("middle", 0), step("load", 2)],
            [step("middle", 1), step("gather", 0)],
            [step("middle", 2), step("line_one", 0), step("gather", 1), spread_out.hops],
            [step("gather", 2), step("line_one", 1), step("line_two", 0)],
            [step("line_one", 2), step("line_two", 1), spread_out.forward],
            [step("line_two", 2), lambda: finish(0), lambda: finish(1)],
            [lambda: finish(2), spread_out.finish],
        ]
    )
    body = ins[:13] + (grads_a, grads_b, grad_out, small_out) + buffers
    backward_layer(0, body, place, tick, sems[:6], sems[6])
    tick.rest()
    reduce.drain()
    spread_out.drain()
    for copy in saves:
        copy.wait()


def last_kernel(*refs):
    prior_a, prior_b, grad_zero, stage_one, done_one, small_zero, small_one = refs[:7]
    out, final, small, inbox, stage_zero = refs[7:12]
    reduces, (small_in, extra), sems = refs[12:17], refs[17:19], refs[19:]
    place = Place()
    place.meet(place.partners())
    reduce = Reduce(place, prior_a, prior_b, inbox, *reduces, sems[:8])
    spread_zero = Spread(place, grad_zero, stage_zero, sems[8:16])
    spread_one = Spread(place, grad_zero, stage_one, sems[16:24])
    line_sum = reduces[4]
    end_local, end_send, end_recv, tiny_send, tiny_recv = sems[24:]
    small[0], small[1] = small_zero[...], small_one[...]
    rows_beside = ((4, 5, 6, 7), (5, 4, 7, 6), (6, 7, 4, 5), (4, 5, 6, 7), (4, 5, 6, 7))
    partners = (
        place.on(section=place.core),
        place.on(tp=place.beside_x),
        place.on(tp=place.beside_y),
        place.on(seq=place.twin),
        place.on(seq=place.far),
    )

    def tiny(i):
        return remote(extra.at[i], small_in.at[i], tiny_send.at[i], tiny_recv.at[i], partners[i])

    def tiny_start(i):
        extra[i] = small[...]
        tiny(i).start()

    def tiny_end(i):
        tiny(i).wait_recv()
        for layer in range(2):
            small[layer, 0:4] = extra[i, layer, 0:4] + small_in[i, layer, 0:4]
            for row, other in enumerate(rows_beside[i]):
                at = row + 4
                small[layer, at : at + 1] = (
                    extra[i, layer, at : at + 1] + small_in[i, layer, other : other + 1]
                )

    def ends(layer, chunk):
        rows = pl.ds(2 * chunk, 2)
        source = line_sum.at[chunk] if layer == 0 else done_one.at[rows]
        target = final.at[place.s, rows]
        here = pltpu.make_async_copy(source, target, end_local.at[layer, chunk])
        there = remote(
            source,
            target,
            end_send.at[layer, chunk],
            end_recv.at[layer, chunk],
            place.on(section=place.core),
        )
        return here, there

    def end_start(layer, chunk):
        here, there = ends(layer, chunk)

        @pl.when(place.s == layer)
        def _():
            here.start()

        @pl.when(place.s != layer)
        def _():
            there.start()

    def end_wait(layer, chunk):
        here, there = ends(layer, chunk)

        @pl.when(place.s == layer)
        def _():
            here.wait()
            there.wait_recv()

        @pl.when(place.s != layer)
        def _():
            there.wait_send()

    for chunk in range(3):
        reduce.start(chunk)
    spread_zero.begin()
    tiny_start(0)
    spread_one.place_out(1, out)
    for chunk in range(3):
        end_start(1, chunk)
    reduce.load(0)
    reduce.load(1)
    reduce.load(2)
    tiny_end(0)
    tiny_start(1)
    spread_zero.hops()
    reduce.middle(0)
    reduce.middle(1)
    reduce.middle(2)
    tiny_end(1)
    tiny_start(2)
    reduce.gather(0)
    reduce.line_one(0)
    spread_zero.forward()
    reduce.gather(1)
    tiny_end(2)
    tiny_start(3)
    reduce.line_one(1)
    reduce.line_two(0)
    reduce.gather(2)
    reduce.line_one(2)
    reduce.line_two(1)
    tiny_end(3)
    tiny_start(4)
    reduce.line_three(0)
    end_start(0, 0)
    reduce.line_two(2)
    reduce.line_three(1)
    end_start(0, 1)
    spread_zero.finish()
    spread_zero.place_out(0, out)
    reduce.line_three(2)
    end_start(0, 2)
    tiny_end(4)
    for layer in range(2):
        for chunk in range(3):
            end_wait(layer, chunk)
    spread_zero.wait_out(0, out)
    spread_one.wait_out(1, out)
    spread_zero.drain()
    reduce.drain()
    for i in range(5):
        tiny(i).wait_send()


def call(kernel, name, number, ins, spaces, shapes, out_spaces, scratch, flops, moved):
    return pl.pallas_call(
        kernel,
        name=name,
        out_shape=[jax.ShapeDtypeStruct(shape, kind) for shape, kind in shapes],
        in_specs=spaces,
        out_specs=out_spaces,
        scratch_shapes=scratch,
        compiler_params=pltpu.CompilerParams(
            collective_id=number, has_side_effects=True, vmem_limit_bytes=62 * 1024 * 1024
        ),
        cost_estimate=pl.CostEstimate(
            flops=flops, bytes_accessed=moved, transcendentals=20_000_000
        ),
    )(*ins)


def run_backward(full_a, full_b, seeded, tokens, low_both, q, kv, att, mid, hid, gains, bias, tables):
    low, full, count = jnp.bfloat16, jnp.float32, 2 * PIECE
    width, units = full_a.shape[-1], full_b.shape[-2]
    grads = [
        ((2, 2, width, width), low),
        ((2, units, width), low),
        ((count, width), low),
        ((8, width), full),
    ]
    out = ((2, 4, count, width), low)
    stage = (4, 2, PIECE, width)
    rows = (2, 192, width)
    common = (q, kv, att, mid, hid, gains, bias, *tables)
    common_spaces = [HBM] * 9 + [VMEM] * 4
    second = call(
        second_kernel,
        "backward_second",
        2,
        (full_a, full_b, seeded, tokens) + common + (low_both,),
        common_spaces + [HBM],
        grads + [out, ((2,) + stage, low)],
        [HBM] * 3 + [VMEM] + [HBM] * 2,
        backward_buffers(width, units) + backward_sems() + spread_sems() + spread_sems(),
        40_000_000_000,
        80_000_000,
    )
    grads_a, grads_b, grad_one, small_one, layer_out, _ = second

    def in_blocks(pair):
        return pair[0].reshape(2, 2, 4, 192, width), pair[1].reshape(2, units // 192, 192, width)

    prior = in_blocks((grads_a, grads_b))
    inbox = ((3, 4) + rows, low)
    first = call(
        first_kernel,
        "backward_first",
        3,
        (full_a, full_b, grad_one, tokens) + common + prior + (grad_one,),
        common_spaces + [HBM] * 3,
        grads + [inbox, ((6, 192, width), low), (stage, low)],
        [HBM] * 3 + [VMEM] + [HBM] * 3,
        backward_buffers(width, units)
        + reduce_buffers(width)
        + backward_sems()
        + reduce_sems()
        + spread_sems()
        + [pltpu.SemaphoreType.DMA((3,))],
        40_000_000_000,
        80_000_000,
    )
    grads_a, grads_b, grad_zero, small_zero, _, done_one, stage_one = first
    prior = in_blocks((grads_a, grads_b))
    dma = pltpu.SemaphoreType.DMA
    last = call(
        last_kernel,
        "sum_and_spread",
        4,
        prior + (grad_zero, stage_one, done_one, small_zero, small_one),
        [HBM] * 5 + [VMEM] * 2,
        [out, ((2, 6, 192, width), low), ((2, 8, width), full), inbox, (stage, low)],
        [HBM] * 2 + [VMEM] + [HBM] * 2,
        reduce_buffers(width)
        + [pltpu.VMEM((5, 2, 8, width), full), pltpu.VMEM((5, 2, 8, width), full)]
        + reduce_sems()
        + spread_sems()
        + spread_sems()
        + [dma((2, 3)), dma((2, 3)), dma((2, 3)), dma((5,)), dma((5,))],
        100_000_000,
        40_000_000,
    )
    return layer_out, last[0], last[1], last[2]


def spread(
    layer_input,
    cotangent,
    doc_lengths,
    ln1_gain,
    w_qkv,
    w_out,
    ln2_gain,
    w_up,
    b_up,
    w_down,
    b_down,
):
    s, t, z = (lax.axis_index(name) for name in ("section", "tp", "seq"))
    micros, rows, width_pos, width = layer_input.shape
    half, group = z % 2, z // 2
    columns = w_out.shape[1]

    own_a = jnp.stack(
        [
            jnp.stack([w_qkv[0, :, 0].T, w_qkv[0, :, 1].T]),
            jnp.stack([w_qkv[0, :, 2].T, w_out[0]]),
        ]
    )
    own_b = jnp.stack([w_up[0].T, w_down[0]])
    gains = jnp.concatenate([ln1_gain, ln2_gain, b_down, jnp.zeros((5, width), jnp.float32)])
    own_c = jnp.stack([gains, jnp.concatenate([b_up, jnp.zeros((7, width), jnp.float32)])])

    block = 2 * half + s
    lengths = doc_lengths.reshape(micros * rows, -1)
    lengths = lax.dynamic_index_in_dim(lengths, 4 * group + t, 0, keepdims=False)
    ends = jnp.cumsum(lengths)
    piece_pos = jnp.arange(PIECE)
    query_base = jnp.tile(block * PIECE + piece_pos, 2)
    key_base = jnp.concatenate([(block - 2 + i) * PIECE + piece_pos for i in (0, 1, 2, 2)])
    query_noisy = jnp.arange(2 * PIECE) < PIECE
    key_noisy = jnp.arange(4 * PIECE) >= 3 * PIECE

    def docs_of(base):
        return jnp.sum((base[:, None] >= ends[None, :]).astype(jnp.int32), axis=-1)

    query_block, key_block = query_base[:, None] // BLOCK, key_base[None, :] // BLOCK
    query_kind, key_kind = query_noisy[:, None], key_noisy[None, :]
    mask = (
        (query_kind & key_kind & (query_block == key_block))
        | (query_kind & ~key_kind & (key_block < query_block))
        | (~query_kind & ~key_kind & (key_block <= query_block))
    )
    mask = mask & (docs_of(query_base)[:, None] == docs_of(key_base)[None, :])
    mask = mask & (key_base >= 0)[None, :]
    bias = jnp.where(mask, 0.0, -1e30)
    frequency = 10000.0 ** (-jnp.arange(HDIM // 2).astype(jnp.float32) * 2.0 / HDIM)
    angles = query_base.astype(jnp.float32)[:, None] * frequency[None, :]
    cosine, sine_table = jnp.cos(angles), jnp.sin(angles)
    turn_cos = jnp.tile(cosine, (1, 4))
    turn_sin = jnp.tile(jnp.concatenate([-sine_table, sine_table], axis=1), (1, 2))

    flat = (micros * rows, width_pos, width)
    forward = run_forward(
        layer_input.reshape(flat), cotangent.reshape(flat), own_a, own_b, own_c, bias, turn_cos, turn_sin
    )
    full_a, full_b, gains, seeded, tokens, low_both, q, kv, att, mid, hid = forward
    layer_out, input_grad, final, small = run_backward(
        full_a, full_b, seeded, tokens, low_both, q, kv, att, mid, hid, gains, bias, (turn_cos, turn_sin)
    )
    small = lax.dynamic_index_in_dim(small, s, 0, keepdims=False)
    final = final.astype(jnp.float32)
    pack_a, pack_b = final[0], final[1]
    grad_qkv = jnp.stack([pack_a[0].T, pack_a[1].T, pack_b[0].T], axis=1)
    grad_up = pack_a[2:].reshape(4 * columns, width).T
    grad_down = pack_b[2:].reshape(4 * columns, width)
    out_shape = (1,) + layer_input.shape
    return (
        layer_out.reshape(out_shape),
        input_grad.reshape(out_shape),
        small[0:1],
        grad_qkv[None],
        pack_b[1][None],
        small[1:2],
        grad_up[None],
        small[4:5],
        grad_down[None],
        small[2:3],
    )


def solution(mesh):
    sizes = tuple(mesh.shape[name] for name in ("section", "tp", "seq"))
    local = spread if sizes == (2, 4, 4) else pipelined
    return jax.shard_map(
        local,
        mesh=mesh,
        in_specs=(
            P(None, None, "seq", None),
            P(None, None, "seq", None),
            P(),
            P("section", None),
            P("section", None, None, "tp"),
            P("section", "tp", None),
            P("section", None),
            P("section", None, "tp"),
            P("section", "tp"),
            P("section", "tp", None),
            P("section", None),
        ),
        out_specs=(
            P("section", None, None, "seq", None),
            P("section", None, None, "seq", None),
            P("section", None),
            P("section", None, None, "tp"),
            P("section", "tp", None),
            P("section", None),
            P("section", None, "tp"),
            P("section", "tp"),
            P("section", "tp", None),
            P("section", None),
        ),
        check_vma=False,
    )
```

```python
import jax
import jax.numpy as jnp
from jax import lax
from jax.experimental import pallas as pl
from jax.experimental.pallas import tpu as pltpu
from jax.sharding import PartitionSpec as P

HDIM = 64
BLOCK = 16
HALF = 1024


def from_behind(value, axis, by):
    size = lax.axis_size(axis)
    pairs = [(i, i + by) for i in range(size) if 0 <= i + by < size]
    return lax.ppermute(value, axis, pairs)


def layer_norm(values, gain):
    center = values - jnp.mean(values, axis=-1, keepdims=True)
    spread = jnp.mean(center * center, axis=-1, keepdims=True)
    return center * lax.rsqrt(spread + 1e-05) * gain


def rotate(values, cosine, sine_table):
    middle = values.shape[-1] // 2
    first_half = values[..., :middle]
    second_half = values[..., middle:]
    return jnp.concatenate(
        [
            first_half * cosine - second_half * sine_table,
            second_half * cosine + first_half * sine_table,
        ],
        axis=-1,
    )


def rotary_tables(positions):
    frequency = 10000.0 ** (-jnp.arange(HDIM // 2).astype(jnp.float32) * 2.0 / HDIM)
    angles = (positions % HALF).astype(jnp.float32)[:, None, None] * frequency[None, None, :]
    return (jnp.cos(angles), jnp.sin(angles))


def allowed(query_pos, query_doc, key_pos, key_doc):
    query_noisy = query_pos < HALF
    key_noisy = key_pos < HALF
    query_block = query_pos % HALF // BLOCK
    key_block = key_pos % HALF // BLOCK
    within = query_noisy & key_noisy & (query_block == key_block)
    earlier = query_noisy & ~key_noisy & (key_block < query_block)
    causal = ~query_noisy & ~key_noisy & (key_block <= query_block)
    return (within | earlier | causal) & (query_doc == key_doc)


def document_ids(doc_lengths):
    doc_ends = jnp.cumsum(doc_lengths, axis=-1)
    base_pos = jnp.arange(2 * HALF) % HALF
    return jnp.sum((base_pos[:, None] >= doc_ends[..., None, :]).astype(jnp.int32), axis=-1)


def gelu_tanh(values):
    return jax.nn.gelu(values, approximate=True)


def keep_slot(storage, value, slot_index, is_active):
    current = lax.dynamic_index_in_dim(storage, slot_index, 0, keepdims=False)
    return lax.dynamic_update_index_in_dim(
        storage, jnp.where(is_active, value, current), slot_index, 0
    )


def local_queries(inputs, ln_one, w_mix, tables):
    cosine, sine_table, query_pos = tables
    row_count, pos_count = (inputs.shape[0], inputs.shape[1])
    normed = layer_norm(inputs, ln_one).astype(jnp.bfloat16)
    mixed = jnp.einsum("rpd,dcf->rpcf", normed, w_mix, preferred_element_type=jnp.float32)
    shaped = mixed.reshape(row_count, pos_count, 3, -1, HDIM)
    queries = rotate(shaped[:, :, 0], cosine, sine_table).astype(jnp.bfloat16)
    keys_own = rotate(shaped[:, :, 1], cosine, sine_table).astype(jnp.bfloat16)
    values_own = shaped[:, :, 2].astype(jnp.bfloat16)
    return (normed, queries, keys_own, values_own)


def masked_scores(queries, keys_heads, query_pos, docs_all):
    pos_count = queries.shape[1]
    query_docs = lax.dynamic_slice_in_dim(docs_all, query_pos[0], pos_count, 1)
    key_pos = jnp.arange(keys_heads.shape[1])
    key_mask = allowed(
        query_pos[None, :, None],
        query_docs[:, :, None],
        key_pos[None, None, :],
        docs_all[:, None, :],
    )
    scores = (
        jnp.einsum("rqhd,rkhd->rhqk", queries, keys_heads, preferred_element_type=jnp.float32)
        * 0.125
    )
    return jnp.where(key_mask[:, None], scores, -1e30)


def forward_step(inputs, weights, tables, docs_all):
    ln_one, w_mix, w_proj, ln_two, w_first, b_first, w_second, b_second = weights
    row_count, pos_count = (inputs.shape[0], inputs.shape[1])
    normed, queries, keys_own, values_own = local_queries(inputs, ln_one, w_mix, tables)
    local_width = w_mix.shape[-1]
    keys_all, values_all = (
        lax.all_gather(
            keys_own.reshape(row_count, pos_count, local_width), "seq", axis=1, tiled=True
        ),
        lax.all_gather(
            values_own.reshape(row_count, pos_count, local_width), "seq", axis=1, tiled=True
        ),
    )
    keys_heads = keys_all.reshape(row_count, keys_all.shape[1], -1, HDIM)
    values_heads = values_all.reshape(row_count, values_all.shape[1], -1, HDIM)
    softmax_out = jax.nn.softmax(
        masked_scores(queries, keys_heads, tables[2], docs_all), axis=-1
    ).astype(jnp.bfloat16)
    attended = jnp.einsum(
        "rhqk,rkhd->rqhd", softmax_out, values_heads, preferred_element_type=jnp.float32
    )
    attended = attended.astype(jnp.bfloat16).reshape(row_count, pos_count, local_width)
    middle = inputs + lax.psum(
        jnp.einsum("rpe,ed->rpd", attended, w_proj, preferred_element_type=jnp.float32).astype(
            jnp.bfloat16
        ),
        "tp",
    ).astype(jnp.float32)
    normed_two = layer_norm(middle, ln_two).astype(jnp.bfloat16)
    hidden_pre = (
        jnp.einsum("rpd,df->rpf", normed_two, w_first, preferred_element_type=jnp.float32) + b_first
    )
    activated = gelu_tanh(hidden_pre).astype(jnp.bfloat16)
    second_terms = jnp.einsum(
        "rpf,fd->rpd", activated, w_second, preferred_element_type=jnp.float32
    )
    result = (
        middle + lax.psum(second_terms.astype(jnp.bfloat16), "tp").astype(jnp.float32) + b_second
    )
    return (result, middle, keys_all, values_all)


def backward_step(inputs, middle, grad_out, weights, tables, docs_all):
    ln_one, w_mix, w_proj, ln_two, w_first, b_first, w_second, b_second = weights
    cosine, sine_table, query_pos = tables
    row_count, pos_count = (inputs.shape[0], inputs.shape[1])
    local_width = w_mix.shape[-1]
    head_count = local_width // HDIM
    normed, queries, keys_own, values_own = local_queries(inputs, ln_one, w_mix, tables)
    keys_all, values_all = (
        lax.all_gather(
            keys_own.reshape(row_count, pos_count, local_width), "seq", axis=1, tiled=True
        ),
        lax.all_gather(
            values_own.reshape(row_count, pos_count, local_width), "seq", axis=1, tiled=True
        ),
    )
    keys_heads = keys_all.reshape(row_count, keys_all.shape[1], head_count, HDIM)
    values_heads = values_all.reshape(row_count, values_all.shape[1], head_count, HDIM)
    scores = masked_scores(queries, keys_heads, query_pos, docs_all)
    softmax_out = jax.nn.softmax(scores, axis=-1)
    probs_low = softmax_out.astype(jnp.bfloat16)
    attended = jnp.einsum(
        "rhqk,rkhd->rqhd", probs_low, values_heads, preferred_element_type=jnp.float32
    )
    attended = attended.astype(jnp.bfloat16).reshape(row_count, pos_count, local_width)
    normed_two = layer_norm(middle, ln_two).astype(jnp.bfloat16)
    hidden_pre = (
        jnp.einsum("rpd,df->rpf", normed_two, w_first, preferred_element_type=jnp.float32) + b_first
    )
    activated = gelu_tanh(hidden_pre).astype(jnp.bfloat16)
    grad_low = grad_out.astype(jnp.bfloat16)
    grad_b_second = jnp.sum(grad_out, axis=(0, 1))
    grad_w_second = jnp.einsum(
        "rpf,rpd->fd", activated, grad_low, preferred_element_type=jnp.float32
    )
    grad_act = jnp.einsum("rpd,fd->rpf", grad_low, w_second, preferred_element_type=jnp.float32)
    unused_value, gelu_back = jax.vjp(gelu_tanh, hidden_pre)
    grad_pre = gelu_back(grad_act)[0].astype(jnp.bfloat16)
    grad_b_first = jnp.sum(grad_pre, axis=(0, 1), dtype=jnp.float32)
    grad_w_first = jnp.einsum(
        "rpd,rpf->df", normed_two, grad_pre, preferred_element_type=jnp.float32
    )
    grad_normed_two = lax.psum(
        jnp.einsum("rpf,df->rpd", grad_pre, w_first, preferred_element_type=jnp.float32).astype(
            jnp.bfloat16
        ),
        "tp",
    ).astype(jnp.float32)
    unused_norm, second_back = jax.vjp(layer_norm, middle, ln_two)
    grad_middle_norm, grad_ln_two = second_back(grad_normed_two)
    grad_middle = grad_out + grad_middle_norm
    middle_low = grad_middle.astype(jnp.bfloat16)
    grad_w_proj = jnp.einsum(
        "rpe,rpd->ed", attended, middle_low, preferred_element_type=jnp.float32
    )
    grad_att = jnp.einsum("rpd,ed->rpe", middle_low, w_proj, preferred_element_type=jnp.float32)
    grad_att = grad_att.astype(jnp.bfloat16).reshape(row_count, pos_count, head_count, HDIM)
    grad_probs = jnp.einsum(
        "rqhd,rkhd->rhqk", grad_att, values_heads, preferred_element_type=jnp.float32
    )
    row_delta = jnp.sum(grad_probs * softmax_out, axis=-1, keepdims=True)
    grad_scores = (softmax_out * (grad_probs - row_delta)).astype(jnp.bfloat16)
    grad_queries = (
        jnp.einsum("rhqk,rkhd->rqhd", grad_scores, keys_heads, preferred_element_type=jnp.float32)
        * 0.125
    )
    full_len = keys_all.shape[1]
    part_keys = (
        jnp.einsum("rhqk,rqhd->rkhd", grad_scores, queries, preferred_element_type=jnp.float32)
        * 0.125
    )
    part_values = jnp.einsum(
        "rhqk,rqhd->rkhd", probs_low, grad_att, preferred_element_type=jnp.float32
    )
    grad_keys, grad_values = (
        lax.psum_scatter(
            part_keys.reshape(row_count, full_len, local_width).astype(jnp.bfloat16),
            "seq",
            scatter_dimension=1,
            tiled=True,
        ).astype(jnp.float32),
        lax.psum_scatter(
            part_values.reshape(row_count, full_len, local_width).astype(jnp.bfloat16),
            "seq",
            scatter_dimension=1,
            tiled=True,
        ).astype(jnp.float32),
    )
    grad_query_raw = rotate(grad_queries.astype(jnp.bfloat16), cosine, -sine_table)
    grad_key_raw = rotate(
        grad_keys.astype(jnp.bfloat16).reshape(row_count, pos_count, head_count, HDIM),
        cosine,
        -sine_table,
    )
    grad_mixed = jnp.stack(
        [
            grad_query_raw.reshape(row_count, pos_count, local_width).astype(jnp.bfloat16),
            grad_key_raw.reshape(row_count, pos_count, local_width).astype(jnp.bfloat16),
            grad_values.astype(jnp.bfloat16),
        ],
        axis=2,
    )
    grad_w_mix = jnp.einsum("rpd,rpcf->dcf", normed, grad_mixed, preferred_element_type=jnp.float32)
    grad_normed = lax.psum(
        jnp.einsum("rpcf,dcf->rpd", grad_mixed, w_mix, preferred_element_type=jnp.float32).astype(
            jnp.bfloat16
        ),
        "tp",
    ).astype(jnp.float32)
    unused_first, first_back = jax.vjp(layer_norm, inputs, ln_one)
    grad_in_norm, grad_ln_one = first_back(grad_normed)
    grad_inputs = grad_middle + grad_in_norm
    return (
        grad_inputs,
        (
            grad_ln_one,
            grad_w_mix,
            grad_w_proj,
            grad_ln_two,
            grad_w_first,
            grad_b_first,
            grad_w_second,
            grad_b_second,
        ),
    )


def pipelined(
    layer_input,
    cotangent,
    doc_lengths,
    ln1_gain,
    w_qkv,
    w_out,
    ln2_gain,
    w_up,
    b_up,
    w_down,
    b_down,
):
    weights = tuple(
        (weight[0] for weight in (ln1_gain, w_qkv, w_out, ln2_gain, w_up, b_up, w_down, b_down))
    )
    micros, row_count, pos_count, width_model = layer_input.shape
    sections = lax.axis_size("section")
    section_index = lax.axis_index("section")
    first_pos = lax.axis_index("seq") * pos_count
    query_pos = first_pos + jnp.arange(pos_count)
    cosine, sine_table = rotary_tables(query_pos)
    tables = (cosine, sine_table, query_pos)
    docs_every = document_ids(doc_lengths)
    kept_inputs = jnp.zeros((micros, row_count, pos_count, width_model), jnp.float32)
    kept_middle = jnp.zeros((micros, row_count, pos_count, width_model), jnp.float32)
    layer_out = jnp.zeros(layer_input.shape, jnp.bfloat16)
    arrived = jnp.zeros((row_count, pos_count, width_model), jnp.bfloat16)
    moments = micros + sections - 1
    for moment in range(moments):
        offset = moment - section_index
        micro_index = jnp.clip(offset, 0, micros - 1)
        is_active = (offset >= 0) & (offset < micros)
        own_input = layer_input[min(moment, micros - 1)]
        inputs = jnp.where(section_index == 0, own_input, arrived).astype(jnp.float32)
        result, middle, keys_all, values_all = forward_step(
            inputs, weights, tables, docs_every[micro_index]
        )
        kept_inputs = keep_slot(kept_inputs, inputs, micro_index, is_active)
        kept_middle = keep_slot(kept_middle, middle, micro_index, is_active)
        result_low = result.astype(jnp.bfloat16)
        layer_out = keep_slot(layer_out, result_low, micro_index, is_active)
        if moment < moments - 1:
            arrived = from_behind(result_low, "section", 1)
    grad_totals = tuple((jnp.zeros(weight.shape, jnp.float32) for weight in weights))
    input_grad = jnp.zeros(layer_input.shape, jnp.bfloat16)
    returned = jnp.zeros((row_count, pos_count, width_model), jnp.bfloat16)
    for moment in range(moments):
        offset = moment - (sections - 1 - section_index)
        micro_index = jnp.clip(offset, 0, micros - 1)
        is_active = (offset >= 0) & (offset < micros)
        incoming = jnp.where(
            section_index == sections - 1, cotangent[min(moment, micros - 1)], returned
        ).astype(jnp.float32)
        incoming = jnp.where(is_active, incoming, 0.0)
        grad_inputs, grad_parts = backward_step(
            kept_inputs[micro_index],
            kept_middle[micro_index],
            incoming,
            weights,
            tables,
            docs_every[micro_index],
        )
        grad_totals = tuple((total + piece for total, piece in zip(grad_totals, grad_parts)))
        grad_sent = grad_inputs.astype(jnp.bfloat16)
        input_grad = keep_slot(input_grad, grad_sent, micro_index, is_active)
        if moment < moments - 1:
            returned = from_behind(grad_sent, "section", -1)
    (
        grad_ln_one,
        grad_w_mix,
        grad_w_proj,
        grad_ln_two,
        grad_w_first,
        grad_b_first,
        grad_w_second,
        grad_b_second,
    ) = grad_totals
    summed = (
        lax.psum(grad_ln_one.astype(jnp.bfloat16), "seq").astype(jnp.float32),
        lax.psum(grad_w_mix.astype(jnp.bfloat16), "seq").astype(jnp.float32),
        lax.psum(grad_w_proj.astype(jnp.bfloat16), "seq").astype(jnp.float32),
        lax.psum(grad_ln_two.astype(jnp.bfloat16), "seq").astype(jnp.float32),
        lax.psum(grad_w_first.astype(jnp.bfloat16), "seq").astype(jnp.float32),
        lax.psum(grad_b_first.astype(jnp.bfloat16), "seq").astype(jnp.float32),
        lax.psum(grad_w_second.astype(jnp.bfloat16), "seq").astype(jnp.float32),
        lax.psum(grad_b_second.astype(jnp.bfloat16), "seq").astype(jnp.float32),
    )
    return (
        layer_out[None],
        input_grad[None],
        summed[0][None],
        summed[1][None],
        summed[2][None],
        summed[3][None],
        summed[4][None],
        summed[5][None],
        summed[6][None],
        summed[7][None],
    )


PIECE = 256
LANES = 256
MESH = pl.DeviceIdType.MESH
HBM = pl.BlockSpec(memory_space=pl.ANY)
VMEM = pl.BlockSpec(memory_space=pltpu.VMEM)


def dot_nn(left, right):
    return lax.dot_general(left, right, (((1,), (0,)), ((), ())), preferred_element_type=jnp.float32)


def dot_nt(left, right):
    return lax.dot_general(left, right, (((1,), (1,)), ((), ())), preferred_element_type=jnp.float32)


def dot_tn(left, right):
    return lax.dot_general(left, right, (((0,), (0,)), ((), ())), preferred_element_type=jnp.float32)


class Place:
    def __init__(self):
        self.s, self.t, self.z = (lax.axis_index(name) for name in ("section", "tp", "seq"))
        self.core = 1 - self.s
        self.half, self.group = self.z % 2, self.z // 2
        beside_x = self.t + 1 - 2 * (self.t % 2)
        beside_y = (self.t + 2) % 4
        self.beside_x, self.beside_y = beside_x, beside_y
        self.hop_one = beside_x * (1 - self.s) + beside_y * self.s
        self.hop_two = beside_y * (1 - self.s) + beside_x * self.s
        self.rel_one, self.rel_two = 1 + self.s, 2 - self.s
        self.far = (self.z + 2) % 4
        self.twin = self.z + 1 - 2 * self.half

    def on(self, section=None, tp=None, seq=None):
        return (
            self.s if section is None else section,
            self.t if tp is None else tp,
            self.z if seq is None else seq,
        )

    def partners(self):
        return [
            self.on(section=self.core),
            self.on(tp=self.beside_x),
            self.on(tp=self.beside_y),
            self.on(seq=self.far),
            self.on(seq=self.twin),
            self.on(seq=3 - self.z),
            self.on(section=self.core, seq=self.twin),
        ]

    def meet(self, partners):
        barrier = pltpu.get_barrier_semaphore()
        for partner in partners:
            pl.semaphore_signal(barrier, inc=1, device_id=partner, device_id_type=MESH)
        pl.semaphore_wait(barrier, len(partners))


def remote(source, target, send, receive, device):
    return pltpu.make_async_remote_copy(
        src_ref=source,
        dst_ref=target,
        send_sem=send,
        recv_sem=receive,
        device_id=device,
        device_id_type=MESH,
    )


def normalize(values):
    center = values - jnp.mean(values, axis=-1, keepdims=True)
    spread = jnp.mean(center * center, axis=-1, keepdims=True)
    scale = lax.rsqrt(spread + 1e-05)
    return center * scale, scale


def turn(values, cosine, sine_table):
    width = values.shape[-1]
    times = width // cosine.shape[-1]
    lane = lax.broadcasted_iota(jnp.int32, values.shape, 1) % HDIM
    ahead = pltpu.roll(values, width - HDIM // 2, 1)
    behind = pltpu.roll(values, HDIM // 2, 1)
    swapped = jnp.where(lane < HDIM // 2, ahead, behind)
    return values * jnp.tile(cosine, (1, times)) + swapped * jnp.tile(sine_table, (1, times))


def gelu(values):
    inner = 0.7978845608028654 * (values + 0.044715 * values * values * values)
    return 0.5 * values * (1.0 + jnp.tanh(inner))


def head_mask(head, scale):
    lane = lax.broadcasted_iota(jnp.int32, (1, LANES), 1)
    inside = (lane >= head * HDIM) & (lane < (head + 1) * HDIM)
    return jnp.where(inside, jnp.float32(scale), jnp.float32(0.0))


def attention_block(q_ref, keys, values, bias):
    def one(head, total):
        query = q_ref[...] * head_mask(head, 0.125).astype(jnp.bfloat16)
        scores = dot_nt(query, keys[...]) + bias[...]
        raised = jnp.exp(scores - jnp.max(scores, axis=-1, keepdims=True))
        share = 1.0 / jnp.sum(raised, axis=-1, keepdims=True)
        found = dot_nn(raised.astype(jnp.bfloat16), values[...])
        return total + found * share * head_mask(head, 1.0)

    zero = jnp.zeros((PIECE, LANES), jnp.float32)
    return lax.fori_loop(0, LANES // HDIM, one, zero).astype(jnp.bfloat16)


class Weights:
    def __init__(self, place, own, full, sems):
        self.place, self.own, self.full = place, own, full
        (
            self.local,
            self.own_send,
            self.own_recv,
            self.hop_send,
            self.hop_recv,
            self.chip_send,
            self.chip_recv,
        ) = sems

    def source(self, chunk, pack):
        if chunk == 0:
            return self.own[0].at[pack]
        if chunk == 3:
            return self.own[2].at[pack]
        return self.own[1].at[pack, chunk - 1]

    def piece(self, layer, chunk, pack, rel):
        if chunk == 0:
            return self.full[0].at[layer, pack, :, pl.ds(pl.multiple_of(rel * 192, 64), 192)]
        if chunk == 3:
            return self.full[2].at[layer, pack, rel]
        return self.full[1].at[layer, pack, rel * 2 + chunk - 1]

    def own_copies(self, chunk, pack):
        s = self.place.s
        here = pltpu.make_async_copy(
            self.source(chunk, pack), self.piece(s, chunk, pack, 0), self.local.at[chunk, pack]
        )
        there = remote(
            self.source(chunk, pack),
            self.piece(s, chunk, pack, 0),
            self.own_send.at[chunk, pack],
            self.own_recv.at[chunk, pack],
            self.place.on(section=self.place.core),
        )
        return here, there

    def start_own(self, chunk):
        for pack in range(2):
            for copy in self.own_copies(chunk, pack):
                copy.start()

    def wait_own(self, layer, chunk):
        for pack in range(2):
            here, there = self.own_copies(chunk, pack)

            @pl.when(self.place.s == layer)
            def _():
                here.wait()

            @pl.when(self.place.s != layer)
            def _():
                there.wait_recv()

    def hops(self, layer, chunk):
        place = self.place
        own = self.piece(layer, chunk, place.s, 0)
        first = self.piece(layer, chunk, place.s, place.rel_one)
        second = self.piece(layer, chunk, place.s, place.rel_two)
        third = self.piece(layer, chunk, place.s, 3)
        moves = ((own, first, place.hop_one), (own, second, place.hop_two), (first, third, place.hop_two))
        return [
            remote(
                source,
                target,
                self.hop_send.at[layer, chunk, i],
                self.hop_recv.at[layer, chunk, i],
                place.on(tp=column),
            )
            for i, (source, target, column) in enumerate(moves)
        ]

    def chips(self, layer, chunk):
        place = self.place
        return [
            remote(
                self.piece(layer, chunk, place.s, rel),
                self.piece(layer, chunk, place.s, rel),
                self.chip_send.at[layer, chunk, i],
                self.chip_recv.at[layer, chunk, i],
                place.on(section=place.core),
            )
            for i, rel in enumerate((place.rel_one, place.rel_two, 3))
        ]

    def begin(self, layer, chunk):
        self.wait_own(layer, chunk)
        first, second, _ = self.hops(layer, chunk)
        first.start()
        second.start()

    def forward(self, layer, chunk):
        first, second, third = self.hops(layer, chunk)
        chips = self.chips(layer, chunk)
        first.wait_recv()
        third.start()
        chips[0].start()
        second.wait_recv()
        chips[1].start()

    def finish(self, layer, chunk):
        self.hops(layer, chunk)[2].wait_recv()
        self.chips(layer, chunk)[2].start()

    def need(self, layer, chunk):
        for copy in self.chips(layer, chunk):
            copy.wait_recv()

    def drain(self):
        for chunk in range(4):
            for pack in range(2):
                self.own_copies(chunk, pack)[1].wait_send()
            for layer in range(2):
                for copy in self.hops(layer, chunk) + self.chips(layer, chunk):
                    copy.wait_send()


class KeyShare:
    def __init__(self, place, kv, layer, sems):
        self.place, self.kv, self.layer = place, kv, layer
        self.near_send, self.near_recv, self.far_send, self.far_recv = sems
        s, odd = place.s, place.half == 1
        self.sends_near = (s == 0) | ~odd
        self.sends_far = (s == 0) & ~odd
        self.passes = (s == 0) & odd
        self.gets_near = (s == 1) | odd
        self.gets_far = odd

    def rows(self, start, part):
        lanes = pl.ds(part * LANES, LANES)
        return self.kv.at[self.layer, :, pl.ds(start, PIECE), lanes]

    def near(self, part):
        place = self.place
        return remote(
            self.rows(2 * PIECE, part),
            self.rows(PIECE, part),
            self.near_send.at[self.layer, part],
            self.near_recv.at[self.layer, part],
            place.on(section=place.core, seq=place.z + place.s * (1 - place.half)),
        )

    def far(self, part):
        place = self.place
        return remote(
            self.rows(2 * PIECE, part),
            self.rows(0, part),
            self.far_send.at[self.layer, part],
            self.far_recv.at[self.layer, part],
            place.on(seq=place.twin),
        )

    def last(self, part):
        place = self.place
        return remote(
            self.rows(PIECE, part),
            self.rows(0, part),
            self.far_send.at[self.layer, part],
            self.far_recv.at[self.layer, part],
            place.on(section=place.core),
        )

    def start(self, part):
        @pl.when(self.sends_near)
        def _():
            self.near(part).start()

        @pl.when(self.sends_far)
        def _():
            self.far(part).start()

    def arrive(self, part):
        @pl.when(self.gets_near)
        def _():
            self.near(part).wait_recv()

        @pl.when(self.passes)
        def _():
            self.last(part).start()

        @pl.when(self.gets_far)
        def _():
            self.far(part).wait_recv()

    def drain(self):
        for part in range(3):

            @pl.when(self.sends_near)
            def _():
                self.near(part).wait_send()

            @pl.when(self.sends_far)
            def _():
                self.far(part).wait_send()

            @pl.when(self.passes)
            def _():
                self.last(part).wait_send()


def forward_kernel(
    tokens,
    cotangent,
    own_a,
    own_b,
    own_c,
    bias,
    cosine,
    sine_table,
    full_a_out,
    full_b_out,
    gains_out,
    seeded_out,
    x_out,
    low_out,
    q_out,
    kv_out,
    att_out,
    mid_out,
    hid_out,
    full_a,
    full_b,
    full_c,
    low,
    x,
    normed,
    q,
    kv,
    att,
    mid,
    hid,
    *sems,
):
    weight_sems, key_sems = sems[:7], sems[7:11]
    token_sem, swap_send, swap_recv, seed_sem, seed_send, seed_recv, save_sem = sems[11:]
    place = Place()
    weights = Weights(place, (own_a, own_b, own_c), (full_a, full_b, full_c), weight_sems)
    kv[:, :, : 2 * PIECE, :] = jnp.zeros((2, 2, 2 * PIECE, kv.shape[-1]), jnp.bfloat16)
    place.meet(place.partners())
    group_rows = pl.ds(pl.multiple_of(place.group * PIECE, PIECE), PIECE)
    columns = pl.ds(pl.multiple_of(place.s * PIECE, PIECE), PIECE)

    def bring(whole, target, here, send, receive):
        kept = whole.at[4 * place.group + place.t, columns]
        sent = whole.at[4 * (1 - place.group) + place.t, columns]
        target = target.at[group_rows]
        return (
            pltpu.make_async_copy(kept, target, here),
            remote(sent, target, send, receive, place.on(seq=place.far)),
        )

    own_tokens, swap = bring(tokens, low, token_sem, swap_send, swap_recv)
    own_seed, seed_swap = bring(cotangent, seeded_out, seed_sem, seed_send, seed_recv)
    own_tokens.start()
    swap.start()
    for chunk in (3, 0, 1, 2):
        weights.start_own(chunk)
    weights.begin(0, 0)
    weights.begin(0, 1)
    weights.begin(0, 3)
    weights.begin(1, 3)
    gains = full_c.at[:, 0, 0]
    gains_out[...] = full_c[:, 0, 0]
    own_tokens.wait()
    swap.wait()
    own_seed.start()
    seed_swap.start()
    x_save = pltpu.make_async_copy(low, x_out, save_sem.at[7])
    x_save.start()
    x[...] = low[...].astype(jnp.float32)

    def saves(layer):
        pairs = [
            (low, low_out.at[layer]),
            (q, q_out.at[layer]),
            (kv.at[layer], kv_out.at[layer]),
            (att, att_out.at[layer]),
            (mid, mid_out.at[layer]),
            (hid, hid_out.at[layer]),
        ]
        return [pltpu.make_async_copy(a, b, save_sem.at[i]) for i, (a, b) in enumerate(pairs)]

    def weight_saves(layer):
        copies = []
        for i, (a, b) in enumerate(((full_a, full_a_out), (full_b, full_b_out))):
            for pack in range(2):
                sem = save_sem.at[8 + 4 * layer + 2 * i + pack]
                copies.append(pltpu.make_async_copy(a.at[layer, pack], b.at[layer, pack], sem))
        return copies

    for layer in range(2):
        share = KeyShare(place, kv, layer, key_sems)
        unit, _ = normalize(x[...])
        normed[...] = (unit * gains[layer, 0:1]).astype(jnp.bfloat16)
        if layer == 0:
            weights.forward(0, 0)
            weights.begin(0, 2)
            weights.finish(0, 0)
        else:
            weights.forward(1, 0)
            weights.begin(1, 2)
            weights.finish(1, 0)
            for copy in saves(0)[1:]:
                copy.wait()
        weights.need(layer, 0)
        for copy in weight_saves(layer)[:2]:
            copy.start()
        for part in range(3):
            lanes = pl.ds(part * LANES, LANES)
            keep = normed[...]
            mixed = dot_nt(keep, full_a[layer, 0, 0, lanes, :])
            q[:, lanes] = turn(mixed, cosine[...], sine_table[...]).astype(jnp.bfloat16)
            mixed = dot_nt(keep, full_a[layer, 0, 1, lanes, :])
            mixed = turn(mixed, cosine[...], sine_table[...]).astype(jnp.bfloat16)
            kv[layer, 0, 2 * PIECE : 3 * PIECE, lanes] = mixed[PIECE:]
            kv[layer, 0, 3 * PIECE :, lanes] = mixed[:PIECE]
            mixed = dot_nt(keep, full_a[layer, 1, 0, lanes, :]).astype(jnp.bfloat16)
            kv[layer, 1, 2 * PIECE : 3 * PIECE, lanes] = mixed[PIECE:]
            kv[layer, 1, 3 * PIECE :, lanes] = mixed[:PIECE]
            share.start(part)
        if layer == 0:
            weights.forward(0, 3)
            weights.forward(1, 3)
            weights.finish(0, 3)
            weights.finish(1, 3)
            weights.forward(0, 1)
            weights.begin(1, 0)
        else:
            weights.forward(1, 1)
        for part in range(3):
            lanes = pl.ds(part * LANES, LANES)
            share.arrive(part)
            att[:PIECE, lanes] = attention_block(
                q.at[:PIECE, lanes],
                kv.at[layer, 0, :, lanes],
                kv.at[layer, 1, :, lanes],
                bias.at[:PIECE],
            )
            att[PIECE:, lanes] = attention_block(
                q.at[PIECE:, lanes],
                kv.at[layer, 0, : 3 * PIECE, lanes],
                kv.at[layer, 1, : 3 * PIECE, lanes],
                bias.at[PIECE:, : 3 * PIECE],
            )
            if part == 0:
                weights.finish(layer, 1)
            elif part == 1:
                weights.forward(layer, 2)
                if layer == 0:
                    weights.begin(1, 1)
            else:
                weights.finish(layer, 2)
        for copy in saves(layer)[1:4]:
            copy.start()

        def project(part, _):
            lanes = pl.ds(pl.multiple_of(part * LANES, LANES), LANES)
            mid[:, lanes] = x[:, lanes] + dot_nn(att[...], full_a[layer, 1, 1, :, lanes])
            return 0

        lax.fori_loop(0, 3, project, 0)
        unit, _ = normalize(mid[...])
        normed[...] = (unit * gains[layer, 1:2]).astype(jnp.bfloat16)
        x[...] = mid[...] + gains[layer, 2:3]
        saves(layer)[4].start()
        weights.need(layer, 3)
        for part in range(2):
            weights.need(layer, part + 1)
            if part == 1:
                for copy in weight_saves(layer)[2:]:
                    copy.start()

            def feed(rel, _):
                start = pl.multiple_of(rel * 768 + part * 384, 128)
                units = pl.ds(start, 384)
                shift = full_c[layer, 1, rel, 0:1, pl.ds(part * 384, 384)]
                tile = rel * 2 + part
                pre = dot_nn(normed[...], full_b[layer, 0, tile]) + shift
                hid[:, units] = pre.astype(jnp.bfloat16)
                active = gelu(pre).astype(jnp.bfloat16)
                x[...] += dot_nt(active, full_b[layer, 1, tile])
                return 0

            lax.fori_loop(0, 4, feed, 0)
        saves(layer)[5].start()
        if layer == 0:
            x_save.wait()
        else:
            saves(0)[0].wait()
        low[...] = x[...].astype(jnp.bfloat16)
        saves(layer)[0].start()
        x[...] = low[...].astype(jnp.float32)
    for copy in saves(1):
        copy.wait()
    for layer in range(2):
        for copy in weight_saves(layer):
            copy.wait()
        KeyShare(place, kv, layer, key_sems).drain()
    weights.drain()
    own_seed.wait()
    seed_swap.wait()


def run_forward(tokens, cotangent, own_a, own_b, own_c, bias, cosine, sine_table):
    shape = jax.ShapeDtypeStruct
    low_type, full_type = jnp.bfloat16, jnp.float32
    count = 2 * PIECE
    width = tokens.shape[-1]
    units = 8 * own_b.shape[-1]
    dma = pltpu.SemaphoreType.DMA
    return pl.pallas_call(
        forward_kernel,
        name="forward_layers",
        out_shape=[
            shape((2, 2, 2, width, width), low_type),
            shape((2, 2, 8, width, units // 8), low_type),
            shape((2, 8, width), full_type),
            shape((count, width), low_type),
            shape((count, width), low_type),
            shape((2, count, width), low_type),
            shape((2, count, width), low_type),
            shape((2, 2, 4 * PIECE, width), low_type),
            shape((2, count, width), low_type),
            shape((2, count, width), full_type),
            shape((2, count, units), low_type),
        ],
        in_specs=[HBM] * 5 + [VMEM] * 3,
        out_specs=[HBM] * 2 + [VMEM] + [HBM] * 8,
        scratch_shapes=[
            pltpu.VMEM((2, 2, 2, width, width), low_type),
            pltpu.VMEM((2, 2, 8, width, units // 8), low_type),
            pltpu.VMEM((2, 2, 4, 8, width), full_type),
            pltpu.VMEM((count, width), low_type),
            pltpu.VMEM((count, width), full_type),
            pltpu.VMEM((count, width), low_type),
            pltpu.VMEM((count, width), low_type),
            pltpu.VMEM((2, 2, 4 * PIECE, width), low_type),
            pltpu.VMEM((count, width), low_type),
            pltpu.VMEM((count, width), full_type),
            pltpu.VMEM((count, units), low_type),
            dma((4, 2)),
            dma((4, 2)),
            dma((4, 2)),
            dma((2, 4, 3)),
            dma((2, 4, 3)),
            dma((2, 4, 3)),
            dma((2, 4, 3)),
            dma((2, 3)),
            dma((2, 3)),
            dma((2, 3)),
            dma((2, 3)),
            dma,
            dma,
            dma,
            dma,
            dma,
            dma,
            dma((16,)),
        ],
        compiler_params=pltpu.CompilerParams(
            collective_id=1, has_side_effects=True, vmem_limit_bytes=62 * 1024 * 1024
        ),
        cost_estimate=pl.CostEstimate(
            flops=30_000_000_000, bytes_accessed=80_000_000, transcendentals=20_000_000
        ),
    )(tokens, cotangent, own_a, own_b, own_c, bias, cosine, sine_table)


def low_sum(*parts):
    total = parts[0].astype(jnp.float32)
    for part in parts[1:]:
        total = total + part.astype(jnp.float32)
    return total.astype(jnp.bfloat16)


class Spread:
    def __init__(self, place, source, stage, sems):
        self.place, self.source, self.stage = place, source, stage
        self.local, self.swap_send, self.swap_recv, self.hop_send, self.hop_recv = sems[:5]
        self.end_local, self.end_send, self.end_recv = sems[5:]

    def entry(self):
        place = self.place
        target = self.stage.at[0, place.group]
        kept = self.source.at[pl.ds(pl.multiple_of(place.group * PIECE, PIECE), PIECE)]
        sent = self.source.at[pl.ds(pl.multiple_of((1 - place.group) * PIECE, PIECE), PIECE)]
        here = pltpu.make_async_copy(kept, target, self.local)
        there = remote(sent, target, self.swap_send, self.swap_recv, place.on(seq=place.far))
        return here, there

    def begin(self):
        for copy in self.entry():
            copy.start()

    def moves(self):
        place, stage = self.place, self.stage
        first, second = stage.at[place.rel_one], stage.at[place.rel_two]
        listed = (
            (stage.at[0], first, place.hop_one),
            (stage.at[0], second, place.hop_two),
            (first, stage.at[3], place.hop_two),
        )
        return [
            remote(source, target, self.hop_send.at[i], self.hop_recv.at[i], place.on(tp=column))
            for i, (source, target, column) in enumerate(listed)
        ]

    def hops(self):
        here, there = self.entry()
        here.wait()
        there.wait_recv()
        first, second, _ = self.moves()
        first.start()
        second.start()

    def forward(self):
        first, _, third = self.moves()
        first.wait_recv()
        third.start()

    def finish(self):
        _, second, third = self.moves()
        second.wait_recv()
        third.wait_recv()

    def drain(self):
        self.entry()[1].wait_send()
        for copy in self.moves():
            copy.wait_send()

    def ends(self, out):
        place = self.place
        rows = pl.ds(pl.multiple_of(place.s * PIECE, PIECE), PIECE)
        pairs = []
        for i, column in enumerate((place.t, place.beside_x, place.beside_y, 3 - place.t)):
            source, target = self.stage.at[i], out.at[:, column, rows]
            here = pltpu.make_async_copy(source, target, self.end_local.at[i])
            there = remote(
                source, target, self.end_send.at[i], self.end_recv.at[i], place.on(section=place.core)
            )
            pairs.append((here, there))
        return pairs

    def place_out(self, layer, out):
        @pl.when(self.place.s == layer)
        def _():
            for here, _ in self.ends(out):
                here.start()

        @pl.when(self.place.s != layer)
        def _():
            for _, there in self.ends(out):
                there.start()

    def wait_out(self, layer, out):
        @pl.when(self.place.s == layer)
        def _():
            for here, there in self.ends(out):
                here.wait()
                there.wait_recv()

        @pl.when(self.place.s != layer)
        def _():
            for _, there in self.ends(out):
                there.wait_send()


def spread_sems():
    dma = pltpu.SemaphoreType.DMA
    return [dma, dma, dma, dma((3,)), dma((3,)), dma((4,)), dma((4,)), dma((4,))]


class Reduce:
    def __init__(self, place, grads_a, grads_b, buffers, sems, shared):
        self.place, self.grads = place, (grads_a, grads_b)
        inbox_a, inbox_b, total_a, total_b, hop_a, hop_b, line_a, line_b = buffers
        last = 0 if shared else 1
        self.shared = shared
        self.inbox = (inbox_a, inbox_b.at[0], inbox_b.at[last])
        self.total, self.hop_in, self.line_in = (
            (first, second.at[0], second.at[1])
            for first, second in ((total_a, total_b), (hop_a, hop_b), (line_a, line_b))
        )
        self.line_sum = [total.at[1] for total in self.total]
        (
            self.mine_sem,
            self.chip_send,
            self.chip_recv,
            self.credit,
            self.hop_send,
            self.hop_recv,
            self.line_send,
            self.line_recv,
        ) = sems
        z = place.z
        self.outer = (z == 0) | (z == 3)
        self.inner = (z == 1) | (z == 2)

    def piece(self, chunk, pack, rel):
        if chunk == 0:
            return self.grads[0].at[pack, :, rel]
        return self.grads[1].at[pack, rel * 2 + chunk - 1]

    def entry(self, chunk):
        place = self.place
        pairs = []
        for rel in range(4):
            mine = pltpu.make_async_copy(
                self.piece(chunk, place.s, rel), self.total[chunk].at[rel], self.mine_sem.at[chunk, rel]
            )
            other = remote(
                self.piece(chunk, place.core, rel),
                self.inbox[chunk].at[rel],
                self.chip_send.at[chunk, rel],
                self.chip_recv.at[chunk, rel],
                place.on(section=place.core),
            )
            pairs.append((mine, other))
        return pairs

    def start(self, chunk):
        if self.shared and chunk == 2:
            pl.semaphore_wait(self.credit, 1)
        pairs = self.entry(chunk)
        for rel in (3, 1, 2, 0):
            mine, other = pairs[rel]
            other.start()
            mine.start()

    def load(self, chunk):
        pairs, total, inbox = self.entry(chunk), self.total[chunk], self.inbox[chunk]
        for rel in (3, 1, 2, 0):
            mine, other = pairs[rel]
            mine.wait()
            other.wait_recv()
            total[rel] = low_sum(total[rel], inbox[rel])
            if rel == 3:
                self.moves(chunk)[0].start()
            elif rel == 2:
                self.moves(chunk)[1].start()
        if self.shared and chunk == 1:
            pl.semaphore_signal(
                self.credit,
                inc=1,
                device_id=self.place.on(section=self.place.core),
                device_id_type=MESH,
            )

    def moves(self, chunk):
        place = self.place
        listed = (
            (3, 0, place.hop_two),
            (place.rel_two, 1, place.hop_two),
            (place.rel_one, 2, place.hop_one),
        )
        return [
            remote(
                self.total[chunk].at[rel],
                self.hop_in[chunk].at[slot],
                self.hop_send.at[chunk, slot],
                self.hop_recv.at[chunk, slot],
                place.on(tp=column),
            )
            for rel, slot, column in listed
        ]

    def middle(self, chunk):
        first, _, third = self.moves(chunk)
        first.wait_recv()
        rel = self.place.rel_one
        total = self.total[chunk]
        total[rel] = low_sum(total[rel], self.hop_in[chunk][0])
        third.start()

    def lines(self, chunk):
        place = self.place
        own, line_sum = self.total[chunk].at[0], self.line_sum[chunk]
        listed = (
            (own, self.line_in[chunk].at[0], place.twin),
            (own, self.line_in[chunk].at[1], 3 - place.z),
            (line_sum, line_sum, place.twin),
        )
        return [
            remote(
                source,
                target,
                self.line_send.at[chunk, i],
                self.line_recv.at[chunk, i],
                place.on(seq=plane),
            )
            for i, (source, target, plane) in enumerate(listed)
        ]

    def gather(self, chunk):
        _, second, third = self.moves(chunk)
        second.wait_recv()
        third.wait_recv()
        total, hop_in = self.total[chunk], self.hop_in[chunk]
        total[0] = low_sum(total[0], hop_in[1], hop_in[2])
        second.wait_send()
        third.wait_send()

        @pl.when(self.outer)
        def _():
            self.lines(chunk)[0].start()

    def line_one(self, chunk):
        @pl.when(self.inner)
        def _():
            self.lines(chunk)[0].wait_recv()
            total = self.total[chunk]
            total[0] = low_sum(total[0], self.line_in[chunk][0])
            self.lines(chunk)[1].start()

    def line_two(self, chunk):
        @pl.when(self.inner)
        def _():
            self.lines(chunk)[1].wait_recv()
            self.line_sum[chunk][...] = low_sum(self.total[chunk][0], self.line_in[chunk][1])
            self.lines(chunk)[2].start()

    def line_three(self, chunk):
        @pl.when(self.outer)
        def _():
            self.lines(chunk)[2].wait_recv()

    def drain(self):
        for chunk in range(3):
            for _, other in self.entry(chunk):
                other.wait_send()
            self.moves(chunk)[0].wait_send()

            @pl.when(self.outer)
            def _():
                self.lines(chunk)[0].wait_send()

            @pl.when(self.inner)
            def _():
                self.lines(chunk)[1].wait_send()
                self.lines(chunk)[2].wait_send()


def reduce_sems():
    dma = pltpu.SemaphoreType.DMA
    return [
        dma((3, 4)),
        dma((3, 4)),
        dma((3, 4)),
        pltpu.SemaphoreType.REGULAR,
        dma((3, 3)),
        dma((3, 3)),
        dma((3, 3)),
        dma((3, 3)),
    ]


def reduce_buffers(width, shared):
    first, second = (2, 192, width), (width, 384)
    counts = (4, 4, 3, 2)
    shapes = []
    for i, count in enumerate(counts):
        kept = 1 if shared and i == 0 else 2
        shapes += [(count,) + first, (kept, count) + second]
    return [pltpu.VMEM(shape, jnp.bfloat16) for shape in shapes]


class KeyReturn:
    def __init__(self, place, kv, near_in, far_in, sems):
        self.place, self.kv = place, kv
        self.near_in, self.far_in, self.pass_in = near_in, far_in, far_in
        (
            self.near_send,
            self.near_recv,
            self.far_send,
            self.far_recv,
            self.pass_send,
            self.pass_recv,
        ) = sems
        s, odd = place.s, place.half == 1
        self.is_third = (s == 0) & odd
        self.is_fourth = (s == 1) & odd
        self.is_second = (s == 1) & ~odd
        self.is_first = (s == 0) & ~odd

    def sources(self, start, part):
        return self.kv.at[:, pl.ds(start, PIECE), pl.ds(part * LANES, LANES)]

    def copies(self, part):
        place = self.place
        lanes = pl.ds(part * LANES, LANES)
        near = remote(
            self.sources(PIECE, part),
            self.near_in.at[:, :, lanes],
            self.near_send.at[part],
            self.near_recv.at[part],
            place.on(section=place.core, seq=place.z - (1 - place.s) * place.half),
        )
        far = remote(
            self.sources(0, part),
            self.far_in.at[:, :, lanes],
            self.far_send.at[part],
            self.far_recv.at[part],
            place.on(seq=place.twin),
        )
        passed = remote(
            self.sources(0, part),
            self.pass_in.at[:, :, lanes],
            self.pass_send.at[part],
            self.pass_recv.at[part],
            place.on(section=place.core),
        )
        return near, far, passed

    def start(self, part):
        near, far, passed = self.copies(part)

        @pl.when(self.is_fourth)
        def _():
            passed.start()
            near.start()

        @pl.when(self.is_second)
        def _():
            near.start()

        @pl.when(self.is_third)
        def _():
            far.start()

    def relay(self, part):
        near, _, passed = self.copies(part)
        lanes = pl.ds(part * LANES, LANES)

        @pl.when(self.is_third)
        def _():
            passed.wait_recv()
            self.kv[:, PIECE : 2 * PIECE, lanes] = low_sum(
                self.kv[:, PIECE : 2 * PIECE, lanes], self.pass_in[:, :, lanes]
            )
            near.start()

    def collect(self, part):
        near, far, _ = self.copies(part)
        lanes = pl.ds(part * LANES, LANES)
        clean = pl.ds(2 * PIECE, PIECE)

        @pl.when(~self.is_fourth)
        def _():
            near.wait_recv()
            self.kv[:, clean, lanes] = low_sum(self.kv[:, clean, lanes], self.near_in[:, :, lanes])

        @pl.when(self.is_first)
        def _():
            far.wait_recv()
            self.kv[:, clean, lanes] = low_sum(self.kv[:, clean, lanes], self.far_in[:, :, lanes])

    def drain(self):
        for part in range(3):
            near, far, passed = self.copies(part)

            @pl.when(self.is_fourth)
            def _():
                passed.wait_send()
                near.wait_send()

            @pl.when(self.is_second)
            def _():
                near.wait_send()

            @pl.when(self.is_third)
            def _():
                far.wait_send()
                near.wait_send()


def normalize_back(grads, unit, scale, gain):
    lifted = grads * gain
    mean = jnp.mean(lifted, axis=-1, keepdims=True)
    along = jnp.mean(lifted * unit, axis=-1, keepdims=True)
    return scale * (lifted - mean - unit * along)


def attention_back(q_ref, grad_ref, keys, values, keys_turned, bias, sums, turned, count):
    def one(head, _):
        rows = pl.ds(pl.multiple_of(head * HDIM, HDIM), HDIM)
        query = q_ref[...] * head_mask(head, 0.125).astype(jnp.bfloat16)
        grad = grad_ref[...] * head_mask(head, 1.0).astype(jnp.bfloat16)
        scores = dot_nt(keys[...], query) + bias[...].astype(jnp.float32)
        raised = jnp.exp(scores - jnp.max(scores, axis=0, keepdims=True))
        probs = raised * (1.0 / jnp.sum(raised, axis=0, keepdims=True))
        grad_probs = dot_nt(values[...], grad)
        delta = jnp.sum(grad_probs * probs, axis=0, keepdims=True)
        grad_scores = (probs * (grad_probs - delta)).astype(jnp.bfloat16)
        sums[0, :count] += dot_nn(grad_scores, query)
        sums[1, :count] += dot_nn(probs.astype(jnp.bfloat16), grad)
        turned[rows, :] = dot_nn(keys_turned[rows, :], grad_scores) * 0.125
        return 0

    lax.fori_loop(0, LANES // HDIM, one, 0)
    q_ref[...] = turned[...].T.astype(jnp.bfloat16)


def backward_layer(layer, refs, place, tick, key_sems, sems, tile_sems):
    (
        full_a,
        full_b,
        grad_in,
        x_in,
        q_in,
        kv_in,
        att_in,
        mid_in,
        hid_in,
        gains,
        bias,
        cosine,
        sine_table,
        grads_a,
        grads_b,
        grad_out,
        small_out,
        wa,
        wb,
        low,
        q,
        kv,
        att,
        mid,
        hid,
        grad,
        gathered,
        grad_low,
        grad_att,
        near_in,
        far_in,
        sums,
        keys_turned,
        turned_q,
        grad_turned,
        normed_turned,
    ) = refs
    share = KeyReturn(place, kv, near_in, far_in, key_sems)
    pairs = [
        (grad_in, grad_low),
        (mid_in.at[layer], mid),
        (hid_in.at[layer], hid),
        (full_a.at[layer], wa),
        (att_in.at[layer], att),
        (q_in.at[layer], q),
        (kv_in.at[layer], kv),
        (x_in, low),
    ]
    loads = [pltpu.make_async_copy(a, b, sems.at[i]) for i, (a, b) in enumerate(pairs)]
    def tile_copy(pack, tile):
        return pltpu.make_async_copy(
            full_b.at[layer, pack, tile], wb.at[pack, tile], tile_sems.at[0, pack, tile]
        )

    def tile_save(pack, tile):
        return pltpu.make_async_copy(
            wb.at[pack, tile], grads_b.at[pack, tile], tile_sems.at[1, pack, tile]
        )

    for copy in loads[:3]:
        copy.start()
    for part in range(2):
        for rel in range(4):
            for pack in (1, 0):
                tile_copy(pack, rel * 2 + part).start()
    for copy in loads[3:]:
        copy.start()
    tick()
    gain_one, gain_two = gains[layer, 0:1], gains[layer, 1:2]
    for copy in loads[:3]:
        copy.wait()
    small_out[...] = jnp.zeros_like(small_out)

    def by_rows(step):
        def one(i, _):
            step(pl.ds(pl.multiple_of(i * 128, 128), 128))
            return 0

        lax.fori_loop(0, grad.shape[0] // 128, one, 0)

    def enter(rows):
        incoming = grad_low[rows, :].astype(jnp.float32)
        grad[rows, :] = incoming
        small_out[2:3] += jnp.sum(incoming, axis=0, keepdims=True)
        grad_turned[:, rows] = incoming.T.astype(jnp.bfloat16)
        unit, _ = normalize(mid[rows, :])
        normed_turned[:, rows] = (unit * gain_two).T.astype(jnp.bfloat16)
        gathered[rows, :] = jnp.zeros((128, grad.shape[1]), jnp.float32)

    by_rows(enter)
    tick()

    def feed(part, rel):
        start = pl.multiple_of(rel * 768 + part * 384, 128)
        units = pl.ds(start, 384)
        tile = rel * 2 + part
        pre = hid[:, units].astype(jnp.float32)
        squared = pre * pre
        bent = jnp.tanh(0.7978845608028654 * pre * (1.0 + 0.044715 * squared))
        raised = 0.5 * (1.0 + bent)
        active = (pre * raised).astype(jnp.bfloat16)
        slope = raised + 0.5 * pre * (1.0 - bent * bent) * (
            0.7978845608028654 * (1.0 + 3 * 0.044715 * squared)
        )
        tile_copy(1, tile).wait()
        grad_act = dot_nn(grad_low[...], wb[1, tile])
        grad_pre = (grad_act * slope).astype(jnp.bfloat16)
        total = jnp.sum(grad_pre.astype(jnp.float32), axis=0, keepdims=True)
        small_out[pl.ds(4 + rel, 1), pl.ds(part * 384, 384)] = total
        wb[1, tile] = dot_nn(grad_turned[...], active).astype(jnp.bfloat16)
        tile_save(1, tile).start()
        tile_copy(0, tile).wait()
        gathered[...] += dot_nt(grad_pre, wb[0, tile])
        wb[0, tile] = dot_nn(normed_turned[...], grad_pre).astype(jnp.bfloat16)
        tile_save(0, tile).start()

    for part in range(2):

        def one(rel, _):
            feed(part, rel)
            return 0

        lax.fori_loop(0, 4, one, 0)
        tick()

    def between(rows):
        found = gathered[rows, :]
        unit, scale = normalize(mid[rows, :])
        small_out[1:2] += jnp.sum(found * unit, axis=0, keepdims=True)
        total = grad[rows, :] + normalize_back(found, unit, scale, gain_two)
        grad[rows, :] = total
        grad_low[rows, :] = total.astype(jnp.bfloat16)

    by_rows(between)
    for copy in loads[3:]:
        copy.wait()

    def project(part, _):
        lanes = pl.ds(pl.multiple_of(part * LANES, LANES), LANES)
        grad_att[:, lanes] = dot_nt(grad_low[...], wa[1, 1, lanes, :]).astype(jnp.bfloat16)
        wa[1, 1, lanes, :] = dot_tn(att[:, lanes], grad_low[...]).astype(jnp.bfloat16)
        return 0

    lax.fori_loop(0, 3, project, 0)
    tick()
    for part in range(3):
        lanes = pl.ds(part * LANES, LANES)
        sums[...] = jnp.zeros_like(sums)
        keys_turned[...] = kv[0, :, lanes].astype(jnp.float32).T.astype(jnp.bfloat16)
        for start, count in ((0, 4 * PIECE), (PIECE, 3 * PIECE)):
            rows = pl.ds(start, PIECE)
            attention_back(
                q.at[rows, lanes],
                grad_att.at[rows, lanes],
                kv.at[0, :count, lanes],
                kv.at[1, :count, lanes],
                keys_turned.at[:, :count],
                bias.at[:count, rows],
                sums,
                turned_q,
                count,
            )
        kv[:, :, lanes] = sums[...].astype(jnp.bfloat16)
        share.start(part)
        if part > 0:
            share.relay(part - 1)
        tick()
    normed = grad_att

    def again(rows):
        unit, _ = normalize(low[rows, :].astype(jnp.float32))
        normed[rows, :] = (unit * gain_one).astype(jnp.bfloat16)

    by_rows(again)

    def turned(part, _):
        lanes = pl.ds(pl.multiple_of(part * LANES, LANES), LANES)
        raw = turn(q[:, lanes].astype(jnp.float32), cosine[...], -sine_table[...])
        raw = raw.astype(jnp.bfloat16)
        found = dot_nn(raw, wa[0, 0, lanes, :])

        @pl.when(part == 0)
        def _():
            gathered[...] = found

        @pl.when(part > 0)
        def _():
            gathered[...] += found

        wa[0, 0, lanes, :] = dot_tn(raw, normed[...]).astype(jnp.bfloat16)
        return 0

    lax.fori_loop(0, 3, turned, 0)
    share.relay(2)
    tick()
    for part in range(3):
        share.collect(part)

    def keyed(part, _):
        lanes = pl.ds(pl.multiple_of(part * LANES, LANES), LANES)
        noisy, clean = pl.ds(3 * PIECE, PIECE), pl.ds(2 * PIECE, PIECE)
        raw = jnp.concatenate([kv[0, noisy, lanes], kv[0, clean, lanes]], axis=0)
        raw = turn(raw.astype(jnp.float32), cosine[...], -sine_table[...]).astype(jnp.bfloat16)
        gathered[...] += dot_nn(raw, wa[0, 1, lanes, :])
        wa[0, 1, lanes, :] = dot_tn(raw, normed[...]).astype(jnp.bfloat16)
        raw = jnp.concatenate([kv[1, noisy, lanes], kv[1, clean, lanes]], axis=0)
        gathered[...] += dot_nn(raw, wa[1, 0, lanes, :])
        wa[1, 0, lanes, :] = dot_tn(raw, normed[...]).astype(jnp.bfloat16)
        return 0

    lax.fori_loop(0, 3, keyed, 0)
    save_a = pltpu.make_async_copy(wa, grads_a, sems.at[10])
    save_a.start()

    def leave(rows):
        found = gathered[rows, :]
        unit, scale = normalize(low[rows, :].astype(jnp.float32))
        small_out[0:1] += jnp.sum(found * unit, axis=0, keepdims=True)
        total = grad[rows, :] + normalize_back(found, unit, scale, gain_one)
        grad_low[rows, :] = total.astype(jnp.bfloat16)

    by_rows(leave)
    save_grad = pltpu.make_async_copy(grad_low, grad_out, sems.at[11])
    save_grad.start()
    tick()
    share.drain()
    for tile in range(8):
        for pack in range(2):
            tile_save(pack, tile).wait()
    save_a.wait()
    save_grad.wait()


class Ticks:
    def __init__(self, groups):
        self.groups = list(groups)

    def __call__(self):
        if self.groups:
            for step in self.groups.pop(0):
                step()

    def rest(self):
        while self.groups:
            self()


def backward_buffers(width, units):
    low, full, count = jnp.bfloat16, jnp.float32, 2 * PIECE
    return [
        pltpu.VMEM((2, 2, width, width), low),
        pltpu.VMEM((2, 8, width, units // 8), low),
        pltpu.VMEM((count, width), low),
        pltpu.VMEM((count, width), low),
        pltpu.VMEM((2, 4 * PIECE, width), low),
        pltpu.VMEM((count, width), low),
        pltpu.VMEM((count, width), full),
        pltpu.VMEM((count, units), low),
        pltpu.VMEM((count, width), full),
        pltpu.VMEM((count, width), full),
        pltpu.VMEM((count, width), low),
        pltpu.VMEM((count, width), low),
        pltpu.VMEM((2, PIECE, width), low),
        pltpu.VMEM((2, PIECE, width), low),
        pltpu.VMEM((2, 4 * PIECE, LANES), full),
        pltpu.VMEM((LANES, 4 * PIECE), low),
        pltpu.VMEM((LANES, PIECE), full),
        pltpu.VMEM((width, count), low),
        pltpu.VMEM((width, count), low),
    ]


def backward_sems():
    dma = pltpu.SemaphoreType.DMA
    return [dma((3,))] * 6 + [dma((12,)), dma((2, 2, 8))]


BUFFERS = 19


def second_kernel(*refs):
    ins, refs = refs[:14], refs[14:]
    outs, refs = refs[:5], refs[5:]
    buffers, stages, sems = refs[:BUFFERS], refs[BUFFERS : BUFFERS + 2], refs[BUFFERS + 2 :]
    low_both = ins[13]
    grads_a, grads_b, grad_out, small_out, out = outs
    place = Place()
    place.meet(place.partners())
    spreads = [
        Spread(place, low_both.at[i], stages[i], sems[8 + 8 * i : 16 + 8 * i]) for i in range(2)
    ]
    tick = Ticks(
        [
            [spreads[0].begin, spreads[1].begin],
            [spreads[0].hops, spreads[1].hops],
            [],
            [spreads[0].forward],
            [],
            [spreads[1].forward],
            [spreads[0].finish, lambda: spreads[0].place_out(0, out)],
            [spreads[1].finish, lambda: spreads[1].place_out(1, out)],
        ]
    )
    body = ins[:3] + (low_both.at[0],) + ins[4:13] + (grads_a, grads_b, grad_out, small_out) + buffers
    backward_layer(1, body, place, tick, sems[:6], sems[6], sems[7])
    tick.rest()
    for i in range(2):
        spreads[i].drain()
        spreads[i].wait_out(i, out)


def first_kernel(*refs):
    ins, refs = refs[:15], refs[15:]
    outs, refs = refs[:6], refs[6:]
    buffers, reduces, sems = refs[:BUFFERS], refs[BUFFERS : BUFFERS + 8], refs[BUFFERS + 8 :]
    prior_a, prior_b = ins[13:]
    grads_a, grads_b, grad_out, small_out, done_a, done_b = outs
    place = Place()
    place.meet(place.partners())
    reduce = Reduce(place, prior_a, prior_b, reduces, sems[8:16], True)
    targets = (done_a, done_b.at[0], done_b.at[1])
    saves = [
        pltpu.make_async_copy(reduce.line_sum[c], targets[c], sems[16].at[c]) for c in range(3)
    ]

    def step(name, chunk):
        return lambda: getattr(reduce, name)(chunk)

    def finish(chunk):
        reduce.line_three(chunk)
        saves[chunk].start()

    tick = Ticks(
        [
            [step("start", 1), step("start", 0)],
            [step("load", 1)],
            [step("start", 2), step("load", 0), step("middle", 1)],
            [step("load", 2), step("middle", 0), step("gather", 1)],
            [step("middle", 2), step("line_one", 1), step("gather", 0)],
            [step("gather", 2), step("line_one", 0), step("line_two", 1)],
            [step("line_one", 2), step("line_two", 0)],
            [step("line_two", 2), lambda: finish(1), lambda: finish(0)],
            [lambda: finish(2)],
        ]
    )
    body = ins[:13] + (grads_a, grads_b, grad_out, small_out) + buffers
    backward_layer(0, body, place, tick, sems[:6], sems[6], sems[7])
    tick.rest()
    reduce.drain()
    for copy in saves:
        copy.wait()


def last_kernel(*refs):
    prior_a, prior_b, grad_zero, grad_one, done_a, done_b, small_zero, small_one = refs[:8]
    out, final_a, final_b, small = refs[8:12]
    reduces, stages, (small_in, extra), sems = refs[12:20], refs[20:22], refs[22:24], refs[24:]
    place = Place()
    place.meet(place.partners())
    reduce = Reduce(place, prior_a, prior_b, reduces, sems[:8], False)
    spread_zero = Spread(place, grad_zero, stages[0], sems[8:16])
    spread_one = Spread(place, grad_one, stages[1], sems[16:24])
    end_local, end_send, end_recv, tiny_send, tiny_recv = sems[24:]
    small[0], small[1] = small_zero[...], small_one[...]
    rows_beside = ((4, 5, 6, 7), (5, 4, 7, 6), (6, 7, 4, 5), (4, 5, 6, 7), (4, 5, 6, 7))
    partners = (
        place.on(section=place.core),
        place.on(tp=place.beside_x),
        place.on(tp=place.beside_y),
        place.on(seq=place.twin),
        place.on(seq=place.far),
    )

    def tiny(i):
        return remote(extra.at[i], small_in.at[i], tiny_send.at[i], tiny_recv.at[i], partners[i])

    def tiny_start(i):
        extra[i] = small[...]
        tiny(i).start()

    def tiny_end(i):
        tiny(i).wait_recv()
        for layer in range(2):
            small[layer, 0:4] = extra[i, layer, 0:4] + small_in[i, layer, 0:4]
            for row, other in enumerate(rows_beside[i]):
                at = row + 4
                small[layer, at : at + 1] = (
                    extra[i, layer, at : at + 1] + small_in[i, layer, other : other + 1]
                )

    def ends(layer, chunk):
        if chunk == 0:
            target, done = final_a.at[place.s], done_a
        else:
            target, done = final_b.at[place.s, chunk - 1], done_b.at[chunk - 1]
        source = reduce.line_sum[chunk] if layer == 0 else done
        here = pltpu.make_async_copy(source, target, end_local.at[layer, chunk])
        there = remote(
            source,
            target,
            end_send.at[layer, chunk],
            end_recv.at[layer, chunk],
            place.on(section=place.core),
        )
        return here, there

    def end_start(layer, chunk):
        here, there = ends(layer, chunk)

        @pl.when(place.s == layer)
        def _():
            here.start()

        @pl.when(place.s != layer)
        def _():
            there.start()

    def end_wait(layer, chunk):
        here, there = ends(layer, chunk)

        @pl.when(place.s == layer)
        def _():
            here.wait()
            there.wait_recv()

        @pl.when(place.s != layer)
        def _():
            there.wait_send()

    for chunk in range(3):
        reduce.start(chunk)
    spread_one.begin()
    spread_zero.begin()
    tiny_start(0)
    reduce.load(0)
    reduce.load(1)
    spread_one.hops()
    reduce.load(2)
    tiny_end(0)
    tiny_start(1)
    for chunk in range(3):
        end_start(1, chunk)
    reduce.middle(0)
    reduce.middle(1)
    spread_zero.hops()
    tiny_end(1)
    tiny_start(2)
    reduce.middle(2)
    spread_one.forward()
    reduce.gather(0)
    reduce.line_one(0)
    reduce.gather(1)
    tiny_end(2)
    tiny_start(3)
    reduce.line_one(1)
    reduce.line_two(0)
    spread_zero.forward()
    reduce.gather(2)
    reduce.line_one(2)
    reduce.line_two(1)
    tiny_end(3)
    tiny_start(4)
    reduce.line_three(0)
    end_start(0, 0)
    spread_one.finish()
    spread_one.place_out(1, out)
    reduce.line_two(2)
    reduce.line_three(1)
    end_start(0, 1)
    spread_zero.finish()
    spread_zero.place_out(0, out)
    reduce.line_three(2)
    end_start(0, 2)
    tiny_end(4)
    for layer in range(2):
        for chunk in range(3):
            end_wait(layer, chunk)
    spread_zero.wait_out(0, out)
    spread_one.wait_out(1, out)
    spread_zero.drain()
    spread_one.drain()
    reduce.drain()
    for i in range(5):
        tiny(i).wait_send()


def call(kernel, name, number, ins, spaces, shapes, out_spaces, scratch, flops, moved):
    return pl.pallas_call(
        kernel,
        name=name,
        out_shape=[jax.ShapeDtypeStruct(shape, kind) for shape, kind in shapes],
        in_specs=spaces,
        out_specs=out_spaces,
        scratch_shapes=scratch,
        compiler_params=pltpu.CompilerParams(
            collective_id=number, has_side_effects=True, vmem_limit_bytes=62 * 1024 * 1024
        ),
        cost_estimate=pl.CostEstimate(
            flops=flops, bytes_accessed=moved, transcendentals=20_000_000
        ),
    )(*ins)


def run_backward(full_a, full_b, seeded, tokens, low_both, q, kv, att, mid, hid, gains, bias, tables):
    low, full, count = jnp.bfloat16, jnp.float32, 2 * PIECE
    width, units = full_a.shape[-1], hid.shape[-1]
    tiles = (8, width, units // 8)
    grads = [
        ((2, 2, width, width), low),
        ((2,) + tiles, low),
        ((count, width), low),
        ((8, width), full),
    ]
    out = ((2, 4, count, width), low)
    stage = pltpu.VMEM((4, 2, PIECE, width), low)
    dma = pltpu.SemaphoreType.DMA
    common = (q, kv, att, mid, hid, gains, bias, *tables)
    common_spaces = [HBM] * 9 + [VMEM] * 4
    second = call(
        second_kernel,
        "backward_second",
        2,
        (full_a, full_b, seeded, tokens) + common + (low_both,),
        common_spaces + [HBM],
        grads + [out],
        [HBM] * 3 + [VMEM, HBM],
        backward_buffers(width, units)
        + [stage, stage]
        + backward_sems()
        + spread_sems()
        + spread_sems(),
        40_000_000_000,
        80_000_000,
    )
    grads_a, grads_b, grad_one, small_one, layer_out = second
    by_shard = (2, 2, 4, 192, width)
    halves = (2,) + tiles[1:]
    first = call(
        first_kernel,
        "backward_first",
        3,
        (full_a, full_b, grad_one, tokens) + common + (grads_a.reshape(by_shard), grads_b),
        common_spaces + [HBM] * 2,
        grads + [((2, 192, width), low), (halves, low)],
        [HBM] * 3 + [VMEM] + [HBM] * 2,
        backward_buffers(width, units)
        + reduce_buffers(width, True)
        + backward_sems()
        + reduce_sems()
        + [dma((3,))],
        40_000_000_000,
        80_000_000,
    )
    grads_a, grads_b, grad_zero, small_zero, done_a, done_b = first
    last = call(
        last_kernel,
        "sum_and_spread",
        4,
        (grads_a.reshape(by_shard), grads_b, grad_zero, grad_one, done_a, done_b, small_zero, small_one),
        [HBM] * 6 + [VMEM] * 2,
        [out, ((2, 2, 192, width), low), ((2,) + halves, low), ((2, 8, width), full)],
        [HBM] * 3 + [VMEM],
        reduce_buffers(width, False)
        + [stage, stage]
        + [pltpu.VMEM((5, 2, 8, width), full), pltpu.VMEM((5, 2, 8, width), full)]
        + reduce_sems()
        + spread_sems()
        + spread_sems()
        + [dma((2, 3)), dma((2, 3)), dma((2, 3)), dma((5,)), dma((5,))],
        100_000_000,
        40_000_000,
    )
    return layer_out, last[0], last[1], last[2], last[3]


def spread(
    layer_input,
    cotangent,
    doc_lengths,
    ln1_gain,
    w_qkv,
    w_out,
    ln2_gain,
    w_up,
    b_up,
    w_down,
    b_down,
):
    s, t, z = (lax.axis_index(name) for name in ("section", "tp", "seq"))
    micros, rows, width_pos, width = layer_input.shape
    half, group = z % 2, z // 2

    own_a = jnp.stack(
        [
            jnp.stack([w_qkv[0, :, 0].T, w_qkv[0, :, 1].T]),
            jnp.stack([w_qkv[0, :, 2].T, w_out[0]]),
        ]
    )
    shard = w_up.shape[-1]
    own_b = jnp.stack([w_up[0], w_down[0].T]).reshape(2, width, 2, shard // 2).transpose(0, 2, 1, 3)
    gains = jnp.concatenate([ln1_gain, ln2_gain, b_down, jnp.zeros((5, width), jnp.float32)])
    own_c = jnp.stack([gains, jnp.concatenate([b_up, jnp.zeros((7, width), jnp.float32)])])

    block = 2 * half + s
    lengths = doc_lengths.reshape(micros * rows, -1)
    lengths = lax.dynamic_index_in_dim(lengths, 4 * group + t, 0, keepdims=False)
    ends = jnp.cumsum(lengths)
    piece_pos = jnp.arange(PIECE)
    query_base = jnp.tile(block * PIECE + piece_pos, 2)
    key_base = jnp.concatenate([(block - 2 + i) * PIECE + piece_pos for i in (0, 1, 2, 2)])
    query_noisy = jnp.arange(2 * PIECE) < PIECE
    key_noisy = jnp.arange(4 * PIECE) >= 3 * PIECE

    def docs_of(base):
        return jnp.sum((base[:, None] >= ends[None, :]).astype(jnp.int32), axis=-1)

    query_block, key_block = query_base[:, None] // BLOCK, key_base[None, :] // BLOCK
    query_kind, key_kind = query_noisy[:, None], key_noisy[None, :]
    mask = (
        (query_kind & key_kind & (query_block == key_block))
        | (query_kind & ~key_kind & (key_block < query_block))
        | (~query_kind & ~key_kind & (key_block <= query_block))
    )
    mask = mask & (docs_of(query_base)[:, None] == docs_of(key_base)[None, :])
    mask = mask & (key_base >= 0)[None, :]
    bias = jnp.where(mask, 0.0, -1e30)
    frequency = 10000.0 ** (-jnp.arange(HDIM // 2).astype(jnp.float32) * 2.0 / HDIM)
    angles = query_base.astype(jnp.float32)[:, None] * frequency[None, :]
    cosine, sine_table = jnp.cos(angles), jnp.sin(angles)
    turn_cos = jnp.tile(cosine, (1, 4))
    turn_sin = jnp.tile(jnp.concatenate([-sine_table, sine_table], axis=1), (1, 2))

    flat = (micros * rows, width_pos, width)
    forward = run_forward(
        layer_input.reshape(flat), cotangent.reshape(flat), own_a, own_b, own_c, bias, turn_cos, turn_sin
    )
    full_a, full_b, gains, seeded, tokens, low_both, q, kv, att, mid, hid = forward
    bias_turned = bias.astype(jnp.bfloat16).T
    tables = (turn_cos, turn_sin)
    layer_out, input_grad, final_a, final_b, small = run_backward(
        full_a, full_b, seeded, tokens, low_both, q, kv, att, mid, hid, gains, bias_turned, tables
    )
    small = lax.dynamic_index_in_dim(small, s, 0, keepdims=False)
    final_a, final_b = final_a.astype(jnp.float32), final_b.astype(jnp.float32)
    grad_qkv = jnp.stack([final_a[0, 0].T, final_a[0, 1].T, final_a[1, 0].T], axis=1)
    grad_up, grad_down = final_b.transpose(0, 2, 1, 3).reshape(2, width, shard)
    out_shape = (1,) + layer_input.shape
    return (
        layer_out.reshape(out_shape),
        input_grad.reshape(out_shape),
        small[0:1],
        grad_qkv[None],
        final_a[1, 1][None],
        small[1:2],
        grad_up[None],
        small[4:5],
        grad_down.T[None],
        small[2:3],
    )


def solution(mesh):
    sizes = tuple(mesh.shape[name] for name in ("section", "tp", "seq"))
    local = spread if sizes == (2, 4, 4) else pipelined
    return jax.shard_map(
        local,
        mesh=mesh,
        in_specs=(
            P(None, None, "seq", None),
            P(None, None, "seq", None),
            P(),
            P("section", None),
            P("section", None, None, "tp"),
            P("section", "tp", None),
            P("section", None),
            P("section", None, "tp"),
            P("section", "tp"),
            P("section", "tp", None),
            P("section", None),
        ),
        out_specs=(
            P("section", None, None, "seq", None),
            P("section", None, None, "seq", None),
            P("section", None),
            P("section", None, None, "tp"),
            P("section", "tp", None),
            P("section", None),
            P("section", None, "tp"),
            P("section", "tp"),
            P("section", "tp", None),
            P("section", None),
        ),
        check_vma=False,
    )
```

```python
import jax
import jax.numpy as jnp
from jax import lax
from jax.experimental import pallas as pl
from jax.experimental.pallas import tpu as pltpu
from jax.sharding import PartitionSpec as P

HDIM = 64
BLOCK = 16
HALF = 1024


def from_behind(value, axis, by):
    size = lax.axis_size(axis)
    pairs = [(i, i + by) for i in range(size) if 0 <= i + by < size]
    return lax.ppermute(value, axis, pairs)


def layer_norm(values, gain):
    center = values - jnp.mean(values, axis=-1, keepdims=True)
    spread = jnp.mean(center * center, axis=-1, keepdims=True)
    return center * lax.rsqrt(spread + 1e-05) * gain


def rotate(values, cosine, sine_table):
    middle = values.shape[-1] // 2
    first_half = values[..., :middle]
    second_half = values[..., middle:]
    return jnp.concatenate(
        [
            first_half * cosine - second_half * sine_table,
            second_half * cosine + first_half * sine_table,
        ],
        axis=-1,
    )


def rotary_tables(positions):
    frequency = 10000.0 ** (-jnp.arange(HDIM // 2).astype(jnp.float32) * 2.0 / HDIM)
    angles = (positions % HALF).astype(jnp.float32)[:, None, None] * frequency[None, None, :]
    return (jnp.cos(angles), jnp.sin(angles))


def allowed(query_pos, query_doc, key_pos, key_doc):
    query_noisy = query_pos < HALF
    key_noisy = key_pos < HALF
    query_block = query_pos % HALF // BLOCK
    key_block = key_pos % HALF // BLOCK
    within = query_noisy & key_noisy & (query_block == key_block)
    earlier = query_noisy & ~key_noisy & (key_block < query_block)
    causal = ~query_noisy & ~key_noisy & (key_block <= query_block)
    return (within | earlier | causal) & (query_doc == key_doc)


def document_ids(doc_lengths):
    doc_ends = jnp.cumsum(doc_lengths, axis=-1)
    base_pos = jnp.arange(2 * HALF) % HALF
    return jnp.sum((base_pos[:, None] >= doc_ends[..., None, :]).astype(jnp.int32), axis=-1)


def gelu_tanh(values):
    return jax.nn.gelu(values, approximate=True)


def keep_slot(storage, value, slot_index, is_active):
    current = lax.dynamic_index_in_dim(storage, slot_index, 0, keepdims=False)
    return lax.dynamic_update_index_in_dim(
        storage, jnp.where(is_active, value, current), slot_index, 0
    )


def local_queries(inputs, ln_one, w_mix, tables):
    cosine, sine_table, query_pos = tables
    row_count, pos_count = (inputs.shape[0], inputs.shape[1])
    normed = layer_norm(inputs, ln_one).astype(jnp.bfloat16)
    mixed = jnp.einsum("rpd,dcf->rpcf", normed, w_mix, preferred_element_type=jnp.float32)
    shaped = mixed.reshape(row_count, pos_count, 3, -1, HDIM)
    queries = rotate(shaped[:, :, 0], cosine, sine_table).astype(jnp.bfloat16)
    keys_own = rotate(shaped[:, :, 1], cosine, sine_table).astype(jnp.bfloat16)
    values_own = shaped[:, :, 2].astype(jnp.bfloat16)
    return (normed, queries, keys_own, values_own)


def masked_scores(queries, keys_heads, query_pos, docs_all):
    pos_count = queries.shape[1]
    query_docs = lax.dynamic_slice_in_dim(docs_all, query_pos[0], pos_count, 1)
    key_pos = jnp.arange(keys_heads.shape[1])
    key_mask = allowed(
        query_pos[None, :, None],
        query_docs[:, :, None],
        key_pos[None, None, :],
        docs_all[:, None, :],
    )
    scores = (
        jnp.einsum("rqhd,rkhd->rhqk", queries, keys_heads, preferred_element_type=jnp.float32)
        * 0.125
    )
    return jnp.where(key_mask[:, None], scores, -1e30)


def forward_step(inputs, weights, tables, docs_all):
    ln_one, w_mix, w_proj, ln_two, w_first, b_first, w_second, b_second = weights
    row_count, pos_count = (inputs.shape[0], inputs.shape[1])
    normed, queries, keys_own, values_own = local_queries(inputs, ln_one, w_mix, tables)
    local_width = w_mix.shape[-1]
    keys_all, values_all = (
        lax.all_gather(
            keys_own.reshape(row_count, pos_count, local_width), "seq", axis=1, tiled=True
        ),
        lax.all_gather(
            values_own.reshape(row_count, pos_count, local_width), "seq", axis=1, tiled=True
        ),
    )
    keys_heads = keys_all.reshape(row_count, keys_all.shape[1], -1, HDIM)
    values_heads = values_all.reshape(row_count, values_all.shape[1], -1, HDIM)
    softmax_out = jax.nn.softmax(
        masked_scores(queries, keys_heads, tables[2], docs_all), axis=-1
    ).astype(jnp.bfloat16)
    attended = jnp.einsum(
        "rhqk,rkhd->rqhd", softmax_out, values_heads, preferred_element_type=jnp.float32
    )
    attended = attended.astype(jnp.bfloat16).reshape(row_count, pos_count, local_width)
    middle = inputs + lax.psum(
        jnp.einsum("rpe,ed->rpd", attended, w_proj, preferred_element_type=jnp.float32).astype(
            jnp.bfloat16
        ),
        "tp",
    ).astype(jnp.float32)
    normed_two = layer_norm(middle, ln_two).astype(jnp.bfloat16)
    hidden_pre = (
        jnp.einsum("rpd,df->rpf", normed_two, w_first, preferred_element_type=jnp.float32) + b_first
    )
    activated = gelu_tanh(hidden_pre).astype(jnp.bfloat16)
    second_terms = jnp.einsum(
        "rpf,fd->rpd", activated, w_second, preferred_element_type=jnp.float32
    )
    result = (
        middle + lax.psum(second_terms.astype(jnp.bfloat16), "tp").astype(jnp.float32) + b_second
    )
    return (result, middle, keys_all, values_all)


def backward_step(inputs, middle, grad_out, weights, tables, docs_all):
    ln_one, w_mix, w_proj, ln_two, w_first, b_first, w_second, b_second = weights
    cosine, sine_table, query_pos = tables
    row_count, pos_count = (inputs.shape[0], inputs.shape[1])
    local_width = w_mix.shape[-1]
    head_count = local_width // HDIM
    normed, queries, keys_own, values_own = local_queries(inputs, ln_one, w_mix, tables)
    keys_all, values_all = (
        lax.all_gather(
            keys_own.reshape(row_count, pos_count, local_width), "seq", axis=1, tiled=True
        ),
        lax.all_gather(
            values_own.reshape(row_count, pos_count, local_width), "seq", axis=1, tiled=True
        ),
    )
    keys_heads = keys_all.reshape(row_count, keys_all.shape[1], head_count, HDIM)
    values_heads = values_all.reshape(row_count, values_all.shape[1], head_count, HDIM)
    scores = masked_scores(queries, keys_heads, query_pos, docs_all)
    softmax_out = jax.nn.softmax(scores, axis=-1)
    probs_low = softmax_out.astype(jnp.bfloat16)
    attended = jnp.einsum(
        "rhqk,rkhd->rqhd", probs_low, values_heads, preferred_element_type=jnp.float32
    )
    attended = attended.astype(jnp.bfloat16).reshape(row_count, pos_count, local_width)
    normed_two = layer_norm(middle, ln_two).astype(jnp.bfloat16)
    hidden_pre = (
        jnp.einsum("rpd,df->rpf", normed_two, w_first, preferred_element_type=jnp.float32) + b_first
    )
    activated = gelu_tanh(hidden_pre).astype(jnp.bfloat16)
    grad_low = grad_out.astype(jnp.bfloat16)
    grad_b_second = jnp.sum(grad_out, axis=(0, 1))
    grad_w_second = jnp.einsum(
        "rpf,rpd->fd", activated, grad_low, preferred_element_type=jnp.float32
    )
    grad_act = jnp.einsum("rpd,fd->rpf", grad_low, w_second, preferred_element_type=jnp.float32)
    unused_value, gelu_back = jax.vjp(gelu_tanh, hidden_pre)
    grad_pre = gelu_back(grad_act)[0].astype(jnp.bfloat16)
    grad_b_first = jnp.sum(grad_pre, axis=(0, 1), dtype=jnp.float32)
    grad_w_first = jnp.einsum(
        "rpd,rpf->df", normed_two, grad_pre, preferred_element_type=jnp.float32
    )
    grad_normed_two = lax.psum(
        jnp.einsum("rpf,df->rpd", grad_pre, w_first, preferred_element_type=jnp.float32).astype(
            jnp.bfloat16
        ),
        "tp",
    ).astype(jnp.float32)
    unused_norm, second_back = jax.vjp(layer_norm, middle, ln_two)
    grad_middle_norm, grad_ln_two = second_back(grad_normed_two)
    grad_middle = grad_out + grad_middle_norm
    middle_low = grad_middle.astype(jnp.bfloat16)
    grad_w_proj = jnp.einsum(
        "rpe,rpd->ed", attended, middle_low, preferred_element_type=jnp.float32
    )
    grad_att = jnp.einsum("rpd,ed->rpe", middle_low, w_proj, preferred_element_type=jnp.float32)
    grad_att = grad_att.astype(jnp.bfloat16).reshape(row_count, pos_count, head_count, HDIM)
    grad_probs = jnp.einsum(
        "rqhd,rkhd->rhqk", grad_att, values_heads, preferred_element_type=jnp.float32
    )
    row_delta = jnp.sum(grad_probs * softmax_out, axis=-1, keepdims=True)
    grad_scores = (softmax_out * (grad_probs - row_delta)).astype(jnp.bfloat16)
    grad_queries = (
        jnp.einsum("rhqk,rkhd->rqhd", grad_scores, keys_heads, preferred_element_type=jnp.float32)
        * 0.125
    )
    full_len = keys_all.shape[1]
    part_keys = (
        jnp.einsum("rhqk,rqhd->rkhd", grad_scores, queries, preferred_element_type=jnp.float32)
        * 0.125
    )
    part_values = jnp.einsum(
        "rhqk,rqhd->rkhd", probs_low, grad_att, preferred_element_type=jnp.float32
    )
    grad_keys, grad_values = (
        lax.psum_scatter(
            part_keys.reshape(row_count, full_len, local_width).astype(jnp.bfloat16),
            "seq",
            scatter_dimension=1,
            tiled=True,
        ).astype(jnp.float32),
        lax.psum_scatter(
            part_values.reshape(row_count, full_len, local_width).astype(jnp.bfloat16),
            "seq",
            scatter_dimension=1,
            tiled=True,
        ).astype(jnp.float32),
    )
    grad_query_raw = rotate(grad_queries.astype(jnp.bfloat16), cosine, -sine_table)
    grad_key_raw = rotate(
        grad_keys.astype(jnp.bfloat16).reshape(row_count, pos_count, head_count, HDIM),
        cosine,
        -sine_table,
    )
    grad_mixed = jnp.stack(
        [
            grad_query_raw.reshape(row_count, pos_count, local_width).astype(jnp.bfloat16),
            grad_key_raw.reshape(row_count, pos_count, local_width).astype(jnp.bfloat16),
            grad_values.astype(jnp.bfloat16),
        ],
        axis=2,
    )
    grad_w_mix = jnp.einsum("rpd,rpcf->dcf", normed, grad_mixed, preferred_element_type=jnp.float32)
    grad_normed = lax.psum(
        jnp.einsum("rpcf,dcf->rpd", grad_mixed, w_mix, preferred_element_type=jnp.float32).astype(
            jnp.bfloat16
        ),
        "tp",
    ).astype(jnp.float32)
    unused_first, first_back = jax.vjp(layer_norm, inputs, ln_one)
    grad_in_norm, grad_ln_one = first_back(grad_normed)
    grad_inputs = grad_middle + grad_in_norm
    return (
        grad_inputs,
        (
            grad_ln_one,
            grad_w_mix,
            grad_w_proj,
            grad_ln_two,
            grad_w_first,
            grad_b_first,
            grad_w_second,
            grad_b_second,
        ),
    )


def pipelined(
    layer_input,
    cotangent,
    doc_lengths,
    ln1_gain,
    w_qkv,
    w_out,
    ln2_gain,
    w_up,
    b_up,
    w_down,
    b_down,
):
    weights = tuple(
        (weight[0] for weight in (ln1_gain, w_qkv, w_out, ln2_gain, w_up, b_up, w_down, b_down))
    )
    micros, row_count, pos_count, width_model = layer_input.shape
    sections = lax.axis_size("section")
    section_index = lax.axis_index("section")
    first_pos = lax.axis_index("seq") * pos_count
    query_pos = first_pos + jnp.arange(pos_count)
    cosine, sine_table = rotary_tables(query_pos)
    tables = (cosine, sine_table, query_pos)
    docs_every = document_ids(doc_lengths)
    kept_inputs = jnp.zeros((micros, row_count, pos_count, width_model), jnp.float32)
    kept_middle = jnp.zeros((micros, row_count, pos_count, width_model), jnp.float32)
    layer_out = jnp.zeros(layer_input.shape, jnp.bfloat16)
    arrived = jnp.zeros((row_count, pos_count, width_model), jnp.bfloat16)
    moments = micros + sections - 1
    for moment in range(moments):
        offset = moment - section_index
        micro_index = jnp.clip(offset, 0, micros - 1)
        is_active = (offset >= 0) & (offset < micros)
        own_input = layer_input[min(moment, micros - 1)]
        inputs = jnp.where(section_index == 0, own_input, arrived).astype(jnp.float32)
        result, middle, keys_all, values_all = forward_step(
            inputs, weights, tables, docs_every[micro_index]
        )
        kept_inputs = keep_slot(kept_inputs, inputs, micro_index, is_active)
        kept_middle = keep_slot(kept_middle, middle, micro_index, is_active)
        result_low = result.astype(jnp.bfloat16)
        layer_out = keep_slot(layer_out, result_low, micro_index, is_active)
        if moment < moments - 1:
            arrived = from_behind(result_low, "section", 1)
    grad_totals = tuple((jnp.zeros(weight.shape, jnp.float32) for weight in weights))
    input_grad = jnp.zeros(layer_input.shape, jnp.bfloat16)
    returned = jnp.zeros((row_count, pos_count, width_model), jnp.bfloat16)
    for moment in range(moments):
        offset = moment - (sections - 1 - section_index)
        micro_index = jnp.clip(offset, 0, micros - 1)
        is_active = (offset >= 0) & (offset < micros)
        incoming = jnp.where(
            section_index == sections - 1, cotangent[min(moment, micros - 1)], returned
        ).astype(jnp.float32)
        incoming = jnp.where(is_active, incoming, 0.0)
        grad_inputs, grad_parts = backward_step(
            kept_inputs[micro_index],
            kept_middle[micro_index],
            incoming,
            weights,
            tables,
            docs_every[micro_index],
        )
        grad_totals = tuple((total + piece for total, piece in zip(grad_totals, grad_parts)))
        grad_sent = grad_inputs.astype(jnp.bfloat16)
        input_grad = keep_slot(input_grad, grad_sent, micro_index, is_active)
        if moment < moments - 1:
            returned = from_behind(grad_sent, "section", -1)
    (
        grad_ln_one,
        grad_w_mix,
        grad_w_proj,
        grad_ln_two,
        grad_w_first,
        grad_b_first,
        grad_w_second,
        grad_b_second,
    ) = grad_totals
    summed = (
        lax.psum(grad_ln_one.astype(jnp.bfloat16), "seq").astype(jnp.float32),
        lax.psum(grad_w_mix.astype(jnp.bfloat16), "seq").astype(jnp.float32),
        lax.psum(grad_w_proj.astype(jnp.bfloat16), "seq").astype(jnp.float32),
        lax.psum(grad_ln_two.astype(jnp.bfloat16), "seq").astype(jnp.float32),
        lax.psum(grad_w_first.astype(jnp.bfloat16), "seq").astype(jnp.float32),
        lax.psum(grad_b_first.astype(jnp.bfloat16), "seq").astype(jnp.float32),
        lax.psum(grad_w_second.astype(jnp.bfloat16), "seq").astype(jnp.float32),
        lax.psum(grad_b_second.astype(jnp.bfloat16), "seq").astype(jnp.float32),
    )
    return (
        layer_out[None],
        input_grad[None],
        summed[0][None],
        summed[1][None],
        summed[2][None],
        summed[3][None],
        summed[4][None],
        summed[5][None],
        summed[6][None],
        summed[7][None],
    )


PIECE = 256
LANES = 256
MESH = pl.DeviceIdType.MESH
HBM = pl.BlockSpec(memory_space=pl.ANY)
VMEM = pl.BlockSpec(memory_space=pltpu.VMEM)


def dot_nn(left, right):
    return lax.dot_general(left, right, (((1,), (0,)), ((), ())), preferred_element_type=jnp.float32)


def dot_nt(left, right):
    return lax.dot_general(left, right, (((1,), (1,)), ((), ())), preferred_element_type=jnp.float32)


def dot_tn(left, right):
    return lax.dot_general(left, right, (((0,), (0,)), ((), ())), preferred_element_type=jnp.float32)


class Place:
    def __init__(self):
        self.s, self.t, self.z = (lax.axis_index(name) for name in ("section", "tp", "seq"))
        self.core = 1 - self.s
        self.half, self.group = self.z % 2, self.z // 2
        beside_x = self.t + 1 - 2 * (self.t % 2)
        beside_y = (self.t + 2) % 4
        self.beside_x, self.beside_y = beside_x, beside_y
        self.hop_one = beside_x * (1 - self.s) + beside_y * self.s
        self.hop_two = beside_y * (1 - self.s) + beside_x * self.s
        self.rel_one, self.rel_two = 1 + self.s, 2 - self.s
        self.far = (self.z + 2) % 4
        self.twin = self.z + 1 - 2 * self.half

    def on(self, section=None, tp=None, seq=None):
        return (
            self.s if section is None else section,
            self.t if tp is None else tp,
            self.z if seq is None else seq,
        )

    def partners(self):
        return [
            self.on(section=self.core),
            self.on(tp=self.beside_x),
            self.on(tp=self.beside_y),
            self.on(seq=self.far),
            self.on(seq=self.twin),
            self.on(seq=3 - self.z),
            self.on(section=self.core, seq=self.twin),
        ]

    def meet(self, partners):
        barrier = pltpu.get_barrier_semaphore()
        for partner in partners:
            pl.semaphore_signal(barrier, inc=1, device_id=partner, device_id_type=MESH)
        pl.semaphore_wait(barrier, len(partners))


def remote(source, target, send, receive, device):
    return pltpu.make_async_remote_copy(
        src_ref=source,
        dst_ref=target,
        send_sem=send,
        recv_sem=receive,
        device_id=device,
        device_id_type=MESH,
    )


def normalize(values):
    center = values - jnp.mean(values, axis=-1, keepdims=True)
    spread = jnp.mean(center * center, axis=-1, keepdims=True)
    scale = lax.rsqrt(spread + 1e-05)
    return center * scale, scale


def turn(values, cosine, sine_table):
    width = values.shape[-1]
    times = width // cosine.shape[-1]
    lane = lax.broadcasted_iota(jnp.int32, values.shape, 1) % HDIM
    ahead = pltpu.roll(values, width - HDIM // 2, 1)
    behind = pltpu.roll(values, HDIM // 2, 1)
    swapped = jnp.where(lane < HDIM // 2, ahead, behind)
    return values * jnp.tile(cosine, (1, times)) + swapped * jnp.tile(sine_table, (1, times))


def gelu(values):
    inner = 0.7978845608028654 * (values + 0.044715 * values * values * values)
    return 0.5 * values * (1.0 + jnp.tanh(inner))


def head_mask(head, scale):
    lane = lax.broadcasted_iota(jnp.int32, (1, LANES), 1)
    inside = (lane >= head * HDIM) & (lane < (head + 1) * HDIM)
    return jnp.where(inside, jnp.float32(scale), jnp.float32(0.0))


def attention_block(q_ref, keys, values_turned, bias, lse, turned):
    def one(head, _):
        rows = pl.ds(pl.multiple_of(head * HDIM, HDIM), HDIM)
        query = q_ref[...] * head_mask(head, 0.125).astype(jnp.bfloat16)
        scores = dot_nt(keys[...], query) + bias[...].astype(jnp.float32)
        top = jnp.max(scores, axis=0, keepdims=True)
        raised = jnp.exp(scores - top)
        total = jnp.sum(raised, axis=0, keepdims=True)
        lse[pl.ds(head, 1), :] = top + jnp.log(total)
        turned[rows, :] = dot_nn(values_turned[rows, :], raised.astype(jnp.bfloat16)) * (1.0 / total)
        return 0

    lax.fori_loop(0, LANES // HDIM, one, 0)
    return turned[...].T.astype(jnp.bfloat16)


class Weights:
    def __init__(self, place, own, full, sems):
        self.place, self.own, self.full = place, own, full
        (
            self.local,
            self.own_send,
            self.own_recv,
            self.hop_send,
            self.hop_recv,
            self.chip_send,
            self.chip_recv,
        ) = sems

    def source(self, chunk, pack):
        if chunk == 0:
            return self.own[0].at[pack]
        if chunk == 3:
            return self.own[2].at[pack]
        return self.own[1].at[pack, chunk - 1]

    def piece(self, layer, chunk, pack, rel):
        if chunk == 0:
            return self.full[0].at[layer, pack, :, pl.ds(pl.multiple_of(rel * 192, 64), 192)]
        if chunk == 3:
            return self.full[2].at[layer, pack, rel]
        return self.full[1].at[layer, pack, rel * 2 + chunk - 1]

    def own_copies(self, chunk, pack):
        s = self.place.s
        here = pltpu.make_async_copy(
            self.source(chunk, pack), self.piece(s, chunk, pack, 0), self.local.at[chunk, pack]
        )
        there = remote(
            self.source(chunk, pack),
            self.piece(s, chunk, pack, 0),
            self.own_send.at[chunk, pack],
            self.own_recv.at[chunk, pack],
            self.place.on(section=self.place.core),
        )
        return here, there

    def start_own(self, chunk):
        for pack in range(2):
            for copy in self.own_copies(chunk, pack):
                copy.start()

    def wait_own(self, layer, chunk):
        for pack in range(2):
            here, there = self.own_copies(chunk, pack)

            @pl.when(self.place.s == layer)
            def _():
                here.wait()

            @pl.when(self.place.s != layer)
            def _():
                there.wait_recv()

    def hops(self, layer, chunk):
        place = self.place
        own = self.piece(layer, chunk, place.s, 0)
        first = self.piece(layer, chunk, place.s, place.rel_one)
        second = self.piece(layer, chunk, place.s, place.rel_two)
        third = self.piece(layer, chunk, place.s, 3)
        moves = ((own, first, place.hop_one), (own, second, place.hop_two), (first, third, place.hop_two))
        return [
            remote(
                source,
                target,
                self.hop_send.at[layer, chunk, i],
                self.hop_recv.at[layer, chunk, i],
                place.on(tp=column),
            )
            for i, (source, target, column) in enumerate(moves)
        ]

    def chips(self, layer, chunk):
        place = self.place
        return [
            remote(
                self.piece(layer, chunk, place.s, rel),
                self.piece(layer, chunk, place.s, rel),
                self.chip_send.at[layer, chunk, i],
                self.chip_recv.at[layer, chunk, i],
                place.on(section=place.core),
            )
            for i, rel in enumerate((place.rel_one, place.rel_two, 3))
        ]

    def begin(self, layer, chunk):
        self.wait_own(layer, chunk)
        first, second, _ = self.hops(layer, chunk)
        first.start()
        second.start()

    def forward(self, layer, chunk):
        first, second, third = self.hops(layer, chunk)
        chips = self.chips(layer, chunk)
        first.wait_recv()
        third.start()
        chips[0].start()
        second.wait_recv()
        chips[1].start()

    def finish(self, layer, chunk):
        self.hops(layer, chunk)[2].wait_recv()
        self.chips(layer, chunk)[2].start()

    def need(self, layer, chunk):
        for copy in self.chips(layer, chunk):
            copy.wait_recv()

    def drain(self):
        for chunk in range(4):
            for pack in range(2):
                self.own_copies(chunk, pack)[1].wait_send()
            for layer in range(2):
                for copy in self.hops(layer, chunk) + self.chips(layer, chunk):
                    copy.wait_send()


class KeyShare:
    def __init__(self, place, kv, layer, sems):
        self.place, self.kv, self.layer = place, kv, layer
        self.near_send, self.near_recv, self.far_send, self.far_recv = sems
        s, odd = place.s, place.half == 1
        self.sends_near = (s == 0) | ~odd
        self.sends_far = (s == 0) & ~odd
        self.passes = (s == 0) & odd
        self.gets_near = (s == 1) | odd
        self.gets_far = odd

    def rows(self, start, part):
        lanes = pl.ds(part * LANES, LANES)
        return self.kv.at[self.layer, :, pl.ds(start, PIECE), lanes]

    def near(self, part):
        place = self.place
        return remote(
            self.rows(2 * PIECE, part),
            self.rows(PIECE, part),
            self.near_send.at[self.layer, part],
            self.near_recv.at[self.layer, part],
            place.on(section=place.core, seq=place.z + place.s * (1 - place.half)),
        )

    def far(self, part):
        place = self.place
        return remote(
            self.rows(2 * PIECE, part),
            self.rows(0, part),
            self.far_send.at[self.layer, part],
            self.far_recv.at[self.layer, part],
            place.on(seq=place.twin),
        )

    def last(self, part):
        place = self.place
        return remote(
            self.rows(PIECE, part),
            self.rows(0, part),
            self.far_send.at[self.layer, part],
            self.far_recv.at[self.layer, part],
            place.on(section=place.core),
        )

    def start(self, part):
        @pl.when(self.sends_near)
        def _():
            self.near(part).start()

        @pl.when(self.sends_far)
        def _():
            self.far(part).start()

    def arrive(self, part):
        @pl.when(self.gets_near)
        def _():
            self.near(part).wait_recv()

        @pl.when(self.passes)
        def _():
            self.last(part).start()

        @pl.when(self.gets_far)
        def _():
            self.far(part).wait_recv()

    def drain(self):
        for part in range(3):

            @pl.when(self.sends_near)
            def _():
                self.near(part).wait_send()

            @pl.when(self.sends_far)
            def _():
                self.far(part).wait_send()

            @pl.when(self.passes)
            def _():
                self.last(part).wait_send()


def forward_kernel(
    tokens,
    cotangent,
    own_a,
    own_b,
    own_c,
    bias,
    cosine,
    sine_table,
    full_a_out,
    full_b_out,
    gains_out,
    seeded_out,
    x_out,
    low_out,
    q_out,
    kv_out,
    att_out,
    mid_out,
    hid_out,
    lse_out,
    full_a,
    full_b,
    full_c,
    low,
    x,
    normed,
    q,
    kv,
    att,
    mid,
    hid,
    lse,
    values_turned,
    turned_att,
    *sems,
):
    weight_sems, key_sems = sems[:7], sems[7:11]
    token_sem, swap_send, swap_recv, seed_sem, seed_send, seed_recv, save_sem = sems[11:]
    place = Place()
    weights = Weights(place, (own_a, own_b, own_c), (full_a, full_b, full_c), weight_sems)
    lse[...] = jnp.zeros_like(lse)
    kv[:, :, : 2 * PIECE, :] = jnp.zeros((2, 2, 2 * PIECE, kv.shape[-1]), jnp.bfloat16)
    place.meet(place.partners())
    group_rows = pl.ds(pl.multiple_of(place.group * PIECE, PIECE), PIECE)
    columns = pl.ds(pl.multiple_of(place.s * PIECE, PIECE), PIECE)

    def bring(whole, target, here, send, receive):
        kept = whole.at[4 * place.group + place.t, columns]
        sent = whole.at[4 * (1 - place.group) + place.t, columns]
        target = target.at[group_rows]
        return (
            pltpu.make_async_copy(kept, target, here),
            remote(sent, target, send, receive, place.on(seq=place.far)),
        )

    own_tokens, swap = bring(tokens, low, token_sem, swap_send, swap_recv)
    own_seed, seed_swap = bring(cotangent, seeded_out, seed_sem, seed_send, seed_recv)
    own_tokens.start()
    swap.start()
    for chunk in (3, 0, 1, 2):
        weights.start_own(chunk)
    weights.begin(0, 0)
    weights.begin(0, 1)
    weights.begin(0, 3)
    weights.begin(1, 3)
    gains = full_c.at[:, 0, 0]
    gains_out[...] = full_c[:, 0, 0]
    own_tokens.wait()
    swap.wait()
    x_save = pltpu.make_async_copy(low, x_out, save_sem.at[16])
    x_save.start()
    x[...] = low[...].astype(jnp.float32)

    def saves(layer):
        pairs = [
            (low, low_out.at[layer]),
            (q, q_out.at[layer]),
            (kv.at[layer], kv_out.at[layer]),
            (att, att_out.at[layer]),
            (mid, mid_out.at[layer]),
            (hid, hid_out.at[layer]),
            (lse, lse_out.at[layer]),
        ]
        return [pltpu.make_async_copy(a, b, save_sem.at[i]) for i, (a, b) in enumerate(pairs)]

    def weight_saves(layer):
        copies = []
        for i, (a, b) in enumerate(((full_a, full_a_out), (full_b, full_b_out))):
            for pack in range(2):
                sem = save_sem.at[8 + 4 * layer + 2 * i + pack]
                copies.append(pltpu.make_async_copy(a.at[layer, pack], b.at[layer, pack], sem))
        return copies

    for layer in range(2):
        share = KeyShare(place, kv, layer, key_sems)
        unit, _ = normalize(x[...])
        normed[...] = (unit * gains[layer, 0:1]).astype(jnp.bfloat16)
        if layer == 0:
            weights.forward(0, 0)
            weights.begin(0, 2)
            weights.finish(0, 0)
        else:
            weights.forward(1, 0)
            weights.begin(1, 2)
            weights.finish(1, 0)
            for copy in saves(0)[1:]:
                copy.wait()
        weights.need(layer, 0)
        for copy in weight_saves(layer)[:2]:
            copy.start()
        for part in range(3):
            lanes = pl.ds(part * LANES, LANES)
            keep = normed[...]
            mixed = dot_nt(keep, full_a[layer, 0, 0, lanes, :])
            q[:, lanes] = turn(mixed, cosine[...], sine_table[...]).astype(jnp.bfloat16)
            mixed = dot_nt(keep, full_a[layer, 0, 1, lanes, :])
            mixed = turn(mixed, cosine[...], sine_table[...]).astype(jnp.bfloat16)
            kv[layer, 0, 2 * PIECE : 3 * PIECE, lanes] = mixed[PIECE:]
            kv[layer, 0, 3 * PIECE :, lanes] = mixed[:PIECE]
            mixed = dot_nt(keep, full_a[layer, 1, 0, lanes, :]).astype(jnp.bfloat16)
            kv[layer, 1, 2 * PIECE : 3 * PIECE, lanes] = mixed[PIECE:]
            kv[layer, 1, 3 * PIECE :, lanes] = mixed[:PIECE]
            share.start(part)
        if layer == 0:
            weights.forward(0, 3)
            weights.forward(1, 3)
            weights.finish(0, 3)
            weights.finish(1, 3)
            own_seed.start()
            weights.forward(0, 1)
            weights.begin(1, 0)
        else:
            weights.forward(1, 1)
        for part in range(3):
            lanes = pl.ds(part * LANES, LANES)
            share.arrive(part)
            values_turned[...] = kv[layer, 1, :, lanes].astype(jnp.float32).T.astype(jnp.bfloat16)
            for start, count in ((0, 4 * PIECE), (PIECE, 3 * PIECE)):
                queries = pl.ds(start, PIECE)
                att[queries, lanes] = attention_block(
                    q.at[queries, lanes],
                    kv.at[layer, 0, :count, lanes],
                    values_turned.at[:, :count],
                    bias.at[:count, queries],
                    lse.at[pl.ds(8 * part, 8), queries],
                    turned_att,
                )
            if part == 2 and layer == 0:
                seed_swap.start()
            if part == 0:
                weights.finish(layer, 1)
            elif part == 1:
                weights.forward(layer, 2)
                if layer == 0:
                    weights.begin(1, 1)
            else:
                weights.finish(layer, 2)
        for copy in saves(layer)[1:4] + saves(layer)[6:]:
            copy.start()

        def project(part, _):
            lanes = pl.ds(pl.multiple_of(part * LANES, LANES), LANES)
            mid[:, lanes] = x[:, lanes] + dot_nn(att[...], full_a[layer, 1, 1, :, lanes])
            return 0

        lax.fori_loop(0, 3, project, 0)
        unit, _ = normalize(mid[...])
        normed[...] = (unit * gains[layer, 1:2]).astype(jnp.bfloat16)
        x[...] = mid[...] + gains[layer, 2:3]
        saves(layer)[4].start()
        weights.need(layer, 3)
        for part in range(2):
            weights.need(layer, part + 1)
            if part == 1:
                for copy in weight_saves(layer)[2:]:
                    copy.start()

            def feed(rel, _):
                start = pl.multiple_of(rel * 768 + part * 384, 128)
                units = pl.ds(start, 384)
                shift = full_c[layer, 1, rel, 0:1, pl.ds(part * 384, 384)]
                tile = rel * 2 + part
                pre = dot_nn(normed[...], full_b[layer, 0, tile]) + shift
                hid[:, units] = pre.astype(jnp.bfloat16)
                active = gelu(pre).astype(jnp.bfloat16)
                x[...] += dot_nt(active, full_b[layer, 1, tile])
                return 0

            lax.fori_loop(0, 4, feed, 0)
        saves(layer)[5].start()
        if layer == 0:
            x_save.wait()
        else:
            saves(0)[0].wait()
        low[...] = x[...].astype(jnp.bfloat16)
        saves(layer)[0].start()
        x[...] = low[...].astype(jnp.float32)
    for copy in saves(1):
        copy.wait()
    for layer in range(2):
        for copy in weight_saves(layer):
            copy.wait()
        KeyShare(place, kv, layer, key_sems).drain()
    weights.drain()
    own_seed.wait()
    seed_swap.wait()


def run_forward(tokens, cotangent, own_a, own_b, own_c, bias, cosine, sine_table):
    shape = jax.ShapeDtypeStruct
    low_type, full_type = jnp.bfloat16, jnp.float32
    count = 2 * PIECE
    width = tokens.shape[-1]
    units = 8 * own_b.shape[-1]
    dma = pltpu.SemaphoreType.DMA
    return pl.pallas_call(
        forward_kernel,
        name="forward_layers",
        out_shape=[
            shape((2, 2, 2, width, width), low_type),
            shape((2, 2, 8, width, units // 8), low_type),
            shape((2, 8, width), full_type),
            shape((count, width), low_type),
            shape((count, width), low_type),
            shape((2, count, width), low_type),
            shape((2, count, width), low_type),
            shape((2, 2, 4 * PIECE, width), low_type),
            shape((2, count, width), low_type),
            shape((2, count, width), full_type),
            shape((2, count, units), low_type),
            shape((2, 24, count), full_type),
        ],
        in_specs=[HBM] * 5 + [VMEM] * 3,
        out_specs=[HBM] * 2 + [VMEM] + [HBM] * 9,
        scratch_shapes=[
            pltpu.VMEM((2, 2, 2, width, width), low_type),
            pltpu.VMEM((2, 2, 8, width, units // 8), low_type),
            pltpu.VMEM((2, 2, 4, 8, width), full_type),
            pltpu.VMEM((count, width), low_type),
            pltpu.VMEM((count, width), full_type),
            pltpu.VMEM((count, width), low_type),
            pltpu.VMEM((count, width), low_type),
            pltpu.VMEM((2, 2, 4 * PIECE, width), low_type),
            pltpu.VMEM((count, width), low_type),
            pltpu.VMEM((count, width), full_type),
            pltpu.VMEM((count, units), low_type),
            pltpu.VMEM((24, count), full_type),
            pltpu.VMEM((LANES, 4 * PIECE), low_type),
            pltpu.VMEM((LANES, PIECE), full_type),
            dma((4, 2)),
            dma((4, 2)),
            dma((4, 2)),
            dma((2, 4, 3)),
            dma((2, 4, 3)),
            dma((2, 4, 3)),
            dma((2, 4, 3)),
            dma((2, 3)),
            dma((2, 3)),
            dma((2, 3)),
            dma((2, 3)),
            dma,
            dma,
            dma,
            dma,
            dma,
            dma,
            dma((17,)),
        ],
        compiler_params=pltpu.CompilerParams(
            collective_id=1, has_side_effects=True, vmem_limit_bytes=62 * 1024 * 1024
        ),
        cost_estimate=pl.CostEstimate(
            flops=30_000_000_000, bytes_accessed=80_000_000, transcendentals=20_000_000
        ),
    )(tokens, cotangent, own_a, own_b, own_c, bias, cosine, sine_table)


def low_sum(*parts):
    total = parts[0].astype(jnp.float32)
    for part in parts[1:]:
        total = total + part.astype(jnp.float32)
    return total.astype(jnp.bfloat16)


class Spread:
    def __init__(self, place, source, stage, sems):
        self.place, self.source, self.stage = place, source, stage
        self.local, self.swap_send, self.swap_recv, self.hop_send, self.hop_recv = sems[:5]
        self.end_local, self.end_send, self.end_recv = sems[5:]

    def entry(self):
        place = self.place
        target = self.stage.at[0, place.group]
        kept = self.source.at[pl.ds(pl.multiple_of(place.group * PIECE, PIECE), PIECE)]
        sent = self.source.at[pl.ds(pl.multiple_of((1 - place.group) * PIECE, PIECE), PIECE)]
        here = pltpu.make_async_copy(kept, target, self.local)
        there = remote(sent, target, self.swap_send, self.swap_recv, place.on(seq=place.far))
        return here, there

    def begin(self):
        for copy in self.entry():
            copy.start()

    def moves(self):
        place, stage = self.place, self.stage
        first, second = stage.at[place.rel_one], stage.at[place.rel_two]
        listed = (
            (stage.at[0], first, place.hop_one),
            (stage.at[0], second, place.hop_two),
            (first, stage.at[3], place.hop_two),
        )
        return [
            remote(source, target, self.hop_send.at[i], self.hop_recv.at[i], place.on(tp=column))
            for i, (source, target, column) in enumerate(listed)
        ]

    def hops(self):
        here, there = self.entry()
        here.wait()
        there.wait_recv()
        first, second, _ = self.moves()
        first.start()
        second.start()

    def forward(self):
        first, _, third = self.moves()
        first.wait_recv()
        third.start()

    def finish(self):
        _, second, third = self.moves()
        second.wait_recv()
        third.wait_recv()

    def drain(self):
        self.entry()[1].wait_send()
        for copy in self.moves():
            copy.wait_send()

    def ends(self, out):
        place = self.place
        rows = pl.ds(pl.multiple_of(place.s * PIECE, PIECE), PIECE)
        pairs = []
        for i, column in enumerate((place.t, place.beside_x, place.beside_y, 3 - place.t)):
            source, target = self.stage.at[i], out.at[:, column, rows]
            here = pltpu.make_async_copy(source, target, self.end_local.at[i])
            there = remote(
                source, target, self.end_send.at[i], self.end_recv.at[i], place.on(section=place.core)
            )
            pairs.append((here, there))
        return pairs

    def place_out(self, layer, out):
        @pl.when(self.place.s == layer)
        def _():
            for here, _ in self.ends(out):
                here.start()

        @pl.when(self.place.s != layer)
        def _():
            for _, there in self.ends(out):
                there.start()

    def wait_out(self, layer, out):
        @pl.when(self.place.s == layer)
        def _():
            for here, there in self.ends(out):
                here.wait()
                there.wait_recv()

        @pl.when(self.place.s != layer)
        def _():
            for _, there in self.ends(out):
                there.wait_send()


def spread_sems():
    dma = pltpu.SemaphoreType.DMA
    return [dma, dma, dma, dma((3,)), dma((3,)), dma((4,)), dma((4,)), dma((4,))]


class Sum:
    def __init__(self, place, source, total, buffers, sems, loaded=False, opens=None, waits=None):
        self.place, self.source, self.total = place, source, total
        self.inbox, self.hop_in, self.line_in = buffers
        self.loaded, self.opens, self.waits = loaded, opens, waits
        (
            self.mine_sem,
            self.chip_send,
            self.chip_recv,
            self.hop_send,
            self.hop_recv,
            self.line_send,
            self.line_recv,
            self.end_local,
            self.end_send,
            self.end_recv,
        ) = sems
        z = place.z
        self.outer = (z == 0) | (z == 3)
        self.inner = (z == 1) | (z == 2)
        self.order = (3, 1, 2, 0)

    def mine(self, rel):
        return pltpu.make_async_copy(
            self.source(self.place.s, rel), self.total(rel), self.mine_sem.at[rel]
        )

    def other(self, rel):
        return remote(
            self.source(self.place.core, rel),
            self.inbox.at[rel],
            self.chip_send.at[rel],
            self.chip_recv.at[rel],
            self.place.on(section=self.place.core),
        )

    def start(self):
        if self.waits is not None:
            pl.semaphore_wait(self.waits, 1)
        for rel in self.order:
            self.other(rel).start()
            if self.loaded:
                self.mine(rel).start()

    def load(self):
        for rel in self.order:
            if self.loaded:
                self.mine(rel).wait()
            self.other(rel).wait_recv()
            total = self.total(rel)
            total[...] = low_sum(total[...], self.inbox[rel])
            if rel == 3:
                self.moves()[0].start()
            elif rel == 2:
                self.moves()[1].start()
        if self.opens is not None:
            pl.semaphore_signal(
                self.opens,
                inc=1,
                device_id=self.place.on(section=self.place.core),
                device_id_type=MESH,
            )

    def moves(self):
        place = self.place
        listed = (
            (3, 0, place.hop_two),
            (place.rel_two, 1, place.hop_two),
            (place.rel_one, 2, place.hop_one),
        )
        return [
            remote(
                self.total(rel),
                self.hop_in.at[slot],
                self.hop_send.at[slot],
                self.hop_recv.at[slot],
                place.on(tp=column),
            )
            for rel, slot, column in listed
        ]

    def middle(self):
        first, _, third = self.moves()
        first.wait_recv()
        total = self.total(self.place.rel_one)
        total[...] = low_sum(total[...], self.hop_in[0])
        third.start()

    def lines(self):
        place = self.place
        own, line_sum = self.total(0), self.total(1)
        listed = (
            (own, self.line_in.at[0], place.twin),
            (own, self.line_in.at[1], 3 - place.z),
            (line_sum, line_sum, place.twin),
        )
        return [
            remote(
                source,
                target,
                self.line_send.at[i],
                self.line_recv.at[i],
                place.on(seq=plane),
            )
            for i, (source, target, plane) in enumerate(listed)
        ]

    def gather(self):
        _, second, third = self.moves()
        second.wait_recv()
        third.wait_recv()
        total = self.total(0)
        total[...] = low_sum(total[...], self.hop_in[1], self.hop_in[2])
        second.wait_send()
        third.wait_send()

        @pl.when(self.outer)
        def _():
            self.lines()[0].start()

    def line_one(self):
        @pl.when(self.inner)
        def _():
            self.lines()[0].wait_recv()
            total = self.total(0)
            total[...] = low_sum(total[...], self.line_in[0])
            self.lines()[1].start()

    def line_two(self):
        @pl.when(self.inner)
        def _():
            self.lines()[1].wait_recv()
            self.total(1)[...] = low_sum(self.total(0)[...], self.line_in[1])
            self.lines()[2].start()

    def line_three(self):
        @pl.when(self.outer)
        def _():
            self.lines()[2].wait_recv()

    def ends(self, target):
        here = pltpu.make_async_copy(self.total(1), target, self.end_local)
        there = remote(
            self.total(1),
            target,
            self.end_send,
            self.end_recv,
            self.place.on(section=self.place.core),
        )
        return here, there

    def finish(self, layer, target):
        self.line_three()
        here, there = self.ends(target)

        @pl.when(self.place.s == layer)
        def _():
            here.start()

        @pl.when(self.place.s != layer)
        def _():
            there.start()

    def drain(self, layer, target):
        here, there = self.ends(target)

        @pl.when(self.place.s == layer)
        def _():
            here.wait()
            there.wait_recv()

        @pl.when(self.place.s != layer)
        def _():
            there.wait_send()

        for rel in range(4):
            self.other(rel).wait_send()
        self.moves()[0].wait_send()

        @pl.when(self.outer)
        def _():
            self.lines()[0].wait_send()

        @pl.when(self.inner)
        def _():
            self.lines()[1].wait_send()
            self.lines()[2].wait_send()


def sum_sems():
    dma = pltpu.SemaphoreType.DMA
    return [dma((4,))] * 3 + [dma((3,))] * 4 + [dma] * 3


SUM_SEMS = 10


def sum_buffers(piece, counts):
    return [pltpu.VMEM((count,) + piece, jnp.bfloat16) for count in counts]


def attention_sums(place, grads, buffers, sems):
    sums = []
    for i in range(2):
        total, inbox, hop_in, line_in = buffers[4 * i : 4 * i + 4]

        def source(pack, rel, i=i):
            return grads.at[pack, i, rel]

        def kept(rel, total=total):
            return total.at[rel]

        own_sems = sems[SUM_SEMS * i : SUM_SEMS * (i + 1)]
        sums.append(Sum(place, source, kept, (inbox, hop_in, line_in), own_sems, loaded=True))
    return sums


def feed_sums(place, wb, buffers, sems, gate):
    inbox, sums = buffers[0], []
    for i in range(2):

        def source(pack, rel, i=i):
            return wb.at[pack, rel * 2 + i]

        def kept(rel, i=i):
            return wb.at[place.s, rel * 2 + i]

        own_sems = sems[SUM_SEMS * i : SUM_SEMS * (i + 1)]
        gates = {"opens": gate} if i == 0 else {"waits": gate}
        parts = (inbox, buffers[1].at[i], buffers[2].at[i])
        sums.append(Sum(place, source, kept, parts, own_sems, **gates))
    return sums


def feed_buffers(piece):
    kind = jnp.bfloat16
    return [
        pltpu.VMEM((4,) + piece, kind),
        pltpu.VMEM((2, 3) + piece, kind),
        pltpu.VMEM((2, 2) + piece, kind),
    ]


class KeyReturn:
    def __init__(self, place, kv, near_in, far_in, sems):
        self.place, self.kv = place, kv
        self.near_in, self.far_in, self.pass_in = near_in, far_in, far_in
        (
            self.near_send,
            self.near_recv,
            self.far_send,
            self.far_recv,
            self.pass_send,
            self.pass_recv,
        ) = sems
        s, odd = place.s, place.half == 1
        self.is_third = (s == 0) & odd
        self.is_fourth = (s == 1) & odd
        self.is_second = (s == 1) & ~odd
        self.is_first = (s == 0) & ~odd

    def sources(self, start, part):
        return self.kv.at[:, pl.ds(start, PIECE), pl.ds(part * LANES, LANES)]

    def copies(self, part):
        place = self.place
        lanes = pl.ds(part * LANES, LANES)
        near = remote(
            self.sources(PIECE, part),
            self.near_in.at[:, :, lanes],
            self.near_send.at[part],
            self.near_recv.at[part],
            place.on(section=place.core, seq=place.z - (1 - place.s) * place.half),
        )
        far = remote(
            self.sources(0, part),
            self.far_in.at[:, :, lanes],
            self.far_send.at[part],
            self.far_recv.at[part],
            place.on(seq=place.twin),
        )
        passed = remote(
            self.sources(0, part),
            self.pass_in.at[:, :, lanes],
            self.pass_send.at[part],
            self.pass_recv.at[part],
            place.on(section=place.core),
        )
        return near, far, passed

    def start(self, part):
        near, far, passed = self.copies(part)

        @pl.when(self.is_fourth)
        def _():
            passed.start()
            near.start()

        @pl.when(self.is_second)
        def _():
            near.start()

        @pl.when(self.is_third)
        def _():
            far.start()

    def relay(self, part):
        near, _, passed = self.copies(part)
        lanes = pl.ds(part * LANES, LANES)

        @pl.when(self.is_third)
        def _():
            passed.wait_recv()
            self.kv[:, PIECE : 2 * PIECE, lanes] = low_sum(
                self.kv[:, PIECE : 2 * PIECE, lanes], self.pass_in[:, :, lanes]
            )
            near.start()

    def collect(self, part):
        near, far, _ = self.copies(part)
        lanes = pl.ds(part * LANES, LANES)
        clean = pl.ds(2 * PIECE, PIECE)

        @pl.when(~self.is_fourth)
        def _():
            near.wait_recv()
            self.kv[:, clean, lanes] = low_sum(self.kv[:, clean, lanes], self.near_in[:, :, lanes])

        @pl.when(self.is_first)
        def _():
            far.wait_recv()
            self.kv[:, clean, lanes] = low_sum(self.kv[:, clean, lanes], self.far_in[:, :, lanes])

    def drain(self):
        for part in range(3):
            near, far, passed = self.copies(part)

            @pl.when(self.is_fourth)
            def _():
                passed.wait_send()
                near.wait_send()

            @pl.when(self.is_second)
            def _():
                near.wait_send()

            @pl.when(self.is_third)
            def _():
                far.wait_send()
                near.wait_send()


def normalize_back(grads, unit, scale, gain):
    lifted = grads * gain
    mean = jnp.mean(lifted, axis=-1, keepdims=True)
    along = jnp.mean(lifted * unit, axis=-1, keepdims=True)
    return scale * (lifted - mean - unit * along)


def attention_back(q_ref, grad_ref, att_ref, keys, values, keys_turned, bias, lse, sums, turned, count):
    turned[...] = (grad_ref[...].astype(jnp.float32) * att_ref[...].astype(jnp.float32)).T

    def one(head, _):
        rows = pl.ds(pl.multiple_of(head * HDIM, HDIM), HDIM)
        query = q_ref[...] * head_mask(head, 0.125).astype(jnp.bfloat16)
        grad = grad_ref[...] * head_mask(head, 1.0).astype(jnp.bfloat16)
        delta = jnp.sum(turned[rows, :], axis=0, keepdims=True)
        scores = dot_nt(keys[...], query) + bias[...].astype(jnp.float32)
        probs = jnp.exp(scores - lse[pl.ds(head, 1), :])
        grad_scores = (probs * (dot_nt(values[...], grad) - delta)).astype(jnp.bfloat16)
        sums[0, :count] += dot_nn(grad_scores, query)
        sums[1, :count] += dot_nn(probs.astype(jnp.bfloat16), grad)
        turned[rows, :] = dot_nn(keys_turned[rows, :], grad_scores) * 0.125
        return 0

    lax.fori_loop(0, LANES // HDIM, one, 0)
    q_ref[...] = turned[...].T.astype(jnp.bfloat16)


def backward_layer(layer, refs, place, tick, key_sems, sems, tile_sems):
    (
        full_a,
        full_b,
        grad_in,
        x_in,
        q_in,
        kv_in,
        att_in,
        mid_in,
        hid_in,
        lse_in,
        gains,
        bias,
        cosine,
        sine_table,
        grads_a,
        grad_out,
        small_out,
        wa,
        wb,
        low,
        q,
        kv,
        att,
        mid,
        hid,
        grad,
        gathered,
        grad_low,
        grad_att,
        near_in,
        far_in,
        sums,
        keys_turned,
        turned_q,
        grad_turned,
        normed_turned,
        lse,
    ) = refs
    share = KeyReturn(place, kv, near_in, far_in, key_sems)
    pairs = [
        (grad_in, grad_low),
        (mid_in.at[layer], mid),
        (hid_in.at[layer], hid),
        (full_a.at[layer], wa),
        (att_in.at[layer], att),
        (q_in.at[layer], q),
        (kv_in.at[layer], kv),
        (x_in, low),
        (lse_in.at[layer], lse),
    ]
    loads = [pltpu.make_async_copy(a, b, sems.at[i]) for i, (a, b) in enumerate(pairs)]
    def tile_copy(pack, tile):
        return pltpu.make_async_copy(
            full_b.at[layer, pack, tile], wb.at[pack, tile], tile_sems.at[pack, tile]
        )

    for copy in loads[:3]:
        copy.start()
    for part in range(2):
        for rel in range(4):
            for pack in (1, 0):
                tile_copy(pack, rel * 2 + part).start()
    for copy in loads[3:]:
        copy.start()
    tick()
    gain_one, gain_two = gains[layer, 0:1], gains[layer, 1:2]
    for copy in loads[:3]:
        copy.wait()
    small_out[...] = jnp.zeros_like(small_out)

    def by_rows(step):
        def one(i, _):
            step(pl.ds(pl.multiple_of(i * 128, 128), 128))
            return 0

        lax.fori_loop(0, grad.shape[0] // 128, one, 0)

    def enter(rows):
        incoming = grad_low[rows, :].astype(jnp.float32)
        grad[rows, :] = incoming
        small_out[2:3] += jnp.sum(incoming, axis=0, keepdims=True)
        grad_turned[:, rows] = incoming.T.astype(jnp.bfloat16)
        unit, _ = normalize(mid[rows, :])
        normed_turned[:, rows] = (unit * gain_two).T.astype(jnp.bfloat16)
        gathered[rows, :] = jnp.zeros((128, grad.shape[1]), jnp.float32)

    by_rows(enter)
    tick()

    def feed(part, rel):
        start = pl.multiple_of(rel * 768 + part * 384, 128)
        units = pl.ds(start, 384)
        tile = rel * 2 + part
        pre = hid[:, units].astype(jnp.float32)
        squared = pre * pre
        bent = jnp.tanh(0.7978845608028654 * pre * (1.0 + 0.044715 * squared))
        raised = 0.5 * (1.0 + bent)
        active = (pre * raised).astype(jnp.bfloat16)
        slope = raised + 0.5 * pre * (1.0 - bent * bent) * (
            0.7978845608028654 * (1.0 + 3 * 0.044715 * squared)
        )
        tile_copy(1, tile).wait()
        grad_act = dot_nn(grad_low[...], wb[1, tile])
        grad_pre = (grad_act * slope).astype(jnp.bfloat16)
        total = jnp.sum(grad_pre.astype(jnp.float32), axis=0, keepdims=True)
        small_out[pl.ds(4 + rel, 1), pl.ds(part * 384, 384)] = total
        wb[1, tile] = dot_nn(grad_turned[...], active).astype(jnp.bfloat16)
        tile_copy(0, tile).wait()
        gathered[...] += dot_nt(grad_pre, wb[0, tile])
        wb[0, tile] = dot_nn(normed_turned[...], grad_pre).astype(jnp.bfloat16)

    for part in range(2):

        def one(rel, _):
            feed(part, rel)
            return 0

        lax.fori_loop(0, 4, one, 0)
        tick()

    def between(rows):
        found = gathered[rows, :]
        unit, scale = normalize(mid[rows, :])
        small_out[1:2] += jnp.sum(found * unit, axis=0, keepdims=True)
        total = grad[rows, :] + normalize_back(found, unit, scale, gain_two)
        grad[rows, :] = total
        grad_low[rows, :] = total.astype(jnp.bfloat16)

    by_rows(between)
    for copy in loads[3:]:
        copy.wait()

    def project(part, _):
        lanes = pl.ds(pl.multiple_of(part * LANES, LANES), LANES)
        grad_att[:, lanes] = dot_nt(grad_low[...], wa[1, 1, lanes, :]).astype(jnp.bfloat16)
        wa[1, 1, lanes, :] = dot_tn(att[:, lanes], grad_low[...]).astype(jnp.bfloat16)
        return 0

    lax.fori_loop(0, 3, project, 0)
    tick()
    for part in range(3):
        lanes = pl.ds(part * LANES, LANES)
        sums[...] = jnp.zeros_like(sums)
        keys_turned[...] = kv[0, :, lanes].astype(jnp.float32).T.astype(jnp.bfloat16)
        for start, count in ((0, 4 * PIECE), (PIECE, 3 * PIECE)):
            rows = pl.ds(start, PIECE)
            attention_back(
                q.at[rows, lanes],
                grad_att.at[rows, lanes],
                att.at[rows, lanes],
                kv.at[0, :count, lanes],
                kv.at[1, :count, lanes],
                keys_turned.at[:, :count],
                bias.at[:count, rows],
                lse.at[pl.ds(8 * part, 8), rows],
                sums,
                turned_q,
                count,
            )
            if start == 0:
                tick()
        kv[:, :, lanes] = sums[...].astype(jnp.bfloat16)
        share.start(part)
        if part > 0:
            share.relay(part - 1)
        tick()
    normed = grad_att

    def again(rows):
        unit, _ = normalize(low[rows, :].astype(jnp.float32))
        normed[rows, :] = (unit * gain_one).astype(jnp.bfloat16)

    by_rows(again)

    def turned(part, _):
        lanes = pl.ds(pl.multiple_of(part * LANES, LANES), LANES)
        raw = turn(q[:, lanes].astype(jnp.float32), cosine[...], -sine_table[...])
        raw = raw.astype(jnp.bfloat16)
        found = dot_nn(raw, wa[0, 0, lanes, :])

        @pl.when(part == 0)
        def _():
            gathered[...] = found

        @pl.when(part > 0)
        def _():
            gathered[...] += found

        wa[0, 0, lanes, :] = dot_tn(raw, normed[...]).astype(jnp.bfloat16)
        return 0

    lax.fori_loop(0, 3, turned, 0)
    share.relay(2)
    tick()
    for part in range(3):
        share.collect(part)

    def keyed(part, _):
        lanes = pl.ds(pl.multiple_of(part * LANES, LANES), LANES)
        noisy, clean = pl.ds(3 * PIECE, PIECE), pl.ds(2 * PIECE, PIECE)
        raw = jnp.concatenate([kv[0, noisy, lanes], kv[0, clean, lanes]], axis=0)
        raw = turn(raw.astype(jnp.float32), cosine[...], -sine_table[...]).astype(jnp.bfloat16)
        gathered[...] += dot_nn(raw, wa[0, 1, lanes, :])
        wa[0, 1, lanes, :] = dot_tn(raw, normed[...]).astype(jnp.bfloat16)
        raw = jnp.concatenate([kv[1, noisy, lanes], kv[1, clean, lanes]], axis=0)
        gathered[...] += dot_nn(raw, wa[1, 0, lanes, :])
        wa[1, 0, lanes, :] = dot_tn(raw, normed[...]).astype(jnp.bfloat16)
        return 0

    lax.fori_loop(0, 3, keyed, 0)
    save_a = pltpu.make_async_copy(wa, grads_a, sems.at[10])
    save_a.start()

    def leave(rows):
        found = gathered[rows, :]
        unit, scale = normalize(low[rows, :].astype(jnp.float32))
        small_out[0:1] += jnp.sum(found * unit, axis=0, keepdims=True)
        total = grad[rows, :] + normalize_back(found, unit, scale, gain_one)
        grad_low[rows, :] = total.astype(jnp.bfloat16)

    by_rows(leave)
    save_grad = pltpu.make_async_copy(grad_low, grad_out, sems.at[11])
    save_grad.start()
    tick()
    share.drain()
    save_a.wait()
    save_grad.wait()


class Ticks:
    def __init__(self, groups):
        self.groups = list(groups)

    def __call__(self):
        if self.groups:
            for step in self.groups.pop(0):
                step()

    def rest(self):
        while self.groups:
            self()


def backward_buffers(width, units):
    low, full, count = jnp.bfloat16, jnp.float32, 2 * PIECE
    return [
        pltpu.VMEM((2, 2, width, width), low),
        pltpu.VMEM((2, 8, width, units // 8), low),
        pltpu.VMEM((count, width), low),
        pltpu.VMEM((count, width), low),
        pltpu.VMEM((2, 4 * PIECE, width), low),
        pltpu.VMEM((count, width), low),
        pltpu.VMEM((count, width), full),
        pltpu.VMEM((count, units), low),
        pltpu.VMEM((count, width), full),
        pltpu.VMEM((count, width), full),
        pltpu.VMEM((count, width), low),
        pltpu.VMEM((count, width), low),
        pltpu.VMEM((2, PIECE, width), low),
        pltpu.VMEM((2, PIECE, width), low),
        pltpu.VMEM((2, 4 * PIECE, LANES), full),
        pltpu.VMEM((LANES, 4 * PIECE), low),
        pltpu.VMEM((LANES, PIECE), full),
        pltpu.VMEM((width, count), low),
        pltpu.VMEM((width, count), low),
        pltpu.VMEM((24, count), full),
    ]


def backward_sems():
    dma = pltpu.SemaphoreType.DMA
    return [dma((3,))] * 6 + [dma((12,)), dma((2, 8))]


BUFFERS = 20


def second_kernel(*refs):
    ins, refs = refs[:15], refs[15:]
    (grads_a, grad_out, small_out, out, final_b), refs = refs[:5], refs[5:]
    buffers, stages, feed, refs = refs[:BUFFERS], refs[BUFFERS : BUFFERS + 2], refs[22:25], refs[25:]
    sems, feed_sem, gate = refs[:24], refs[24:-1], refs[-1]
    low_both = ins[14]
    place = Place()
    place.meet(place.partners())
    spreads = [
        Spread(place, low_both.at[i], stages[i], sems[8 + 8 * i : 16 + 8 * i]) for i in range(2)
    ]
    one, two = feed_sums(place, buffers[1], feed, feed_sem, gate)
    tick = Ticks(
        [
            [spreads[0].begin, spreads[1].begin],
            [spreads[0].hops],
            [one.start],
            [one.load, two.start],
            [two.load, spreads[0].forward],
            [one.middle],
            [two.middle, spreads[0].finish, lambda: spreads[0].place_out(0, out)],
            [one.gather, spreads[1].hops],
            [one.line_one, two.gather],
            [one.line_two, two.line_one],
            [two.line_two, spreads[1].forward],
            [lambda: one.finish(1, final_b.at[place.s, 0])],
            [
                lambda: two.finish(1, final_b.at[place.s, 1]),
                spreads[1].finish,
                lambda: spreads[1].place_out(1, out),
            ],
        ]
    )
    body = ins[:3] + (low_both.at[0],) + ins[4:14] + (grads_a, grad_out, small_out) + buffers
    backward_layer(1, body, place, tick, sems[:6], sems[6], sems[7])
    tick.rest()
    for i in range(2):
        spreads[i].drain()
        spreads[i].wait_out(i, out)
    one.drain(1, final_b.at[place.s, 0])
    two.drain(1, final_b.at[place.s, 1])


def first_kernel(*refs):
    ins, refs = refs[:16], refs[16:]
    (grads_a, grad_out, small_out, out, final_a, final_b), refs = refs[:6], refs[6:]
    buffers, stage, refs = refs[:BUFFERS], refs[BUFFERS], refs[BUFFERS + 1 :]
    feed, held, refs = refs[:3], refs[3:11], refs[11:]
    sems, feed_sem, held_sem, gate = refs[:16], refs[16:36], refs[36:56], refs[56]
    prior, prior_grad = ins[14:]
    place = Place()
    place.meet(place.partners())
    spread_one = Spread(place, prior_grad, stage, sems[8:16])
    one, two = feed_sums(place, buffers[1], feed, feed_sem, gate)
    first, second = attention_sums(place, prior, held, held_sem)
    tick = Ticks(
        [
            [first.start, second.start, spread_one.begin],
            [first.load, second.load],
            [one.start, first.middle, second.middle, spread_one.hops],
            [one.load, two.start, first.gather, second.gather],
            [two.load, first.line_one, second.line_one, spread_one.forward],
            [one.middle, first.line_two, second.line_two],
            [
                two.middle,
                lambda: first.finish(1, final_a.at[place.s, 0]),
                lambda: second.finish(1, final_a.at[place.s, 1]),
            ],
            [one.gather, spread_one.finish, lambda: spread_one.place_out(1, out)],
            [one.line_one, two.gather],
            [one.line_two, two.line_one],
            [two.line_two],
            [lambda: one.finish(0, final_b.at[place.s, 0])],
            [lambda: two.finish(0, final_b.at[place.s, 1])],
        ]
    )
    body = ins[:14] + (grads_a, grad_out, small_out) + buffers
    backward_layer(0, body, place, tick, sems[:6], sems[6], sems[7])
    tick.rest()
    spread_one.drain()
    spread_one.wait_out(1, out)
    first.drain(1, final_a.at[place.s, 0])
    second.drain(1, final_a.at[place.s, 1])
    one.drain(0, final_b.at[place.s, 0])
    two.drain(0, final_b.at[place.s, 1])


def last_kernel(*refs):
    prior, grad_zero, small_zero, small_one, out, final_a, small = refs[:7]
    held, stage, (small_in, extra), sems = refs[7:15], refs[15], refs[16:18], refs[18:]
    held_sem, spread_sem, (tiny_send, tiny_recv) = sems[:20], sems[20:28], sems[28:]
    place = Place()
    place.meet(place.partners())
    first, second = attention_sums(place, prior, held, held_sem)
    spread_zero = Spread(place, grad_zero, stage, spread_sem)
    small[0], small[1] = small_zero[...], small_one[...]
    rows_beside = ((4, 5, 6, 7), (5, 4, 7, 6), (6, 7, 4, 5), (4, 5, 6, 7), (4, 5, 6, 7))
    partners = (
        place.on(section=place.core),
        place.on(tp=place.beside_x),
        place.on(tp=place.beside_y),
        place.on(seq=place.twin),
        place.on(seq=place.far),
    )

    def tiny(i):
        return remote(extra.at[i], small_in.at[i], tiny_send.at[i], tiny_recv.at[i], partners[i])

    def tiny_start(i):
        extra[i] = small[...]
        tiny(i).start()

    def tiny_end(i):
        tiny(i).wait_recv()
        for layer in range(2):
            small[layer, 0:4] = extra[i, layer, 0:4] + small_in[i, layer, 0:4]
            for row, other in enumerate(rows_beside[i]):
                at = row + 4
                small[layer, at : at + 1] = (
                    extra[i, layer, at : at + 1] + small_in[i, layer, other : other + 1]
                )

    tiny_start(0)
    first.start()
    second.start()
    spread_zero.begin()
    first.load()
    second.load()
    tiny_end(0)
    tiny_start(1)
    first.middle()
    second.middle()
    spread_zero.hops()
    tiny_end(1)
    tiny_start(2)
    first.gather()
    first.line_one()
    second.gather()
    second.line_one()
    tiny_end(2)
    tiny_start(3)
    first.line_two()
    second.line_two()
    spread_zero.forward()
    tiny_end(3)
    tiny_start(4)
    first.finish(0, final_a.at[place.s, 0])
    second.finish(0, final_a.at[place.s, 1])
    spread_zero.finish()
    spread_zero.place_out(0, out)
    tiny_end(4)
    first.drain(0, final_a.at[place.s, 0])
    second.drain(0, final_a.at[place.s, 1])
    spread_zero.wait_out(0, out)
    spread_zero.drain()
    for i in range(5):
        tiny(i).wait_send()


def call(kernel, name, number, ins, spaces, shapes, out_spaces, scratch, flops, moved):
    return pl.pallas_call(
        kernel,
        name=name,
        out_shape=[jax.ShapeDtypeStruct(shape, kind) for shape, kind in shapes],
        in_specs=spaces,
        out_specs=out_spaces,
        scratch_shapes=scratch,
        compiler_params=pltpu.CompilerParams(
            collective_id=number, has_side_effects=True, vmem_limit_bytes=62 * 1024 * 1024
        ),
        cost_estimate=pl.CostEstimate(
            flops=flops, bytes_accessed=moved, transcendentals=20_000_000
        ),
    )(*ins)


def run_backward(full_a, full_b, seeded, tokens, low_both, kept, gains, bias, tables):
    low, full, count = jnp.bfloat16, jnp.float32, 2 * PIECE
    width, units = full_a.shape[-1], 8 * full_b.shape[-1]
    grads = [
        ((2, 2, width, width), low),
        ((count, width), low),
        ((8, width), full),
    ]
    out = ((2, 4, count, width), low)
    row_piece, tile_piece = (192, width), (width, units // 8)
    final_a, final_b = ((2, 2) + row_piece, low), ((2, 2) + tile_piece, low)
    stage = pltpu.VMEM((4, 2, PIECE, width), low)
    dma, gate = pltpu.SemaphoreType.DMA, pltpu.SemaphoreType.REGULAR
    common = (*kept, gains, bias, *tables)
    common_spaces = [HBM] * 10 + [VMEM] * 4
    held = sum_buffers(row_piece, (4, 4, 3, 2) * 2)
    second = call(
        second_kernel,
        "backward_second",
        2,
        (full_a, full_b, seeded, tokens) + common + (low_both,),
        common_spaces + [HBM],
        grads + [out, final_b],
        [HBM] * 2 + [VMEM] + [HBM] * 2,
        backward_buffers(width, units)
        + [stage, stage]
        + feed_buffers(tile_piece)
        + backward_sems()
        + spread_sems()
        + spread_sems()
        + sum_sems()
        + sum_sems()
        + [gate],
        40_000_000_000,
        80_000_000,
    )
    grads_a, grad_one, small_one, layer_out, feed_one = second
    by_shard = (2, 2, 4, 192, width)
    first = call(
        first_kernel,
        "backward_first",
        3,
        (full_a, full_b, grad_one, tokens) + common + (grads_a.reshape(by_shard), grad_one),
        common_spaces + [HBM] * 2,
        grads + [out, final_a, final_b],
        [HBM] * 2 + [VMEM] + [HBM] * 3,
        backward_buffers(width, units)
        + [stage]
        + feed_buffers(tile_piece)
        + held
        + backward_sems()
        + spread_sems()
        + sum_sems()
        + sum_sems()
        + sum_sems()
        + sum_sems()
        + [gate],
        40_000_000_000,
        80_000_000,
    )
    grads_a, grad_zero, small_zero, out_one, rows_one, feed_zero = first
    last = call(
        last_kernel,
        "sum_and_spread",
        4,
        (grads_a.reshape(by_shard), grad_zero, small_zero, small_one),
        [HBM] * 2 + [VMEM] * 2,
        [out, final_a, ((2, 8, width), full)],
        [HBM] * 2 + [VMEM],
        held
        + [stage]
        + [pltpu.VMEM((5, 2, 8, width), full), pltpu.VMEM((5, 2, 8, width), full)]
        + sum_sems()
        + sum_sems()
        + spread_sems()
        + [dma((5,)), dma((5,))],
        100_000_000,
        40_000_000,
    )
    out_zero, rows_zero, small = last
    return layer_out, (out_zero, out_one), (rows_zero, rows_one), (feed_zero, feed_one), small


def spread(
    layer_input,
    cotangent,
    doc_lengths,
    ln1_gain,
    w_qkv,
    w_out,
    ln2_gain,
    w_up,
    b_up,
    w_down,
    b_down,
):
    s, t, z = (lax.axis_index(name) for name in ("section", "tp", "seq"))
    micros, rows, width_pos, width = layer_input.shape
    half, group = z % 2, z // 2

    own_a = jnp.stack(
        [
            jnp.stack([w_qkv[0, :, 0].T, w_qkv[0, :, 1].T]),
            jnp.stack([w_qkv[0, :, 2].T, w_out[0]]),
        ]
    )
    shard = w_up.shape[-1]
    own_b = jnp.stack([w_up[0], w_down[0].T]).reshape(2, width, 2, shard // 2).transpose(0, 2, 1, 3)
    gains = jnp.concatenate([ln1_gain, ln2_gain, b_down, jnp.zeros((5, width), jnp.float32)])
    own_c = jnp.stack([gains, jnp.concatenate([b_up, jnp.zeros((7, width), jnp.float32)])])

    block = 2 * half + s
    lengths = doc_lengths.reshape(micros * rows, -1)
    lengths = lax.dynamic_index_in_dim(lengths, 4 * group + t, 0, keepdims=False)
    ends = jnp.cumsum(lengths)
    piece_pos = jnp.arange(PIECE)
    query_base = jnp.tile(block * PIECE + piece_pos, 2)
    key_base = jnp.concatenate([(block - 2 + i) * PIECE + piece_pos for i in (0, 1, 2, 2)])
    query_noisy = jnp.arange(2 * PIECE) < PIECE
    key_noisy = jnp.arange(4 * PIECE) >= 3 * PIECE

    def docs_of(base):
        return jnp.sum((base[:, None] >= ends[None, :]).astype(jnp.int32), axis=-1)

    query_block, key_block = query_base[None, :] // BLOCK, key_base[:, None] // BLOCK
    query_kind, key_kind = query_noisy[None, :], key_noisy[:, None]
    mask = (
        (query_kind & key_kind & (query_block == key_block))
        | (query_kind & ~key_kind & (key_block < query_block))
        | (~query_kind & ~key_kind & (key_block <= query_block))
    )
    mask = mask & (docs_of(query_base)[None, :] == docs_of(key_base)[:, None])
    mask = mask & (key_base >= 0)[:, None]
    bias = jnp.where(mask, 0.0, -1e30).astype(jnp.bfloat16)
    frequency = 10000.0 ** (-jnp.arange(HDIM // 2).astype(jnp.float32) * 2.0 / HDIM)
    angles = query_base.astype(jnp.float32)[:, None] * frequency[None, :]
    cosine, sine_table = jnp.cos(angles), jnp.sin(angles)
    turn_cos = jnp.tile(cosine, (1, 4))
    turn_sin = jnp.tile(jnp.concatenate([-sine_table, sine_table], axis=1), (1, 2))

    flat = (micros * rows, width_pos, width)
    forward = run_forward(
        layer_input.reshape(flat), cotangent.reshape(flat), own_a, own_b, own_c, bias, turn_cos, turn_sin
    )
    full_a, full_b, gains, seeded, tokens, low_both, *kept = forward
    tables = (turn_cos, turn_sin)
    layer_out, input_grads, rows_sums, feed_sums_both, small = run_backward(
        full_a, full_b, seeded, tokens, low_both, kept, gains, bias, tables
    )
    input_grad, final_a, final_b = (
        jnp.where(s == 0, *pair) for pair in (input_grads, rows_sums, feed_sums_both)
    )
    small = lax.dynamic_index_in_dim(small, s, 0, keepdims=False)
    final_a, final_b = final_a.astype(jnp.float32), final_b.astype(jnp.float32)
    grad_qkv = jnp.stack([final_a[0, 0].T, final_a[0, 1].T, final_a[1, 0].T], axis=1)
    grad_up, grad_down = final_b.transpose(0, 2, 1, 3).reshape(2, width, shard)
    out_shape = (1,) + layer_input.shape
    return (
        layer_out.reshape(out_shape),
        input_grad.reshape(out_shape),
        small[0:1],
        grad_qkv[None],
        final_a[1, 1][None],
        small[1:2],
        grad_up[None],
        small[4:5],
        grad_down.T[None],
        small[2:3],
    )


def solution(mesh):
    sizes = tuple(mesh.shape[name] for name in ("section", "tp", "seq"))
    local = spread if sizes == (2, 4, 4) else pipelined
    return jax.shard_map(
        local,
        mesh=mesh,
        in_specs=(
            P(None, None, "seq", None),
            P(None, None, "seq", None),
            P(),
            P("section", None),
            P("section", None, None, "tp"),
            P("section", "tp", None),
            P("section", None),
            P("section", None, "tp"),
            P("section", "tp"),
            P("section", "tp", None),
            P("section", None),
        ),
        out_specs=(
            P("section", None, None, "seq", None),
            P("section", None, None, "seq", None),
            P("section", None),
            P("section", None, None, "tp"),
            P("section", "tp", None),
            P("section", None),
            P("section", None, "tp"),
            P("section", "tp"),
            P("section", "tp", None),
            P("section", None),
        ),
        check_vma=False,
    )
```

```python
import jax
import jax.numpy as jnp
from jax import lax
from jax.experimental import pallas as pl
from jax.experimental.pallas import tpu as pltpu
from jax.sharding import PartitionSpec as P

HDIM = 64
BLOCK = 16
HALF = 1024


def from_behind(value, axis, by):
    size = lax.axis_size(axis)
    pairs = [(i, i + by) for i in range(size) if 0 <= i + by < size]
    return lax.ppermute(value, axis, pairs)


def layer_norm(values, gain):
    center = values - jnp.mean(values, axis=-1, keepdims=True)
    spread = jnp.mean(center * center, axis=-1, keepdims=True)
    return center * lax.rsqrt(spread + 1e-05) * gain


def rotate(values, cosine, sine_table):
    middle = values.shape[-1] // 2
    first_half = values[..., :middle]
    second_half = values[..., middle:]
    return jnp.concatenate(
        [
            first_half * cosine - second_half * sine_table,
            second_half * cosine + first_half * sine_table,
        ],
        axis=-1,
    )


def rotary_tables(positions):
    frequency = 10000.0 ** (-jnp.arange(HDIM // 2).astype(jnp.float32) * 2.0 / HDIM)
    angles = (positions % HALF).astype(jnp.float32)[:, None, None] * frequency[None, None, :]
    return (jnp.cos(angles), jnp.sin(angles))


def allowed(query_pos, query_doc, key_pos, key_doc):
    query_noisy = query_pos < HALF
    key_noisy = key_pos < HALF
    query_block = query_pos % HALF // BLOCK
    key_block = key_pos % HALF // BLOCK
    within = query_noisy & key_noisy & (query_block == key_block)
    earlier = query_noisy & ~key_noisy & (key_block < query_block)
    causal = ~query_noisy & ~key_noisy & (key_block <= query_block)
    return (within | earlier | causal) & (query_doc == key_doc)


def document_ids(doc_lengths):
    doc_ends = jnp.cumsum(doc_lengths, axis=-1)
    base_pos = jnp.arange(2 * HALF) % HALF
    return jnp.sum((base_pos[:, None] >= doc_ends[..., None, :]).astype(jnp.int32), axis=-1)


def gelu_tanh(values):
    return jax.nn.gelu(values, approximate=True)


def keep_slot(storage, value, slot_index, is_active):
    current = lax.dynamic_index_in_dim(storage, slot_index, 0, keepdims=False)
    return lax.dynamic_update_index_in_dim(
        storage, jnp.where(is_active, value, current), slot_index, 0
    )


def local_queries(inputs, ln_one, w_mix, tables):
    cosine, sine_table, query_pos = tables
    row_count, pos_count = (inputs.shape[0], inputs.shape[1])
    normed = layer_norm(inputs, ln_one).astype(jnp.bfloat16)
    mixed = jnp.einsum("rpd,dcf->rpcf", normed, w_mix, preferred_element_type=jnp.float32)
    shaped = mixed.reshape(row_count, pos_count, 3, -1, HDIM)
    queries = rotate(shaped[:, :, 0], cosine, sine_table).astype(jnp.bfloat16)
    keys_own = rotate(shaped[:, :, 1], cosine, sine_table).astype(jnp.bfloat16)
    values_own = shaped[:, :, 2].astype(jnp.bfloat16)
    return (normed, queries, keys_own, values_own)


def masked_scores(queries, keys_heads, query_pos, docs_all):
    pos_count = queries.shape[1]
    query_docs = lax.dynamic_slice_in_dim(docs_all, query_pos[0], pos_count, 1)
    key_pos = jnp.arange(keys_heads.shape[1])
    key_mask = allowed(
        query_pos[None, :, None],
        query_docs[:, :, None],
        key_pos[None, None, :],
        docs_all[:, None, :],
    )
    scores = (
        jnp.einsum("rqhd,rkhd->rhqk", queries, keys_heads, preferred_element_type=jnp.float32)
        * 0.125
    )
    return jnp.where(key_mask[:, None], scores, -1e30)


def forward_step(inputs, weights, tables, docs_all):
    ln_one, w_mix, w_proj, ln_two, w_first, b_first, w_second, b_second = weights
    row_count, pos_count = (inputs.shape[0], inputs.shape[1])
    normed, queries, keys_own, values_own = local_queries(inputs, ln_one, w_mix, tables)
    local_width = w_mix.shape[-1]
    keys_all, values_all = (
        lax.all_gather(
            keys_own.reshape(row_count, pos_count, local_width), "seq", axis=1, tiled=True
        ),
        lax.all_gather(
            values_own.reshape(row_count, pos_count, local_width), "seq", axis=1, tiled=True
        ),
    )
    keys_heads = keys_all.reshape(row_count, keys_all.shape[1], -1, HDIM)
    values_heads = values_all.reshape(row_count, values_all.shape[1], -1, HDIM)
    softmax_out = jax.nn.softmax(
        masked_scores(queries, keys_heads, tables[2], docs_all), axis=-1
    ).astype(jnp.bfloat16)
    attended = jnp.einsum(
        "rhqk,rkhd->rqhd", softmax_out, values_heads, preferred_element_type=jnp.float32
    )
    attended = attended.astype(jnp.bfloat16).reshape(row_count, pos_count, local_width)
    middle = inputs + lax.psum(
        jnp.einsum("rpe,ed->rpd", attended, w_proj, preferred_element_type=jnp.float32).astype(
            jnp.bfloat16
        ),
        "tp",
    ).astype(jnp.float32)
    normed_two = layer_norm(middle, ln_two).astype(jnp.bfloat16)
    hidden_pre = (
        jnp.einsum("rpd,df->rpf", normed_two, w_first, preferred_element_type=jnp.float32) + b_first
    )
    activated = gelu_tanh(hidden_pre).astype(jnp.bfloat16)
    second_terms = jnp.einsum(
        "rpf,fd->rpd", activated, w_second, preferred_element_type=jnp.float32
    )
    result = (
        middle + lax.psum(second_terms.astype(jnp.bfloat16), "tp").astype(jnp.float32) + b_second
    )
    return (result, middle, keys_all, values_all)


def backward_step(inputs, middle, grad_out, weights, tables, docs_all):
    ln_one, w_mix, w_proj, ln_two, w_first, b_first, w_second, b_second = weights
    cosine, sine_table, query_pos = tables
    row_count, pos_count = (inputs.shape[0], inputs.shape[1])
    local_width = w_mix.shape[-1]
    head_count = local_width // HDIM
    normed, queries, keys_own, values_own = local_queries(inputs, ln_one, w_mix, tables)
    keys_all, values_all = (
        lax.all_gather(
            keys_own.reshape(row_count, pos_count, local_width), "seq", axis=1, tiled=True
        ),
        lax.all_gather(
            values_own.reshape(row_count, pos_count, local_width), "seq", axis=1, tiled=True
        ),
    )
    keys_heads = keys_all.reshape(row_count, keys_all.shape[1], head_count, HDIM)
    values_heads = values_all.reshape(row_count, values_all.shape[1], head_count, HDIM)
    scores = masked_scores(queries, keys_heads, query_pos, docs_all)
    softmax_out = jax.nn.softmax(scores, axis=-1)
    probs_low = softmax_out.astype(jnp.bfloat16)
    attended = jnp.einsum(
        "rhqk,rkhd->rqhd", probs_low, values_heads, preferred_element_type=jnp.float32
    )
    attended = attended.astype(jnp.bfloat16).reshape(row_count, pos_count, local_width)
    normed_two = layer_norm(middle, ln_two).astype(jnp.bfloat16)
    hidden_pre = (
        jnp.einsum("rpd,df->rpf", normed_two, w_first, preferred_element_type=jnp.float32) + b_first
    )
    activated = gelu_tanh(hidden_pre).astype(jnp.bfloat16)
    grad_low = grad_out.astype(jnp.bfloat16)
    grad_b_second = jnp.sum(grad_out, axis=(0, 1))
    grad_w_second = jnp.einsum(
        "rpf,rpd->fd", activated, grad_low, preferred_element_type=jnp.float32
    )
    grad_act = jnp.einsum("rpd,fd->rpf", grad_low, w_second, preferred_element_type=jnp.float32)
    unused_value, gelu_back = jax.vjp(gelu_tanh, hidden_pre)
    grad_pre = gelu_back(grad_act)[0].astype(jnp.bfloat16)
    grad_b_first = jnp.sum(grad_pre, axis=(0, 1), dtype=jnp.float32)
    grad_w_first = jnp.einsum(
        "rpd,rpf->df", normed_two, grad_pre, preferred_element_type=jnp.float32
    )
    grad_normed_two = lax.psum(
        jnp.einsum("rpf,df->rpd", grad_pre, w_first, preferred_element_type=jnp.float32).astype(
            jnp.bfloat16
        ),
        "tp",
    ).astype(jnp.float32)
    unused_norm, second_back = jax.vjp(layer_norm, middle, ln_two)
    grad_middle_norm, grad_ln_two = second_back(grad_normed_two)
    grad_middle = grad_out + grad_middle_norm
    middle_low = grad_middle.astype(jnp.bfloat16)
    grad_w_proj = jnp.einsum(
        "rpe,rpd->ed", attended, middle_low, preferred_element_type=jnp.float32
    )
    grad_att = jnp.einsum("rpd,ed->rpe", middle_low, w_proj, preferred_element_type=jnp.float32)
    grad_att = grad_att.astype(jnp.bfloat16).reshape(row_count, pos_count, head_count, HDIM)
    grad_probs = jnp.einsum(
        "rqhd,rkhd->rhqk", grad_att, values_heads, preferred_element_type=jnp.float32
    )
    row_delta = jnp.sum(grad_probs * softmax_out, axis=-1, keepdims=True)
    grad_scores = (softmax_out * (grad_probs - row_delta)).astype(jnp.bfloat16)
    grad_queries = (
        jnp.einsum("rhqk,rkhd->rqhd", grad_scores, keys_heads, preferred_element_type=jnp.float32)
        * 0.125
    )
    full_len = keys_all.shape[1]
    part_keys = (
        jnp.einsum("rhqk,rqhd->rkhd", grad_scores, queries, preferred_element_type=jnp.float32)
        * 0.125
    )
    part_values = jnp.einsum(
        "rhqk,rqhd->rkhd", probs_low, grad_att, preferred_element_type=jnp.float32
    )
    grad_keys, grad_values = (
        lax.psum_scatter(
            part_keys.reshape(row_count, full_len, local_width).astype(jnp.bfloat16),
            "seq",
            scatter_dimension=1,
            tiled=True,
        ).astype(jnp.float32),
        lax.psum_scatter(
            part_values.reshape(row_count, full_len, local_width).astype(jnp.bfloat16),
            "seq",
            scatter_dimension=1,
            tiled=True,
        ).astype(jnp.float32),
    )
    grad_query_raw = rotate(grad_queries.astype(jnp.bfloat16), cosine, -sine_table)
    grad_key_raw = rotate(
        grad_keys.astype(jnp.bfloat16).reshape(row_count, pos_count, head_count, HDIM),
        cosine,
        -sine_table,
    )
    grad_mixed = jnp.stack(
        [
            grad_query_raw.reshape(row_count, pos_count, local_width).astype(jnp.bfloat16),
            grad_key_raw.reshape(row_count, pos_count, local_width).astype(jnp.bfloat16),
            grad_values.astype(jnp.bfloat16),
        ],
        axis=2,
    )
    grad_w_mix = jnp.einsum("rpd,rpcf->dcf", normed, grad_mixed, preferred_element_type=jnp.float32)
    grad_normed = lax.psum(
        jnp.einsum("rpcf,dcf->rpd", grad_mixed, w_mix, preferred_element_type=jnp.float32).astype(
            jnp.bfloat16
        ),
        "tp",
    ).astype(jnp.float32)
    unused_first, first_back = jax.vjp(layer_norm, inputs, ln_one)
    grad_in_norm, grad_ln_one = first_back(grad_normed)
    grad_inputs = grad_middle + grad_in_norm
    return (
        grad_inputs,
        (
            grad_ln_one,
            grad_w_mix,
            grad_w_proj,
            grad_ln_two,
            grad_w_first,
            grad_b_first,
            grad_w_second,
            grad_b_second,
        ),
    )


def pipelined(
    layer_input,
    cotangent,
    doc_lengths,
    ln1_gain,
    w_qkv,
    w_out,
    ln2_gain,
    w_up,
    b_up,
    w_down,
    b_down,
):
    weights = tuple(
        (weight[0] for weight in (ln1_gain, w_qkv, w_out, ln2_gain, w_up, b_up, w_down, b_down))
    )
    micros, row_count, pos_count, width_model = layer_input.shape
    sections = lax.axis_size("section")
    section_index = lax.axis_index("section")
    first_pos = lax.axis_index("seq") * pos_count
    query_pos = first_pos + jnp.arange(pos_count)
    cosine, sine_table = rotary_tables(query_pos)
    tables = (cosine, sine_table, query_pos)
    docs_every = document_ids(doc_lengths)
    kept_inputs = jnp.zeros((micros, row_count, pos_count, width_model), jnp.float32)
    kept_middle = jnp.zeros((micros, row_count, pos_count, width_model), jnp.float32)
    layer_out = jnp.zeros(layer_input.shape, jnp.bfloat16)
    arrived = jnp.zeros((row_count, pos_count, width_model), jnp.bfloat16)
    moments = micros + sections - 1
    for moment in range(moments):
        offset = moment - section_index
        micro_index = jnp.clip(offset, 0, micros - 1)
        is_active = (offset >= 0) & (offset < micros)
        own_input = layer_input[min(moment, micros - 1)]
        inputs = jnp.where(section_index == 0, own_input, arrived).astype(jnp.float32)
        result, middle, keys_all, values_all = forward_step(
            inputs, weights, tables, docs_every[micro_index]
        )
        kept_inputs = keep_slot(kept_inputs, inputs, micro_index, is_active)
        kept_middle = keep_slot(kept_middle, middle, micro_index, is_active)
        result_low = result.astype(jnp.bfloat16)
        layer_out = keep_slot(layer_out, result_low, micro_index, is_active)
        if moment < moments - 1:
            arrived = from_behind(result_low, "section", 1)
    grad_totals = tuple((jnp.zeros(weight.shape, jnp.float32) for weight in weights))
    input_grad = jnp.zeros(layer_input.shape, jnp.bfloat16)
    returned = jnp.zeros((row_count, pos_count, width_model), jnp.bfloat16)
    for moment in range(moments):
        offset = moment - (sections - 1 - section_index)
        micro_index = jnp.clip(offset, 0, micros - 1)
        is_active = (offset >= 0) & (offset < micros)
        incoming = jnp.where(
            section_index == sections - 1, cotangent[min(moment, micros - 1)], returned
        ).astype(jnp.float32)
        incoming = jnp.where(is_active, incoming, 0.0)
        grad_inputs, grad_parts = backward_step(
            kept_inputs[micro_index],
            kept_middle[micro_index],
            incoming,
            weights,
            tables,
            docs_every[micro_index],
        )
        grad_totals = tuple((total + piece for total, piece in zip(grad_totals, grad_parts)))
        grad_sent = grad_inputs.astype(jnp.bfloat16)
        input_grad = keep_slot(input_grad, grad_sent, micro_index, is_active)
        if moment < moments - 1:
            returned = from_behind(grad_sent, "section", -1)
    (
        grad_ln_one,
        grad_w_mix,
        grad_w_proj,
        grad_ln_two,
        grad_w_first,
        grad_b_first,
        grad_w_second,
        grad_b_second,
    ) = grad_totals
    summed = (
        lax.psum(grad_ln_one.astype(jnp.bfloat16), "seq").astype(jnp.float32),
        lax.psum(grad_w_mix.astype(jnp.bfloat16), "seq").astype(jnp.float32),
        lax.psum(grad_w_proj.astype(jnp.bfloat16), "seq").astype(jnp.float32),
        lax.psum(grad_ln_two.astype(jnp.bfloat16), "seq").astype(jnp.float32),
        lax.psum(grad_w_first.astype(jnp.bfloat16), "seq").astype(jnp.float32),
        lax.psum(grad_b_first.astype(jnp.bfloat16), "seq").astype(jnp.float32),
        lax.psum(grad_w_second.astype(jnp.bfloat16), "seq").astype(jnp.float32),
        lax.psum(grad_b_second.astype(jnp.bfloat16), "seq").astype(jnp.float32),
    )
    return (
        layer_out[None],
        input_grad[None],
        summed[0][None],
        summed[1][None],
        summed[2][None],
        summed[3][None],
        summed[4][None],
        summed[5][None],
        summed[6][None],
        summed[7][None],
    )


PIECE = 256
LANES = 256
MESH = pl.DeviceIdType.MESH
HBM = pl.BlockSpec(memory_space=pl.ANY)
VMEM = pl.BlockSpec(memory_space=pltpu.VMEM)


def dot_nn(left, right):
    return lax.dot_general(left, right, (((1,), (0,)), ((), ())), preferred_element_type=jnp.float32)


def dot_nt(left, right):
    return lax.dot_general(left, right, (((1,), (1,)), ((), ())), preferred_element_type=jnp.float32)


def dot_tn(left, right):
    return lax.dot_general(left, right, (((0,), (0,)), ((), ())), preferred_element_type=jnp.float32)


class Place:
    def __init__(self):
        self.s, self.t, self.z = (lax.axis_index(name) for name in ("section", "tp", "seq"))
        self.core = 1 - self.s
        self.half, self.group = self.z % 2, self.z // 2
        beside_x = self.t + 1 - 2 * (self.t % 2)
        beside_y = (self.t + 2) % 4
        self.beside_x, self.beside_y = beside_x, beside_y
        self.hop_one = beside_x * (1 - self.s) + beside_y * self.s
        self.hop_two = beside_y * (1 - self.s) + beside_x * self.s
        self.rel_one, self.rel_two = 1 + self.s, 2 - self.s
        self.far = (self.z + 2) % 4
        self.twin = self.z + 1 - 2 * self.half

    def on(self, section=None, tp=None, seq=None):
        return (
            self.s if section is None else section,
            self.t if tp is None else tp,
            self.z if seq is None else seq,
        )

    def partners(self):
        return [
            self.on(section=self.core),
            self.on(tp=self.beside_x),
            self.on(tp=self.beside_y),
            self.on(seq=self.far),
            self.on(seq=self.twin),
            self.on(seq=3 - self.z),
            self.on(section=self.core, seq=self.twin),
        ]

    def meet(self, partners):
        barrier = pltpu.get_barrier_semaphore()
        for partner in partners:
            pl.semaphore_signal(barrier, inc=1, device_id=partner, device_id_type=MESH)
        pl.semaphore_wait(barrier, len(partners))


def remote(source, target, send, receive, device):
    return pltpu.make_async_remote_copy(
        src_ref=source,
        dst_ref=target,
        send_sem=send,
        recv_sem=receive,
        device_id=device,
        device_id_type=MESH,
    )


def normalize(values):
    center = values - jnp.mean(values, axis=-1, keepdims=True)
    spread = jnp.mean(center * center, axis=-1, keepdims=True)
    scale = lax.rsqrt(spread + 1e-05)
    return center * scale, scale


def turn(values, cosine, sine_table):
    width = values.shape[-1]
    times = width // cosine.shape[-1]
    lane = lax.broadcasted_iota(jnp.int32, values.shape, 1) % HDIM
    ahead = pltpu.roll(values, width - HDIM // 2, 1)
    behind = pltpu.roll(values, HDIM // 2, 1)
    swapped = jnp.where(lane < HDIM // 2, ahead, behind)
    return values * jnp.tile(cosine, (1, times)) + swapped * jnp.tile(sine_table, (1, times))


def gelu(values):
    inner = 0.7978845608028654 * (values + 0.044715 * values * values * values)
    return 0.5 * values * (1.0 + jnp.tanh(inner))


def head_mask(head, scale):
    lane = lax.broadcasted_iota(jnp.int32, (1, LANES), 1)
    inside = (lane >= head * HDIM) & (lane < (head + 1) * HDIM)
    return jnp.where(inside, jnp.float32(scale), jnp.float32(0.0))


def attention_block(q_ref, keys, values_turned, bias, lse, turned):
    def one(head, _):
        rows = pl.ds(pl.multiple_of(head * HDIM, HDIM), HDIM)
        query = q_ref[...] * head_mask(head, 0.125).astype(jnp.bfloat16)
        scores = dot_nt(keys[...], query) + bias[...].astype(jnp.float32)
        top = jnp.max(scores, axis=0, keepdims=True)
        raised = jnp.exp(scores - top)
        total = jnp.sum(raised, axis=0, keepdims=True)
        lse[pl.ds(head, 1), :] = top + jnp.log(total)
        turned[rows, :] = dot_nn(values_turned[rows, :], raised.astype(jnp.bfloat16)) * (1.0 / total)
        return 0

    lax.fori_loop(0, LANES // HDIM, one, 0)
    return turned[...].T.astype(jnp.bfloat16)


class Weights:
    def __init__(self, place, own, full, sems):
        self.place, self.own, self.full = place, own, full
        (
            self.local,
            self.own_send,
            self.own_recv,
            self.hop_send,
            self.hop_recv,
            self.chip_send,
            self.chip_recv,
        ) = sems

    def source(self, chunk, pack):
        if chunk == 0:
            return self.own[0].at[pack]
        if chunk == 3:
            return self.own[2].at[pack]
        return self.own[1].at[pack, chunk - 1]

    def piece(self, layer, chunk, pack, rel):
        if chunk == 0:
            return self.full[0].at[layer, pack, :, pl.ds(pl.multiple_of(rel * 192, 64), 192)]
        if chunk == 3:
            return self.full[2].at[layer, pack, rel]
        return self.full[1].at[layer, pack, rel * 2 + chunk - 1]

    def own_copies(self, chunk, pack):
        s = self.place.s
        here = pltpu.make_async_copy(
            self.source(chunk, pack), self.piece(s, chunk, pack, 0), self.local.at[chunk, pack]
        )
        there = remote(
            self.source(chunk, pack),
            self.piece(s, chunk, pack, 0),
            self.own_send.at[chunk, pack],
            self.own_recv.at[chunk, pack],
            self.place.on(section=self.place.core),
        )
        return here, there

    def start_own(self, chunk):
        for pack in range(2):
            for copy in self.own_copies(chunk, pack):
                copy.start()

    def wait_own(self, layer, chunk):
        for pack in range(2):
            here, there = self.own_copies(chunk, pack)

            @pl.when(self.place.s == layer)
            def _():
                here.wait()

            @pl.when(self.place.s != layer)
            def _():
                there.wait_recv()

    def hops(self, layer, chunk):
        place = self.place
        own = self.piece(layer, chunk, place.s, 0)
        first = self.piece(layer, chunk, place.s, place.rel_one)
        second = self.piece(layer, chunk, place.s, place.rel_two)
        third = self.piece(layer, chunk, place.s, 3)
        moves = ((own, first, place.hop_one), (own, second, place.hop_two), (first, third, place.hop_two))
        return [
            remote(
                source,
                target,
                self.hop_send.at[layer, chunk, i],
                self.hop_recv.at[layer, chunk, i],
                place.on(tp=column),
            )
            for i, (source, target, column) in enumerate(moves)
        ]

    def chips(self, layer, chunk):
        place = self.place
        return [
            remote(
                self.piece(layer, chunk, place.s, rel),
                self.piece(layer, chunk, place.s, rel),
                self.chip_send.at[layer, chunk, i],
                self.chip_recv.at[layer, chunk, i],
                place.on(section=place.core),
            )
            for i, rel in enumerate((place.rel_one, place.rel_two, 3))
        ]

    def begin(self, layer, chunk):
        self.wait_own(layer, chunk)
        first, second, _ = self.hops(layer, chunk)
        first.start()
        second.start()

    def forward(self, layer, chunk):
        first, second, third = self.hops(layer, chunk)
        chips = self.chips(layer, chunk)
        first.wait_recv()
        third.start()
        chips[0].start()
        second.wait_recv()
        chips[1].start()

    def finish(self, layer, chunk):
        self.hops(layer, chunk)[2].wait_recv()
        self.chips(layer, chunk)[2].start()

    def need(self, layer, chunk):
        for copy in self.chips(layer, chunk):
            copy.wait_recv()

    def drain(self):
        for chunk in range(4):
            for pack in range(2):
                self.own_copies(chunk, pack)[1].wait_send()
            for layer in range(2):
                for copy in self.hops(layer, chunk) + self.chips(layer, chunk):
                    copy.wait_send()


class KeyShare:
    def __init__(self, place, kv, layer, sems):
        self.place, self.kv, self.layer = place, kv, layer
        self.near_send, self.near_recv, self.far_send, self.far_recv = sems
        s, odd = place.s, place.half == 1
        self.sends_near = (s == 0) | ~odd
        self.sends_far = (s == 0) & ~odd
        self.passes = (s == 0) & odd
        self.gets_near = (s == 1) | odd
        self.gets_far = odd

    def rows(self, start, part):
        lanes = pl.ds(part * LANES, LANES)
        return self.kv.at[self.layer, :, pl.ds(start, PIECE), lanes]

    def near(self, part):
        place = self.place
        return remote(
            self.rows(2 * PIECE, part),
            self.rows(PIECE, part),
            self.near_send.at[self.layer, part],
            self.near_recv.at[self.layer, part],
            place.on(section=place.core, seq=place.z + place.s * (1 - place.half)),
        )

    def far(self, part):
        place = self.place
        return remote(
            self.rows(2 * PIECE, part),
            self.rows(0, part),
            self.far_send.at[self.layer, part],
            self.far_recv.at[self.layer, part],
            place.on(seq=place.twin),
        )

    def last(self, part):
        place = self.place
        return remote(
            self.rows(PIECE, part),
            self.rows(0, part),
            self.far_send.at[self.layer, part],
            self.far_recv.at[self.layer, part],
            place.on(section=place.core),
        )

    def start(self, part):
        @pl.when(self.sends_near)
        def _():
            self.near(part).start()

        @pl.when(self.sends_far)
        def _():
            self.far(part).start()

    def arrive(self, part):
        @pl.when(self.gets_near)
        def _():
            self.near(part).wait_recv()

        @pl.when(self.passes)
        def _():
            self.last(part).start()

        @pl.when(self.gets_far)
        def _():
            self.far(part).wait_recv()

    def drain(self):
        for part in range(3):

            @pl.when(self.sends_near)
            def _():
                self.near(part).wait_send()

            @pl.when(self.sends_far)
            def _():
                self.far(part).wait_send()

            @pl.when(self.passes)
            def _():
                self.last(part).wait_send()


def forward_kernel(
    tokens,
    cotangent,
    own_a,
    own_b,
    own_c,
    bias,
    cosine,
    sine_table,
    full_a_out,
    full_b_out,
    gains_out,
    seeded_out,
    x_out,
    low_out,
    q_out,
    kv_out,
    att_out,
    mid_out,
    hid_out,
    lse_out,
    full_a,
    full_b,
    full_c,
    low,
    x,
    normed,
    q,
    kv,
    att,
    mid,
    hid,
    lse,
    values_turned,
    turned_att,
    *sems,
):
    weight_sems, key_sems = sems[:7], sems[7:11]
    token_sem, swap_send, swap_recv, seed_sem, seed_send, seed_recv, save_sem = sems[11:]
    place = Place()
    weights = Weights(place, (own_a, own_b, own_c), (full_a, full_b, full_c), weight_sems)
    lse[...] = jnp.zeros_like(lse)
    kv[:, :, : 2 * PIECE, :] = jnp.zeros((2, 2, 2 * PIECE, kv.shape[-1]), jnp.bfloat16)
    place.meet(place.partners())
    group_rows = pl.ds(pl.multiple_of(place.group * PIECE, PIECE), PIECE)
    columns = pl.ds(pl.multiple_of(place.s * PIECE, PIECE), PIECE)

    def bring(whole, target, here, send, receive):
        kept = whole.at[4 * place.group + place.t, columns]
        sent = whole.at[4 * (1 - place.group) + place.t, columns]
        target = target.at[group_rows]
        return (
            pltpu.make_async_copy(kept, target, here),
            remote(sent, target, send, receive, place.on(seq=place.far)),
        )

    own_tokens, swap = bring(tokens, low, token_sem, swap_send, swap_recv)
    own_seed, seed_swap = bring(cotangent, seeded_out, seed_sem, seed_send, seed_recv)
    own_tokens.start()
    swap.start()
    for chunk in (3, 0, 1, 2):
        weights.start_own(chunk)
    weights.begin(0, 0)
    weights.begin(0, 1)
    weights.begin(0, 3)
    weights.begin(1, 3)
    gains = full_c.at[:, 0, 0]
    gains_out[...] = full_c[:, 0, 0]
    own_tokens.wait()
    swap.wait()
    x_save = pltpu.make_async_copy(low, x_out, save_sem.at[16])
    x_save.start()
    x[...] = low[...].astype(jnp.float32)

    def saves(layer):
        pairs = [
            (low, low_out.at[layer]),
            (q, q_out.at[layer]),
            (kv.at[layer], kv_out.at[layer]),
            (att, att_out.at[layer]),
            (mid, mid_out.at[layer]),
            (hid, hid_out.at[layer]),
            (lse, lse_out.at[layer]),
        ]
        return [pltpu.make_async_copy(a, b, save_sem.at[i]) for i, (a, b) in enumerate(pairs)]

    def weight_saves(layer):
        copies = []
        for i, (a, b) in enumerate(((full_a, full_a_out), (full_b, full_b_out))):
            for pack in range(2):
                sem = save_sem.at[8 + 4 * layer + 2 * i + pack]
                copies.append(pltpu.make_async_copy(a.at[layer, pack], b.at[layer, pack], sem))
        return copies

    for layer in range(2):
        share = KeyShare(place, kv, layer, key_sems)
        unit, _ = normalize(x[...])
        normed[...] = (unit * gains[layer, 0:1]).astype(jnp.bfloat16)
        if layer == 0:
            weights.forward(0, 0)
            weights.begin(0, 2)
            weights.finish(0, 0)
        else:
            weights.forward(1, 0)
            weights.begin(1, 2)
            weights.finish(1, 0)
            for copy in saves(0)[1:]:
                copy.wait()
        weights.need(layer, 0)
        for copy in weight_saves(layer)[:2]:
            copy.start()
        for part in range(3):
            lanes = pl.ds(part * LANES, LANES)
            keep = normed[...]
            mixed = dot_nt(keep, full_a[layer, 0, 0, lanes, :])
            q[:, lanes] = turn(mixed, cosine[...], sine_table[...]).astype(jnp.bfloat16)
            mixed = dot_nt(keep, full_a[layer, 0, 1, lanes, :])
            mixed = turn(mixed, cosine[...], sine_table[...]).astype(jnp.bfloat16)
            kv[layer, 0, 2 * PIECE : 3 * PIECE, lanes] = mixed[PIECE:]
            kv[layer, 0, 3 * PIECE :, lanes] = mixed[:PIECE]
            mixed = dot_nt(keep, full_a[layer, 1, 0, lanes, :]).astype(jnp.bfloat16)
            kv[layer, 1, 2 * PIECE : 3 * PIECE, lanes] = mixed[PIECE:]
            kv[layer, 1, 3 * PIECE :, lanes] = mixed[:PIECE]
            share.start(part)
        if layer == 0:
            weights.forward(0, 3)
            weights.forward(1, 3)
            weights.finish(0, 3)
            weights.finish(1, 3)
            own_seed.start()
            weights.forward(0, 1)
            weights.begin(1, 0)
        else:
            weights.forward(1, 1)
        for part in range(3):
            lanes = pl.ds(part * LANES, LANES)
            share.arrive(part)
            values_turned[...] = kv[layer, 1, :, lanes].astype(jnp.float32).T.astype(jnp.bfloat16)
            for start, count in ((0, 4 * PIECE), (PIECE, 3 * PIECE)):
                queries = pl.ds(start, PIECE)
                att[queries, lanes] = attention_block(
                    q.at[queries, lanes],
                    kv.at[layer, 0, :count, lanes],
                    values_turned.at[:, :count],
                    bias.at[:count, queries],
                    lse.at[pl.ds(8 * part, 8), queries],
                    turned_att,
                )
            if part == 2 and layer == 0:
                seed_swap.start()
            if part == 0:
                weights.finish(layer, 1)
            elif part == 1:
                weights.forward(layer, 2)
                if layer == 0:
                    weights.begin(1, 1)
            else:
                weights.finish(layer, 2)
        for copy in saves(layer)[1:4] + saves(layer)[6:]:
            copy.start()

        def project(part, _):
            lanes = pl.ds(pl.multiple_of(part * LANES, LANES), LANES)
            mid[:, lanes] = x[:, lanes] + dot_nn(att[...], full_a[layer, 1, 1, :, lanes])
            return 0

        lax.fori_loop(0, 3, project, 0)
        unit, _ = normalize(mid[...])
        normed[...] = (unit * gains[layer, 1:2]).astype(jnp.bfloat16)
        x[...] = mid[...] + gains[layer, 2:3]
        saves(layer)[4].start()
        weights.need(layer, 3)
        for part in range(2):
            weights.need(layer, part + 1)
            if part == 1:
                for copy in weight_saves(layer)[2:]:
                    copy.start()

            def feed(rel, _):
                start = pl.multiple_of(rel * 768 + part * 384, 128)
                units = pl.ds(start, 384)
                shift = full_c[layer, 1, rel, 0:1, pl.ds(part * 384, 384)]
                tile = rel * 2 + part
                pre = dot_nn(normed[...], full_b[layer, 0, tile]) + shift
                hid[:, units] = pre.astype(jnp.bfloat16)
                active = gelu(pre).astype(jnp.bfloat16)
                x[...] += dot_nt(active, full_b[layer, 1, tile])
                return 0

            lax.fori_loop(0, 4, feed, 0)
        saves(layer)[5].start()
        if layer == 0:
            x_save.wait()
        else:
            saves(0)[0].wait()
        low[...] = x[...].astype(jnp.bfloat16)
        saves(layer)[0].start()
        x[...] = low[...].astype(jnp.float32)
    for copy in saves(1):
        copy.wait()
    for layer in range(2):
        for copy in weight_saves(layer):
            copy.wait()
        KeyShare(place, kv, layer, key_sems).drain()
    weights.drain()
    own_seed.wait()
    seed_swap.wait()


def run_forward(tokens, cotangent, own_a, own_b, own_c, bias, cosine, sine_table):
    shape = jax.ShapeDtypeStruct
    low_type, full_type = jnp.bfloat16, jnp.float32
    count = 2 * PIECE
    width = tokens.shape[-1]
    units = 8 * own_b.shape[-1]
    dma = pltpu.SemaphoreType.DMA
    return pl.pallas_call(
        forward_kernel,
        name="forward_layers",
        out_shape=[
            shape((2, 2, 2, width, width), low_type),
            shape((2, 2, 8, width, units // 8), low_type),
            shape((2, 8, width), full_type),
            shape((count, width), low_type),
            shape((count, width), low_type),
            shape((2, count, width), low_type),
            shape((2, count, width), low_type),
            shape((2, 2, 4 * PIECE, width), low_type),
            shape((2, count, width), low_type),
            shape((2, count, width), full_type),
            shape((2, count, units), low_type),
            shape((2, 24, count), full_type),
        ],
        in_specs=[HBM] * 5 + [VMEM] * 3,
        out_specs=[HBM] * 2 + [VMEM] + [HBM] * 9,
        scratch_shapes=[
            pltpu.VMEM((2, 2, 2, width, width), low_type),
            pltpu.VMEM((2, 2, 8, width, units // 8), low_type),
            pltpu.VMEM((2, 2, 4, 8, width), full_type),
            pltpu.VMEM((count, width), low_type),
            pltpu.VMEM((count, width), full_type),
            pltpu.VMEM((count, width), low_type),
            pltpu.VMEM((count, width), low_type),
            pltpu.VMEM((2, 2, 4 * PIECE, width), low_type),
            pltpu.VMEM((count, width), low_type),
            pltpu.VMEM((count, width), full_type),
            pltpu.VMEM((count, units), low_type),
            pltpu.VMEM((24, count), full_type),
            pltpu.VMEM((LANES, 4 * PIECE), low_type),
            pltpu.VMEM((LANES, PIECE), full_type),
            dma((4, 2)),
            dma((4, 2)),
            dma((4, 2)),
            dma((2, 4, 3)),
            dma((2, 4, 3)),
            dma((2, 4, 3)),
            dma((2, 4, 3)),
            dma((2, 3)),
            dma((2, 3)),
            dma((2, 3)),
            dma((2, 3)),
            dma,
            dma,
            dma,
            dma,
            dma,
            dma,
            dma((17,)),
        ],
        compiler_params=pltpu.CompilerParams(
            collective_id=1, has_side_effects=True, vmem_limit_bytes=62 * 1024 * 1024
        ),
        cost_estimate=pl.CostEstimate(
            flops=30_000_000_000, bytes_accessed=80_000_000, transcendentals=20_000_000
        ),
    )(tokens, cotangent, own_a, own_b, own_c, bias, cosine, sine_table)


def low_sum(*parts):
    total = parts[0].astype(jnp.float32)
    for part in parts[1:]:
        total = total + part.astype(jnp.float32)
    return total.astype(jnp.bfloat16)


class Spread:
    def __init__(self, place, source, stage, layer, out, sems):
        self.place, self.source, self.stage = place, source, stage
        self.layer, self.out = layer, out
        self.local, self.swap_send, self.swap_recv, self.hop_send, self.hop_recv = sems[:5]
        self.end_local, self.end_send, self.end_recv = sems[5:]
        self.groups = (place.group, 1 - place.group)

    def entry(self):
        place = self.place
        kept = self.source.at[pl.ds(pl.multiple_of(place.group * PIECE, PIECE), PIECE)]
        sent = self.source.at[pl.ds(pl.multiple_of((1 - place.group) * PIECE, PIECE), PIECE)]
        target = self.stage.at[0, place.group]
        here = pltpu.make_async_copy(kept, target, self.local)
        there = remote(sent, target, self.swap_send, self.swap_recv, place.on(seq=place.far))
        return here, there

    def take(self):
        self.entry()[0].start()

    def swap(self):
        self.entry()[1].start()

    def moves(self, half):
        place, group = self.place, self.groups[half]
        own = self.stage.at[0, group]
        first = self.stage.at[place.rel_one, group]
        second = self.stage.at[place.rel_two, group]
        third = self.stage.at[3, group]
        listed = (
            (own, first, place.hop_one),
            (own, second, place.hop_two),
            (first, third, place.hop_two),
        )
        return [
            remote(
                source,
                target,
                self.hop_send.at[half, i],
                self.hop_recv.at[half, i],
                place.on(tp=column),
            )
            for i, (source, target, column) in enumerate(listed)
        ]

    def hops(self, half):
        here, there = self.entry()
        if half == 0:
            here.wait()
        else:
            there.wait_recv()
        first, second, _ = self.moves(half)
        first.start()
        second.start()
        self.put(half, 0)

    def forward(self, half):
        first, _, third = self.moves(half)
        first.wait_recv()
        third.start()
        self.put(half, 1)

    def finish(self, half):
        _, second, third = self.moves(half)
        second.wait_recv()
        self.put(half, 2)
        third.wait_recv()
        self.put(half, 3)

    def ends(self, half, step):
        place, group = self.place, self.groups[half]
        rows = pl.ds(pl.multiple_of(place.s * PIECE, PIECE), PIECE)
        rel = (0, place.rel_one, place.rel_two, 3)[step]
        column = (place.t, place.hop_one, place.hop_two, 3 - place.t)[step]
        source, target = self.stage.at[rel, group], self.out.at[group, column, rows]
        here = pltpu.make_async_copy(source, target, self.end_local.at[half, step])
        there = remote(
            source,
            target,
            self.end_send.at[half, step],
            self.end_recv.at[half, step],
            place.on(section=place.core),
        )
        return here, there

    def put(self, half, step):
        @pl.when(self.place.s == self.layer)
        def _():
            self.ends(half, step)[0].start()

        @pl.when(self.place.s != self.layer)
        def _():
            self.ends(half, step)[1].start()

    def drain(self):
        self.entry()[1].wait_send()
        for half in range(2):
            for copy in self.moves(half):
                copy.wait_send()

        @pl.when(self.place.s == self.layer)
        def _():
            for half in range(2):
                for step in range(4):
                    here, there = self.ends(half, step)
                    here.wait()
                    there.wait_recv()

        @pl.when(self.place.s != self.layer)
        def _():
            for half in range(2):
                for step in range(4):
                    self.ends(half, step)[1].wait_send()


def spread_sems():
    dma = pltpu.SemaphoreType.DMA
    return [dma, dma, dma, dma((2, 3)), dma((2, 3)), dma((2, 4)), dma((2, 4)), dma((2, 4))]


class Sum:
    def __init__(self, place, source, total, buffers, sems, loaded=False, opens=None, waits=None):
        self.place, self.source, self.total = place, source, total
        self.inbox, self.hop_in, self.line_in = buffers
        self.loaded, self.opens, self.waits = loaded, opens, waits
        (
            self.mine_sem,
            self.chip_send,
            self.chip_recv,
            self.hop_send,
            self.hop_recv,
            self.line_send,
            self.line_recv,
            self.end_local,
            self.end_send,
            self.end_recv,
        ) = sems
        z = place.z
        self.outer = (z == 0) | (z == 3)
        self.inner = (z == 1) | (z == 2)
        self.order = (3, 1, 2, 0)

    def mine(self, rel):
        return pltpu.make_async_copy(
            self.source(self.place.s, rel), self.total(rel), self.mine_sem.at[rel]
        )

    def other(self, rel):
        return remote(
            self.source(self.place.core, rel),
            self.inbox.at[rel],
            self.chip_send.at[rel],
            self.chip_recv.at[rel],
            self.place.on(section=self.place.core),
        )

    def start(self):
        if self.waits is not None:
            pl.semaphore_wait(self.waits, 1)
        for rel in self.order:
            if self.inbox is not None:
                self.other(rel).start()
            if self.loaded:
                self.mine(rel).start()

    def load(self, travels=True):
        for rel in self.order:
            if self.loaded:
                self.mine(rel).wait()
            if self.inbox is not None:
                self.other(rel).wait_recv()
                total = self.total(rel)
                total[...] = low_sum(total[...], self.inbox[rel])
            if travels and rel == 3:
                self.moves()[0].start()
            elif travels and rel == 2:
                self.moves()[1].start()
        if self.opens is not None:
            pl.semaphore_signal(
                self.opens,
                inc=1,
                device_id=self.place.on(section=self.place.core),
                device_id_type=MESH,
            )

    def moves(self):
        place = self.place
        listed = (
            (3, 0, place.hop_two),
            (place.rel_two, 1, place.hop_two),
            (place.rel_one, 2, place.hop_one),
        )
        return [
            remote(
                self.total(rel),
                self.hop_in.at[slot],
                self.hop_send.at[slot],
                self.hop_recv.at[slot],
                place.on(tp=column),
            )
            for rel, slot, column in listed
        ]

    def middle(self):
        first, _, third = self.moves()
        first.wait_recv()
        total = self.total(self.place.rel_one)
        total[...] = low_sum(total[...], self.hop_in[0])
        third.start()

    def lines(self):
        place = self.place
        own, line_sum = self.total(0), self.total(1)
        listed = (
            (own, self.line_in.at[0], place.twin),
            (own, self.line_in.at[1], 3 - place.z),
            (line_sum, line_sum, place.twin),
        )
        return [
            remote(
                source,
                target,
                self.line_send.at[i],
                self.line_recv.at[i],
                place.on(seq=plane),
            )
            for i, (source, target, plane) in enumerate(listed)
        ]

    def gather(self):
        _, second, third = self.moves()
        second.wait_recv()
        third.wait_recv()
        total = self.total(0)
        total[...] = low_sum(total[...], self.hop_in[1], self.hop_in[2])
        second.wait_send()
        third.wait_send()

        @pl.when(self.outer)
        def _():
            self.lines()[0].start()

    def line_one(self):
        @pl.when(self.inner)
        def _():
            self.lines()[0].wait_recv()
            total = self.total(0)
            total[...] = low_sum(total[...], self.line_in[0])
            self.lines()[1].start()

    def line_two(self):
        @pl.when(self.inner)
        def _():
            self.lines()[1].wait_recv()
            self.total(1)[...] = low_sum(self.total(0)[...], self.line_in[1])
            self.lines()[2].start()

    def line_three(self):
        @pl.when(self.outer)
        def _():
            self.lines()[2].wait_recv()

    def ends(self, target):
        here = pltpu.make_async_copy(self.total(1), target, self.end_local)
        there = remote(
            self.total(1),
            target,
            self.end_send,
            self.end_recv,
            self.place.on(section=self.place.core),
        )
        return here, there

    def finish(self, layer, target):
        self.line_three()
        here, there = self.ends(target)

        @pl.when(self.place.s == layer)
        def _():
            here.start()

        @pl.when(self.place.s != layer)
        def _():
            there.start()

    def drain_exchange(self):
        if self.inbox is not None:
            for rel in range(4):
                self.other(rel).wait_send()

    def drain(self, layer, target):
        here, there = self.ends(target)

        @pl.when(self.place.s == layer)
        def _():
            here.wait()
            there.wait_recv()

        @pl.when(self.place.s != layer)
        def _():
            there.wait_send()

        self.drain_exchange()
        self.moves()[0].wait_send()

        @pl.when(self.outer)
        def _():
            self.lines()[0].wait_send()

        @pl.when(self.inner)
        def _():
            self.lines()[1].wait_send()
            self.lines()[2].wait_send()


def sum_sems():
    dma = pltpu.SemaphoreType.DMA
    return [dma((4,))] * 3 + [dma((3,))] * 4 + [dma] * 3


SUM_SEMS = 10


def sum_buffers(piece, counts):
    return [pltpu.VMEM((count,) + piece, jnp.bfloat16) for count in counts]


def attention_sums(place, grads, buffers, sems):
    sums = []
    for i in range(2):
        total, inbox, hop_in, line_in = buffers[4 * i : 4 * i + 4]

        def source(pack, rel, i=i):
            return grads.at[pack, i, rel]

        def kept(rel, total=total):
            return total.at[rel]

        own_sems = sems[SUM_SEMS * i : SUM_SEMS * (i + 1)]
        sums.append(Sum(place, source, kept, (inbox, hop_in, line_in), own_sems, loaded=True))
    return sums


def feed_sums(place, wb, buffers, sems, gate):
    inbox, sums = buffers[0], []
    for i in range(2):

        def source(pack, rel, i=i):
            return wb.at[pack, rel * 2 + i]

        def kept(rel, i=i):
            return wb.at[place.s, rel * 2 + i]

        own_sems = sems[SUM_SEMS * i : SUM_SEMS * (i + 1)]
        gates = {"opens": gate} if i == 0 else {"waits": gate}
        at = min(i, buffers[1].shape[0] - 1)
        parts = (inbox, buffers[1].at[at], buffers[2].at[at])
        sums.append(Sum(place, source, kept, parts, own_sems, **gates))
    return sums


def feed_buffers(piece, count):
    kind = jnp.bfloat16
    return [
        pltpu.VMEM((4,) + piece, kind),
        pltpu.VMEM((count, 3) + piece, kind),
        pltpu.VMEM((count, 2) + piece, kind),
    ]


class KeyReturn:
    def __init__(self, place, kv, near_in, far_in, sems):
        self.place, self.kv = place, kv
        self.near_in, self.far_in, self.pass_in = near_in, far_in, far_in
        (
            self.near_send,
            self.near_recv,
            self.far_send,
            self.far_recv,
            self.pass_send,
            self.pass_recv,
        ) = sems
        s, odd = place.s, place.half == 1
        self.is_third = (s == 0) & odd
        self.is_fourth = (s == 1) & odd
        self.is_second = (s == 1) & ~odd
        self.is_first = (s == 0) & ~odd

    def sources(self, start, part):
        return self.kv.at[:, pl.ds(start, PIECE), pl.ds(part * LANES, LANES)]

    def copies(self, part):
        place = self.place
        lanes = pl.ds(part * LANES, LANES)
        near = remote(
            self.sources(PIECE, part),
            self.near_in.at[:, :, lanes],
            self.near_send.at[part],
            self.near_recv.at[part],
            place.on(section=place.core, seq=place.z - (1 - place.s) * place.half),
        )
        far = remote(
            self.sources(0, part),
            self.far_in.at[:, :, lanes],
            self.far_send.at[part],
            self.far_recv.at[part],
            place.on(seq=place.twin),
        )
        passed = remote(
            self.sources(0, part),
            self.pass_in.at[:, :, lanes],
            self.pass_send.at[part],
            self.pass_recv.at[part],
            place.on(section=place.core),
        )
        return near, far, passed

    def start(self, part):
        near, far, passed = self.copies(part)

        @pl.when(self.is_fourth)
        def _():
            passed.start()
            near.start()

        @pl.when(self.is_second)
        def _():
            near.start()

        @pl.when(self.is_third)
        def _():
            far.start()

    def relay(self, part):
        near, _, passed = self.copies(part)
        lanes = pl.ds(part * LANES, LANES)

        @pl.when(self.is_third)
        def _():
            passed.wait_recv()
            self.kv[:, PIECE : 2 * PIECE, lanes] = low_sum(
                self.kv[:, PIECE : 2 * PIECE, lanes], self.pass_in[:, :, lanes]
            )
            near.start()

    def collect(self, part):
        near, far, _ = self.copies(part)
        lanes = pl.ds(part * LANES, LANES)
        clean = pl.ds(2 * PIECE, PIECE)

        @pl.when(~self.is_fourth)
        def _():
            near.wait_recv()
            self.kv[:, clean, lanes] = low_sum(self.kv[:, clean, lanes], self.near_in[:, :, lanes])

        @pl.when(self.is_first)
        def _():
            far.wait_recv()
            self.kv[:, clean, lanes] = low_sum(self.kv[:, clean, lanes], self.far_in[:, :, lanes])

    def drain(self):
        for part in range(3):
            near, far, passed = self.copies(part)

            @pl.when(self.is_fourth)
            def _():
                passed.wait_send()
                near.wait_send()

            @pl.when(self.is_second)
            def _():
                near.wait_send()

            @pl.when(self.is_third)
            def _():
                far.wait_send()
                near.wait_send()


def normalize_back(grads, unit, scale, gain):
    lifted = grads * gain
    mean = jnp.mean(lifted, axis=-1, keepdims=True)
    along = jnp.mean(lifted * unit, axis=-1, keepdims=True)
    return scale * (lifted - mean - unit * along)


def attention_back(q_ref, grad_ref, att_ref, keys, values, keys_turned, bias, lse, sums, turned, count):
    turned[...] = (grad_ref[...].astype(jnp.float32) * att_ref[...].astype(jnp.float32)).T

    def one(head, _):
        rows = pl.ds(pl.multiple_of(head * HDIM, HDIM), HDIM)
        query = q_ref[...] * head_mask(head, 0.125).astype(jnp.bfloat16)
        grad = grad_ref[...] * head_mask(head, 1.0).astype(jnp.bfloat16)
        delta = jnp.sum(turned[rows, :], axis=0, keepdims=True)
        scores = dot_nt(keys[...], query) + bias[...].astype(jnp.float32)
        probs = jnp.exp(scores - lse[pl.ds(head, 1), :])
        grad_scores = (probs * (dot_nt(values[...], grad) - delta)).astype(jnp.bfloat16)
        sums[0, :count] += dot_nn(grad_scores, query)
        sums[1, :count] += dot_nn(probs.astype(jnp.bfloat16), grad)
        turned[rows, :] = dot_nn(keys_turned[rows, :], grad_scores) * 0.125
        return 0

    lax.fori_loop(0, LANES // HDIM, one, 0)
    q_ref[...] = turned[...].T.astype(jnp.bfloat16)


def backward_layer(layer, refs, place, tick, key_sems, sems, tile_sems):
    (
        full_a,
        full_b,
        grad_in,
        x_in,
        q_in,
        kv_in,
        att_in,
        mid_in,
        hid_in,
        lse_in,
        gains,
        bias,
        cosine,
        sine_table,
        grads_a,
        grad_out,
        small_out,
        wa,
        wb,
        low,
        q,
        kv,
        att,
        mid,
        hid,
        grad,
        gathered,
        grad_low,
        grad_att,
        near_in,
        far_in,
        sums,
        keys_turned,
        turned_q,
        grad_turned,
        normed_turned,
        lse,
    ) = refs
    share = KeyReturn(place, kv, near_in, far_in, key_sems)
    pairs = [
        (grad_in, grad_low),
        (mid_in.at[layer], mid),
        (hid_in.at[layer], hid),
        (full_a.at[layer], wa),
        (att_in.at[layer], att),
        (q_in.at[layer], q),
        (kv_in.at[layer], kv),
        (x_in, low),
        (lse_in.at[layer], lse),
    ]
    loads = [pltpu.make_async_copy(a, b, sems.at[i]) for i, (a, b) in enumerate(pairs)]
    def tile_copy(pack, tile):
        return pltpu.make_async_copy(
            full_b.at[layer, pack, tile], wb.at[pack, tile], tile_sems.at[pack, tile]
        )

    for copy in loads[:3]:
        copy.start()
    for part in range(2):
        for rel in range(4):
            for pack in (1, 0):
                tile_copy(pack, rel * 2 + part).start()
    for copy in loads[3:]:
        copy.start()
    tick()
    gain_one, gain_two = gains[layer, 0:1], gains[layer, 1:2]
    for copy in loads[:3]:
        copy.wait()
    small_out[...] = jnp.zeros_like(small_out)

    def by_rows(step):
        def one(i, _):
            step(pl.ds(pl.multiple_of(i * 128, 128), 128))
            return 0

        lax.fori_loop(0, grad.shape[0] // 128, one, 0)

    def enter(rows):
        incoming = grad_low[rows, :].astype(jnp.float32)
        grad[rows, :] = incoming
        small_out[2:3] += jnp.sum(incoming, axis=0, keepdims=True)
        grad_turned[:, rows] = incoming.T.astype(jnp.bfloat16)
        unit, _ = normalize(mid[rows, :])
        normed_turned[:, rows] = (unit * gain_two).T.astype(jnp.bfloat16)
        gathered[rows, :] = jnp.zeros((128, grad.shape[1]), jnp.float32)

    by_rows(enter)
    tick()

    def feed(part, rel):
        start = pl.multiple_of(rel * 768 + part * 384, 128)
        units = pl.ds(start, 384)
        tile = rel * 2 + part
        pre = hid[:, units].astype(jnp.float32)
        squared = pre * pre
        bent = jnp.tanh(0.7978845608028654 * pre * (1.0 + 0.044715 * squared))
        raised = 0.5 * (1.0 + bent)
        active = (pre * raised).astype(jnp.bfloat16)
        slope = raised + 0.5 * pre * (1.0 - bent * bent) * (
            0.7978845608028654 * (1.0 + 3 * 0.044715 * squared)
        )
        tile_copy(1, tile).wait()
        grad_act = dot_nn(grad_low[...], wb[1, tile])
        grad_pre = (grad_act * slope).astype(jnp.bfloat16)
        total = jnp.sum(grad_pre.astype(jnp.float32), axis=0, keepdims=True)
        small_out[pl.ds(4 + rel, 1), pl.ds(part * 384, 384)] = total
        wb[1, tile] = dot_nn(grad_turned[...], active).astype(jnp.bfloat16)
        tile_copy(0, tile).wait()
        gathered[...] += dot_nt(grad_pre, wb[0, tile])
        wb[0, tile] = dot_nn(normed_turned[...], grad_pre).astype(jnp.bfloat16)

    for part in range(2):
        for pair in range(2):

            def one(i, _):
                feed(part, 2 * pair + i)
                return 0

            lax.fori_loop(0, 2, one, 0)
            tick()

    def between(rows):
        found = gathered[rows, :]
        unit, scale = normalize(mid[rows, :])
        small_out[1:2] += jnp.sum(found * unit, axis=0, keepdims=True)
        total = grad[rows, :] + normalize_back(found, unit, scale, gain_two)
        grad[rows, :] = total
        grad_low[rows, :] = total.astype(jnp.bfloat16)

    by_rows(between)
    for copy in loads[3:]:
        copy.wait()

    def project(part, _):
        lanes = pl.ds(pl.multiple_of(part * LANES, LANES), LANES)
        grad_att[:, lanes] = dot_nt(grad_low[...], wa[1, 1, lanes, :]).astype(jnp.bfloat16)
        wa[1, 1, lanes, :] = dot_tn(att[:, lanes], grad_low[...]).astype(jnp.bfloat16)
        return 0

    lax.fori_loop(0, 3, project, 0)
    tick()
    for part in range(3):
        lanes = pl.ds(part * LANES, LANES)
        sums[...] = jnp.zeros_like(sums)
        keys_turned[...] = kv[0, :, lanes].astype(jnp.float32).T.astype(jnp.bfloat16)
        for start, count in ((0, 4 * PIECE), (PIECE, 3 * PIECE)):
            rows = pl.ds(start, PIECE)
            attention_back(
                q.at[rows, lanes],
                grad_att.at[rows, lanes],
                att.at[rows, lanes],
                kv.at[0, :count, lanes],
                kv.at[1, :count, lanes],
                keys_turned.at[:, :count],
                bias.at[:count, rows],
                lse.at[pl.ds(8 * part, 8), rows],
                sums,
                turned_q,
                count,
            )
            if start == 0:
                tick()
        kv[:, :, lanes] = sums[...].astype(jnp.bfloat16)
        share.start(part)
        if part > 0:
            share.relay(part - 1)
        tick()
    normed = grad_att

    def again(rows):
        unit, _ = normalize(low[rows, :].astype(jnp.float32))
        normed[rows, :] = (unit * gain_one).astype(jnp.bfloat16)

    by_rows(again)

    def turned(part, _):
        lanes = pl.ds(pl.multiple_of(part * LANES, LANES), LANES)
        raw = turn(q[:, lanes].astype(jnp.float32), cosine[...], -sine_table[...])
        raw = raw.astype(jnp.bfloat16)
        found = dot_nn(raw, wa[0, 0, lanes, :])

        @pl.when(part == 0)
        def _():
            gathered[...] = found

        @pl.when(part > 0)
        def _():
            gathered[...] += found

        wa[0, 0, lanes, :] = dot_tn(raw, normed[...]).astype(jnp.bfloat16)
        return 0

    lax.fori_loop(0, 3, turned, 0)
    share.relay(2)
    tick()
    for part in range(3):
        share.collect(part)

    def keyed(part, _):
        lanes = pl.ds(pl.multiple_of(part * LANES, LANES), LANES)
        noisy, clean = pl.ds(3 * PIECE, PIECE), pl.ds(2 * PIECE, PIECE)
        raw = jnp.concatenate([kv[0, noisy, lanes], kv[0, clean, lanes]], axis=0)
        raw = turn(raw.astype(jnp.float32), cosine[...], -sine_table[...]).astype(jnp.bfloat16)
        gathered[...] += dot_nn(raw, wa[0, 1, lanes, :])
        wa[0, 1, lanes, :] = dot_tn(raw, normed[...]).astype(jnp.bfloat16)
        raw = jnp.concatenate([kv[1, noisy, lanes], kv[1, clean, lanes]], axis=0)
        gathered[...] += dot_nn(raw, wa[1, 0, lanes, :])
        wa[1, 0, lanes, :] = dot_tn(raw, normed[...]).astype(jnp.bfloat16)
        return 0

    lax.fori_loop(0, 3, keyed, 0)
    tick()
    save_a = pltpu.make_async_copy(wa, grads_a, sems.at[10])
    save_a.start()

    def leave(rows):
        found = gathered[rows, :]
        unit, scale = normalize(low[rows, :].astype(jnp.float32))
        small_out[0:1] += jnp.sum(found * unit, axis=0, keepdims=True)
        total = grad[rows, :] + normalize_back(found, unit, scale, gain_one)
        grad_low[rows, :] = total.astype(jnp.bfloat16)

    by_rows(leave)
    save_grad = pltpu.make_async_copy(grad_low, grad_out, sems.at[11])
    save_grad.start()
    tick()
    share.drain()
    save_a.wait()
    save_grad.wait()


class Ticks:
    def __init__(self, groups):
        self.groups = list(groups)

    def __call__(self):
        if self.groups:
            for step in self.groups.pop(0):
                step()

    def rest(self):
        while self.groups:
            self()


def backward_buffers(width, units):
    low, full, count = jnp.bfloat16, jnp.float32, 2 * PIECE
    return [
        pltpu.VMEM((2, 2, width, width), low),
        pltpu.VMEM((2, 8, width, units // 8), low),
        pltpu.VMEM((count, width), low),
        pltpu.VMEM((count, width), low),
        pltpu.VMEM((2, 4 * PIECE, width), low),
        pltpu.VMEM((count, width), low),
        pltpu.VMEM((count, width), full),
        pltpu.VMEM((count, units), low),
        pltpu.VMEM((count, width), full),
        pltpu.VMEM((count, width), full),
        pltpu.VMEM((count, width), low),
        pltpu.VMEM((count, width), low),
        pltpu.VMEM((2, PIECE, width), low),
        pltpu.VMEM((2, PIECE, width), low),
        pltpu.VMEM((2, 4 * PIECE, LANES), full),
        pltpu.VMEM((LANES, 4 * PIECE), low),
        pltpu.VMEM((LANES, PIECE), full),
        pltpu.VMEM((width, count), low),
        pltpu.VMEM((width, count), low),
        pltpu.VMEM((24, count), full),
    ]


def backward_sems():
    dma = pltpu.SemaphoreType.DMA
    return [dma((3,))] * 6 + [dma((12,)), dma((2, 8))]


BUFFERS = 20


def later(step, *args):
    return lambda: step(*args)


def second_kernel(*refs):
    ins, refs = refs[:15], refs[15:]
    (grads_a, grad_out, small_out, out, final_b, carry), refs = refs[:6], refs[6:]
    buffers, stages, feed, refs = refs[:BUFFERS], refs[BUFFERS : BUFFERS + 2], refs[22:25], refs[25:]
    sems, feed_sem, gate, carry_sem = refs[:24], refs[24:-2], refs[-2], refs[-1]
    low_both = ins[14]
    place = Place()
    place.meet(place.partners())
    zero, last = [
        Spread(place, low_both.at[i], stages[i], i, out, sems[8 + 8 * i : 16 + 8 * i])
        for i in range(2)
    ]
    one, two = feed_sums(place, buffers[1], feed, feed_sem, gate)
    carries = [
        pltpu.make_async_copy(two.total(rel), carry.at[rel], carry_sem.at[rel]) for rel in range(4)
    ]

    def hand_on():
        two.load(travels=False)
        for copy in carries:
            copy.start()

    tick = Ticks(
        [
            [zero.take, last.take, zero.swap, later(zero.hops, 0), later(last.hops, 0)],
            [],
            [later(zero.forward, 0)],
            [one.start, last.swap],
            [later(zero.hops, 1), later(last.forward, 0)],
            [later(zero.finish, 0)],
            [one.load],
            [later(zero.forward, 1), two.start],
            [later(last.finish, 0)],
            [one.middle],
            [later(last.hops, 1), later(zero.finish, 1)],
            [one.gather],
            [hand_on],
            [one.line_one, later(last.forward, 1)],
            [one.line_two],
            [later(last.finish, 1), later(one.finish, 1, final_b.at[place.s])],
        ]
    )
    body = ins[:3] + (low_both.at[0],) + ins[4:14] + (grads_a, grad_out, small_out) + buffers
    backward_layer(1, body, place, tick, sems[:6], sems[6], sems[7])
    tick.rest()
    zero.drain()
    last.drain()
    one.drain(1, final_b.at[place.s])
    two.drain_exchange()
    for copy in carries:
        copy.wait()


def first_kernel(*refs):
    ins, refs = refs[:16], refs[16:]
    (grads_a, grad_out, small_out, out, final_b), refs = refs[:5], refs[5:]
    buffers, stage, refs = refs[:BUFFERS], refs[BUFFERS], refs[BUFFERS + 1 :]
    feed, (total, hop_in, line_in), refs = refs[:3], refs[3:6], refs[6:]
    sems, feed_sem, kept_sem, gate = refs[:16], refs[16:36], refs[36:46], refs[46]
    carry, prior_grad = ins[14:]
    place = Place()
    place.meet(place.partners())
    back = Spread(place, prior_grad, stage, 1, out, sems[8:16])
    one, two = feed_sums(place, buffers[1], feed, feed_sem, gate)
    kept = Sum(
        place,
        lambda pack, rel: carry.at[rel],
        lambda rel: total.at[rel],
        (None, hop_in, line_in),
        kept_sem,
        loaded=True,
    )
    targets = [final_b.at[place.s, 0], final_b.at[place.s, 1]]
    tick = Ticks(
        [
            [back.take, back.swap, kept.start, later(back.hops, 0)],
            [kept.load],
            [later(back.forward, 0)],
            [one.start, kept.middle],
            [later(back.hops, 1)],
            [kept.gather, later(back.finish, 0)],
            [one.load],
            [kept.line_one, two.start],
            [later(back.forward, 1)],
            [one.middle, kept.line_two],
            [two.load],
            [later(back.finish, 1), one.gather],
            [two.middle, later(kept.finish, 1, targets[1])],
            [one.line_one],
            [two.gather, one.line_two],
            [later(one.finish, 0, targets[0]), two.line_one],
            [two.line_two, later(two.finish, 0, targets[1])],
        ]
    )
    body = ins[:14] + (grads_a, grad_out, small_out) + buffers
    backward_layer(0, body, place, tick, sems[:6], sems[6], sems[7])
    tick.rest()
    back.drain()
    kept.drain(1, targets[1])
    one.drain(0, targets[0])
    two.drain(0, targets[1])


def last_kernel(*refs):
    priors, (grad_zero, small_zero, small_one, out, final_a, small) = refs[:2], refs[2:8]
    held, stage, (small_in, extra), sems = refs[8:24], refs[24], refs[25:27], refs[27:]
    held_sem, spread_sem, (tiny_send, tiny_recv) = sems[:40], sems[40:48], sems[48:]
    place = Place()
    place.meet(place.partners())
    sums = []
    for i in range(2):
        sums += attention_sums(
            place, priors[i], held[8 * i : 8 * i + 8], held_sem[20 * i : 20 * i + 20]
        )
    back = Spread(place, grad_zero, stage, 0, out, spread_sem)
    targets = [final_a.at[place.s, 0], final_a.at[place.s, 1]] * 2
    layers = (1, 1, 0, 0)
    small[0], small[1] = small_zero[...], small_one[...]
    rows_beside = ((4, 5, 6, 7), (5, 4, 7, 6), (6, 7, 4, 5), (4, 5, 6, 7), (4, 5, 6, 7))
    partners = (
        place.on(section=place.core),
        place.on(tp=place.beside_x),
        place.on(tp=place.beside_y),
        place.on(seq=place.twin),
        place.on(seq=place.far),
    )

    def tiny(i):
        return remote(extra.at[i], small_in.at[i], tiny_send.at[i], tiny_recv.at[i], partners[i])

    def tiny_start(i):
        extra[i] = small[...]
        tiny(i).start()

    def tiny_end(i):
        tiny(i).wait_recv()
        for layer in range(2):
            small[layer, 0:4] = extra[i, layer, 0:4] + small_in[i, layer, 0:4]
            for row, other in enumerate(rows_beside[i]):
                at = row + 4
                small[layer, at : at + 1] = (
                    extra[i, layer, at : at + 1] + small_in[i, layer, other : other + 1]
                )

    tiny_start(0)
    back.take()
    back.swap()
    sums[0].start()
    back.hops(0)
    for item in sums[1:]:
        item.start()
    sums[0].load()
    sums[1].load()
    tiny_end(0)
    tiny_start(1)
    back.forward(0)
    sums[2].load()
    sums[0].middle()
    sums[3].load()
    sums[1].middle()
    tiny_end(1)
    tiny_start(2)
    sums[0].gather()
    sums[2].middle()
    sums[1].gather()
    sums[0].line_one()
    sums[3].middle()
    back.hops(1)
    sums[1].line_one()
    tiny_end(2)
    tiny_start(3)
    sums[2].gather()
    sums[0].line_two()
    sums[2].line_one()
    sums[3].gather()
    sums[1].line_two()
    sums[3].line_one()
    back.forward(1)
    tiny_end(3)
    tiny_start(4)
    sums[2].line_two()
    sums[0].finish(1, targets[0])
    sums[1].finish(1, targets[1])
    sums[3].line_two()
    back.finish(0)
    sums[2].finish(0, targets[2])
    back.finish(1)
    sums[3].finish(0, targets[3])
    tiny_end(4)
    for item, layer, target in zip(sums, layers, targets):
        item.drain(layer, target)
    back.drain()
    for i in range(5):
        tiny(i).wait_send()


def call(kernel, name, number, ins, spaces, shapes, out_spaces, scratch, flops, moved):
    return pl.pallas_call(
        kernel,
        name=name,
        out_shape=[jax.ShapeDtypeStruct(shape, kind) for shape, kind in shapes],
        in_specs=spaces,
        out_specs=out_spaces,
        scratch_shapes=scratch,
        compiler_params=pltpu.CompilerParams(
            collective_id=number, has_side_effects=True, vmem_limit_bytes=62 * 1024 * 1024
        ),
        cost_estimate=pl.CostEstimate(
            flops=flops, bytes_accessed=moved, transcendentals=20_000_000
        ),
    )(*ins)


def run_backward(full_a, full_b, seeded, tokens, low_both, kept, gains, bias, tables):
    low, full, count = jnp.bfloat16, jnp.float32, 2 * PIECE
    width, units = full_a.shape[-1], 8 * full_b.shape[-1]
    grads = [
        ((2, 2, width, width), low),
        ((count, width), low),
        ((8, width), full),
    ]
    out = ((2, 4, count, width), low)
    row_piece, tile_piece = (192, width), (width, units // 8)
    final_a, final_b = ((2, 2) + row_piece, low), ((2, 2) + tile_piece, low)
    half_b, carry = ((2,) + tile_piece, low), ((4,) + tile_piece, low)
    stage = pltpu.VMEM((4, 2, PIECE, width), low)
    dma, gate = pltpu.SemaphoreType.DMA, pltpu.SemaphoreType.REGULAR
    common = (*kept, gains, bias, *tables)
    common_spaces = [HBM] * 10 + [VMEM] * 4
    held = sum_buffers(row_piece, (4, 4, 3, 2) * 2)
    second = call(
        second_kernel,
        "backward_second",
        2,
        (full_a, full_b, seeded, tokens) + common + (low_both,),
        common_spaces + [HBM],
        grads + [out, half_b, carry],
        [HBM] * 2 + [VMEM] + [HBM] * 3,
        backward_buffers(width, units)
        + [stage, stage]
        + feed_buffers(tile_piece, 1)
        + backward_sems()
        + spread_sems()
        + spread_sems()
        + sum_sems()
        + sum_sems()
        + [gate, dma((4,))],
        40_000_000_000,
        80_000_000,
    )
    prior_a, grad_one, small_one, layer_out, feed_one, carried = second
    first = call(
        first_kernel,
        "backward_first",
        3,
        (full_a, full_b, grad_one, tokens) + common + (carried, grad_one),
        common_spaces + [HBM] * 2,
        grads + [out, final_b],
        [HBM] * 2 + [VMEM] + [HBM] * 2,
        backward_buffers(width, units)
        + [stage]
        + feed_buffers(tile_piece, 2)
        + sum_buffers(tile_piece, (4, 3, 2))
        + backward_sems()
        + spread_sems()
        + sum_sems()
        + sum_sems()
        + sum_sems()
        + [gate],
        40_000_000_000,
        80_000_000,
    )
    grads_a, grad_zero, small_zero, out_one, feed_zero = first
    by_shard = (2, 2, 4, 192, width)
    last = call(
        last_kernel,
        "sum_and_spread",
        4,
        (prior_a.reshape(by_shard), grads_a.reshape(by_shard), grad_zero, small_zero, small_one),
        [HBM] * 3 + [VMEM] * 2,
        [out, final_a, ((2, 8, width), full)],
        [HBM] * 2 + [VMEM],
        held
        + held
        + [stage]
        + [pltpu.VMEM((5, 2, 8, width), full), pltpu.VMEM((5, 2, 8, width), full)]
        + sum_sems()
        + sum_sems()
        + sum_sems()
        + sum_sems()
        + spread_sems()
        + [dma((5,)), dma((5,))],
        100_000_000,
        40_000_000,
    )
    out_zero, rows, small = last
    return layer_out, (out_zero, out_one), rows, (feed_zero, feed_one), small


def spread(
    layer_input,
    cotangent,
    doc_lengths,
    ln1_gain,
    w_qkv,
    w_out,
    ln2_gain,
    w_up,
    b_up,
    w_down,
    b_down,
):
    s, t, z = (lax.axis_index(name) for name in ("section", "tp", "seq"))
    micros, rows, width_pos, width = layer_input.shape
    half, group = z % 2, z // 2

    own_a = jnp.stack(
        [
            jnp.stack([w_qkv[0, :, 0].T, w_qkv[0, :, 1].T]),
            jnp.stack([w_qkv[0, :, 2].T, w_out[0]]),
        ]
    )
    shard = w_up.shape[-1]
    own_b = jnp.stack([w_up[0], w_down[0].T]).reshape(2, width, 2, shard // 2).transpose(0, 2, 1, 3)
    gains = jnp.concatenate([ln1_gain, ln2_gain, b_down, jnp.zeros((5, width), jnp.float32)])
    own_c = jnp.stack([gains, jnp.concatenate([b_up, jnp.zeros((7, width), jnp.float32)])])

    block = 2 * half + s
    lengths = doc_lengths.reshape(micros * rows, -1)
    lengths = lax.dynamic_index_in_dim(lengths, 4 * group + t, 0, keepdims=False)
    ends = jnp.cumsum(lengths)
    piece_pos = jnp.arange(PIECE)
    query_base = jnp.tile(block * PIECE + piece_pos, 2)
    key_base = jnp.concatenate([(block - 2 + i) * PIECE + piece_pos for i in (0, 1, 2, 2)])
    query_noisy = jnp.arange(2 * PIECE) < PIECE
    key_noisy = jnp.arange(4 * PIECE) >= 3 * PIECE

    def docs_of(base):
        return jnp.sum((base[:, None] >= ends[None, :]).astype(jnp.int32), axis=-1)

    query_block, key_block = query_base[None, :] // BLOCK, key_base[:, None] // BLOCK
    query_kind, key_kind = query_noisy[None, :], key_noisy[:, None]
    mask = (
        (query_kind & key_kind & (query_block == key_block))
        | (query_kind & ~key_kind & (key_block < query_block))
        | (~query_kind & ~key_kind & (key_block <= query_block))
    )
    mask = mask & (docs_of(query_base)[None, :] == docs_of(key_base)[:, None])
    mask = mask & (key_base >= 0)[:, None]
    bias = jnp.where(mask, 0.0, -1e30).astype(jnp.bfloat16)
    frequency = 10000.0 ** (-jnp.arange(HDIM // 2).astype(jnp.float32) * 2.0 / HDIM)
    angles = query_base.astype(jnp.float32)[:, None] * frequency[None, :]
    cosine, sine_table = jnp.cos(angles), jnp.sin(angles)
    turn_cos = jnp.tile(cosine, (1, 4))
    turn_sin = jnp.tile(jnp.concatenate([-sine_table, sine_table], axis=1), (1, 2))

    flat = (micros * rows, width_pos, width)
    forward = run_forward(
        layer_input.reshape(flat), cotangent.reshape(flat), own_a, own_b, own_c, bias, turn_cos, turn_sin
    )
    full_a, full_b, gains, seeded, tokens, low_both, *kept = forward
    tables = (turn_cos, turn_sin)
    layer_out, input_grads, final_a, feeds, small = run_backward(
        full_a, full_b, seeded, tokens, low_both, kept, gains, bias, tables
    )
    input_grad = jnp.where(s == 0, *input_grads)
    final_b = jnp.stack([jnp.where(s == 0, feeds[0][:, 0], feeds[1]), feeds[0][:, 1]], axis=1)
    small = lax.dynamic_index_in_dim(small, s, 0, keepdims=False)
    final_a, final_b = final_a.astype(jnp.float32), final_b.astype(jnp.float32)
    grad_qkv = jnp.stack([final_a[0, 0].T, final_a[0, 1].T, final_a[1, 0].T], axis=1)
    grad_up, grad_down = final_b.transpose(0, 2, 1, 3).reshape(2, width, shard)
    out_shape = (1,) + layer_input.shape
    return (
        layer_out.reshape(out_shape),
        input_grad.reshape(out_shape),
        small[0:1],
        grad_qkv[None],
        final_a[1, 1][None],
        small[1:2],
        grad_up[None],
        small[4:5],
        grad_down.T[None],
        small[2:3],
    )


def solution(mesh):
    sizes = tuple(mesh.shape[name] for name in ("section", "tp", "seq"))
    local = spread if sizes == (2, 4, 4) else pipelined
    return jax.shard_map(
        local,
        mesh=mesh,
        in_specs=(
            P(None, None, "seq", None),
            P(None, None, "seq", None),
            P(),
            P("section", None),
            P("section", None, None, "tp"),
            P("section", "tp", None),
            P("section", None),
            P("section", None, "tp"),
            P("section", "tp"),
            P("section", "tp", None),
            P("section", None),
        ),
        out_specs=(
            P("section", None, None, "seq", None),
            P("section", None, None, "seq", None),
            P("section", None),
            P("section", None, None, "tp"),
            P("section", "tp", None),
            P("section", None),
            P("section", None, "tp"),
            P("section", "tp"),
            P("section", "tp", None),
            P("section", None),
        ),
        check_vma=False,
    )
```

```python
import jax
import jax.numpy as jnp
from jax import lax
from jax.experimental import pallas as pl
from jax.experimental.pallas import tpu as pltpu
from jax.sharding import PartitionSpec as P

HDIM = 64
BLOCK = 16
HALF = 1024


def from_behind(value, axis, by):
    size = lax.axis_size(axis)
    pairs = [(i, i + by) for i in range(size) if 0 <= i + by < size]
    return lax.ppermute(value, axis, pairs)


def layer_norm(values, gain):
    center = values - jnp.mean(values, axis=-1, keepdims=True)
    spread = jnp.mean(center * center, axis=-1, keepdims=True)
    return center * lax.rsqrt(spread + 1e-05) * gain


def rotate(values, cosine, sine_table):
    middle = values.shape[-1] // 2
    first_half = values[..., :middle]
    second_half = values[..., middle:]
    return jnp.concatenate(
        [
            first_half * cosine - second_half * sine_table,
            second_half * cosine + first_half * sine_table,
        ],
        axis=-1,
    )


def rotary_tables(positions):
    frequency = 10000.0 ** (-jnp.arange(HDIM // 2).astype(jnp.float32) * 2.0 / HDIM)
    angles = (positions % HALF).astype(jnp.float32)[:, None, None] * frequency[None, None, :]
    return (jnp.cos(angles), jnp.sin(angles))


def allowed(query_pos, query_doc, key_pos, key_doc):
    query_noisy = query_pos < HALF
    key_noisy = key_pos < HALF
    query_block = query_pos % HALF // BLOCK
    key_block = key_pos % HALF // BLOCK
    within = query_noisy & key_noisy & (query_block == key_block)
    earlier = query_noisy & ~key_noisy & (key_block < query_block)
    causal = ~query_noisy & ~key_noisy & (key_block <= query_block)
    return (within | earlier | causal) & (query_doc == key_doc)


def document_ids(doc_lengths):
    doc_ends = jnp.cumsum(doc_lengths, axis=-1)
    base_pos = jnp.arange(2 * HALF) % HALF
    return jnp.sum((base_pos[:, None] >= doc_ends[..., None, :]).astype(jnp.int32), axis=-1)


def gelu_tanh(values):
    return jax.nn.gelu(values, approximate=True)


def keep_slot(storage, value, slot_index, is_active):
    current = lax.dynamic_index_in_dim(storage, slot_index, 0, keepdims=False)
    return lax.dynamic_update_index_in_dim(
        storage, jnp.where(is_active, value, current), slot_index, 0
    )


def local_queries(inputs, ln_one, w_mix, tables):
    cosine, sine_table, query_pos = tables
    row_count, pos_count = (inputs.shape[0], inputs.shape[1])
    normed = layer_norm(inputs, ln_one).astype(jnp.bfloat16)
    mixed = jnp.einsum("rpd,dcf->rpcf", normed, w_mix, preferred_element_type=jnp.float32)
    shaped = mixed.reshape(row_count, pos_count, 3, -1, HDIM)
    queries = rotate(shaped[:, :, 0], cosine, sine_table).astype(jnp.bfloat16)
    keys_own = rotate(shaped[:, :, 1], cosine, sine_table).astype(jnp.bfloat16)
    values_own = shaped[:, :, 2].astype(jnp.bfloat16)
    return (normed, queries, keys_own, values_own)


def masked_scores(queries, keys_heads, query_pos, docs_all):
    pos_count = queries.shape[1]
    query_docs = lax.dynamic_slice_in_dim(docs_all, query_pos[0], pos_count, 1)
    key_pos = jnp.arange(keys_heads.shape[1])
    key_mask = allowed(
        query_pos[None, :, None],
        query_docs[:, :, None],
        key_pos[None, None, :],
        docs_all[:, None, :],
    )
    scores = (
        jnp.einsum("rqhd,rkhd->rhqk", queries, keys_heads, preferred_element_type=jnp.float32)
        * 0.125
    )
    return jnp.where(key_mask[:, None], scores, -1e30)


def forward_step(inputs, weights, tables, docs_all):
    ln_one, w_mix, w_proj, ln_two, w_first, b_first, w_second, b_second = weights
    row_count, pos_count = (inputs.shape[0], inputs.shape[1])
    normed, queries, keys_own, values_own = local_queries(inputs, ln_one, w_mix, tables)
    local_width = w_mix.shape[-1]
    keys_all, values_all = (
        lax.all_gather(
            keys_own.reshape(row_count, pos_count, local_width), "seq", axis=1, tiled=True
        ),
        lax.all_gather(
            values_own.reshape(row_count, pos_count, local_width), "seq", axis=1, tiled=True
        ),
    )
    keys_heads = keys_all.reshape(row_count, keys_all.shape[1], -1, HDIM)
    values_heads = values_all.reshape(row_count, values_all.shape[1], -1, HDIM)
    softmax_out = jax.nn.softmax(
        masked_scores(queries, keys_heads, tables[2], docs_all), axis=-1
    ).astype(jnp.bfloat16)
    attended = jnp.einsum(
        "rhqk,rkhd->rqhd", softmax_out, values_heads, preferred_element_type=jnp.float32
    )
    attended = attended.astype(jnp.bfloat16).reshape(row_count, pos_count, local_width)
    middle = inputs + lax.psum(
        jnp.einsum("rpe,ed->rpd", attended, w_proj, preferred_element_type=jnp.float32).astype(
            jnp.bfloat16
        ),
        "tp",
    ).astype(jnp.float32)
    normed_two = layer_norm(middle, ln_two).astype(jnp.bfloat16)
    hidden_pre = (
        jnp.einsum("rpd,df->rpf", normed_two, w_first, preferred_element_type=jnp.float32) + b_first
    )
    activated = gelu_tanh(hidden_pre).astype(jnp.bfloat16)
    second_terms = jnp.einsum(
        "rpf,fd->rpd", activated, w_second, preferred_element_type=jnp.float32
    )
    result = (
        middle + lax.psum(second_terms.astype(jnp.bfloat16), "tp").astype(jnp.float32) + b_second
    )
    return (result, middle, keys_all, values_all)


def backward_step(inputs, middle, grad_out, weights, tables, docs_all):
    ln_one, w_mix, w_proj, ln_two, w_first, b_first, w_second, b_second = weights
    cosine, sine_table, query_pos = tables
    row_count, pos_count = (inputs.shape[0], inputs.shape[1])
    local_width = w_mix.shape[-1]
    head_count = local_width // HDIM
    normed, queries, keys_own, values_own = local_queries(inputs, ln_one, w_mix, tables)
    keys_all, values_all = (
        lax.all_gather(
            keys_own.reshape(row_count, pos_count, local_width), "seq", axis=1, tiled=True
        ),
        lax.all_gather(
            values_own.reshape(row_count, pos_count, local_width), "seq", axis=1, tiled=True
        ),
    )
    keys_heads = keys_all.reshape(row_count, keys_all.shape[1], head_count, HDIM)
    values_heads = values_all.reshape(row_count, values_all.shape[1], head_count, HDIM)
    scores = masked_scores(queries, keys_heads, query_pos, docs_all)
    softmax_out = jax.nn.softmax(scores, axis=-1)
    probs_low = softmax_out.astype(jnp.bfloat16)
    attended = jnp.einsum(
        "rhqk,rkhd->rqhd", probs_low, values_heads, preferred_element_type=jnp.float32
    )
    attended = attended.astype(jnp.bfloat16).reshape(row_count, pos_count, local_width)
    normed_two = layer_norm(middle, ln_two).astype(jnp.bfloat16)
    hidden_pre = (
        jnp.einsum("rpd,df->rpf", normed_two, w_first, preferred_element_type=jnp.float32) + b_first
    )
    activated = gelu_tanh(hidden_pre).astype(jnp.bfloat16)
    grad_low = grad_out.astype(jnp.bfloat16)
    grad_b_second = jnp.sum(grad_out, axis=(0, 1))
    grad_w_second = jnp.einsum(
        "rpf,rpd->fd", activated, grad_low, preferred_element_type=jnp.float32
    )
    grad_act = jnp.einsum("rpd,fd->rpf", grad_low, w_second, preferred_element_type=jnp.float32)
    unused_value, gelu_back = jax.vjp(gelu_tanh, hidden_pre)
    grad_pre = gelu_back(grad_act)[0].astype(jnp.bfloat16)
    grad_b_first = jnp.sum(grad_pre, axis=(0, 1), dtype=jnp.float32)
    grad_w_first = jnp.einsum(
        "rpd,rpf->df", normed_two, grad_pre, preferred_element_type=jnp.float32
    )
    grad_normed_two = lax.psum(
        jnp.einsum("rpf,df->rpd", grad_pre, w_first, preferred_element_type=jnp.float32).astype(
            jnp.bfloat16
        ),
        "tp",
    ).astype(jnp.float32)
    unused_norm, second_back = jax.vjp(layer_norm, middle, ln_two)
    grad_middle_norm, grad_ln_two = second_back(grad_normed_two)
    grad_middle = grad_out + grad_middle_norm
    middle_low = grad_middle.astype(jnp.bfloat16)
    grad_w_proj = jnp.einsum(
        "rpe,rpd->ed", attended, middle_low, preferred_element_type=jnp.float32
    )
    grad_att = jnp.einsum("rpd,ed->rpe", middle_low, w_proj, preferred_element_type=jnp.float32)
    grad_att = grad_att.astype(jnp.bfloat16).reshape(row_count, pos_count, head_count, HDIM)
    grad_probs = jnp.einsum(
        "rqhd,rkhd->rhqk", grad_att, values_heads, preferred_element_type=jnp.float32
    )
    row_delta = jnp.sum(grad_probs * softmax_out, axis=-1, keepdims=True)
    grad_scores = (softmax_out * (grad_probs - row_delta)).astype(jnp.bfloat16)
    grad_queries = (
        jnp.einsum("rhqk,rkhd->rqhd", grad_scores, keys_heads, preferred_element_type=jnp.float32)
        * 0.125
    )
    full_len = keys_all.shape[1]
    part_keys = (
        jnp.einsum("rhqk,rqhd->rkhd", grad_scores, queries, preferred_element_type=jnp.float32)
        * 0.125
    )
    part_values = jnp.einsum(
        "rhqk,rqhd->rkhd", probs_low, grad_att, preferred_element_type=jnp.float32
    )
    grad_keys, grad_values = (
        lax.psum_scatter(
            part_keys.reshape(row_count, full_len, local_width).astype(jnp.bfloat16),
            "seq",
            scatter_dimension=1,
            tiled=True,
        ).astype(jnp.float32),
        lax.psum_scatter(
            part_values.reshape(row_count, full_len, local_width).astype(jnp.bfloat16),
            "seq",
            scatter_dimension=1,
            tiled=True,
        ).astype(jnp.float32),
    )
    grad_query_raw = rotate(grad_queries.astype(jnp.bfloat16), cosine, -sine_table)
    grad_key_raw = rotate(
        grad_keys.astype(jnp.bfloat16).reshape(row_count, pos_count, head_count, HDIM),
        cosine,
        -sine_table,
    )
    grad_mixed = jnp.stack(
        [
            grad_query_raw.reshape(row_count, pos_count, local_width).astype(jnp.bfloat16),
            grad_key_raw.reshape(row_count, pos_count, local_width).astype(jnp.bfloat16),
            grad_values.astype(jnp.bfloat16),
        ],
        axis=2,
    )
    grad_w_mix = jnp.einsum("rpd,rpcf->dcf", normed, grad_mixed, preferred_element_type=jnp.float32)
    grad_normed = lax.psum(
        jnp.einsum("rpcf,dcf->rpd", grad_mixed, w_mix, preferred_element_type=jnp.float32).astype(
            jnp.bfloat16
        ),
        "tp",
    ).astype(jnp.float32)
    unused_first, first_back = jax.vjp(layer_norm, inputs, ln_one)
    grad_in_norm, grad_ln_one = first_back(grad_normed)
    grad_inputs = grad_middle + grad_in_norm
    return (
        grad_inputs,
        (
            grad_ln_one,
            grad_w_mix,
            grad_w_proj,
            grad_ln_two,
            grad_w_first,
            grad_b_first,
            grad_w_second,
            grad_b_second,
        ),
    )


def pipelined(
    layer_input,
    cotangent,
    doc_lengths,
    ln1_gain,
    w_qkv,
    w_out,
    ln2_gain,
    w_up,
    b_up,
    w_down,
    b_down,
):
    weights = tuple(
        (weight[0] for weight in (ln1_gain, w_qkv, w_out, ln2_gain, w_up, b_up, w_down, b_down))
    )
    micros, row_count, pos_count, width_model = layer_input.shape
    sections = lax.axis_size("section")
    section_index = lax.axis_index("section")
    first_pos = lax.axis_index("seq") * pos_count
    query_pos = first_pos + jnp.arange(pos_count)
    cosine, sine_table = rotary_tables(query_pos)
    tables = (cosine, sine_table, query_pos)
    docs_every = document_ids(doc_lengths)
    kept_inputs = jnp.zeros((micros, row_count, pos_count, width_model), jnp.float32)
    kept_middle = jnp.zeros((micros, row_count, pos_count, width_model), jnp.float32)
    layer_out = jnp.zeros(layer_input.shape, jnp.bfloat16)
    arrived = jnp.zeros((row_count, pos_count, width_model), jnp.bfloat16)
    moments = micros + sections - 1
    for moment in range(moments):
        offset = moment - section_index
        micro_index = jnp.clip(offset, 0, micros - 1)
        is_active = (offset >= 0) & (offset < micros)
        own_input = layer_input[min(moment, micros - 1)]
        inputs = jnp.where(section_index == 0, own_input, arrived).astype(jnp.float32)
        result, middle, keys_all, values_all = forward_step(
            inputs, weights, tables, docs_every[micro_index]
        )
        kept_inputs = keep_slot(kept_inputs, inputs, micro_index, is_active)
        kept_middle = keep_slot(kept_middle, middle, micro_index, is_active)
        result_low = result.astype(jnp.bfloat16)
        layer_out = keep_slot(layer_out, result_low, micro_index, is_active)
        if moment < moments - 1:
            arrived = from_behind(result_low, "section", 1)
    grad_totals = tuple((jnp.zeros(weight.shape, jnp.float32) for weight in weights))
    input_grad = jnp.zeros(layer_input.shape, jnp.bfloat16)
    returned = jnp.zeros((row_count, pos_count, width_model), jnp.bfloat16)
    for moment in range(moments):
        offset = moment - (sections - 1 - section_index)
        micro_index = jnp.clip(offset, 0, micros - 1)
        is_active = (offset >= 0) & (offset < micros)
        incoming = jnp.where(
            section_index == sections - 1, cotangent[min(moment, micros - 1)], returned
        ).astype(jnp.float32)
        incoming = jnp.where(is_active, incoming, 0.0)
        grad_inputs, grad_parts = backward_step(
            kept_inputs[micro_index],
            kept_middle[micro_index],
            incoming,
            weights,
            tables,
            docs_every[micro_index],
        )
        grad_totals = tuple((total + piece for total, piece in zip(grad_totals, grad_parts)))
        grad_sent = grad_inputs.astype(jnp.bfloat16)
        input_grad = keep_slot(input_grad, grad_sent, micro_index, is_active)
        if moment < moments - 1:
            returned = from_behind(grad_sent, "section", -1)
    (
        grad_ln_one,
        grad_w_mix,
        grad_w_proj,
        grad_ln_two,
        grad_w_first,
        grad_b_first,
        grad_w_second,
        grad_b_second,
    ) = grad_totals
    summed = (
        lax.psum(grad_ln_one.astype(jnp.bfloat16), "seq").astype(jnp.float32),
        lax.psum(grad_w_mix.astype(jnp.bfloat16), "seq").astype(jnp.float32),
        lax.psum(grad_w_proj.astype(jnp.bfloat16), "seq").astype(jnp.float32),
        lax.psum(grad_ln_two.astype(jnp.bfloat16), "seq").astype(jnp.float32),
        lax.psum(grad_w_first.astype(jnp.bfloat16), "seq").astype(jnp.float32),
        lax.psum(grad_b_first.astype(jnp.bfloat16), "seq").astype(jnp.float32),
        lax.psum(grad_w_second.astype(jnp.bfloat16), "seq").astype(jnp.float32),
        lax.psum(grad_b_second.astype(jnp.bfloat16), "seq").astype(jnp.float32),
    )
    return (
        layer_out[None],
        input_grad[None],
        summed[0][None],
        summed[1][None],
        summed[2][None],
        summed[3][None],
        summed[4][None],
        summed[5][None],
        summed[6][None],
        summed[7][None],
    )


PIECE = 256
LANES = 256
MESH = pl.DeviceIdType.MESH
HBM = pl.BlockSpec(memory_space=pl.ANY)
VMEM = pl.BlockSpec(memory_space=pltpu.VMEM)


def dot_nn(left, right):
    return lax.dot_general(left, right, (((1,), (0,)), ((), ())), preferred_element_type=jnp.float32)


def dot_nt(left, right):
    return lax.dot_general(left, right, (((1,), (1,)), ((), ())), preferred_element_type=jnp.float32)


def dot_tn(left, right):
    return lax.dot_general(left, right, (((0,), (0,)), ((), ())), preferred_element_type=jnp.float32)


class Place:
    def __init__(self):
        self.s, self.t, self.z = (lax.axis_index(name) for name in ("section", "tp", "seq"))
        self.core = 1 - self.s
        self.half, self.group = self.z % 2, self.z // 2
        beside_x = self.t + 1 - 2 * (self.t % 2)
        beside_y = (self.t + 2) % 4
        self.beside_x, self.beside_y = beside_x, beside_y
        self.hop_one = beside_x * (1 - self.s) + beside_y * self.s
        self.hop_two = beside_y * (1 - self.s) + beside_x * self.s
        self.rel_one, self.rel_two = 1 + self.s, 2 - self.s
        self.far = (self.z + 2) % 4
        self.twin = self.z + 1 - 2 * self.half

    def on(self, section=None, tp=None, seq=None):
        return (
            self.s if section is None else section,
            self.t if tp is None else tp,
            self.z if seq is None else seq,
        )

    def partners(self):
        return [
            self.on(section=self.core),
            self.on(tp=self.beside_x),
            self.on(tp=self.beside_y),
            self.on(seq=self.far),
            self.on(seq=self.twin),
            self.on(seq=3 - self.z),
            self.on(section=self.core, seq=self.twin),
        ]

    def meet(self, partners):
        barrier = pltpu.get_barrier_semaphore()
        for partner in partners:
            pl.semaphore_signal(barrier, inc=1, device_id=partner, device_id_type=MESH)
        pl.semaphore_wait(barrier, len(partners))


def remote(source, target, send, receive, device):
    return pltpu.make_async_remote_copy(
        src_ref=source,
        dst_ref=target,
        send_sem=send,
        recv_sem=receive,
        device_id=device,
        device_id_type=MESH,
    )


def normalize(values):
    center = values - jnp.mean(values, axis=-1, keepdims=True)
    spread = jnp.mean(center * center, axis=-1, keepdims=True)
    scale = lax.rsqrt(spread + 1e-05)
    return center * scale, scale


def turn(values, cosine, sine_table):
    width = values.shape[-1]
    times = width // cosine.shape[-1]
    lane = lax.broadcasted_iota(jnp.int32, values.shape, 1) % HDIM
    ahead = pltpu.roll(values, width - HDIM // 2, 1)
    behind = pltpu.roll(values, HDIM // 2, 1)
    swapped = jnp.where(lane < HDIM // 2, ahead, behind)
    return values * jnp.tile(cosine, (1, times)) + swapped * jnp.tile(sine_table, (1, times))


def gelu(values):
    inner = 0.7978845608028654 * (values + 0.044715 * values * values * values)
    return 0.5 * values * (1.0 + jnp.tanh(inner))


def head_mask(head, scale):
    lane = lax.broadcasted_iota(jnp.int32, (1, LANES), 1)
    inside = (lane >= head * HDIM) & (lane < (head + 1) * HDIM)
    return jnp.where(inside, jnp.float32(scale), jnp.float32(0.0))


def attention_block(q_ref, keys, values_turned, bias, lse, turned):
    def one(head, _):
        rows = pl.ds(pl.multiple_of(head * HDIM, HDIM), HDIM)
        query = q_ref[...] * head_mask(head, 0.125).astype(jnp.bfloat16)
        scores = dot_nt(keys[...], query) + bias[...].astype(jnp.float32)
        top = jnp.max(scores, axis=0, keepdims=True)
        raised = jnp.exp(scores - top)
        total = jnp.sum(raised, axis=0, keepdims=True)
        lse[pl.ds(head, 1), :] = top + jnp.log(total)
        turned[rows, :] = dot_nn(values_turned[rows, :], raised.astype(jnp.bfloat16)) * (1.0 / total)
        return 0

    lax.fori_loop(0, LANES // HDIM, one, 0)
    return turned[...].T.astype(jnp.bfloat16)


class Weights:
    def __init__(self, place, own, full, sems):
        self.place, self.own, self.full = place, own, full
        (
            self.local,
            self.own_send,
            self.own_recv,
            self.hop_send,
            self.hop_recv,
            self.chip_send,
            self.chip_recv,
        ) = sems

    def source(self, chunk, pack):
        if chunk == 0:
            return self.own[0].at[pack]
        if chunk == 3:
            return self.own[2].at[pack]
        return self.own[1].at[pack, chunk - 1]

    def piece(self, layer, chunk, pack, rel):
        if chunk == 0:
            return self.full[0].at[layer, pack, :, pl.ds(pl.multiple_of(rel * 192, 64), 192)]
        if chunk == 3:
            return self.full[2].at[layer, pack, rel]
        return self.full[1].at[layer, pack, rel * 2 + chunk - 1]

    def own_copies(self, chunk, pack):
        s = self.place.s
        here = pltpu.make_async_copy(
            self.source(chunk, pack), self.piece(s, chunk, pack, 0), self.local.at[chunk, pack]
        )
        there = remote(
            self.source(chunk, pack),
            self.piece(s, chunk, pack, 0),
            self.own_send.at[chunk, pack],
            self.own_recv.at[chunk, pack],
            self.place.on(section=self.place.core),
        )
        return here, there

    def start_own(self, chunk):
        for pack in (self.place.core, self.place.s):
            for copy in self.own_copies(chunk, pack)[::-1]:
                copy.start()

    def wait_own(self, layer, chunk, pack):
        here, there = self.own_copies(chunk, pack)

        @pl.when(self.place.s == layer)
        def _():
            here.wait()

        @pl.when(self.place.s != layer)
        def _():
            there.wait_recv()

    def hops(self, layer, chunk):
        place = self.place
        own = self.piece(layer, chunk, place.s, 0)
        first = self.piece(layer, chunk, place.s, place.rel_one)
        second = self.piece(layer, chunk, place.s, place.rel_two)
        third = self.piece(layer, chunk, place.s, 3)
        moves = ((own, first, place.hop_one), (own, second, place.hop_two), (first, third, place.hop_two))
        return [
            remote(
                source,
                target,
                self.hop_send.at[layer, chunk, i],
                self.hop_recv.at[layer, chunk, i],
                place.on(tp=column),
            )
            for i, (source, target, column) in enumerate(moves)
        ]

    def chips(self, layer, chunk):
        place = self.place
        return [
            remote(
                self.piece(layer, chunk, place.s, rel),
                self.piece(layer, chunk, place.s, rel),
                self.chip_send.at[layer, chunk, i],
                self.chip_recv.at[layer, chunk, i],
                place.on(section=place.core),
            )
            for i, rel in enumerate((place.rel_one, place.rel_two, 3))
        ]

    def begin(self, layer, chunk):
        self.wait_own(layer, chunk, self.place.s)
        first, second, _ = self.hops(layer, chunk)
        first.start()
        second.start()

    def forward(self, layer, chunk):
        first, second, third = self.hops(layer, chunk)
        chips = self.chips(layer, chunk)
        first.wait_recv()
        third.start()
        chips[0].start()
        second.wait_recv()
        chips[1].start()

    def finish(self, layer, chunk):
        self.hops(layer, chunk)[2].wait_recv()
        self.chips(layer, chunk)[2].start()

    def need(self, layer, chunk):
        if chunk < 3:
            self.wait_own(layer, chunk, self.place.core)
        for copy in self.chips(layer, chunk):
            copy.wait_recv()

    def drain(self):
        for chunk in range(4):
            for pack in range(2):
                self.own_copies(chunk, pack)[1].wait_send()
            for layer in range(2):
                for copy in self.hops(layer, chunk) + self.chips(layer, chunk):
                    copy.wait_send()


class KeyShare:
    def __init__(self, place, kv, layer, sems):
        self.place, self.kv, self.layer = place, kv, layer
        self.near_send, self.near_recv, self.far_send, self.far_recv = sems
        s, odd = place.s, place.half == 1
        self.sends_near = (s == 0) | ~odd
        self.sends_far = (s == 0) & ~odd
        self.passes = (s == 0) & odd
        self.gets_near = (s == 1) | odd
        self.gets_far = odd

    def rows(self, start, part):
        lanes = pl.ds(part * LANES, LANES)
        return self.kv.at[self.layer, :, pl.ds(start, PIECE), lanes]

    def near(self, part):
        place = self.place
        return remote(
            self.rows(2 * PIECE, part),
            self.rows(PIECE, part),
            self.near_send.at[self.layer, part],
            self.near_recv.at[self.layer, part],
            place.on(section=place.core, seq=place.z + place.s * (1 - place.half)),
        )

    def far(self, part):
        place = self.place
        return remote(
            self.rows(2 * PIECE, part),
            self.rows(0, part),
            self.far_send.at[self.layer, part],
            self.far_recv.at[self.layer, part],
            place.on(seq=place.twin),
        )

    def last(self, part):
        place = self.place
        return remote(
            self.rows(PIECE, part),
            self.rows(0, part),
            self.far_send.at[self.layer, part],
            self.far_recv.at[self.layer, part],
            place.on(section=place.core),
        )

    def start(self, part):
        @pl.when(self.sends_near)
        def _():
            self.near(part).start()

        @pl.when(self.sends_far)
        def _():
            self.far(part).start()

    def arrive(self, part):
        @pl.when(self.gets_near)
        def _():
            self.near(part).wait_recv()

        @pl.when(self.passes)
        def _():
            self.last(part).start()

        @pl.when(self.gets_far)
        def _():
            self.far(part).wait_recv()

    def drain(self):
        for part in range(3):

            @pl.when(self.sends_near)
            def _():
                self.near(part).wait_send()

            @pl.when(self.sends_far)
            def _():
                self.far(part).wait_send()

            @pl.when(self.passes)
            def _():
                self.last(part).wait_send()


def forward_kernel(
    tokens,
    cotangent,
    own_a,
    own_b,
    own_c,
    bias,
    cosine,
    sine_table,
    full_a_out,
    full_b_out,
    gains_out,
    seeded_out,
    x_out,
    low_out,
    q_out,
    kv_out,
    att_out,
    mid_out,
    hid_out,
    lse_out,
    full_a,
    full_b,
    full_c,
    low,
    x,
    normed,
    q,
    kv,
    att,
    mid,
    hid,
    lse,
    values_turned,
    turned_att,
    *sems,
):
    weight_sems, key_sems = sems[:7], sems[7:11]
    token_sem, swap_send, swap_recv, seed_sem, seed_send, seed_recv, save_sem = sems[11:]
    place = Place()
    weights = Weights(place, (own_a, own_b, own_c), (full_a, full_b, full_c), weight_sems)
    lse[...] = jnp.zeros_like(lse)
    kv[:, :, : 2 * PIECE, :] = jnp.zeros((2, 2, 2 * PIECE, kv.shape[-1]), jnp.bfloat16)
    place.meet(place.partners())
    group_rows = pl.ds(pl.multiple_of(place.group * PIECE, PIECE), PIECE)
    columns = pl.ds(pl.multiple_of(place.s * PIECE, PIECE), PIECE)

    def bring(whole, target, here, send, receive):
        kept = whole.at[4 * place.group + place.t, columns]
        sent = whole.at[4 * (1 - place.group) + place.t, columns]
        target = target.at[group_rows]
        return (
            pltpu.make_async_copy(kept, target, here),
            remote(sent, target, send, receive, place.on(seq=place.far)),
        )

    own_tokens, swap = bring(tokens, low, token_sem, swap_send, swap_recv)
    own_seed, seed_swap = bring(cotangent, seeded_out, seed_sem, seed_send, seed_recv)
    own_tokens.start()
    swap.start()
    weights.start_own(0)
    weights.begin(0, 0)
    weights.start_own(3)
    weights.start_own(1)
    for layer in range(2):
        weights.begin(layer, 3)
        weights.wait_own(layer, 3, place.core)
    gains = full_c.at[:, 0, 0]
    gains_out[...] = full_c[:, 0, 0]
    weights.forward(0, 0)
    own_tokens.wait()
    swap.wait()
    x_save = pltpu.make_async_copy(low, x_out, save_sem.at[16])
    x_save.start()
    x[...] = low[...].astype(jnp.float32)

    def saves(layer):
        pairs = [
            (low, low_out.at[layer]),
            (q, q_out.at[layer]),
            (kv.at[layer], kv_out.at[layer]),
            (att, att_out.at[layer]),
            (mid, mid_out.at[layer]),
            (hid, hid_out.at[layer]),
            (lse, lse_out.at[layer]),
        ]
        return [pltpu.make_async_copy(a, b, save_sem.at[i]) for i, (a, b) in enumerate(pairs)]

    def weight_saves(layer):
        copies = []
        for i, (a, b) in enumerate(((full_a, full_a_out), (full_b, full_b_out))):
            for pack in range(2):
                sem = save_sem.at[8 + 4 * layer + 2 * i + pack]
                copies.append(pltpu.make_async_copy(a.at[layer, pack], b.at[layer, pack], sem))
        return copies

    for layer in range(2):
        share = KeyShare(place, kv, layer, key_sems)
        unit, _ = normalize(x[...])
        normed[...] = (unit * gains[layer, 0:1]).astype(jnp.bfloat16)
        if layer == 0:
            weights.finish(0, 0)
            weights.begin(0, 1)
            weights.start_own(2)
        else:
            weights.finish(1, 0)
            weights.begin(1, 2)
            for copy in saves(0)[1:]:
                copy.wait()
        weights.need(layer, 0)
        for copy in weight_saves(layer)[:2]:
            copy.start()
        for part in range(3):
            lanes = pl.ds(part * LANES, LANES)
            keep = normed[...]
            mixed = dot_nt(keep, full_a[layer, 0, 0, lanes, :])
            q[:, lanes] = turn(mixed, cosine[...], sine_table[...]).astype(jnp.bfloat16)
            mixed = dot_nt(keep, full_a[layer, 0, 1, lanes, :])
            mixed = turn(mixed, cosine[...], sine_table[...]).astype(jnp.bfloat16)
            kv[layer, 0, 2 * PIECE : 3 * PIECE, lanes] = mixed[PIECE:]
            kv[layer, 0, 3 * PIECE :, lanes] = mixed[:PIECE]
            mixed = dot_nt(keep, full_a[layer, 1, 0, lanes, :]).astype(jnp.bfloat16)
            kv[layer, 1, 2 * PIECE : 3 * PIECE, lanes] = mixed[PIECE:]
            kv[layer, 1, 3 * PIECE :, lanes] = mixed[:PIECE]
            share.start(part)
        if layer == 0:
            weights.forward(0, 3)
            weights.forward(1, 3)
            weights.finish(0, 3)
            weights.finish(1, 3)
            own_seed.start()
            weights.begin(0, 2)
        else:
            weights.forward(1, 1)
        for part in range(3):
            lanes = pl.ds(part * LANES, LANES)
            share.arrive(part)
            values_turned[...] = kv[layer, 1, :, lanes].astype(jnp.float32).T.astype(jnp.bfloat16)
            for start, count in ((0, 4 * PIECE), (PIECE, 3 * PIECE)):
                queries = pl.ds(start, PIECE)
                att[queries, lanes] = attention_block(
                    q.at[queries, lanes],
                    kv.at[layer, 0, :count, lanes],
                    values_turned.at[:, :count],
                    bias.at[:count, queries],
                    lse.at[pl.ds(8 * part, 8), queries],
                    turned_att,
                )
            if part == 2 and layer == 0:
                seed_swap.start()
            if layer == 0:
                if part == 0:
                    weights.forward(0, 1)
                elif part == 1:
                    weights.finish(0, 1)
                    weights.begin(1, 0)
                else:
                    weights.forward(0, 2)
            else:
                if part == 1:
                    weights.finish(1, 1)
                elif part == 2:
                    weights.forward(1, 2)
        for copy in saves(layer)[1:4] + saves(layer)[6:]:
            copy.start()

        def project(part, _):
            lanes = pl.ds(pl.multiple_of(part * LANES, LANES), LANES)
            mid[:, lanes] = x[:, lanes] + dot_nn(att[...], full_a[layer, 1, 1, :, lanes])
            return 0

        lax.fori_loop(0, 3, project, 0)
        unit, _ = normalize(mid[...])
        normed[...] = (unit * gains[layer, 1:2]).astype(jnp.bfloat16)
        x[...] = mid[...] + gains[layer, 2:3]
        saves(layer)[4].start()
        weights.need(layer, 3)
        for part in range(2):
            if part == 1:
                weights.finish(layer, 2)
                if layer == 0:
                    weights.begin(1, 1)
            weights.need(layer, part + 1)
            if part == 1:
                for copy in weight_saves(layer)[2:]:
                    copy.start()

            def feed(rel, _):
                start = pl.multiple_of(rel * 768 + part * 384, 128)
                units = pl.ds(start, 384)
                shift = full_c[layer, 1, rel, 0:1, pl.ds(part * 384, 384)]
                tile = rel * 2 + part
                pre = dot_nn(normed[...], full_b[layer, 0, tile]) + shift
                hid[:, units] = pre.astype(jnp.bfloat16)
                active = gelu(pre).astype(jnp.bfloat16)
                x[...] += dot_nt(active, full_b[layer, 1, tile])
                return 0

            lax.fori_loop(0, 4, feed, 0)
        saves(layer)[5].start()
        if layer == 0:
            x_save.wait()
        else:
            saves(0)[0].wait()
        low[...] = x[...].astype(jnp.bfloat16)
        saves(layer)[0].start()
        x[...] = low[...].astype(jnp.float32)
        if layer == 0:
            weights.forward(1, 0)
    for copy in saves(1):
        copy.wait()
    for layer in range(2):
        for copy in weight_saves(layer):
            copy.wait()
        KeyShare(place, kv, layer, key_sems).drain()
    weights.drain()
    own_seed.wait()
    seed_swap.wait()


def run_forward(tokens, cotangent, own_a, own_b, own_c, bias, cosine, sine_table):
    shape = jax.ShapeDtypeStruct
    low_type, full_type = jnp.bfloat16, jnp.float32
    count = 2 * PIECE
    width = tokens.shape[-1]
    units = 8 * own_b.shape[-1]
    dma = pltpu.SemaphoreType.DMA
    return pl.pallas_call(
        forward_kernel,
        name="forward_layers",
        out_shape=[
            shape((2, 2, 2, width, width), low_type),
            shape((2, 2, 8, width, units // 8), low_type),
            shape((2, 8, width), full_type),
            shape((count, width), low_type),
            shape((count, width), low_type),
            shape((2, count, width), low_type),
            shape((2, count, width), low_type),
            shape((2, 2, 4 * PIECE, width), low_type),
            shape((2, count, width), low_type),
            shape((2, count, width), full_type),
            shape((2, count, units), low_type),
            shape((2, 24, count), full_type),
        ],
        in_specs=[HBM] * 5 + [VMEM] * 3,
        out_specs=[HBM] * 2 + [VMEM] + [HBM] * 9,
        scratch_shapes=[
            pltpu.VMEM((2, 2, 2, width, width), low_type),
            pltpu.VMEM((2, 2, 8, width, units // 8), low_type),
            pltpu.VMEM((2, 2, 4, 8, width), full_type),
            pltpu.VMEM((count, width), low_type),
            pltpu.VMEM((count, width), full_type),
            pltpu.VMEM((count, width), low_type),
            pltpu.VMEM((count, width), low_type),
            pltpu.VMEM((2, 2, 4 * PIECE, width), low_type),
            pltpu.VMEM((count, width), low_type),
            pltpu.VMEM((count, width), full_type),
            pltpu.VMEM((count, units), low_type),
            pltpu.VMEM((24, count), full_type),
            pltpu.VMEM((LANES, 4 * PIECE), low_type),
            pltpu.VMEM((LANES, PIECE), full_type),
            dma((4, 2)),
            dma((4, 2)),
            dma((4, 2)),
            dma((2, 4, 3)),
            dma((2, 4, 3)),
            dma((2, 4, 3)),
            dma((2, 4, 3)),
            dma((2, 3)),
            dma((2, 3)),
            dma((2, 3)),
            dma((2, 3)),
            dma,
            dma,
            dma,
            dma,
            dma,
            dma,
            dma((17,)),
        ],
        compiler_params=pltpu.CompilerParams(
            collective_id=1, has_side_effects=True, vmem_limit_bytes=62 * 1024 * 1024
        ),
        cost_estimate=pl.CostEstimate(
            flops=30_000_000_000, bytes_accessed=80_000_000, transcendentals=20_000_000
        ),
    )(tokens, cotangent, own_a, own_b, own_c, bias, cosine, sine_table)


def low_sum(*parts):
    total = parts[0].astype(jnp.float32)
    for part in parts[1:]:
        total = total + part.astype(jnp.float32)
    return total.astype(jnp.bfloat16)


class Spread:
    def __init__(self, place, source, stage, layer, out, sems):
        self.place, self.source, self.stage = place, source, stage
        self.layer, self.out = layer, out
        self.local, self.swap_send, self.swap_recv, self.hop_send, self.hop_recv = sems[:5]
        self.end_local, self.end_send, self.end_recv = sems[5:]
        self.groups = (place.group, 1 - place.group)

    def entry(self):
        place = self.place
        kept = self.source.at[pl.ds(pl.multiple_of(place.group * PIECE, PIECE), PIECE)]
        sent = self.source.at[pl.ds(pl.multiple_of((1 - place.group) * PIECE, PIECE), PIECE)]
        target = self.stage.at[0, place.group]
        here = pltpu.make_async_copy(kept, target, self.local)
        there = remote(sent, target, self.swap_send, self.swap_recv, place.on(seq=place.far))
        return here, there

    def take(self):
        self.entry()[0].start()

    def swap(self):
        self.entry()[1].start()

    def moves(self, half):
        place, group = self.place, self.groups[half]
        own = self.stage.at[0, group]
        first = self.stage.at[place.rel_one, group]
        second = self.stage.at[place.rel_two, group]
        third = self.stage.at[3, group]
        listed = (
            (own, first, place.hop_one),
            (own, second, place.hop_two),
            (first, third, place.hop_two),
        )
        return [
            remote(
                source,
                target,
                self.hop_send.at[half, i],
                self.hop_recv.at[half, i],
                place.on(tp=column),
            )
            for i, (source, target, column) in enumerate(listed)
        ]

    def hops(self, half):
        here, there = self.entry()
        if half == 0:
            here.wait()
        else:
            there.wait_recv()
        first, second, _ = self.moves(half)
        first.start()
        second.start()
        self.put(half, 0)

    def forward(self, half):
        first, _, third = self.moves(half)
        first.wait_recv()
        third.start()
        self.put(half, 1)

    def finish(self, half):
        _, second, third = self.moves(half)
        second.wait_recv()
        self.put(half, 2)
        third.wait_recv()
        self.put(half, 3)

    def ends(self, half, step):
        place, group = self.place, self.groups[half]
        rows = pl.ds(pl.multiple_of(place.s * PIECE, PIECE), PIECE)
        rel = (0, place.rel_one, place.rel_two, 3)[step]
        column = (place.t, place.hop_one, place.hop_two, 3 - place.t)[step]
        source, target = self.stage.at[rel, group], self.out.at[group, column, rows]
        here = pltpu.make_async_copy(source, target, self.end_local.at[half, step])
        there = remote(
            source,
            target,
            self.end_send.at[half, step],
            self.end_recv.at[half, step],
            place.on(section=place.core),
        )
        return here, there

    def put(self, half, step):
        @pl.when(self.place.s == self.layer)
        def _():
            self.ends(half, step)[0].start()

        @pl.when(self.place.s != self.layer)
        def _():
            self.ends(half, step)[1].start()

    def drain(self):
        self.entry()[1].wait_send()
        for half in range(2):
            for copy in self.moves(half):
                copy.wait_send()

        @pl.when(self.place.s == self.layer)
        def _():
            for half in range(2):
                for step in range(4):
                    here, there = self.ends(half, step)
                    here.wait()
                    there.wait_recv()

        @pl.when(self.place.s != self.layer)
        def _():
            for half in range(2):
                for step in range(4):
                    self.ends(half, step)[1].wait_send()


def spread_sems():
    dma = pltpu.SemaphoreType.DMA
    return [dma, dma, dma, dma((2, 3)), dma((2, 3)), dma((2, 4)), dma((2, 4)), dma((2, 4))]


class Sum:
    def __init__(self, place, source, total, buffers, sems, loaded=False, opens=None, waits=None):
        self.place, self.source, self.total = place, source, total
        self.inbox, self.hop_in, self.line_in = buffers
        self.loaded, self.opens, self.waits = loaded, opens, waits
        (
            self.mine_sem,
            self.chip_send,
            self.chip_recv,
            self.hop_send,
            self.hop_recv,
            self.line_send,
            self.line_recv,
            self.end_local,
            self.end_send,
            self.end_recv,
        ) = sems
        z = place.z
        self.outer = (z == 0) | (z == 3)
        self.inner = (z == 1) | (z == 2)
        self.order = (3, 1, 2, 0)

    def mine(self, rel):
        return pltpu.make_async_copy(
            self.source(self.place.s, rel), self.total(rel), self.mine_sem.at[rel]
        )

    def other(self, rel):
        return remote(
            self.source(self.place.core, rel),
            self.inbox.at[rel],
            self.chip_send.at[rel],
            self.chip_recv.at[rel],
            self.place.on(section=self.place.core),
        )

    def start(self):
        if self.waits is not None:
            pl.semaphore_wait(self.waits, 1)
        for rel in self.order:
            if self.inbox is not None:
                self.other(rel).start()
            if self.loaded:
                self.mine(rel).start()

    def load(self, travels=True):
        for rel in self.order:
            if self.loaded:
                self.mine(rel).wait()
            if self.inbox is not None:
                self.other(rel).wait_recv()
                total = self.total(rel)
                total[...] = low_sum(total[...], self.inbox[rel])
            if travels and rel == 3:
                self.moves()[0].start()
            elif travels and rel == 2:
                self.moves()[1].start()
        if self.opens is not None:
            pl.semaphore_signal(
                self.opens,
                inc=1,
                device_id=self.place.on(section=self.place.core),
                device_id_type=MESH,
            )

    def moves(self):
        place = self.place
        listed = (
            (3, 0, place.hop_two),
            (place.rel_two, 1, place.hop_two),
            (place.rel_one, 2, place.hop_one),
        )
        return [
            remote(
                self.total(rel),
                self.hop_in.at[slot],
                self.hop_send.at[slot],
                self.hop_recv.at[slot],
                place.on(tp=column),
            )
            for rel, slot, column in listed
        ]

    def middle(self):
        first, _, third = self.moves()
        first.wait_recv()
        total = self.total(self.place.rel_one)
        total[...] = low_sum(total[...], self.hop_in[0])
        third.start()

    def lines(self):
        place = self.place
        own, line_sum = self.total(0), self.total(1)
        listed = (
            (own, self.line_in.at[0], place.twin),
            (own, self.line_in.at[1], 3 - place.z),
            (line_sum, line_sum, place.twin),
        )
        return [
            remote(
                source,
                target,
                self.line_send.at[i],
                self.line_recv.at[i],
                place.on(seq=plane),
            )
            for i, (source, target, plane) in enumerate(listed)
        ]

    def gather(self, save=None):
        _, second, third = self.moves()
        second.wait_recv()
        third.wait_recv()
        total = self.total(0)
        total[...] = low_sum(total[...], self.hop_in[1], self.hop_in[2])
        second.wait_send()
        third.wait_send()
        if save is not None:
            save.start()
        else:
            self.enter_line()

    def resume(self, saved):
        saved.wait()
        self.enter_line()

    def enter_line(self):
        @pl.when(self.outer)
        def _():
            self.lines()[0].start()

    def line_one(self):
        @pl.when(self.inner)
        def _():
            self.lines()[0].wait_recv()
            total = self.total(0)
            total[...] = low_sum(total[...], self.line_in[0])
            self.lines()[1].start()

    def line_two(self):
        @pl.when(self.inner)
        def _():
            self.lines()[1].wait_recv()
            self.total(1)[...] = low_sum(self.total(0)[...], self.line_in[1])
            self.lines()[2].start()

    def line_three(self):
        @pl.when(self.outer)
        def _():
            self.lines()[2].wait_recv()

    def ends(self, target):
        here = pltpu.make_async_copy(self.total(1), target, self.end_local)
        there = remote(
            self.total(1),
            target,
            self.end_send,
            self.end_recv,
            self.place.on(section=self.place.core),
        )
        return here, there

    def store(self, save):
        self.line_three()
        save.start()

    def finish(self, layer, target):
        self.line_three()
        here, there = self.ends(target)

        @pl.when(self.place.s == layer)
        def _():
            here.start()

        @pl.when(self.place.s != layer)
        def _():
            there.start()

    def drain_exchange(self):
        if self.inbox is not None:
            for rel in range(4):
                self.other(rel).wait_send()

    def drain_end(self, layer, target):
        here, there = self.ends(target)

        @pl.when(self.place.s == layer)
        def _():
            here.wait()
            there.wait_recv()

        @pl.when(self.place.s != layer)
        def _():
            there.wait_send()

    def drain_plane(self):
        self.drain_exchange()
        self.moves()[0].wait_send()

    def drain_line(self):
        @pl.when(self.outer)
        def _():
            self.lines()[0].wait_send()

        @pl.when(self.inner)
        def _():
            self.lines()[1].wait_send()
            self.lines()[2].wait_send()


def sum_sems():
    dma = pltpu.SemaphoreType.DMA
    return [dma((4,))] * 3 + [dma((3,))] * 4 + [dma] * 3


SUM_SEMS = 10


def sum_buffers(piece, counts):
    return [pltpu.VMEM((count,) + piece, jnp.bfloat16) for count in counts]


def attention_sums(place, grads, buffers, sems):
    sums = []
    for i in range(2):
        total, inbox, hop_in, line_in = buffers[4 * i : 4 * i + 4]

        def source(pack, rel, i=i):
            return grads.at[pack, i, rel]

        def kept(rel, total=total):
            return total.at[rel]

        own_sems = sems[SUM_SEMS * i : SUM_SEMS * (i + 1)]
        sums.append(Sum(place, source, kept, (inbox, hop_in, line_in), own_sems, loaded=True))
    return sums


def feed_sums(place, wb, buffers, sems, gate):
    inbox, sums = buffers[0], []
    for i in range(2):

        def source(pack, rel, i=i):
            return wb.at[pack, rel * 2 + i]

        def kept(rel, i=i):
            return wb.at[place.s, rel * 2 + i]

        own_sems = sems[SUM_SEMS * i : SUM_SEMS * (i + 1)]
        gates = {"opens": gate} if i == 0 else {"waits": gate}
        at = min(i, buffers[1].shape[0] - 1)
        sums.append(Sum(place, source, kept, (inbox, buffers[1].at[at], None), own_sems, **gates))
    return sums


def feed_buffers(piece, count):
    kind = jnp.bfloat16
    return [pltpu.VMEM((4,) + piece, kind), pltpu.VMEM((count, 3) + piece, kind)]


def line_sum(place, total, line_in, sems):
    return Sum(place, None, lambda rel: total.at[rel], (None, None, line_in), sems)


class KeyReturn:
    def __init__(self, place, kv, near_in, far_in, sems):
        self.place, self.kv = place, kv
        self.near_in, self.far_in, self.pass_in = near_in, far_in, far_in
        (
            self.near_send,
            self.near_recv,
            self.far_send,
            self.far_recv,
            self.pass_send,
            self.pass_recv,
        ) = sems
        s, odd = place.s, place.half == 1
        self.is_third = (s == 0) & odd
        self.is_fourth = (s == 1) & odd
        self.is_second = (s == 1) & ~odd
        self.is_first = (s == 0) & ~odd

    def sources(self, start, part):
        return self.kv.at[:, pl.ds(start, PIECE), pl.ds(part * LANES, LANES)]

    def copies(self, part):
        place = self.place
        lanes = pl.ds(part * LANES, LANES)
        near = remote(
            self.sources(PIECE, part),
            self.near_in.at[:, :, lanes],
            self.near_send.at[part],
            self.near_recv.at[part],
            place.on(section=place.core, seq=place.z - (1 - place.s) * place.half),
        )
        far = remote(
            self.sources(0, part),
            self.far_in.at[:, :, lanes],
            self.far_send.at[part],
            self.far_recv.at[part],
            place.on(seq=place.twin),
        )
        passed = remote(
            self.sources(0, part),
            self.pass_in.at[:, :, lanes],
            self.pass_send.at[part],
            self.pass_recv.at[part],
            place.on(section=place.core),
        )
        return near, far, passed

    def start(self, part):
        near, far, passed = self.copies(part)

        @pl.when(self.is_fourth)
        def _():
            passed.start()
            near.start()

        @pl.when(self.is_second)
        def _():
            near.start()

        @pl.when(self.is_third)
        def _():
            far.start()

    def relay(self, part):
        near, _, passed = self.copies(part)
        lanes = pl.ds(part * LANES, LANES)

        @pl.when(self.is_third)
        def _():
            passed.wait_recv()
            self.kv[:, PIECE : 2 * PIECE, lanes] = low_sum(
                self.kv[:, PIECE : 2 * PIECE, lanes], self.pass_in[:, :, lanes]
            )
            near.start()

    def collect(self, part):
        near, far, _ = self.copies(part)
        lanes = pl.ds(part * LANES, LANES)
        clean = pl.ds(2 * PIECE, PIECE)

        @pl.when(~self.is_fourth)
        def _():
            near.wait_recv()
            self.kv[:, clean, lanes] = low_sum(self.kv[:, clean, lanes], self.near_in[:, :, lanes])

        @pl.when(self.is_first)
        def _():
            far.wait_recv()
            self.kv[:, clean, lanes] = low_sum(self.kv[:, clean, lanes], self.far_in[:, :, lanes])

    def drain(self):
        for part in range(3):
            near, far, passed = self.copies(part)

            @pl.when(self.is_fourth)
            def _():
                passed.wait_send()
                near.wait_send()

            @pl.when(self.is_second)
            def _():
                near.wait_send()

            @pl.when(self.is_third)
            def _():
                far.wait_send()
                near.wait_send()


def normalize_back(grads, unit, scale, gain):
    lifted = grads * gain
    mean = jnp.mean(lifted, axis=-1, keepdims=True)
    along = jnp.mean(lifted * unit, axis=-1, keepdims=True)
    return scale * (lifted - mean - unit * along)


def attention_back(q_ref, grad_ref, att_ref, keys, values, keys_turned, bias, lse, sums, turned, count):
    turned[...] = (grad_ref[...].astype(jnp.float32) * att_ref[...].astype(jnp.float32)).T

    def one(head, _):
        rows = pl.ds(pl.multiple_of(head * HDIM, HDIM), HDIM)
        query = q_ref[...] * head_mask(head, 0.125).astype(jnp.bfloat16)
        grad = grad_ref[...] * head_mask(head, 1.0).astype(jnp.bfloat16)
        delta = jnp.sum(turned[rows, :], axis=0, keepdims=True)
        scores = dot_nt(keys[...], query) + bias[...].astype(jnp.float32)
        probs = jnp.exp(scores - lse[pl.ds(head, 1), :])
        grad_scores = (probs * (dot_nt(values[...], grad) - delta)).astype(jnp.bfloat16)
        sums[0, :count] += dot_nn(grad_scores, query)
        sums[1, :count] += dot_nn(probs.astype(jnp.bfloat16), grad)
        turned[rows, :] = dot_nn(keys_turned[rows, :], grad_scores) * 0.125
        return 0

    lax.fori_loop(0, LANES // HDIM, one, 0)
    q_ref[...] = turned[...].T.astype(jnp.bfloat16)


def backward_layer(layer, refs, place, tick, key_sems, sems, tile_sems):
    (
        full_a,
        full_b,
        grad_in,
        x_in,
        q_in,
        kv_in,
        att_in,
        mid_in,
        hid_in,
        lse_in,
        gains,
        bias,
        cosine,
        sine_table,
        grads_a,
        grad_out,
        small_out,
        wa,
        wb,
        low,
        q,
        kv,
        att,
        mid,
        hid,
        grad,
        gathered,
        grad_low,
        grad_att,
        near_in,
        far_in,
        sums,
        keys_turned,
        turned_q,
        grad_turned,
        normed_turned,
        lse,
    ) = refs
    share = KeyReturn(place, kv, near_in, far_in, key_sems)
    pairs = [
        (grad_in, grad_low),
        (mid_in.at[layer], mid),
        (hid_in.at[layer], hid),
        (full_a.at[layer], wa),
        (att_in.at[layer], att),
        (q_in.at[layer], q),
        (kv_in.at[layer], kv),
        (x_in, low),
        (lse_in.at[layer], lse),
    ]
    loads = [pltpu.make_async_copy(a, b, sems.at[i]) for i, (a, b) in enumerate(pairs)]
    def tile_copy(pack, tile):
        return pltpu.make_async_copy(
            full_b.at[layer, pack, tile], wb.at[pack, tile], tile_sems.at[pack, tile]
        )

    for copy in loads[:3]:
        copy.start()
    for part in range(2):
        for rel in range(4):
            for pack in (1, 0):
                tile_copy(pack, rel * 2 + part).start()
    for copy in loads[3:]:
        copy.start()
    tick()
    gain_one, gain_two = gains[layer, 0:1], gains[layer, 1:2]
    for copy in loads[:3]:
        copy.wait()
    small_out[...] = jnp.zeros_like(small_out)

    def by_rows(step):
        def one(i, _):
            step(pl.ds(pl.multiple_of(i * 128, 128), 128))
            return 0

        lax.fori_loop(0, grad.shape[0] // 128, one, 0)

    def enter(rows):
        incoming = grad_low[rows, :].astype(jnp.float32)
        grad[rows, :] = incoming
        small_out[2:3] += jnp.sum(incoming, axis=0, keepdims=True)
        grad_turned[:, rows] = incoming.T.astype(jnp.bfloat16)
        unit, _ = normalize(mid[rows, :])
        normed_turned[:, rows] = (unit * gain_two).T.astype(jnp.bfloat16)
        gathered[rows, :] = jnp.zeros((128, grad.shape[1]), jnp.float32)

    by_rows(enter)
    tick()

    def feed(part, rel):
        start = pl.multiple_of(rel * 768 + part * 384, 128)
        units = pl.ds(start, 384)
        tile = rel * 2 + part
        pre = hid[:, units].astype(jnp.float32)
        squared = pre * pre
        bent = jnp.tanh(0.7978845608028654 * pre * (1.0 + 0.044715 * squared))
        raised = 0.5 * (1.0 + bent)
        active = (pre * raised).astype(jnp.bfloat16)
        slope = raised + 0.5 * pre * (1.0 - bent * bent) * (
            0.7978845608028654 * (1.0 + 3 * 0.044715 * squared)
        )
        tile_copy(1, tile).wait()
        grad_act = dot_nn(grad_low[...], wb[1, tile])
        grad_pre = (grad_act * slope).astype(jnp.bfloat16)
        total = jnp.sum(grad_pre.astype(jnp.float32), axis=0, keepdims=True)
        small_out[pl.ds(4 + rel, 1), pl.ds(part * 384, 384)] = total
        wb[1, tile] = dot_nn(grad_turned[...], active).astype(jnp.bfloat16)
        tile_copy(0, tile).wait()
        gathered[...] += dot_nt(grad_pre, wb[0, tile])
        wb[0, tile] = dot_nn(normed_turned[...], grad_pre).astype(jnp.bfloat16)

    for part in range(2):
        for pair in range(2):

            def one(i, _):
                feed(part, 2 * pair + i)
                return 0

            lax.fori_loop(0, 2, one, 0)
            tick()

    def between(rows):
        found = gathered[rows, :]
        unit, scale = normalize(mid[rows, :])
        small_out[1:2] += jnp.sum(found * unit, axis=0, keepdims=True)
        total = grad[rows, :] + normalize_back(found, unit, scale, gain_two)
        grad[rows, :] = total
        grad_low[rows, :] = total.astype(jnp.bfloat16)

    by_rows(between)
    for copy in loads[3:]:
        copy.wait()

    def project(part, _):
        lanes = pl.ds(pl.multiple_of(part * LANES, LANES), LANES)
        grad_att[:, lanes] = dot_nt(grad_low[...], wa[1, 1, lanes, :]).astype(jnp.bfloat16)
        wa[1, 1, lanes, :] = dot_tn(att[:, lanes], grad_low[...]).astype(jnp.bfloat16)
        return 0

    lax.fori_loop(0, 3, project, 0)
    tick()
    for part in range(3):
        lanes = pl.ds(part * LANES, LANES)
        sums[...] = jnp.zeros_like(sums)
        keys_turned[...] = kv[0, :, lanes].astype(jnp.float32).T.astype(jnp.bfloat16)
        for start, count in ((0, 4 * PIECE), (PIECE, 3 * PIECE)):
            rows = pl.ds(start, PIECE)
            attention_back(
                q.at[rows, lanes],
                grad_att.at[rows, lanes],
                att.at[rows, lanes],
                kv.at[0, :count, lanes],
                kv.at[1, :count, lanes],
                keys_turned.at[:, :count],
                bias.at[:count, rows],
                lse.at[pl.ds(8 * part, 8), rows],
                sums,
                turned_q,
                count,
            )
            if start == 0:
                tick()
        kv[:, :, lanes] = sums[...].astype(jnp.bfloat16)
        share.start(part)
        if part > 0:
            share.relay(part - 1)
        tick()
    normed = grad_att

    def again(rows):
        unit, _ = normalize(low[rows, :].astype(jnp.float32))
        normed[rows, :] = (unit * gain_one).astype(jnp.bfloat16)

    by_rows(again)

    def turned(part, _):
        lanes = pl.ds(pl.multiple_of(part * LANES, LANES), LANES)
        raw = turn(q[:, lanes].astype(jnp.float32), cosine[...], -sine_table[...])
        raw = raw.astype(jnp.bfloat16)
        found = dot_nn(raw, wa[0, 0, lanes, :])

        @pl.when(part == 0)
        def _():
            gathered[...] = found

        @pl.when(part > 0)
        def _():
            gathered[...] += found

        wa[0, 0, lanes, :] = dot_tn(raw, normed[...]).astype(jnp.bfloat16)
        return 0

    lax.fori_loop(0, 3, turned, 0)
    share.relay(2)
    tick()
    for part in range(3):
        share.collect(part)

    def keyed(part, _):
        lanes = pl.ds(pl.multiple_of(part * LANES, LANES), LANES)
        noisy, clean = pl.ds(3 * PIECE, PIECE), pl.ds(2 * PIECE, PIECE)
        raw = jnp.concatenate([kv[0, noisy, lanes], kv[0, clean, lanes]], axis=0)
        raw = turn(raw.astype(jnp.float32), cosine[...], -sine_table[...]).astype(jnp.bfloat16)
        gathered[...] += dot_nn(raw, wa[0, 1, lanes, :])
        wa[0, 1, lanes, :] = dot_tn(raw, normed[...]).astype(jnp.bfloat16)
        raw = jnp.concatenate([kv[1, noisy, lanes], kv[1, clean, lanes]], axis=0)
        gathered[...] += dot_nn(raw, wa[1, 0, lanes, :])
        wa[1, 0, lanes, :] = dot_tn(raw, normed[...]).astype(jnp.bfloat16)
        return 0

    lax.fori_loop(0, 3, keyed, 0)
    tick()
    save_a = pltpu.make_async_copy(wa, grads_a, sems.at[10])
    save_a.start()

    def leave(rows):
        found = gathered[rows, :]
        unit, scale = normalize(low[rows, :].astype(jnp.float32))
        small_out[0:1] += jnp.sum(found * unit, axis=0, keepdims=True)
        total = grad[rows, :] + normalize_back(found, unit, scale, gain_one)
        grad_low[rows, :] = total.astype(jnp.bfloat16)

    by_rows(leave)
    save_grad = pltpu.make_async_copy(grad_low, grad_out, sems.at[11])
    save_grad.start()
    tick()
    share.drain()
    save_a.wait()
    save_grad.wait()


class Ticks:
    def __init__(self, groups):
        self.groups = list(groups)

    def __call__(self):
        if self.groups:
            for step in self.groups.pop(0):
                step()

    def rest(self):
        while self.groups:
            self()


def backward_buffers(width, units):
    low, full, count = jnp.bfloat16, jnp.float32, 2 * PIECE
    return [
        pltpu.VMEM((2, 2, width, width), low),
        pltpu.VMEM((2, 8, width, units // 8), low),
        pltpu.VMEM((count, width), low),
        pltpu.VMEM((count, width), low),
        pltpu.VMEM((2, 4 * PIECE, width), low),
        pltpu.VMEM((count, width), low),
        pltpu.VMEM((count, width), full),
        pltpu.VMEM((count, units), low),
        pltpu.VMEM((count, width), full),
        pltpu.VMEM((count, width), full),
        pltpu.VMEM((count, width), low),
        pltpu.VMEM((count, width), low),
        pltpu.VMEM((2, PIECE, width), low),
        pltpu.VMEM((2, PIECE, width), low),
        pltpu.VMEM((2, 4 * PIECE, LANES), full),
        pltpu.VMEM((LANES, 4 * PIECE), low),
        pltpu.VMEM((LANES, PIECE), full),
        pltpu.VMEM((width, count), low),
        pltpu.VMEM((width, count), low),
        pltpu.VMEM((24, count), full),
    ]


def backward_sems():
    dma = pltpu.SemaphoreType.DMA
    return [dma((3,))] * 6 + [dma((12,)), dma((2, 8))]


BUFFERS = 20


def later(step, *args):
    return lambda: step(*args)


def second_kernel(*refs):
    ins, refs = refs[:15], refs[15:]
    (grads_a, grad_out, small_out, out, carry_one, carry), refs = refs[:6], refs[6:]
    buffers, stages, feed, refs = refs[:BUFFERS], refs[BUFFERS : BUFFERS + 2], refs[22:24], refs[24:]
    sems, feed_sem, gate, carry_sem = refs[:24], refs[24:-2], refs[-2], refs[-1]
    low_both = ins[14]
    place = Place()
    place.meet(place.partners())
    zero, last = [
        Spread(place, low_both.at[i], stages[i], i, out, sems[8 + 8 * i : 16 + 8 * i])
        for i in range(2)
    ]
    one, two = feed_sums(place, buffers[1], feed, feed_sem, gate)
    carries = [
        pltpu.make_async_copy(two.total(rel), carry.at[rel], carry_sem.at[rel]) for rel in range(4)
    ]
    save_one = pltpu.make_async_copy(one.total(0), carry_one, carry_sem.at[4])

    def hand_on():
        two.load(travels=False)
        for copy in carries:
            copy.start()

    tick = Ticks(
        [
            [zero.take, last.take, zero.swap, later(zero.hops, 0), later(last.hops, 0)],
            [],
            [later(zero.forward, 0)],
            [one.start, last.swap],
            [later(zero.hops, 1), later(last.forward, 0)],
            [later(zero.finish, 0)],
            [one.load],
            [later(zero.forward, 1), two.start],
            [later(last.finish, 0)],
            [one.middle],
            [later(last.hops, 1), later(zero.finish, 1)],
            [],
            [hand_on],
            [later(one.gather, save_one), later(last.forward, 1)],
            [],
            [later(last.finish, 1)],
        ]
    )
    body = ins[:3] + (low_both.at[0],) + ins[4:14] + (grads_a, grad_out, small_out) + buffers
    backward_layer(1, body, place, tick, sems[:6], sems[6], sems[7])
    tick.rest()
    zero.drain()
    last.drain()
    one.drain_plane()
    save_one.wait()
    two.drain_exchange()
    for copy in carries:
        copy.wait()


def first_kernel(*refs):
    ins, refs = refs[:17], refs[17:]
    (grads_a, grad_out, small_out, out, done, carry_out), refs = refs[:6], refs[6:]
    buffers, stage, refs = refs[:BUFFERS], refs[BUFFERS], refs[BUFFERS + 1 :]
    feed, (total, hop_in, line_in, line_total, line_in_one), refs = refs[:2], refs[2:7], refs[7:]
    sems, feed_sem, kept_sem, line_sem = refs[:16], refs[16:36], refs[36:46], refs[46:56]
    gate, carry_sem = refs[56:]
    carry_one, carry, prior_grad = ins[14:]
    place = Place()
    place.meet(place.partners())
    back = Spread(place, prior_grad, stage, 1, out, sems[8:16])
    one, two = feed_sums(place, buffers[1], feed, feed_sem, gate)
    kept = Sum(
        place,
        lambda pack, rel: carry.at[rel],
        lambda rel: total.at[rel],
        (None, hop_in, line_in),
        kept_sem,
        loaded=True,
    )
    line = line_sum(place, line_total, line_in_one, line_sem)
    line_load = pltpu.make_async_copy(carry_one, line_total.at[0], carry_sem.at[0])
    saves = [
        pltpu.make_async_copy(line.total(1), done.at[0], carry_sem.at[1]),
        pltpu.make_async_copy(kept.total(1), done.at[1], carry_sem.at[2]),
        pltpu.make_async_copy(one.total(0), carry_out.at[0], carry_sem.at[3]),
        pltpu.make_async_copy(two.total(0), carry_out.at[1], carry_sem.at[4]),
    ]
    tick = Ticks(
        [
            [back.take, back.swap, line_load.start, kept.start, later(back.hops, 0)],
            [later(line.resume, line_load), kept.load],
            [later(back.forward, 0)],
            [one.start, line.line_one],
            [kept.middle, later(back.hops, 1)],
            [line.line_two, later(back.finish, 0)],
            [one.load],
            [kept.gather, two.start],
            [later(back.forward, 1), later(line.store, saves[0])],
            [kept.line_one],
            [one.middle, two.load],
            [kept.line_two, later(back.finish, 1)],
            [],
            [later(one.gather, saves[2]), later(kept.store, saves[1])],
            [two.middle],
            [],
            [later(two.gather, saves[3])],
        ]
    )
    body = ins[:14] + (grads_a, grad_out, small_out) + buffers
    backward_layer(0, body, place, tick, sems[:6], sems[6], sems[7])
    tick.rest()
    back.drain()
    for item in (kept, one, two):
        item.drain_plane()
    line.drain_line()
    kept.drain_line()
    for copy in saves:
        copy.wait()


def last_kernel(*refs):
    priors, (done, carry, grad_zero, small_zero, small_one), refs = refs[:2], refs[2:7], refs[7:]
    (out, final_a, final_b, small), refs = refs[:4], refs[4:]
    held, stage, (small_in, extra), refs = refs[:16], refs[16], refs[17:19], refs[19:]
    (line_total, line_in), sems = refs[:2], refs[2:]
    held_sem, spread_sem, line_sem, sems = sems[:40], sems[40:48], sems[48:68], sems[68:]
    tiny_send, tiny_recv, carry_sem, end_local, end_send, end_recv = sems
    place = Place()
    place.meet(place.partners())
    sums = []
    for i in range(2):
        sums += attention_sums(
            place, priors[i], held[8 * i : 8 * i + 8], held_sem[20 * i : 20 * i + 20]
        )
    lines, loads = [], []
    for i in range(2):
        lines.append(line_sum(place, line_total.at[i], line_in.at[i], line_sem[10 * i : 10 * i + 10]))
        loads.append(pltpu.make_async_copy(carry.at[i], line_total.at[i, 0], carry_sem.at[i]))
    back = Spread(place, grad_zero, stage, 0, out, spread_sem)
    targets = [final_a.at[place.s, 0], final_a.at[place.s, 1]] * 2
    halves = [final_b.at[place.s, :, pl.ds(384 * i, 384)] for i in range(2)]
    layers = (1, 1, 0, 0)
    small[0], small[1] = small_zero[...], small_one[...]
    rows_beside = ((4, 5, 6, 7), (5, 4, 7, 6), (6, 7, 4, 5), (4, 5, 6, 7), (4, 5, 6, 7))
    partners = (
        place.on(section=place.core),
        place.on(tp=place.beside_x),
        place.on(tp=place.beside_y),
        place.on(seq=place.twin),
        place.on(seq=place.far),
    )

    def done_ends(i):
        here = pltpu.make_async_copy(done.at[i], halves[i], end_local.at[i])
        there = remote(
            done.at[i], halves[i], end_send.at[i], end_recv.at[i], place.on(section=place.core)
        )
        return here, there

    def done_start():
        @pl.when(place.s == 1)
        def _():
            for i in range(2):
                done_ends(i)[0].start()

        @pl.when(place.s == 0)
        def _():
            for i in range(2):
                done_ends(i)[1].start()

    def done_wait():
        @pl.when(place.s == 1)
        def _():
            for i in range(2):
                here, there = done_ends(i)
                here.wait()
                there.wait_recv()

        @pl.when(place.s == 0)
        def _():
            for i in range(2):
                done_ends(i)[1].wait_send()

    def tiny(i):
        return remote(extra.at[i], small_in.at[i], tiny_send.at[i], tiny_recv.at[i], partners[i])

    def tiny_start(i):
        extra[i] = small[...]
        tiny(i).start()

    def tiny_end(i):
        tiny(i).wait_recv()
        for layer in range(2):
            small[layer, 0:4] = extra[i, layer, 0:4] + small_in[i, layer, 0:4]
            for row, other in enumerate(rows_beside[i]):
                at = row + 4
                small[layer, at : at + 1] = (
                    extra[i, layer, at : at + 1] + small_in[i, layer, other : other + 1]
                )

    back.take()
    sums[0].start()
    for load in loads:
        load.start()
    back.swap()
    tiny_start(0)
    sums[1].start()
    back.hops(0)
    for line, load in zip(lines, loads):
        line.resume(load)
    sums[0].load()
    sums[2].start()
    sums[1].load()
    sums[3].start()
    tiny_end(0)
    tiny_start(1)
    back.forward(0)
    sums[2].load()
    done_start()
    lines[0].line_one()
    sums[0].middle()
    sums[3].load()
    lines[1].line_one()
    sums[1].middle()
    lines[0].line_two()
    tiny_end(1)
    tiny_start(2)
    sums[0].gather()
    sums[2].middle()
    lines[1].line_two()
    sums[1].gather()
    sums[3].middle()
    back.hops(1)
    lines[0].finish(0, halves[0])
    sums[0].line_one()
    sums[2].gather()
    sums[1].line_one()
    tiny_end(2)
    tiny_start(3)
    lines[1].finish(0, halves[1])
    back.finish(0)
    sums[3].gather()
    sums[0].line_two()
    sums[2].line_one()
    sums[1].line_two()
    back.forward(1)
    sums[3].line_one()
    tiny_end(3)
    tiny_start(4)
    sums[0].finish(1, targets[0])
    sums[2].line_two()
    sums[1].finish(1, targets[1])
    sums[3].line_two()
    back.finish(1)
    sums[2].finish(0, targets[2])
    sums[3].finish(0, targets[3])
    tiny_end(4)
    for item, layer, target in zip(sums, layers, targets):
        item.drain_plane()
        item.drain_line()
        item.drain_end(layer, target)
    for item, target in zip(lines, halves):
        item.drain_line()
        item.drain_end(0, target)
    done_wait()
    back.drain()
    for i in range(5):
        tiny(i).wait_send()


def call(kernel, name, number, ins, spaces, shapes, out_spaces, scratch, flops, moved):
    return pl.pallas_call(
        kernel,
        name=name,
        out_shape=[jax.ShapeDtypeStruct(shape, kind) for shape, kind in shapes],
        in_specs=spaces,
        out_specs=out_spaces,
        scratch_shapes=scratch,
        compiler_params=pltpu.CompilerParams(
            collective_id=number, has_side_effects=True, vmem_limit_bytes=62 * 1024 * 1024
        ),
        cost_estimate=pl.CostEstimate(
            flops=flops, bytes_accessed=moved, transcendentals=20_000_000
        ),
    )(*ins)


def run_backward(full_a, full_b, seeded, tokens, low_both, kept, gains, bias, tables):
    low, full, count = jnp.bfloat16, jnp.float32, 2 * PIECE
    width, units = full_a.shape[-1], 8 * full_b.shape[-1]
    grads = [
        ((2, 2, width, width), low),
        ((count, width), low),
        ((8, width), full),
    ]
    out = ((2, 4, count, width), low)
    row_piece, tile_piece = (192, width), (width, units // 8)
    final_a, final_b = ((2, 2) + row_piece, low), ((2, width, 2 * tile_piece[1]), low)
    carry_one, carry, two_tiles = (tile_piece, low), ((4,) + tile_piece, low), ((2,) + tile_piece, low)
    stage = pltpu.VMEM((4, 2, PIECE, width), low)
    dma, gate = pltpu.SemaphoreType.DMA, pltpu.SemaphoreType.REGULAR
    common = (*kept, gains, bias, *tables)
    common_spaces = [HBM] * 10 + [VMEM] * 4
    held = sum_buffers(row_piece, (4, 4, 3, 2) * 2)
    second = call(
        second_kernel,
        "backward_second",
        2,
        (full_a, full_b, seeded, tokens) + common + (low_both,),
        common_spaces + [HBM],
        grads + [out, carry_one, carry],
        [HBM] * 2 + [VMEM] + [HBM] * 3,
        backward_buffers(width, units)
        + [stage, stage]
        + feed_buffers(tile_piece, 1)
        + backward_sems()
        + spread_sems()
        + spread_sems()
        + sum_sems()
        + sum_sems()
        + [gate, dma((5,))],
        40_000_000_000,
        80_000_000,
    )
    prior_a, grad_one, small_one, layer_out, carried_one, carried = second
    first = call(
        first_kernel,
        "backward_first",
        3,
        (full_a, full_b, grad_one, tokens) + common + (carried_one, carried, grad_one),
        common_spaces + [HBM] * 3,
        grads + [out, two_tiles, two_tiles],
        [HBM] * 2 + [VMEM] + [HBM] * 3,
        backward_buffers(width, units)
        + [stage]
        + feed_buffers(tile_piece, 2)
        + sum_buffers(tile_piece, (4, 3, 2, 2, 2))
        + backward_sems()
        + spread_sems()
        + sum_sems()
        + sum_sems()
        + sum_sems()
        + sum_sems()
        + [gate, dma((5,))],
        40_000_000_000,
        80_000_000,
    )
    grads_a, grad_zero, small_zero, out_one, done, carried = first
    by_shard = (2, 2, 4, 192, width)
    last = call(
        last_kernel,
        "sum_and_spread",
        4,
        (prior_a.reshape(by_shard), grads_a.reshape(by_shard), done, carried, grad_zero)
        + (small_zero, small_one),
        [HBM] * 5 + [VMEM] * 2,
        [out, final_a, final_b, ((2, 8, width), full)],
        [HBM] * 3 + [VMEM],
        held
        + held
        + [stage]
        + [pltpu.VMEM((5, 2, 8, width), full), pltpu.VMEM((5, 2, 8, width), full)]
        + [pltpu.VMEM((2, 2) + tile_piece, low), pltpu.VMEM((2, 2) + tile_piece, low)]
        + sum_sems()
        + sum_sems()
        + sum_sems()
        + sum_sems()
        + spread_sems()
        + sum_sems()
        + sum_sems()
        + [dma((5,)), dma((5,))]
        + [dma((2,))] * 4,
        100_000_000,
        40_000_000,
    )
    out_zero, final_a, final_b, small = last
    return layer_out, (out_zero, out_one), final_a, final_b, small


def spread(
    layer_input,
    cotangent,
    doc_lengths,
    ln1_gain,
    w_qkv,
    w_out,
    ln2_gain,
    w_up,
    b_up,
    w_down,
    b_down,
):
    s, t, z = (lax.axis_index(name) for name in ("section", "tp", "seq"))
    micros, rows, width_pos, width = layer_input.shape
    half, group = z % 2, z // 2

    own_a = jnp.stack(
        [
            jnp.stack([w_qkv[0, :, 0].T, w_qkv[0, :, 1].T]),
            jnp.stack([w_qkv[0, :, 2].T, w_out[0]]),
        ]
    )
    shard = w_up.shape[-1]
    own_b = jnp.stack([w_up[0], w_down[0].T]).reshape(2, width, 2, shard // 2).transpose(0, 2, 1, 3)
    gains = jnp.concatenate([ln1_gain, ln2_gain, b_down, jnp.zeros((5, width), jnp.float32)])
    own_c = jnp.stack([gains, jnp.concatenate([b_up, jnp.zeros((7, width), jnp.float32)])])

    block = 2 * half + s
    lengths = doc_lengths.reshape(micros * rows, -1)
    lengths = lax.dynamic_index_in_dim(lengths, 4 * group + t, 0, keepdims=False)
    ends = jnp.cumsum(lengths)
    piece_pos = jnp.arange(PIECE)
    query_base = jnp.tile(block * PIECE + piece_pos, 2)
    key_base = jnp.concatenate([(block - 2 + i) * PIECE + piece_pos for i in (0, 1, 2, 2)])
    query_noisy = jnp.arange(2 * PIECE) < PIECE
    key_noisy = jnp.arange(4 * PIECE) >= 3 * PIECE

    def docs_of(base):
        return jnp.sum((base[:, None] >= ends[None, :]).astype(jnp.int32), axis=-1)

    query_block, key_block = query_base[None, :] // BLOCK, key_base[:, None] // BLOCK
    query_kind, key_kind = query_noisy[None, :], key_noisy[:, None]
    mask = (
        (query_kind & key_kind & (query_block == key_block))
        | (query_kind & ~key_kind & (key_block < query_block))
        | (~query_kind & ~key_kind & (key_block <= query_block))
    )
    mask = mask & (docs_of(query_base)[None, :] == docs_of(key_base)[:, None])
    mask = mask & (key_base >= 0)[:, None]
    bias = jnp.where(mask, 0.0, -1e30).astype(jnp.bfloat16)
    frequency = 10000.0 ** (-jnp.arange(HDIM // 2).astype(jnp.float32) * 2.0 / HDIM)
    angles = query_base.astype(jnp.float32)[:, None] * frequency[None, :]
    cosine, sine_table = jnp.cos(angles), jnp.sin(angles)
    turn_cos = jnp.tile(cosine, (1, 4))
    turn_sin = jnp.tile(jnp.concatenate([-sine_table, sine_table], axis=1), (1, 2))

    flat = (micros * rows, width_pos, width)
    forward = run_forward(
        layer_input.reshape(flat), cotangent.reshape(flat), own_a, own_b, own_c, bias, turn_cos, turn_sin
    )
    full_a, full_b, gains, seeded, tokens, low_both, *kept = forward
    tables = (turn_cos, turn_sin)
    layer_out, input_grads, final_a, final_b, small = run_backward(
        full_a, full_b, seeded, tokens, low_both, kept, gains, bias, tables
    )
    input_grad = jnp.where(s == 0, *input_grads)
    small = lax.dynamic_index_in_dim(small, s, 0, keepdims=False)
    final_a, final_b = final_a.astype(jnp.float32), final_b.astype(jnp.float32)
    grad_qkv = jnp.stack([final_a[0, 0].T, final_a[0, 1].T, final_a[1, 0].T], axis=1)
    out_shape = (1,) + layer_input.shape
    return (
        layer_out.reshape(out_shape),
        input_grad.reshape(out_shape),
        small[0:1],
        grad_qkv[None],
        final_a[1, 1][None],
        small[1:2],
        final_b[0][None],
        small[4:5],
        final_b[1].T[None],
        small[2:3],
    )


def solution(mesh):
    sizes = tuple(mesh.shape[name] for name in ("section", "tp", "seq"))
    local = spread if sizes == (2, 4, 4) else pipelined
    return jax.shard_map(
        local,
        mesh=mesh,
        in_specs=(
            P(None, None, "seq", None),
            P(None, None, "seq", None),
            P(),
            P("section", None),
            P("section", None, None, "tp"),
            P("section", "tp", None),
            P("section", None),
            P("section", None, "tp"),
            P("section", "tp"),
            P("section", "tp", None),
            P("section", None),
        ),
        out_specs=(
            P("section", None, None, "seq", None),
            P("section", None, None, "seq", None),
            P("section", None),
            P("section", None, None, "tp"),
            P("section", "tp", None),
            P("section", None),
            P("section", None, "tp"),
            P("section", "tp"),
            P("section", "tp", None),
            P("section", None),
        ),
        check_vma=False,
    )
```

```python
import jax
import jax.numpy as jnp
from jax import lax
from jax.experimental import pallas as pl
from jax.experimental.pallas import tpu as pltpu
from jax.sharding import PartitionSpec as P

HDIM = 64
BLOCK = 16
HALF = 1024


def from_behind(value, axis, by):
    size = lax.axis_size(axis)
    pairs = [(i, i + by) for i in range(size) if 0 <= i + by < size]
    return lax.ppermute(value, axis, pairs)


def layer_norm(values, gain):
    center = values - jnp.mean(values, axis=-1, keepdims=True)
    spread = jnp.mean(center * center, axis=-1, keepdims=True)
    return center * lax.rsqrt(spread + 1e-05) * gain


def rotate(values, cosine, sine_table):
    middle = values.shape[-1] // 2
    first_half = values[..., :middle]
    second_half = values[..., middle:]
    return jnp.concatenate(
        [
            first_half * cosine - second_half * sine_table,
            second_half * cosine + first_half * sine_table,
        ],
        axis=-1,
    )


def rotary_tables(positions):
    frequency = 10000.0 ** (-jnp.arange(HDIM // 2).astype(jnp.float32) * 2.0 / HDIM)
    angles = (positions % HALF).astype(jnp.float32)[:, None, None] * frequency[None, None, :]
    return (jnp.cos(angles), jnp.sin(angles))


def allowed(query_pos, query_doc, key_pos, key_doc):
    query_noisy = query_pos < HALF
    key_noisy = key_pos < HALF
    query_block = query_pos % HALF // BLOCK
    key_block = key_pos % HALF // BLOCK
    within = query_noisy & key_noisy & (query_block == key_block)
    earlier = query_noisy & ~key_noisy & (key_block < query_block)
    causal = ~query_noisy & ~key_noisy & (key_block <= query_block)
    return (within | earlier | causal) & (query_doc == key_doc)


def document_ids(doc_lengths):
    doc_ends = jnp.cumsum(doc_lengths, axis=-1)
    base_pos = jnp.arange(2 * HALF) % HALF
    return jnp.sum((base_pos[:, None] >= doc_ends[..., None, :]).astype(jnp.int32), axis=-1)


def gelu_tanh(values):
    return jax.nn.gelu(values, approximate=True)


def keep_slot(storage, value, slot_index, is_active):
    current = lax.dynamic_index_in_dim(storage, slot_index, 0, keepdims=False)
    return lax.dynamic_update_index_in_dim(
        storage, jnp.where(is_active, value, current), slot_index, 0
    )


def local_queries(inputs, ln_one, w_mix, tables):
    cosine, sine_table, query_pos = tables
    row_count, pos_count = (inputs.shape[0], inputs.shape[1])
    normed = layer_norm(inputs, ln_one).astype(jnp.bfloat16)
    mixed = jnp.einsum("rpd,dcf->rpcf", normed, w_mix, preferred_element_type=jnp.float32)
    shaped = mixed.reshape(row_count, pos_count, 3, -1, HDIM)
    queries = rotate(shaped[:, :, 0], cosine, sine_table).astype(jnp.bfloat16)
    keys_own = rotate(shaped[:, :, 1], cosine, sine_table).astype(jnp.bfloat16)
    values_own = shaped[:, :, 2].astype(jnp.bfloat16)
    return (normed, queries, keys_own, values_own)


def masked_scores(queries, keys_heads, query_pos, docs_all):
    pos_count = queries.shape[1]
    query_docs = lax.dynamic_slice_in_dim(docs_all, query_pos[0], pos_count, 1)
    key_pos = jnp.arange(keys_heads.shape[1])
    key_mask = allowed(
        query_pos[None, :, None],
        query_docs[:, :, None],
        key_pos[None, None, :],
        docs_all[:, None, :],
    )
    scores = (
        jnp.einsum("rqhd,rkhd->rhqk", queries, keys_heads, preferred_element_type=jnp.float32)
        * 0.125
    )
    return jnp.where(key_mask[:, None], scores, -1e30)


def forward_step(inputs, weights, tables, docs_all):
    ln_one, w_mix, w_proj, ln_two, w_first, b_first, w_second, b_second = weights
    row_count, pos_count = (inputs.shape[0], inputs.shape[1])
    normed, queries, keys_own, values_own = local_queries(inputs, ln_one, w_mix, tables)
    local_width = w_mix.shape[-1]
    keys_all, values_all = (
        lax.all_gather(
            keys_own.reshape(row_count, pos_count, local_width), "seq", axis=1, tiled=True
        ),
        lax.all_gather(
            values_own.reshape(row_count, pos_count, local_width), "seq", axis=1, tiled=True
        ),
    )
    keys_heads = keys_all.reshape(row_count, keys_all.shape[1], -1, HDIM)
    values_heads = values_all.reshape(row_count, values_all.shape[1], -1, HDIM)
    softmax_out = jax.nn.softmax(
        masked_scores(queries, keys_heads, tables[2], docs_all), axis=-1
    ).astype(jnp.bfloat16)
    attended = jnp.einsum(
        "rhqk,rkhd->rqhd", softmax_out, values_heads, preferred_element_type=jnp.float32
    )
    attended = attended.astype(jnp.bfloat16).reshape(row_count, pos_count, local_width)
    middle = inputs + lax.psum(
        jnp.einsum("rpe,ed->rpd", attended, w_proj, preferred_element_type=jnp.float32).astype(
            jnp.bfloat16
        ),
        "tp",
    ).astype(jnp.float32)
    normed_two = layer_norm(middle, ln_two).astype(jnp.bfloat16)
    hidden_pre = (
        jnp.einsum("rpd,df->rpf", normed_two, w_first, preferred_element_type=jnp.float32) + b_first
    )
    activated = gelu_tanh(hidden_pre).astype(jnp.bfloat16)
    second_terms = jnp.einsum(
        "rpf,fd->rpd", activated, w_second, preferred_element_type=jnp.float32
    )
    result = (
        middle + lax.psum(second_terms.astype(jnp.bfloat16), "tp").astype(jnp.float32) + b_second
    )
    return (result, middle, keys_all, values_all)


def backward_step(inputs, middle, grad_out, weights, tables, docs_all):
    ln_one, w_mix, w_proj, ln_two, w_first, b_first, w_second, b_second = weights
    cosine, sine_table, query_pos = tables
    row_count, pos_count = (inputs.shape[0], inputs.shape[1])
    local_width = w_mix.shape[-1]
    head_count = local_width // HDIM
    normed, queries, keys_own, values_own = local_queries(inputs, ln_one, w_mix, tables)
    keys_all, values_all = (
        lax.all_gather(
            keys_own.reshape(row_count, pos_count, local_width), "seq", axis=1, tiled=True
        ),
        lax.all_gather(
            values_own.reshape(row_count, pos_count, local_width), "seq", axis=1, tiled=True
        ),
    )
    keys_heads = keys_all.reshape(row_count, keys_all.shape[1], head_count, HDIM)
    values_heads = values_all.reshape(row_count, values_all.shape[1], head_count, HDIM)
    scores = masked_scores(queries, keys_heads, query_pos, docs_all)
    softmax_out = jax.nn.softmax(scores, axis=-1)
    probs_low = softmax_out.astype(jnp.bfloat16)
    attended = jnp.einsum(
        "rhqk,rkhd->rqhd", probs_low, values_heads, preferred_element_type=jnp.float32
    )
    attended = attended.astype(jnp.bfloat16).reshape(row_count, pos_count, local_width)
    normed_two = layer_norm(middle, ln_two).astype(jnp.bfloat16)
    hidden_pre = (
        jnp.einsum("rpd,df->rpf", normed_two, w_first, preferred_element_type=jnp.float32) + b_first
    )
    activated = gelu_tanh(hidden_pre).astype(jnp.bfloat16)
    grad_low = grad_out.astype(jnp.bfloat16)
    grad_b_second = jnp.sum(grad_out, axis=(0, 1))
    grad_w_second = jnp.einsum(
        "rpf,rpd->fd", activated, grad_low, preferred_element_type=jnp.float32
    )
    grad_act = jnp.einsum("rpd,fd->rpf", grad_low, w_second, preferred_element_type=jnp.float32)
    unused_value, gelu_back = jax.vjp(gelu_tanh, hidden_pre)
    grad_pre = gelu_back(grad_act)[0].astype(jnp.bfloat16)
    grad_b_first = jnp.sum(grad_pre, axis=(0, 1), dtype=jnp.float32)
    grad_w_first = jnp.einsum(
        "rpd,rpf->df", normed_two, grad_pre, preferred_element_type=jnp.float32
    )
    grad_normed_two = lax.psum(
        jnp.einsum("rpf,df->rpd", grad_pre, w_first, preferred_element_type=jnp.float32).astype(
            jnp.bfloat16
        ),
        "tp",
    ).astype(jnp.float32)
    unused_norm, second_back = jax.vjp(layer_norm, middle, ln_two)
    grad_middle_norm, grad_ln_two = second_back(grad_normed_two)
    grad_middle = grad_out + grad_middle_norm
    middle_low = grad_middle.astype(jnp.bfloat16)
    grad_w_proj = jnp.einsum(
        "rpe,rpd->ed", attended, middle_low, preferred_element_type=jnp.float32
    )
    grad_att = jnp.einsum("rpd,ed->rpe", middle_low, w_proj, preferred_element_type=jnp.float32)
    grad_att = grad_att.astype(jnp.bfloat16).reshape(row_count, pos_count, head_count, HDIM)
    grad_probs = jnp.einsum(
        "rqhd,rkhd->rhqk", grad_att, values_heads, preferred_element_type=jnp.float32
    )
    row_delta = jnp.sum(grad_probs * softmax_out, axis=-1, keepdims=True)
    grad_scores = (softmax_out * (grad_probs - row_delta)).astype(jnp.bfloat16)
    grad_queries = (
        jnp.einsum("rhqk,rkhd->rqhd", grad_scores, keys_heads, preferred_element_type=jnp.float32)
        * 0.125
    )
    full_len = keys_all.shape[1]
    part_keys = (
        jnp.einsum("rhqk,rqhd->rkhd", grad_scores, queries, preferred_element_type=jnp.float32)
        * 0.125
    )
    part_values = jnp.einsum(
        "rhqk,rqhd->rkhd", probs_low, grad_att, preferred_element_type=jnp.float32
    )
    grad_keys, grad_values = (
        lax.psum_scatter(
            part_keys.reshape(row_count, full_len, local_width).astype(jnp.bfloat16),
            "seq",
            scatter_dimension=1,
            tiled=True,
        ).astype(jnp.float32),
        lax.psum_scatter(
            part_values.reshape(row_count, full_len, local_width).astype(jnp.bfloat16),
            "seq",
            scatter_dimension=1,
            tiled=True,
        ).astype(jnp.float32),
    )
    grad_query_raw = rotate(grad_queries.astype(jnp.bfloat16), cosine, -sine_table)
    grad_key_raw = rotate(
        grad_keys.astype(jnp.bfloat16).reshape(row_count, pos_count, head_count, HDIM),
        cosine,
        -sine_table,
    )
    grad_mixed = jnp.stack(
        [
            grad_query_raw.reshape(row_count, pos_count, local_width).astype(jnp.bfloat16),
            grad_key_raw.reshape(row_count, pos_count, local_width).astype(jnp.bfloat16),
            grad_values.astype(jnp.bfloat16),
        ],
        axis=2,
    )
    grad_w_mix = jnp.einsum("rpd,rpcf->dcf", normed, grad_mixed, preferred_element_type=jnp.float32)
    grad_normed = lax.psum(
        jnp.einsum("rpcf,dcf->rpd", grad_mixed, w_mix, preferred_element_type=jnp.float32).astype(
            jnp.bfloat16
        ),
        "tp",
    ).astype(jnp.float32)
    unused_first, first_back = jax.vjp(layer_norm, inputs, ln_one)
    grad_in_norm, grad_ln_one = first_back(grad_normed)
    grad_inputs = grad_middle + grad_in_norm
    return (
        grad_inputs,
        (
            grad_ln_one,
            grad_w_mix,
            grad_w_proj,
            grad_ln_two,
            grad_w_first,
            grad_b_first,
            grad_w_second,
            grad_b_second,
        ),
    )


def pipelined(
    layer_input,
    cotangent,
    doc_lengths,
    ln1_gain,
    w_qkv,
    w_out,
    ln2_gain,
    w_up,
    b_up,
    w_down,
    b_down,
):
    weights = tuple(
        (weight[0] for weight in (ln1_gain, w_qkv, w_out, ln2_gain, w_up, b_up, w_down, b_down))
    )
    micros, row_count, pos_count, width_model = layer_input.shape
    sections = lax.axis_size("section")
    section_index = lax.axis_index("section")
    first_pos = lax.axis_index("seq") * pos_count
    query_pos = first_pos + jnp.arange(pos_count)
    cosine, sine_table = rotary_tables(query_pos)
    tables = (cosine, sine_table, query_pos)
    docs_every = document_ids(doc_lengths)
    kept_inputs = jnp.zeros((micros, row_count, pos_count, width_model), jnp.float32)
    kept_middle = jnp.zeros((micros, row_count, pos_count, width_model), jnp.float32)
    layer_out = jnp.zeros(layer_input.shape, jnp.bfloat16)
    arrived = jnp.zeros((row_count, pos_count, width_model), jnp.bfloat16)
    moments = micros + sections - 1
    for moment in range(moments):
        offset = moment - section_index
        micro_index = jnp.clip(offset, 0, micros - 1)
        is_active = (offset >= 0) & (offset < micros)
        own_input = layer_input[min(moment, micros - 1)]
        inputs = jnp.where(section_index == 0, own_input, arrived).astype(jnp.float32)
        result, middle, keys_all, values_all = forward_step(
            inputs, weights, tables, docs_every[micro_index]
        )
        kept_inputs = keep_slot(kept_inputs, inputs, micro_index, is_active)
        kept_middle = keep_slot(kept_middle, middle, micro_index, is_active)
        result_low = result.astype(jnp.bfloat16)
        layer_out = keep_slot(layer_out, result_low, micro_index, is_active)
        if moment < moments - 1:
            arrived = from_behind(result_low, "section", 1)
    grad_totals = tuple((jnp.zeros(weight.shape, jnp.float32) for weight in weights))
    input_grad = jnp.zeros(layer_input.shape, jnp.bfloat16)
    returned = jnp.zeros((row_count, pos_count, width_model), jnp.bfloat16)
    for moment in range(moments):
        offset = moment - (sections - 1 - section_index)
        micro_index = jnp.clip(offset, 0, micros - 1)
        is_active = (offset >= 0) & (offset < micros)
        incoming = jnp.where(
            section_index == sections - 1, cotangent[min(moment, micros - 1)], returned
        ).astype(jnp.float32)
        incoming = jnp.where(is_active, incoming, 0.0)
        grad_inputs, grad_parts = backward_step(
            kept_inputs[micro_index],
            kept_middle[micro_index],
            incoming,
            weights,
            tables,
            docs_every[micro_index],
        )
        grad_totals = tuple((total + piece for total, piece in zip(grad_totals, grad_parts)))
        grad_sent = grad_inputs.astype(jnp.bfloat16)
        input_grad = keep_slot(input_grad, grad_sent, micro_index, is_active)
        if moment < moments - 1:
            returned = from_behind(grad_sent, "section", -1)
    (
        grad_ln_one,
        grad_w_mix,
        grad_w_proj,
        grad_ln_two,
        grad_w_first,
        grad_b_first,
        grad_w_second,
        grad_b_second,
    ) = grad_totals
    summed = (
        lax.psum(grad_ln_one.astype(jnp.bfloat16), "seq").astype(jnp.float32),
        lax.psum(grad_w_mix.astype(jnp.bfloat16), "seq").astype(jnp.float32),
        lax.psum(grad_w_proj.astype(jnp.bfloat16), "seq").astype(jnp.float32),
        lax.psum(grad_ln_two.astype(jnp.bfloat16), "seq").astype(jnp.float32),
        lax.psum(grad_w_first.astype(jnp.bfloat16), "seq").astype(jnp.float32),
        lax.psum(grad_b_first.astype(jnp.bfloat16), "seq").astype(jnp.float32),
        lax.psum(grad_w_second.astype(jnp.bfloat16), "seq").astype(jnp.float32),
        lax.psum(grad_b_second.astype(jnp.bfloat16), "seq").astype(jnp.float32),
    )
    return (
        layer_out[None],
        input_grad[None],
        summed[0][None],
        summed[1][None],
        summed[2][None],
        summed[3][None],
        summed[4][None],
        summed[5][None],
        summed[6][None],
        summed[7][None],
    )


PIECE = 256
LANES = 256
MESH = pl.DeviceIdType.MESH
HBM = pl.BlockSpec(memory_space=pl.ANY)
VMEM = pl.BlockSpec(memory_space=pltpu.VMEM)


def dot_nn(left, right):
    return lax.dot_general(left, right, (((1,), (0,)), ((), ())), preferred_element_type=jnp.float32)


def dot_nt(left, right):
    return lax.dot_general(left, right, (((1,), (1,)), ((), ())), preferred_element_type=jnp.float32)


def dot_tn(left, right):
    return lax.dot_general(left, right, (((0,), (0,)), ((), ())), preferred_element_type=jnp.float32)


class Place:
    def __init__(self):
        self.s, self.t, self.z = (lax.axis_index(name) for name in ("section", "tp", "seq"))
        self.core = 1 - self.s
        self.half, self.group = self.z % 2, self.z // 2
        beside_x = self.t + 1 - 2 * (self.t % 2)
        beside_y = (self.t + 2) % 4
        self.beside_x, self.beside_y = beside_x, beside_y
        self.hop_one = beside_x * (1 - self.s) + beside_y * self.s
        self.hop_two = beside_y * (1 - self.s) + beside_x * self.s
        self.rel_one, self.rel_two = 1 + self.s, 2 - self.s
        self.far = (self.z + 2) % 4
        self.twin = self.z + 1 - 2 * self.half

    def on(self, section=None, tp=None, seq=None):
        return (
            self.s if section is None else section,
            self.t if tp is None else tp,
            self.z if seq is None else seq,
        )

    def partners(self):
        return [
            self.on(section=self.core),
            self.on(tp=self.beside_x),
            self.on(tp=self.beside_y),
            self.on(seq=self.far),
            self.on(seq=self.twin),
            self.on(seq=3 - self.z),
            self.on(section=self.core, seq=self.twin),
        ]

    def meet(self, partners):
        barrier = pltpu.get_barrier_semaphore()
        for partner in partners:
            pl.semaphore_signal(barrier, inc=1, device_id=partner, device_id_type=MESH)
        pl.semaphore_wait(barrier, len(partners))


def remote(source, target, send, receive, device):
    return pltpu.make_async_remote_copy(
        src_ref=source,
        dst_ref=target,
        send_sem=send,
        recv_sem=receive,
        device_id=device,
        device_id_type=MESH,
    )


def normalize(values):
    center = values - jnp.mean(values, axis=-1, keepdims=True)
    spread = jnp.mean(center * center, axis=-1, keepdims=True)
    scale = lax.rsqrt(spread + 1e-05)
    return center * scale, scale


def turn(values, cosine, sine_table):
    width = values.shape[-1]
    times = width // cosine.shape[-1]
    lane = lax.broadcasted_iota(jnp.int32, values.shape, 1) % HDIM
    ahead = pltpu.roll(values, width - HDIM // 2, 1)
    behind = pltpu.roll(values, HDIM // 2, 1)
    swapped = jnp.where(lane < HDIM // 2, ahead, behind)
    return values * jnp.tile(cosine, (1, times)) + swapped * jnp.tile(sine_table, (1, times))


def gelu(values):
    inner = 0.7978845608028654 * (values + 0.044715 * values * values * values)
    return 0.5 * values * (1.0 + jnp.tanh(inner))


def head_mask(head, scale):
    lane = lax.broadcasted_iota(jnp.int32, (1, LANES), 1)
    inside = (lane >= head * HDIM) & (lane < (head + 1) * HDIM)
    return jnp.where(inside, jnp.float32(scale), jnp.float32(0.0))


def attention_block(q_ref, keys, values_turned, bias, lse, turned):
    def one(head, _):
        rows = pl.ds(pl.multiple_of(head * HDIM, HDIM), HDIM)
        query = q_ref[...] * head_mask(head, 0.125).astype(jnp.bfloat16)
        scores = dot_nt(keys[...], query) + bias[...]
        top = jnp.max(scores, axis=0, keepdims=True)
        raised = jnp.exp(scores - top)
        total = jnp.sum(raised, axis=0, keepdims=True)
        lse[pl.ds(head, 1), :] = top + jnp.log(total)
        turned[rows, :] = dot_nn(values_turned[rows, :], raised.astype(jnp.bfloat16)) * (1.0 / total)
        return 0

    lax.fori_loop(0, LANES // HDIM, one, 0)
    return turned[...].T.astype(jnp.bfloat16)


def fill_bias(bias, lengths, row, block):
    ends, total = [], 0
    for i in range(lengths.shape[1]):
        total = total + lengths[row, i]
        ends.append(total)

    def docs_of(base):
        return sum((base >= end).astype(jnp.int32) for end in ends)

    shape = (PIECE, bias.shape[1])
    lane = lax.broadcasted_iota(jnp.int32, shape, 1)
    query_noisy = lane < PIECE
    query_base = block * PIECE + lane - jnp.where(query_noisy, 0, PIECE)
    query_doc, query_block = docs_of(query_base), query_base >> 4
    for i in range(4):
        start = (block - 2 + min(i, 2)) * PIECE
        key_base = start + lax.broadcasted_iota(jnp.int32, shape, 0)
        key_block = key_base >> 4
        if i == 3:
            allow = query_noisy & (key_block == query_block)
        else:
            later = jnp.where(query_noisy, key_block + 1, key_block)
            allow = (later <= query_block) & (key_base >= 0)
        allow = allow & (docs_of(key_base) == query_doc)
        bias[i * PIECE : (i + 1) * PIECE, :] = jnp.where(allow, 0.0, -1e30)


class Weights:
    def __init__(self, place, own, full, sems):
        self.place, self.own, self.full = place, own, full
        (
            self.local,
            self.own_send,
            self.own_recv,
            self.hop_send,
            self.hop_recv,
            self.chip_send,
            self.chip_recv,
        ) = sems

    def source(self, chunk, pack):
        if chunk == 0:
            return self.own[0].at[pack]
        if chunk == 3:
            return self.own[2].at[pack]
        return self.own[1].at[pack, chunk - 1]

    def piece(self, layer, chunk, pack, rel):
        if chunk == 0:
            return self.full[0].at[layer, pack, :, pl.ds(pl.multiple_of(rel * 192, 64), 192)]
        if chunk == 3:
            return self.full[2].at[layer, pack, rel]
        return self.full[1].at[layer, pack, rel * 2 + chunk - 1]

    def own_copies(self, chunk, pack):
        s = self.place.s
        here = pltpu.make_async_copy(
            self.source(chunk, pack), self.piece(s, chunk, pack, 0), self.local.at[chunk, pack]
        )
        there = remote(
            self.source(chunk, pack),
            self.piece(s, chunk, pack, 0),
            self.own_send.at[chunk, pack],
            self.own_recv.at[chunk, pack],
            self.place.on(section=self.place.core),
        )
        return here, there

    def start_own(self, chunk):
        for pack in (self.place.core, self.place.s):
            for copy in self.own_copies(chunk, pack)[::-1]:
                copy.start()

    def wait_own(self, layer, chunk, pack):
        here, there = self.own_copies(chunk, pack)

        @pl.when(self.place.s == layer)
        def _():
            here.wait()

        @pl.when(self.place.s != layer)
        def _():
            there.wait_recv()

    def hops(self, layer, chunk):
        place = self.place
        own = self.piece(layer, chunk, place.s, 0)
        first = self.piece(layer, chunk, place.s, place.rel_one)
        second = self.piece(layer, chunk, place.s, place.rel_two)
        third = self.piece(layer, chunk, place.s, 3)
        moves = ((own, first, place.hop_one), (own, second, place.hop_two), (first, third, place.hop_two))
        return [
            remote(
                source,
                target,
                self.hop_send.at[layer, chunk, i],
                self.hop_recv.at[layer, chunk, i],
                place.on(tp=column),
            )
            for i, (source, target, column) in enumerate(moves)
        ]

    def chips(self, layer, chunk):
        place = self.place
        return [
            remote(
                self.piece(layer, chunk, place.s, rel),
                self.piece(layer, chunk, place.s, rel),
                self.chip_send.at[layer, chunk, i],
                self.chip_recv.at[layer, chunk, i],
                place.on(section=place.core),
            )
            for i, rel in enumerate((place.rel_one, place.rel_two, 3))
        ]

    def begin(self, layer, chunk):
        self.wait_own(layer, chunk, self.place.s)
        first, second, _ = self.hops(layer, chunk)
        first.start()
        second.start()

    def forward(self, layer, chunk):
        first, second, third = self.hops(layer, chunk)
        chips = self.chips(layer, chunk)
        first.wait_recv()
        third.start()
        chips[0].start()
        second.wait_recv()
        chips[1].start()

    def finish(self, layer, chunk):
        self.hops(layer, chunk)[2].wait_recv()
        self.chips(layer, chunk)[2].start()

    def need(self, layer, chunk):
        if chunk < 3:
            self.wait_own(layer, chunk, self.place.core)
        for copy in self.chips(layer, chunk):
            copy.wait_recv()

    def drain(self):
        for chunk in range(4):
            for pack in range(2):
                self.own_copies(chunk, pack)[1].wait_send()
            for layer in range(2):
                for copy in self.hops(layer, chunk) + self.chips(layer, chunk):
                    copy.wait_send()


class KeyShare:
    def __init__(self, place, kv, layer, sems):
        self.place, self.kv, self.layer = place, kv, layer
        self.near_send, self.near_recv, self.far_send, self.far_recv = sems
        s, odd = place.s, place.half == 1
        self.sends_near = (s == 0) | ~odd
        self.sends_far = (s == 0) & ~odd
        self.passes = (s == 0) & odd
        self.gets_near = (s == 1) | odd
        self.gets_far = odd

    def rows(self, start, part):
        lanes = pl.ds(part * LANES, LANES)
        return self.kv.at[self.layer, :, pl.ds(start, PIECE), lanes]

    def near(self, part):
        place = self.place
        return remote(
            self.rows(2 * PIECE, part),
            self.rows(PIECE, part),
            self.near_send.at[self.layer, part],
            self.near_recv.at[self.layer, part],
            place.on(section=place.core, seq=place.z + place.s * (1 - place.half)),
        )

    def far(self, part):
        place = self.place
        return remote(
            self.rows(2 * PIECE, part),
            self.rows(0, part),
            self.far_send.at[self.layer, part],
            self.far_recv.at[self.layer, part],
            place.on(seq=place.twin),
        )

    def last(self, part):
        place = self.place
        return remote(
            self.rows(PIECE, part),
            self.rows(0, part),
            self.far_send.at[self.layer, part],
            self.far_recv.at[self.layer, part],
            place.on(section=place.core),
        )

    def start(self, part):
        @pl.when(self.sends_near)
        def _():
            self.near(part).start()

        @pl.when(self.sends_far)
        def _():
            self.far(part).start()

    def arrive(self, part):
        @pl.when(self.gets_near)
        def _():
            self.near(part).wait_recv()

        @pl.when(self.passes)
        def _():
            self.last(part).start()

        @pl.when(self.gets_far)
        def _():
            self.far(part).wait_recv()

    def drain(self):
        for part in range(3):

            @pl.when(self.sends_near)
            def _():
                self.near(part).wait_send()

            @pl.when(self.sends_far)
            def _():
                self.far(part).wait_send()

            @pl.when(self.passes)
            def _():
                self.last(part).wait_send()


def forward_kernel(
    tokens,
    cotangent,
    own_a,
    own_b,
    own_c,
    lengths,
    cosine,
    sine_table,
    full_a_out,
    full_b_out,
    gains_out,
    seeded_out,
    x_out,
    low_out,
    q_out,
    kv_out,
    att_out,
    mid_out,
    hid_out,
    lse_out,
    bias_out,
    full_a,
    full_b,
    full_c,
    low,
    x,
    normed,
    q,
    kv,
    att,
    mid,
    hid,
    lse,
    values_turned,
    turned_att,
    bias,
    *sems,
):
    weight_sems, key_sems = sems[:7], sems[7:11]
    token_sem, swap_send, swap_recv, seed_sem, seed_send, seed_recv, save_sem = sems[11:]
    place = Place()
    weights = Weights(place, (own_a, own_b, own_c), (full_a, full_b, full_c), weight_sems)
    lse[...] = jnp.zeros_like(lse)
    kv[:, :, : 2 * PIECE, :] = jnp.zeros((2, 2, 2 * PIECE, kv.shape[-1]), jnp.bfloat16)
    place.meet(place.partners())
    group_rows = pl.ds(pl.multiple_of(place.group * PIECE, PIECE), PIECE)
    columns = pl.ds(pl.multiple_of(place.s * PIECE, PIECE), PIECE)

    def bring(whole, target, here, send, receive):
        kept = whole.at[4 * place.group + place.t, columns]
        sent = whole.at[4 * (1 - place.group) + place.t, columns]
        target = target.at[group_rows]
        return (
            pltpu.make_async_copy(kept, target, here),
            remote(sent, target, send, receive, place.on(seq=place.far)),
        )

    own_tokens, swap = bring(tokens, low, token_sem, swap_send, swap_recv)
    own_seed, seed_swap = bring(cotangent, seeded_out, seed_sem, seed_send, seed_recv)
    own_tokens.start()
    swap.start()
    weights.start_own(0)
    weights.begin(0, 0)
    weights.start_own(3)
    weights.start_own(1)
    for layer in range(2):
        weights.begin(layer, 3)
        weights.wait_own(layer, 3, place.core)
    gains = full_c.at[:, 0, 0]
    gains_out[...] = full_c[:, 0, 0]
    fill_bias(bias, lengths, 4 * place.group + place.t, 2 * place.half + place.s)
    bias_save = pltpu.make_async_copy(bias, bias_out, save_sem.at[17])
    bias_save.start()
    weights.forward(0, 0)
    own_tokens.wait()
    swap.wait()
    x_save = pltpu.make_async_copy(low, x_out, save_sem.at[16])
    x_save.start()
    x[...] = low[...].astype(jnp.float32)

    def saves(layer):
        pairs = [
            (low, low_out.at[layer]),
            (q, q_out.at[layer]),
            (kv.at[layer], kv_out.at[layer]),
            (att, att_out.at[layer]),
            (mid, mid_out.at[layer]),
            (hid, hid_out.at[layer]),
            (lse, lse_out.at[layer]),
        ]
        return [pltpu.make_async_copy(a, b, save_sem.at[i]) for i, (a, b) in enumerate(pairs)]

    def weight_saves(layer):
        copies = []
        for i, (a, b) in enumerate(((full_a, full_a_out), (full_b, full_b_out))):
            for pack in range(2):
                sem = save_sem.at[8 + 4 * layer + 2 * i + pack]
                copies.append(pltpu.make_async_copy(a.at[layer, pack], b.at[layer, pack], sem))
        return copies

    for layer in range(2):
        share = KeyShare(place, kv, layer, key_sems)
        unit, _ = normalize(x[...])
        normed[...] = (unit * gains[layer, 0:1]).astype(jnp.bfloat16)
        if layer == 0:
            weights.finish(0, 0)
            weights.begin(0, 1)
            weights.start_own(2)
        else:
            weights.finish(1, 0)
            weights.begin(1, 2)
            for copy in saves(0)[1:]:
                copy.wait()
        weights.need(layer, 0)
        for copy in weight_saves(layer)[:2]:
            copy.start()
        for part in range(3):
            lanes = pl.ds(part * LANES, LANES)
            keep = normed[...]
            mixed = dot_nt(keep, full_a[layer, 0, 0, lanes, :])
            q[:, lanes] = turn(mixed, cosine[...], sine_table[...]).astype(jnp.bfloat16)
            mixed = dot_nt(keep, full_a[layer, 0, 1, lanes, :])
            mixed = turn(mixed, cosine[...], sine_table[...]).astype(jnp.bfloat16)
            kv[layer, 0, 2 * PIECE : 3 * PIECE, lanes] = mixed[PIECE:]
            kv[layer, 0, 3 * PIECE :, lanes] = mixed[:PIECE]
            mixed = dot_nt(keep, full_a[layer, 1, 0, lanes, :]).astype(jnp.bfloat16)
            kv[layer, 1, 2 * PIECE : 3 * PIECE, lanes] = mixed[PIECE:]
            kv[layer, 1, 3 * PIECE :, lanes] = mixed[:PIECE]
            share.start(part)
        if layer == 0:
            weights.forward(0, 3)
            weights.forward(1, 3)
            weights.finish(0, 3)
            weights.finish(1, 3)
            own_seed.start()
            weights.begin(0, 2)
        else:
            weights.forward(1, 1)
        for part in range(3):
            lanes = pl.ds(part * LANES, LANES)
            share.arrive(part)
            values_turned[...] = kv[layer, 1, :, lanes].astype(jnp.float32).T.astype(jnp.bfloat16)
            for start, count in ((0, 4 * PIECE), (PIECE, 3 * PIECE)):
                queries = pl.ds(start, PIECE)
                att[queries, lanes] = attention_block(
                    q.at[queries, lanes],
                    kv.at[layer, 0, :count, lanes],
                    values_turned.at[:, :count],
                    bias.at[:count, queries],
                    lse.at[pl.ds(8 * part, 8), queries],
                    turned_att,
                )
            if part == 2 and layer == 0:
                seed_swap.start()
            if layer == 0:
                if part == 0:
                    weights.forward(0, 1)
                elif part == 1:
                    weights.finish(0, 1)
                    weights.begin(1, 0)
                else:
                    weights.forward(0, 2)
            else:
                if part == 1:
                    weights.finish(1, 1)
                elif part == 2:
                    weights.forward(1, 2)
        for copy in saves(layer)[1:4] + saves(layer)[6:]:
            copy.start()

        def project(part, _):
            lanes = pl.ds(pl.multiple_of(part * LANES, LANES), LANES)
            mid[:, lanes] = x[:, lanes] + dot_nn(att[...], full_a[layer, 1, 1, :, lanes])
            return 0

        lax.fori_loop(0, 3, project, 0)
        unit, _ = normalize(mid[...])
        normed[...] = (unit * gains[layer, 1:2]).astype(jnp.bfloat16)
        x[...] = mid[...] + gains[layer, 2:3]
        saves(layer)[4].start()
        weights.need(layer, 3)
        for part in range(2):
            if part == 1:
                weights.finish(layer, 2)
                if layer == 0:
                    weights.begin(1, 1)
            weights.need(layer, part + 1)
            if part == 1:
                for copy in weight_saves(layer)[2:]:
                    copy.start()

            def feed(rel, _):
                start = pl.multiple_of(rel * 768 + part * 384, 128)
                units = pl.ds(start, 384)
                shift = full_c[layer, 1, rel, 0:1, pl.ds(part * 384, 384)]
                tile = rel * 2 + part
                pre = dot_nn(normed[...], full_b[layer, 0, tile]) + shift
                hid[:, units] = pre.astype(jnp.bfloat16)
                active = gelu(pre).astype(jnp.bfloat16)
                x[...] += dot_nt(active, full_b[layer, 1, tile])
                return 0

            lax.fori_loop(0, 4, feed, 0)
        saves(layer)[5].start()
        if layer == 0:
            x_save.wait()
        else:
            saves(0)[0].wait()
        low[...] = x[...].astype(jnp.bfloat16)
        saves(layer)[0].start()
        x[...] = low[...].astype(jnp.float32)
        if layer == 0:
            weights.forward(1, 0)
    for copy in saves(1):
        copy.wait()
    for layer in range(2):
        for copy in weight_saves(layer):
            copy.wait()
        KeyShare(place, kv, layer, key_sems).drain()
    weights.drain()
    bias_save.wait()
    own_seed.wait()
    seed_swap.wait()


def run_forward(tokens, cotangent, own_a, own_b, own_c, lengths, cosine, sine_table):
    shape = jax.ShapeDtypeStruct
    low_type, full_type = jnp.bfloat16, jnp.float32
    count = 2 * PIECE
    width = tokens.shape[-1]
    units = 8 * own_b.shape[-1]
    dma = pltpu.SemaphoreType.DMA
    return pl.pallas_call(
        forward_kernel,
        name="forward_layers",
        out_shape=[
            shape((2, 2, 2, width, width), low_type),
            shape((2, 2, 8, width, units // 8), low_type),
            shape((2, 8, width), full_type),
            shape((count, width), low_type),
            shape((count, width), low_type),
            shape((2, count, width), low_type),
            shape((2, count, width), low_type),
            shape((2, 2, 4 * PIECE, width), low_type),
            shape((2, count, width), low_type),
            shape((2, count, width), full_type),
            shape((2, count, units), low_type),
            shape((2, 24, count), full_type),
            shape((4 * PIECE, count), full_type),
        ],
        in_specs=[HBM] * 5 + [pl.BlockSpec(memory_space=pltpu.SMEM)] + [VMEM] * 2,
        out_specs=[HBM] * 2 + [VMEM] + [HBM] * 10,
        scratch_shapes=[
            pltpu.VMEM((2, 2, 2, width, width), low_type),
            pltpu.VMEM((2, 2, 8, width, units // 8), low_type),
            pltpu.VMEM((2, 2, 4, 8, width), full_type),
            pltpu.VMEM((count, width), low_type),
            pltpu.VMEM((count, width), full_type),
            pltpu.VMEM((count, width), low_type),
            pltpu.VMEM((count, width), low_type),
            pltpu.VMEM((2, 2, 4 * PIECE, width), low_type),
            pltpu.VMEM((count, width), low_type),
            pltpu.VMEM((count, width), full_type),
            pltpu.VMEM((count, units), low_type),
            pltpu.VMEM((24, count), full_type),
            pltpu.VMEM((LANES, 4 * PIECE), low_type),
            pltpu.VMEM((LANES, PIECE), full_type),
            pltpu.VMEM((4 * PIECE, count), full_type),
            dma((4, 2)),
            dma((4, 2)),
            dma((4, 2)),
            dma((2, 4, 3)),
            dma((2, 4, 3)),
            dma((2, 4, 3)),
            dma((2, 4, 3)),
            dma((2, 3)),
            dma((2, 3)),
            dma((2, 3)),
            dma((2, 3)),
            dma,
            dma,
            dma,
            dma,
            dma,
            dma,
            dma((18,)),
        ],
        compiler_params=pltpu.CompilerParams(
            collective_id=1, has_side_effects=True, vmem_limit_bytes=62 * 1024 * 1024
        ),
        cost_estimate=pl.CostEstimate(
            flops=30_000_000_000, bytes_accessed=80_000_000, transcendentals=20_000_000
        ),
    )(tokens, cotangent, own_a, own_b, own_c, lengths, cosine, sine_table)


def low_sum(*parts):
    total = parts[0].astype(jnp.float32)
    for part in parts[1:]:
        total = total + part.astype(jnp.float32)
    return total.astype(jnp.bfloat16)


class Spread:
    def __init__(self, place, source, stage, layer, out, sems):
        self.place, self.source, self.stage = place, source, stage
        self.layer, self.out = layer, out
        self.local, self.swap_send, self.swap_recv, self.hop_send, self.hop_recv = sems[:5]
        self.end_local, self.end_send, self.end_recv = sems[5:]
        self.groups = (place.group, 1 - place.group)

    def entry(self):
        place = self.place
        kept = self.source.at[pl.ds(pl.multiple_of(place.group * PIECE, PIECE), PIECE)]
        sent = self.source.at[pl.ds(pl.multiple_of((1 - place.group) * PIECE, PIECE), PIECE)]
        target = self.stage.at[0, place.group]
        here = pltpu.make_async_copy(kept, target, self.local)
        there = remote(sent, target, self.swap_send, self.swap_recv, place.on(seq=place.far))
        return here, there

    def take(self):
        self.entry()[0].start()

    def swap(self):
        self.entry()[1].start()

    def moves(self, half):
        place, group = self.place, self.groups[half]
        own = self.stage.at[0, group]
        first = self.stage.at[place.rel_one, group]
        second = self.stage.at[place.rel_two, group]
        third = self.stage.at[3, group]
        listed = (
            (own, first, place.hop_one),
            (own, second, place.hop_two),
            (first, third, place.hop_two),
        )
        return [
            remote(
                source,
                target,
                self.hop_send.at[half, i],
                self.hop_recv.at[half, i],
                place.on(tp=column),
            )
            for i, (source, target, column) in enumerate(listed)
        ]

    def hops(self, half):
        here, there = self.entry()
        if half == 0:
            here.wait()
        else:
            there.wait_recv()
        first, second, _ = self.moves(half)
        first.start()
        second.start()
        self.put(half, 0)

    def forward(self, half):
        first, _, third = self.moves(half)
        first.wait_recv()
        third.start()
        self.put(half, 1)

    def finish(self, half):
        _, second, third = self.moves(half)
        second.wait_recv()
        self.put(half, 2)
        third.wait_recv()
        self.put(half, 3)

    def ends(self, half, step):
        place, group = self.place, self.groups[half]
        rows = pl.ds(pl.multiple_of(place.s * PIECE, PIECE), PIECE)
        rel = (0, place.rel_one, place.rel_two, 3)[step]
        column = (place.t, place.hop_one, place.hop_two, 3 - place.t)[step]
        source, target = self.stage.at[rel, group], self.out.at[group, column, rows]
        here = pltpu.make_async_copy(source, target, self.end_local.at[half, step])
        there = remote(
            source,
            target,
            self.end_send.at[half, step],
            self.end_recv.at[half, step],
            place.on(section=place.core),
        )
        return here, there

    def put(self, half, step):
        @pl.when(self.place.s == self.layer)
        def _():
            self.ends(half, step)[0].start()

        @pl.when(self.place.s != self.layer)
        def _():
            self.ends(half, step)[1].start()

    def drain(self):
        self.entry()[1].wait_send()
        for half in range(2):
            for copy in self.moves(half):
                copy.wait_send()

        @pl.when(self.place.s == self.layer)
        def _():
            for half in range(2):
                for step in range(4):
                    here, there = self.ends(half, step)
                    here.wait()
                    there.wait_recv()

        @pl.when(self.place.s != self.layer)
        def _():
            for half in range(2):
                for step in range(4):
                    self.ends(half, step)[1].wait_send()


def spread_sems():
    dma = pltpu.SemaphoreType.DMA
    return [dma, dma, dma, dma((2, 3)), dma((2, 3)), dma((2, 4)), dma((2, 4)), dma((2, 4))]


class Sum:
    def __init__(self, place, source, total, buffers, sems, loaded=False, opens=None, waits=None):
        self.place, self.source, self.total = place, source, total
        self.inbox, self.hop_in, self.line_in = buffers
        self.loaded, self.opens, self.waits = loaded, opens, waits
        (
            self.mine_sem,
            self.chip_send,
            self.chip_recv,
            self.hop_send,
            self.hop_recv,
            self.line_send,
            self.line_recv,
            self.end_local,
            self.end_send,
            self.end_recv,
        ) = sems
        z = place.z
        self.outer = (z == 0) | (z == 3)
        self.inner = (z == 1) | (z == 2)
        self.order = (3, 1, 2, 0)

    def mine(self, rel):
        return pltpu.make_async_copy(
            self.source(self.place.s, rel), self.total(rel), self.mine_sem.at[rel]
        )

    def other(self, rel):
        return remote(
            self.source(self.place.core, rel),
            self.inbox.at[rel],
            self.chip_send.at[rel],
            self.chip_recv.at[rel],
            self.place.on(section=self.place.core),
        )

    def start(self):
        if self.waits is not None:
            pl.semaphore_wait(self.waits, 1)
        for rel in self.order:
            if self.inbox is not None:
                self.other(rel).start()
            if self.loaded:
                self.mine(rel).start()

    def load(self, travels=True):
        for rel in self.order:
            if self.loaded:
                self.mine(rel).wait()
            if self.inbox is not None:
                self.other(rel).wait_recv()
                total = self.total(rel)
                total[...] = low_sum(total[...], self.inbox[rel])
            if travels and rel == 3:
                self.moves()[0].start()
            elif travels and rel == 2:
                self.moves()[1].start()
        if self.opens is not None:
            pl.semaphore_signal(
                self.opens,
                inc=1,
                device_id=self.place.on(section=self.place.core),
                device_id_type=MESH,
            )

    def moves(self):
        place = self.place
        listed = (
            (3, 0, place.hop_two),
            (place.rel_two, 1, place.hop_two),
            (place.rel_one, 2, place.hop_one),
        )
        return [
            remote(
                self.total(rel),
                self.hop_in.at[slot],
                self.hop_send.at[slot],
                self.hop_recv.at[slot],
                place.on(tp=column),
            )
            for rel, slot, column in listed
        ]

    def middle(self):
        first, _, third = self.moves()
        first.wait_recv()
        total = self.total(self.place.rel_one)
        total[...] = low_sum(total[...], self.hop_in[0])
        third.start()

    def lines(self):
        place = self.place
        own, line_sum = self.total(0), self.total(1)
        listed = (
            (own, self.line_in.at[0], place.twin),
            (own, self.line_in.at[1], 3 - place.z),
            (line_sum, line_sum, place.twin),
        )
        return [
            remote(
                source,
                target,
                self.line_send.at[i],
                self.line_recv.at[i],
                place.on(seq=plane),
            )
            for i, (source, target, plane) in enumerate(listed)
        ]

    def gather(self, save=None):
        _, second, third = self.moves()
        second.wait_recv()
        third.wait_recv()
        total = self.total(0)
        total[...] = low_sum(total[...], self.hop_in[1], self.hop_in[2])
        second.wait_send()
        third.wait_send()
        if save is not None:
            save.start()
        else:
            self.enter_line()

    def resume(self, saved):
        saved.wait()
        self.enter_line()

    def enter_line(self):
        @pl.when(self.outer)
        def _():
            self.lines()[0].start()

    def line_one(self):
        @pl.when(self.inner)
        def _():
            self.lines()[0].wait_recv()
            total = self.total(0)
            total[...] = low_sum(total[...], self.line_in[0])
            self.lines()[1].start()

    def line_two(self):
        @pl.when(self.inner)
        def _():
            self.lines()[1].wait_recv()
            self.total(1)[...] = low_sum(self.total(0)[...], self.line_in[1])
            self.lines()[2].start()

    def line_three(self):
        @pl.when(self.outer)
        def _():
            self.lines()[2].wait_recv()

    def ends(self, target):
        here = pltpu.make_async_copy(self.total(1), target, self.end_local)
        there = remote(
            self.total(1),
            target,
            self.end_send,
            self.end_recv,
            self.place.on(section=self.place.core),
        )
        return here, there

    def store(self, save):
        self.line_three()
        save.start()

    def finish(self, layer, target):
        self.line_three()
        here, there = self.ends(target)

        @pl.when(self.place.s == layer)
        def _():
            here.start()

        @pl.when(self.place.s != layer)
        def _():
            there.start()

    def drain_exchange(self):
        if self.inbox is not None:
            for rel in range(4):
                self.other(rel).wait_send()

    def drain_end(self, layer, target):
        here, there = self.ends(target)

        @pl.when(self.place.s == layer)
        def _():
            here.wait()
            there.wait_recv()

        @pl.when(self.place.s != layer)
        def _():
            there.wait_send()

    def drain_plane(self):
        self.drain_exchange()
        self.moves()[0].wait_send()

    def drain_line(self):
        @pl.when(self.outer)
        def _():
            self.lines()[0].wait_send()

        @pl.when(self.inner)
        def _():
            self.lines()[1].wait_send()
            self.lines()[2].wait_send()


def sum_sems():
    dma = pltpu.SemaphoreType.DMA
    return [dma((4,))] * 3 + [dma((3,))] * 4 + [dma] * 3


SUM_SEMS = 10


def sum_buffers(piece, counts):
    return [pltpu.VMEM((count,) + piece, jnp.bfloat16) for count in counts]


def attention_sums(place, grads, buffers, sems):
    sums = []
    for i in range(2):
        total, inbox, hop_in, line_in = buffers[4 * i : 4 * i + 4]

        def source(pack, rel, i=i):
            return grads.at[pack, i, rel]

        def kept(rel, total=total):
            return total.at[rel]

        own_sems = sems[SUM_SEMS * i : SUM_SEMS * (i + 1)]
        sums.append(Sum(place, source, kept, (inbox, hop_in, line_in), own_sems, loaded=True))
    return sums


def feed_sums(place, wb, buffers, sems, gate):
    inbox, sums = buffers[0], []
    for i in range(2):

        def source(pack, rel, i=i):
            return wb.at[pack, rel * 2 + i]

        def kept(rel, i=i):
            return wb.at[place.s, rel * 2 + i]

        own_sems = sems[SUM_SEMS * i : SUM_SEMS * (i + 1)]
        gates = {"opens": gate} if i == 0 else {"waits": gate}
        at = min(i, buffers[1].shape[0] - 1)
        sums.append(Sum(place, source, kept, (inbox, buffers[1].at[at], None), own_sems, **gates))
    return sums


def feed_buffers(piece, count):
    kind = jnp.bfloat16
    return [pltpu.VMEM((4,) + piece, kind), pltpu.VMEM((count, 3) + piece, kind)]


def line_sum(place, total, line_in, sems):
    return Sum(place, None, lambda rel: total.at[rel], (None, None, line_in), sems)


class KeyReturn:
    def __init__(self, place, kv, near_in, far_in, sems):
        self.place, self.kv = place, kv
        self.near_in, self.far_in, self.pass_in = near_in, far_in, far_in
        (
            self.near_send,
            self.near_recv,
            self.far_send,
            self.far_recv,
            self.pass_send,
            self.pass_recv,
        ) = sems
        s, odd = place.s, place.half == 1
        self.is_third = (s == 0) & odd
        self.is_fourth = (s == 1) & odd
        self.is_second = (s == 1) & ~odd
        self.is_first = (s == 0) & ~odd

    def sources(self, start, part):
        return self.kv.at[:, pl.ds(start, PIECE), pl.ds(part * LANES, LANES)]

    def copies(self, part):
        place = self.place
        lanes = pl.ds(part * LANES, LANES)
        near = remote(
            self.sources(PIECE, part),
            self.near_in.at[:, :, lanes],
            self.near_send.at[part],
            self.near_recv.at[part],
            place.on(section=place.core, seq=place.z - (1 - place.s) * place.half),
        )
        far = remote(
            self.sources(0, part),
            self.far_in.at[:, :, lanes],
            self.far_send.at[part],
            self.far_recv.at[part],
            place.on(seq=place.twin),
        )
        passed = remote(
            self.sources(0, part),
            self.pass_in.at[:, :, lanes],
            self.pass_send.at[part],
            self.pass_recv.at[part],
            place.on(section=place.core),
        )
        return near, far, passed

    def start(self, part):
        near, far, passed = self.copies(part)

        @pl.when(self.is_fourth)
        def _():
            passed.start()
            near.start()

        @pl.when(self.is_second)
        def _():
            near.start()

        @pl.when(self.is_third)
        def _():
            far.start()

    def relay(self, part):
        near, _, passed = self.copies(part)
        lanes = pl.ds(part * LANES, LANES)

        @pl.when(self.is_third)
        def _():
            passed.wait_recv()
            self.kv[:, PIECE : 2 * PIECE, lanes] = low_sum(
                self.kv[:, PIECE : 2 * PIECE, lanes], self.pass_in[:, :, lanes]
            )
            near.start()

    def collect(self, part):
        near, far, _ = self.copies(part)
        lanes = pl.ds(part * LANES, LANES)
        clean = pl.ds(2 * PIECE, PIECE)

        @pl.when(~self.is_fourth)
        def _():
            near.wait_recv()
            self.kv[:, clean, lanes] = low_sum(self.kv[:, clean, lanes], self.near_in[:, :, lanes])

        @pl.when(self.is_first)
        def _():
            far.wait_recv()
            self.kv[:, clean, lanes] = low_sum(self.kv[:, clean, lanes], self.far_in[:, :, lanes])

    def drain(self):
        for part in range(3):
            near, far, passed = self.copies(part)

            @pl.when(self.is_fourth)
            def _():
                passed.wait_send()
                near.wait_send()

            @pl.when(self.is_second)
            def _():
                near.wait_send()

            @pl.when(self.is_third)
            def _():
                far.wait_send()
                near.wait_send()


def normalize_back(grads, unit, scale, gain):
    lifted = grads * gain
    mean = jnp.mean(lifted, axis=-1, keepdims=True)
    along = jnp.mean(lifted * unit, axis=-1, keepdims=True)
    return scale * (lifted - mean - unit * along)


def attention_back(q_ref, grad_ref, att_ref, keys, values, keys_turned, bias, lse, sums, turned, count):
    turned[...] = (grad_ref[...].astype(jnp.float32) * att_ref[...].astype(jnp.float32)).T

    def head_terms(head):
        rows = pl.ds(pl.multiple_of(head * HDIM, HDIM), HDIM)
        query = q_ref[...] * head_mask(head, 0.125).astype(jnp.bfloat16)
        grad = grad_ref[...] * head_mask(head, 1.0).astype(jnp.bfloat16)
        delta = jnp.sum(turned[rows, :], axis=0, keepdims=True)
        scores = dot_nt(keys[...], query) + bias[...]
        probs = jnp.exp(scores - lse[pl.ds(head, 1), :])
        grad_scores = (probs * (dot_nt(values[...], grad) - delta)).astype(jnp.bfloat16)
        turned[rows, :] = dot_nn(keys_turned[rows, :], grad_scores) * 0.125
        return query, grad, grad_scores, probs.astype(jnp.bfloat16)

    def one(pair, _):
        left, right = head_terms(2 * pair), head_terms(2 * pair + 1)
        query, grad = (jnp.concatenate([left[i], right[i]], axis=0) for i in (0, 1))
        grad_scores, probs = (jnp.concatenate([left[i], right[i]], axis=1) for i in (2, 3))
        sums[0, :count] += dot_nn(grad_scores, query)
        sums[1, :count] += dot_nn(probs, grad)
        return 0

    lax.fori_loop(0, LANES // HDIM // 2, one, 0)
    q_ref[...] = turned[...].T.astype(jnp.bfloat16)


def backward_layer(layer, refs, place, tick, key_sems, sems, tile_sems):
    (
        full_a,
        full_b,
        grad_in,
        x_in,
        q_in,
        kv_in,
        att_in,
        mid_in,
        hid_in,
        lse_in,
        bias_in,
        gains,
        cosine,
        sine_table,
        grads_a,
        grad_out,
        small_out,
        wa,
        wb,
        low,
        q,
        kv,
        att,
        mid,
        hid,
        grad,
        gathered,
        grad_low,
        grad_att,
        near_in,
        far_in,
        sums,
        keys_turned,
        turned_q,
        grad_turned,
        normed_turned,
        lse,
        bias,
    ) = refs
    share = KeyReturn(place, kv, near_in, far_in, key_sems)
    pairs = [
        (grad_in, grad_low),
        (mid_in.at[layer], mid),
        (hid_in.at[layer], hid),
        (full_a.at[layer], wa),
        (att_in.at[layer], att),
        (q_in.at[layer], q),
        (kv_in.at[layer], kv),
        (x_in, low),
        (lse_in.at[layer], lse),
        (bias_in, bias),
    ]
    loads = [pltpu.make_async_copy(a, b, sems.at[i]) for i, (a, b) in enumerate(pairs)]
    def tile_copy(pack, tile):
        return pltpu.make_async_copy(
            full_b.at[layer, pack, tile], wb.at[pack, tile], tile_sems.at[pack, tile]
        )

    for copy in loads[:3]:
        copy.start()
    for part in range(2):
        for rel in range(4):
            for pack in (1, 0):
                tile_copy(pack, rel * 2 + part).start()
    for copy in loads[3:]:
        copy.start()
    tick()
    gain_one, gain_two = gains[layer, 0:1], gains[layer, 1:2]
    for copy in loads[:3]:
        copy.wait()
    small_out[...] = jnp.zeros_like(small_out)

    def by_rows(step):
        def one(i, _):
            step(pl.ds(pl.multiple_of(i * 128, 128), 128))
            return 0

        lax.fori_loop(0, grad.shape[0] // 128, one, 0)

    def enter(rows):
        incoming = grad_low[rows, :].astype(jnp.float32)
        grad[rows, :] = incoming
        small_out[2:3] += jnp.sum(incoming, axis=0, keepdims=True)
        grad_turned[:, rows] = incoming.T.astype(jnp.bfloat16)
        unit, _ = normalize(mid[rows, :])
        normed_turned[:, rows] = (unit * gain_two).T.astype(jnp.bfloat16)
        gathered[rows, :] = jnp.zeros((128, grad.shape[1]), jnp.float32)

    by_rows(enter)
    tick()

    def feed(part, rel):
        start = pl.multiple_of(rel * 768 + part * 384, 128)
        units = pl.ds(start, 384)
        tile = rel * 2 + part
        pre = hid[:, units].astype(jnp.float32)
        squared = pre * pre
        bent = jnp.tanh(0.7978845608028654 * pre * (1.0 + 0.044715 * squared))
        raised = 0.5 * (1.0 + bent)
        active = (pre * raised).astype(jnp.bfloat16)
        slope = raised + 0.5 * pre * (1.0 - bent * bent) * (
            0.7978845608028654 * (1.0 + 3 * 0.044715 * squared)
        )
        tile_copy(1, tile).wait()
        grad_act = dot_nn(grad_low[...], wb[1, tile])
        grad_pre = (grad_act * slope).astype(jnp.bfloat16)
        total = jnp.sum(grad_pre.astype(jnp.float32), axis=0, keepdims=True)
        small_out[pl.ds(4 + rel, 1), pl.ds(part * 384, 384)] = total
        wb[1, tile] = dot_nn(grad_turned[...], active).astype(jnp.bfloat16)
        tile_copy(0, tile).wait()
        gathered[...] += dot_nt(grad_pre, wb[0, tile])
        wb[0, tile] = dot_nn(normed_turned[...], grad_pre).astype(jnp.bfloat16)

    for part in range(2):
        for pair in range(2):

            def one(i, _):
                feed(part, 2 * pair + i)
                return 0

            lax.fori_loop(0, 2, one, 0)
            tick()

    def between(rows):
        found = gathered[rows, :]
        unit, scale = normalize(mid[rows, :])
        small_out[1:2] += jnp.sum(found * unit, axis=0, keepdims=True)
        total = grad[rows, :] + normalize_back(found, unit, scale, gain_two)
        grad[rows, :] = total
        grad_low[rows, :] = total.astype(jnp.bfloat16)

    by_rows(between)
    for copy in loads[3:]:
        copy.wait()

    def project(part, _):
        lanes = pl.ds(pl.multiple_of(part * LANES, LANES), LANES)
        grad_att[:, lanes] = dot_nt(grad_low[...], wa[1, 1, lanes, :]).astype(jnp.bfloat16)
        wa[1, 1, lanes, :] = dot_tn(att[:, lanes], grad_low[...]).astype(jnp.bfloat16)
        return 0

    lax.fori_loop(0, 3, project, 0)
    tick()
    for part in range(3):
        lanes = pl.ds(part * LANES, LANES)
        sums[...] = jnp.zeros_like(sums)
        keys_turned[...] = kv[0, :, lanes].astype(jnp.float32).T.astype(jnp.bfloat16)
        for start, count in ((0, 4 * PIECE), (PIECE, 3 * PIECE)):
            rows = pl.ds(start, PIECE)
            attention_back(
                q.at[rows, lanes],
                grad_att.at[rows, lanes],
                att.at[rows, lanes],
                kv.at[0, :count, lanes],
                kv.at[1, :count, lanes],
                keys_turned.at[:, :count],
                bias.at[:count, rows],
                lse.at[pl.ds(8 * part, 8), rows],
                sums,
                turned_q,
                count,
            )
            if start == 0:
                tick()
        kv[:, :, lanes] = sums[...].astype(jnp.bfloat16)
        share.start(part)
        if part > 0:
            share.relay(part - 1)
        tick()
    normed = grad_att

    def again(rows):
        unit, _ = normalize(low[rows, :].astype(jnp.float32))
        normed[rows, :] = (unit * gain_one).astype(jnp.bfloat16)

    by_rows(again)

    def turned(part, _):
        lanes = pl.ds(pl.multiple_of(part * LANES, LANES), LANES)
        raw = turn(q[:, lanes].astype(jnp.float32), cosine[...], -sine_table[...])
        raw = raw.astype(jnp.bfloat16)
        found = dot_nn(raw, wa[0, 0, lanes, :])

        @pl.when(part == 0)
        def _():
            gathered[...] = found

        @pl.when(part > 0)
        def _():
            gathered[...] += found

        wa[0, 0, lanes, :] = dot_tn(raw, normed[...]).astype(jnp.bfloat16)
        return 0

    lax.fori_loop(0, 3, turned, 0)
    share.relay(2)
    tick()
    for part in range(3):
        share.collect(part)

    def keyed(part, _):
        lanes = pl.ds(pl.multiple_of(part * LANES, LANES), LANES)
        noisy, clean = pl.ds(3 * PIECE, PIECE), pl.ds(2 * PIECE, PIECE)
        raw = jnp.concatenate([kv[0, noisy, lanes], kv[0, clean, lanes]], axis=0)
        raw = turn(raw.astype(jnp.float32), cosine[...], -sine_table[...]).astype(jnp.bfloat16)
        gathered[...] += dot_nn(raw, wa[0, 1, lanes, :])
        wa[0, 1, lanes, :] = dot_tn(raw, normed[...]).astype(jnp.bfloat16)
        raw = jnp.concatenate([kv[1, noisy, lanes], kv[1, clean, lanes]], axis=0)
        gathered[...] += dot_nn(raw, wa[1, 0, lanes, :])
        wa[1, 0, lanes, :] = dot_tn(raw, normed[...]).astype(jnp.bfloat16)
        return 0

    lax.fori_loop(0, 3, keyed, 0)
    tick()
    save_a = pltpu.make_async_copy(wa, grads_a, sems.at[10])
    save_a.start()

    def leave(rows):
        found = gathered[rows, :]
        unit, scale = normalize(low[rows, :].astype(jnp.float32))
        small_out[0:1] += jnp.sum(found * unit, axis=0, keepdims=True)
        total = grad[rows, :] + normalize_back(found, unit, scale, gain_one)
        grad_low[rows, :] = total.astype(jnp.bfloat16)

    by_rows(leave)
    save_grad = pltpu.make_async_copy(grad_low, grad_out, sems.at[11])
    save_grad.start()
    tick()
    share.drain()
    save_a.wait()
    save_grad.wait()


class Ticks:
    def __init__(self, groups):
        self.groups = list(groups)

    def __call__(self):
        if self.groups:
            for step in self.groups.pop(0):
                step()

    def rest(self):
        while self.groups:
            self()


def backward_buffers(width, units):
    low, full, count = jnp.bfloat16, jnp.float32, 2 * PIECE
    return [
        pltpu.VMEM((2, 2, width, width), low),
        pltpu.VMEM((2, 8, width, units // 8), low),
        pltpu.VMEM((count, width), low),
        pltpu.VMEM((count, width), low),
        pltpu.VMEM((2, 4 * PIECE, width), low),
        pltpu.VMEM((count, width), low),
        pltpu.VMEM((count, width), full),
        pltpu.VMEM((count, units), low),
        pltpu.VMEM((count, width), full),
        pltpu.VMEM((count, width), full),
        pltpu.VMEM((count, width), low),
        pltpu.VMEM((count, width), low),
        pltpu.VMEM((2, PIECE, width), low),
        pltpu.VMEM((2, PIECE, width), low),
        pltpu.VMEM((2, 4 * PIECE, LANES), full),
        pltpu.VMEM((LANES, 4 * PIECE), low),
        pltpu.VMEM((LANES, PIECE), full),
        pltpu.VMEM((width, count), low),
        pltpu.VMEM((width, count), low),
        pltpu.VMEM((24, count), full),
        pltpu.VMEM((4 * PIECE, count), full),
    ]


def backward_sems():
    dma = pltpu.SemaphoreType.DMA
    return [dma((3,))] * 6 + [dma((12,)), dma((2, 8))]


BUFFERS = 21


def later(step, *args):
    return lambda: step(*args)


def second_kernel(*refs):
    ins, refs = refs[:15], refs[15:]
    (grads_a, grad_out, small_out, out, carry_one, carry), refs = refs[:6], refs[6:]
    buffers, stages, feed, refs = refs[:BUFFERS], refs[BUFFERS : BUFFERS + 2], refs[23:25], refs[25:]
    sems, feed_sem, gate, carry_sem = refs[:24], refs[24:-2], refs[-2], refs[-1]
    low_both = ins[14]
    place = Place()
    place.meet(place.partners())
    zero, last = [
        Spread(place, low_both.at[i], stages[i], i, out, sems[8 + 8 * i : 16 + 8 * i])
        for i in range(2)
    ]
    one, two = feed_sums(place, buffers[1], feed, feed_sem, gate)
    carries = [
        pltpu.make_async_copy(two.total(rel), carry.at[rel], carry_sem.at[rel]) for rel in range(4)
    ]
    save_one = pltpu.make_async_copy(one.total(0), carry_one, carry_sem.at[4])

    def hand_on():
        two.load(travels=False)
        for copy in carries:
            copy.start()

    tick = Ticks(
        [
            [zero.take, last.take, zero.swap, later(zero.hops, 0), later(last.hops, 0)],
            [],
            [later(zero.forward, 0)],
            [one.start, last.swap],
            [later(zero.hops, 1), later(last.forward, 0)],
            [later(zero.finish, 0)],
            [one.load],
            [later(zero.forward, 1), two.start],
            [later(last.finish, 0)],
            [one.middle],
            [later(last.hops, 1), later(zero.finish, 1)],
            [],
            [hand_on],
            [later(one.gather, save_one), later(last.forward, 1)],
            [],
            [later(last.finish, 1)],
        ]
    )
    body = ins[:3] + (low_both.at[0],) + ins[4:14] + (grads_a, grad_out, small_out) + buffers
    backward_layer(1, body, place, tick, sems[:6], sems[6], sems[7])
    tick.rest()
    zero.drain()
    last.drain()
    one.drain_plane()
    save_one.wait()
    two.drain_exchange()
    for copy in carries:
        copy.wait()


def first_kernel(*refs):
    ins, refs = refs[:17], refs[17:]
    (grads_a, grad_out, small_out, out, done, carry_out), refs = refs[:6], refs[6:]
    buffers, stage, refs = refs[:BUFFERS], refs[BUFFERS], refs[BUFFERS + 1 :]
    feed, (total, hop_in, line_in, line_total, line_in_one), refs = refs[:2], refs[2:7], refs[7:]
    sems, feed_sem, kept_sem, line_sem = refs[:16], refs[16:36], refs[36:46], refs[46:56]
    gate, carry_sem = refs[56:]
    carry_one, carry, prior_grad = ins[14:]
    place = Place()
    place.meet(place.partners())
    back = Spread(place, prior_grad, stage, 1, out, sems[8:16])
    one, two = feed_sums(place, buffers[1], feed, feed_sem, gate)
    kept = Sum(
        place,
        lambda pack, rel: carry.at[rel],
        lambda rel: total.at[rel],
        (None, hop_in, line_in),
        kept_sem,
        loaded=True,
    )
    line = line_sum(place, line_total, line_in_one, line_sem)
    line_load = pltpu.make_async_copy(carry_one, line_total.at[0], carry_sem.at[0])
    saves = [
        pltpu.make_async_copy(line.total(1), done.at[0], carry_sem.at[1]),
        pltpu.make_async_copy(kept.total(1), done.at[1], carry_sem.at[2]),
        pltpu.make_async_copy(one.total(0), carry_out.at[0], carry_sem.at[3]),
        pltpu.make_async_copy(two.total(0), carry_out.at[1], carry_sem.at[4]),
    ]
    tick = Ticks(
        [
            [back.take, back.swap, line_load.start, kept.start, later(back.hops, 0)],
            [later(line.resume, line_load), kept.load],
            [later(back.forward, 0)],
            [one.start, line.line_one],
            [kept.middle, later(back.hops, 1)],
            [line.line_two, later(back.finish, 0)],
            [one.load],
            [kept.gather, two.start],
            [later(back.forward, 1), later(line.store, saves[0])],
            [kept.line_one],
            [one.middle, two.load],
            [kept.line_two, later(back.finish, 1)],
            [],
            [later(one.gather, saves[2]), later(kept.store, saves[1])],
            [two.middle],
            [],
            [later(two.gather, saves[3])],
        ]
    )
    body = ins[:14] + (grads_a, grad_out, small_out) + buffers
    backward_layer(0, body, place, tick, sems[:6], sems[6], sems[7])
    tick.rest()
    back.drain()
    for item in (kept, one, two):
        item.drain_plane()
    line.drain_line()
    kept.drain_line()
    for copy in saves:
        copy.wait()


def last_kernel(*refs):
    priors, (done, carry, grad_zero, small_zero, small_one), refs = refs[:2], refs[2:7], refs[7:]
    (out, final_a, final_b, small), refs = refs[:4], refs[4:]
    held, stage, (small_in, extra), refs = refs[:16], refs[16], refs[17:19], refs[19:]
    (line_total, line_in), sems = refs[:2], refs[2:]
    held_sem, spread_sem, line_sem, sems = sems[:40], sems[40:48], sems[48:68], sems[68:]
    tiny_send, tiny_recv, carry_sem, end_local, end_send, end_recv = sems
    place = Place()
    place.meet(place.partners())
    sums = []
    for i in range(2):
        sums += attention_sums(
            place, priors[i], held[8 * i : 8 * i + 8], held_sem[20 * i : 20 * i + 20]
        )
    lines, loads = [], []
    for i in range(2):
        lines.append(line_sum(place, line_total.at[i], line_in.at[i], line_sem[10 * i : 10 * i + 10]))
        loads.append(pltpu.make_async_copy(carry.at[i], line_total.at[i, 0], carry_sem.at[i]))
    back = Spread(place, grad_zero, stage, 0, out, spread_sem)
    targets = [final_a.at[place.s, 0], final_a.at[place.s, 1]] * 2
    halves = [final_b.at[place.s, :, pl.ds(384 * i, 384)] for i in range(2)]
    layers = (1, 1, 0, 0)
    small[0], small[1] = small_zero[...], small_one[...]
    rows_beside = ((4, 5, 6, 7), (5, 4, 7, 6), (6, 7, 4, 5), (4, 5, 6, 7), (4, 5, 6, 7))
    partners = (
        place.on(section=place.core),
        place.on(tp=place.beside_x),
        place.on(tp=place.beside_y),
        place.on(seq=place.twin),
        place.on(seq=place.far),
    )

    def done_ends(i):
        here = pltpu.make_async_copy(done.at[i], halves[i], end_local.at[i])
        there = remote(
            done.at[i], halves[i], end_send.at[i], end_recv.at[i], place.on(section=place.core)
        )
        return here, there

    def done_start():
        @pl.when(place.s == 1)
        def _():
            for i in range(2):
                done_ends(i)[0].start()

        @pl.when(place.s == 0)
        def _():
            for i in range(2):
                done_ends(i)[1].start()

    def done_wait():
        @pl.when(place.s == 1)
        def _():
            for i in range(2):
                here, there = done_ends(i)
                here.wait()
                there.wait_recv()

        @pl.when(place.s == 0)
        def _():
            for i in range(2):
                done_ends(i)[1].wait_send()

    def tiny(i):
        return remote(extra.at[i], small_in.at[i], tiny_send.at[i], tiny_recv.at[i], partners[i])

    def tiny_start(i):
        extra[i] = small[...]
        tiny(i).start()

    def tiny_end(i):
        tiny(i).wait_recv()
        for layer in range(2):
            small[layer, 0:4] = extra[i, layer, 0:4] + small_in[i, layer, 0:4]
            for row, other in enumerate(rows_beside[i]):
                at = row + 4
                small[layer, at : at + 1] = (
                    extra[i, layer, at : at + 1] + small_in[i, layer, other : other + 1]
                )

    back.take()
    sums[0].start()
    back.swap()
    sums[1].start()
    for load in loads:
        load.start()
    tiny_start(0)
    back.hops(0)
    lines[0].resume(loads[0])
    sums[0].load()
    sums[2].start()
    back.forward(0)
    tiny_end(0)
    tiny_start(1)
    lines[1].resume(loads[1])
    sums[1].load()
    sums[3].start()
    sums[0].middle()
    lines[0].line_one()
    tiny_end(1)
    tiny_start(2)
    sums[2].load()
    sums[0].gather()
    back.finish(0)
    sums[1].middle()
    back.hops(1)
    sums[1].gather()
    tiny_end(2)
    tiny_start(3)
    sums[3].load()
    sums[2].middle()
    lines[1].line_one()
    done_start()
    lines[0].line_two()
    sums[2].gather()
    back.forward(1)
    sums[3].middle()
    sums[0].line_one()
    tiny_end(3)
    tiny_start(4)
    sums[3].gather()
    sums[1].line_one()
    back.finish(1)
    lines[1].line_two()
    lines[0].finish(0, halves[0])
    sums[2].line_one()
    sums[0].line_two()
    tiny_end(4)
    sums[3].line_one()
    sums[1].line_two()
    sums[0].finish(1, targets[0])
    sums[2].line_two()
    lines[1].finish(0, halves[1])
    sums[1].finish(1, targets[1])
    sums[3].line_two()
    sums[2].finish(0, targets[2])
    sums[3].finish(0, targets[3])
    for item, layer, target in zip(sums, layers, targets):
        item.drain_plane()
        item.drain_line()
        item.drain_end(layer, target)
    for item, target in zip(lines, halves):
        item.drain_line()
        item.drain_end(0, target)
    done_wait()
    back.drain()
    for i in range(5):
        tiny(i).wait_send()


def call(kernel, name, number, ins, spaces, shapes, out_spaces, scratch, flops, moved):
    return pl.pallas_call(
        kernel,
        name=name,
        out_shape=[jax.ShapeDtypeStruct(shape, kind) for shape, kind in shapes],
        in_specs=spaces,
        out_specs=out_spaces,
        scratch_shapes=scratch,
        compiler_params=pltpu.CompilerParams(
            collective_id=number, has_side_effects=True, vmem_limit_bytes=62 * 1024 * 1024
        ),
        cost_estimate=pl.CostEstimate(
            flops=flops, bytes_accessed=moved, transcendentals=20_000_000
        ),
    )(*ins)


def results_kernel(*refs):
    layer_raw, zero_raw, one_raw, final_a, final_b = refs[:5]
    layer_out, input_grad, grad_out, grad_up, grad_down = refs[5:10]
    rows, turned, part, tiles, converted, row_sem, tile_sem = refs[10:]
    s = lax.axis_index("section")
    count = rows.shape[0] // 2

    def load(i):
        sem = row_sem.at[0, i]
        if i < count:
            return [pltpu.make_async_copy(layer_raw.at[i // 4, i % 4], rows.at[i], sem)] * 2
        at = i - count
        return [
            pltpu.make_async_copy(raw.at[at // 4, at % 4], rows.at[i], sem) for raw in (zero_raw, one_raw)
        ]

    def store(i):
        target, at = (layer_out, i) if i < count else (input_grad, i - count)
        return pltpu.make_async_copy(rows.at[i], target.at[at // 4, at % 4], row_sem.at[1, i])

    loads = [
        pltpu.make_async_copy(final_b.at[0], tiles.at[0], tile_sem.at[0]),
        pltpu.make_async_copy(final_b.at[1], tiles.at[1], tile_sem.at[1]),
        pltpu.make_async_copy(final_a.at[1, 1], part, tile_sem.at[2]),
    ]
    stores = [
        pltpu.make_async_copy(converted, grad_up, tile_sem.at[3]),
        pltpu.make_async_copy(turned, grad_down, tile_sem.at[4]),
    ]
    for copy in loads:
        copy.start()
    for i in range(count):
        load(i)[0].start()

    @pl.when(s == 0)
    def _():
        for i in range(count, 2 * count):
            load(i)[0].start()

    @pl.when(s != 0)
    def _():
        for i in range(count, 2 * count):
            load(i)[1].start()

    for copy in loads:
        copy.wait()
    converted[...] = tiles[0].astype(jnp.float32)
    stores[0].start()
    grad_out[...] = part[...].astype(jnp.float32)
    turned[...] = tiles[1].astype(jnp.float32).T
    stores[1].start()
    for i in range(2 * count):
        load(i)[0].wait()
        store(i).start()
    for i in range(2 * count):
        store(i).wait()
    for copy in stores:
        copy.wait()


def run_results(layer_raw, zero_raw, one_raw, final_a, final_b):
    full = jnp.float32
    width = final_b.shape[-1]
    big = jax.ShapeDtypeStruct(layer_raw.shape, layer_raw.dtype)
    square = jax.ShapeDtypeStruct((width, width), full)
    dma = pltpu.SemaphoreType.DMA
    return pl.pallas_call(
        results_kernel,
        name="place_results",
        out_shape=[big, big, jax.ShapeDtypeStruct((192, width), full), square, square],
        in_specs=[HBM] * 5,
        out_specs=[HBM] * 2 + [VMEM] + [HBM] * 2,
        scratch_shapes=[
            pltpu.VMEM((16,) + layer_raw.shape[2:], jnp.bfloat16),
            pltpu.VMEM((width, width), full),
            pltpu.VMEM((192, width), jnp.bfloat16),
            pltpu.VMEM((2, width, width), jnp.bfloat16),
            pltpu.VMEM((width, width), full),
            dma((2, 16)),
            dma((5,)),
        ],
        compiler_params=pltpu.CompilerParams(vmem_limit_bytes=48 * 1024 * 1024),
        cost_estimate=pl.CostEstimate(flops=1_000_000, bytes_accessed=35_000_000, transcendentals=0),
    )(layer_raw, zero_raw, one_raw, final_a, final_b)


def run_backward(full_a, full_b, seeded, tokens, low_both, kept, gains, tables):
    low, full, count = jnp.bfloat16, jnp.float32, 2 * PIECE
    width, units = full_a.shape[-1], 8 * full_b.shape[-1]
    grads = [
        ((2, 2, width, width), low),
        ((count, width), low),
        ((8, width), full),
    ]
    out = ((2, 4, count, width), low)
    row_piece, tile_piece = (192, width), (width, units // 8)
    final_a, final_b = ((2, 2) + row_piece, low), ((2, width, 2 * tile_piece[1]), low)
    carry_one, carry, two_tiles = (tile_piece, low), ((4,) + tile_piece, low), ((2,) + tile_piece, low)
    stage = pltpu.VMEM((4, 2, PIECE, width), low)
    dma, gate = pltpu.SemaphoreType.DMA, pltpu.SemaphoreType.REGULAR
    common = (*kept, gains, *tables)
    common_spaces = [HBM] * 11 + [VMEM] * 3
    held = sum_buffers(row_piece, (4, 4, 3, 2) * 2)
    second = call(
        second_kernel,
        "backward_second",
        2,
        (full_a, full_b, seeded, tokens) + common + (low_both,),
        common_spaces + [HBM],
        grads + [out, carry_one, carry],
        [HBM] * 2 + [VMEM] + [HBM] * 3,
        backward_buffers(width, units)
        + [stage, stage]
        + feed_buffers(tile_piece, 1)
        + backward_sems()
        + spread_sems()
        + spread_sems()
        + sum_sems()
        + sum_sems()
        + [gate, dma((5,))],
        40_000_000_000,
        80_000_000,
    )
    prior_a, grad_one, small_one, layer_out, carried_one, carried = second
    first = call(
        first_kernel,
        "backward_first",
        3,
        (full_a, full_b, grad_one, tokens) + common + (carried_one, carried, grad_one),
        common_spaces + [HBM] * 3,
        grads + [out, two_tiles, two_tiles],
        [HBM] * 2 + [VMEM] + [HBM] * 3,
        backward_buffers(width, units)
        + [stage]
        + feed_buffers(tile_piece, 2)
        + sum_buffers(tile_piece, (4, 3, 2, 2, 2))
        + backward_sems()
        + spread_sems()
        + sum_sems()
        + sum_sems()
        + sum_sems()
        + sum_sems()
        + [gate, dma((5,))],
        40_000_000_000,
        80_000_000,
    )
    grads_a, grad_zero, small_zero, out_one, done, carried = first
    by_shard = (2, 2, 4, 192, width)
    last = call(
        last_kernel,
        "sum_and_spread",
        4,
        (prior_a.reshape(by_shard), grads_a.reshape(by_shard), done, carried, grad_zero)
        + (small_zero, small_one),
        [HBM] * 5 + [VMEM] * 2,
        [out, final_a, final_b, ((2, 8, width), full)],
        [HBM] * 3 + [VMEM],
        held
        + held
        + [stage]
        + [pltpu.VMEM((5, 2, 8, width), full), pltpu.VMEM((5, 2, 8, width), full)]
        + [pltpu.VMEM((2, 2) + tile_piece, low), pltpu.VMEM((2, 2) + tile_piece, low)]
        + sum_sems()
        + sum_sems()
        + sum_sems()
        + sum_sems()
        + spread_sems()
        + sum_sems()
        + sum_sems()
        + [dma((5,)), dma((5,))]
        + [dma((2,))] * 4,
        100_000_000,
        40_000_000,
    )
    out_zero, final_a, final_b, small = last
    return layer_out, (out_zero, out_one), final_a, final_b, small


def spread(
    layer_input,
    cotangent,
    doc_lengths,
    ln1_gain,
    w_qkv,
    w_out,
    ln2_gain,
    w_up,
    b_up,
    w_down,
    b_down,
):
    s, t, z = (lax.axis_index(name) for name in ("section", "tp", "seq"))
    micros, rows, width_pos, width = layer_input.shape
    half, group = z % 2, z // 2

    own_a = jnp.stack(
        [
            jnp.stack([w_qkv[0, :, 0].T, w_qkv[0, :, 1].T]),
            jnp.stack([w_qkv[0, :, 2].T, w_out[0]]),
        ]
    )
    shard = w_up.shape[-1]
    own_b = jnp.stack([w_up[0], w_down[0].T]).reshape(2, width, 2, shard // 2).transpose(0, 2, 1, 3)
    gains = jnp.concatenate([ln1_gain, ln2_gain, b_down, jnp.zeros((5, width), jnp.float32)])
    own_c = jnp.stack([gains, jnp.concatenate([b_up, jnp.zeros((7, width), jnp.float32)])])

    lane = jnp.arange(128)
    block_base = (2 * half + s) * PIECE
    query_base = block_base + jnp.arange(2 * PIECE) % PIECE
    frequency = 10000.0 ** (-(lane % (HDIM // 2)).astype(jnp.float32) * 2.0 / HDIM)
    angles = query_base.astype(jnp.float32)[:, None] * frequency[None, :]
    sign = jnp.where(lane % HDIM < HDIM // 2, -1.0, 1.0)
    turn_cos, turn_sin = jnp.cos(angles), jnp.sin(angles) * sign

    lengths = doc_lengths.reshape(micros * rows, -1)
    flat = (micros * rows, width_pos, width)
    forward = run_forward(
        layer_input.reshape(flat), cotangent.reshape(flat), own_a, own_b, own_c, lengths, turn_cos, turn_sin
    )
    full_a, full_b, gains, seeded, tokens, low_both, *kept = forward
    tables = (turn_cos, turn_sin)
    layer_raw, input_raws, final_a, final_b, small = run_backward(
        full_a, full_b, seeded, tokens, low_both, kept, gains, tables
    )
    layer_out, input_grad, grad_out, grad_up, grad_down = run_results(
        layer_raw, *input_raws, final_a, final_b
    )
    small = lax.dynamic_index_in_dim(small, s, 0, keepdims=False)
    final_a = final_a.astype(jnp.float32)
    grad_qkv = jnp.stack([final_a[0, 0].T, final_a[0, 1].T, final_a[1, 0].T], axis=1)
    out_shape = (1,) + layer_input.shape
    return (
        layer_out.reshape(out_shape),
        input_grad.reshape(out_shape),
        small[0:1],
        grad_qkv[None],
        grad_out[None],
        small[1:2],
        grad_up[None],
        small[4:5],
        grad_down[None],
        small[2:3],
    )


def solution(mesh):
    sizes = tuple(mesh.shape[name] for name in ("section", "tp", "seq"))
    local = spread if sizes == (2, 4, 4) else pipelined
    return jax.shard_map(
        local,
        mesh=mesh,
        in_specs=(
            P(None, None, "seq", None),
            P(None, None, "seq", None),
            P(),
            P("section", None),
            P("section", None, None, "tp"),
            P("section", "tp", None),
            P("section", None),
            P("section", None, "tp"),
            P("section", "tp"),
            P("section", "tp", None),
            P("section", None),
        ),
        out_specs=(
            P("section", None, None, "seq", None),
            P("section", None, None, "seq", None),
            P("section", None),
            P("section", None, None, "tp"),
            P("section", "tp", None),
            P("section", None),
            P("section", None, "tp"),
            P("section", "tp"),
            P("section", "tp", None),
            P("section", None),
        ),
        check_vma=False,
    )
```

```python
import jax
import jax.numpy as jnp
from jax import lax
from jax.experimental import pallas as pl
from jax.experimental.pallas import tpu as pltpu
from jax.sharding import PartitionSpec as P

HDIM = 64
BLOCK = 16
HALF = 1024


def from_behind(value, axis, by):
    size = lax.axis_size(axis)
    pairs = [(i, i + by) for i in range(size) if 0 <= i + by < size]
    return lax.ppermute(value, axis, pairs)


def layer_norm(values, gain):
    center = values - jnp.mean(values, axis=-1, keepdims=True)
    spread = jnp.mean(center * center, axis=-1, keepdims=True)
    return center * lax.rsqrt(spread + 1e-05) * gain


def rotate(values, cosine, sine_table):
    middle = values.shape[-1] // 2
    first_half = values[..., :middle]
    second_half = values[..., middle:]
    return jnp.concatenate(
        [
            first_half * cosine - second_half * sine_table,
            second_half * cosine + first_half * sine_table,
        ],
        axis=-1,
    )


def rotary_tables(positions):
    frequency = 10000.0 ** (-jnp.arange(HDIM // 2).astype(jnp.float32) * 2.0 / HDIM)
    angles = (positions % HALF).astype(jnp.float32)[:, None, None] * frequency[None, None, :]
    return (jnp.cos(angles), jnp.sin(angles))


def allowed(query_pos, query_doc, key_pos, key_doc):
    query_noisy = query_pos < HALF
    key_noisy = key_pos < HALF
    query_block = query_pos % HALF // BLOCK
    key_block = key_pos % HALF // BLOCK
    within = query_noisy & key_noisy & (query_block == key_block)
    earlier = query_noisy & ~key_noisy & (key_block < query_block)
    causal = ~query_noisy & ~key_noisy & (key_block <= query_block)
    return (within | earlier | causal) & (query_doc == key_doc)


def document_ids(doc_lengths):
    doc_ends = jnp.cumsum(doc_lengths, axis=-1)
    base_pos = jnp.arange(2 * HALF) % HALF
    return jnp.sum((base_pos[:, None] >= doc_ends[..., None, :]).astype(jnp.int32), axis=-1)


def gelu_tanh(values):
    return jax.nn.gelu(values, approximate=True)


def keep_slot(storage, value, slot_index, is_active):
    current = lax.dynamic_index_in_dim(storage, slot_index, 0, keepdims=False)
    return lax.dynamic_update_index_in_dim(
        storage, jnp.where(is_active, value, current), slot_index, 0
    )


def local_queries(inputs, ln_one, w_mix, tables):
    cosine, sine_table, query_pos = tables
    row_count, pos_count = (inputs.shape[0], inputs.shape[1])
    normed = layer_norm(inputs, ln_one).astype(jnp.bfloat16)
    mixed = jnp.einsum("rpd,dcf->rpcf", normed, w_mix, preferred_element_type=jnp.float32)
    shaped = mixed.reshape(row_count, pos_count, 3, -1, HDIM)
    queries = rotate(shaped[:, :, 0], cosine, sine_table).astype(jnp.bfloat16)
    keys_own = rotate(shaped[:, :, 1], cosine, sine_table).astype(jnp.bfloat16)
    values_own = shaped[:, :, 2].astype(jnp.bfloat16)
    return (normed, queries, keys_own, values_own)


def masked_scores(queries, keys_heads, query_pos, docs_all):
    pos_count = queries.shape[1]
    query_docs = lax.dynamic_slice_in_dim(docs_all, query_pos[0], pos_count, 1)
    key_pos = jnp.arange(keys_heads.shape[1])
    key_mask = allowed(
        query_pos[None, :, None],
        query_docs[:, :, None],
        key_pos[None, None, :],
        docs_all[:, None, :],
    )
    scores = (
        jnp.einsum("rqhd,rkhd->rhqk", queries, keys_heads, preferred_element_type=jnp.float32)
        * 0.125
    )
    return jnp.where(key_mask[:, None], scores, -1e30)


def forward_step(inputs, weights, tables, docs_all):
    ln_one, w_mix, w_proj, ln_two, w_first, b_first, w_second, b_second = weights
    row_count, pos_count = (inputs.shape[0], inputs.shape[1])
    normed, queries, keys_own, values_own = local_queries(inputs, ln_one, w_mix, tables)
    local_width = w_mix.shape[-1]
    keys_all, values_all = (
        lax.all_gather(
            keys_own.reshape(row_count, pos_count, local_width), "seq", axis=1, tiled=True
        ),
        lax.all_gather(
            values_own.reshape(row_count, pos_count, local_width), "seq", axis=1, tiled=True
        ),
    )
    keys_heads = keys_all.reshape(row_count, keys_all.shape[1], -1, HDIM)
    values_heads = values_all.reshape(row_count, values_all.shape[1], -1, HDIM)
    softmax_out = jax.nn.softmax(
        masked_scores(queries, keys_heads, tables[2], docs_all), axis=-1
    ).astype(jnp.bfloat16)
    attended = jnp.einsum(
        "rhqk,rkhd->rqhd", softmax_out, values_heads, preferred_element_type=jnp.float32
    )
    attended = attended.astype(jnp.bfloat16).reshape(row_count, pos_count, local_width)
    middle = inputs + lax.psum(
        jnp.einsum("rpe,ed->rpd", attended, w_proj, preferred_element_type=jnp.float32).astype(
            jnp.bfloat16
        ),
        "tp",
    ).astype(jnp.float32)
    normed_two = layer_norm(middle, ln_two).astype(jnp.bfloat16)
    hidden_pre = (
        jnp.einsum("rpd,df->rpf", normed_two, w_first, preferred_element_type=jnp.float32) + b_first
    )
    activated = gelu_tanh(hidden_pre).astype(jnp.bfloat16)
    second_terms = jnp.einsum(
        "rpf,fd->rpd", activated, w_second, preferred_element_type=jnp.float32
    )
    result = (
        middle + lax.psum(second_terms.astype(jnp.bfloat16), "tp").astype(jnp.float32) + b_second
    )
    return (result, middle, keys_all, values_all)


def backward_step(inputs, middle, grad_out, weights, tables, docs_all):
    ln_one, w_mix, w_proj, ln_two, w_first, b_first, w_second, b_second = weights
    cosine, sine_table, query_pos = tables
    row_count, pos_count = (inputs.shape[0], inputs.shape[1])
    local_width = w_mix.shape[-1]
    head_count = local_width // HDIM
    normed, queries, keys_own, values_own = local_queries(inputs, ln_one, w_mix, tables)
    keys_all, values_all = (
        lax.all_gather(
            keys_own.reshape(row_count, pos_count, local_width), "seq", axis=1, tiled=True
        ),
        lax.all_gather(
            values_own.reshape(row_count, pos_count, local_width), "seq", axis=1, tiled=True
        ),
    )
    keys_heads = keys_all.reshape(row_count, keys_all.shape[1], head_count, HDIM)
    values_heads = values_all.reshape(row_count, values_all.shape[1], head_count, HDIM)
    scores = masked_scores(queries, keys_heads, query_pos, docs_all)
    softmax_out = jax.nn.softmax(scores, axis=-1)
    probs_low = softmax_out.astype(jnp.bfloat16)
    attended = jnp.einsum(
        "rhqk,rkhd->rqhd", probs_low, values_heads, preferred_element_type=jnp.float32
    )
    attended = attended.astype(jnp.bfloat16).reshape(row_count, pos_count, local_width)
    normed_two = layer_norm(middle, ln_two).astype(jnp.bfloat16)
    hidden_pre = (
        jnp.einsum("rpd,df->rpf", normed_two, w_first, preferred_element_type=jnp.float32) + b_first
    )
    activated = gelu_tanh(hidden_pre).astype(jnp.bfloat16)
    grad_low = grad_out.astype(jnp.bfloat16)
    grad_b_second = jnp.sum(grad_out, axis=(0, 1))
    grad_w_second = jnp.einsum(
        "rpf,rpd->fd", activated, grad_low, preferred_element_type=jnp.float32
    )
    grad_act = jnp.einsum("rpd,fd->rpf", grad_low, w_second, preferred_element_type=jnp.float32)
    unused_value, gelu_back = jax.vjp(gelu_tanh, hidden_pre)
    grad_pre = gelu_back(grad_act)[0].astype(jnp.bfloat16)
    grad_b_first = jnp.sum(grad_pre, axis=(0, 1), dtype=jnp.float32)
    grad_w_first = jnp.einsum(
        "rpd,rpf->df", normed_two, grad_pre, preferred_element_type=jnp.float32
    )
    grad_normed_two = lax.psum(
        jnp.einsum("rpf,df->rpd", grad_pre, w_first, preferred_element_type=jnp.float32).astype(
            jnp.bfloat16
        ),
        "tp",
    ).astype(jnp.float32)
    unused_norm, second_back = jax.vjp(layer_norm, middle, ln_two)
    grad_middle_norm, grad_ln_two = second_back(grad_normed_two)
    grad_middle = grad_out + grad_middle_norm
    middle_low = grad_middle.astype(jnp.bfloat16)
    grad_w_proj = jnp.einsum(
        "rpe,rpd->ed", attended, middle_low, preferred_element_type=jnp.float32
    )
    grad_att = jnp.einsum("rpd,ed->rpe", middle_low, w_proj, preferred_element_type=jnp.float32)
    grad_att = grad_att.astype(jnp.bfloat16).reshape(row_count, pos_count, head_count, HDIM)
    grad_probs = jnp.einsum(
        "rqhd,rkhd->rhqk", grad_att, values_heads, preferred_element_type=jnp.float32
    )
    row_delta = jnp.sum(grad_probs * softmax_out, axis=-1, keepdims=True)
    grad_scores = (softmax_out * (grad_probs - row_delta)).astype(jnp.bfloat16)
    grad_queries = (
        jnp.einsum("rhqk,rkhd->rqhd", grad_scores, keys_heads, preferred_element_type=jnp.float32)
        * 0.125
    )
    full_len = keys_all.shape[1]
    part_keys = (
        jnp.einsum("rhqk,rqhd->rkhd", grad_scores, queries, preferred_element_type=jnp.float32)
        * 0.125
    )
    part_values = jnp.einsum(
        "rhqk,rqhd->rkhd", probs_low, grad_att, preferred_element_type=jnp.float32
    )
    grad_keys, grad_values = (
        lax.psum_scatter(
            part_keys.reshape(row_count, full_len, local_width).astype(jnp.bfloat16),
            "seq",
            scatter_dimension=1,
            tiled=True,
        ).astype(jnp.float32),
        lax.psum_scatter(
            part_values.reshape(row_count, full_len, local_width).astype(jnp.bfloat16),
            "seq",
            scatter_dimension=1,
            tiled=True,
        ).astype(jnp.float32),
    )
    grad_query_raw = rotate(grad_queries.astype(jnp.bfloat16), cosine, -sine_table)
    grad_key_raw = rotate(
        grad_keys.astype(jnp.bfloat16).reshape(row_count, pos_count, head_count, HDIM),
        cosine,
        -sine_table,
    )
    grad_mixed = jnp.stack(
        [
            grad_query_raw.reshape(row_count, pos_count, local_width).astype(jnp.bfloat16),
            grad_key_raw.reshape(row_count, pos_count, local_width).astype(jnp.bfloat16),
            grad_values.astype(jnp.bfloat16),
        ],
        axis=2,
    )
    grad_w_mix = jnp.einsum("rpd,rpcf->dcf", normed, grad_mixed, preferred_element_type=jnp.float32)
    grad_normed = lax.psum(
        jnp.einsum("rpcf,dcf->rpd", grad_mixed, w_mix, preferred_element_type=jnp.float32).astype(
            jnp.bfloat16
        ),
        "tp",
    ).astype(jnp.float32)
    unused_first, first_back = jax.vjp(layer_norm, inputs, ln_one)
    grad_in_norm, grad_ln_one = first_back(grad_normed)
    grad_inputs = grad_middle + grad_in_norm
    return (
        grad_inputs,
        (
            grad_ln_one,
            grad_w_mix,
            grad_w_proj,
            grad_ln_two,
            grad_w_first,
            grad_b_first,
            grad_w_second,
            grad_b_second,
        ),
    )


def pipelined(
    layer_input,
    cotangent,
    doc_lengths,
    ln1_gain,
    w_qkv,
    w_out,
    ln2_gain,
    w_up,
    b_up,
    w_down,
    b_down,
):
    weights = tuple(
        (weight[0] for weight in (ln1_gain, w_qkv, w_out, ln2_gain, w_up, b_up, w_down, b_down))
    )
    micros, row_count, pos_count, width_model = layer_input.shape
    sections = lax.axis_size("section")
    section_index = lax.axis_index("section")
    first_pos = lax.axis_index("seq") * pos_count
    query_pos = first_pos + jnp.arange(pos_count)
    cosine, sine_table = rotary_tables(query_pos)
    tables = (cosine, sine_table, query_pos)
    docs_every = document_ids(doc_lengths)
    kept_inputs = jnp.zeros((micros, row_count, pos_count, width_model), jnp.float32)
    kept_middle = jnp.zeros((micros, row_count, pos_count, width_model), jnp.float32)
    layer_out = jnp.zeros(layer_input.shape, jnp.bfloat16)
    arrived = jnp.zeros((row_count, pos_count, width_model), jnp.bfloat16)
    moments = micros + sections - 1
    for moment in range(moments):
        offset = moment - section_index
        micro_index = jnp.clip(offset, 0, micros - 1)
        is_active = (offset >= 0) & (offset < micros)
        own_input = layer_input[min(moment, micros - 1)]
        inputs = jnp.where(section_index == 0, own_input, arrived).astype(jnp.float32)
        result, middle, keys_all, values_all = forward_step(
            inputs, weights, tables, docs_every[micro_index]
        )
        kept_inputs = keep_slot(kept_inputs, inputs, micro_index, is_active)
        kept_middle = keep_slot(kept_middle, middle, micro_index, is_active)
        result_low = result.astype(jnp.bfloat16)
        layer_out = keep_slot(layer_out, result_low, micro_index, is_active)
        if moment < moments - 1:
            arrived = from_behind(result_low, "section", 1)
    grad_totals = tuple((jnp.zeros(weight.shape, jnp.float32) for weight in weights))
    input_grad = jnp.zeros(layer_input.shape, jnp.bfloat16)
    returned = jnp.zeros((row_count, pos_count, width_model), jnp.bfloat16)
    for moment in range(moments):
        offset = moment - (sections - 1 - section_index)
        micro_index = jnp.clip(offset, 0, micros - 1)
        is_active = (offset >= 0) & (offset < micros)
        incoming = jnp.where(
            section_index == sections - 1, cotangent[min(moment, micros - 1)], returned
        ).astype(jnp.float32)
        incoming = jnp.where(is_active, incoming, 0.0)
        grad_inputs, grad_parts = backward_step(
            kept_inputs[micro_index],
            kept_middle[micro_index],
            incoming,
            weights,
            tables,
            docs_every[micro_index],
        )
        grad_totals = tuple((total + piece for total, piece in zip(grad_totals, grad_parts)))
        grad_sent = grad_inputs.astype(jnp.bfloat16)
        input_grad = keep_slot(input_grad, grad_sent, micro_index, is_active)
        if moment < moments - 1:
            returned = from_behind(grad_sent, "section", -1)
    (
        grad_ln_one,
        grad_w_mix,
        grad_w_proj,
        grad_ln_two,
        grad_w_first,
        grad_b_first,
        grad_w_second,
        grad_b_second,
    ) = grad_totals
    summed = (
        lax.psum(grad_ln_one.astype(jnp.bfloat16), "seq").astype(jnp.float32),
        lax.psum(grad_w_mix.astype(jnp.bfloat16), "seq").astype(jnp.float32),
        lax.psum(grad_w_proj.astype(jnp.bfloat16), "seq").astype(jnp.float32),
        lax.psum(grad_ln_two.astype(jnp.bfloat16), "seq").astype(jnp.float32),
        lax.psum(grad_w_first.astype(jnp.bfloat16), "seq").astype(jnp.float32),
        lax.psum(grad_b_first.astype(jnp.bfloat16), "seq").astype(jnp.float32),
        lax.psum(grad_w_second.astype(jnp.bfloat16), "seq").astype(jnp.float32),
        lax.psum(grad_b_second.astype(jnp.bfloat16), "seq").astype(jnp.float32),
    )
    return (
        layer_out[None],
        input_grad[None],
        summed[0][None],
        summed[1][None],
        summed[2][None],
        summed[3][None],
        summed[4][None],
        summed[5][None],
        summed[6][None],
        summed[7][None],
    )


PIECE = 256
LANES = 256
MESH = pl.DeviceIdType.MESH
HBM = pl.BlockSpec(memory_space=pl.ANY)
VMEM = pl.BlockSpec(memory_space=pltpu.VMEM)


def dot_nn(left, right):
    return lax.dot_general(left, right, (((1,), (0,)), ((), ())), preferred_element_type=jnp.float32)


def dot_nt(left, right):
    return lax.dot_general(left, right, (((1,), (1,)), ((), ())), preferred_element_type=jnp.float32)


def dot_tn(left, right):
    return lax.dot_general(left, right, (((0,), (0,)), ((), ())), preferred_element_type=jnp.float32)


class Place:
    def __init__(self):
        self.s, self.t, self.z = (lax.axis_index(name) for name in ("section", "tp", "seq"))
        self.core = 1 - self.s
        self.half, self.group = self.z % 2, self.z // 2
        beside_x = self.t + 1 - 2 * (self.t % 2)
        beside_y = (self.t + 2) % 4
        self.beside_x, self.beside_y = beside_x, beside_y
        self.hop_one = beside_x * (1 - self.s) + beside_y * self.s
        self.hop_two = beside_y * (1 - self.s) + beside_x * self.s
        self.rel_one, self.rel_two = 1 + self.s, 2 - self.s
        self.far = (self.z + 2) % 4
        self.twin = self.z + 1 - 2 * self.half

    def on(self, section=None, tp=None, seq=None):
        return (
            self.s if section is None else section,
            self.t if tp is None else tp,
            self.z if seq is None else seq,
        )

    def partners(self):
        return [
            self.on(section=self.core),
            self.on(tp=self.beside_x),
            self.on(tp=self.beside_y),
            self.on(seq=self.far),
            self.on(seq=self.twin),
            self.on(seq=3 - self.z),
            self.on(section=self.core, seq=self.twin),
        ]

    def meet(self, partners):
        barrier = pltpu.get_barrier_semaphore()
        for partner in partners:
            pl.semaphore_signal(barrier, inc=1, device_id=partner, device_id_type=MESH)
        pl.semaphore_wait(barrier, len(partners))


def remote(source, target, send, receive, device):
    return pltpu.make_async_remote_copy(
        src_ref=source,
        dst_ref=target,
        send_sem=send,
        recv_sem=receive,
        device_id=device,
        device_id_type=MESH,
    )


def normalize(values):
    center = values - jnp.mean(values, axis=-1, keepdims=True)
    spread = jnp.mean(center * center, axis=-1, keepdims=True)
    scale = lax.rsqrt(spread + 1e-05)
    return center * scale, scale


def turn(values, cosine, sine_table):
    width = values.shape[-1]
    times = width // cosine.shape[-1]
    lane = lax.broadcasted_iota(jnp.int32, values.shape, 1) % HDIM
    ahead = pltpu.roll(values, width - HDIM // 2, 1)
    behind = pltpu.roll(values, HDIM // 2, 1)
    swapped = jnp.where(lane < HDIM // 2, ahead, behind)
    return values * jnp.tile(cosine, (1, times)) + swapped * jnp.tile(sine_table, (1, times))


def gelu(values):
    inner = 0.7978845608028654 * (values + 0.044715 * values * values * values)
    return 0.5 * values * (1.0 + jnp.tanh(inner))


def head_mask(head, scale):
    lane = lax.broadcasted_iota(jnp.int32, (1, LANES), 1)
    inside = (lane >= head * HDIM) & (lane < (head + 1) * HDIM)
    return jnp.where(inside, jnp.float32(scale), jnp.float32(0.0))


def attention_block(q_ref, keys, values_turned, bias, lse, turned):
    def one(head, _):
        rows = pl.ds(pl.multiple_of(head * HDIM, HDIM), HDIM)
        query = q_ref[...] * head_mask(head, 0.125).astype(jnp.bfloat16)
        scores = dot_nt(keys[...], query) + bias[...]
        top = jnp.max(scores, axis=0, keepdims=True)
        raised = jnp.exp(scores - top)
        total = jnp.sum(raised, axis=0, keepdims=True)
        lse[pl.ds(head, 1), :] = top + jnp.log(total)
        turned[rows, :] = dot_nn(values_turned[rows, :], raised.astype(jnp.bfloat16)) * (1.0 / total)
        return 0

    lax.fori_loop(0, LANES // HDIM, one, 0)
    return turned[...].T.astype(jnp.bfloat16)


def fill_bias(bias, lengths, row, block):
    ends, total = [], 0
    for i in range(lengths.shape[1]):
        total = total + lengths[row, i]
        ends.append(total)

    def docs_of(base):
        return sum((base >= end).astype(jnp.int32) for end in ends)

    shape = (PIECE, bias.shape[1])
    lane = lax.broadcasted_iota(jnp.int32, shape, 1)
    query_noisy = lane < PIECE
    query_base = block * PIECE + lane - jnp.where(query_noisy, 0, PIECE)
    query_doc, query_block = docs_of(query_base), query_base >> 4
    for i in range(4):
        start = (block - 2 + min(i, 2)) * PIECE
        key_base = start + lax.broadcasted_iota(jnp.int32, shape, 0)
        key_block = key_base >> 4
        if i == 3:
            allow = query_noisy & (key_block == query_block)
        else:
            later = jnp.where(query_noisy, key_block + 1, key_block)
            allow = (later <= query_block) & (key_base >= 0)
        allow = allow & (docs_of(key_base) == query_doc)
        bias[i * PIECE : (i + 1) * PIECE, :] = jnp.where(allow, 0.0, -1e30)


SHARED = ((0, 2), (1, 1))


class Weights:
    def __init__(self, place, own, full, sems):
        self.place, self.own, self.full = place, own, full
        (
            self.local,
            self.own_send,
            self.own_recv,
            self.hop_send,
            self.hop_recv,
            self.chip_send,
            self.chip_recv,
            self.twin_send,
            self.twin_recv,
            self.late_send,
            self.late_recv,
        ) = sems

    def source(self, chunk, pack):
        if chunk == 0:
            return self.own[0].at[pack]
        if chunk == 3:
            return self.own[2].at[pack]
        return self.own[1].at[pack, chunk - 1]

    def piece(self, layer, chunk, pack, rel):
        if chunk == 0:
            return self.full[0].at[layer, pack, :, pl.ds(pl.multiple_of(rel * 192, 64), 192)]
        if chunk == 3:
            return self.full[2].at[layer, pack, rel]
        return self.full[1].at[layer, pack, rel * 2 + chunk - 1]

    def own_copies(self, chunk, pack):
        s = self.place.s
        here = pltpu.make_async_copy(
            self.source(chunk, pack), self.piece(s, chunk, pack, 0), self.local.at[chunk, pack]
        )
        there = remote(
            self.source(chunk, pack),
            self.piece(s, chunk, pack, 0),
            self.own_send.at[chunk, pack],
            self.own_recv.at[chunk, pack],
            self.place.on(section=self.place.core),
        )
        return here, there

    def start_own(self, chunk):
        for pack in (self.place.core, self.place.s):
            for copy in self.own_copies(chunk, pack)[::-1]:
                copy.start()

    def wait_own(self, layer, chunk, pack):
        here, there = self.own_copies(chunk, pack)

        @pl.when(self.place.s == layer)
        def _():
            here.wait()

        @pl.when(self.place.s != layer)
        def _():
            there.wait_recv()

    def half_of(self, layer, chunk, rel, half):
        piece = self.piece(layer, chunk, self.place.s, rel)
        if (layer, chunk) not in SHARED:
            return piece
        return piece.at[pl.ds(pl.multiple_of(half * 384, 128), 384)]

    def hops(self, layer, chunk):
        place = self.place
        own, first, second, third = (
            self.half_of(layer, chunk, rel, place.half) for rel in (0, place.rel_one, place.rel_two, 3)
        )
        moves = ((own, first, place.hop_one), (own, second, place.hop_two), (first, third, place.hop_two))
        return [
            remote(
                source,
                target,
                self.hop_send.at[layer, chunk, i],
                self.hop_recv.at[layer, chunk, i],
                place.on(tp=column),
            )
            for i, (source, target, column) in enumerate(moves)
        ]

    def passes(self, layer, chunk, half, device, send, receive):
        place = self.place
        found = []
        for i, rel in enumerate((place.rel_one, place.rel_two, 3)):
            piece = self.half_of(layer, chunk, rel, half)
            sems = send.at[layer, chunk, i], receive.at[layer, chunk, i]
            found.append(remote(piece, piece, *sems, device))
        return found

    def chips(self, layer, chunk):
        place = self.place
        device = place.on(section=place.core)
        return self.passes(layer, chunk, place.half, device, self.chip_send, self.chip_recv)

    def twins(self, layer, chunk):
        place = self.place
        device = place.on(seq=place.twin)
        return self.passes(layer, chunk, place.half, device, self.twin_send, self.twin_recv)

    def twins_in(self, layer, chunk):
        place = self.place
        device = place.on(seq=place.twin)
        return self.passes(layer, chunk, 1 - place.half, device, self.twin_send, self.twin_recv)

    def lates(self, layer, chunk):
        place = self.place
        device = place.on(section=place.core)
        return self.passes(layer, chunk, 1 - place.half, device, self.late_send, self.late_recv)

    def onward(self, layer, chunk, i):
        self.chips(layer, chunk)[i].start()
        if (layer, chunk) in SHARED:
            self.twins(layer, chunk)[i].start()

    def begin(self, layer, chunk):
        self.wait_own(layer, chunk, self.place.s)
        first, second, _ = self.hops(layer, chunk)
        first.start()
        second.start()

    def forward(self, layer, chunk):
        first, second, third = self.hops(layer, chunk)
        first.wait_recv()
        third.start()
        self.onward(layer, chunk, 0)
        second.wait_recv()
        self.onward(layer, chunk, 1)

    def finish(self, layer, chunk):
        self.hops(layer, chunk)[2].wait_recv()
        self.onward(layer, chunk, 2)

    def complete(self, layer, chunk):
        for arrived, late in zip(self.twins_in(layer, chunk), self.lates(layer, chunk)):
            arrived.wait_recv()
            late.start()

    def need(self, layer, chunk):
        if chunk < 3:
            self.wait_own(layer, chunk, self.place.core)
        for copy in self.chips(layer, chunk):
            copy.wait_recv()
        if (layer, chunk) in SHARED:
            for copy in self.lates(layer, chunk):
                copy.wait_recv()

    def drain(self):
        for chunk in range(4):
            for pack in range(2):
                self.own_copies(chunk, pack)[1].wait_send()
            for layer in range(2):
                sent = self.hops(layer, chunk) + self.chips(layer, chunk)
                if (layer, chunk) in SHARED:
                    sent += self.twins(layer, chunk) + self.lates(layer, chunk)
                for copy in sent:
                    copy.wait_send()


class KeyShare:
    def __init__(self, place, kv, layer, sems):
        self.place, self.kv, self.layer = place, kv, layer
        self.near_send, self.near_recv, self.far_send, self.far_recv = sems
        s, odd = place.s, place.half == 1
        self.sends_near = (s == 0) | ~odd
        self.sends_far = (s == 0) & ~odd
        self.passes = (s == 0) & odd
        self.gets_near = (s == 1) | odd
        self.gets_far = odd

    def rows(self, start, part):
        lanes = pl.ds(part * LANES, LANES)
        return self.kv.at[self.layer, :, pl.ds(start, PIECE), lanes]

    def near(self, part):
        place = self.place
        return remote(
            self.rows(2 * PIECE, part),
            self.rows(PIECE, part),
            self.near_send.at[self.layer, part],
            self.near_recv.at[self.layer, part],
            place.on(section=place.core, seq=place.z + place.s * (1 - place.half)),
        )

    def far(self, part):
        place = self.place
        return remote(
            self.rows(2 * PIECE, part),
            self.rows(0, part),
            self.far_send.at[self.layer, part],
            self.far_recv.at[self.layer, part],
            place.on(seq=place.twin),
        )

    def last(self, part):
        place = self.place
        return remote(
            self.rows(PIECE, part),
            self.rows(0, part),
            self.far_send.at[self.layer, part],
            self.far_recv.at[self.layer, part],
            place.on(section=place.core),
        )

    def start(self, part):
        @pl.when(self.sends_near)
        def _():
            self.near(part).start()

        @pl.when(self.sends_far)
        def _():
            self.far(part).start()

    def arrive(self, part):
        @pl.when(self.gets_near)
        def _():
            self.near(part).wait_recv()

        @pl.when(self.passes)
        def _():
            self.last(part).start()

        @pl.when(self.gets_far)
        def _():
            self.far(part).wait_recv()

    def drain(self):
        for part in range(3):

            @pl.when(self.sends_near)
            def _():
                self.near(part).wait_send()

            @pl.when(self.sends_far)
            def _():
                self.far(part).wait_send()

            @pl.when(self.passes)
            def _():
                self.last(part).wait_send()


def forward_kernel(
    tokens,
    cotangent,
    own_a,
    own_b,
    own_c,
    lengths,
    cosine,
    sine_table,
    full_a_out,
    full_b_out,
    gains_out,
    seeded_out,
    x_out,
    low_out,
    q_out,
    kv_out,
    att_out,
    mid_out,
    hid_out,
    lse_out,
    bias_out,
    full_a,
    full_b,
    full_c,
    low,
    x,
    normed,
    q,
    kv,
    att,
    mid,
    hid,
    lse,
    values_turned,
    turned_att,
    bias,
    *sems,
):
    weight_sems, key_sems = sems[:11], sems[11:15]
    token_sem, swap_send, swap_recv, seed_sem, seed_send, seed_recv, save_sem = sems[15:]
    place = Place()
    weights = Weights(place, (own_a, own_b, own_c), (full_a, full_b, full_c), weight_sems)
    lse[...] = jnp.zeros_like(lse)
    kv[:, :, : 2 * PIECE, :] = jnp.zeros((2, 2, 2 * PIECE, kv.shape[-1]), jnp.bfloat16)
    place.meet(place.partners())
    group_rows = pl.ds(pl.multiple_of(place.group * PIECE, PIECE), PIECE)
    columns = pl.ds(pl.multiple_of(place.s * PIECE, PIECE), PIECE)

    def bring(whole, target, here, send, receive):
        kept = whole.at[4 * place.group + place.t, columns]
        sent = whole.at[4 * (1 - place.group) + place.t, columns]
        target = target.at[group_rows]
        return (
            pltpu.make_async_copy(kept, target, here),
            remote(sent, target, send, receive, place.on(seq=place.far)),
        )

    own_tokens, swap = bring(tokens, low, token_sem, swap_send, swap_recv)
    own_seed, seed_swap = bring(cotangent, seeded_out, seed_sem, seed_send, seed_recv)
    own_tokens.start()
    swap.start()
    weights.start_own(0)
    weights.begin(0, 0)
    weights.start_own(3)
    weights.start_own(1)
    for layer in range(2):
        weights.begin(layer, 3)
        weights.wait_own(layer, 3, place.core)
    gains = full_c.at[:, 0, 0]
    gains_out[...] = full_c[:, 0, 0]
    fill_bias(bias, lengths, 4 * place.group + place.t, 2 * place.half + place.s)
    bias_save = pltpu.make_async_copy(bias, bias_out, save_sem.at[17])
    bias_save.start()
    weights.forward(0, 0)
    own_tokens.wait()
    swap.wait()
    x_save = pltpu.make_async_copy(low, x_out, save_sem.at[16])
    x_save.start()
    x[...] = low[...].astype(jnp.float32)

    def saves(layer):
        pairs = [
            (low, low_out.at[layer]),
            (q, q_out.at[layer]),
            (kv.at[layer], kv_out.at[layer]),
            (att, att_out.at[layer]),
            (mid, mid_out.at[layer]),
            (hid, hid_out.at[layer]),
            (lse, lse_out.at[layer]),
        ]
        return [pltpu.make_async_copy(a, b, save_sem.at[i]) for i, (a, b) in enumerate(pairs)]

    def weight_saves(layer):
        copies = []
        for i, (a, b) in enumerate(((full_a, full_a_out), (full_b, full_b_out))):
            for pack in range(2):
                sem = save_sem.at[8 + 4 * layer + 2 * i + pack]
                copies.append(pltpu.make_async_copy(a.at[layer, pack], b.at[layer, pack], sem))
        return copies

    for layer in range(2):
        share = KeyShare(place, kv, layer, key_sems)
        unit, _ = normalize(x[...])
        normed[...] = (unit * gains[layer, 0:1]).astype(jnp.bfloat16)
        if layer == 0:
            weights.finish(0, 0)
            weights.begin(0, 1)
            weights.start_own(2)
        else:
            weights.finish(1, 0)
            weights.begin(1, 2)
            for copy in saves(0)[1:]:
                copy.wait()
        weights.need(layer, 0)
        for copy in weight_saves(layer)[:2]:
            copy.start()
        for part in range(3):
            lanes = pl.ds(part * LANES, LANES)
            keep = normed[...]
            mixed = dot_nt(keep, full_a[layer, 0, 0, lanes, :])
            q[:, lanes] = turn(mixed, cosine[...], sine_table[...]).astype(jnp.bfloat16)
            mixed = dot_nt(keep, full_a[layer, 0, 1, lanes, :])
            mixed = turn(mixed, cosine[...], sine_table[...]).astype(jnp.bfloat16)
            kv[layer, 0, 2 * PIECE : 3 * PIECE, lanes] = mixed[PIECE:]
            kv[layer, 0, 3 * PIECE :, lanes] = mixed[:PIECE]
            mixed = dot_nt(keep, full_a[layer, 1, 0, lanes, :]).astype(jnp.bfloat16)
            kv[layer, 1, 2 * PIECE : 3 * PIECE, lanes] = mixed[PIECE:]
            kv[layer, 1, 3 * PIECE :, lanes] = mixed[:PIECE]
            share.start(part)
        if layer == 0:
            weights.forward(0, 3)
            weights.forward(1, 3)
            weights.finish(0, 3)
            weights.finish(1, 3)
            own_seed.start()
            weights.begin(0, 2)
        else:
            weights.forward(1, 1)
        for part in range(3):
            lanes = pl.ds(part * LANES, LANES)
            share.arrive(part)
            values_turned[...] = kv[layer, 1, :, lanes].astype(jnp.float32).T.astype(jnp.bfloat16)
            for start, count in ((0, 4 * PIECE), (PIECE, 3 * PIECE)):
                queries = pl.ds(start, PIECE)
                att[queries, lanes] = attention_block(
                    q.at[queries, lanes],
                    kv.at[layer, 0, :count, lanes],
                    values_turned.at[:, :count],
                    bias.at[:count, queries],
                    lse.at[pl.ds(8 * part, 8), queries],
                    turned_att,
                )
            if part == 2 and layer == 0:
                seed_swap.start()
            if layer == 0:
                if part == 0:
                    weights.forward(0, 1)
                elif part == 1:
                    weights.finish(0, 1)
                    weights.begin(1, 0)
                else:
                    weights.forward(0, 2)
            else:
                if part == 1:
                    weights.finish(1, 1)
                elif part == 2:
                    weights.forward(1, 2)
                    weights.complete(1, 1)
        for copy in saves(layer)[1:4] + saves(layer)[6:]:
            copy.start()

        def project(part, _):
            lanes = pl.ds(pl.multiple_of(part * LANES, LANES), LANES)
            mid[:, lanes] = x[:, lanes] + dot_nn(att[...], full_a[layer, 1, 1, :, lanes])
            return 0

        lax.fori_loop(0, 3, project, 0)
        unit, _ = normalize(mid[...])
        normed[...] = (unit * gains[layer, 1:2]).astype(jnp.bfloat16)
        x[...] = mid[...] + gains[layer, 2:3]
        saves(layer)[4].start()
        weights.need(layer, 3)
        for part in range(2):
            if part == 0 and layer == 0:
                weights.finish(0, 2)
                weights.begin(1, 1)
            elif part == 1 and layer == 0:
                weights.complete(0, 2)
            elif part == 1:
                weights.finish(1, 2)
            weights.need(layer, part + 1)
            if part == 1:
                for copy in weight_saves(layer)[2:]:
                    copy.start()

            def feed(rel, _):
                start = pl.multiple_of(rel * 768 + part * 384, 128)
                units = pl.ds(start, 384)
                shift = full_c[layer, 1, rel, 0:1, pl.ds(part * 384, 384)]
                tile = rel * 2 + part
                pre = dot_nn(normed[...], full_b[layer, 0, tile]) + shift
                hid[:, units] = pre.astype(jnp.bfloat16)
                active = gelu(pre).astype(jnp.bfloat16)
                x[...] += dot_nt(active, full_b[layer, 1, tile])
                return 0

            lax.fori_loop(0, 4, feed, 0)
        saves(layer)[5].start()
        if layer == 0:
            x_save.wait()
        else:
            saves(0)[0].wait()
        low[...] = x[...].astype(jnp.bfloat16)
        saves(layer)[0].start()
        x[...] = low[...].astype(jnp.float32)
        if layer == 0:
            weights.forward(1, 0)
    for copy in saves(1):
        copy.wait()
    for layer in range(2):
        for copy in weight_saves(layer):
            copy.wait()
        KeyShare(place, kv, layer, key_sems).drain()
    weights.drain()
    bias_save.wait()
    own_seed.wait()
    seed_swap.wait()


def run_forward(tokens, cotangent, own_a, own_b, own_c, lengths, cosine, sine_table):
    shape = jax.ShapeDtypeStruct
    low_type, full_type = jnp.bfloat16, jnp.float32
    count = 2 * PIECE
    width = tokens.shape[-1]
    units = 8 * own_b.shape[-1]
    dma = pltpu.SemaphoreType.DMA
    return pl.pallas_call(
        forward_kernel,
        name="forward_layers",
        out_shape=[
            shape((2, 2, 2, width, width), low_type),
            shape((2, 2, 8, width, units // 8), low_type),
            shape((2, 8, width), full_type),
            shape((count, width), low_type),
            shape((count, width), low_type),
            shape((2, count, width), low_type),
            shape((2, count, width), low_type),
            shape((2, 2, 4 * PIECE, width), low_type),
            shape((2, count, width), low_type),
            shape((2, count, width), full_type),
            shape((2, count, units), low_type),
            shape((2, 24, count), full_type),
            shape((4 * PIECE, count), full_type),
        ],
        in_specs=[HBM] * 5 + [pl.BlockSpec(memory_space=pltpu.SMEM)] + [VMEM] * 2,
        out_specs=[HBM] * 2 + [VMEM] + [HBM] * 10,
        scratch_shapes=[
            pltpu.VMEM((2, 2, 2, width, width), low_type),
            pltpu.VMEM((2, 2, 8, width, units // 8), low_type),
            pltpu.VMEM((2, 2, 4, 8, width), full_type),
            pltpu.VMEM((count, width), low_type),
            pltpu.VMEM((count, width), full_type),
            pltpu.VMEM((count, width), low_type),
            pltpu.VMEM((count, width), low_type),
            pltpu.VMEM((2, 2, 4 * PIECE, width), low_type),
            pltpu.VMEM((count, width), low_type),
            pltpu.VMEM((count, width), full_type),
            pltpu.VMEM((count, units), low_type),
            pltpu.VMEM((24, count), full_type),
            pltpu.VMEM((LANES, 4 * PIECE), low_type),
            pltpu.VMEM((LANES, PIECE), full_type),
            pltpu.VMEM((4 * PIECE, count), full_type),
            dma((4, 2)),
            dma((4, 2)),
            dma((4, 2)),
            dma((2, 4, 3)),
            dma((2, 4, 3)),
            dma((2, 4, 3)),
            dma((2, 4, 3)),
            dma((2, 4, 3)),
            dma((2, 4, 3)),
            dma((2, 4, 3)),
            dma((2, 4, 3)),
            dma((2, 3)),
            dma((2, 3)),
            dma((2, 3)),
            dma((2, 3)),
            dma,
            dma,
            dma,
            dma,
            dma,
            dma,
            dma((18,)),
        ],
        compiler_params=pltpu.CompilerParams(
            collective_id=1, has_side_effects=True, vmem_limit_bytes=62 * 1024 * 1024
        ),
        cost_estimate=pl.CostEstimate(
            flops=30_000_000_000, bytes_accessed=80_000_000, transcendentals=20_000_000
        ),
    )(tokens, cotangent, own_a, own_b, own_c, lengths, cosine, sine_table)


def low_sum(*parts):
    total = parts[0].astype(jnp.float32)
    for part in parts[1:]:
        total = total + part.astype(jnp.float32)
    return total.astype(jnp.bfloat16)


class Spread:
    def __init__(self, place, source, stage, layer, out, sems):
        self.place, self.source, self.stage = place, source, stage
        self.layer, self.out = layer, out
        self.local, self.swap_send, self.swap_recv, self.hop_send, self.hop_recv = sems[:5]
        self.end_local, self.end_send, self.end_recv = sems[5:]
        self.groups = (place.group, 1 - place.group)

    def entry(self):
        place = self.place
        kept = self.source.at[pl.ds(pl.multiple_of(place.group * PIECE, PIECE), PIECE)]
        sent = self.source.at[pl.ds(pl.multiple_of((1 - place.group) * PIECE, PIECE), PIECE)]
        target = self.stage.at[0, place.group]
        here = pltpu.make_async_copy(kept, target, self.local)
        there = remote(sent, target, self.swap_send, self.swap_recv, place.on(seq=place.far))
        return here, there

    def take(self):
        self.entry()[0].start()

    def swap(self):
        self.entry()[1].start()

    def moves(self, half):
        place, group = self.place, self.groups[half]
        own = self.stage.at[0, group]
        first = self.stage.at[place.rel_one, group]
        second = self.stage.at[place.rel_two, group]
        third = self.stage.at[3, group]
        listed = (
            (own, first, place.hop_one),
            (own, second, place.hop_two),
            (first, third, place.hop_two),
        )
        return [
            remote(
                source,
                target,
                self.hop_send.at[half, i],
                self.hop_recv.at[half, i],
                place.on(tp=column),
            )
            for i, (source, target, column) in enumerate(listed)
        ]

    def hops(self, half):
        here, there = self.entry()
        if half == 0:
            here.wait()
        else:
            there.wait_recv()
        first, second, _ = self.moves(half)
        first.start()
        second.start()
        self.put(half, 0)

    def forward(self, half):
        first, _, third = self.moves(half)
        first.wait_recv()
        third.start()
        self.put(half, 1)

    def finish(self, half):
        _, second, third = self.moves(half)
        second.wait_recv()
        self.put(half, 2)
        third.wait_recv()
        self.put(half, 3)

    def ends(self, half, step):
        place, group = self.place, self.groups[half]
        rows = pl.ds(pl.multiple_of(place.s * PIECE, PIECE), PIECE)
        rel = (0, place.rel_one, place.rel_two, 3)[step]
        column = (place.t, place.hop_one, place.hop_two, 3 - place.t)[step]
        source, target = self.stage.at[rel, group], self.out.at[group, column, rows]
        here = pltpu.make_async_copy(source, target, self.end_local.at[half, step])
        there = remote(
            source,
            target,
            self.end_send.at[half, step],
            self.end_recv.at[half, step],
            place.on(section=place.core),
        )
        return here, there

    def put(self, half, step):
        @pl.when(self.place.s == self.layer)
        def _():
            self.ends(half, step)[0].start()

        @pl.when(self.place.s != self.layer)
        def _():
            self.ends(half, step)[1].start()

    def drain(self):
        self.entry()[1].wait_send()
        for half in range(2):
            for copy in self.moves(half):
                copy.wait_send()

        @pl.when(self.place.s == self.layer)
        def _():
            for half in range(2):
                for step in range(4):
                    here, there = self.ends(half, step)
                    here.wait()
                    there.wait_recv()

        @pl.when(self.place.s != self.layer)
        def _():
            for half in range(2):
                for step in range(4):
                    self.ends(half, step)[1].wait_send()


def spread_sems():
    dma = pltpu.SemaphoreType.DMA
    return [dma, dma, dma, dma((2, 3)), dma((2, 3)), dma((2, 4)), dma((2, 4)), dma((2, 4))]


class Sum:
    def __init__(self, place, source, total, buffers, sems, loaded=False, opens=None, waits=None):
        self.place, self.source, self.total = place, source, total
        self.inbox, self.hop_in, self.line_in = buffers
        self.loaded, self.opens, self.waits = loaded, opens, waits
        (
            self.mine_sem,
            self.chip_send,
            self.chip_recv,
            self.hop_send,
            self.hop_recv,
            self.line_send,
            self.line_recv,
            self.end_local,
            self.end_send,
            self.end_recv,
        ) = sems
        z = place.z
        self.outer = (z == 0) | (z == 3)
        self.inner = (z == 1) | (z == 2)
        self.order = (3, 1, 2, 0)

    def mine(self, rel):
        return pltpu.make_async_copy(
            self.source(self.place.s, rel), self.total(rel), self.mine_sem.at[rel]
        )

    def other(self, rel):
        return remote(
            self.source(self.place.core, rel),
            self.inbox.at[rel],
            self.chip_send.at[rel],
            self.chip_recv.at[rel],
            self.place.on(section=self.place.core),
        )

    def start(self):
        if self.waits is not None:
            pl.semaphore_wait(self.waits, 1)
        for rel in self.order:
            if self.inbox is not None:
                self.other(rel).start()
            if self.loaded:
                self.mine(rel).start()

    def load(self, travels=True):
        for rel in self.order:
            if self.loaded:
                self.mine(rel).wait()
            if self.inbox is not None:
                self.other(rel).wait_recv()
                total = self.total(rel)
                total[...] = low_sum(total[...], self.inbox[rel])
            if travels and rel == 3:
                self.moves()[0].start()
            elif travels and rel == 2:
                self.moves()[1].start()
        if self.opens is not None:
            pl.semaphore_signal(
                self.opens,
                inc=1,
                device_id=self.place.on(section=self.place.core),
                device_id_type=MESH,
            )

    def moves(self):
        place = self.place
        listed = (
            (3, 0, place.hop_two),
            (place.rel_two, 1, place.hop_two),
            (place.rel_one, 2, place.hop_one),
        )
        return [
            remote(
                self.total(rel),
                self.hop_in.at[slot],
                self.hop_send.at[slot],
                self.hop_recv.at[slot],
                place.on(tp=column),
            )
            for rel, slot, column in listed
        ]

    def middle(self):
        first, _, third = self.moves()
        first.wait_recv()
        total = self.total(self.place.rel_one)
        total[...] = low_sum(total[...], self.hop_in[0])
        third.start()

    def lines(self):
        place = self.place
        own, line_sum = self.total(0), self.total(1)
        listed = (
            (own, self.line_in.at[0], place.twin),
            (own, self.line_in.at[1], 3 - place.z),
            (line_sum, line_sum, place.twin),
        )
        return [
            remote(
                source,
                target,
                self.line_send.at[i],
                self.line_recv.at[i],
                place.on(seq=plane),
            )
            for i, (source, target, plane) in enumerate(listed)
        ]

    def gather(self, save=None):
        _, second, third = self.moves()
        second.wait_recv()
        third.wait_recv()
        total = self.total(0)
        total[...] = low_sum(total[...], self.hop_in[1], self.hop_in[2])
        second.wait_send()
        third.wait_send()
        if save is not None:
            save.start()
        else:
            self.enter_line()

    def resume(self, saved):
        saved.wait()
        self.enter_line()

    def enter_line(self):
        @pl.when(self.outer)
        def _():
            self.lines()[0].start()

    def line_one(self):
        @pl.when(self.inner)
        def _():
            self.lines()[0].wait_recv()
            total = self.total(0)
            total[...] = low_sum(total[...], self.line_in[0])
            self.lines()[1].start()

    def line_two(self):
        @pl.when(self.inner)
        def _():
            self.lines()[1].wait_recv()
            self.total(1)[...] = low_sum(self.total(0)[...], self.line_in[1])
            self.lines()[2].start()

    def line_three(self):
        @pl.when(self.outer)
        def _():
            self.lines()[2].wait_recv()

    def ends(self, target):
        here = pltpu.make_async_copy(self.total(1), target, self.end_local)
        there = remote(
            self.total(1),
            target,
            self.end_send,
            self.end_recv,
            self.place.on(section=self.place.core),
        )
        return here, there

    def store(self, save):
        self.line_three()
        save.start()

    def finish(self, layer, target):
        self.line_three()
        here, there = self.ends(target)

        @pl.when(self.place.s == layer)
        def _():
            here.start()

        @pl.when(self.place.s != layer)
        def _():
            there.start()

    def drain_exchange(self):
        if self.inbox is not None:
            for rel in range(4):
                self.other(rel).wait_send()

    def drain_end(self, layer, target):
        here, there = self.ends(target)

        @pl.when(self.place.s == layer)
        def _():
            here.wait()
            there.wait_recv()

        @pl.when(self.place.s != layer)
        def _():
            there.wait_send()

    def drain_plane(self):
        self.drain_exchange()
        self.moves()[0].wait_send()

    def drain_line(self):
        @pl.when(self.outer)
        def _():
            self.lines()[0].wait_send()

        @pl.when(self.inner)
        def _():
            self.lines()[1].wait_send()
            self.lines()[2].wait_send()


def sum_sems():
    dma = pltpu.SemaphoreType.DMA
    return [dma((4,))] * 3 + [dma((3,))] * 4 + [dma] * 3


SUM_SEMS = 10


def sum_buffers(piece, counts):
    return [pltpu.VMEM((count,) + piece, jnp.bfloat16) for count in counts]


def attention_sums(place, grads, buffers, sems):
    sums = []
    for i in range(2):
        total, inbox, hop_in, line_in = buffers[4 * i : 4 * i + 4]

        def source(pack, rel, i=i):
            return grads.at[pack, i, rel]

        def kept(rel, total=total):
            return total.at[rel]

        own_sems = sems[SUM_SEMS * i : SUM_SEMS * (i + 1)]
        sums.append(Sum(place, source, kept, (inbox, hop_in, line_in), own_sems, loaded=True))
    return sums


def feed_sums(place, wb, buffers, sems, gate):
    inbox, sums = buffers[0], []
    for i in range(2):

        def source(pack, rel, i=i):
            return wb.at[pack, rel * 2 + i]

        def kept(rel, i=i):
            return wb.at[place.s, rel * 2 + i]

        own_sems = sems[SUM_SEMS * i : SUM_SEMS * (i + 1)]
        gates = {"opens": gate} if i == 0 else {"waits": gate}
        at = min(i, buffers[1].shape[0] - 1)
        sums.append(Sum(place, source, kept, (inbox, buffers[1].at[at], None), own_sems, **gates))
    return sums


def feed_buffers(piece, count):
    kind = jnp.bfloat16
    return [pltpu.VMEM((4,) + piece, kind), pltpu.VMEM((count, 3) + piece, kind)]


def line_sum(place, total, line_in, sems):
    return Sum(place, None, lambda rel: total.at[rel], (None, None, line_in), sems)


class KeyReturn:
    def __init__(self, place, kv, near_in, far_in, sems):
        self.place, self.kv = place, kv
        self.near_in, self.far_in, self.pass_in = near_in, far_in, far_in
        (
            self.near_send,
            self.near_recv,
            self.far_send,
            self.far_recv,
            self.pass_send,
            self.pass_recv,
        ) = sems
        s, odd = place.s, place.half == 1
        self.is_third = (s == 0) & odd
        self.is_fourth = (s == 1) & odd
        self.is_second = (s == 1) & ~odd
        self.is_first = (s == 0) & ~odd

    def sources(self, start, part):
        return self.kv.at[:, pl.ds(start, PIECE), pl.ds(part * LANES, LANES)]

    def copies(self, part):
        place = self.place
        lanes = pl.ds(part * LANES, LANES)
        near = remote(
            self.sources(PIECE, part),
            self.near_in.at[:, :, lanes],
            self.near_send.at[part],
            self.near_recv.at[part],
            place.on(section=place.core, seq=place.z - (1 - place.s) * place.half),
        )
        far = remote(
            self.sources(0, part),
            self.far_in.at[:, :, lanes],
            self.far_send.at[part],
            self.far_recv.at[part],
            place.on(seq=place.twin),
        )
        passed = remote(
            self.sources(0, part),
            self.pass_in.at[:, :, lanes],
            self.pass_send.at[part],
            self.pass_recv.at[part],
            place.on(section=place.core),
        )
        return near, far, passed

    def start(self, part):
        near, far, passed = self.copies(part)

        @pl.when(self.is_fourth)
        def _():
            passed.start()
            near.start()

        @pl.when(self.is_second)
        def _():
            near.start()

        @pl.when(self.is_third)
        def _():
            far.start()

    def relay(self, part):
        near, _, passed = self.copies(part)
        lanes = pl.ds(part * LANES, LANES)

        @pl.when(self.is_third)
        def _():
            passed.wait_recv()
            self.kv[:, PIECE : 2 * PIECE, lanes] = low_sum(
                self.kv[:, PIECE : 2 * PIECE, lanes], self.pass_in[:, :, lanes]
            )
            near.start()

    def collect(self, part):
        near, far, _ = self.copies(part)
        lanes = pl.ds(part * LANES, LANES)
        clean = pl.ds(2 * PIECE, PIECE)

        @pl.when(~self.is_fourth)
        def _():
            near.wait_recv()
            self.kv[:, clean, lanes] = low_sum(self.kv[:, clean, lanes], self.near_in[:, :, lanes])

        @pl.when(self.is_first)
        def _():
            far.wait_recv()
            self.kv[:, clean, lanes] = low_sum(self.kv[:, clean, lanes], self.far_in[:, :, lanes])

    def drain(self):
        for part in range(3):
            near, far, passed = self.copies(part)

            @pl.when(self.is_fourth)
            def _():
                passed.wait_send()
                near.wait_send()

            @pl.when(self.is_second)
            def _():
                near.wait_send()

            @pl.when(self.is_third)
            def _():
                far.wait_send()
                near.wait_send()


def normalize_back(grads, unit, scale, gain):
    lifted = grads * gain
    mean = jnp.mean(lifted, axis=-1, keepdims=True)
    along = jnp.mean(lifted * unit, axis=-1, keepdims=True)
    return scale * (lifted - mean - unit * along)


def attention_back(q_ref, grad_ref, att_ref, keys, values, keys_turned, bias, lse, sums, turned, count):
    turned[...] = (grad_ref[...].astype(jnp.float32) * att_ref[...].astype(jnp.float32)).T

    def head_terms(head):
        rows = pl.ds(pl.multiple_of(head * HDIM, HDIM), HDIM)
        query = q_ref[...] * head_mask(head, 0.125).astype(jnp.bfloat16)
        grad = grad_ref[...] * head_mask(head, 1.0).astype(jnp.bfloat16)
        delta = jnp.sum(turned[rows, :], axis=0, keepdims=True)
        scores = dot_nt(keys[...], query) + bias[...]
        probs = jnp.exp(scores - lse[pl.ds(head, 1), :])
        grad_scores = (probs * (dot_nt(values[...], grad) - delta)).astype(jnp.bfloat16)
        turned[rows, :] = dot_nn(keys_turned[rows, :], grad_scores) * 0.125
        return query, grad, grad_scores, probs.astype(jnp.bfloat16)

    def one(pair, _):
        left, right = head_terms(2 * pair), head_terms(2 * pair + 1)
        query, grad = (jnp.concatenate([left[i], right[i]], axis=0) for i in (0, 1))
        grad_scores, probs = (jnp.concatenate([left[i], right[i]], axis=1) for i in (2, 3))
        sums[0, :count] += dot_nn(grad_scores, query)
        sums[1, :count] += dot_nn(probs, grad)
        return 0

    lax.fori_loop(0, LANES // HDIM // 2, one, 0)
    q_ref[...] = turned[...].T.astype(jnp.bfloat16)


def backward_layer(layer, refs, place, tick, key_sems, sems, tile_sems):
    (
        full_a,
        full_b,
        grad_in,
        x_in,
        q_in,
        kv_in,
        att_in,
        mid_in,
        hid_in,
        lse_in,
        bias_in,
        gains,
        cosine,
        sine_table,
        grads_a,
        grad_out,
        small_out,
        wa,
        wb,
        low,
        q,
        kv,
        att,
        mid,
        hid,
        grad,
        gathered,
        grad_low,
        grad_att,
        near_in,
        far_in,
        sums,
        keys_turned,
        turned_q,
        grad_turned,
        normed_turned,
        lse,
        bias,
    ) = refs
    share = KeyReturn(place, kv, near_in, far_in, key_sems)
    pairs = [
        (grad_in, grad_low),
        (mid_in.at[layer], mid),
        (hid_in.at[layer], hid),
        (full_a.at[layer], wa),
        (att_in.at[layer], att),
        (q_in.at[layer], q),
        (kv_in.at[layer], kv),
        (x_in, low),
        (lse_in.at[layer], lse),
        (bias_in, bias),
    ]
    loads = [pltpu.make_async_copy(a, b, sems.at[i]) for i, (a, b) in enumerate(pairs)]
    def tile_copy(pack, tile):
        return pltpu.make_async_copy(
            full_b.at[layer, pack, tile], wb.at[pack, tile], tile_sems.at[pack, tile]
        )

    for copy in loads[:3]:
        copy.start()
    for part in range(2):
        for rel in range(4):
            for pack in (1, 0):
                tile_copy(pack, rel * 2 + part).start()
    for copy in loads[3:]:
        copy.start()
    tick()
    gain_one, gain_two = gains[layer, 0:1], gains[layer, 1:2]
    for copy in loads[:3]:
        copy.wait()
    small_out[...] = jnp.zeros_like(small_out)

    def by_rows(step):
        def one(i, _):
            step(pl.ds(pl.multiple_of(i * 128, 128), 128))
            return 0

        lax.fori_loop(0, grad.shape[0] // 128, one, 0)

    def enter(rows):
        incoming = grad_low[rows, :].astype(jnp.float32)
        grad[rows, :] = incoming
        small_out[2:3] += jnp.sum(incoming, axis=0, keepdims=True)
        grad_turned[:, rows] = incoming.T.astype(jnp.bfloat16)
        unit, _ = normalize(mid[rows, :])
        normed_turned[:, rows] = (unit * gain_two).T.astype(jnp.bfloat16)
        gathered[rows, :] = jnp.zeros((128, grad.shape[1]), jnp.float32)

    by_rows(enter)
    tick()

    def feed(part, rel):
        start = pl.multiple_of(rel * 768 + part * 384, 128)
        units = pl.ds(start, 384)
        tile = rel * 2 + part
        pre = hid[:, units].astype(jnp.float32)
        squared = pre * pre
        bent = jnp.tanh(0.7978845608028654 * pre * (1.0 + 0.044715 * squared))
        raised = 0.5 * (1.0 + bent)
        active = (pre * raised).astype(jnp.bfloat16)
        slope = raised + 0.5 * pre * (1.0 - bent * bent) * (
            0.7978845608028654 * (1.0 + 3 * 0.044715 * squared)
        )
        tile_copy(1, tile).wait()
        grad_act = dot_nn(grad_low[...], wb[1, tile])
        grad_pre = (grad_act * slope).astype(jnp.bfloat16)
        total = jnp.sum(grad_pre.astype(jnp.float32), axis=0, keepdims=True)
        small_out[pl.ds(4 + rel, 1), pl.ds(part * 384, 384)] = total
        wb[1, tile] = dot_nn(grad_turned[...], active).astype(jnp.bfloat16)
        tile_copy(0, tile).wait()
        gathered[...] += dot_nt(grad_pre, wb[0, tile])
        wb[0, tile] = dot_nn(normed_turned[...], grad_pre).astype(jnp.bfloat16)

    for part in range(2):
        for pair in range(2):

            def one(i, _):
                feed(part, 2 * pair + i)
                return 0

            lax.fori_loop(0, 2, one, 0)
            tick()

    def between(rows):
        found = gathered[rows, :]
        unit, scale = normalize(mid[rows, :])
        small_out[1:2] += jnp.sum(found * unit, axis=0, keepdims=True)
        total = grad[rows, :] + normalize_back(found, unit, scale, gain_two)
        grad[rows, :] = total
        grad_low[rows, :] = total.astype(jnp.bfloat16)

    by_rows(between)
    for copy in loads[3:]:
        copy.wait()

    def project(part, _):
        lanes = pl.ds(pl.multiple_of(part * LANES, LANES), LANES)
        grad_att[:, lanes] = dot_nt(grad_low[...], wa[1, 1, lanes, :]).astype(jnp.bfloat16)
        wa[1, 1, lanes, :] = dot_tn(att[:, lanes], grad_low[...]).astype(jnp.bfloat16)
        return 0

    lax.fori_loop(0, 3, project, 0)
    tick()
    for part in range(3):
        lanes = pl.ds(part * LANES, LANES)
        sums[...] = jnp.zeros_like(sums)
        keys_turned[...] = kv[0, :, lanes].astype(jnp.float32).T.astype(jnp.bfloat16)
        for start, count in ((0, 4 * PIECE), (PIECE, 3 * PIECE)):
            rows = pl.ds(start, PIECE)
            attention_back(
                q.at[rows, lanes],
                grad_att.at[rows, lanes],
                att.at[rows, lanes],
                kv.at[0, :count, lanes],
                kv.at[1, :count, lanes],
                keys_turned.at[:, :count],
                bias.at[:count, rows],
                lse.at[pl.ds(8 * part, 8), rows],
                sums,
                turned_q,
                count,
            )
            if start == 0:
                tick()
        kv[:, :, lanes] = sums[...].astype(jnp.bfloat16)
        share.start(part)
        if part > 0:
            share.relay(part - 1)
        tick()
    normed = grad_att

    def again(rows):
        unit, _ = normalize(low[rows, :].astype(jnp.float32))
        normed[rows, :] = (unit * gain_one).astype(jnp.bfloat16)

    by_rows(again)

    def turned(part, _):
        lanes = pl.ds(pl.multiple_of(part * LANES, LANES), LANES)
        raw = turn(q[:, lanes].astype(jnp.float32), cosine[...], -sine_table[...])
        raw = raw.astype(jnp.bfloat16)
        found = dot_nn(raw, wa[0, 0, lanes, :])

        @pl.when(part == 0)
        def _():
            gathered[...] = found

        @pl.when(part > 0)
        def _():
            gathered[...] += found

        wa[0, 0, lanes, :] = dot_tn(raw, normed[...]).astype(jnp.bfloat16)
        return 0

    lax.fori_loop(0, 3, turned, 0)
    share.relay(2)
    tick()
    for part in range(3):
        share.collect(part)

    def keyed(part, _):
        lanes = pl.ds(pl.multiple_of(part * LANES, LANES), LANES)
        noisy, clean = pl.ds(3 * PIECE, PIECE), pl.ds(2 * PIECE, PIECE)
        raw = jnp.concatenate([kv[0, noisy, lanes], kv[0, clean, lanes]], axis=0)
        raw = turn(raw.astype(jnp.float32), cosine[...], -sine_table[...]).astype(jnp.bfloat16)
        gathered[...] += dot_nn(raw, wa[0, 1, lanes, :])
        wa[0, 1, lanes, :] = dot_tn(raw, normed[...]).astype(jnp.bfloat16)
        raw = jnp.concatenate([kv[1, noisy, lanes], kv[1, clean, lanes]], axis=0)
        gathered[...] += dot_nn(raw, wa[1, 0, lanes, :])
        wa[1, 0, lanes, :] = dot_tn(raw, normed[...]).astype(jnp.bfloat16)
        return 0

    lax.fori_loop(0, 3, keyed, 0)
    tick()
    save_a = pltpu.make_async_copy(wa, grads_a, sems.at[10])
    save_a.start()

    def leave(rows):
        found = gathered[rows, :]
        unit, scale = normalize(low[rows, :].astype(jnp.float32))
        small_out[0:1] += jnp.sum(found * unit, axis=0, keepdims=True)
        total = grad[rows, :] + normalize_back(found, unit, scale, gain_one)
        grad_low[rows, :] = total.astype(jnp.bfloat16)

    by_rows(leave)
    save_grad = pltpu.make_async_copy(grad_low, grad_out, sems.at[11])
    save_grad.start()
    tick()
    share.drain()
    save_a.wait()
    save_grad.wait()


class Ticks:
    def __init__(self, groups):
        self.groups = list(groups)

    def __call__(self):
        if self.groups:
            for step in self.groups.pop(0):
                step()

    def rest(self):
        while self.groups:
            self()


def backward_buffers(width, units):
    low, full, count = jnp.bfloat16, jnp.float32, 2 * PIECE
    return [
        pltpu.VMEM((2, 2, width, width), low),
        pltpu.VMEM((2, 8, width, units // 8), low),
        pltpu.VMEM((count, width), low),
        pltpu.VMEM((count, width), low),
        pltpu.VMEM((2, 4 * PIECE, width), low),
        pltpu.VMEM((count, width), low),
        pltpu.VMEM((count, width), full),
        pltpu.VMEM((count, units), low),
        pltpu.VMEM((count, width), full),
        pltpu.VMEM((count, width), full),
        pltpu.VMEM((count, width), low),
        pltpu.VMEM((count, width), low),
        pltpu.VMEM((2, PIECE, width), low),
        pltpu.VMEM((2, PIECE, width), low),
        pltpu.VMEM((2, 4 * PIECE, LANES), full),
        pltpu.VMEM((LANES, 4 * PIECE), low),
        pltpu.VMEM((LANES, PIECE), full),
        pltpu.VMEM((width, count), low),
        pltpu.VMEM((width, count), low),
        pltpu.VMEM((24, count), full),
        pltpu.VMEM((4 * PIECE, count), full),
    ]


def backward_sems():
    dma = pltpu.SemaphoreType.DMA
    return [dma((3,))] * 6 + [dma((12,)), dma((2, 8))]


BUFFERS = 21


def later(step, *args):
    return lambda: step(*args)


def second_kernel(*refs):
    ins, refs = refs[:15], refs[15:]
    (grads_a, grad_out, small_out, out, carry_one, carry), refs = refs[:6], refs[6:]
    buffers, stages, feed, refs = refs[:BUFFERS], refs[BUFFERS : BUFFERS + 2], refs[23:25], refs[25:]
    sems, feed_sem, gate, carry_sem = refs[:24], refs[24:-2], refs[-2], refs[-1]
    low_both = ins[14]
    place = Place()
    place.meet(place.partners())
    zero, last = [
        Spread(place, low_both.at[i], stages[i], i, out, sems[8 + 8 * i : 16 + 8 * i])
        for i in range(2)
    ]
    one, two = feed_sums(place, buffers[1], feed, feed_sem, gate)
    carries = [
        pltpu.make_async_copy(two.total(rel), carry.at[rel], carry_sem.at[rel]) for rel in range(4)
    ]
    save_one = pltpu.make_async_copy(one.total(0), carry_one, carry_sem.at[4])

    def hand_on():
        two.load(travels=False)
        for copy in carries:
            copy.start()

    tick = Ticks(
        [
            [zero.take, last.take, zero.swap, later(zero.hops, 0), later(last.hops, 0)],
            [],
            [later(zero.forward, 0)],
            [one.start, last.swap],
            [later(zero.hops, 1), later(last.forward, 0)],
            [later(zero.finish, 0)],
            [one.load],
            [later(zero.forward, 1), two.start],
            [later(last.finish, 0)],
            [one.middle],
            [later(last.hops, 1), later(zero.finish, 1)],
            [],
            [hand_on],
            [later(one.gather, save_one), later(last.forward, 1)],
            [],
            [later(last.finish, 1)],
        ]
    )
    body = ins[:3] + (low_both.at[0],) + ins[4:14] + (grads_a, grad_out, small_out) + buffers
    backward_layer(1, body, place, tick, sems[:6], sems[6], sems[7])
    tick.rest()
    zero.drain()
    last.drain()
    one.drain_plane()
    save_one.wait()
    two.drain_exchange()
    for copy in carries:
        copy.wait()


def first_kernel(*refs):
    ins, refs = refs[:17], refs[17:]
    (grads_a, grad_out, small_out, out, done, carry_out), refs = refs[:6], refs[6:]
    buffers, stage, refs = refs[:BUFFERS], refs[BUFFERS], refs[BUFFERS + 1 :]
    feed, (total, hop_in, line_in, line_total, line_in_one), refs = refs[:2], refs[2:7], refs[7:]
    sems, feed_sem, kept_sem, line_sem = refs[:16], refs[16:36], refs[36:46], refs[46:56]
    gate, carry_sem = refs[56:]
    carry_one, carry, prior_grad = ins[14:]
    place = Place()
    place.meet(place.partners())
    back = Spread(place, prior_grad, stage, 1, out, sems[8:16])
    one, two = feed_sums(place, buffers[1], feed, feed_sem, gate)
    kept = Sum(
        place,
        lambda pack, rel: carry.at[rel],
        lambda rel: total.at[rel],
        (None, hop_in, line_in),
        kept_sem,
        loaded=True,
    )
    line = line_sum(place, line_total, line_in_one, line_sem)
    line_load = pltpu.make_async_copy(carry_one, line_total.at[0], carry_sem.at[0])
    saves = [
        pltpu.make_async_copy(line.total(1), done.at[0], carry_sem.at[1]),
        pltpu.make_async_copy(kept.total(1), done.at[1], carry_sem.at[2]),
        pltpu.make_async_copy(one.total(0), carry_out.at[0], carry_sem.at[3]),
        pltpu.make_async_copy(two.total(0), carry_out.at[1], carry_sem.at[4]),
    ]
    tick = Ticks(
        [
            [back.take, back.swap, line_load.start, kept.start, later(back.hops, 0)],
            [later(line.resume, line_load), kept.load],
            [later(back.forward, 0)],
            [one.start, line.line_one],
            [kept.middle, later(back.hops, 1)],
            [line.line_two, later(back.finish, 0)],
            [one.load],
            [kept.gather, two.start],
            [later(back.forward, 1), later(line.store, saves[0])],
            [kept.line_one],
            [one.middle, two.load],
            [kept.line_two, later(back.finish, 1)],
            [],
            [later(one.gather, saves[2]), later(kept.store, saves[1])],
            [two.middle],
            [],
            [later(two.gather, saves[3])],
        ]
    )
    body = ins[:14] + (grads_a, grad_out, small_out) + buffers
    backward_layer(0, body, place, tick, sems[:6], sems[6], sems[7])
    tick.rest()
    back.drain()
    for item in (kept, one, two):
        item.drain_plane()
    line.drain_line()
    kept.drain_line()
    for copy in saves:
        copy.wait()


def last_kernel(*refs):
    priors, (done, carry, grad_zero, small_zero, small_one), refs = refs[:2], refs[2:7], refs[7:]
    (out, final_a, final_b, small), refs = refs[:4], refs[4:]
    held, stage, (small_in, extra), refs = refs[:16], refs[16], refs[17:19], refs[19:]
    (line_total, line_in), sems = refs[:2], refs[2:]
    held_sem, spread_sem, line_sem, sems = sems[:40], sems[40:48], sems[48:68], sems[68:]
    tiny_send, tiny_recv, carry_sem, end_local, end_send, end_recv = sems
    place = Place()
    place.meet(place.partners())
    sums = []
    for i in range(2):
        sums += attention_sums(
            place, priors[i], held[8 * i : 8 * i + 8], held_sem[20 * i : 20 * i + 20]
        )
    lines, loads = [], []
    for i in range(2):
        lines.append(line_sum(place, line_total.at[i], line_in.at[i], line_sem[10 * i : 10 * i + 10]))
        loads.append(pltpu.make_async_copy(carry.at[i], line_total.at[i, 0], carry_sem.at[i]))
    back = Spread(place, grad_zero, stage, 0, out, spread_sem)
    targets = [final_a.at[place.s, 0], final_a.at[place.s, 1]] * 2
    halves = [final_b.at[place.s, :, pl.ds(384 * i, 384)] for i in range(2)]
    layers = (1, 1, 0, 0)
    small[0], small[1] = small_zero[...], small_one[...]
    rows_beside = ((4, 5, 6, 7), (5, 4, 7, 6), (6, 7, 4, 5), (4, 5, 6, 7), (4, 5, 6, 7))
    partners = (
        place.on(section=place.core),
        place.on(tp=place.beside_x),
        place.on(tp=place.beside_y),
        place.on(seq=place.twin),
        place.on(seq=place.far),
    )

    def done_ends(i):
        here = pltpu.make_async_copy(done.at[i], halves[i], end_local.at[i])
        there = remote(
            done.at[i], halves[i], end_send.at[i], end_recv.at[i], place.on(section=place.core)
        )
        return here, there

    def done_start():
        @pl.when(place.s == 1)
        def _():
            for i in range(2):
                done_ends(i)[0].start()

        @pl.when(place.s == 0)
        def _():
            for i in range(2):
                done_ends(i)[1].start()

    def done_wait():
        @pl.when(place.s == 1)
        def _():
            for i in range(2):
                here, there = done_ends(i)
                here.wait()
                there.wait_recv()

        @pl.when(place.s == 0)
        def _():
            for i in range(2):
                done_ends(i)[1].wait_send()

    def tiny(i):
        return remote(extra.at[i], small_in.at[i], tiny_send.at[i], tiny_recv.at[i], partners[i])

    def tiny_start(i):
        extra[i] = small[...]
        tiny(i).start()

    def tiny_end(i):
        tiny(i).wait_recv()
        for layer in range(2):
            small[layer, 0:4] = extra[i, layer, 0:4] + small_in[i, layer, 0:4]
            for row, other in enumerate(rows_beside[i]):
                at = row + 4
                small[layer, at : at + 1] = (
                    extra[i, layer, at : at + 1] + small_in[i, layer, other : other + 1]
                )

    back.take()
    sums[0].start()
    for load in loads:
        load.start()
    back.swap()
    tiny_start(0)
    sums[1].start()
    back.hops(0)
    for line, load in zip(lines, loads):
        line.resume(load)
    sums[0].load()
    sums[2].start()
    sums[1].load()
    sums[3].start()
    tiny_end(0)
    tiny_start(1)
    back.forward(0)
    sums[2].load()
    done_start()
    lines[0].line_one()
    sums[0].middle()
    sums[3].load()
    lines[1].line_one()
    sums[1].middle()
    lines[0].line_two()
    tiny_end(1)
    tiny_start(2)
    sums[0].gather()
    sums[2].middle()
    lines[1].line_two()
    sums[1].gather()
    sums[3].middle()
    back.hops(1)
    lines[0].finish(0, halves[0])
    sums[0].line_one()
    sums[2].gather()
    sums[1].line_one()
    tiny_end(2)
    tiny_start(3)
    lines[1].finish(0, halves[1])
    back.finish(0)
    sums[3].gather()
    sums[0].line_two()
    sums[2].line_one()
    sums[1].line_two()
    back.forward(1)
    sums[3].line_one()
    tiny_end(3)
    tiny_start(4)
    sums[0].finish(1, targets[0])
    sums[2].line_two()
    sums[1].finish(1, targets[1])
    sums[3].line_two()
    back.finish(1)
    sums[2].finish(0, targets[2])
    sums[3].finish(0, targets[3])
    tiny_end(4)
    for item, layer, target in zip(sums, layers, targets):
        item.drain_plane()
        item.drain_line()
        item.drain_end(layer, target)
    for item, target in zip(lines, halves):
        item.drain_line()
        item.drain_end(0, target)
    done_wait()
    back.drain()
    for i in range(5):
        tiny(i).wait_send()


def call(kernel, name, number, ins, spaces, shapes, out_spaces, scratch, flops, moved):
    return pl.pallas_call(
        kernel,
        name=name,
        out_shape=[jax.ShapeDtypeStruct(shape, kind) for shape, kind in shapes],
        in_specs=spaces,
        out_specs=out_spaces,
        scratch_shapes=scratch,
        compiler_params=pltpu.CompilerParams(
            collective_id=number, has_side_effects=True, vmem_limit_bytes=62 * 1024 * 1024
        ),
        cost_estimate=pl.CostEstimate(
            flops=flops, bytes_accessed=moved, transcendentals=20_000_000
        ),
    )(*ins)


def results_kernel(*refs):
    layer_raw, zero_raw, one_raw, final_a, final_b = refs[:5]
    layer_out, input_grad, grad_out, grad_up, grad_down = refs[5:10]
    rows, turned, part, tiles, converted, row_sem, tile_sem = refs[10:]
    s = lax.axis_index("section")
    count = rows.shape[0] // 2

    def load(i):
        sem = row_sem.at[0, i]
        if i < count:
            return [pltpu.make_async_copy(layer_raw.at[i // 4, i % 4], rows.at[i], sem)] * 2
        at = i - count
        return [
            pltpu.make_async_copy(raw.at[at // 4, at % 4], rows.at[i], sem) for raw in (zero_raw, one_raw)
        ]

    def store(i):
        target, at = (layer_out, i) if i < count else (input_grad, i - count)
        return pltpu.make_async_copy(rows.at[i], target.at[at // 4, at % 4], row_sem.at[1, i])

    loads = [
        pltpu.make_async_copy(final_b.at[0], tiles.at[0], tile_sem.at[0]),
        pltpu.make_async_copy(final_b.at[1], tiles.at[1], tile_sem.at[1]),
        pltpu.make_async_copy(final_a.at[1, 1], part, tile_sem.at[2]),
    ]
    stores = [
        pltpu.make_async_copy(converted, grad_up, tile_sem.at[3]),
        pltpu.make_async_copy(turned, grad_down, tile_sem.at[4]),
    ]
    for copy in loads:
        copy.start()
    for i in range(count):
        load(i)[0].start()

    @pl.when(s == 0)
    def _():
        for i in range(count, 2 * count):
            load(i)[0].start()

    @pl.when(s != 0)
    def _():
        for i in range(count, 2 * count):
            load(i)[1].start()

    for copy in loads:
        copy.wait()
    converted[...] = tiles[0].astype(jnp.float32)
    stores[0].start()
    grad_out[...] = part[...].astype(jnp.float32)
    turned[...] = tiles[1].astype(jnp.float32).T
    stores[1].start()
    for i in range(2 * count):
        load(i)[0].wait()
        store(i).start()
    for i in range(2 * count):
        store(i).wait()
    for copy in stores:
        copy.wait()


def run_results(layer_raw, zero_raw, one_raw, final_a, final_b):
    full = jnp.float32
    width = final_b.shape[-1]
    big = jax.ShapeDtypeStruct(layer_raw.shape, layer_raw.dtype)
    square = jax.ShapeDtypeStruct((width, width), full)
    dma = pltpu.SemaphoreType.DMA
    return pl.pallas_call(
        results_kernel,
        name="place_results",
        out_shape=[big, big, jax.ShapeDtypeStruct((192, width), full), square, square],
        in_specs=[HBM] * 5,
        out_specs=[HBM] * 2 + [VMEM] + [HBM] * 2,
        scratch_shapes=[
            pltpu.VMEM((16,) + layer_raw.shape[2:], jnp.bfloat16),
            pltpu.VMEM((width, width), full),
            pltpu.VMEM((192, width), jnp.bfloat16),
            pltpu.VMEM((2, width, width), jnp.bfloat16),
            pltpu.VMEM((width, width), full),
            dma((2, 16)),
            dma((5,)),
        ],
        compiler_params=pltpu.CompilerParams(vmem_limit_bytes=48 * 1024 * 1024),
        cost_estimate=pl.CostEstimate(flops=1_000_000, bytes_accessed=35_000_000, transcendentals=0),
    )(layer_raw, zero_raw, one_raw, final_a, final_b)


def run_backward(full_a, full_b, seeded, tokens, low_both, kept, gains, tables):
    low, full, count = jnp.bfloat16, jnp.float32, 2 * PIECE
    width, units = full_a.shape[-1], 8 * full_b.shape[-1]
    grads = [
        ((2, 2, width, width), low),
        ((count, width), low),
        ((8, width), full),
    ]
    out = ((2, 4, count, width), low)
    row_piece, tile_piece = (192, width), (width, units // 8)
    final_a, final_b = ((2, 2) + row_piece, low), ((2, width, 2 * tile_piece[1]), low)
    carry_one, carry, two_tiles = (tile_piece, low), ((4,) + tile_piece, low), ((2,) + tile_piece, low)
    stage = pltpu.VMEM((4, 2, PIECE, width), low)
    dma, gate = pltpu.SemaphoreType.DMA, pltpu.SemaphoreType.REGULAR
    common = (*kept, gains, *tables)
    common_spaces = [HBM] * 11 + [VMEM] * 3
    held = sum_buffers(row_piece, (4, 4, 3, 2) * 2)
    second = call(
        second_kernel,
        "backward_second",
        2,
        (full_a, full_b, seeded, tokens) + common + (low_both,),
        common_spaces + [HBM],
        grads + [out, carry_one, carry],
        [HBM] * 2 + [VMEM] + [HBM] * 3,
        backward_buffers(width, units)
        + [stage, stage]
        + feed_buffers(tile_piece, 1)
        + backward_sems()
        + spread_sems()
        + spread_sems()
        + sum_sems()
        + sum_sems()
        + [gate, dma((5,))],
        40_000_000_000,
        80_000_000,
    )
    prior_a, grad_one, small_one, layer_out, carried_one, carried = second
    first = call(
        first_kernel,
        "backward_first",
        3,
        (full_a, full_b, grad_one, tokens) + common + (carried_one, carried, grad_one),
        common_spaces + [HBM] * 3,
        grads + [out, two_tiles, two_tiles],
        [HBM] * 2 + [VMEM] + [HBM] * 3,
        backward_buffers(width, units)
        + [stage]
        + feed_buffers(tile_piece, 2)
        + sum_buffers(tile_piece, (4, 3, 2, 2, 2))
        + backward_sems()
        + spread_sems()
        + sum_sems()
        + sum_sems()
        + sum_sems()
        + sum_sems()
        + [gate, dma((5,))],
        40_000_000_000,
        80_000_000,
    )
    grads_a, grad_zero, small_zero, out_one, done, carried = first
    by_shard = (2, 2, 4, 192, width)
    last = call(
        last_kernel,
        "sum_and_spread",
        4,
        (prior_a.reshape(by_shard), grads_a.reshape(by_shard), done, carried, grad_zero)
        + (small_zero, small_one),
        [HBM] * 5 + [VMEM] * 2,
        [out, final_a, final_b, ((2, 8, width), full)],
        [HBM] * 3 + [VMEM],
        held
        + held
        + [stage]
        + [pltpu.VMEM((5, 2, 8, width), full), pltpu.VMEM((5, 2, 8, width), full)]
        + [pltpu.VMEM((2, 2) + tile_piece, low), pltpu.VMEM((2, 2) + tile_piece, low)]
        + sum_sems()
        + sum_sems()
        + sum_sems()
        + sum_sems()
        + spread_sems()
        + sum_sems()
        + sum_sems()
        + [dma((5,)), dma((5,))]
        + [dma((2,))] * 4,
        100_000_000,
        40_000_000,
    )
    out_zero, final_a, final_b, small = last
    return layer_out, (out_zero, out_one), final_a, final_b, small


def spread(
    layer_input,
    cotangent,
    doc_lengths,
    ln1_gain,
    w_qkv,
    w_out,
    ln2_gain,
    w_up,
    b_up,
    w_down,
    b_down,
):
    s, t, z = (lax.axis_index(name) for name in ("section", "tp", "seq"))
    micros, rows, width_pos, width = layer_input.shape
    half, group = z % 2, z // 2

    own_a = jnp.stack(
        [
            jnp.stack([w_qkv[0, :, 0].T, w_qkv[0, :, 1].T]),
            jnp.stack([w_qkv[0, :, 2].T, w_out[0]]),
        ]
    )
    shard = w_up.shape[-1]
    own_b = jnp.stack([w_up[0], w_down[0].T]).reshape(2, width, 2, shard // 2).transpose(0, 2, 1, 3)
    gains = jnp.concatenate([ln1_gain, ln2_gain, b_down, jnp.zeros((5, width), jnp.float32)])
    own_c = jnp.stack([gains, jnp.concatenate([b_up, jnp.zeros((7, width), jnp.float32)])])

    lane = jnp.arange(128)
    block_base = (2 * half + s) * PIECE
    query_base = block_base + jnp.arange(2 * PIECE) % PIECE
    frequency = 10000.0 ** (-(lane % (HDIM // 2)).astype(jnp.float32) * 2.0 / HDIM)
    angles = query_base.astype(jnp.float32)[:, None] * frequency[None, :]
    sign = jnp.where(lane % HDIM < HDIM // 2, -1.0, 1.0)
    turn_cos, turn_sin = jnp.cos(angles), jnp.sin(angles) * sign

    lengths = doc_lengths.reshape(micros * rows, -1)
    flat = (micros * rows, width_pos, width)
    forward = run_forward(
        layer_input.reshape(flat), cotangent.reshape(flat), own_a, own_b, own_c, lengths, turn_cos, turn_sin
    )
    full_a, full_b, gains, seeded, tokens, low_both, *kept = forward
    tables = (turn_cos, turn_sin)
    layer_raw, input_raws, final_a, final_b, small = run_backward(
        full_a, full_b, seeded, tokens, low_both, kept, gains, tables
    )
    layer_out, input_grad, grad_out, grad_up, grad_down = run_results(
        layer_raw, *input_raws, final_a, final_b
    )
    small = lax.dynamic_index_in_dim(small, s, 0, keepdims=False)
    final_a = final_a.astype(jnp.float32)
    grad_qkv = jnp.stack([final_a[0, 0].T, final_a[0, 1].T, final_a[1, 0].T], axis=1)
    out_shape = (1,) + layer_input.shape
    return (
        layer_out.reshape(out_shape),
        input_grad.reshape(out_shape),
        small[0:1],
        grad_qkv[None],
        grad_out[None],
        small[1:2],
        grad_up[None],
        small[4:5],
        grad_down[None],
        small[2:3],
    )


def solution(mesh):
    sizes = tuple(mesh.shape[name] for name in ("section", "tp", "seq"))
    local = spread if sizes == (2, 4, 4) else pipelined
    return jax.shard_map(
        local,
        mesh=mesh,
        in_specs=(
            P(None, None, "seq", None),
            P(None, None, "seq", None),
            P(),
            P("section", None),
            P("section", None, None, "tp"),
            P("section", "tp", None),
            P("section", None),
            P("section", None, "tp"),
            P("section", "tp"),
            P("section", "tp", None),
            P("section", None),
        ),
        out_specs=(
            P("section", None, None, "seq", None),
            P("section", None, None, "seq", None),
            P("section", None),
            P("section", None, None, "tp"),
            P("section", "tp", None),
            P("section", None),
            P("section", None, "tp"),
            P("section", "tp"),
            P("section", "tp", None),
            P("section", None),
        ),
        check_vma=False,
    )
```

```python
import jax
import jax.numpy as jnp
from jax import lax
from jax.experimental import pallas as pl
from jax.experimental.pallas import tpu as pltpu
from jax.sharding import PartitionSpec as P

HDIM = 64
BLOCK = 16
HALF = 1024


def from_behind(value, axis, by):
    size = lax.axis_size(axis)
    pairs = [(i, i + by) for i in range(size) if 0 <= i + by < size]
    return lax.ppermute(value, axis, pairs)


def layer_norm(values, gain):
    center = values - jnp.mean(values, axis=-1, keepdims=True)
    spread = jnp.mean(center * center, axis=-1, keepdims=True)
    return center * lax.rsqrt(spread + 1e-05) * gain


def rotate(values, cosine, sine_table):
    middle = values.shape[-1] // 2
    first_half = values[..., :middle]
    second_half = values[..., middle:]
    return jnp.concatenate(
        [
            first_half * cosine - second_half * sine_table,
            second_half * cosine + first_half * sine_table,
        ],
        axis=-1,
    )


def rotary_tables(positions):
    frequency = 10000.0 ** (-jnp.arange(HDIM // 2).astype(jnp.float32) * 2.0 / HDIM)
    angles = (positions % HALF).astype(jnp.float32)[:, None, None] * frequency[None, None, :]
    return (jnp.cos(angles), jnp.sin(angles))


def allowed(query_pos, query_doc, key_pos, key_doc):
    query_noisy = query_pos < HALF
    key_noisy = key_pos < HALF
    query_block = query_pos % HALF // BLOCK
    key_block = key_pos % HALF // BLOCK
    within = query_noisy & key_noisy & (query_block == key_block)
    earlier = query_noisy & ~key_noisy & (key_block < query_block)
    causal = ~query_noisy & ~key_noisy & (key_block <= query_block)
    return (within | earlier | causal) & (query_doc == key_doc)


def document_ids(doc_lengths):
    doc_ends = jnp.cumsum(doc_lengths, axis=-1)
    base_pos = jnp.arange(2 * HALF) % HALF
    return jnp.sum((base_pos[:, None] >= doc_ends[..., None, :]).astype(jnp.int32), axis=-1)


def gelu_tanh(values):
    return jax.nn.gelu(values, approximate=True)


def keep_slot(storage, value, slot_index, is_active):
    current = lax.dynamic_index_in_dim(storage, slot_index, 0, keepdims=False)
    return lax.dynamic_update_index_in_dim(
        storage, jnp.where(is_active, value, current), slot_index, 0
    )


def local_queries(inputs, ln_one, w_mix, tables):
    cosine, sine_table, query_pos = tables
    row_count, pos_count = (inputs.shape[0], inputs.shape[1])
    normed = layer_norm(inputs, ln_one).astype(jnp.bfloat16)
    mixed = jnp.einsum("rpd,dcf->rpcf", normed, w_mix, preferred_element_type=jnp.float32)
    shaped = mixed.reshape(row_count, pos_count, 3, -1, HDIM)
    queries = rotate(shaped[:, :, 0], cosine, sine_table).astype(jnp.bfloat16)
    keys_own = rotate(shaped[:, :, 1], cosine, sine_table).astype(jnp.bfloat16)
    values_own = shaped[:, :, 2].astype(jnp.bfloat16)
    return (normed, queries, keys_own, values_own)


def masked_scores(queries, keys_heads, query_pos, docs_all):
    pos_count = queries.shape[1]
    query_docs = lax.dynamic_slice_in_dim(docs_all, query_pos[0], pos_count, 1)
    key_pos = jnp.arange(keys_heads.shape[1])
    key_mask = allowed(
        query_pos[None, :, None],
        query_docs[:, :, None],
        key_pos[None, None, :],
        docs_all[:, None, :],
    )
    scores = (
        jnp.einsum("rqhd,rkhd->rhqk", queries, keys_heads, preferred_element_type=jnp.float32)
        * 0.125
    )
    return jnp.where(key_mask[:, None], scores, -1e30)


def forward_step(inputs, weights, tables, docs_all):
    ln_one, w_mix, w_proj, ln_two, w_first, b_first, w_second, b_second = weights
    row_count, pos_count = (inputs.shape[0], inputs.shape[1])
    normed, queries, keys_own, values_own = local_queries(inputs, ln_one, w_mix, tables)
    local_width = w_mix.shape[-1]
    keys_all, values_all = (
        lax.all_gather(
            keys_own.reshape(row_count, pos_count, local_width), "seq", axis=1, tiled=True
        ),
        lax.all_gather(
            values_own.reshape(row_count, pos_count, local_width), "seq", axis=1, tiled=True
        ),
    )
    keys_heads = keys_all.reshape(row_count, keys_all.shape[1], -1, HDIM)
    values_heads = values_all.reshape(row_count, values_all.shape[1], -1, HDIM)
    softmax_out = jax.nn.softmax(
        masked_scores(queries, keys_heads, tables[2], docs_all), axis=-1
    ).astype(jnp.bfloat16)
    attended = jnp.einsum(
        "rhqk,rkhd->rqhd", softmax_out, values_heads, preferred_element_type=jnp.float32
    )
    attended = attended.astype(jnp.bfloat16).reshape(row_count, pos_count, local_width)
    middle = inputs + lax.psum(
        jnp.einsum("rpe,ed->rpd", attended, w_proj, preferred_element_type=jnp.float32).astype(
            jnp.bfloat16
        ),
        "tp",
    ).astype(jnp.float32)
    normed_two = layer_norm(middle, ln_two).astype(jnp.bfloat16)
    hidden_pre = (
        jnp.einsum("rpd,df->rpf", normed_two, w_first, preferred_element_type=jnp.float32) + b_first
    )
    activated = gelu_tanh(hidden_pre).astype(jnp.bfloat16)
    second_terms = jnp.einsum(
        "rpf,fd->rpd", activated, w_second, preferred_element_type=jnp.float32
    )
    result = (
        middle + lax.psum(second_terms.astype(jnp.bfloat16), "tp").astype(jnp.float32) + b_second
    )
    return (result, middle, keys_all, values_all)


def backward_step(inputs, middle, grad_out, weights, tables, docs_all):
    ln_one, w_mix, w_proj, ln_two, w_first, b_first, w_second, b_second = weights
    cosine, sine_table, query_pos = tables
    row_count, pos_count = (inputs.shape[0], inputs.shape[1])
    local_width = w_mix.shape[-1]
    head_count = local_width // HDIM
    normed, queries, keys_own, values_own = local_queries(inputs, ln_one, w_mix, tables)
    keys_all, values_all = (
        lax.all_gather(
            keys_own.reshape(row_count, pos_count, local_width), "seq", axis=1, tiled=True
        ),
        lax.all_gather(
            values_own.reshape(row_count, pos_count, local_width), "seq", axis=1, tiled=True
        ),
    )
    keys_heads = keys_all.reshape(row_count, keys_all.shape[1], head_count, HDIM)
    values_heads = values_all.reshape(row_count, values_all.shape[1], head_count, HDIM)
    scores = masked_scores(queries, keys_heads, query_pos, docs_all)
    softmax_out = jax.nn.softmax(scores, axis=-1)
    probs_low = softmax_out.astype(jnp.bfloat16)
    attended = jnp.einsum(
        "rhqk,rkhd->rqhd", probs_low, values_heads, preferred_element_type=jnp.float32
    )
    attended = attended.astype(jnp.bfloat16).reshape(row_count, pos_count, local_width)
    normed_two = layer_norm(middle, ln_two).astype(jnp.bfloat16)
    hidden_pre = (
        jnp.einsum("rpd,df->rpf", normed_two, w_first, preferred_element_type=jnp.float32) + b_first
    )
    activated = gelu_tanh(hidden_pre).astype(jnp.bfloat16)
    grad_low = grad_out.astype(jnp.bfloat16)
    grad_b_second = jnp.sum(grad_out, axis=(0, 1))
    grad_w_second = jnp.einsum(
        "rpf,rpd->fd", activated, grad_low, preferred_element_type=jnp.float32
    )
    grad_act = jnp.einsum("rpd,fd->rpf", grad_low, w_second, preferred_element_type=jnp.float32)
    unused_value, gelu_back = jax.vjp(gelu_tanh, hidden_pre)
    grad_pre = gelu_back(grad_act)[0].astype(jnp.bfloat16)
    grad_b_first = jnp.sum(grad_pre, axis=(0, 1), dtype=jnp.float32)
    grad_w_first = jnp.einsum(
        "rpd,rpf->df", normed_two, grad_pre, preferred_element_type=jnp.float32
    )
    grad_normed_two = lax.psum(
        jnp.einsum("rpf,df->rpd", grad_pre, w_first, preferred_element_type=jnp.float32).astype(
            jnp.bfloat16
        ),
        "tp",
    ).astype(jnp.float32)
    unused_norm, second_back = jax.vjp(layer_norm, middle, ln_two)
    grad_middle_norm, grad_ln_two = second_back(grad_normed_two)
    grad_middle = grad_out + grad_middle_norm
    middle_low = grad_middle.astype(jnp.bfloat16)
    grad_w_proj = jnp.einsum(
        "rpe,rpd->ed", attended, middle_low, preferred_element_type=jnp.float32
    )
    grad_att = jnp.einsum("rpd,ed->rpe", middle_low, w_proj, preferred_element_type=jnp.float32)
    grad_att = grad_att.astype(jnp.bfloat16).reshape(row_count, pos_count, head_count, HDIM)
    grad_probs = jnp.einsum(
        "rqhd,rkhd->rhqk", grad_att, values_heads, preferred_element_type=jnp.float32
    )
    row_delta = jnp.sum(grad_probs * softmax_out, axis=-1, keepdims=True)
    grad_scores = (softmax_out * (grad_probs - row_delta)).astype(jnp.bfloat16)
    grad_queries = (
        jnp.einsum("rhqk,rkhd->rqhd", grad_scores, keys_heads, preferred_element_type=jnp.float32)
        * 0.125
    )
    full_len = keys_all.shape[1]
    part_keys = (
        jnp.einsum("rhqk,rqhd->rkhd", grad_scores, queries, preferred_element_type=jnp.float32)
        * 0.125
    )
    part_values = jnp.einsum(
        "rhqk,rqhd->rkhd", probs_low, grad_att, preferred_element_type=jnp.float32
    )
    grad_keys, grad_values = (
        lax.psum_scatter(
            part_keys.reshape(row_count, full_len, local_width).astype(jnp.bfloat16),
            "seq",
            scatter_dimension=1,
            tiled=True,
        ).astype(jnp.float32),
        lax.psum_scatter(
            part_values.reshape(row_count, full_len, local_width).astype(jnp.bfloat16),
            "seq",
            scatter_dimension=1,
            tiled=True,
        ).astype(jnp.float32),
    )
    grad_query_raw = rotate(grad_queries.astype(jnp.bfloat16), cosine, -sine_table)
    grad_key_raw = rotate(
        grad_keys.astype(jnp.bfloat16).reshape(row_count, pos_count, head_count, HDIM),
        cosine,
        -sine_table,
    )
    grad_mixed = jnp.stack(
        [
            grad_query_raw.reshape(row_count, pos_count, local_width).astype(jnp.bfloat16),
            grad_key_raw.reshape(row_count, pos_count, local_width).astype(jnp.bfloat16),
            grad_values.astype(jnp.bfloat16),
        ],
        axis=2,
    )
    grad_w_mix = jnp.einsum("rpd,rpcf->dcf", normed, grad_mixed, preferred_element_type=jnp.float32)
    grad_normed = lax.psum(
        jnp.einsum("rpcf,dcf->rpd", grad_mixed, w_mix, preferred_element_type=jnp.float32).astype(
            jnp.bfloat16
        ),
        "tp",
    ).astype(jnp.float32)
    unused_first, first_back = jax.vjp(layer_norm, inputs, ln_one)
    grad_in_norm, grad_ln_one = first_back(grad_normed)
    grad_inputs = grad_middle + grad_in_norm
    return (
        grad_inputs,
        (
            grad_ln_one,
            grad_w_mix,
            grad_w_proj,
            grad_ln_two,
            grad_w_first,
            grad_b_first,
            grad_w_second,
            grad_b_second,
        ),
    )


def pipelined(
    layer_input,
    cotangent,
    doc_lengths,
    ln1_gain,
    w_qkv,
    w_out,
    ln2_gain,
    w_up,
    b_up,
    w_down,
    b_down,
):
    weights = tuple(
        (weight[0] for weight in (ln1_gain, w_qkv, w_out, ln2_gain, w_up, b_up, w_down, b_down))
    )
    micros, row_count, pos_count, width_model = layer_input.shape
    sections = lax.axis_size("section")
    section_index = lax.axis_index("section")
    first_pos = lax.axis_index("seq") * pos_count
    query_pos = first_pos + jnp.arange(pos_count)
    cosine, sine_table = rotary_tables(query_pos)
    tables = (cosine, sine_table, query_pos)
    docs_every = document_ids(doc_lengths)
    kept_inputs = jnp.zeros((micros, row_count, pos_count, width_model), jnp.float32)
    kept_middle = jnp.zeros((micros, row_count, pos_count, width_model), jnp.float32)
    layer_out = jnp.zeros(layer_input.shape, jnp.bfloat16)
    arrived = jnp.zeros((row_count, pos_count, width_model), jnp.bfloat16)
    moments = micros + sections - 1
    for moment in range(moments):
        offset = moment - section_index
        micro_index = jnp.clip(offset, 0, micros - 1)
        is_active = (offset >= 0) & (offset < micros)
        own_input = layer_input[min(moment, micros - 1)]
        inputs = jnp.where(section_index == 0, own_input, arrived).astype(jnp.float32)
        result, middle, keys_all, values_all = forward_step(
            inputs, weights, tables, docs_every[micro_index]
        )
        kept_inputs = keep_slot(kept_inputs, inputs, micro_index, is_active)
        kept_middle = keep_slot(kept_middle, middle, micro_index, is_active)
        result_low = result.astype(jnp.bfloat16)
        layer_out = keep_slot(layer_out, result_low, micro_index, is_active)
        if moment < moments - 1:
            arrived = from_behind(result_low, "section", 1)
    grad_totals = tuple((jnp.zeros(weight.shape, jnp.float32) for weight in weights))
    input_grad = jnp.zeros(layer_input.shape, jnp.bfloat16)
    returned = jnp.zeros((row_count, pos_count, width_model), jnp.bfloat16)
    for moment in range(moments):
        offset = moment - (sections - 1 - section_index)
        micro_index = jnp.clip(offset, 0, micros - 1)
        is_active = (offset >= 0) & (offset < micros)
        incoming = jnp.where(
            section_index == sections - 1, cotangent[min(moment, micros - 1)], returned
        ).astype(jnp.float32)
        incoming = jnp.where(is_active, incoming, 0.0)
        grad_inputs, grad_parts = backward_step(
            kept_inputs[micro_index],
            kept_middle[micro_index],
            incoming,
            weights,
            tables,
            docs_every[micro_index],
        )
        grad_totals = tuple((total + piece for total, piece in zip(grad_totals, grad_parts)))
        grad_sent = grad_inputs.astype(jnp.bfloat16)
        input_grad = keep_slot(input_grad, grad_sent, micro_index, is_active)
        if moment < moments - 1:
            returned = from_behind(grad_sent, "section", -1)
    (
        grad_ln_one,
        grad_w_mix,
        grad_w_proj,
        grad_ln_two,
        grad_w_first,
        grad_b_first,
        grad_w_second,
        grad_b_second,
    ) = grad_totals
    summed = (
        lax.psum(grad_ln_one.astype(jnp.bfloat16), "seq").astype(jnp.float32),
        lax.psum(grad_w_mix.astype(jnp.bfloat16), "seq").astype(jnp.float32),
        lax.psum(grad_w_proj.astype(jnp.bfloat16), "seq").astype(jnp.float32),
        lax.psum(grad_ln_two.astype(jnp.bfloat16), "seq").astype(jnp.float32),
        lax.psum(grad_w_first.astype(jnp.bfloat16), "seq").astype(jnp.float32),
        lax.psum(grad_b_first.astype(jnp.bfloat16), "seq").astype(jnp.float32),
        lax.psum(grad_w_second.astype(jnp.bfloat16), "seq").astype(jnp.float32),
        lax.psum(grad_b_second.astype(jnp.bfloat16), "seq").astype(jnp.float32),
    )
    return (
        layer_out[None],
        input_grad[None],
        summed[0][None],
        summed[1][None],
        summed[2][None],
        summed[3][None],
        summed[4][None],
        summed[5][None],
        summed[6][None],
        summed[7][None],
    )


PIECE = 256
LANES = 256
MESH = pl.DeviceIdType.MESH
HBM = pl.BlockSpec(memory_space=pl.ANY)
VMEM = pl.BlockSpec(memory_space=pltpu.VMEM)


def dot_nn(left, right):
    return lax.dot_general(left, right, (((1,), (0,)), ((), ())), preferred_element_type=jnp.float32)


def dot_nt(left, right):
    return lax.dot_general(left, right, (((1,), (1,)), ((), ())), preferred_element_type=jnp.float32)


def dot_tn(left, right):
    return lax.dot_general(left, right, (((0,), (0,)), ((), ())), preferred_element_type=jnp.float32)


class Place:
    def __init__(self):
        self.s, self.t, self.z = (lax.axis_index(name) for name in ("section", "tp", "seq"))
        self.core = 1 - self.s
        self.half, self.group = self.z % 2, self.z // 2
        beside_x = self.t + 1 - 2 * (self.t % 2)
        beside_y = (self.t + 2) % 4
        self.beside_x, self.beside_y = beside_x, beside_y
        self.hop_one = beside_x * (1 - self.s) + beside_y * self.s
        self.hop_two = beside_y * (1 - self.s) + beside_x * self.s
        self.rel_one, self.rel_two = 1 + self.s, 2 - self.s
        self.far = (self.z + 2) % 4
        self.twin = self.z + 1 - 2 * self.half

    def on(self, section=None, tp=None, seq=None):
        return (
            self.s if section is None else section,
            self.t if tp is None else tp,
            self.z if seq is None else seq,
        )

    def partners(self):
        return [
            self.on(section=self.core),
            self.on(tp=self.beside_x),
            self.on(tp=self.beside_y),
            self.on(seq=self.far),
            self.on(seq=self.twin),
            self.on(seq=3 - self.z),
            self.on(section=self.core, seq=self.twin),
        ]

    def meet(self, partners):
        barrier = pltpu.get_barrier_semaphore()
        for partner in partners:
            pl.semaphore_signal(barrier, inc=1, device_id=partner, device_id_type=MESH)
        pl.semaphore_wait(barrier, len(partners))


def remote(source, target, send, receive, device):
    return pltpu.make_async_remote_copy(
        src_ref=source,
        dst_ref=target,
        send_sem=send,
        recv_sem=receive,
        device_id=device,
        device_id_type=MESH,
    )


def normalize(values):
    center = values - jnp.mean(values, axis=-1, keepdims=True)
    spread = jnp.mean(center * center, axis=-1, keepdims=True)
    scale = lax.rsqrt(spread + 1e-05)
    return center * scale, scale


def turn(values, cosine, sine_table):
    width = values.shape[-1]
    times = width // cosine.shape[-1]
    lane = lax.broadcasted_iota(jnp.int32, values.shape, 1) % HDIM
    ahead = pltpu.roll(values, width - HDIM // 2, 1)
    behind = pltpu.roll(values, HDIM // 2, 1)
    swapped = jnp.where(lane < HDIM // 2, ahead, behind)
    return values * jnp.tile(cosine, (1, times)) + swapped * jnp.tile(sine_table, (1, times))


def gelu(values):
    inner = 0.7978845608028654 * (values + 0.044715 * values * values * values)
    return 0.5 * values * (1.0 + jnp.tanh(inner))


def head_mask(head, scale):
    lane = lax.broadcasted_iota(jnp.int32, (1, LANES), 1)
    inside = (lane >= head * HDIM) & (lane < (head + 1) * HDIM)
    return jnp.where(inside, jnp.float32(scale), jnp.float32(0.0))


def attention_block(q_ref, keys, values_turned, bias, lse, turned):
    def head_scores(head):
        query = q_ref[...] * head_mask(head, 0.125).astype(jnp.bfloat16)
        return dot_nt(keys[...], query) + bias[...]

    def head_rest(head, scores):
        rows = pl.ds(pl.multiple_of(head * HDIM, HDIM), HDIM)
        top = jnp.max(scores, axis=0, keepdims=True)
        raised = jnp.exp(scores - top)
        total = jnp.sum(raised, axis=0, keepdims=True)
        lse[pl.ds(head, 1), :] = top + jnp.log(total)
        turned[rows, :] = dot_nn(values_turned[rows, :], raised.astype(jnp.bfloat16)) * (1.0 / total)

    def one(pair, _):
        left, right = head_scores(2 * pair), head_scores(2 * pair + 1)
        head_rest(2 * pair, left)
        head_rest(2 * pair + 1, right)
        return 0

    lax.fori_loop(0, LANES // HDIM // 2, one, 0)
    return turned[...].T.astype(jnp.bfloat16)


def fill_bias(bias, lengths, row, block):
    ends, total = [], 0
    for i in range(lengths.shape[1]):
        total = total + lengths[row, i]
        ends.append(total)

    def docs_of(base):
        return sum((base >= end).astype(jnp.int32) for end in ends)

    shape = (PIECE, bias.shape[1])
    lane = lax.broadcasted_iota(jnp.int32, shape, 1)
    query_noisy = lane < PIECE
    query_base = block * PIECE + lane - jnp.where(query_noisy, 0, PIECE)
    query_doc, query_block = docs_of(query_base), query_base >> 4
    for i in range(4):
        start = (block - 2 + min(i, 2)) * PIECE
        key_base = start + lax.broadcasted_iota(jnp.int32, shape, 0)
        key_block = key_base >> 4
        if i == 3:
            allow = query_noisy & (key_block == query_block)
        else:
            later = jnp.where(query_noisy, key_block + 1, key_block)
            allow = (later <= query_block) & (key_base >= 0)
        allow = allow & (docs_of(key_base) == query_doc)
        bias[i * PIECE : (i + 1) * PIECE, :] = jnp.where(allow, 0.0, -1e30)


class Spread:
    def __init__(self, place, source, stage, layer, out, sems):
        self.place, self.source, self.stage = place, source, stage
        self.layer, self.out = layer, out
        self.local, self.swap_send, self.swap_recv, self.hop_send, self.hop_recv = sems[:5]
        self.end_local, self.end_send, self.end_recv = sems[5:]
        self.groups = (place.group, 1 - place.group)

    def entry(self):
        place = self.place
        kept = self.source.at[pl.ds(pl.multiple_of(place.group * PIECE, PIECE), PIECE)]
        sent = self.source.at[pl.ds(pl.multiple_of((1 - place.group) * PIECE, PIECE), PIECE)]
        target = self.stage.at[0, place.group]
        here = pltpu.make_async_copy(kept, target, self.local)
        there = remote(sent, target, self.swap_send, self.swap_recv, place.on(seq=place.far))
        return here, there

    def take(self):
        self.entry()[0].start()

    def swap(self):
        self.entry()[1].start()

    def moves(self, half):
        place, group = self.place, self.groups[half]
        own = self.stage.at[0, group]
        first = self.stage.at[place.rel_one, group]
        second = self.stage.at[place.rel_two, group]
        third = self.stage.at[3, group]
        listed = (
            (own, first, place.hop_one),
            (own, second, place.hop_two),
            (first, third, place.hop_two),
        )
        return [
            remote(
                source,
                target,
                self.hop_send.at[half, i],
                self.hop_recv.at[half, i],
                place.on(tp=column),
            )
            for i, (source, target, column) in enumerate(listed)
        ]

    def hops(self, half):
        here, there = self.entry()
        if half == 0:
            here.wait()
        else:
            there.wait_recv()
        first, second, _ = self.moves(half)
        first.start()
        second.start()
        self.put(half, 0)

    def forward(self, half):
        first, _, third = self.moves(half)
        first.wait_recv()
        third.start()
        self.put(half, 1)

    def finish(self, half):
        _, second, third = self.moves(half)
        second.wait_recv()
        self.put(half, 2)
        third.wait_recv()
        self.put(half, 3)

    def ends(self, half, step):
        place, group = self.place, self.groups[half]
        rows = pl.ds(pl.multiple_of(place.s * PIECE, PIECE), PIECE)
        rel = (0, place.rel_one, place.rel_two, 3)[step]
        column = (place.t, place.hop_one, place.hop_two, 3 - place.t)[step]
        source, target = self.stage.at[rel, group], self.out.at[group, column, rows]
        here = pltpu.make_async_copy(source, target, self.end_local.at[half, step])
        there = remote(
            source,
            target,
            self.end_send.at[half, step],
            self.end_recv.at[half, step],
            place.on(section=place.core),
        )
        return here, there

    def put(self, half, step):
        @pl.when(self.place.s == self.layer)
        def _():
            self.ends(half, step)[0].start()

        @pl.when(self.place.s != self.layer)
        def _():
            self.ends(half, step)[1].start()

    def drain(self):
        self.entry()[1].wait_send()
        for half in range(2):
            for copy in self.moves(half):
                copy.wait_send()

        @pl.when(self.place.s == self.layer)
        def _():
            for half in range(2):
                for step in range(4):
                    here, there = self.ends(half, step)
                    here.wait()
                    there.wait_recv()

        @pl.when(self.place.s != self.layer)
        def _():
            for half in range(2):
                for step in range(4):
                    self.ends(half, step)[1].wait_send()


def spread_sems():
    dma = pltpu.SemaphoreType.DMA
    return [dma, dma, dma, dma((2, 3)), dma((2, 3)), dma((2, 4)), dma((2, 4)), dma((2, 4))]


class Weights:
    def __init__(self, place, own, full, sems):
        self.place, self.own, self.full = place, own, full
        (
            self.local,
            self.own_send,
            self.own_recv,
            self.hop_send,
            self.hop_recv,
            self.chip_send,
            self.chip_recv,
        ) = sems

    def source(self, chunk, pack):
        if chunk == 0:
            return self.own[0].at[pack]
        if chunk == 3:
            return self.own[2].at[pack]
        return self.own[1].at[pack, chunk - 1]

    def piece(self, layer, chunk, pack, rel):
        if chunk == 0:
            return self.full[0].at[layer, pack, :, pl.ds(pl.multiple_of(rel * 192, 64), 192)]
        if chunk == 3:
            return self.full[2].at[layer, pack, rel]
        return self.full[1].at[layer, pack, rel * 2 + chunk - 1]

    def own_copies(self, chunk, pack):
        s = self.place.s
        here = pltpu.make_async_copy(
            self.source(chunk, pack), self.piece(s, chunk, pack, 0), self.local.at[chunk, pack]
        )
        there = remote(
            self.source(chunk, pack),
            self.piece(s, chunk, pack, 0),
            self.own_send.at[chunk, pack],
            self.own_recv.at[chunk, pack],
            self.place.on(section=self.place.core),
        )
        return here, there

    def start_own(self, chunk):
        for pack in (self.place.core, self.place.s):
            for copy in self.own_copies(chunk, pack)[::-1]:
                copy.start()

    def wait_own(self, layer, chunk, pack):
        here, there = self.own_copies(chunk, pack)

        @pl.when(self.place.s == layer)
        def _():
            here.wait()

        @pl.when(self.place.s != layer)
        def _():
            there.wait_recv()

    def hops(self, layer, chunk):
        place = self.place
        own = self.piece(layer, chunk, place.s, 0)
        first = self.piece(layer, chunk, place.s, place.rel_one)
        second = self.piece(layer, chunk, place.s, place.rel_two)
        third = self.piece(layer, chunk, place.s, 3)
        moves = ((own, first, place.hop_one), (own, second, place.hop_two), (first, third, place.hop_two))
        return [
            remote(
                source,
                target,
                self.hop_send.at[layer, chunk, i],
                self.hop_recv.at[layer, chunk, i],
                place.on(tp=column),
            )
            for i, (source, target, column) in enumerate(moves)
        ]

    def chips(self, layer, chunk):
        place = self.place
        return [
            remote(
                self.piece(layer, chunk, place.s, rel),
                self.piece(layer, chunk, place.s, rel),
                self.chip_send.at[layer, chunk, i],
                self.chip_recv.at[layer, chunk, i],
                place.on(section=place.core),
            )
            for i, rel in enumerate((place.rel_one, place.rel_two, 3))
        ]

    def begin(self, layer, chunk):
        self.wait_own(layer, chunk, self.place.s)
        first, second, _ = self.hops(layer, chunk)
        first.start()
        second.start()

    def forward(self, layer, chunk):
        first, second, third = self.hops(layer, chunk)
        chips = self.chips(layer, chunk)
        first.wait_recv()
        third.start()
        chips[0].start()
        second.wait_recv()
        chips[1].start()

    def finish(self, layer, chunk):
        self.hops(layer, chunk)[2].wait_recv()
        self.chips(layer, chunk)[2].start()

    def need(self, layer, chunk):
        if chunk < 3:
            self.wait_own(layer, chunk, self.place.core)
        for copy in self.chips(layer, chunk):
            copy.wait_recv()

    def drain(self):
        for chunk in range(4):
            for pack in range(2):
                self.own_copies(chunk, pack)[1].wait_send()
            for layer in range(2):
                for copy in self.hops(layer, chunk) + self.chips(layer, chunk):
                    copy.wait_send()


class KeyShare:
    def __init__(self, place, kv, layer, sems):
        self.place, self.kv, self.layer = place, kv, layer
        self.near_send, self.near_recv, self.far_send, self.far_recv = sems
        s, odd = place.s, place.half == 1
        self.sends_near = (s == 0) | ~odd
        self.sends_far = (s == 0) & ~odd
        self.passes = (s == 0) & odd
        self.gets_near = (s == 1) | odd
        self.gets_far = odd

    def rows(self, start, part):
        lanes = pl.ds(part * LANES, LANES)
        return self.kv.at[self.layer, :, pl.ds(start, PIECE), lanes]

    def near(self, part):
        place = self.place
        return remote(
            self.rows(2 * PIECE, part),
            self.rows(PIECE, part),
            self.near_send.at[self.layer, part],
            self.near_recv.at[self.layer, part],
            place.on(section=place.core, seq=place.z + place.s * (1 - place.half)),
        )

    def far(self, part):
        place = self.place
        return remote(
            self.rows(2 * PIECE, part),
            self.rows(0, part),
            self.far_send.at[self.layer, part],
            self.far_recv.at[self.layer, part],
            place.on(seq=place.twin),
        )

    def last(self, part):
        place = self.place
        return remote(
            self.rows(PIECE, part),
            self.rows(0, part),
            self.far_send.at[self.layer, part],
            self.far_recv.at[self.layer, part],
            place.on(section=place.core),
        )

    def start(self, part):
        @pl.when(self.sends_near)
        def _():
            self.near(part).start()

        @pl.when(self.sends_far)
        def _():
            self.far(part).start()

    def arrive(self, part):
        @pl.when(self.gets_near)
        def _():
            self.near(part).wait_recv()

        @pl.when(self.passes)
        def _():
            self.last(part).start()

        @pl.when(self.gets_far)
        def _():
            self.far(part).wait_recv()

    def drain(self):
        for part in range(3):

            @pl.when(self.sends_near)
            def _():
                self.near(part).wait_send()

            @pl.when(self.sends_far)
            def _():
                self.far(part).wait_send()

            @pl.when(self.passes)
            def _():
                self.last(part).wait_send()


def forward_kernel(
    tokens,
    cotangent,
    own_a,
    own_b,
    own_c,
    lengths,
    cosine,
    sine_table,
    full_a_out,
    full_b_out,
    gains_out,
    seeded_out,
    x_out,
    low_out,
    q_out,
    kv_out,
    att_out,
    mid_out,
    hid_out,
    lse_out,
    bias_out,
    out,
    full_a,
    full_b,
    full_c,
    low,
    x,
    normed,
    q,
    kv,
    att,
    mid,
    hid,
    lse,
    values_turned,
    turned_att,
    bias,
    bias_low,
    stage,
    *sems,
):
    weight_sems, key_sems = sems[:7], sems[7:11]
    token_sem, swap_send, swap_recv, seed_sem, seed_send, seed_recv, save_sem = sems[11:18]
    place = Place()
    zero = Spread(place, low_out.at[0], stage, 0, out, sems[18:])
    weights = Weights(place, (own_a, own_b, own_c), (full_a, full_b, full_c), weight_sems)
    lse[...] = jnp.zeros_like(lse)
    kv[:, :, : 2 * PIECE, :] = jnp.zeros((2, 2, 2 * PIECE, kv.shape[-1]), jnp.bfloat16)
    place.meet(place.partners())
    group_rows = pl.ds(pl.multiple_of(place.group * PIECE, PIECE), PIECE)
    columns = pl.ds(pl.multiple_of(place.s * PIECE, PIECE), PIECE)

    def bring(whole, target, here, send, receive):
        kept = whole.at[4 * place.group + place.t, columns]
        sent = whole.at[4 * (1 - place.group) + place.t, columns]
        target = target.at[group_rows]
        return (
            pltpu.make_async_copy(kept, target, here),
            remote(sent, target, send, receive, place.on(seq=place.far)),
        )

    own_tokens, swap = bring(tokens, low, token_sem, swap_send, swap_recv)
    own_seed, seed_swap = bring(cotangent, seeded_out, seed_sem, seed_send, seed_recv)
    own_tokens.start()
    swap.start()
    weights.start_own(0)
    weights.begin(0, 0)
    weights.start_own(3)
    weights.start_own(1)
    for layer in range(2):
        weights.begin(layer, 3)
        weights.wait_own(layer, 3, place.core)
    gains = full_c.at[:, 0, 0]
    gains_out[...] = full_c[:, 0, 0]
    fill_bias(bias, lengths, 4 * place.group + place.t, 2 * place.half + place.s)
    bias_low[...] = bias[...].astype(jnp.bfloat16)
    bias_save = pltpu.make_async_copy(bias_low, bias_out, save_sem.at[17])
    bias_save.start()
    weights.forward(0, 0)
    own_tokens.wait()
    swap.wait()
    x_save = pltpu.make_async_copy(low, x_out, save_sem.at[16])
    x_save.start()
    x[...] = low[...].astype(jnp.float32)

    def saves(layer):
        pairs = [
            (low, low_out.at[layer]),
            (q, q_out.at[layer]),
            (kv.at[layer], kv_out.at[layer]),
            (att, att_out.at[layer]),
            (mid, mid_out.at[layer]),
            (hid, hid_out.at[layer]),
            (lse, lse_out.at[layer]),
        ]
        return [pltpu.make_async_copy(a, b, save_sem.at[i]) for i, (a, b) in enumerate(pairs)]

    def weight_saves(layer):
        copies = []
        for i, (a, b) in enumerate(((full_a, full_a_out), (full_b, full_b_out))):
            for pack in range(2):
                sem = save_sem.at[8 + 4 * layer + 2 * i + pack]
                copies.append(pltpu.make_async_copy(a.at[layer, pack], b.at[layer, pack], sem))
        return copies

    for layer in range(2):
        share = KeyShare(place, kv, layer, key_sems)
        unit, _ = normalize(x[...])
        normed[...] = (unit * gains[layer, 0:1]).astype(jnp.bfloat16)
        if layer == 0:
            weights.finish(0, 0)
            weights.begin(0, 1)
            weights.start_own(2)
        else:
            weights.finish(1, 0)
            weights.begin(1, 2)
            zero.hops(0)
            for copy in saves(0)[1:]:
                copy.wait()
        weights.need(layer, 0)
        for copy in weight_saves(layer)[:2]:
            copy.start()
        for part in range(3):
            lanes = pl.ds(part * LANES, LANES)
            keep = normed[...]
            mixed = dot_nt(keep, full_a[layer, 0, 0, lanes, :])
            q[:, lanes] = turn(mixed, cosine[...], sine_table[...]).astype(jnp.bfloat16)
            mixed = dot_nt(keep, full_a[layer, 0, 1, lanes, :])
            mixed = turn(mixed, cosine[...], sine_table[...]).astype(jnp.bfloat16)
            kv[layer, 0, 2 * PIECE : 3 * PIECE, lanes] = mixed[PIECE:]
            kv[layer, 0, 3 * PIECE :, lanes] = mixed[:PIECE]
            mixed = dot_nt(keep, full_a[layer, 1, 0, lanes, :]).astype(jnp.bfloat16)
            kv[layer, 1, 2 * PIECE : 3 * PIECE, lanes] = mixed[PIECE:]
            kv[layer, 1, 3 * PIECE :, lanes] = mixed[:PIECE]
            share.start(part)
        if layer == 0:
            weights.forward(0, 3)
            weights.forward(1, 3)
            weights.finish(0, 3)
            weights.finish(1, 3)
            own_seed.start()
            weights.begin(0, 2)
        else:
            weights.forward(1, 1)
            zero.hops(1)
        for part in range(3):
            lanes = pl.ds(part * LANES, LANES)
            share.arrive(part)
            values_turned[...] = kv[layer, 1, :, lanes].astype(jnp.float32).T.astype(jnp.bfloat16)
            for start, count in ((0, 4 * PIECE), (PIECE, 3 * PIECE)):
                queries = pl.ds(start, PIECE)
                att[queries, lanes] = attention_block(
                    q.at[queries, lanes],
                    kv.at[layer, 0, :count, lanes],
                    values_turned.at[:, :count],
                    bias.at[:count, queries],
                    lse.at[pl.ds(8 * part, 8), queries],
                    turned_att,
                )
            if part == 2 and layer == 0:
                seed_swap.start()
            if layer == 0:
                if part == 0:
                    weights.forward(0, 1)
                elif part == 1:
                    weights.finish(0, 1)
                    weights.begin(1, 0)
                else:
                    weights.forward(0, 2)
            else:
                if part == 0:
                    zero.forward(0)
                elif part == 1:
                    weights.finish(1, 1)
                    zero.forward(1)
                else:
                    weights.forward(1, 2)
                    zero.finish(0)
        for copy in saves(layer)[1:4] + saves(layer)[6:]:
            copy.start()

        def project(part, _):
            lanes = pl.ds(pl.multiple_of(part * LANES, LANES), LANES)
            mid[:, lanes] = x[:, lanes] + dot_nn(att[...], full_a[layer, 1, 1, :, lanes])
            return 0

        lax.fori_loop(0, 3, project, 0)
        unit, _ = normalize(mid[...])
        normed[...] = (unit * gains[layer, 1:2]).astype(jnp.bfloat16)
        x[...] = mid[...] + gains[layer, 2:3]
        saves(layer)[4].start()
        weights.need(layer, 3)
        for part in range(2):
            if part == 1:
                weights.finish(layer, 2)
                if layer == 0:
                    weights.begin(1, 1)
                else:
                    zero.finish(1)
            weights.need(layer, part + 1)
            if part == 1:
                for copy in weight_saves(layer)[2:]:
                    copy.start()

            def feed(rel, _):
                start = pl.multiple_of(rel * 768 + part * 384, 128)
                units = pl.ds(start, 384)
                shift = full_c[layer, 1, rel, 0:1, pl.ds(part * 384, 384)]
                tile = rel * 2 + part
                pre = dot_nn(normed[...], full_b[layer, 0, tile]) + shift
                hid[:, units] = pre.astype(jnp.bfloat16)
                active = gelu(pre).astype(jnp.bfloat16)
                x[...] += dot_nt(active, full_b[layer, 1, tile])
                return 0

            lax.fori_loop(0, 4, feed, 0)
        saves(layer)[5].start()
        if layer == 0:
            x_save.wait()
        low[...] = x[...].astype(jnp.bfloat16)
        saves(layer)[0].start()
        x[...] = low[...].astype(jnp.float32)
        if layer == 0:
            saves(0)[0].wait()
            zero.take()
            zero.swap()
            weights.forward(1, 0)
    for copy in saves(1):
        copy.wait()
    for layer in range(2):
        for copy in weight_saves(layer):
            copy.wait()
        KeyShare(place, kv, layer, key_sems).drain()
    weights.drain()
    zero.drain()
    bias_save.wait()
    own_seed.wait()
    seed_swap.wait()


def run_forward(tokens, cotangent, own_a, own_b, own_c, lengths, cosine, sine_table):
    shape = jax.ShapeDtypeStruct
    low_type, full_type = jnp.bfloat16, jnp.float32
    count = 2 * PIECE
    width = tokens.shape[-1]
    units = 8 * own_b.shape[-1]
    dma = pltpu.SemaphoreType.DMA
    return pl.pallas_call(
        forward_kernel,
        name="forward_layers",
        out_shape=[
            shape((2, 2, 2, width, width), low_type),
            shape((2, 2, 8, width, units // 8), low_type),
            shape((2, 8, width), full_type),
            shape((count, width), low_type),
            shape((count, width), low_type),
            shape((2, count, width), low_type),
            shape((2, count, width), low_type),
            shape((2, 2, 4 * PIECE, width), low_type),
            shape((2, count, width), low_type),
            shape((2, count, width), full_type),
            shape((2, count, units), low_type),
            shape((2, 24, count), full_type),
            shape((4 * PIECE, count), low_type),
            shape((2, 4, count, width), low_type),
        ],
        in_specs=[HBM] * 5 + [pl.BlockSpec(memory_space=pltpu.SMEM)] + [VMEM] * 2,
        out_specs=[HBM] * 2 + [VMEM] + [HBM] * 11,
        scratch_shapes=[
            pltpu.VMEM((2, 2, 2, width, width), low_type),
            pltpu.VMEM((2, 2, 8, width, units // 8), low_type),
            pltpu.VMEM((2, 2, 4, 8, width), full_type),
            pltpu.VMEM((count, width), low_type),
            pltpu.VMEM((count, width), full_type),
            pltpu.VMEM((count, width), low_type),
            pltpu.VMEM((count, width), low_type),
            pltpu.VMEM((2, 2, 4 * PIECE, width), low_type),
            pltpu.VMEM((count, width), low_type),
            pltpu.VMEM((count, width), full_type),
            pltpu.VMEM((count, units), low_type),
            pltpu.VMEM((24, count), full_type),
            pltpu.VMEM((LANES, 4 * PIECE), low_type),
            pltpu.VMEM((LANES, PIECE), full_type),
            pltpu.VMEM((4 * PIECE, count), full_type),
            pltpu.VMEM((4 * PIECE, count), low_type),
            pltpu.VMEM((4, 2, PIECE, width), low_type),
            dma((4, 2)),
            dma((4, 2)),
            dma((4, 2)),
            dma((2, 4, 3)),
            dma((2, 4, 3)),
            dma((2, 4, 3)),
            dma((2, 4, 3)),
            dma((2, 3)),
            dma((2, 3)),
            dma((2, 3)),
            dma((2, 3)),
            dma,
            dma,
            dma,
            dma,
            dma,
            dma,
            dma((18,)),
            *spread_sems(),
        ],
        compiler_params=pltpu.CompilerParams(
            collective_id=1, has_side_effects=True, vmem_limit_bytes=62 * 1024 * 1024
        ),
        cost_estimate=pl.CostEstimate(
            flops=30_000_000_000, bytes_accessed=80_000_000, transcendentals=20_000_000
        ),
    )(tokens, cotangent, own_a, own_b, own_c, lengths, cosine, sine_table)


def low_sum(*parts):
    total = parts[0].astype(jnp.float32)
    for part in parts[1:]:
        total = total + part.astype(jnp.float32)
    return total.astype(jnp.bfloat16)


class Sum:
    def __init__(self, place, source, total, buffers, sems, loaded=False, opens=None, waits=None, slim=False):
        self.place, self.source, self.total = place, source, total
        self.inbox, self.hop_in, self.line_in = buffers
        self.loaded, self.opens, self.waits = loaded, opens, waits
        self.slim = slim
        (
            self.mine_sem,
            self.chip_send,
            self.chip_recv,
            self.hop_send,
            self.hop_recv,
            self.line_send,
            self.line_recv,
            self.end_local,
            self.end_send,
            self.end_recv,
        ) = sems
        z = place.z
        self.outer = (z == 0) | (z == 3)
        self.inner = (z == 1) | (z == 2)
        self.order = (3, 1, 2, 0)

    def mine(self, rel):
        return pltpu.make_async_copy(
            self.source(self.place.s, rel), self.total(rel), self.mine_sem.at[rel]
        )

    def other(self, rel):
        return remote(
            self.source(self.place.core, rel),
            self.inbox.at[rel],
            self.chip_send.at[rel],
            self.chip_recv.at[rel],
            self.place.on(section=self.place.core),
        )

    def start(self):
        if self.waits is not None:
            pl.semaphore_wait(self.waits, 1)
        for rel in self.order:
            if self.inbox is not None:
                self.other(rel).start()
            if self.loaded:
                self.mine(rel).start()

    def load(self, travels=True):
        for rel in self.order:
            if self.loaded:
                self.mine(rel).wait()
            if self.inbox is not None:
                self.other(rel).wait_recv()
                total = self.total(rel)
                total[...] = low_sum(total[...], self.inbox[rel])
            if travels and rel == 3:
                self.moves()[0].start()
            elif travels and rel == 2:
                self.moves()[1].start()
        if self.opens is not None:
            pl.semaphore_signal(
                self.opens,
                inc=1,
                device_id=self.place.on(section=self.place.core),
                device_id_type=MESH,
            )

    def moves(self):
        place = self.place
        listed = (
            (3, 0, place.hop_two),
            (place.rel_two, 1, place.hop_two),
            (place.rel_one, 2, place.hop_one),
        )
        return [
            remote(
                self.total(rel),
                self.hop_in.at[slot],
                self.hop_send.at[slot],
                self.hop_recv.at[slot],
                place.on(tp=column),
            )
            for rel, slot, column in listed
        ]

    def middle(self):
        first, _, third = self.moves()
        first.wait_recv()
        total = self.total(self.place.rel_one)
        total[...] = low_sum(total[...], self.hop_in[0])
        third.start()

    def line_slots(self):
        if self.slim:
            return self.total(1), self.line_in.at[0]
        return self.line_in.at[0], self.line_in.at[1]

    def lines(self):
        place = self.place
        own, line_sum = self.total(0), self.total(1)
        first, second = self.line_slots()
        listed = (
            (own, first, place.twin),
            (own, second, 3 - place.z),
            (line_sum, line_sum, place.twin),
        )
        return [
            remote(
                source,
                target,
                self.line_send.at[i],
                self.line_recv.at[i],
                place.on(seq=plane),
            )
            for i, (source, target, plane) in enumerate(listed)
        ]

    def gather(self, save=None):
        _, second, third = self.moves()
        second.wait_recv()
        third.wait_recv()
        total = self.total(0)
        total[...] = low_sum(total[...], self.hop_in[1], self.hop_in[2])
        second.wait_send()
        third.wait_send()
        if save is not None:
            save.start()
        else:
            self.enter_line()

    def resume(self, saved):
        saved.wait()
        self.enter_line()

    def enter_line(self):
        @pl.when(self.outer)
        def _():
            self.lines()[0].start()

    def line_one(self):
        @pl.when(self.inner)
        def _():
            self.lines()[0].wait_recv()
            total = self.total(0)
            total[...] = low_sum(total[...], self.line_slots()[0][...])
            self.lines()[1].start()

    def line_two(self):
        @pl.when(self.inner)
        def _():
            self.lines()[1].wait_recv()
            self.total(1)[...] = low_sum(self.total(0)[...], self.line_slots()[1][...])
            self.lines()[2].start()

    def line_three(self):
        @pl.when(self.outer)
        def _():
            self.lines()[2].wait_recv()

    def ends(self, target):
        here = pltpu.make_async_copy(self.total(1), target, self.end_local)
        there = remote(
            self.total(1),
            target,
            self.end_send,
            self.end_recv,
            self.place.on(section=self.place.core),
        )
        return here, there

    def store(self, save):
        self.line_three()
        save.start()

    def finish(self, layer, target):
        self.line_three()
        here, there = self.ends(target)

        @pl.when(self.place.s == layer)
        def _():
            here.start()

        @pl.when(self.place.s != layer)
        def _():
            there.start()

    def drain_exchange(self):
        if self.inbox is not None:
            for rel in range(4):
                self.other(rel).wait_send()

    def drain_end(self, layer, target):
        here, there = self.ends(target)

        @pl.when(self.place.s == layer)
        def _():
            here.wait()
            there.wait_recv()

        @pl.when(self.place.s != layer)
        def _():
            there.wait_send()

    def drain_plane(self):
        self.drain_exchange()
        self.moves()[0].wait_send()

    def drain_line(self):
        @pl.when(self.outer)
        def _():
            self.lines()[0].wait_send()

        @pl.when(self.inner)
        def _():
            self.lines()[1].wait_send()
            self.lines()[2].wait_send()


def sum_sems():
    dma = pltpu.SemaphoreType.DMA
    return [dma((4,))] * 3 + [dma((3,))] * 4 + [dma] * 3


SUM_SEMS = 10


def sum_buffers(piece, counts):
    return [pltpu.VMEM((count,) + piece, jnp.bfloat16) for count in counts]


def attention_sums(place, grads, buffers, sems, gate=None):
    sums = []
    for i in range(2):
        total, inbox, hop_in, line_in = buffers[4 * i : 4 * i + 4]
        gates = {}
        if gate is not None:
            inbox = buffers[1]
            gates = {"opens": gate} if i == 0 else {"waits": gate}

        def source(pack, rel, i=i):
            return grads.at[pack, i, rel]

        def kept(rel, total=total):
            return total.at[rel]

        own_sems = sems[SUM_SEMS * i : SUM_SEMS * (i + 1)]
        sums.append(Sum(place, source, kept, (inbox, hop_in, line_in), own_sems, loaded=True, **gates))
    return sums


def feed_sums(place, wb, buffers, sems, gate):
    inbox, sums = buffers[0], []
    for i in range(2):

        def source(pack, rel, i=i):
            return wb.at[pack, rel * 2 + i]

        def kept(rel, i=i):
            return wb.at[place.s, rel * 2 + i]

        own_sems = sems[SUM_SEMS * i : SUM_SEMS * (i + 1)]
        gates = {"opens": gate} if i == 0 else {"waits": gate}
        at = min(i, buffers[1].shape[0] - 1)
        sums.append(Sum(place, source, kept, (inbox, buffers[1].at[at], None), own_sems, **gates))
    return sums


def feed_buffers(piece, count):
    kind = jnp.bfloat16
    return [pltpu.VMEM((4,) + piece, kind), pltpu.VMEM((count, 3) + piece, kind)]


def line_sum(place, total, line_in, sems):
    return Sum(place, None, lambda rel: total.at[rel], (None, None, line_in), sems, slim=True)


class KeyReturn:
    def __init__(self, place, kv, near_in, far_in, sems):
        self.place, self.kv = place, kv
        self.near_in, self.far_in, self.pass_in = near_in, far_in, far_in
        (
            self.near_send,
            self.near_recv,
            self.far_send,
            self.far_recv,
            self.pass_send,
            self.pass_recv,
        ) = sems
        s, odd = place.s, place.half == 1
        self.is_third = (s == 0) & odd
        self.is_fourth = (s == 1) & odd
        self.is_second = (s == 1) & ~odd
        self.is_first = (s == 0) & ~odd

    def sources(self, start, part):
        return self.kv.at[:, pl.ds(start, PIECE), pl.ds(part * LANES, LANES)]

    def copies(self, part):
        place = self.place
        lanes = pl.ds(part * LANES, LANES)
        near = remote(
            self.sources(PIECE, part),
            self.near_in.at[:, :, lanes],
            self.near_send.at[part],
            self.near_recv.at[part],
            place.on(section=place.core, seq=place.z - (1 - place.s) * place.half),
        )
        far = remote(
            self.sources(0, part),
            self.far_in.at[:, :, lanes],
            self.far_send.at[part],
            self.far_recv.at[part],
            place.on(seq=place.twin),
        )
        passed = remote(
            self.sources(0, part),
            self.pass_in.at[:, :, lanes],
            self.pass_send.at[part],
            self.pass_recv.at[part],
            place.on(section=place.core),
        )
        return near, far, passed

    def start(self, part):
        near, far, passed = self.copies(part)

        @pl.when(self.is_fourth)
        def _():
            passed.start()
            near.start()

        @pl.when(self.is_second)
        def _():
            near.start()

        @pl.when(self.is_third)
        def _():
            far.start()

    def relay(self, part):
        near, _, passed = self.copies(part)
        lanes = pl.ds(part * LANES, LANES)

        @pl.when(self.is_third)
        def _():
            passed.wait_recv()
            self.kv[:, PIECE : 2 * PIECE, lanes] = low_sum(
                self.kv[:, PIECE : 2 * PIECE, lanes], self.pass_in[:, :, lanes]
            )
            near.start()

    def collect(self, part):
        near, far, _ = self.copies(part)
        lanes = pl.ds(part * LANES, LANES)
        clean = pl.ds(2 * PIECE, PIECE)

        @pl.when(~self.is_fourth)
        def _():
            near.wait_recv()
            self.kv[:, clean, lanes] = low_sum(self.kv[:, clean, lanes], self.near_in[:, :, lanes])

        @pl.when(self.is_first)
        def _():
            far.wait_recv()
            self.kv[:, clean, lanes] = low_sum(self.kv[:, clean, lanes], self.far_in[:, :, lanes])

    def drain(self):
        for part in range(3):
            near, far, passed = self.copies(part)

            @pl.when(self.is_fourth)
            def _():
                passed.wait_send()
                near.wait_send()

            @pl.when(self.is_second)
            def _():
                near.wait_send()

            @pl.when(self.is_third)
            def _():
                far.wait_send()
                near.wait_send()


def normalize_back(grads, unit, scale, gain):
    lifted = grads * gain
    mean = jnp.mean(lifted, axis=-1, keepdims=True)
    along = jnp.mean(lifted * unit, axis=-1, keepdims=True)
    return scale * (lifted - mean - unit * along)


def attention_back(q_ref, grad_ref, att_ref, keys, values, keys_turned, bias, lse, sums, turned, count):
    turned[...] = (grad_ref[...].astype(jnp.float32) * att_ref[...].astype(jnp.float32)).T

    def one(head, _):
        rows = pl.ds(pl.multiple_of(head * HDIM, HDIM), HDIM)
        query = q_ref[...] * head_mask(head, 0.125).astype(jnp.bfloat16)
        grad = grad_ref[...] * head_mask(head, 1.0).astype(jnp.bfloat16)
        delta = jnp.sum(turned[rows, :], axis=0, keepdims=True)
        scores = dot_nt(keys[...], query) + bias[...].astype(jnp.float32)
        probs = jnp.exp(scores - lse[pl.ds(head, 1), :])
        grad_scores = (probs * (dot_nt(values[...], grad) - delta)).astype(jnp.bfloat16)
        sums[0, :count] += dot_nn(grad_scores, query)
        sums[1, :count] += dot_nn(probs.astype(jnp.bfloat16), grad)
        turned[rows, :] = dot_nn(keys_turned[rows, :], grad_scores) * 0.125
        return 0

    lax.fori_loop(0, LANES // HDIM, one, 0)
    q_ref[...] = turned[...].T.astype(jnp.bfloat16)


def backward_layer(layer, refs, place, tick, key_sems, sems, tile_sems):
    (
        full_a,
        full_b,
        grad_in,
        x_in,
        q_in,
        kv_in,
        att_in,
        mid_in,
        hid_in,
        lse_in,
        bias_in,
        gains,
        cosine,
        sine_table,
        grads_a,
        grad_out,
        small_out,
        wa,
        wb,
        q,
        kv,
        att,
        mid,
        hid,
        grad,
        gathered,
        grad_low,
        grad_att,
        near_in,
        far_in,
        sums,
        keys_turned,
        turned_q,
        grad_turned,
        normed_turned,
        lse,
        bias,
    ) = refs
    share = KeyReturn(place, kv, near_in, far_in, key_sems)
    pairs = [
        (grad_in, grad_low),
        (mid_in.at[layer], mid),
        (hid_in.at[layer], hid),
        (full_a.at[layer], wa),
        (att_in.at[layer], att),
        (q_in.at[layer], q),
        (kv_in.at[layer], kv),
        (lse_in.at[layer], lse),
        (bias_in, bias),
    ]
    loads = [pltpu.make_async_copy(a, b, sems.at[i]) for i, (a, b) in enumerate(pairs)]
    def tile_copy(pack, tile):
        return pltpu.make_async_copy(
            full_b.at[layer, pack, tile], wb.at[pack, tile], tile_sems.at[pack, tile]
        )

    for copy in loads[:3]:
        copy.start()
    for part in range(2):
        for rel in range(4):
            for pack in (1, 0):
                tile_copy(pack, rel * 2 + part).start()
    for copy in loads[3:]:
        copy.start()
    tick()
    gain_one, gain_two = gains[layer, 0:1], gains[layer, 1:2]
    for copy in loads[:3]:
        copy.wait()
    small_out[...] = jnp.zeros_like(small_out)

    def by_rows(step):
        def one(i, _):
            step(pl.ds(pl.multiple_of(i * 128, 128), 128))
            return 0

        lax.fori_loop(0, grad.shape[0] // 128, one, 0)

    def enter(rows):
        incoming = grad_low[rows, :].astype(jnp.float32)
        grad[rows, :] = incoming
        small_out[2:3] += jnp.sum(incoming, axis=0, keepdims=True)
        grad_turned[:, rows] = incoming.T.astype(jnp.bfloat16)
        unit, _ = normalize(mid[rows, :])
        normed_turned[:, rows] = (unit * gain_two).T.astype(jnp.bfloat16)
        gathered[rows, :] = jnp.zeros((128, grad.shape[1]), jnp.float32)

    by_rows(enter)
    tick()

    def feed(part, rel):
        start = pl.multiple_of(rel * 768 + part * 384, 128)
        units = pl.ds(start, 384)
        tile = rel * 2 + part
        pre = hid[:, units].astype(jnp.float32)
        squared = pre * pre
        bent = jnp.tanh(0.7978845608028654 * pre * (1.0 + 0.044715 * squared))
        raised = 0.5 * (1.0 + bent)
        active = (pre * raised).astype(jnp.bfloat16)
        slope = raised + 0.5 * pre * (1.0 - bent * bent) * (
            0.7978845608028654 * (1.0 + 3 * 0.044715 * squared)
        )
        tile_copy(1, tile).wait()
        grad_act = dot_nn(grad_low[...], wb[1, tile])
        grad_pre = (grad_act * slope).astype(jnp.bfloat16)
        total = jnp.sum(grad_pre.astype(jnp.float32), axis=0, keepdims=True)
        small_out[pl.ds(4 + rel, 1), pl.ds(part * 384, 384)] = total
        wb[1, tile] = dot_nn(grad_turned[...], active).astype(jnp.bfloat16)
        tile_copy(0, tile).wait()
        gathered[...] += dot_nt(grad_pre, wb[0, tile])
        wb[0, tile] = dot_nn(normed_turned[...], grad_pre).astype(jnp.bfloat16)

    for part in range(2):
        for pair in range(2):

            def one(i, _):
                feed(part, 2 * pair + i)
                return 0

            lax.fori_loop(0, 2, one, 0)
            tick()

    def between(rows):
        found = gathered[rows, :]
        unit, scale = normalize(mid[rows, :])
        small_out[1:2] += jnp.sum(found * unit, axis=0, keepdims=True)
        total = grad[rows, :] + normalize_back(found, unit, scale, gain_two)
        grad[rows, :] = total
        grad_low[rows, :] = total.astype(jnp.bfloat16)

    by_rows(between)
    for copy in loads[3:]:
        copy.wait()

    def project(part, _):
        lanes = pl.ds(pl.multiple_of(part * LANES, LANES), LANES)
        grad_att[:, lanes] = dot_nt(grad_low[...], wa[1, 1, lanes, :]).astype(jnp.bfloat16)
        wa[1, 1, lanes, :] = dot_tn(att[:, lanes], grad_low[...]).astype(jnp.bfloat16)
        return 0

    lax.fori_loop(0, 3, project, 0)
    tick()
    for part in range(3):
        lanes = pl.ds(part * LANES, LANES)
        sums[...] = jnp.zeros_like(sums)
        keys_turned[...] = kv[0, :, lanes].astype(jnp.float32).T.astype(jnp.bfloat16)
        for start, count in ((0, 4 * PIECE), (PIECE, 3 * PIECE)):
            rows = pl.ds(start, PIECE)
            attention_back(
                q.at[rows, lanes],
                grad_att.at[rows, lanes],
                att.at[rows, lanes],
                kv.at[0, :count, lanes],
                kv.at[1, :count, lanes],
                keys_turned.at[:, :count],
                bias.at[:count, rows],
                lse.at[pl.ds(8 * part, 8), rows],
                sums,
                turned_q,
                count,
            )
            if start == 0:
                tick()
        kv[:, :, lanes] = sums[...].astype(jnp.bfloat16)
        share.start(part)
        if part > 0:
            share.relay(part - 1)
        tick()
    low_load = pltpu.make_async_copy(x_in, att, sems.at[9])
    low_load.start()
    low_load.wait()
    low = att
    normed = grad_att

    def again(rows):
        unit, _ = normalize(low[rows, :].astype(jnp.float32))
        normed[rows, :] = (unit * gain_one).astype(jnp.bfloat16)

    by_rows(again)

    def turned(part, _):
        lanes = pl.ds(pl.multiple_of(part * LANES, LANES), LANES)
        raw = turn(q[:, lanes].astype(jnp.float32), cosine[...], -sine_table[...])
        raw = raw.astype(jnp.bfloat16)
        found = dot_nn(raw, wa[0, 0, lanes, :])

        @pl.when(part == 0)
        def _():
            gathered[...] = found

        @pl.when(part > 0)
        def _():
            gathered[...] += found

        wa[0, 0, lanes, :] = dot_tn(raw, normed[...]).astype(jnp.bfloat16)
        return 0

    lax.fori_loop(0, 3, turned, 0)
    share.relay(2)
    tick()
    for part in range(3):
        share.collect(part)

    def keyed(part, _):
        lanes = pl.ds(pl.multiple_of(part * LANES, LANES), LANES)
        noisy, clean = pl.ds(3 * PIECE, PIECE), pl.ds(2 * PIECE, PIECE)
        raw = jnp.concatenate([kv[0, noisy, lanes], kv[0, clean, lanes]], axis=0)
        raw = turn(raw.astype(jnp.float32), cosine[...], -sine_table[...]).astype(jnp.bfloat16)
        gathered[...] += dot_nn(raw, wa[0, 1, lanes, :])
        wa[0, 1, lanes, :] = dot_tn(raw, normed[...]).astype(jnp.bfloat16)
        raw = jnp.concatenate([kv[1, noisy, lanes], kv[1, clean, lanes]], axis=0)
        gathered[...] += dot_nn(raw, wa[1, 0, lanes, :])
        wa[1, 0, lanes, :] = dot_tn(raw, normed[...]).astype(jnp.bfloat16)
        return 0

    lax.fori_loop(0, 3, keyed, 0)
    tick()
    save_a = pltpu.make_async_copy(wa, grads_a, sems.at[10])
    save_a.start()

    def leave(rows):
        found = gathered[rows, :]
        unit, scale = normalize(low[rows, :].astype(jnp.float32))
        small_out[0:1] += jnp.sum(found * unit, axis=0, keepdims=True)
        total = grad[rows, :] + normalize_back(found, unit, scale, gain_one)
        grad_low[rows, :] = total.astype(jnp.bfloat16)

    by_rows(leave)
    save_grad = pltpu.make_async_copy(grad_low, grad_out, sems.at[11])
    save_grad.start()
    tick()
    share.drain()
    save_a.wait()
    save_grad.wait()


class Ticks:
    def __init__(self, groups):
        self.groups = list(groups)

    def __call__(self):
        if self.groups:
            for step in self.groups.pop(0):
                step()

    def rest(self):
        while self.groups:
            self()


def backward_buffers(width, units):
    low, full, count = jnp.bfloat16, jnp.float32, 2 * PIECE
    return [
        pltpu.VMEM((2, 2, width, width), low),
        pltpu.VMEM((2, 8, width, units // 8), low),
        pltpu.VMEM((count, width), low),
        pltpu.VMEM((2, 4 * PIECE, width), low),
        pltpu.VMEM((count, width), low),
        pltpu.VMEM((count, width), full),
        pltpu.VMEM((count, units), low),
        pltpu.VMEM((count, width), full),
        pltpu.VMEM((count, width), full),
        pltpu.VMEM((count, width), low),
        pltpu.VMEM((count, width), low),
        pltpu.VMEM((2, PIECE, width), low),
        pltpu.VMEM((2, PIECE, width), low),
        pltpu.VMEM((2, 4 * PIECE, LANES), full),
        pltpu.VMEM((LANES, 4 * PIECE), low),
        pltpu.VMEM((LANES, PIECE), full),
        pltpu.VMEM((width, count), low),
        pltpu.VMEM((width, count), low),
        pltpu.VMEM((24, count), full),
        pltpu.VMEM((4 * PIECE, count), low),
    ]


def backward_sems():
    dma = pltpu.SemaphoreType.DMA
    return [dma((3,))] * 6 + [dma((12,)), dma((2, 8))]


BUFFERS = 20


def later(step, *args):
    return lambda: step(*args)


def second_kernel(*refs):
    ins, refs = refs[:15], refs[15:]
    (grads_a, grad_out, small_out, out, carry), refs = refs[:5], refs[5:]
    buffers, stage, feed, refs = refs[:BUFFERS], refs[BUFFERS], refs[21:23], refs[23:]
    sems, feed_sem, gate, carry_sem = refs[:16], refs[16:-2], refs[-2], refs[-1]
    low_both = ins[14]
    place = Place()
    place.meet(place.partners())
    back = Spread(place, low_both.at[1], stage, 1, out, sems[8:16])
    one, two = feed_sums(place, buffers[1], feed, feed_sem, gate)
    saves = [
        pltpu.make_async_copy(item.total(0), carry.at[i], carry_sem.at[i])
        for i, item in enumerate((one, two))
    ]
    tick = Ticks(
        [
            [back.take, back.swap, later(back.hops, 0)],
            [],
            [later(back.forward, 0)],
            [one.start],
            [later(back.hops, 1), later(back.finish, 0)],
            [],
            [one.load],
            [two.start, later(back.forward, 1)],
            [],
            [one.middle],
            [two.load, later(back.finish, 1)],
            [],
            [later(one.gather, saves[0])],
            [two.middle],
            [],
            [later(two.gather, saves[1])],
        ]
    )
    body = ins[:3] + (low_both.at[0],) + ins[4:14] + (grads_a, grad_out, small_out) + buffers
    backward_layer(1, body, place, tick, sems[:6], sems[6], sems[7])
    tick.rest()
    back.drain()
    one.drain_plane()
    two.drain_plane()
    for copy in saves:
        copy.wait()


def first_kernel(*refs):
    ins, refs = refs[:17], refs[17:]
    (grads_a, grad_out, small_out, out, done, done_a, carry_out), refs = refs[:7], refs[7:]
    buffers, stage, refs = refs[:BUFFERS], refs[BUFFERS], refs[BUFFERS + 1 :]
    feed, held, (line_total, line_in), refs = refs[:2], refs[2:10], refs[10:12], refs[12:]
    sems, feed_sem, held_sem, line_sem = refs[:16], refs[16:36], refs[36:56], refs[56:76]
    gate, gate_rows, carry_sem = refs[76:]
    carry, prior, prior_grad = ins[14:]
    place = Place()
    place.meet(place.partners())
    back = Spread(place, prior_grad, stage, 1, out, sems[8:16])
    one, two = feed_sums(place, buffers[1], feed, feed_sem, gate)
    first, second = attention_sums(place, prior, held, held_sem, gate_rows)
    lines, loads, saves = [], [], []
    for i in range(2):
        line = line_sum(place, line_total.at[i], line_in.at[i], line_sem[10 * i : 10 * i + 10])
        lines.append(line)
        loads.append(pltpu.make_async_copy(carry.at[i], line_total.at[i, 0], carry_sem.at[i]))
        saves.append(pltpu.make_async_copy(line.total(1), done.at[i], carry_sem.at[2 + i]))
    saves += [
        pltpu.make_async_copy(first.total(1), done_a.at[0], carry_sem.at[4]),
        pltpu.make_async_copy(second.total(1), done_a.at[1], carry_sem.at[5]),
        pltpu.make_async_copy(one.total(0), carry_out.at[0], carry_sem.at[6]),
        pltpu.make_async_copy(two.total(0), carry_out.at[1], carry_sem.at[7]),
    ]
    tick = Ticks(
        [
            [back.take, back.swap, loads[0].start, loads[1].start, first.start, later(back.hops, 0)],
            [later(lines[0].resume, loads[0]), first.load, second.start],
            [later(lines[1].resume, loads[1]), later(back.forward, 0)],
            [second.load, one.start, first.middle],
            [second.middle, later(back.hops, 1), lines[0].line_one],
            [first.gather, later(back.finish, 0)],
            [one.load, second.gather],
            [two.start, lines[1].line_one, lines[0].line_two],
            [later(back.forward, 1), first.line_one],
            [one.middle, second.line_one],
            [two.load, lines[1].line_two],
            [later(back.finish, 1), first.line_two, later(lines[0].store, saves[0])],
            [second.line_two],
            [later(one.gather, saves[4]), later(lines[1].store, saves[1])],
            [two.middle, later(first.store, saves[2])],
            [later(second.store, saves[3])],
            [later(two.gather, saves[5])],
        ]
    )
    body = ins[:14] + (grads_a, grad_out, small_out) + buffers
    backward_layer(0, body, place, tick, sems[:6], sems[6], sems[7])
    tick.rest()
    back.drain()
    for item in (first, second, one, two):
        item.drain_plane()
    for item in (first, second, *lines):
        item.drain_line()
    for copy in saves:
        copy.wait()


def last_kernel(*refs):
    (prior, done, done_a, carry, grad_zero, small_zero, small_one), refs = refs[:7], refs[7:]
    (out, final_a, final_b, small), refs = refs[:4], refs[4:]
    held, stage, (small_in, extra), refs = refs[:8], refs[8], refs[9:11], refs[11:]
    (line_total, line_in), sems = refs[:2], refs[2:]
    held_sem, spread_sem, line_sem, sems = sems[:20], sems[20:28], sems[28:48], sems[48:]
    tiny_send, tiny_recv, carry_sem, end_local, end_send, end_recv = sems
    place = Place()
    place.meet(place.partners())
    first, second = attention_sums(place, prior, held, held_sem)
    lines, loads = [], []
    for i in range(2):
        lines.append(line_sum(place, line_total.at[i], line_in.at[i], line_sem[10 * i : 10 * i + 10]))
        loads.append(pltpu.make_async_copy(carry.at[i], line_total.at[i, 0], carry_sem.at[i]))
    back = Spread(place, grad_zero, stage, 0, out, spread_sem)
    parts = [final_a.at[place.s, i] for i in range(2)]
    halves = [final_b.at[place.s, :, pl.ds(384 * i, 384)] for i in range(2)]
    small[0], small[1] = small_zero[...], small_one[...]
    rows_beside = ((4, 5, 6, 7), (5, 4, 7, 6), (6, 7, 4, 5), (4, 5, 6, 7), (4, 5, 6, 7))
    partners = (
        place.on(section=place.core),
        place.on(tp=place.beside_x),
        place.on(tp=place.beside_y),
        place.on(seq=place.twin),
        place.on(seq=place.far),
    )
    sources = [done.at[0], done.at[1], done_a.at[0], done_a.at[1]]

    def done_ends(i):
        source, target = sources[i], (halves + parts)[i]
        here = pltpu.make_async_copy(source, target, end_local.at[i])
        there = remote(
            source, target, end_send.at[i], end_recv.at[i], place.on(section=place.core)
        )
        return here, there

    def done_start():
        @pl.when(place.s == 1)
        def _():
            for i in range(4):
                done_ends(i)[0].start()

        @pl.when(place.s == 0)
        def _():
            for i in range(4):
                done_ends(i)[1].start()

    def done_wait():
        @pl.when(place.s == 1)
        def _():
            for i in range(4):
                here, there = done_ends(i)
                here.wait()
                there.wait_recv()

        @pl.when(place.s == 0)
        def _():
            for i in range(4):
                done_ends(i)[1].wait_send()

    def tiny(i):
        return remote(extra.at[i], small_in.at[i], tiny_send.at[i], tiny_recv.at[i], partners[i])

    def tiny_start(i):
        extra[i] = small[...]
        tiny(i).start()

    def tiny_end(i):
        tiny(i).wait_recv()
        for layer in range(2):
            small[layer, 0:4] = extra[i, layer, 0:4] + small_in[i, layer, 0:4]
            for row, other in enumerate(rows_beside[i]):
                at = row + 4
                small[layer, at : at + 1] = (
                    extra[i, layer, at : at + 1] + small_in[i, layer, other : other + 1]
                )

    first.start()
    back.take()
    for load in loads:
        load.start()
    second.start()
    back.swap()
    tiny_start(0)
    back.hops(0)
    lines[0].resume(loads[0])
    lines[1].resume(loads[1])
    first.load()
    second.load()
    tiny_end(0)
    tiny_start(1)
    back.forward(0)
    done_start()
    first.middle()
    second.middle()
    lines[0].line_one()
    tiny_end(1)
    tiny_start(2)
    first.gather()
    back.hops(1)
    second.gather()
    lines[1].line_one()
    first.line_one()
    second.line_one()
    tiny_end(2)
    tiny_start(3)
    back.finish(0)
    lines[0].line_two()
    lines[1].line_two()
    back.forward(1)
    first.line_two()
    second.line_two()
    tiny_end(3)
    tiny_start(4)
    lines[0].finish(0, halves[0])
    lines[1].finish(0, halves[1])
    back.finish(1)
    first.finish(0, parts[0])
    second.finish(0, parts[1])
    tiny_end(4)
    for item, target in ((first, parts[0]), (second, parts[1])):
        item.drain_plane()
        item.drain_line()
        item.drain_end(0, target)
    for item, target in zip(lines, halves):
        item.drain_line()
        item.drain_end(0, target)
    done_wait()
    back.drain()
    for i in range(5):
        tiny(i).wait_send()


def call(kernel, name, number, ins, spaces, shapes, out_spaces, scratch, flops, moved):
    return pl.pallas_call(
        kernel,
        name=name,
        out_shape=[jax.ShapeDtypeStruct(shape, kind) for shape, kind in shapes],
        in_specs=spaces,
        out_specs=out_spaces,
        scratch_shapes=scratch,
        compiler_params=pltpu.CompilerParams(
            collective_id=number, has_side_effects=True, vmem_limit_bytes=62 * 1024 * 1024
        ),
        cost_estimate=pl.CostEstimate(
            flops=flops, bytes_accessed=moved, transcendentals=20_000_000
        ),
    )(*ins)


def results_kernel(*refs):
    (out_zero, out_one, zero_raw, one_raw, final_a, final_b), refs = refs[:6], refs[6:]
    layer_out, input_grad, grad_out, grad_up, grad_down = refs[:5]
    rows, turned, part, tiles, converted, row_sem, tile_sem = refs[5:]
    s = lax.axis_index("section")
    count = rows.shape[0] // 2

    def load(i):
        sem = row_sem.at[0, i]
        pair, at = ((out_zero, out_one), i) if i < count else ((zero_raw, one_raw), i - count)
        return [pltpu.make_async_copy(raw.at[at // 4, at % 4], rows.at[i], sem) for raw in pair]

    def store(i):
        target, at = (layer_out, i) if i < count else (input_grad, i - count)
        return pltpu.make_async_copy(rows.at[i], target.at[at // 4, at % 4], row_sem.at[1, i])

    loads = [
        pltpu.make_async_copy(final_b.at[0], tiles.at[0], tile_sem.at[0]),
        pltpu.make_async_copy(final_b.at[1], tiles.at[1], tile_sem.at[1]),
        pltpu.make_async_copy(final_a.at[1, 1], part, tile_sem.at[2]),
    ]
    stores = [
        pltpu.make_async_copy(converted, grad_up, tile_sem.at[3]),
        pltpu.make_async_copy(turned, grad_down, tile_sem.at[4]),
    ]
    for copy in loads:
        copy.start()

    @pl.when(s == 0)
    def _():
        for i in range(2 * count):
            load(i)[0].start()

    @pl.when(s != 0)
    def _():
        for i in range(2 * count):
            load(i)[1].start()

    for copy in loads:
        copy.wait()
    converted[...] = tiles[0].astype(jnp.float32)
    stores[0].start()
    grad_out[...] = part[...].astype(jnp.float32)
    turned[...] = tiles[1].astype(jnp.float32).T
    stores[1].start()
    for i in range(2 * count):
        load(i)[0].wait()
        store(i).start()
    for i in range(2 * count):
        store(i).wait()
    for copy in stores:
        copy.wait()


def run_results(out_zero, out_one, zero_raw, one_raw, final_a, final_b):
    full = jnp.float32
    width = final_b.shape[-1]
    big = jax.ShapeDtypeStruct(out_zero.shape, out_zero.dtype)
    square = jax.ShapeDtypeStruct((width, width), full)
    dma = pltpu.SemaphoreType.DMA
    return pl.pallas_call(
        results_kernel,
        name="place_results",
        out_shape=[big, big, jax.ShapeDtypeStruct((192, width), full), square, square],
        in_specs=[HBM] * 6,
        out_specs=[HBM] * 2 + [VMEM] + [HBM] * 2,
        scratch_shapes=[
            pltpu.VMEM((16,) + out_zero.shape[2:], jnp.bfloat16),
            pltpu.VMEM((width, width), full),
            pltpu.VMEM((192, width), jnp.bfloat16),
            pltpu.VMEM((2, width, width), jnp.bfloat16),
            pltpu.VMEM((width, width), full),
            dma((2, 16)),
            dma((5,)),
        ],
        compiler_params=pltpu.CompilerParams(vmem_limit_bytes=48 * 1024 * 1024),
        cost_estimate=pl.CostEstimate(flops=1_000_000, bytes_accessed=35_000_000, transcendentals=0),
    )(out_zero, out_one, zero_raw, one_raw, final_a, final_b)


def run_backward(full_a, full_b, seeded, tokens, low_both, kept, gains, tables):
    low, full, count = jnp.bfloat16, jnp.float32, 2 * PIECE
    width, units = full_a.shape[-1], 8 * full_b.shape[-1]
    grads = [
        ((2, 2, width, width), low),
        ((count, width), low),
        ((8, width), full),
    ]
    out = ((2, 4, count, width), low)
    row_piece, tile_piece = (192, width), (width, units // 8)
    final_a, final_b = ((2, 2) + row_piece, low), ((2, width, 2 * tile_piece[1]), low)
    two_tiles, two_rows = ((2,) + tile_piece, low), ((2,) + row_piece, low)
    stage = pltpu.VMEM((4, 2, PIECE, width), low)
    dma, gate = pltpu.SemaphoreType.DMA, pltpu.SemaphoreType.REGULAR
    common = (*kept, gains, *tables)
    common_spaces = [HBM] * 11 + [VMEM] * 3
    held = sum_buffers(row_piece, (4, 4, 3, 2) * 2)
    lines = [pltpu.VMEM((2, 2) + tile_piece, low), pltpu.VMEM((2, 1) + tile_piece, low)]
    second = call(
        second_kernel,
        "backward_second",
        2,
        (full_a, full_b, seeded, tokens) + common + (low_both,),
        common_spaces + [HBM],
        grads + [out, two_tiles],
        [HBM] * 2 + [VMEM] + [HBM] * 2,
        backward_buffers(width, units)
        + [stage]
        + feed_buffers(tile_piece, 2)
        + backward_sems()
        + spread_sems()
        + sum_sems() * 2
        + [gate, dma((2,))],
        40_000_000_000,
        80_000_000,
    )
    prior, grad_one, small_one, layer_one, carried = second
    by_shard = (2, 2, 4, 192, width)
    first = call(
        first_kernel,
        "backward_first",
        3,
        (full_a, full_b, grad_one, tokens) + common + (carried, prior.reshape(by_shard), grad_one),
        common_spaces + [HBM] * 3,
        grads + [out, two_tiles, two_rows, two_tiles],
        [HBM] * 2 + [VMEM] + [HBM] * 4,
        backward_buffers(width, units)
        + [stage]
        + feed_buffers(tile_piece, 2)
        + sum_buffers(row_piece, (4, 4, 3, 2))
        + [held[4], pltpu.VMEM((1, 8, 128), low), held[6], held[7]]
        + lines
        + backward_sems()
        + spread_sems()
        + sum_sems() * 6
        + [gate, gate, dma((8,))],
        40_000_000_000,
        80_000_000,
    )
    grads_a, grad_zero, small_zero, input_one, done, done_a, carried = first
    last = call(
        last_kernel,
        "sum_and_spread",
        4,
        (grads_a.reshape(by_shard), done, done_a, carried, grad_zero, small_zero, small_one),
        [HBM] * 5 + [VMEM] * 2,
        [out, final_a, final_b, ((2, 8, width), full)],
        [HBM] * 3 + [VMEM],
        held
        + [stage]
        + [pltpu.VMEM((5, 2, 8, width), full), pltpu.VMEM((5, 2, 8, width), full)]
        + lines
        + sum_sems() * 2
        + spread_sems()
        + sum_sems() * 2
        + [dma((5,)), dma((5,)), dma((2,))]
        + [dma((4,))] * 3,
        100_000_000,
        40_000_000,
    )
    input_zero, final_a, final_b, small = last
    return layer_one, (input_zero, input_one), final_a, final_b, small


def spread(
    layer_input,
    cotangent,
    doc_lengths,
    ln1_gain,
    w_qkv,
    w_out,
    ln2_gain,
    w_up,
    b_up,
    w_down,
    b_down,
):
    s, t, z = (lax.axis_index(name) for name in ("section", "tp", "seq"))
    micros, rows, width_pos, width = layer_input.shape
    half, group = z % 2, z // 2

    own_a = jnp.stack(
        [
            jnp.stack([w_qkv[0, :, 0].T, w_qkv[0, :, 1].T]),
            jnp.stack([w_qkv[0, :, 2].T, w_out[0]]),
        ]
    )
    shard = w_up.shape[-1]
    own_b = jnp.stack([w_up[0], w_down[0].T]).reshape(2, width, 2, shard // 2).transpose(0, 2, 1, 3)
    gains = jnp.concatenate([ln1_gain, ln2_gain, b_down, jnp.zeros((5, width), jnp.float32)])
    own_c = jnp.stack([gains, jnp.concatenate([b_up, jnp.zeros((7, width), jnp.float32)])])

    lane = jnp.arange(128)
    block_base = (2 * half + s) * PIECE
    query_base = block_base + jnp.arange(2 * PIECE) % PIECE
    frequency = 10000.0 ** (-(lane % (HDIM // 2)).astype(jnp.float32) * 2.0 / HDIM)
    angles = query_base.astype(jnp.float32)[:, None] * frequency[None, :]
    sign = jnp.where(lane % HDIM < HDIM // 2, -1.0, 1.0)
    turn_cos, turn_sin = jnp.cos(angles), jnp.sin(angles) * sign

    lengths = doc_lengths.reshape(micros * rows, -1)
    flat = (micros * rows, width_pos, width)
    forward = run_forward(
        layer_input.reshape(flat), cotangent.reshape(flat), own_a, own_b, own_c, lengths, turn_cos, turn_sin
    )
    full_a, full_b, gains, seeded, tokens, low_both, *kept, layer_zero = forward
    tables = (turn_cos, turn_sin)
    layer_one, input_raws, final_a, final_b, small = run_backward(
        full_a, full_b, seeded, tokens, low_both, kept, gains, tables
    )
    layer_out, input_grad, grad_out, grad_up, grad_down = run_results(
        layer_zero, layer_one, *input_raws, final_a, final_b
    )
    small = lax.dynamic_index_in_dim(small, s, 0, keepdims=False)
    final_a = final_a.astype(jnp.float32)
    grad_qkv = jnp.stack([final_a[0, 0].T, final_a[0, 1].T, final_a[1, 0].T], axis=1)
    out_shape = (1,) + layer_input.shape
    return (
        layer_out.reshape(out_shape),
        input_grad.reshape(out_shape),
        small[0:1],
        grad_qkv[None],
        grad_out[None],
        small[1:2],
        grad_up[None],
        small[4:5],
        grad_down[None],
        small[2:3],
    )


def solution(mesh):
    sizes = tuple(mesh.shape[name] for name in ("section", "tp", "seq"))
    local = spread if sizes == (2, 4, 4) else pipelined
    return jax.shard_map(
        local,
        mesh=mesh,
        in_specs=(
            P(None, None, "seq", None),
            P(None, None, "seq", None),
            P(),
            P("section", None),
            P("section", None, None, "tp"),
            P("section", "tp", None),
            P("section", None),
            P("section", None, "tp"),
            P("section", "tp"),
            P("section", "tp", None),
            P("section", None),
        ),
        out_specs=(
            P("section", None, None, "seq", None),
            P("section", None, None, "seq", None),
            P("section", None),
            P("section", None, None, "tp"),
            P("section", "tp", None),
            P("section", None),
            P("section", None, "tp"),
            P("section", "tp"),
            P("section", "tp", None),
            P("section", None),
        ),
        check_vma=False,
    )
```

```python
import jax
import jax.numpy as jnp
from jax import lax
from jax.experimental import pallas as pl
from jax.experimental.pallas import tpu as pltpu
from jax.sharding import PartitionSpec as P

HDIM = 64
BLOCK = 16
HALF = 1024


def from_behind(value, axis, by):
    size = lax.axis_size(axis)
    pairs = [(i, i + by) for i in range(size) if 0 <= i + by < size]
    return lax.ppermute(value, axis, pairs)


def layer_norm(values, gain):
    center = values - jnp.mean(values, axis=-1, keepdims=True)
    spread = jnp.mean(center * center, axis=-1, keepdims=True)
    return center * lax.rsqrt(spread + 1e-05) * gain


def rotate(values, cosine, sine_table):
    middle = values.shape[-1] // 2
    first_half = values[..., :middle]
    second_half = values[..., middle:]
    return jnp.concatenate(
        [
            first_half * cosine - second_half * sine_table,
            second_half * cosine + first_half * sine_table,
        ],
        axis=-1,
    )


def rotary_tables(positions):
    frequency = 10000.0 ** (-jnp.arange(HDIM // 2).astype(jnp.float32) * 2.0 / HDIM)
    angles = (positions % HALF).astype(jnp.float32)[:, None, None] * frequency[None, None, :]
    return (jnp.cos(angles), jnp.sin(angles))


def allowed(query_pos, query_doc, key_pos, key_doc):
    query_noisy = query_pos < HALF
    key_noisy = key_pos < HALF
    query_block = query_pos % HALF // BLOCK
    key_block = key_pos % HALF // BLOCK
    within = query_noisy & key_noisy & (query_block == key_block)
    earlier = query_noisy & ~key_noisy & (key_block < query_block)
    causal = ~query_noisy & ~key_noisy & (key_block <= query_block)
    return (within | earlier | causal) & (query_doc == key_doc)


def document_ids(doc_lengths):
    doc_ends = jnp.cumsum(doc_lengths, axis=-1)
    base_pos = jnp.arange(2 * HALF) % HALF
    return jnp.sum((base_pos[:, None] >= doc_ends[..., None, :]).astype(jnp.int32), axis=-1)


def gelu_tanh(values):
    return jax.nn.gelu(values, approximate=True)


def keep_slot(storage, value, slot_index, is_active):
    current = lax.dynamic_index_in_dim(storage, slot_index, 0, keepdims=False)
    return lax.dynamic_update_index_in_dim(
        storage, jnp.where(is_active, value, current), slot_index, 0
    )


def local_queries(inputs, ln_one, w_mix, tables):
    cosine, sine_table, query_pos = tables
    row_count, pos_count = (inputs.shape[0], inputs.shape[1])
    normed = layer_norm(inputs, ln_one).astype(jnp.bfloat16)
    mixed = jnp.einsum("rpd,dcf->rpcf", normed, w_mix, preferred_element_type=jnp.float32)
    shaped = mixed.reshape(row_count, pos_count, 3, -1, HDIM)
    queries = rotate(shaped[:, :, 0], cosine, sine_table).astype(jnp.bfloat16)
    keys_own = rotate(shaped[:, :, 1], cosine, sine_table).astype(jnp.bfloat16)
    values_own = shaped[:, :, 2].astype(jnp.bfloat16)
    return (normed, queries, keys_own, values_own)


def masked_scores(queries, keys_heads, query_pos, docs_all):
    pos_count = queries.shape[1]
    query_docs = lax.dynamic_slice_in_dim(docs_all, query_pos[0], pos_count, 1)
    key_pos = jnp.arange(keys_heads.shape[1])
    key_mask = allowed(
        query_pos[None, :, None],
        query_docs[:, :, None],
        key_pos[None, None, :],
        docs_all[:, None, :],
    )
    scores = (
        jnp.einsum("rqhd,rkhd->rhqk", queries, keys_heads, preferred_element_type=jnp.float32)
        * 0.125
    )
    return jnp.where(key_mask[:, None], scores, -1e30)


def forward_step(inputs, weights, tables, docs_all):
    ln_one, w_mix, w_proj, ln_two, w_first, b_first, w_second, b_second = weights
    row_count, pos_count = (inputs.shape[0], inputs.shape[1])
    normed, queries, keys_own, values_own = local_queries(inputs, ln_one, w_mix, tables)
    local_width = w_mix.shape[-1]
    keys_all, values_all = (
        lax.all_gather(
            keys_own.reshape(row_count, pos_count, local_width), "seq", axis=1, tiled=True
        ),
        lax.all_gather(
            values_own.reshape(row_count, pos_count, local_width), "seq", axis=1, tiled=True
        ),
    )
    keys_heads = keys_all.reshape(row_count, keys_all.shape[1], -1, HDIM)
    values_heads = values_all.reshape(row_count, values_all.shape[1], -1, HDIM)
    softmax_out = jax.nn.softmax(
        masked_scores(queries, keys_heads, tables[2], docs_all), axis=-1
    ).astype(jnp.bfloat16)
    attended = jnp.einsum(
        "rhqk,rkhd->rqhd", softmax_out, values_heads, preferred_element_type=jnp.float32
    )
    attended = attended.astype(jnp.bfloat16).reshape(row_count, pos_count, local_width)
    middle = inputs + lax.psum(
        jnp.einsum("rpe,ed->rpd", attended, w_proj, preferred_element_type=jnp.float32).astype(
            jnp.bfloat16
        ),
        "tp",
    ).astype(jnp.float32)
    normed_two = layer_norm(middle, ln_two).astype(jnp.bfloat16)
    hidden_pre = (
        jnp.einsum("rpd,df->rpf", normed_two, w_first, preferred_element_type=jnp.float32) + b_first
    )
    activated = gelu_tanh(hidden_pre).astype(jnp.bfloat16)
    second_terms = jnp.einsum(
        "rpf,fd->rpd", activated, w_second, preferred_element_type=jnp.float32
    )
    result = (
        middle + lax.psum(second_terms.astype(jnp.bfloat16), "tp").astype(jnp.float32) + b_second
    )
    return (result, middle, keys_all, values_all)


def backward_step(inputs, middle, grad_out, weights, tables, docs_all):
    ln_one, w_mix, w_proj, ln_two, w_first, b_first, w_second, b_second = weights
    cosine, sine_table, query_pos = tables
    row_count, pos_count = (inputs.shape[0], inputs.shape[1])
    local_width = w_mix.shape[-1]
    head_count = local_width // HDIM
    normed, queries, keys_own, values_own = local_queries(inputs, ln_one, w_mix, tables)
    keys_all, values_all = (
        lax.all_gather(
            keys_own.reshape(row_count, pos_count, local_width), "seq", axis=1, tiled=True
        ),
        lax.all_gather(
            values_own.reshape(row_count, pos_count, local_width), "seq", axis=1, tiled=True
        ),
    )
    keys_heads = keys_all.reshape(row_count, keys_all.shape[1], head_count, HDIM)
    values_heads = values_all.reshape(row_count, values_all.shape[1], head_count, HDIM)
    scores = masked_scores(queries, keys_heads, query_pos, docs_all)
    softmax_out = jax.nn.softmax(scores, axis=-1)
    probs_low = softmax_out.astype(jnp.bfloat16)
    attended = jnp.einsum(
        "rhqk,rkhd->rqhd", probs_low, values_heads, preferred_element_type=jnp.float32
    )
    attended = attended.astype(jnp.bfloat16).reshape(row_count, pos_count, local_width)
    normed_two = layer_norm(middle, ln_two).astype(jnp.bfloat16)
    hidden_pre = (
        jnp.einsum("rpd,df->rpf", normed_two, w_first, preferred_element_type=jnp.float32) + b_first
    )
    activated = gelu_tanh(hidden_pre).astype(jnp.bfloat16)
    grad_low = grad_out.astype(jnp.bfloat16)
    grad_b_second = jnp.sum(grad_out, axis=(0, 1))
    grad_w_second = jnp.einsum(
        "rpf,rpd->fd", activated, grad_low, preferred_element_type=jnp.float32
    )
    grad_act = jnp.einsum("rpd,fd->rpf", grad_low, w_second, preferred_element_type=jnp.float32)
    unused_value, gelu_back = jax.vjp(gelu_tanh, hidden_pre)
    grad_pre = gelu_back(grad_act)[0].astype(jnp.bfloat16)
    grad_b_first = jnp.sum(grad_pre, axis=(0, 1), dtype=jnp.float32)
    grad_w_first = jnp.einsum(
        "rpd,rpf->df", normed_two, grad_pre, preferred_element_type=jnp.float32
    )
    grad_normed_two = lax.psum(
        jnp.einsum("rpf,df->rpd", grad_pre, w_first, preferred_element_type=jnp.float32).astype(
            jnp.bfloat16
        ),
        "tp",
    ).astype(jnp.float32)
    unused_norm, second_back = jax.vjp(layer_norm, middle, ln_two)
    grad_middle_norm, grad_ln_two = second_back(grad_normed_two)
    grad_middle = grad_out + grad_middle_norm
    middle_low = grad_middle.astype(jnp.bfloat16)
    grad_w_proj = jnp.einsum(
        "rpe,rpd->ed", attended, middle_low, preferred_element_type=jnp.float32
    )
    grad_att = jnp.einsum("rpd,ed->rpe", middle_low, w_proj, preferred_element_type=jnp.float32)
    grad_att = grad_att.astype(jnp.bfloat16).reshape(row_count, pos_count, head_count, HDIM)
    grad_probs = jnp.einsum(
        "rqhd,rkhd->rhqk", grad_att, values_heads, preferred_element_type=jnp.float32
    )
    row_delta = jnp.sum(grad_probs * softmax_out, axis=-1, keepdims=True)
    grad_scores = (softmax_out * (grad_probs - row_delta)).astype(jnp.bfloat16)
    grad_queries = (
        jnp.einsum("rhqk,rkhd->rqhd", grad_scores, keys_heads, preferred_element_type=jnp.float32)
        * 0.125
    )
    full_len = keys_all.shape[1]
    part_keys = (
        jnp.einsum("rhqk,rqhd->rkhd", grad_scores, queries, preferred_element_type=jnp.float32)
        * 0.125
    )
    part_values = jnp.einsum(
        "rhqk,rqhd->rkhd", probs_low, grad_att, preferred_element_type=jnp.float32
    )
    grad_keys, grad_values = (
        lax.psum_scatter(
            part_keys.reshape(row_count, full_len, local_width).astype(jnp.bfloat16),
            "seq",
            scatter_dimension=1,
            tiled=True,
        ).astype(jnp.float32),
        lax.psum_scatter(
            part_values.reshape(row_count, full_len, local_width).astype(jnp.bfloat16),
            "seq",
            scatter_dimension=1,
            tiled=True,
        ).astype(jnp.float32),
    )
    grad_query_raw = rotate(grad_queries.astype(jnp.bfloat16), cosine, -sine_table)
    grad_key_raw = rotate(
        grad_keys.astype(jnp.bfloat16).reshape(row_count, pos_count, head_count, HDIM),
        cosine,
        -sine_table,
    )
    grad_mixed = jnp.stack(
        [
            grad_query_raw.reshape(row_count, pos_count, local_width).astype(jnp.bfloat16),
            grad_key_raw.reshape(row_count, pos_count, local_width).astype(jnp.bfloat16),
            grad_values.astype(jnp.bfloat16),
        ],
        axis=2,
    )
    grad_w_mix = jnp.einsum("rpd,rpcf->dcf", normed, grad_mixed, preferred_element_type=jnp.float32)
    grad_normed = lax.psum(
        jnp.einsum("rpcf,dcf->rpd", grad_mixed, w_mix, preferred_element_type=jnp.float32).astype(
            jnp.bfloat16
        ),
        "tp",
    ).astype(jnp.float32)
    unused_first, first_back = jax.vjp(layer_norm, inputs, ln_one)
    grad_in_norm, grad_ln_one = first_back(grad_normed)
    grad_inputs = grad_middle + grad_in_norm
    return (
        grad_inputs,
        (
            grad_ln_one,
            grad_w_mix,
            grad_w_proj,
            grad_ln_two,
            grad_w_first,
            grad_b_first,
            grad_w_second,
            grad_b_second,
        ),
    )


def pipelined(
    layer_input,
    cotangent,
    doc_lengths,
    ln1_gain,
    w_qkv,
    w_out,
    ln2_gain,
    w_up,
    b_up,
    w_down,
    b_down,
):
    weights = tuple(
        (weight[0] for weight in (ln1_gain, w_qkv, w_out, ln2_gain, w_up, b_up, w_down, b_down))
    )
    micros, row_count, pos_count, width_model = layer_input.shape
    sections = lax.axis_size("section")
    section_index = lax.axis_index("section")
    first_pos = lax.axis_index("seq") * pos_count
    query_pos = first_pos + jnp.arange(pos_count)
    cosine, sine_table = rotary_tables(query_pos)
    tables = (cosine, sine_table, query_pos)
    docs_every = document_ids(doc_lengths)
    kept_inputs = jnp.zeros((micros, row_count, pos_count, width_model), jnp.float32)
    kept_middle = jnp.zeros((micros, row_count, pos_count, width_model), jnp.float32)
    layer_out = jnp.zeros(layer_input.shape, jnp.bfloat16)
    arrived = jnp.zeros((row_count, pos_count, width_model), jnp.bfloat16)
    moments = micros + sections - 1
    for moment in range(moments):
        offset = moment - section_index
        micro_index = jnp.clip(offset, 0, micros - 1)
        is_active = (offset >= 0) & (offset < micros)
        own_input = layer_input[min(moment, micros - 1)]
        inputs = jnp.where(section_index == 0, own_input, arrived).astype(jnp.float32)
        result, middle, keys_all, values_all = forward_step(
            inputs, weights, tables, docs_every[micro_index]
        )
        kept_inputs = keep_slot(kept_inputs, inputs, micro_index, is_active)
        kept_middle = keep_slot(kept_middle, middle, micro_index, is_active)
        result_low = result.astype(jnp.bfloat16)
        layer_out = keep_slot(layer_out, result_low, micro_index, is_active)
        if moment < moments - 1:
            arrived = from_behind(result_low, "section", 1)
    grad_totals = tuple((jnp.zeros(weight.shape, jnp.float32) for weight in weights))
    input_grad = jnp.zeros(layer_input.shape, jnp.bfloat16)
    returned = jnp.zeros((row_count, pos_count, width_model), jnp.bfloat16)
    for moment in range(moments):
        offset = moment - (sections - 1 - section_index)
        micro_index = jnp.clip(offset, 0, micros - 1)
        is_active = (offset >= 0) & (offset < micros)
        incoming = jnp.where(
            section_index == sections - 1, cotangent[min(moment, micros - 1)], returned
        ).astype(jnp.float32)
        incoming = jnp.where(is_active, incoming, 0.0)
        grad_inputs, grad_parts = backward_step(
            kept_inputs[micro_index],
            kept_middle[micro_index],
            incoming,
            weights,
            tables,
            docs_every[micro_index],
        )
        grad_totals = tuple((total + piece for total, piece in zip(grad_totals, grad_parts)))
        grad_sent = grad_inputs.astype(jnp.bfloat16)
        input_grad = keep_slot(input_grad, grad_sent, micro_index, is_active)
        if moment < moments - 1:
            returned = from_behind(grad_sent, "section", -1)
    (
        grad_ln_one,
        grad_w_mix,
        grad_w_proj,
        grad_ln_two,
        grad_w_first,
        grad_b_first,
        grad_w_second,
        grad_b_second,
    ) = grad_totals
    summed = (
        lax.psum(grad_ln_one.astype(jnp.bfloat16), "seq").astype(jnp.float32),
        lax.psum(grad_w_mix.astype(jnp.bfloat16), "seq").astype(jnp.float32),
        lax.psum(grad_w_proj.astype(jnp.bfloat16), "seq").astype(jnp.float32),
        lax.psum(grad_ln_two.astype(jnp.bfloat16), "seq").astype(jnp.float32),
        lax.psum(grad_w_first.astype(jnp.bfloat16), "seq").astype(jnp.float32),
        lax.psum(grad_b_first.astype(jnp.bfloat16), "seq").astype(jnp.float32),
        lax.psum(grad_w_second.astype(jnp.bfloat16), "seq").astype(jnp.float32),
        lax.psum(grad_b_second.astype(jnp.bfloat16), "seq").astype(jnp.float32),
    )
    return (
        layer_out[None],
        input_grad[None],
        summed[0][None],
        summed[1][None],
        summed[2][None],
        summed[3][None],
        summed[4][None],
        summed[5][None],
        summed[6][None],
        summed[7][None],
    )


PIECE = 256
LANES = 256
MESH = pl.DeviceIdType.MESH
HBM = pl.BlockSpec(memory_space=pl.ANY)
VMEM = pl.BlockSpec(memory_space=pltpu.VMEM)


def dot_nn(left, right):
    return lax.dot_general(left, right, (((1,), (0,)), ((), ())), preferred_element_type=jnp.float32)


def dot_nt(left, right):
    return lax.dot_general(left, right, (((1,), (1,)), ((), ())), preferred_element_type=jnp.float32)


def dot_tn(left, right):
    return lax.dot_general(left, right, (((0,), (0,)), ((), ())), preferred_element_type=jnp.float32)


class Place:
    def __init__(self):
        self.s, self.t, self.z = (lax.axis_index(name) for name in ("section", "tp", "seq"))
        self.core = 1 - self.s
        self.half, self.group = self.z % 2, self.z // 2
        beside_x = self.t + 1 - 2 * (self.t % 2)
        beside_y = (self.t + 2) % 4
        self.beside_x, self.beside_y = beside_x, beside_y
        self.hop_one = beside_x * (1 - self.s) + beside_y * self.s
        self.hop_two = beside_y * (1 - self.s) + beside_x * self.s
        self.rel_one, self.rel_two = 1 + self.s, 2 - self.s
        self.far = (self.z + 2) % 4
        self.twin = self.z + 1 - 2 * self.half

    def on(self, section=None, tp=None, seq=None):
        return (
            self.s if section is None else section,
            self.t if tp is None else tp,
            self.z if seq is None else seq,
        )

    def partners(self):
        return [
            self.on(section=self.core),
            self.on(tp=self.beside_x),
            self.on(tp=self.beside_y),
            self.on(seq=self.far),
            self.on(seq=self.twin),
            self.on(seq=3 - self.z),
            self.on(section=self.core, seq=self.twin),
        ]

    def meet(self, partners):
        barrier = pltpu.get_barrier_semaphore()
        for partner in partners:
            pl.semaphore_signal(barrier, inc=1, device_id=partner, device_id_type=MESH)
        pl.semaphore_wait(barrier, len(partners))


def remote(source, target, send, receive, device):
    return pltpu.make_async_remote_copy(
        src_ref=source,
        dst_ref=target,
        send_sem=send,
        recv_sem=receive,
        device_id=device,
        device_id_type=MESH,
    )


def normalize(values):
    center = values - jnp.mean(values, axis=-1, keepdims=True)
    spread = jnp.mean(center * center, axis=-1, keepdims=True)
    scale = lax.rsqrt(spread + 1e-05)
    return center * scale, scale


def turn(values, cosine, sine_table):
    width = values.shape[-1]
    times = width // cosine.shape[-1]
    lane = lax.broadcasted_iota(jnp.int32, values.shape, 1) % HDIM
    ahead = pltpu.roll(values, width - HDIM // 2, 1)
    behind = pltpu.roll(values, HDIM // 2, 1)
    swapped = jnp.where(lane < HDIM // 2, ahead, behind)
    return values * jnp.tile(cosine, (1, times)) + swapped * jnp.tile(sine_table, (1, times))


def gelu(values):
    inner = 0.7978845608028654 * (values + 0.044715 * values * values * values)
    return 0.5 * values * (1.0 + jnp.tanh(inner))


def head_mask(head, scale):
    lane = lax.broadcasted_iota(jnp.int32, (1, LANES), 1)
    inside = (lane >= head * HDIM) & (lane < (head + 1) * HDIM)
    return jnp.where(inside, jnp.float32(scale), jnp.float32(0.0))


def attention_block(q_ref, keys, values_turned, bias, lse, turned):
    def one(head, _):
        rows = pl.ds(pl.multiple_of(head * HDIM, HDIM), HDIM)
        query = q_ref[...] * head_mask(head, 0.125).astype(jnp.bfloat16)
        scores = dot_nt(keys[...], query) + bias[...]
        top = jnp.max(scores, axis=0, keepdims=True)
        raised = jnp.exp(scores - top)
        total = jnp.sum(raised, axis=0, keepdims=True)
        lse[pl.ds(head, 1), :] = top + jnp.log(total)
        turned[rows, :] = dot_nn(values_turned[rows, :], raised.astype(jnp.bfloat16)) * (1.0 / total)
        return 0

    lax.fori_loop(0, LANES // HDIM, one, 0)
    return turned[...].T.astype(jnp.bfloat16)


def fill_bias(bias, lengths, row, block):
    ends, total = [], 0
    for i in range(lengths.shape[1]):
        total = total + lengths[row, i]
        ends.append(total)

    def docs_of(base):
        return sum((base >= end).astype(jnp.int32) for end in ends)

    shape = (PIECE, bias.shape[1])
    lane = lax.broadcasted_iota(jnp.int32, shape, 1)
    query_noisy = lane < PIECE
    query_base = block * PIECE + lane - jnp.where(query_noisy, 0, PIECE)
    query_doc, query_block = docs_of(query_base), query_base >> 4
    for i in range(4):
        start = (block - 2 + min(i, 2)) * PIECE
        key_base = start + lax.broadcasted_iota(jnp.int32, shape, 0)
        key_block = key_base >> 4
        if i == 3:
            allow = query_noisy & (key_block == query_block)
        else:
            later = jnp.where(query_noisy, key_block + 1, key_block)
            allow = (later <= query_block) & (key_base >= 0)
        allow = allow & (docs_of(key_base) == query_doc)
        bias[i * PIECE : (i + 1) * PIECE, :] = jnp.where(allow, 0.0, -1e30)


class Weights:
    def __init__(self, place, own, full, sems):
        self.place, self.own, self.full = place, own, full
        (
            self.local,
            self.own_send,
            self.own_recv,
            self.hop_send,
            self.hop_recv,
            self.chip_send,
            self.chip_recv,
        ) = sems

    def source(self, chunk, pack):
        if chunk == 0:
            return self.own[0].at[pack]
        if chunk == 3:
            return self.own[2].at[pack]
        return self.own[1].at[pack, chunk - 1]

    def piece(self, layer, chunk, pack, rel):
        if chunk == 0:
            return self.full[0].at[layer, pack, :, pl.ds(pl.multiple_of(rel * 192, 64), 192)]
        if chunk == 3:
            return self.full[2].at[layer, pack, rel]
        return self.full[1].at[layer, pack, rel * 2 + chunk - 1]

    def own_copies(self, chunk, pack):
        s = self.place.s
        here = pltpu.make_async_copy(
            self.source(chunk, pack), self.piece(s, chunk, pack, 0), self.local.at[chunk, pack]
        )
        there = remote(
            self.source(chunk, pack),
            self.piece(s, chunk, pack, 0),
            self.own_send.at[chunk, pack],
            self.own_recv.at[chunk, pack],
            self.place.on(section=self.place.core),
        )
        return here, there

    def start_own(self, chunk):
        for pack in (self.place.core, self.place.s):
            for copy in self.own_copies(chunk, pack)[::-1]:
                copy.start()

    def wait_own(self, layer, chunk, pack):
        here, there = self.own_copies(chunk, pack)

        @pl.when(self.place.s == layer)
        def _():
            here.wait()

        @pl.when(self.place.s != layer)
        def _():
            there.wait_recv()

    def hops(self, layer, chunk):
        place = self.place
        own = self.piece(layer, chunk, place.s, 0)
        first = self.piece(layer, chunk, place.s, place.rel_one)
        second = self.piece(layer, chunk, place.s, place.rel_two)
        third = self.piece(layer, chunk, place.s, 3)
        moves = ((own, first, place.hop_one), (own, second, place.hop_two), (first, third, place.hop_two))
        return [
            remote(
                source,
                target,
                self.hop_send.at[layer, chunk, i],
                self.hop_recv.at[layer, chunk, i],
                place.on(tp=column),
            )
            for i, (source, target, column) in enumerate(moves)
        ]

    def chips(self, layer, chunk):
        place = self.place
        return [
            remote(
                self.piece(layer, chunk, place.s, rel),
                self.piece(layer, chunk, place.s, rel),
                self.chip_send.at[layer, chunk, i],
                self.chip_recv.at[layer, chunk, i],
                place.on(section=place.core),
            )
            for i, rel in enumerate((place.rel_one, place.rel_two, 3))
        ]

    def begin(self, layer, chunk):
        self.wait_own(layer, chunk, self.place.s)
        first, second, _ = self.hops(layer, chunk)
        first.start()
        second.start()

    def forward(self, layer, chunk):
        first, second, third = self.hops(layer, chunk)
        chips = self.chips(layer, chunk)
        first.wait_recv()
        third.start()
        chips[0].start()
        second.wait_recv()
        chips[1].start()

    def finish(self, layer, chunk):
        self.hops(layer, chunk)[2].wait_recv()
        self.chips(layer, chunk)[2].start()

    def need(self, layer, chunk):
        if chunk < 3:
            self.wait_own(layer, chunk, self.place.core)
        for copy in self.chips(layer, chunk):
            copy.wait_recv()

    def drain(self):
        for chunk in range(4):
            for pack in range(2):
                self.own_copies(chunk, pack)[1].wait_send()
            for layer in range(2):
                for copy in self.hops(layer, chunk) + self.chips(layer, chunk):
                    copy.wait_send()


class KeyShare:
    def __init__(self, place, kv, layer, sems):
        self.place, self.kv, self.layer = place, kv, layer
        self.near_send, self.near_recv, self.far_send, self.far_recv = sems
        s, odd = place.s, place.half == 1
        self.sends_near = (s == 0) | ~odd
        self.sends_far = (s == 0) & ~odd
        self.passes = (s == 0) & odd
        self.gets_near = (s == 1) | odd
        self.gets_far = odd

    def rows(self, start, part):
        lanes = pl.ds(part * LANES, LANES)
        return self.kv.at[self.layer, :, pl.ds(start, PIECE), lanes]

    def near(self, part):
        place = self.place
        return remote(
            self.rows(2 * PIECE, part),
            self.rows(PIECE, part),
            self.near_send.at[self.layer, part],
            self.near_recv.at[self.layer, part],
            place.on(section=place.core, seq=place.z + place.s * (1 - place.half)),
        )

    def far(self, part):
        place = self.place
        return remote(
            self.rows(2 * PIECE, part),
            self.rows(0, part),
            self.far_send.at[self.layer, part],
            self.far_recv.at[self.layer, part],
            place.on(seq=place.twin),
        )

    def last(self, part):
        place = self.place
        return remote(
            self.rows(PIECE, part),
            self.rows(0, part),
            self.far_send.at[self.layer, part],
            self.far_recv.at[self.layer, part],
            place.on(section=place.core),
        )

    def start(self, part):
        @pl.when(self.sends_near)
        def _():
            self.near(part).start()

        @pl.when(self.sends_far)
        def _():
            self.far(part).start()

    def arrive(self, part):
        @pl.when(self.gets_near)
        def _():
            self.near(part).wait_recv()

        @pl.when(self.passes)
        def _():
            self.last(part).start()

        @pl.when(self.gets_far)
        def _():
            self.far(part).wait_recv()

    def drain(self):
        for part in range(3):

            @pl.when(self.sends_near)
            def _():
                self.near(part).wait_send()

            @pl.when(self.sends_far)
            def _():
                self.far(part).wait_send()

            @pl.when(self.passes)
            def _():
                self.last(part).wait_send()


def forward_kernel(
    tokens,
    cotangent,
    own_a,
    own_b,
    own_c,
    lengths,
    cosine,
    sine_table,
    full_a_out,
    full_b_out,
    gains_out,
    seeded_out,
    x_out,
    low_out,
    q_out,
    kv_out,
    att_out,
    mid_out,
    hid_out,
    lse_out,
    bias_out,
    full_a,
    full_b,
    full_c,
    low,
    x,
    normed,
    q,
    kv,
    att,
    mid,
    hid,
    lse,
    values_turned,
    turned_att,
    bias,
    *sems,
):
    weight_sems, key_sems = sems[:7], sems[7:11]
    token_sem, swap_send, swap_recv, seed_sem, seed_send, seed_recv, save_sem = sems[11:]
    place = Place()
    weights = Weights(place, (own_a, own_b, own_c), (full_a, full_b, full_c), weight_sems)
    lse[...] = jnp.zeros_like(lse)
    kv[:, :, : 2 * PIECE, :] = jnp.zeros((2, 2, 2 * PIECE, kv.shape[-1]), jnp.bfloat16)
    place.meet(place.partners())
    group_rows = pl.ds(pl.multiple_of(place.group * PIECE, PIECE), PIECE)
    columns = pl.ds(pl.multiple_of(place.s * PIECE, PIECE), PIECE)

    def bring(whole, target, here, send, receive):
        kept = whole.at[4 * place.group + place.t, columns]
        sent = whole.at[4 * (1 - place.group) + place.t, columns]
        target = target.at[group_rows]
        return (
            pltpu.make_async_copy(kept, target, here),
            remote(sent, target, send, receive, place.on(seq=place.far)),
        )

    own_tokens, swap = bring(tokens, low, token_sem, swap_send, swap_recv)
    own_seed, seed_swap = bring(cotangent, seeded_out, seed_sem, seed_send, seed_recv)
    own_tokens.start()
    swap.start()
    weights.start_own(0)
    weights.begin(0, 0)
    weights.start_own(3)
    weights.start_own(1)
    for layer in range(2):
        weights.begin(layer, 3)
        weights.wait_own(layer, 3, place.core)
    gains = full_c.at[:, 0, 0]
    gains_out[...] = full_c[:, 0, 0]
    fill_bias(bias, lengths, 4 * place.group + place.t, 2 * place.half + place.s)
    bias_save = pltpu.make_async_copy(bias, bias_out, save_sem.at[17])
    bias_save.start()
    weights.forward(0, 0)
    own_tokens.wait()
    swap.wait()
    x_save = pltpu.make_async_copy(low, x_out, save_sem.at[16])
    x_save.start()
    x[...] = low[...].astype(jnp.float32)

    def saves(layer):
        pairs = [
            (low, low_out.at[layer]),
            (q, q_out.at[layer]),
            (kv.at[layer], kv_out.at[layer]),
            (att, att_out.at[layer]),
            (mid, mid_out.at[layer]),
            (hid, hid_out.at[layer]),
            (lse, lse_out.at[layer]),
        ]
        return [pltpu.make_async_copy(a, b, save_sem.at[i]) for i, (a, b) in enumerate(pairs)]

    def weight_saves(layer):
        copies = []
        for i, (a, b) in enumerate(((full_a, full_a_out), (full_b, full_b_out))):
            for pack in range(2):
                sem = save_sem.at[8 + 4 * layer + 2 * i + pack]
                copies.append(pltpu.make_async_copy(a.at[layer, pack], b.at[layer, pack], sem))
        return copies

    for layer in range(2):
        share = KeyShare(place, kv, layer, key_sems)
        unit, _ = normalize(x[...])
        normed[...] = (unit * gains[layer, 0:1]).astype(jnp.bfloat16)
        if layer == 0:
            weights.finish(0, 0)
            weights.begin(0, 1)
            weights.start_own(2)
        else:
            weights.finish(1, 0)
            weights.begin(1, 2)
            for copy in saves(0)[1:]:
                copy.wait()
        weights.need(layer, 0)
        for copy in weight_saves(layer)[:2]:
            copy.start()
        for part in range(3):
            lanes = pl.ds(part * LANES, LANES)
            keep = normed[...]
            mixed = dot_nt(keep, full_a[layer, 0, 0, lanes, :])
            q[:, lanes] = turn(mixed, cosine[...], sine_table[...]).astype(jnp.bfloat16)
            mixed = dot_nt(keep, full_a[layer, 0, 1, lanes, :])
            mixed = turn(mixed, cosine[...], sine_table[...]).astype(jnp.bfloat16)
            kv[layer, 0, 2 * PIECE : 3 * PIECE, lanes] = mixed[PIECE:]
            kv[layer, 0, 3 * PIECE :, lanes] = mixed[:PIECE]
            mixed = dot_nt(keep, full_a[layer, 1, 0, lanes, :]).astype(jnp.bfloat16)
            kv[layer, 1, 2 * PIECE : 3 * PIECE, lanes] = mixed[PIECE:]
            kv[layer, 1, 3 * PIECE :, lanes] = mixed[:PIECE]
            share.start(part)
        if layer == 0:
            weights.forward(0, 3)
            weights.forward(1, 3)
            weights.finish(0, 3)
            weights.finish(1, 3)
            own_seed.start()
            weights.begin(0, 2)
        else:
            weights.forward(1, 1)
        for part in range(3):
            lanes = pl.ds(part * LANES, LANES)
            share.arrive(part)
            values_turned[...] = kv[layer, 1, :, lanes].astype(jnp.float32).T.astype(jnp.bfloat16)
            for start, count in ((0, 4 * PIECE), (PIECE, 3 * PIECE)):
                queries = pl.ds(start, PIECE)
                att[queries, lanes] = attention_block(
                    q.at[queries, lanes],
                    kv.at[layer, 0, :count, lanes],
                    values_turned.at[:, :count],
                    bias.at[:count, queries],
                    lse.at[pl.ds(8 * part, 8), queries],
                    turned_att,
                )
            if part == 2 and layer == 0:
                seed_swap.start()
            if layer == 0:
                if part == 0:
                    weights.forward(0, 1)
                elif part == 1:
                    weights.finish(0, 1)
                    weights.begin(1, 0)
                else:
                    weights.forward(0, 2)
            else:
                if part == 1:
                    weights.finish(1, 1)
                elif part == 2:
                    weights.forward(1, 2)
        for copy in saves(layer)[1:4] + saves(layer)[6:]:
            copy.start()

        def project(part, _):
            lanes = pl.ds(pl.multiple_of(part * LANES, LANES), LANES)
            mid[:, lanes] = x[:, lanes] + dot_nn(att[...], full_a[layer, 1, 1, :, lanes])
            return 0

        lax.fori_loop(0, 3, project, 0)
        unit, _ = normalize(mid[...])
        normed[...] = (unit * gains[layer, 1:2]).astype(jnp.bfloat16)
        x[...] = mid[...] + gains[layer, 2:3]
        saves(layer)[4].start()
        weights.need(layer, 3)
        for part in range(2):
            if part == 1:
                weights.finish(layer, 2)
                if layer == 0:
                    weights.begin(1, 1)
            weights.need(layer, part + 1)
            if part == 1:
                for copy in weight_saves(layer)[2:]:
                    copy.start()

            def feed(rel, _):
                start = pl.multiple_of(rel * 768 + part * 384, 128)
                units = pl.ds(start, 384)
                shift = full_c[layer, 1, rel, 0:1, pl.ds(part * 384, 384)]
                tile = rel * 2 + part
                pre = dot_nn(normed[...], full_b[layer, 0, tile]) + shift
                hid[:, units] = pre.astype(jnp.bfloat16)
                active = gelu(pre).astype(jnp.bfloat16)
                x[...] += dot_nt(active, full_b[layer, 1, tile])
                return 0

            lax.fori_loop(0, 4, feed, 0)
        saves(layer)[5].start()
        if layer == 0:
            x_save.wait()
        else:
            saves(0)[0].wait()
        low[...] = x[...].astype(jnp.bfloat16)
        saves(layer)[0].start()
        x[...] = low[...].astype(jnp.float32)
        if layer == 0:
            weights.forward(1, 0)
    for copy in saves(1):
        copy.wait()
    for layer in range(2):
        for copy in weight_saves(layer):
            copy.wait()
        KeyShare(place, kv, layer, key_sems).drain()
    weights.drain()
    bias_save.wait()
    own_seed.wait()
    seed_swap.wait()


def run_forward(tokens, cotangent, own_a, own_b, own_c, lengths, cosine, sine_table):
    shape = jax.ShapeDtypeStruct
    low_type, full_type = jnp.bfloat16, jnp.float32
    count = 2 * PIECE
    width = tokens.shape[-1]
    units = 8 * own_b.shape[-1]
    dma = pltpu.SemaphoreType.DMA
    return pl.pallas_call(
        forward_kernel,
        name="forward_layers",
        out_shape=[
            shape((2, 2, 2, width, width), low_type),
            shape((2, 2, 8, width, units // 8), low_type),
            shape((2, 8, width), full_type),
            shape((count, width), low_type),
            shape((count, width), low_type),
            shape((2, count, width), low_type),
            shape((2, count, width), low_type),
            shape((2, 2, 4 * PIECE, width), low_type),
            shape((2, count, width), low_type),
            shape((2, count, width), full_type),
            shape((2, count, units), low_type),
            shape((2, 24, count), full_type),
            shape((4 * PIECE, count), full_type),
        ],
        in_specs=[HBM] * 5 + [pl.BlockSpec(memory_space=pltpu.SMEM)] + [VMEM] * 2,
        out_specs=[HBM] * 2 + [VMEM] + [HBM] * 10,
        scratch_shapes=[
            pltpu.VMEM((2, 2, 2, width, width), low_type),
            pltpu.VMEM((2, 2, 8, width, units // 8), low_type),
            pltpu.VMEM((2, 2, 4, 8, width), full_type),
            pltpu.VMEM((count, width), low_type),
            pltpu.VMEM((count, width), full_type),
            pltpu.VMEM((count, width), low_type),
            pltpu.VMEM((count, width), low_type),
            pltpu.VMEM((2, 2, 4 * PIECE, width), low_type),
            pltpu.VMEM((count, width), low_type),
            pltpu.VMEM((count, width), full_type),
            pltpu.VMEM((count, units), low_type),
            pltpu.VMEM((24, count), full_type),
            pltpu.VMEM((LANES, 4 * PIECE), low_type),
            pltpu.VMEM((LANES, PIECE), full_type),
            pltpu.VMEM((4 * PIECE, count), full_type),
            dma((4, 2)),
            dma((4, 2)),
            dma((4, 2)),
            dma((2, 4, 3)),
            dma((2, 4, 3)),
            dma((2, 4, 3)),
            dma((2, 4, 3)),
            dma((2, 3)),
            dma((2, 3)),
            dma((2, 3)),
            dma((2, 3)),
            dma,
            dma,
            dma,
            dma,
            dma,
            dma,
            dma((18,)),
        ],
        compiler_params=pltpu.CompilerParams(
            collective_id=1, has_side_effects=True, vmem_limit_bytes=62 * 1024 * 1024
        ),
        cost_estimate=pl.CostEstimate(
            flops=30_000_000_000, bytes_accessed=80_000_000, transcendentals=20_000_000
        ),
    )(tokens, cotangent, own_a, own_b, own_c, lengths, cosine, sine_table)


def low_sum(*parts):
    total = parts[0].astype(jnp.float32)
    for part in parts[1:]:
        total = total + part.astype(jnp.float32)
    return total.astype(jnp.bfloat16)


class Spread:
    def __init__(self, place, source, stage, layer, out, sems):
        self.place, self.source, self.stage = place, source, stage
        self.layer, self.out = layer, out
        self.local, self.swap_send, self.swap_recv, self.hop_send, self.hop_recv = sems[:5]
        self.end_local, self.end_send, self.end_recv = sems[5:]
        self.groups = (place.group, 1 - place.group)

    def entry(self):
        place = self.place
        kept = self.source.at[pl.ds(pl.multiple_of(place.group * PIECE, PIECE), PIECE)]
        sent = self.source.at[pl.ds(pl.multiple_of((1 - place.group) * PIECE, PIECE), PIECE)]
        target = self.stage.at[0, place.group]
        here = pltpu.make_async_copy(kept, target, self.local)
        there = remote(sent, target, self.swap_send, self.swap_recv, place.on(seq=place.far))
        return here, there

    def take(self):
        self.entry()[0].start()

    def swap(self):
        self.entry()[1].start()

    def moves(self, half):
        place, group = self.place, self.groups[half]
        own = self.stage.at[0, group]
        first = self.stage.at[place.rel_one, group]
        second = self.stage.at[place.rel_two, group]
        third = self.stage.at[3, group]
        listed = (
            (own, first, place.hop_one),
            (own, second, place.hop_two),
            (first, third, place.hop_two),
        )
        return [
            remote(
                source,
                target,
                self.hop_send.at[half, i],
                self.hop_recv.at[half, i],
                place.on(tp=column),
            )
            for i, (source, target, column) in enumerate(listed)
        ]

    def hops(self, half):
        here, there = self.entry()
        if half == 0:
            here.wait()
        else:
            there.wait_recv()
        first, second, _ = self.moves(half)
        first.start()
        second.start()
        self.put(half, 0)

    def forward(self, half):
        first, _, third = self.moves(half)
        first.wait_recv()
        third.start()
        self.put(half, 1)

    def finish(self, half):
        _, second, third = self.moves(half)
        second.wait_recv()
        self.put(half, 2)
        third.wait_recv()
        self.put(half, 3)

    def ends(self, half, step):
        place, group = self.place, self.groups[half]
        rows = pl.ds(pl.multiple_of(place.s * PIECE, PIECE), PIECE)
        rel = (0, place.rel_one, place.rel_two, 3)[step]
        column = (place.t, place.hop_one, place.hop_two, 3 - place.t)[step]
        source, target = self.stage.at[rel, group], self.out.at[group, column, rows]
        here = pltpu.make_async_copy(source, target, self.end_local.at[half, step])
        there = remote(
            source,
            target,
            self.end_send.at[half, step],
            self.end_recv.at[half, step],
            place.on(section=place.core),
        )
        return here, there

    def put(self, half, step):
        @pl.when(self.place.s == self.layer)
        def _():
            self.ends(half, step)[0].start()

        @pl.when(self.place.s != self.layer)
        def _():
            self.ends(half, step)[1].start()

    def drain(self):
        self.entry()[1].wait_send()
        for half in range(2):
            for copy in self.moves(half):
                copy.wait_send()

        @pl.when(self.place.s == self.layer)
        def _():
            for half in range(2):
                for step in range(4):
                    here, there = self.ends(half, step)
                    here.wait()
                    there.wait_recv()

        @pl.when(self.place.s != self.layer)
        def _():
            for half in range(2):
                for step in range(4):
                    self.ends(half, step)[1].wait_send()


def spread_sems():
    dma = pltpu.SemaphoreType.DMA
    return [dma, dma, dma, dma((2, 3)), dma((2, 3)), dma((2, 4)), dma((2, 4)), dma((2, 4))]


class Sum:
    def __init__(self, place, source, total, buffers, sems, loaded=False, opens=None, waits=None):
        self.place, self.source, self.total = place, source, total
        self.inbox, self.hop_in, self.line_in = buffers
        self.loaded, self.opens, self.waits = loaded, opens, waits
        (
            self.mine_sem,
            self.chip_send,
            self.chip_recv,
            self.hop_send,
            self.hop_recv,
            self.line_send,
            self.line_recv,
            self.end_local,
            self.end_send,
            self.end_recv,
        ) = sems
        z = place.z
        self.outer = (z == 0) | (z == 3)
        self.inner = (z == 1) | (z == 2)
        self.order = (3, 1, 2, 0)

    def mine(self, rel):
        return pltpu.make_async_copy(
            self.source(self.place.s, rel), self.total(rel), self.mine_sem.at[rel]
        )

    def other(self, rel):
        return remote(
            self.source(self.place.core, rel),
            self.inbox.at[rel],
            self.chip_send.at[rel],
            self.chip_recv.at[rel],
            self.place.on(section=self.place.core),
        )

    def start(self):
        if self.waits is not None:
            pl.semaphore_wait(self.waits, 1)
        for rel in self.order:
            if self.inbox is not None:
                self.other(rel).start()
            if self.loaded:
                self.mine(rel).start()

    def load(self, travels=True):
        for rel in self.order:
            if self.loaded:
                self.mine(rel).wait()
            if self.inbox is not None:
                self.other(rel).wait_recv()
                total = self.total(rel)
                total[...] = low_sum(total[...], self.inbox[rel])
            if travels and rel == 3:
                self.moves()[0].start()
            elif travels and rel == 2:
                self.moves()[1].start()
        if self.opens is not None:
            pl.semaphore_signal(
                self.opens,
                inc=1,
                device_id=self.place.on(section=self.place.core),
                device_id_type=MESH,
            )

    def moves(self):
        place = self.place
        listed = (
            (3, 0, place.hop_two),
            (place.rel_two, 1, place.hop_two),
            (place.rel_one, 2, place.hop_one),
        )
        return [
            remote(
                self.total(rel),
                self.hop_in.at[slot],
                self.hop_send.at[slot],
                self.hop_recv.at[slot],
                place.on(tp=column),
            )
            for rel, slot, column in listed
        ]

    def middle(self):
        first, _, third = self.moves()
        first.wait_recv()
        total = self.total(self.place.rel_one)
        total[...] = low_sum(total[...], self.hop_in[0])
        third.start()

    def lines(self):
        place = self.place
        own, line_sum = self.total(0), self.total(1)
        listed = (
            (own, self.line_in.at[0], place.twin),
            (own, self.line_in.at[1], 3 - place.z),
            (line_sum, line_sum, place.twin),
        )
        return [
            remote(
                source,
                target,
                self.line_send.at[i],
                self.line_recv.at[i],
                place.on(seq=plane),
            )
            for i, (source, target, plane) in enumerate(listed)
        ]

    def gather(self, save=None):
        _, second, third = self.moves()
        second.wait_recv()
        third.wait_recv()
        total = self.total(0)
        total[...] = low_sum(total[...], self.hop_in[1], self.hop_in[2])
        second.wait_send()
        third.wait_send()
        if save is not None:
            save.start()
        else:
            self.enter_line()

    def resume(self, saved):
        saved.wait()
        self.enter_line()

    def enter_line(self):
        @pl.when(self.outer)
        def _():
            self.lines()[0].start()

    def line_one(self):
        @pl.when(self.inner)
        def _():
            self.lines()[0].wait_recv()
            total = self.total(0)
            total[...] = low_sum(total[...], self.line_in[0])
            self.lines()[1].start()

    def line_two(self):
        @pl.when(self.inner)
        def _():
            self.lines()[1].wait_recv()
            self.total(1)[...] = low_sum(self.total(0)[...], self.line_in[1])
            self.lines()[2].start()

    def line_three(self):
        @pl.when(self.outer)
        def _():
            self.lines()[2].wait_recv()

    def ends(self, target):
        here = pltpu.make_async_copy(self.total(1), target, self.end_local)
        there = remote(
            self.total(1),
            target,
            self.end_send,
            self.end_recv,
            self.place.on(section=self.place.core),
        )
        return here, there

    def store(self, save):
        self.line_three()
        save.start()

    def finish(self, layer, target):
        self.line_three()
        here, there = self.ends(target)

        @pl.when(self.place.s == layer)
        def _():
            here.start()

        @pl.when(self.place.s != layer)
        def _():
            there.start()

    def drain_exchange(self):
        if self.inbox is not None:
            for rel in range(4):
                self.other(rel).wait_send()

    def drain_end(self, layer, target):
        here, there = self.ends(target)

        @pl.when(self.place.s == layer)
        def _():
            here.wait()
            there.wait_recv()

        @pl.when(self.place.s != layer)
        def _():
            there.wait_send()

    def drain_plane(self):
        self.drain_exchange()
        self.moves()[0].wait_send()

    def drain_line(self):
        @pl.when(self.outer)
        def _():
            self.lines()[0].wait_send()

        @pl.when(self.inner)
        def _():
            self.lines()[1].wait_send()
            self.lines()[2].wait_send()


def sum_sems():
    dma = pltpu.SemaphoreType.DMA
    return [dma((4,))] * 3 + [dma((3,))] * 4 + [dma] * 3


SUM_SEMS = 10


def sum_buffers(piece, counts):
    return [pltpu.VMEM((count,) + piece, jnp.bfloat16) for count in counts]


def attention_sums(place, grads, buffers, sems):
    sums = []
    for i in range(2):
        total, inbox, hop_in, line_in = buffers[4 * i : 4 * i + 4]

        def source(pack, rel, i=i):
            return grads.at[pack, i, rel]

        def kept(rel, total=total):
            return total.at[rel]

        own_sems = sems[SUM_SEMS * i : SUM_SEMS * (i + 1)]
        sums.append(Sum(place, source, kept, (inbox, hop_in, line_in), own_sems, loaded=True))
    return sums


def feed_sums(place, wb, buffers, sems, gate):
    inbox, sums = buffers[0], []
    for i in range(2):

        def source(pack, rel, i=i):
            return wb.at[pack, rel * 2 + i]

        def kept(rel, i=i):
            return wb.at[place.s, rel * 2 + i]

        own_sems = sems[SUM_SEMS * i : SUM_SEMS * (i + 1)]
        gates = {"opens": gate} if i == 0 else {"waits": gate}
        at = min(i, buffers[1].shape[0] - 1)
        sums.append(Sum(place, source, kept, (inbox, buffers[1].at[at], None), own_sems, **gates))
    return sums


def feed_buffers(piece, count):
    kind = jnp.bfloat16
    return [pltpu.VMEM((4,) + piece, kind), pltpu.VMEM((count, 3) + piece, kind)]


def line_sum(place, total, line_in, sems):
    return Sum(place, None, lambda rel: total.at[rel], (None, None, line_in), sems)


class KeyReturn:
    def __init__(self, place, kv, near_in, far_in, sems):
        self.place, self.kv = place, kv
        self.near_in, self.far_in, self.pass_in = near_in, far_in, far_in
        (
            self.near_send,
            self.near_recv,
            self.far_send,
            self.far_recv,
            self.pass_send,
            self.pass_recv,
        ) = sems
        s, odd = place.s, place.half == 1
        self.is_third = (s == 0) & odd
        self.is_fourth = (s == 1) & odd
        self.is_second = (s == 1) & ~odd
        self.is_first = (s == 0) & ~odd

    def sources(self, start, part):
        return self.kv.at[:, pl.ds(start, PIECE), pl.ds(part * LANES, LANES)]

    def copies(self, part):
        place = self.place
        lanes = pl.ds(part * LANES, LANES)
        near = remote(
            self.sources(PIECE, part),
            self.near_in.at[:, :, lanes],
            self.near_send.at[part],
            self.near_recv.at[part],
            place.on(section=place.core, seq=place.z - (1 - place.s) * place.half),
        )
        far = remote(
            self.sources(0, part),
            self.far_in.at[:, :, lanes],
            self.far_send.at[part],
            self.far_recv.at[part],
            place.on(seq=place.twin),
        )
        passed = remote(
            self.sources(0, part),
            self.pass_in.at[:, :, lanes],
            self.pass_send.at[part],
            self.pass_recv.at[part],
            place.on(section=place.core),
        )
        return near, far, passed

    def start(self, part):
        near, far, passed = self.copies(part)

        @pl.when(self.is_fourth)
        def _():
            passed.start()
            near.start()

        @pl.when(self.is_second)
        def _():
            near.start()

        @pl.when(self.is_third)
        def _():
            far.start()

    def relay(self, part):
        near, _, passed = self.copies(part)
        lanes = pl.ds(part * LANES, LANES)

        @pl.when(self.is_third)
        def _():
            passed.wait_recv()
            self.kv[:, PIECE : 2 * PIECE, lanes] = low_sum(
                self.kv[:, PIECE : 2 * PIECE, lanes], self.pass_in[:, :, lanes]
            )
            near.start()

    def collect(self, part):
        near, far, _ = self.copies(part)
        lanes = pl.ds(part * LANES, LANES)
        clean = pl.ds(2 * PIECE, PIECE)

        @pl.when(~self.is_fourth)
        def _():
            near.wait_recv()
            self.kv[:, clean, lanes] = low_sum(self.kv[:, clean, lanes], self.near_in[:, :, lanes])

        @pl.when(self.is_first)
        def _():
            far.wait_recv()
            self.kv[:, clean, lanes] = low_sum(self.kv[:, clean, lanes], self.far_in[:, :, lanes])

    def drain(self):
        for part in range(3):
            near, far, passed = self.copies(part)

            @pl.when(self.is_fourth)
            def _():
                passed.wait_send()
                near.wait_send()

            @pl.when(self.is_second)
            def _():
                near.wait_send()

            @pl.when(self.is_third)
            def _():
                far.wait_send()
                near.wait_send()


def normalize_back(grads, unit, scale, gain):
    lifted = grads * gain
    mean = jnp.mean(lifted, axis=-1, keepdims=True)
    along = jnp.mean(lifted * unit, axis=-1, keepdims=True)
    return scale * (lifted - mean - unit * along)


def attention_back(q_ref, grad_ref, att_ref, keys, values, keys_turned, bias, lse, sums, turned, count):
    turned[...] = (grad_ref[...].astype(jnp.float32) * att_ref[...].astype(jnp.float32)).T

    def head_terms(head):
        rows = pl.ds(pl.multiple_of(head * HDIM, HDIM), HDIM)
        query = q_ref[...] * head_mask(head, 0.125).astype(jnp.bfloat16)
        grad = grad_ref[...] * head_mask(head, 1.0).astype(jnp.bfloat16)
        delta = jnp.sum(turned[rows, :], axis=0, keepdims=True)
        scores = dot_nt(keys[...], query) + bias[...]
        probs = jnp.exp(scores - lse[pl.ds(head, 1), :])
        grad_scores = (probs * (dot_nt(values[...], grad) - delta)).astype(jnp.bfloat16)
        turned[rows, :] = dot_nn(keys_turned[rows, :], grad_scores) * 0.125
        return query, grad, grad_scores, probs.astype(jnp.bfloat16)

    def one(pair, _):
        left, right = head_terms(2 * pair), head_terms(2 * pair + 1)
        query, grad = (jnp.concatenate([left[i], right[i]], axis=0) for i in (0, 1))
        grad_scores, probs = (jnp.concatenate([left[i], right[i]], axis=1) for i in (2, 3))
        sums[0, :count] += dot_nn(grad_scores, query)
        sums[1, :count] += dot_nn(probs, grad)
        return 0

    lax.fori_loop(0, LANES // HDIM // 2, one, 0)
    q_ref[...] = turned[...].T.astype(jnp.bfloat16)


def backward_layer(layer, refs, place, tick, key_sems, sems, tile_sems):
    (
        full_a,
        full_b,
        grad_in,
        x_in,
        q_in,
        kv_in,
        att_in,
        mid_in,
        hid_in,
        lse_in,
        bias_in,
        gains,
        cosine,
        sine_table,
        grads_a,
        grad_out,
        small_out,
        wa,
        wb,
        low,
        q,
        kv,
        att,
        mid,
        hid,
        grad,
        gathered,
        grad_low,
        grad_att,
        near_in,
        far_in,
        sums,
        keys_turned,
        turned_q,
        grad_turned,
        normed_turned,
        lse,
        bias,
    ) = refs
    share = KeyReturn(place, kv, near_in, far_in, key_sems)
    pairs = [
        (grad_in, grad_low),
        (mid_in.at[layer], mid),
        (hid_in.at[layer], hid),
        (full_a.at[layer], wa),
        (att_in.at[layer], att),
        (q_in.at[layer], q),
        (kv_in.at[layer], kv),
        (x_in, low),
        (lse_in.at[layer], lse),
        (bias_in, bias),
    ]
    loads = [pltpu.make_async_copy(a, b, sems.at[i]) for i, (a, b) in enumerate(pairs)]
    def tile_copy(pack, tile):
        return pltpu.make_async_copy(
            full_b.at[layer, pack, tile], wb.at[pack, tile], tile_sems.at[pack, tile]
        )

    for copy in loads[:3]:
        copy.start()
    for part in range(2):
        for rel in range(4):
            for pack in (1, 0):
                tile_copy(pack, rel * 2 + part).start()
    for copy in loads[3:]:
        copy.start()
    tick()
    gain_one, gain_two = gains[layer, 0:1], gains[layer, 1:2]
    for copy in loads[:3]:
        copy.wait()
    small_out[...] = jnp.zeros_like(small_out)

    def by_rows(step):
        def one(i, _):
            step(pl.ds(pl.multiple_of(i * 128, 128), 128))
            return 0

        lax.fori_loop(0, grad.shape[0] // 128, one, 0)

    def enter(rows):
        incoming = grad_low[rows, :].astype(jnp.float32)
        grad[rows, :] = incoming
        small_out[2:3] += jnp.sum(incoming, axis=0, keepdims=True)
        grad_turned[:, rows] = incoming.T.astype(jnp.bfloat16)
        unit, _ = normalize(mid[rows, :])
        normed_turned[:, rows] = (unit * gain_two).T.astype(jnp.bfloat16)
        gathered[rows, :] = jnp.zeros((128, grad.shape[1]), jnp.float32)

    by_rows(enter)
    tick()

    def feed(part, rel):
        start = pl.multiple_of(rel * 768 + part * 384, 128)
        units = pl.ds(start, 384)
        tile = rel * 2 + part
        pre = hid[:, units].astype(jnp.float32)
        squared = pre * pre
        bent = jnp.tanh(0.7978845608028654 * pre * (1.0 + 0.044715 * squared))
        raised = 0.5 * (1.0 + bent)
        active = (pre * raised).astype(jnp.bfloat16)
        slope = raised + 0.5 * pre * (1.0 - bent * bent) * (
            0.7978845608028654 * (1.0 + 3 * 0.044715 * squared)
        )
        tile_copy(1, tile).wait()
        grad_act = dot_nn(grad_low[...], wb[1, tile])
        grad_pre = (grad_act * slope).astype(jnp.bfloat16)
        total = jnp.sum(grad_pre.astype(jnp.float32), axis=0, keepdims=True)
        small_out[pl.ds(4 + rel, 1), pl.ds(part * 384, 384)] = total
        wb[1, tile] = dot_nn(grad_turned[...], active).astype(jnp.bfloat16)
        tile_copy(0, tile).wait()
        gathered[...] += dot_nt(grad_pre, wb[0, tile])
        wb[0, tile] = dot_nn(normed_turned[...], grad_pre).astype(jnp.bfloat16)

    for part in range(2):
        for pair in range(2):

            def one(i, _):
                feed(part, 2 * pair + i)
                return 0

            lax.fori_loop(0, 2, one, 0)
            tick()

    def between(rows):
        found = gathered[rows, :]
        unit, scale = normalize(mid[rows, :])
        small_out[1:2] += jnp.sum(found * unit, axis=0, keepdims=True)
        total = grad[rows, :] + normalize_back(found, unit, scale, gain_two)
        grad[rows, :] = total
        grad_low[rows, :] = total.astype(jnp.bfloat16)

    by_rows(between)
    for copy in loads[3:]:
        copy.wait()

    def project(part, _):
        lanes = pl.ds(pl.multiple_of(part * LANES, LANES), LANES)
        grad_att[:, lanes] = dot_nt(grad_low[...], wa[1, 1, lanes, :]).astype(jnp.bfloat16)
        wa[1, 1, lanes, :] = dot_tn(att[:, lanes], grad_low[...]).astype(jnp.bfloat16)
        return 0

    lax.fori_loop(0, 3, project, 0)
    tick()
    for part in range(3):
        lanes = pl.ds(part * LANES, LANES)
        sums[...] = jnp.zeros_like(sums)
        keys_turned[...] = kv[0, :, lanes].astype(jnp.float32).T.astype(jnp.bfloat16)
        for start, count in ((0, 4 * PIECE), (PIECE, 3 * PIECE)):
            rows = pl.ds(start, PIECE)
            attention_back(
                q.at[rows, lanes],
                grad_att.at[rows, lanes],
                att.at[rows, lanes],
                kv.at[0, :count, lanes],
                kv.at[1, :count, lanes],
                keys_turned.at[:, :count],
                bias.at[:count, rows],
                lse.at[pl.ds(8 * part, 8), rows],
                sums,
                turned_q,
                count,
            )
            if start == 0:
                tick()
        kv[:, :, lanes] = sums[...].astype(jnp.bfloat16)
        share.start(part)
        if part > 0:
            share.relay(part - 1)
        tick()
    normed = grad_att

    def again(rows):
        unit, _ = normalize(low[rows, :].astype(jnp.float32))
        normed[rows, :] = (unit * gain_one).astype(jnp.bfloat16)

    by_rows(again)

    def turned(part, _):
        lanes = pl.ds(pl.multiple_of(part * LANES, LANES), LANES)
        raw = turn(q[:, lanes].astype(jnp.float32), cosine[...], -sine_table[...])
        raw = raw.astype(jnp.bfloat16)
        found = dot_nn(raw, wa[0, 0, lanes, :])

        @pl.when(part == 0)
        def _():
            gathered[...] = found

        @pl.when(part > 0)
        def _():
            gathered[...] += found

        wa[0, 0, lanes, :] = dot_tn(raw, normed[...]).astype(jnp.bfloat16)
        return 0

    lax.fori_loop(0, 3, turned, 0)
    share.relay(2)
    tick()
    for part in range(3):
        share.collect(part)

    def keyed(part, _):
        lanes = pl.ds(pl.multiple_of(part * LANES, LANES), LANES)
        noisy, clean = pl.ds(3 * PIECE, PIECE), pl.ds(2 * PIECE, PIECE)
        raw = jnp.concatenate([kv[0, noisy, lanes], kv[0, clean, lanes]], axis=0)
        raw = turn(raw.astype(jnp.float32), cosine[...], -sine_table[...]).astype(jnp.bfloat16)
        gathered[...] += dot_nn(raw, wa[0, 1, lanes, :])
        wa[0, 1, lanes, :] = dot_tn(raw, normed[...]).astype(jnp.bfloat16)
        raw = jnp.concatenate([kv[1, noisy, lanes], kv[1, clean, lanes]], axis=0)
        gathered[...] += dot_nn(raw, wa[1, 0, lanes, :])
        wa[1, 0, lanes, :] = dot_tn(raw, normed[...]).astype(jnp.bfloat16)
        return 0

    lax.fori_loop(0, 3, keyed, 0)
    tick()
    save_a = pltpu.make_async_copy(wa, grads_a, sems.at[10])
    save_a.start()

    def leave(rows):
        found = gathered[rows, :]
        unit, scale = normalize(low[rows, :].astype(jnp.float32))
        small_out[0:1] += jnp.sum(found * unit, axis=0, keepdims=True)
        total = grad[rows, :] + normalize_back(found, unit, scale, gain_one)
        grad_low[rows, :] = total.astype(jnp.bfloat16)

    by_rows(leave)
    save_grad = pltpu.make_async_copy(grad_low, grad_out, sems.at[11])
    save_grad.start()
    tick()
    share.drain()
    save_a.wait()
    save_grad.wait()


class Ticks:
    def __init__(self, groups):
        self.groups = list(groups)

    def __call__(self):
        if self.groups:
            for step in self.groups.pop(0):
                step()

    def rest(self):
        while self.groups:
            self()


def backward_buffers(width, units):
    low, full, count = jnp.bfloat16, jnp.float32, 2 * PIECE
    return [
        pltpu.VMEM((2, 2, width, width), low),
        pltpu.VMEM((2, 8, width, units // 8), low),
        pltpu.VMEM((count, width), low),
        pltpu.VMEM((count, width), low),
        pltpu.VMEM((2, 4 * PIECE, width), low),
        pltpu.VMEM((count, width), low),
        pltpu.VMEM((count, width), full),
        pltpu.VMEM((count, units), low),
        pltpu.VMEM((count, width), full),
        pltpu.VMEM((count, width), full),
        pltpu.VMEM((count, width), low),
        pltpu.VMEM((count, width), low),
        pltpu.VMEM((2, PIECE, width), low),
        pltpu.VMEM((2, PIECE, width), low),
        pltpu.VMEM((2, 4 * PIECE, LANES), full),
        pltpu.VMEM((LANES, 4 * PIECE), low),
        pltpu.VMEM((LANES, PIECE), full),
        pltpu.VMEM((width, count), low),
        pltpu.VMEM((width, count), low),
        pltpu.VMEM((24, count), full),
        pltpu.VMEM((4 * PIECE, count), full),
    ]


def backward_sems():
    dma = pltpu.SemaphoreType.DMA
    return [dma((3,))] * 6 + [dma((12,)), dma((2, 8))]


BUFFERS = 21


def later(step, *args):
    return lambda: step(*args)


def second_kernel(*refs):
    ins, refs = refs[:15], refs[15:]
    (grads_a, grad_out, small_out, out, carry_one, carry), refs = refs[:6], refs[6:]
    buffers, stages, feed, refs = refs[:BUFFERS], refs[BUFFERS : BUFFERS + 2], refs[23:25], refs[25:]
    sems, feed_sem, gate, carry_sem = refs[:24], refs[24:-2], refs[-2], refs[-1]
    low_both = ins[14]
    place = Place()
    place.meet(place.partners())
    zero, last = [
        Spread(place, low_both.at[i], stages[i], i, out, sems[8 + 8 * i : 16 + 8 * i])
        for i in range(2)
    ]
    one, two = feed_sums(place, buffers[1], feed, feed_sem, gate)
    carries = [
        pltpu.make_async_copy(two.total(rel), carry.at[rel], carry_sem.at[rel]) for rel in range(4)
    ]
    save_one = pltpu.make_async_copy(one.total(0), carry_one, carry_sem.at[4])

    def hand_on():
        two.load(travels=False)
        for copy in carries:
            copy.start()

    tick = Ticks(
        [
            [zero.take, last.take, zero.swap, later(zero.hops, 0), later(last.hops, 0)],
            [],
            [later(zero.forward, 0)],
            [one.start, last.swap],
            [later(zero.hops, 1), later(last.forward, 0)],
            [later(zero.finish, 0)],
            [one.load],
            [later(zero.forward, 1), two.start],
            [later(last.finish, 0)],
            [one.middle],
            [later(last.hops, 1), later(zero.finish, 1)],
            [],
            [hand_on],
            [later(one.gather, save_one), later(last.forward, 1)],
            [],
            [later(last.finish, 1)],
        ]
    )
    body = ins[:3] + (low_both.at[0],) + ins[4:14] + (grads_a, grad_out, small_out) + buffers
    backward_layer(1, body, place, tick, sems[:6], sems[6], sems[7])
    tick.rest()
    zero.drain()
    last.drain()
    one.drain_plane()
    save_one.wait()
    two.drain_exchange()
    for copy in carries:
        copy.wait()


def first_kernel(*refs):
    ins, refs = refs[:17], refs[17:]
    (grads_a, grad_out, small_out, out, done, carry_out), refs = refs[:6], refs[6:]
    buffers, stage, refs = refs[:BUFFERS], refs[BUFFERS], refs[BUFFERS + 1 :]
    feed, (total, hop_in, line_in, line_total, line_in_one), refs = refs[:2], refs[2:7], refs[7:]
    sems, feed_sem, kept_sem, line_sem = refs[:16], refs[16:36], refs[36:46], refs[46:56]
    gate, carry_sem = refs[56:]
    carry_one, carry, prior_grad = ins[14:]
    place = Place()
    place.meet(place.partners())
    back = Spread(place, prior_grad, stage, 1, out, sems[8:16])
    one, two = feed_sums(place, buffers[1], feed, feed_sem, gate)
    kept = Sum(
        place,
        lambda pack, rel: carry.at[rel],
        lambda rel: total.at[rel],
        (None, hop_in, line_in),
        kept_sem,
        loaded=True,
    )
    line = line_sum(place, line_total, line_in_one, line_sem)
    line_load = pltpu.make_async_copy(carry_one, line_total.at[0], carry_sem.at[0])
    saves = [
        pltpu.make_async_copy(line.total(1), done.at[0], carry_sem.at[1]),
        pltpu.make_async_copy(kept.total(1), done.at[1], carry_sem.at[2]),
        pltpu.make_async_copy(one.total(0), carry_out.at[0], carry_sem.at[3]),
        pltpu.make_async_copy(two.total(0), carry_out.at[1], carry_sem.at[4]),
    ]
    tick = Ticks(
        [
            [back.take, back.swap, line_load.start, kept.start, later(back.hops, 0)],
            [later(line.resume, line_load), kept.load],
            [later(back.forward, 0)],
            [one.start, line.line_one],
            [kept.middle, later(back.hops, 1)],
            [line.line_two, later(back.finish, 0)],
            [one.load],
            [kept.gather, two.start],
            [later(back.forward, 1), later(line.store, saves[0])],
            [kept.line_one],
            [one.middle, two.load],
            [kept.line_two, later(back.finish, 1)],
            [],
            [later(one.gather, saves[2]), later(kept.store, saves[1])],
            [two.middle],
            [],
            [later(two.gather, saves[3])],
        ]
    )
    body = ins[:14] + (grads_a, grad_out, small_out) + buffers
    backward_layer(0, body, place, tick, sems[:6], sems[6], sems[7])
    tick.rest()
    back.drain()
    for item in (kept, one, two):
        item.drain_plane()
    line.drain_line()
    kept.drain_line()
    for copy in saves:
        copy.wait()


def last_kernel(*refs):
    priors, (done, carry, grad_zero, small_zero, small_one), refs = refs[:2], refs[2:7], refs[7:]
    (out, final_a, final_b, small), refs = refs[:4], refs[4:]
    held, stage, (small_in, extra), refs = refs[:16], refs[16], refs[17:19], refs[19:]
    (line_total, line_in), sems = refs[:2], refs[2:]
    held_sem, spread_sem, line_sem, sems = sems[:40], sems[40:48], sems[48:68], sems[68:]
    tiny_send, tiny_recv, carry_sem, end_local, end_send, end_recv = sems
    place = Place()
    place.meet(place.partners())
    sums = []
    for i in range(2):
        sums += attention_sums(
            place, priors[i], held[8 * i : 8 * i + 8], held_sem[20 * i : 20 * i + 20]
        )
    lines, loads = [], []
    for i in range(2):
        lines.append(line_sum(place, line_total.at[i], line_in.at[i], line_sem[10 * i : 10 * i + 10]))
        loads.append(pltpu.make_async_copy(carry.at[i], line_total.at[i, 0], carry_sem.at[i]))
    back = Spread(place, grad_zero, stage, 0, out, spread_sem)
    targets = [final_a.at[place.s, 0], final_a.at[place.s, 1]] * 2
    halves = [final_b.at[place.s, :, pl.ds(384 * i, 384)] for i in range(2)]
    layers = (1, 1, 0, 0)
    small[0], small[1] = small_zero[...], small_one[...]
    rows_beside = ((4, 5, 6, 7), (5, 4, 7, 6), (6, 7, 4, 5), (4, 5, 6, 7), (4, 5, 6, 7))
    partners = (
        place.on(section=place.core),
        place.on(tp=place.beside_x),
        place.on(tp=place.beside_y),
        place.on(seq=place.twin),
        place.on(seq=place.far),
    )

    def done_ends(i):
        here = pltpu.make_async_copy(done.at[i], halves[i], end_local.at[i])
        there = remote(
            done.at[i], halves[i], end_send.at[i], end_recv.at[i], place.on(section=place.core)
        )
        return here, there

    def done_start():
        @pl.when(place.s == 1)
        def _():
            for i in range(2):
                done_ends(i)[0].start()

        @pl.when(place.s == 0)
        def _():
            for i in range(2):
                done_ends(i)[1].start()

    def done_wait():
        @pl.when(place.s == 1)
        def _():
            for i in range(2):
                here, there = done_ends(i)
                here.wait()
                there.wait_recv()

        @pl.when(place.s == 0)
        def _():
            for i in range(2):
                done_ends(i)[1].wait_send()

    def tiny(i):
        return remote(extra.at[i], small_in.at[i], tiny_send.at[i], tiny_recv.at[i], partners[i])

    def tiny_start(i):
        extra[i] = small[...]
        tiny(i).start()

    def tiny_end(i):
        tiny(i).wait_recv()
        for layer in range(2):
            small[layer, 0:4] = extra[i, layer, 0:4] + small_in[i, layer, 0:4]
            for row, other in enumerate(rows_beside[i]):
                at = row + 4
                small[layer, at : at + 1] = (
                    extra[i, layer, at : at + 1] + small_in[i, layer, other : other + 1]
                )

    back.take()
    sums[0].start()
    for load in loads:
        load.start()
    back.swap()
    tiny_start(0)
    sums[1].start()
    back.hops(0)
    for line, load in zip(lines, loads):
        line.resume(load)
    sums[0].load()
    sums[2].start()
    sums[1].load()
    sums[3].start()
    tiny_end(0)
    tiny_start(1)
    back.forward(0)
    sums[2].load()
    done_start()
    lines[0].line_one()
    sums[0].middle()
    sums[3].load()
    lines[1].line_one()
    sums[1].middle()
    lines[0].line_two()
    tiny_end(1)
    tiny_start(2)
    sums[0].gather()
    sums[2].middle()
    lines[1].line_two()
    sums[1].gather()
    sums[3].middle()
    back.hops(1)
    lines[0].finish(0, halves[0])
    sums[0].line_one()
    sums[2].gather()
    sums[1].line_one()
    tiny_end(2)
    tiny_start(3)
    lines[1].finish(0, halves[1])
    back.finish(0)
    sums[3].gather()
    sums[0].line_two()
    sums[2].line_one()
    sums[1].line_two()
    back.forward(1)
    sums[3].line_one()
    tiny_end(3)
    tiny_start(4)
    sums[0].finish(1, targets[0])
    sums[2].line_two()
    sums[1].finish(1, targets[1])
    sums[3].line_two()
    back.finish(1)
    sums[2].finish(0, targets[2])
    sums[3].finish(0, targets[3])
    tiny_end(4)
    for item, layer, target in zip(sums, layers, targets):
        item.drain_plane()
        item.drain_line()
        item.drain_end(layer, target)
    for item, target in zip(lines, halves):
        item.drain_line()
        item.drain_end(0, target)
    done_wait()
    back.drain()
    for i in range(5):
        tiny(i).wait_send()


def call(kernel, name, number, ins, spaces, shapes, out_spaces, scratch, flops, moved):
    return pl.pallas_call(
        kernel,
        name=name,
        out_shape=[jax.ShapeDtypeStruct(shape, kind) for shape, kind in shapes],
        in_specs=spaces,
        out_specs=out_spaces,
        scratch_shapes=scratch,
        compiler_params=pltpu.CompilerParams(
            collective_id=number, has_side_effects=True, vmem_limit_bytes=62 * 1024 * 1024
        ),
        cost_estimate=pl.CostEstimate(
            flops=flops, bytes_accessed=moved, transcendentals=20_000_000
        ),
    )(*ins)


def results_kernel(*refs):
    layer_raw, zero_raw, one_raw, final_a, final_b = refs[:5]
    layer_out, input_grad, grad_out, grad_up, grad_down = refs[5:10]
    rows, turned, part, tiles, converted, row_sem, tile_sem = refs[10:]
    s = lax.axis_index("section")
    count = rows.shape[0] // 2

    def load(i):
        sem = row_sem.at[0, i]
        if i < count:
            return [pltpu.make_async_copy(layer_raw.at[i // 4, i % 4], rows.at[i], sem)] * 2
        at = i - count
        return [
            pltpu.make_async_copy(raw.at[at // 4, at % 4], rows.at[i], sem) for raw in (zero_raw, one_raw)
        ]

    def store(i):
        target, at = (layer_out, i) if i < count else (input_grad, i - count)
        return pltpu.make_async_copy(rows.at[i], target.at[at // 4, at % 4], row_sem.at[1, i])

    loads = [
        pltpu.make_async_copy(final_b.at[0], tiles.at[0], tile_sem.at[0]),
        pltpu.make_async_copy(final_b.at[1], tiles.at[1], tile_sem.at[1]),
        pltpu.make_async_copy(final_a.at[1, 1], part, tile_sem.at[2]),
    ]
    stores = [
        pltpu.make_async_copy(converted, grad_up, tile_sem.at[3]),
        pltpu.make_async_copy(turned, grad_down, tile_sem.at[4]),
    ]
    for copy in loads:
        copy.start()
    for i in range(count):
        load(i)[0].start()

    @pl.when(s == 0)
    def _():
        for i in range(count, 2 * count):
            load(i)[0].start()

    @pl.when(s != 0)
    def _():
        for i in range(count, 2 * count):
            load(i)[1].start()

    for copy in loads:
        copy.wait()
    converted[...] = tiles[0].astype(jnp.float32)
    stores[0].start()
    grad_out[...] = part[...].astype(jnp.float32)
    turned[...] = tiles[1].astype(jnp.float32).T
    stores[1].start()
    for i in range(2 * count):
        load(i)[0].wait()
        store(i).start()
    for i in range(2 * count):
        store(i).wait()
    for copy in stores:
        copy.wait()


def run_results(layer_raw, zero_raw, one_raw, final_a, final_b):
    full = jnp.float32
    width = final_b.shape[-1]
    big = jax.ShapeDtypeStruct(layer_raw.shape, layer_raw.dtype)
    square = jax.ShapeDtypeStruct((width, width), full)
    dma = pltpu.SemaphoreType.DMA
    return pl.pallas_call(
        results_kernel,
        name="place_results",
        out_shape=[big, big, jax.ShapeDtypeStruct((192, width), full), square, square],
        in_specs=[HBM] * 5,
        out_specs=[HBM] * 2 + [VMEM] + [HBM] * 2,
        scratch_shapes=[
            pltpu.VMEM((16,) + layer_raw.shape[2:], jnp.bfloat16),
            pltpu.VMEM((width, width), full),
            pltpu.VMEM((192, width), jnp.bfloat16),
            pltpu.VMEM((2, width, width), jnp.bfloat16),
            pltpu.VMEM((width, width), full),
            dma((2, 16)),
            dma((5,)),
        ],
        compiler_params=pltpu.CompilerParams(vmem_limit_bytes=48 * 1024 * 1024),
        cost_estimate=pl.CostEstimate(flops=1_000_000, bytes_accessed=35_000_000, transcendentals=0),
    )(layer_raw, zero_raw, one_raw, final_a, final_b)


def run_backward(full_a, full_b, seeded, tokens, low_both, kept, gains, tables):
    low, full, count = jnp.bfloat16, jnp.float32, 2 * PIECE
    width, units = full_a.shape[-1], 8 * full_b.shape[-1]
    grads = [
        ((2, 2, width, width), low),
        ((count, width), low),
        ((8, width), full),
    ]
    out = ((2, 4, count, width), low)
    row_piece, tile_piece = (192, width), (width, units // 8)
    final_a, final_b = ((2, 2) + row_piece, low), ((2, width, 2 * tile_piece[1]), low)
    carry_one, carry, two_tiles = (tile_piece, low), ((4,) + tile_piece, low), ((2,) + tile_piece, low)
    stage = pltpu.VMEM((4, 2, PIECE, width), low)
    dma, gate = pltpu.SemaphoreType.DMA, pltpu.SemaphoreType.REGULAR
    common = (*kept, gains, *tables)
    common_spaces = [HBM] * 11 + [VMEM] * 3
    held = sum_buffers(row_piece, (4, 4, 3, 2) * 2)
    second = call(
        second_kernel,
        "backward_second",
        2,
        (full_a, full_b, seeded, tokens) + common + (low_both,),
        common_spaces + [HBM],
        grads + [out, carry_one, carry],
        [HBM] * 2 + [VMEM] + [HBM] * 3,
        backward_buffers(width, units)
        + [stage, stage]
        + feed_buffers(tile_piece, 1)
        + backward_sems()
        + spread_sems()
        + spread_sems()
        + sum_sems()
        + sum_sems()
        + [gate, dma((5,))],
        40_000_000_000,
        80_000_000,
    )
    prior_a, grad_one, small_one, layer_out, carried_one, carried = second
    first = call(
        first_kernel,
        "backward_first",
        3,
        (full_a, full_b, grad_one, tokens) + common + (carried_one, carried, grad_one),
        common_spaces + [HBM] * 3,
        grads + [out, two_tiles, two_tiles],
        [HBM] * 2 + [VMEM] + [HBM] * 3,
        backward_buffers(width, units)
        + [stage]
        + feed_buffers(tile_piece, 2)
        + sum_buffers(tile_piece, (4, 3, 2, 2, 2))
        + backward_sems()
        + spread_sems()
        + sum_sems()
        + sum_sems()
        + sum_sems()
        + sum_sems()
        + [gate, dma((5,))],
        40_000_000_000,
        80_000_000,
    )
    grads_a, grad_zero, small_zero, out_one, done, carried = first
    by_shard = (2, 2, 4, 192, width)
    last = call(
        last_kernel,
        "sum_and_spread",
        4,
        (prior_a.reshape(by_shard), grads_a.reshape(by_shard), done, carried, grad_zero)
        + (small_zero, small_one),
        [HBM] * 5 + [VMEM] * 2,
        [out, final_a, final_b, ((2, 8, width), full)],
        [HBM] * 3 + [VMEM],
        held
        + held
        + [stage]
        + [pltpu.VMEM((5, 2, 8, width), full), pltpu.VMEM((5, 2, 8, width), full)]
        + [pltpu.VMEM((2, 2) + tile_piece, low), pltpu.VMEM((2, 2) + tile_piece, low)]
        + sum_sems()
        + sum_sems()
        + sum_sems()
        + sum_sems()
        + spread_sems()
        + sum_sems()
        + sum_sems()
        + [dma((5,)), dma((5,))]
        + [dma((2,))] * 4,
        100_000_000,
        40_000_000,
    )
    out_zero, final_a, final_b, small = last
    return layer_out, (out_zero, out_one), final_a, final_b, small


def spread(
    layer_input,
    cotangent,
    doc_lengths,
    ln1_gain,
    w_qkv,
    w_out,
    ln2_gain,
    w_up,
    b_up,
    w_down,
    b_down,
):
    s, t, z = (lax.axis_index(name) for name in ("section", "tp", "seq"))
    micros, rows, width_pos, width = layer_input.shape
    half, group = z % 2, z // 2

    own_a = jnp.stack(
        [
            jnp.stack([w_qkv[0, :, 0].T, w_qkv[0, :, 1].T]),
            jnp.stack([w_qkv[0, :, 2].T, w_out[0]]),
        ]
    )
    shard = w_up.shape[-1]
    own_b = jnp.stack([w_up[0], w_down[0].T]).reshape(2, width, 2, shard // 2).transpose(0, 2, 1, 3)
    gains = jnp.concatenate([ln1_gain, ln2_gain, b_down, jnp.zeros((5, width), jnp.float32)])
    own_c = jnp.stack([gains, jnp.concatenate([b_up, jnp.zeros((7, width), jnp.float32)])])

    lane = jnp.arange(128)
    block_base = (2 * half + s) * PIECE
    query_base = block_base + jnp.arange(2 * PIECE) % PIECE
    frequency = 10000.0 ** (-(lane % (HDIM // 2)).astype(jnp.float32) * 2.0 / HDIM)
    angles = query_base.astype(jnp.float32)[:, None] * frequency[None, :]
    sign = jnp.where(lane % HDIM < HDIM // 2, -1.0, 1.0)
    turn_cos, turn_sin = jnp.cos(angles), jnp.sin(angles) * sign

    lengths = doc_lengths.reshape(micros * rows, -1)
    flat = (micros * rows, width_pos, width)
    forward = run_forward(
        layer_input.reshape(flat), cotangent.reshape(flat), own_a, own_b, own_c, lengths, turn_cos, turn_sin
    )
    full_a, full_b, gains, seeded, tokens, low_both, *kept = forward
    tables = (turn_cos, turn_sin)
    layer_raw, input_raws, final_a, final_b, small = run_backward(
        full_a, full_b, seeded, tokens, low_both, kept, gains, tables
    )
    layer_out, input_grad, grad_out, grad_up, grad_down = run_results(
        layer_raw, *input_raws, final_a, final_b
    )
    small = lax.dynamic_index_in_dim(small, s, 0, keepdims=False)
    final_a = final_a.astype(jnp.float32)
    grad_qkv = jnp.stack([final_a[0, 0].T, final_a[0, 1].T, final_a[1, 0].T], axis=1)
    out_shape = (1,) + layer_input.shape
    return (
        layer_out.reshape(out_shape),
        input_grad.reshape(out_shape),
        small[0:1],
        grad_qkv[None],
        grad_out[None],
        small[1:2],
        grad_up[None],
        small[4:5],
        grad_down[None],
        small[2:3],
    )


def solution(mesh):
    sizes = tuple(mesh.shape[name] for name in ("section", "tp", "seq"))
    local = spread if sizes == (2, 4, 4) else pipelined
    return jax.shard_map(
        local,
        mesh=mesh,
        in_specs=(
            P(None, None, "seq", None),
            P(None, None, "seq", None),
            P(),
            P("section", None),
            P("section", None, None, "tp"),
            P("section", "tp", None),
            P("section", None),
            P("section", None, "tp"),
            P("section", "tp"),
            P("section", "tp", None),
            P("section", None),
        ),
        out_specs=(
            P("section", None, None, "seq", None),
            P("section", None, None, "seq", None),
            P("section", None),
            P("section", None, None, "tp"),
            P("section", "tp", None),
            P("section", None),
            P("section", None, "tp"),
            P("section", "tp"),
            P("section", "tp", None),
            P("section", None),
        ),
        check_vma=False,
    )
```
